32 devices in a mesh: dp: 2 (over y), seq: 16 (over z, x, core).
Axes of the slice: x: 2, y: 2, z: 4, core: 2. Of those that a mesh axis runs over, the one named last changes fastest.
Arguments:
- tokens: bfloat16 [4096, 2048], P(('dp', 'seq')), may hold values from -6 to 6
- cotangent: bfloat16 [4096, 2048], P(('dp', 'seq')), may hold values from -6 to 6
- doc_lengths: int32 [2, 4], P('dp'), may hold values from 1 to 2045, as said below
- attn_gain: bfloat16 [2048], P(('dp', 'seq')), may hold values from 0.099609375 to 1.8984375
- mlp_gain: bfloat16 [2048], P(('dp', 'seq')), may hold values from 0.099609375 to 1.8984375
- query_weight: bfloat16 [2048, 2048], P(('dp', 'seq')), may hold values from -0.125 to 0.125
- key_weight: bfloat16 [2048, 512], P(('dp', 'seq')), may hold values from -0.125 to 0.125
- value_weight: bfloat16 [2048, 512], P(('dp', 'seq')), may hold values from -0.125 to 0.125
- output_weight: bfloat16 [2048, 2048], P(('dp', 'seq')), may hold values from -0.75 to 0.75
- gate_weight: bfloat16 [2048, 8192], P(('dp', 'seq')), may hold values from -0.125 to 0.125
- up_weight: bfloat16 [2048, 8192], P(('dp', 'seq')), may hold values from -0.125 to 0.125
- down_weight: bfloat16 [8192, 2048], P(('dp', 'seq')), may hold values from -0.0625 to 0.0625
Outputs:
- mixed: float32 [4096, 2048], P(('dp', 'seq'))
- token_grad: float32 [4096, 2048], P(('dp', 'seq'))
- attn_gain_grad: float32 [2048], P(('dp', 'seq'))
- mlp_gain_grad: float32 [2048], P(('dp', 'seq'))
- query_grad: float32 [2048, 2048], P(('dp', 'seq'))
- key_grad: float32 [2048, 512], P(('dp', 'seq'))
- value_grad: float32 [2048, 512], P(('dp', 'seq'))
- output_grad: float32 [2048, 2048], P(('dp', 'seq'))
- gate_grad: float32 [2048, 8192], P(('dp', 'seq'))
- up_grad: float32 [2048, 8192], P(('dp', 'seq'))
- down_grad: float32 [8192, 2048], P(('dp', 'seq'))
The draws below stay inside these ranges and needn't reach their ends.
Inputs may be any that keep to these rules, and one draw needn't show every extreme that they name: `doc_lengths`: row b lists the lengths of the 4 documents packed in order from the start of bucket b; the places after them, at most 16, are padding.
All inputs are finite; a program needn't handle non-finite values.
Results may differ from the reference program's by a relative error of at most 0.017.
Values may be sent and summed in bfloat16 or wider, within the bound.
A program may use at most 512 MiB of HBM per device.

```python
import math
import jax
import jax.numpy as jnp
from jax import lax

D = 2048
HEADS = 32
KV_HEADS = 8
HEAD_DIM = 64
FF = 8192
TOK_DEV = 128
DOCS = 4
KV_WIDTH = 512
BUCKET = 2048
TOKENS = 4096


def draw_doc_lengths(key, part):
    key = jax.random.fold_in(key, 11)

    def one_bucket(bucket_key, bucket_index):
        short_key, padding_key, chosen_key = jax.random.split(bucket_key, 3)
        first = bucket_index == 0
        shorts = jax.random.randint(short_key, (DOCS,), 1, TOK_DEV // 8 + 1)
        shorts = jnp.where(first, 1, shorts)
        padding = jax.random.randint(padding_key, (), 0, TOK_DEV // 8 + 1)
        padding = jnp.where(first, 0, padding)
        chosen = jax.random.randint(chosen_key, (), 0, DOCS)
        places = jnp.arange(DOCS)
        shorts = jnp.where(places == (chosen + 1) % DOCS, 1, shorts)
        others = jnp.sum(jnp.where(places == chosen, 0, shorts))
        longest = BUCKET - padding - others
        return jnp.where(places == chosen, longest, shorts).astype(jnp.int32)
    count = TOKENS // BUCKET
    return jax.vmap(one_bucket)(jax.random.split(key, count), jnp.arange(count, dtype=jnp.int32))


def shard_levels(key, dims, pieces, low, top_value):
    def one(dim, blocks):
        steps = jax.random.uniform(jax.random.fold_in(jax.random.fold_in(key, 6), dim), (blocks,), jnp.float32, low / len(pieces), top_value / len(pieces))
        return jnp.repeat(jnp.exp(steps), dims[dim] // blocks).reshape((-1,) + (1,) * (len(dims) - dim - 1))

    loudness = one(*pieces[0])
    for cut in pieces[1:]:
        loudness = loudness * one(*cut)
    return loudness


def normal_values(rng, dims, scale, reach, cuts=(), held_as=jnp.bfloat16):
    gain = shard_levels(rng, dims, cuts, -0.22, 0.18) if cuts else 1.0
    entries = jax.random.normal(rng, dims, jnp.float32) * scale * gain
    return jnp.minimum(jnp.maximum(entries, -reach), reach).astype(held_as)


def setup_inputs(seed: int = 0) -> dict:
    streams_of = jax.random.split(jax.random.key(seed), 13)
    return {
        "tokens": normal_values(streams_of[0], (TOKENS, D), 1.0, 6.0, ((0, 32),)),
        "cotangent": normal_values(streams_of[1], (TOKENS, D), 1.0, 6.0, ((0, 32),)),
        "doc_lengths": draw_doc_lengths(jax.random.fold_in(streams_of[12], 71), 0),
        "attn_gain": jnp.clip(1.0 + 0.18 * jax.random.normal(streams_of[3], (D,), jnp.float32), 0.099609375, 1.8984375).astype(jnp.bfloat16),
        "mlp_gain": jnp.clip(1.0 + 0.18 * jax.random.normal(streams_of[4], (D,), jnp.float32), 0.099609375, 1.8984375).astype(jnp.bfloat16),
        "query_weight": normal_values(streams_of[5], (D, D), D ** -0.5, 0.125, ((0, 32),)),
        "key_weight": normal_values(streams_of[6], (D, KV_WIDTH), D ** -0.5, 0.125, ((0, 32),)),
        "value_weight": normal_values(streams_of[7], (D, KV_WIDTH), D ** -0.5, 0.125, ((0, 32),)),
        "output_weight": normal_values(streams_of[8], (D, D), (D // 32) ** -0.5, 0.75, ((0, 32),)),
        "gate_weight": normal_values(streams_of[9], (D, FF), D ** -0.5, 0.125, ((0, 32),)),
        "up_weight": normal_values(streams_of[10], (D, FF), D ** -0.5, 0.125, ((0, 32),)),
        "down_weight": normal_values(streams_of[11], (FF, D), FF ** -0.5, 0.0625, ((0, 32),)),
    }


EPS = 1e-05
HIGHEST = lax.Precision.HIGHEST

@jax.custom_vjp
def low(v):
    return lax.optimization_barrier(v.astype(jnp.bfloat16)).astype(jnp.float32)

@jax.custom_vjp
def low_back(v):
    return v

def low_keep(v):
    return (low(v), None)

def low_pass(kept, grad):
    return (grad,)

def back_keep(v):
    return (v, None)

def back_low(kept, grad):
    return (low(grad),)
low.defvjp(low_keep, low_pass)
low_back.defvjp(back_keep, back_low)

def rotary_table(head_dim):
    exponent = jnp.arange(0, head_dim, 2, dtype=jnp.float32) / head_dim
    inverse = jnp.power(jnp.float32(500000.0), -exponent)
    wavelength = 2.0 * math.pi / inverse
    smooth = (8192.0 / wavelength - 1.0) / 3.0
    blended = (1.0 - smooth) * inverse / 32.0 + smooth * inverse
    scaled = jnp.where(wavelength < 2048.0, inverse, jnp.where(wavelength > 8192.0, inverse / 32.0, blended))
    return scaled.astype(jnp.float32)

def segment_of(doc_ends, places):
    return lax.optimization_barrier(jnp.sum((doc_ends[None, :] <= places[:, None]).astype(jnp.int32), axis=1)).astype(jnp.int32)

def opening_of(doc_ends, places):
    return lax.optimization_barrier(jnp.max(jnp.where(doc_ends[None, :] <= places[:, None], doc_ends[None, :], 0), axis=1)).astype(jnp.int32)

def rotate(values, cosine_table, sine_table):
    middle = values.shape[-1] // 2
    leading, trailing = (values[..., :middle], values[..., middle:])
    return jnp.concatenate([leading * cosine_table - trailing * sine_table, trailing * cosine_table + leading * sine_table], axis=-1)

def matmul(left_side, right_side):
    return jnp.dot(left_side, right_side, precision=HIGHEST)

def rms_scale(values):
    return values * lax.rsqrt(lax.optimization_barrier(jnp.mean(values * values, axis=-1, keepdims=True)) + EPS)

def attention(queries, key_rows, value_rows, segment):
    group_size = HEADS // KV_HEADS
    block_rows = min(512, BUCKET)
    score_scale = 1.0 / math.sqrt(HEAD_DIM)
    grouped = queries.reshape(TOKENS, KV_HEADS, group_size, HEAD_DIM)

    def one_block(block_index):
        first_row = block_index * block_rows
        opening = first_row // BUCKET * BUCKET
        query_block = lax.dynamic_slice_in_dim(grouped, first_row, block_rows, 0)
        key_block = lax.dynamic_slice_in_dim(key_rows, opening, BUCKET, 0)
        value_block = lax.dynamic_slice_in_dim(value_rows, opening, BUCKET, 0)
        query_place = first_row + jnp.arange(block_rows, dtype=jnp.int32)
        key_place = opening + jnp.arange(BUCKET, dtype=jnp.int32)
        query_seg = lax.dynamic_slice_in_dim(segment, first_row, block_rows, 0)
        key_seg = lax.dynamic_slice_in_dim(segment, opening, BUCKET, 0)
        allowed = ((query_seg[:, None] == key_seg[None, :]) & (key_place[None, :] <= query_place[:, None]))[:, None, None, :]
        scores = low_back(jnp.einsum('tkgd,ukd->tkgu', query_block, key_block, precision=HIGHEST) * score_scale)
        masked = jnp.where(allowed, scores, -1e+30)
        row_peak = lax.optimization_barrier(jnp.max(masked, axis=-1, keepdims=True))
        spread = jnp.where(allowed, jnp.exp(masked - row_peak), 0.0)
        weights = low(spread / lax.optimization_barrier(jnp.sum(spread, axis=-1, keepdims=True)))
        return jnp.einsum('tkgu,ukd->tkgd', weights, value_block, precision=HIGHEST)
    blocks = lax.map(jax.checkpoint(one_block), jnp.arange(TOKENS // block_rows, dtype=jnp.int32))
    return blocks.reshape(TOKENS, HEADS * HEAD_DIM)

def reference(tokens, cotangent, doc_lengths, attn_gain, mlp_gain, query_weight, key_weight, value_weight, output_weight, gate_weight, up_weight, down_weight):
    places = jnp.arange(BUCKET, dtype=jnp.int32)
    doc_ends = jnp.cumsum(doc_lengths, axis=1).astype(jnp.int32)
    segment = jax.vmap(segment_of, in_axes=(0, None))(doc_ends, places).reshape(TOKENS)
    openings = jax.vmap(opening_of, in_axes=(0, None))(doc_ends, places)
    position = (places[None, :] - openings).reshape(TOKENS)
    keeping = (segment < DOCS).astype(jnp.float32)[:, None]
    angles = position.astype(jnp.float32)[:, None] * rotary_table(HEAD_DIM)[None, :]
    cosine_table = jnp.cos(angles)[:, None, :]
    sine_table = jnp.sin(angles)[:, None, :]

    def forward(inputs, gain_one, gain_two, w_query, w_key, w_value, w_output, w_gate, w_up, w_down):
        normed_one = low(rms_scale(inputs) * gain_one)
        query_lin = low_back(matmul(normed_one, w_query)).reshape(TOKENS, HEADS, HEAD_DIM)
        key_lin = low_back(matmul(normed_one, w_key)).reshape(TOKENS, KV_HEADS, HEAD_DIM)
        value_rows = low(low_back(matmul(normed_one, w_value))).reshape(TOKENS, KV_HEADS, HEAD_DIM)
        queries = low(rotate(query_lin, cosine_table, sine_table))
        key_rows = low(rotate(key_lin, cosine_table, sine_table))
        attended = low(low_back(attention(queries, key_rows, value_rows, segment)))
        middle = inputs + low_back(matmul(attended, w_output))
        normed_two = low(rms_scale(middle) * gain_two)
        gate_lin = low_back(matmul(normed_two, w_gate))
        upward = low_back(matmul(normed_two, w_up))
        hidden = low(jax.nn.silu(gate_lin) * upward)
        return middle + matmul(hidden, w_down)
    mixed, pullback = jax.vjp(forward, tokens.astype(jnp.float32), attn_gain.astype(jnp.float32), mlp_gain.astype(jnp.float32), query_weight.astype(jnp.float32), key_weight.astype(jnp.float32), value_weight.astype(jnp.float32), output_weight.astype(jnp.float32), gate_weight.astype(jnp.float32), up_weight.astype(jnp.float32), down_weight.astype(jnp.float32))
    gradients = pullback(cotangent.astype(jnp.float32) * keeping)
    return (mixed, gradients[0], gradients[1], gradients[2], gradients[3], gradients[4], gradients[5], gradients[6], gradients[7], gradients[8], gradients[9])
```

```python
import functools
import math

import jax
import jax.numpy as jnp
from jax import lax
from jax.experimental import pallas as pl
from jax.experimental.pallas import tpu as pltpu
from jax.sharding import PartitionSpec as P

HEADS = 32
KV_HEADS = 8
HEAD_DIM = 64
DOCS = 4
EPS = 1e-05
NEG = -1e30
F32 = jnp.float32
BF16 = jnp.bfloat16


def rotary_table(head_dim):
    exponent = jnp.arange(0, head_dim, 2, dtype=F32) / head_dim
    inverse = jnp.power(F32(500000.0), -exponent)
    wavelength = 2.0 * math.pi / inverse
    smooth = (8192.0 / wavelength - 1.0) / 3.0
    blended = (1.0 - smooth) * inverse / 32.0 + smooth * inverse
    return jnp.where(
        wavelength < 2048.0, inverse, jnp.where(wavelength > 8192.0, inverse / 32.0, blended)
    )


def swap_halves(values):
    rows, cols = values.shape
    halves = values.reshape(rows, cols // HEAD_DIM, 2, HEAD_DIM // 2)
    return halves[:, :, ::-1].reshape(rows, cols)


def dot(a, b):
    return jnp.dot(a, b, preferred_element_type=F32)


def dot_t(a, b):
    return lax.dot_general(a, b, (((1,), (1,)), ((), ())), preferred_element_type=F32)


def t_dot(a, b):
    return lax.dot_general(a, b, (((0,), (0,)), ((), ())), preferred_element_type=F32)


def allowed_tile(opening, q_first, k_first, shape):
    rows = q_first + lax.broadcasted_iota(jnp.int32, shape, 0)
    cols = k_first + lax.broadcasted_iota(jnp.int32, shape, 1)
    return (cols <= rows) & (cols >= opening)


def attention_kernel(block, q_ref, k_ref, v_ref, open_ref, out_ref, lse_ref):
    tile = pl.program_id(0)
    opening = open_ref[...]
    for head in range(q_ref.shape[1] // HEAD_DIM):
        lanes = slice(head * HEAD_DIM, (head + 1) * HEAD_DIM)
        query = q_ref[:, lanes]

        def step(j, carry, lanes=lanes, query=query):
            peak, total, acc = carry
            first = pl.multiple_of(j * block, block)
            scores = dot_t(query, k_ref[pl.ds(first, block), lanes])
            allowed = allowed_tile(opening, tile * block, first, scores.shape)
            scores = jnp.where(allowed, scores, NEG)
            new_peak = jnp.maximum(peak, jnp.max(scores, axis=1, keepdims=True))
            spread = jnp.where(allowed, jnp.exp(scores - new_peak), 0.0)
            fade = jnp.exp(peak - new_peak)
            total = total * fade + jnp.sum(spread, axis=1, keepdims=True)
            acc = acc * fade + dot(spread.astype(BF16), v_ref[pl.ds(first, block), lanes])
            return new_peak, total, acc

        peak, total, acc = lax.fori_loop(
            0,
            tile + 1,
            step,
            (
                jnp.full((block, 1), NEG, F32),
                jnp.zeros((block, 1), F32),
                jnp.zeros((block, HEAD_DIM), F32),
            ),
        )
        out_ref[:, lanes] = acc / total
        lse_ref[:, head : head + 1] = peak + jnp.log(total)


def attention(queries, keys, values, opening, block):
    rows, cols = queries.shape
    heads = cols // HEAD_DIM
    tiled = lambda width: pl.BlockSpec((block, width), lambda i: (i, 0))
    whole = pl.BlockSpec((rows, cols), lambda i: (0, 0))
    return pl.pallas_call(
        functools.partial(attention_kernel, block),
        grid=(rows // block,),
        in_specs=[tiled(cols), whole, whole, tiled(1)],
        out_specs=[tiled(cols), tiled(heads)],
        out_shape=[
            jax.ShapeDtypeStruct((rows, cols), F32),
            jax.ShapeDtypeStruct((rows, heads), F32),
        ],
        compiler_params=pltpu.CompilerParams(vmem_limit_bytes=48 << 20),
        cost_estimate=pl.CostEstimate(
            flops=2 * rows * rows * cols, bytes_accessed=10 * rows * cols, transcendentals=0
        ),
    )(queries, keys, values, opening)


def attention_back_kernel(
    block, q_ref, k_ref, v_ref, g_ref, att_ref, lse_ref, open_ref, dq_ref, dk_ref, dv_ref
):
    tile = pl.program_id(0)

    @pl.when(tile == 0)
    def _():
        dk_ref[...] = jnp.zeros_like(dk_ref)
        dv_ref[...] = jnp.zeros_like(dv_ref)

    opening = open_ref[...]
    for head in range(q_ref.shape[1] // HEAD_DIM):
        lanes = slice(head * HEAD_DIM, (head + 1) * HEAD_DIM)
        query = q_ref[:, lanes]
        grad = g_ref[:, lanes]
        log_total = lse_ref[:, head : head + 1]
        row_sum = jnp.sum(grad.astype(F32) * att_ref[:, lanes], axis=1, keepdims=True)

        def step(j, acc, lanes=lanes, query=query, grad=grad, log_total=log_total, row_sum=row_sum):
            first = pl.multiple_of(j * block, block)
            here = pl.ds(first, block)
            key = k_ref[here, lanes]
            scores = dot_t(query, key)
            allowed = allowed_tile(opening, tile * block, first, scores.shape)
            chance = jnp.where(allowed, jnp.exp(scores - log_total), 0.0)
            prob_grad = dot_t(grad, v_ref[here, lanes])
            score_grad = (chance * (prob_grad - row_sum)).astype(BF16)
            dk_ref[here, lanes] += t_dot(score_grad, query)
            dv_ref[here, lanes] += t_dot(chance.astype(BF16), grad)
            return acc + dot(score_grad, key)

        acc = lax.fori_loop(0, tile + 1, step, jnp.zeros((block, HEAD_DIM), F32))
        dq_ref[:, lanes] = acc


def attention_back(queries, keys, values, grads, attended, log_total, opening, block):
    rows, cols = queries.shape
    heads = cols // HEAD_DIM
    tiled = lambda width: pl.BlockSpec((block, width), lambda i: (i, 0))
    whole = pl.BlockSpec((rows, cols), lambda i: (0, 0))
    return pl.pallas_call(
        functools.partial(attention_back_kernel, block),
        grid=(rows // block,),
        in_specs=[tiled(cols), whole, whole, tiled(cols), tiled(cols), tiled(heads), tiled(1)],
        out_specs=[tiled(cols), whole, whole],
        out_shape=[jax.ShapeDtypeStruct((rows, cols), F32)] * 3,
        compiler_params=pltpu.CompilerParams(vmem_limit_bytes=60 << 20),
        cost_estimate=pl.CostEstimate(
            flops=5 * rows * rows * cols, bytes_accessed=20 * rows * cols, transcendentals=0
        ),
    )(queries, keys, values, grads, attended, log_total, opening)


def swap_dp(values):
    count = lax.axis_size("dp")
    return lax.ppermute(values, "dp", [(i, (i + 1) % count) for i in range(count)])


def gather_dp(values):
    return lax.all_gather(values, "dp", axis=0, tiled=True)


def sum_dp(partial):
    half = partial.shape[0] // 2
    mine = lax.axis_index("dp")
    away = lax.dynamic_slice_in_dim(partial, (1 - mine) * half, half, 0).astype(BF16)
    kept = lax.dynamic_slice_in_dim(partial, mine * half, half, 0)
    return kept + swap_dp(away).astype(F32)


def gather_rows(values):
    return lax.all_gather(values, "seq", axis=0, tiled=True)


def scatter_rows(partial):
    return lax.psum_scatter(partial.astype(BF16), "seq", scatter_dimension=0, tiled=True).astype(F32)


def exchange(blocks):
    return lax.all_to_all(blocks, "seq", split_axis=0, concat_axis=0, tiled=True)


def norm_factor(values):
    return lax.rsqrt(jnp.mean(values * values, axis=-1, keepdims=True) + EPS)


def norm_back(inputs, factor, gain_row, upstream):
    scaled_up = gain_row * upstream
    inner_mean = jnp.mean(scaled_up * inputs, axis=-1, keepdims=True)
    grad_in = factor * scaled_up - inputs * factor * factor * factor * inner_mean
    grad_gain = jnp.sum(upstream * inputs * factor, axis=0)
    return grad_in, grad_gain


def shards(
    tokens,
    cotangent,
    doc_lengths,
    attn_gain,
    mlp_gain,
    query_weight,
    key_weight,
    value_weight,
    output_weight,
    gate_weight,
    up_weight,
    down_weight,
):
    dp = lax.axis_size("dp")
    seq = lax.axis_size("seq")
    mine = lax.axis_index("seq")
    tok_count, width = tokens.shape
    rows = tok_count * seq
    slab = query_weight.shape[0]
    share = HEAD_DIM // slab
    half_heads = HEADS // dp
    half_kv = KV_HEADS // dp
    hidden_dev = down_weight.shape[0]
    block = 512

    doc_ends = jnp.cumsum(doc_lengths[0])
    place = jnp.arange(rows, dtype=jnp.int32)
    passed = doc_ends[None, :] <= place[:, None]
    opening = jnp.max(jnp.where(passed, doc_ends[None, :], 0), axis=1)
    position = place - opening
    keeping = place < doc_ends[DOCS - 1]
    angles = position.astype(F32)[:, None] * rotary_table(HEAD_DIM)[None, :]
    cosine = jnp.cos(angles)
    sine = jnp.sin(angles)
    cos_heads = jnp.tile(cosine, (1, 2 * dp))
    sin_heads = jnp.tile(jnp.concatenate([-sine, sine], axis=1), (1, dp))
    own_keeping = lax.dynamic_slice_in_dim(keeping, mine * tok_count, tok_count, 0)

    def head_columns(weight, kept):
        split = weight.reshape(slab, dp, kept, HEAD_DIM)
        return jnp.repeat(split, seq // kept, axis=2)

    qkv_blocks = jnp.stack(
        [
            head_columns(query_weight, half_heads),
            head_columns(key_weight, half_kv),
            head_columns(value_weight, half_kv),
        ],
        axis=1,
    )
    qkv_blocks = jnp.transpose(qkv_blocks, (3, 0, 1, 2, 4)).reshape(seq * slab, 3 * dp * HEAD_DIM)
    qkv_weight = gather_dp(exchange(qkv_blocks))
    feed_blocks = jnp.stack(
        [w.reshape(slab, dp, seq, hidden_dev) for w in (gate_weight, up_weight)], axis=1
    )
    feed_blocks = jnp.transpose(feed_blocks, (3, 0, 1, 2, 4)).reshape(
        seq * slab, 2 * dp * hidden_dev
    )
    feed_weight = gather_dp(exchange(feed_blocks))
    down_own = gather_dp(down_weight)
    output_own = output_weight
    if share > 1:
        groups = [list(range(i, i + share)) for i in range(0, seq, share)]
        output_own = lax.all_gather(
            output_own, "seq", axis=0, tiled=True, axis_index_groups=groups
        )
    output_own = gather_dp(output_own)
    gains = lax.all_gather(
        jnp.stack([attn_gain, mlp_gain]), ("dp", "seq"), axis=1, tiled=True
    ).astype(F32)
    gain_one, gain_two = gains[0], gains[1]

    inputs_all = gather_rows(tokens).astype(F32)
    normed_one = (inputs_all * norm_factor(inputs_all) * gain_one).astype(BF16)
    qkv = dot(normed_one, qkv_weight)
    head_cols = dp * HEAD_DIM
    query_lin, key_lin = qkv[:, :head_cols], qkv[:, head_cols : 2 * head_cols]
    values = qkv[:, 2 * head_cols :].astype(BF16)
    scale = 1.0 / math.sqrt(HEAD_DIM)
    queries = (query_lin * cos_heads + swap_halves(query_lin) * sin_heads).astype(BF16) * BF16(scale)
    keys = (key_lin * cos_heads + swap_halves(key_lin) * sin_heads).astype(BF16)
    attended_sum, log_total = attention(queries, keys, values, opening[:, None], block)
    if share > 1:
        own_rows = ((place // tok_count) % share == mine % share)[:, None]
        attended_sum = jnp.where(own_rows, attended_sum, 0.0)
    attended = attended_sum.astype(BF16)
    inputs = tokens.astype(F32)
    middle = inputs + scatter_rows(dot(attended, output_own))

    factor_two = norm_factor(middle)
    normed_two = gather_rows((middle * factor_two * gain_two).astype(BF16))
    grad_own = jnp.where(own_keeping[:, None], cotangent, BF16(0))
    grad_out = gather_rows(grad_own)
    feed = dot(normed_two, feed_weight)
    feed_cols = dp * hidden_dev
    gate_lin, upward = feed[:, :feed_cols], feed[:, feed_cols:]
    sigmoid = jax.nn.sigmoid(gate_lin)
    hidden = (gate_lin * sigmoid * upward).astype(BF16)
    hidden_grad = dot_t(grad_out, down_own)
    gate_back = (hidden_grad * upward * sigmoid * (1.0 + gate_lin * (1.0 - sigmoid))).astype(BF16)
    up_back = (hidden_grad * gate_lin * sigmoid).astype(BF16)
    feed_back = jnp.concatenate([gate_back, up_back], axis=1)
    normed_two_grad = scatter_rows(dot_t(feed_back, feed_weight))
    mixed = middle + scatter_rows(dot(hidden, down_own))
    middle_in, gain_two_part = norm_back(middle, factor_two, gain_two, normed_two_grad)
    middle_grad = grad_own.astype(F32) + middle_in
    middle_back = gather_rows(middle_grad.astype(BF16))

    attended_grad = dot_t(middle_back, output_own).astype(BF16)
    if share > 1:
        attended_grad = jnp.where(own_rows, attended_grad, BF16(0))
    query_acc, key_acc, value_acc = attention_back(
        queries, keys, values, attended_grad, attended_sum, log_total, opening[:, None], block
    )
    query_acc = query_acc * scale
    query_back = query_acc * cos_heads - swap_halves(query_acc) * sin_heads
    key_back = key_acc * cos_heads - swap_halves(key_acc) * sin_heads
    qkv_back = jnp.concatenate([query_back, key_back, value_acc], axis=1).astype(BF16)
    normed_one_grad = scatter_rows(dot_t(qkv_back, qkv_weight))
    input_in, gain_one_part = norm_back(inputs, norm_factor(inputs), gain_one, normed_one_grad)
    token_grad = middle_grad + input_in

    feed_grad = exchange(sum_dp(t_dot(normed_two, feed_back)).astype(BF16)).astype(F32)
    feed_grad = feed_grad.reshape(seq, slab, 2, dp, hidden_dev)
    feed_grad = jnp.transpose(feed_grad, (2, 1, 3, 0, 4)).reshape(2, slab, dp * seq * hidden_dev)
    down_grad = sum_dp(t_dot(hidden, grad_out))
    output_part = t_dot(attended, middle_back)
    if share > 1:
        split = output_part.reshape(dp, share, slab, width)
        split = jnp.transpose(split, (1, 0, 2, 3)).reshape(share * dp * slab, width)
        output_part = lax.psum_scatter(
            split, "seq", scatter_dimension=0, tiled=True, axis_index_groups=groups
        )
    output_grad = sum_dp(output_part)
    qkv_grad = exchange(sum_dp(t_dot(normed_one, qkv_back)).astype(BF16)).astype(F32)
    qkv_grad = qkv_grad.reshape(seq, slab, 3, dp, HEAD_DIM)

    def own_columns(part, kept):
        summed = jnp.sum(part.reshape(kept, seq // kept, slab, dp, HEAD_DIM), axis=1)
        return jnp.transpose(summed, (1, 2, 0, 3)).reshape(slab, dp * kept * HEAD_DIM)

    query_grad = own_columns(qkv_grad[:, :, 0], half_heads)
    key_grad = own_columns(qkv_grad[:, :, 1], half_kv)
    value_grad = own_columns(qkv_grad[:, :, 2], half_kv)
    gain_parts = lax.psum(jnp.stack([gain_one_part, gain_two_part]), ("dp", "seq"))
    own = lax.axis_index("dp") * seq + mine
    gain_grads = lax.dynamic_slice_in_dim(gain_parts, own * slab, slab, 1)
    return (
        mixed,
        token_grad,
        gain_grads[0],
        gain_grads[1],
        query_grad,
        key_grad,
        value_grad,
        output_grad,
        feed_grad[0],
        feed_grad[1],
        down_grad,
    )


def solution(mesh):
    both = P(("dp", "seq"), None)
    line = P(("dp", "seq"))
    return jax.shard_map(
        shards,
        mesh=mesh,
        in_specs=(both, both, P("dp", None), line, line) + (both,) * 7,
        out_specs=(both, both, line, line) + (both,) * 7,
        check_vma=False,
    )
```

```python
import functools
import math

import jax
import jax.numpy as jnp
from jax import lax
from jax.experimental import pallas as pl
from jax.experimental.pallas import tpu as pltpu
from jax.sharding import PartitionSpec as P

HEADS = 32
KV_HEADS = 8
HEAD_DIM = 64
DOCS = 4
EPS = 1e-05
NEG = -1e30
MESH = pl.DeviceIdType.MESH
F32 = jnp.float32
BF16 = jnp.bfloat16


def rotary_table(head_dim):
    exponent = jnp.arange(0, head_dim, 2, dtype=F32) / head_dim
    inverse = jnp.power(F32(500000.0), -exponent)
    wavelength = 2.0 * math.pi / inverse
    smooth = (8192.0 / wavelength - 1.0) / 3.0
    blended = (1.0 - smooth) * inverse / 32.0 + smooth * inverse
    return jnp.where(
        wavelength < 2048.0, inverse, jnp.where(wavelength > 8192.0, inverse / 32.0, blended)
    )


def swap_halves(values):
    rows, cols = values.shape
    halves = values.reshape(rows, cols // HEAD_DIM, 2, HEAD_DIM // 2)
    return halves[:, :, ::-1].reshape(rows, cols)


def dot(a, b):
    return jnp.dot(a, b, preferred_element_type=F32)


def dot_t(a, b):
    return lax.dot_general(a, b, (((1,), (1,)), ((), ())), preferred_element_type=F32)


def t_dot(a, b):
    return lax.dot_general(a, b, (((0,), (0,)), ((), ())), preferred_element_type=F32)


def allowed_tile(opening, q_first, k_first, shape):
    rows = q_first + lax.broadcasted_iota(jnp.int32, shape, 0)
    cols = k_first + lax.broadcasted_iota(jnp.int32, shape, 1)
    return (cols <= rows) & (cols >= opening)


def attention_kernel(block, q_ref, k_ref, v_ref, open_ref, out_ref, lse_ref):
    tile = pl.program_id(0)
    opening = open_ref[...]
    for head in range(q_ref.shape[1] // HEAD_DIM):
        lanes = slice(head * HEAD_DIM, (head + 1) * HEAD_DIM)
        query = q_ref[:, lanes]

        def step(j, carry, lanes=lanes, query=query):
            peak, total, acc = carry
            first = pl.multiple_of(j * block, block)
            scores = dot_t(query, k_ref[pl.ds(first, block), lanes])
            allowed = allowed_tile(opening, tile * block, first, scores.shape)
            scores = jnp.where(allowed, scores, NEG)
            new_peak = jnp.maximum(peak, jnp.max(scores, axis=1, keepdims=True))
            spread = jnp.where(allowed, jnp.exp(scores - new_peak), 0.0)
            fade = jnp.exp(peak - new_peak)
            total = total * fade + jnp.sum(spread, axis=1, keepdims=True)
            acc = acc * fade + dot(spread.astype(BF16), v_ref[pl.ds(first, block), lanes])
            return new_peak, total, acc

        peak, total, acc = lax.fori_loop(
            0,
            tile + 1,
            step,
            (
                jnp.full((block, 1), NEG, F32),
                jnp.zeros((block, 1), F32),
                jnp.zeros((block, HEAD_DIM), F32),
            ),
        )
        out_ref[:, lanes] = acc / total
        lse_ref[:, head : head + 1] = peak + jnp.log(total)


def attention(queries, keys, values, opening, block):
    rows, cols = queries.shape
    heads = cols // HEAD_DIM
    tiled = lambda width: pl.BlockSpec((block, width), lambda i: (i, 0))
    whole = pl.BlockSpec((rows, cols), lambda i: (0, 0))
    return pl.pallas_call(
        functools.partial(attention_kernel, block),
        grid=(rows // block,),
        in_specs=[tiled(cols), whole, whole, tiled(1)],
        out_specs=[tiled(cols), tiled(heads)],
        out_shape=[
            jax.ShapeDtypeStruct((rows, cols), F32),
            jax.ShapeDtypeStruct((rows, heads), F32),
        ],
        compiler_params=pltpu.CompilerParams(vmem_limit_bytes=48 << 20),
        cost_estimate=pl.CostEstimate(
            flops=2 * rows * rows * cols, bytes_accessed=10 * rows * cols, transcendentals=0
        ),
    )(queries, keys, values, opening)


def attention_back_kernel(
    block, q_ref, k_ref, v_ref, g_ref, att_ref, lse_ref, open_ref, dq_ref, dk_ref, dv_ref
):
    tile = pl.program_id(0)

    @pl.when(tile == 0)
    def _():
        dk_ref[...] = jnp.zeros_like(dk_ref)
        dv_ref[...] = jnp.zeros_like(dv_ref)

    opening = open_ref[...]
    for head in range(q_ref.shape[1] // HEAD_DIM):
        lanes = slice(head * HEAD_DIM, (head + 1) * HEAD_DIM)
        query = q_ref[:, lanes]
        grad = g_ref[:, lanes]
        log_total = lse_ref[:, head : head + 1]
        row_sum = jnp.sum(grad.astype(F32) * att_ref[:, lanes], axis=1, keepdims=True)

        def step(j, acc, lanes=lanes, query=query, grad=grad, log_total=log_total, row_sum=row_sum):
            first = pl.multiple_of(j * block, block)
            here = pl.ds(first, block)
            key = k_ref[here, lanes]
            scores = dot_t(query, key)
            allowed = allowed_tile(opening, tile * block, first, scores.shape)
            chance = jnp.where(allowed, jnp.exp(scores - log_total), 0.0)
            prob_grad = dot_t(grad, v_ref[here, lanes])
            score_grad = (chance * (prob_grad - row_sum)).astype(BF16)
            dk_ref[here, lanes] += t_dot(score_grad, query)
            dv_ref[here, lanes] += t_dot(chance.astype(BF16), grad)
            return acc + dot(score_grad, key)

        acc = lax.fori_loop(0, tile + 1, step, jnp.zeros((block, HEAD_DIM), F32))
        dq_ref[:, lanes] = acc


def attention_back(queries, keys, values, grads, attended, log_total, opening, block):
    rows, cols = queries.shape
    heads = cols // HEAD_DIM
    tiled = lambda width: pl.BlockSpec((block, width), lambda i: (i, 0))
    whole = pl.BlockSpec((rows, cols), lambda i: (0, 0))
    return pl.pallas_call(
        functools.partial(attention_back_kernel, block),
        grid=(rows // block,),
        in_specs=[tiled(cols), whole, whole, tiled(cols), tiled(cols), tiled(heads), tiled(1)],
        out_specs=[tiled(cols), whole, whole],
        out_shape=[jax.ShapeDtypeStruct((rows, cols), F32)] * 3,
        compiler_params=pltpu.CompilerParams(vmem_limit_bytes=60 << 20),
        cost_estimate=pl.CostEstimate(
            flops=5 * rows * rows * cols, bytes_accessed=20 * rows * cols, transcendentals=0
        ),
    )(queries, keys, values, grads, attended, log_total, opening)


class Place:
    def __init__(self):
        self.dp = lax.axis_index("dp")
        seq = lax.axis_index("seq")
        self.length = lax.axis_size("seq") // 4
        self.line = lax.div(seq, 4)
        self.pair = lax.rem(lax.div(seq, 2), 2)
        self.core = lax.rem(seq, 2)

    def index(self, line, pair, core):
        return (line * 2 + pair) * 2 + core

    def device(self, line, pair, core):
        return (self.dp, self.index(line, pair, core))

    def sibling(self):
        return self.device(self.line, self.pair, 1 - self.core)

    def across(self):
        return self.device(self.line, 1 - self.pair, self.core)

    def above(self):
        return self.device(self.line + 1, self.pair, self.core)

    def below(self):
        return self.device(self.line - 1, self.pair, self.core)

    def greet(self):
        barrier = pltpu.get_barrier_semaphore()

        def signal(device):
            pl.semaphore_signal(barrier, inc=1, device_id=device, device_id_type=MESH)

        signal(self.sibling())
        signal(self.across())
        pl.when(self.line > 0)(lambda: signal(self.below()))
        pl.when(self.line < self.length - 1)(lambda: signal(self.above()))
        inner = (self.line > 0) & (self.line < self.length - 1)
        pl.semaphore_wait(barrier, jnp.where(inner, 4, 3))


def remote(src, dst, send_sem, recv_sem, device):
    return pltpu.make_async_remote_copy(
        src_ref=src,
        dst_ref=dst,
        send_sem=send_sem,
        recv_sem=recv_sem,
        device_id=device,
        device_id_type=MESH,
    )


def scatter_kernel(
    transposed,
    parts,
    tile,
    a_ref,
    b_ref,
    out_ref,
    core_out,
    core_in,
    pair_out,
    pair_in,
    line_out,
    up_in,
    down_in,
    held,
    core_sems,
    pair_sems,
    line_sems,
    up_sems,
    down_sems,
):
    here = Place()
    here.greet()
    length = here.length
    rows = out_ref.shape[0]
    width = out_ref.shape[1] // parts
    tiles = width // tile
    steps = length * parts

    def target(i):
        ups = length - 1 - here.line
        near = here.line < length // 2
        if_near = jnp.where(i < ups, length - 1 - i, i - ups)
        if_far = jnp.where(i < here.line, i, length - 1 - (i - here.line))
        return jnp.where(i == length - 1, here.line, jnp.where(near, if_near, if_far))

    def product(line, pair, core, part, use):
        first = pl.multiple_of(here.index(line, pair, core) * rows, rows)
        a = a_ref[pl.ds(first, rows), :]

        @pl.loop(0, tiles)
        def _(t):
            into = pl.ds(pl.multiple_of(t * tile, tile), tile)
            cols = pl.ds(pl.multiple_of(part * width + t * tile, tile), tile)
            use(dot_t(a, b_ref[cols, :]) if transposed else dot(a, b_ref[:, cols]), into)

    def core_copy(slot):
        return remote(
            core_out.at[slot],
            core_in.at[slot],
            core_sems.at[0, slot],
            core_sems.at[1, slot],
            here.sibling(),
        )

    def pair_copy(slot):
        return remote(
            pair_out.at[slot],
            pair_in.at[slot],
            pair_sems.at[0, slot],
            pair_sems.at[1, slot],
            here.across(),
        )

    def up_copy(slot, into):
        return remote(
            line_out.at[slot], up_in.at[into], line_sems.at[slot], up_sems.at[into], here.above()
        )

    def down_copy(slot, into):
        return remote(
            line_out.at[slot], down_in.at[into], line_sems.at[slot], down_sems.at[into], here.below()
        )

    def for_sibling(step, pair, slot):
        def use(value, cols):
            core_out[slot, :, cols] = value.astype(BF16)

        product(target(step // parts), pair, 1 - here.core, step % parts, use)
        core_copy(slot).start()

    for_sibling(0, 1 - here.pair, 0)

    @pl.loop(0, steps)
    def _(step):
        pl.when(step < steps - 1)(lambda: for_sibling(step + 1, 1 - here.pair, step + 1))
        core_copy(step).wait_recv()

        def use(value, cols):
            pair_out[step, :, cols] = (value + core_in[step, :, cols].astype(F32)).astype(BF16)

        product(target(step // parts), 1 - here.pair, here.core, step % parts, use)
        pair_copy(step).start()

    for_sibling(0, here.pair, steps)

    @pl.loop(0, steps)
    def _(step):
        pl.when(step < steps - 1)(lambda: for_sibling(step + 1, here.pair, steps + step + 1))
        core_copy(steps + step).wait_recv()
        line = target(step // parts)
        part = step % parts
        into = line * parts + part

        def use(value, cols):
            held[:, cols] = value + core_in[steps + step, :, cols].astype(F32)

        product(line, here.pair, here.core, part, use)
        pair_copy(step).wait_recv()
        from_above = (line <= here.line) & (here.line < length - 1)
        from_below = (line >= here.line) & (here.line > 0)
        held[...] += pair_in[step].astype(F32)

        @pl.when(from_above)
        def _():
            down_copy(0, into).wait_recv()
            held[...] += down_in[into].astype(F32)

        @pl.when(from_below)
        def _():
            up_copy(0, into).wait_recv()
            held[...] += up_in[into].astype(F32)

        @pl.when(line == here.line)
        def _():
            out_ref[:, pl.ds(pl.multiple_of(part * width, width), width)] = held[...]

        @pl.when(line < here.line)
        def _():
            line_out[step] = held[...].astype(BF16)
            down_copy(step, into).start()

        @pl.when(line > here.line)
        def _():
            line_out[step] = held[...].astype(BF16)
            up_copy(step, into).start()

    @pl.loop(0, steps)
    def _(step):
        core_copy(step).wait_send()
        core_copy(steps + step).wait_send()
        pair_copy(step).wait_send()
        line = target(step // parts)
        pl.when(line < here.line)(lambda: down_copy(step, 0).wait_send())
        pl.when(line > here.line)(lambda: up_copy(step, 0).wait_send())


def product_scatter(a, b, transposed, call_id, parts=2):
    seq = lax.axis_size("seq")
    steps = seq // 4 * parts
    rows = a.shape[0] // seq
    width = b.shape[0] if transposed else b.shape[1]
    block = (rows, width // parts)
    vmem = pl.BlockSpec(memory_space=pltpu.VMEM)
    return pl.pallas_call(
        functools.partial(scatter_kernel, transposed, parts, min(width // parts, 512)),
        out_shape=jax.ShapeDtypeStruct((rows, width), F32),
        in_specs=[vmem, vmem],
        out_specs=vmem,
        scratch_shapes=[
            pltpu.VMEM((2 * steps, *block), BF16),
            pltpu.VMEM((2 * steps, *block), BF16),
            pltpu.VMEM((steps, *block), BF16),
            pltpu.VMEM((steps, *block), BF16),
            pltpu.VMEM((steps, *block), BF16),
            pltpu.VMEM((steps, *block), BF16),
            pltpu.VMEM((steps, *block), BF16),
            pltpu.VMEM(block, F32),
            pltpu.SemaphoreType.DMA((2, 2 * steps)),
            pltpu.SemaphoreType.DMA((2, steps)),
            pltpu.SemaphoreType.DMA((steps,)),
            pltpu.SemaphoreType.DMA((steps,)),
            pltpu.SemaphoreType.DMA((steps,)),
        ],
        compiler_params=pltpu.CompilerParams(
            collective_id=call_id, has_side_effects=True, vmem_limit_bytes=48 << 20
        ),
        cost_estimate=pl.CostEstimate(
            flops=2 * a.shape[0] * a.shape[1] * width,
            bytes_accessed=4 * a.shape[0] * width,
            transcendentals=0,
        ),
    )(a, b)

def gather_units(here, own_ref, buf, send_sems, recv_sems, compute):
    length = here.length
    last = length - 1
    steps = 2 * length
    half = own_ref.shape[0] // 2
    mine = here.index(here.line, here.pair, here.core)
    shorter = jnp.minimum(here.line, last - here.line)
    longer = jnp.where(here.line < last - here.line, 1, -1)

    def column(j):
        i = j - 1
        paired = jnp.where(i % 2 == 0, here.line - i // 2 - 1, here.line + i // 2 + 1)
        single = here.line + longer * (i - shorter + 1)
        return jnp.where(j == 0, here.line, jnp.where(i < 2 * shorter, paired, single))

    def copy(way, device, block, part):
        ref = buf.at[block, part]
        return remote(
            ref, ref, send_sems.at[way, block, part], recv_sems.at[block, part], device
        )

    def up(block, part):
        return copy(0, here.above(), block, part)

    def down(block, part):
        return copy(1, here.below(), block, part)

    def across(block, part):
        return copy(2, here.across(), block, part)

    def sideways(block, part):
        return copy(3, here.sibling(), block, part)

    for part in range(2):
        buf[mine, part] = own_ref[pl.ds(part * half, half), :]
        pl.when(here.line < last)(lambda part=part: up(mine, part).start())
        pl.when(here.line > 0)(lambda part=part: down(mine, part).start())
        across(mine, part).start()
        sideways(mine, part).start()

    @pl.loop(0, steps)
    def _(step):
        part = step % 2
        far = step // 2 + 1

        @pl.when(here.line >= far)
        def _():
            block = here.index(here.line - far, here.pair, here.core)
            up(block, part).wait_recv()
            pl.when(here.line < last)(lambda: up(block, part).start())
            sideways(block, part).start()

        @pl.when(here.line + far <= last)
        def _():
            block = here.index(here.line + far, here.pair, here.core)
            down(block, part).wait_recv()
            pl.when(here.line > 0)(lambda: down(block, part).start())
            sideways(block, part).start()

        @pl.when(step + 2 < steps)
        def _():
            across(here.index(column(step // 2 + 1), here.pair, here.core), part).start()

        block = here.index(column(step // 2), 1 - here.pair, here.core)
        across(block, part).wait_recv()
        sideways(block, part).start()

        in_column = (step % 2 == 1) & (step < steps - 1) | (step == 0)
        order = jnp.where(in_column, (step + 1) // 2, jnp.where(step == steps - 1, last, step // 2 - 1))
        line = column(order)
        pair = jnp.where(in_column, here.pair, 1 - here.pair)
        other = here.index(line, pair, 1 - here.core)
        sideways(other, 0).wait_recv()
        sideways(other, 1).wait_recv()
        compute(step, here.index(line, pair, 0))

    @pl.loop(0, length)
    def _(line):
        for part in range(2):
            block = here.index(line, here.pair, here.core)

            @pl.when((line <= here.line) & (here.line < last))
            def _():
                up(block, part).wait_send()

            @pl.when((line >= here.line) & (here.line > 0))
            def _():
                down(block, part).wait_send()

            across(block, part).wait_send()
            sideways(block, part).wait_send()
            sideways(here.index(line, 1 - here.pair, here.core), part).wait_send()


def gather_scratch(seq, rows, width):
    return [
        pltpu.VMEM((seq, 2, rows // 2, width), BF16),
        pltpu.SemaphoreType.DMA((4, seq, 2)),
        pltpu.SemaphoreType.DMA((seq, 2)),
    ]


def unit_rows(first, rows):
    return pl.ds(pl.multiple_of(first * rows, 2 * rows), 2 * rows)


def take_unit(buf, first):
    blocks = buf[pl.ds(first, 2)]
    return blocks.reshape(-1, blocks.shape[-1])


def rotated(values, cosine, sine):
    cols = values.shape[1]
    lane = lax.broadcasted_iota(jnp.int32, values.shape, 1)
    ahead = pltpu.roll(values, cols - HEAD_DIM // 2, 1)
    behind = pltpu.roll(values, HEAD_DIM // 2, 1)
    swapped = jnp.where(lane % HEAD_DIM < HEAD_DIM // 2, ahead, behind)
    return values * cosine + swapped * sine


def project_kernel(
    own_ref,
    gain_ref,
    weight_ref,
    cos_ref,
    sin_ref,
    normed_ref,
    q_ref,
    k_ref,
    v_ref,
    buf,
    send_sems,
    recv_sems,
    held,
    held_sems,
):
    here = Place()
    here.greet()
    rows = own_ref.shape[0]
    cols = q_ref.shape[1]
    chunk = min(32, rows // 2)

    def store(step, first):
        slot = step % 2
        return pltpu.make_async_copy(
            held.at[slot], normed_ref.at[unit_rows(first, rows)], held_sems.at[slot]
        )

    def compute(step, first):
        slot = step % 2
        pl.when(step >= 2)(lambda: store(step, first).wait())

        @pl.loop(0, 2 * rows // chunk)
        def _(i):
            at = i * chunk
            block = lax.div(at, rows)
            part = lax.div(at % rows, rows // 2)
            values = buf[first + block, part, pl.ds(at % (rows // 2), chunk), :].astype(F32)
            factor = lax.rsqrt(jnp.mean(values * values, axis=1, keepdims=True) + EPS)
            held[slot, pl.ds(at, chunk), :] = (values * factor * gain_ref[...]).astype(BF16)

        store(step, first).start()
        qkv = dot(held[slot], weight_ref[...])
        where = unit_rows(first, rows)
        cosine = cos_ref[where, :]
        sine = sin_ref[where, :]
        scale = BF16(1.0 / 8.0)
        q_ref[where, :] = rotated(qkv[:, :cols], cosine, sine).astype(BF16) * scale
        k_ref[where, :] = rotated(qkv[:, cols : 2 * cols], cosine, sine).astype(BF16)
        v_ref[where, :] = qkv[:, 2 * cols :].astype(BF16)

    gather_units(here, own_ref, buf, send_sems, recv_sems, compute)
    store(0, 0).wait()
    store(1, 0).wait()


def gather_project(own, gain, weight, cosine, sine, call_id):
    seq = lax.axis_size("seq")
    rows, width = own.shape
    cols = cosine.shape[1]
    vmem = pl.BlockSpec(memory_space=pltpu.VMEM)
    head = jax.ShapeDtypeStruct((seq * rows, cols), BF16)
    return pl.pallas_call(
        project_kernel,
        out_shape=[jax.ShapeDtypeStruct((seq * rows, width), BF16), head, head, head],
        in_specs=[vmem] * 5,
        out_specs=[pl.BlockSpec(memory_space=pl.ANY), vmem, vmem, vmem],
        scratch_shapes=gather_scratch(seq, rows, width)
        + [pltpu.VMEM((2, 2 * rows, width), BF16), pltpu.SemaphoreType.DMA((2,))],
        compiler_params=pltpu.CompilerParams(
            collective_id=call_id, has_side_effects=True, vmem_limit_bytes=48 << 20
        ),
        cost_estimate=pl.CostEstimate(
            flops=2 * seq * rows * width * weight.shape[1],
            bytes_accessed=4 * seq * rows * width,
            transcendentals=0,
        ),
    )(own, gain, weight, cosine, sine)


def feed_kernel(
    own_ref,
    grad_ref,
    feed_ref,
    down_ref,
    normed_ref,
    hidden_ref,
    back_ref,
    buf,
    send_sems,
    recv_sems,
    out_sems,
):
    here = Place()
    here.greet()
    rows = own_ref.shape[0]
    hidden = hidden_ref.shape[1]
    tile = 256

    def store(first, block, part, step):
        begin = (first + block) * rows + part * (rows // 2)
        return pltpu.make_async_copy(
            buf.at[first + block, part],
            normed_ref.at[pl.ds(pl.multiple_of(begin, rows // 2), rows // 2)],
            out_sems.at[step, block, part],
        )

    def stores(first, step):
        return [store(first, block, part, step) for block in range(2) for part in range(2)]

    def compute(step, first):
        for one in stores(first, step):
            one.start()
        where = unit_rows(first, rows)
        normed = take_unit(buf, first)
        grad = grad_ref[where, :]

        @pl.loop(0, hidden // tile)
        def _(t):
            cols = pl.ds(pl.multiple_of(t * tile, tile), tile)
            later = pl.ds(pl.multiple_of(hidden + t * tile, tile), tile)
            gate = dot(normed, feed_ref[:, cols])
            upward = dot(normed, feed_ref[:, later])
            hidden_grad = dot_t(grad, down_ref[cols, :])
            sigmoid = jax.nn.sigmoid(gate)
            silu = gate * sigmoid
            hidden_ref[where, cols] = (silu * upward).astype(BF16)
            back_ref[where, cols] = (
                hidden_grad * upward * sigmoid * (1.0 + gate * (1.0 - sigmoid))
            ).astype(BF16)
            back_ref[where, later] = (hidden_grad * silu).astype(BF16)

    gather_units(here, own_ref, buf, send_sems, recv_sems, compute)

    @pl.loop(0, 2 * here.length)
    def _(step):
        for one in stores(0, step):
            one.wait()


def gather_feed(own, grad_out, feed_weight, down_weight, call_id):
    seq = lax.axis_size("seq")
    rows, width = own.shape
    hidden = down_weight.shape[0]
    vmem = pl.BlockSpec(memory_space=pltpu.VMEM)
    return pl.pallas_call(
        feed_kernel,
        out_shape=[
            jax.ShapeDtypeStruct((seq * rows, width), BF16),
            jax.ShapeDtypeStruct((seq * rows, hidden), BF16),
            jax.ShapeDtypeStruct((seq * rows, 2 * hidden), BF16),
        ],
        in_specs=[vmem] * 4,
        out_specs=[pl.BlockSpec(memory_space=pl.ANY), vmem, vmem],
        scratch_shapes=gather_scratch(seq, rows, width)
        + [pltpu.SemaphoreType.DMA((seq // 2, 2, 2))],
        compiler_params=pltpu.CompilerParams(
            collective_id=call_id, has_side_effects=True, vmem_limit_bytes=56 << 20
        ),
        cost_estimate=pl.CostEstimate(
            flops=6 * seq * rows * width * hidden,
            bytes_accessed=6 * seq * rows * width,
            transcendentals=0,
        ),
    )(own, grad_out, feed_weight, down_weight)


def back_kernel(
    own_ref, weight_ref, attended_ref, grad_ref, part_ref, buf, send_sems, recv_sems
):
    here = Place()
    here.greet()
    rows = own_ref.shape[0]
    width = own_ref.shape[1]
    tile = 512
    part_ref[...] = jnp.zeros_like(part_ref)

    def compute(step, first):
        where = unit_rows(first, rows)
        unit = take_unit(buf, first)
        grad_ref[where, :] = dot_t(unit, weight_ref[...]).astype(BF16)
        attended = attended_ref[where, :]
        for t in range(width // tile):
            cols = slice(t * tile, (t + 1) * tile)
            part_ref[:, cols] += t_dot(attended, unit[:, cols])

    gather_units(here, own_ref, buf, send_sems, recv_sems, compute)


def gather_back(own, weight, attended, call_id):
    seq = lax.axis_size("seq")
    rows, width = own.shape
    cols = weight.shape[0]
    vmem = pl.BlockSpec(memory_space=pltpu.VMEM)
    return pl.pallas_call(
        back_kernel,
        out_shape=[
            jax.ShapeDtypeStruct((seq * rows, cols), BF16),
            jax.ShapeDtypeStruct((cols, width), F32),
        ],
        in_specs=[vmem] * 3,
        out_specs=[vmem] * 2,
        scratch_shapes=gather_scratch(seq, rows, width),
        compiler_params=pltpu.CompilerParams(
            collective_id=call_id, has_side_effects=True, vmem_limit_bytes=40 << 20
        ),
        cost_estimate=pl.CostEstimate(
            flops=4 * seq * rows * width * cols,
            bytes_accessed=4 * seq * rows * width,
            transcendentals=0,
        ),
    )(own, weight, attended)


def swap_dp(values):
    count = lax.axis_size("dp")
    return lax.ppermute(values, "dp", [(i, (i + 1) % count) for i in range(count)])


def gather_dp(values):
    return lax.all_gather(values, "dp", axis=0, tiled=True)


def sum_dp(partial):
    half = partial.shape[0] // 2
    mine = lax.axis_index("dp")
    away = lax.dynamic_slice_in_dim(partial, (1 - mine) * half, half, 0).astype(BF16)
    kept = lax.dynamic_slice_in_dim(partial, mine * half, half, 0)
    return kept + swap_dp(away).astype(F32)


def gather_rows(values):
    return lax.all_gather(values, "seq", axis=0, tiled=True)


def scatter_rows(partial):
    return lax.psum_scatter(partial.astype(BF16), "seq", scatter_dimension=0, tiled=True).astype(F32)


def exchange(blocks):
    return lax.all_to_all(blocks, "seq", split_axis=0, concat_axis=0, tiled=True)


def norm_factor(values):
    return lax.rsqrt(jnp.mean(values * values, axis=-1, keepdims=True) + EPS)


def norm_back(inputs, factor, gain_row, upstream):
    scaled_up = gain_row * upstream
    inner_mean = jnp.mean(scaled_up * inputs, axis=-1, keepdims=True)
    grad_in = factor * scaled_up - inputs * factor * factor * factor * inner_mean
    grad_gain = jnp.sum(upstream * inputs * factor, axis=0)
    return grad_in, grad_gain


def shards(
    tokens,
    cotangent,
    doc_lengths,
    attn_gain,
    mlp_gain,
    query_weight,
    key_weight,
    value_weight,
    output_weight,
    gate_weight,
    up_weight,
    down_weight,
):
    dp = lax.axis_size("dp")
    seq = lax.axis_size("seq")
    mine = lax.axis_index("seq")
    tok_count, width = tokens.shape
    rows = tok_count * seq
    slab = query_weight.shape[0]
    share = HEAD_DIM // slab
    half_heads = HEADS // dp
    half_kv = KV_HEADS // dp
    hidden_dev = down_weight.shape[0]
    block = 512
    in_kernels = seq % 4 == 0 and 2 * rows * width <= 16 << 20

    doc_ends = jnp.cumsum(doc_lengths[0])
    place = jnp.arange(rows, dtype=jnp.int32)
    passed = doc_ends[None, :] <= place[:, None]
    opening = jnp.max(jnp.where(passed, doc_ends[None, :], 0), axis=1)
    position = place - opening
    keeping = place < doc_ends[DOCS - 1]
    angles = position.astype(F32)[:, None] * rotary_table(HEAD_DIM)[None, :]
    cosine = jnp.cos(angles)
    sine = jnp.sin(angles)
    cos_heads = jnp.tile(cosine, (1, 2 * dp))
    sin_heads = jnp.tile(jnp.concatenate([-sine, sine], axis=1), (1, dp))
    own_keeping = lax.dynamic_slice_in_dim(keeping, mine * tok_count, tok_count, 0)

    def head_columns(weight, kept):
        split = weight.reshape(slab, dp, kept, HEAD_DIM)
        return jnp.repeat(split, seq // kept, axis=2)

    qkv_blocks = jnp.stack(
        [
            head_columns(query_weight, half_heads),
            head_columns(key_weight, half_kv),
            head_columns(value_weight, half_kv),
        ],
        axis=1,
    )
    qkv_blocks = jnp.transpose(qkv_blocks, (3, 0, 1, 2, 4)).reshape(seq * slab, 3 * dp * HEAD_DIM)
    qkv_weight = gather_dp(exchange(qkv_blocks))
    feed_blocks = jnp.stack(
        [w.reshape(slab, dp, seq, hidden_dev) for w in (gate_weight, up_weight)], axis=1
    )
    feed_blocks = jnp.transpose(feed_blocks, (3, 0, 1, 2, 4)).reshape(
        seq * slab, 2 * dp * hidden_dev
    )
    feed_weight = gather_dp(exchange(feed_blocks))
    down_own = gather_dp(down_weight)
    output_own = output_weight
    if share > 1:
        groups = [list(range(i, i + share)) for i in range(0, seq, share)]
        output_own = lax.all_gather(
            output_own, "seq", axis=0, tiled=True, axis_index_groups=groups
        )
    output_own = gather_dp(output_own)
    gains = lax.all_gather(
        jnp.stack([attn_gain, mlp_gain]), ("dp", "seq"), axis=1, tiled=True
    ).astype(F32)
    gain_one, gain_two = gains[0], gains[1]

    scale = 1.0 / math.sqrt(HEAD_DIM)
    head_cols = dp * HEAD_DIM
    if in_kernels:
        normed_one, queries, keys, values = gather_project(
            tokens, gain_one[None, :], qkv_weight, cos_heads, sin_heads, 0
        )
    else:
        inputs_all = gather_rows(tokens).astype(F32)
        normed_one = (inputs_all * norm_factor(inputs_all) * gain_one).astype(BF16)
        qkv = dot(normed_one, qkv_weight)
        query_lin, key_lin = qkv[:, :head_cols], qkv[:, head_cols : 2 * head_cols]
        values = qkv[:, 2 * head_cols :].astype(BF16)
        queries = query_lin * cos_heads + swap_halves(query_lin) * sin_heads
        queries = queries.astype(BF16) * BF16(scale)
        keys = (key_lin * cos_heads + swap_halves(key_lin) * sin_heads).astype(BF16)
    attended_sum, log_total = attention(queries, keys, values, opening[:, None], block)
    if share > 1:
        own_rows = ((place // tok_count) % share == mine % share)[:, None]
        attended_sum = jnp.where(own_rows, attended_sum, 0.0)
    attended = attended_sum.astype(BF16)
    inputs = tokens.astype(F32)
    if in_kernels:
        middle = inputs + product_scatter(attended, output_own, False, 1)
    else:
        middle = inputs + scatter_rows(dot(attended, output_own))

    factor_two = norm_factor(middle)
    normed_own = (middle * factor_two * gain_two).astype(BF16)
    grad_own = jnp.where(own_keeping[:, None], cotangent, BF16(0))
    grad_out = gather_rows(grad_own)
    if in_kernels:
        normed_two, hidden, feed_back = gather_feed(
            normed_own, grad_out, feed_weight, down_own, 2
        )
        normed_two_grad = product_scatter(feed_back, feed_weight.T, False, 3)
    else:
        normed_two = gather_rows(normed_own)
        feed = dot(normed_two, feed_weight)
        feed_cols = dp * hidden_dev
        gate_lin, upward = feed[:, :feed_cols], feed[:, feed_cols:]
        sigmoid = jax.nn.sigmoid(gate_lin)
        hidden = (gate_lin * sigmoid * upward).astype(BF16)
        hidden_grad = dot_t(grad_out, down_own)
        gate_back = hidden_grad * upward * sigmoid * (1.0 + gate_lin * (1.0 - sigmoid))
        up_back = hidden_grad * gate_lin * sigmoid
        feed_back = jnp.concatenate([gate_back, up_back], axis=1).astype(BF16)
        normed_two_grad = scatter_rows(dot_t(feed_back, feed_weight))
    mixed = middle + scatter_rows(dot(hidden, down_own))
    middle_in, gain_two_part = norm_back(middle, factor_two, gain_two, normed_two_grad)
    middle_grad = grad_own.astype(F32) + middle_in
    if in_kernels:
        attended_grad, output_part = gather_back(
            middle_grad.astype(BF16), output_own, attended, 4
        )
    else:
        middle_back = gather_rows(middle_grad.astype(BF16))
        attended_grad = dot_t(middle_back, output_own).astype(BF16)
        output_part = t_dot(attended, middle_back)
    if share > 1:
        attended_grad = jnp.where(own_rows, attended_grad, BF16(0))
    query_acc, key_acc, value_acc = attention_back(
        queries, keys, values, attended_grad, attended_sum, log_total, opening[:, None], block
    )
    query_acc = query_acc * scale
    query_back = query_acc * cos_heads - swap_halves(query_acc) * sin_heads
    key_back = key_acc * cos_heads - swap_halves(key_acc) * sin_heads
    qkv_back = jnp.concatenate([query_back, key_back, value_acc], axis=1).astype(BF16)
    if in_kernels:
        normed_one_grad = product_scatter(qkv_back, qkv_weight, True, 5)
    else:
        normed_one_grad = scatter_rows(dot_t(qkv_back, qkv_weight))
    input_in, gain_one_part = norm_back(inputs, norm_factor(inputs), gain_one, normed_one_grad)
    token_grad = middle_grad + input_in

    feed_grad = exchange(sum_dp(t_dot(normed_two, feed_back)).astype(BF16)).astype(F32)
    feed_grad = feed_grad.reshape(seq, slab, 2, dp, hidden_dev)
    feed_grad = jnp.transpose(feed_grad, (2, 1, 3, 0, 4)).reshape(2, slab, dp * seq * hidden_dev)
    down_grad = sum_dp(t_dot(hidden, grad_out))
    if share > 1:
        split = output_part.reshape(dp, share, slab, width)
        split = jnp.transpose(split, (1, 0, 2, 3)).reshape(share * dp * slab, width)
        output_part = lax.psum_scatter(
            split, "seq", scatter_dimension=0, tiled=True, axis_index_groups=groups
        )
    output_grad = sum_dp(output_part)
    qkv_grad = exchange(sum_dp(t_dot(normed_one, qkv_back)).astype(BF16)).astype(F32)
    qkv_grad = qkv_grad.reshape(seq, slab, 3, dp, HEAD_DIM)

    def own_columns(part, kept):
        summed = jnp.sum(part.reshape(kept, seq // kept, slab, dp, HEAD_DIM), axis=1)
        return jnp.transpose(summed, (1, 2, 0, 3)).reshape(slab, dp * kept * HEAD_DIM)

    query_grad = own_columns(qkv_grad[:, :, 0], half_heads)
    key_grad = own_columns(qkv_grad[:, :, 1], half_kv)
    value_grad = own_columns(qkv_grad[:, :, 2], half_kv)
    gain_parts = lax.psum(jnp.stack([gain_one_part, gain_two_part]), ("dp", "seq"))
    own = lax.axis_index("dp") * seq + mine
    gain_grads = lax.dynamic_slice_in_dim(gain_parts, own * slab, slab, 1)
    return (
        mixed,
        token_grad,
        gain_grads[0],
        gain_grads[1],
        query_grad,
        key_grad,
        value_grad,
        output_grad,
        feed_grad[0],
        feed_grad[1],
        down_grad,
    )


def solution(mesh):
    both = P(("dp", "seq"), None)
    line = P(("dp", "seq"))
    return jax.shard_map(
        shards,
        mesh=mesh,
        in_specs=(both, both, P("dp", None), line, line) + (both,) * 7,
        out_specs=(both, both, line, line) + (both,) * 7,
        check_vma=False,
    )
```

```python
import functools
import math

import jax
import jax.numpy as jnp
from jax import lax
from jax.experimental import pallas as pl
from jax.experimental.pallas import tpu as pltpu
from jax.sharding import PartitionSpec as P

HEADS = 32
KV_HEADS = 8
HEAD_DIM = 64
DOCS = 4
EPS = 1e-05
NEG = -1e30
MESH = pl.DeviceIdType.MESH
F32 = jnp.float32
BF16 = jnp.bfloat16


def rotary_table(head_dim):
    exponent = jnp.arange(0, head_dim, 2, dtype=F32) / head_dim
    inverse = jnp.power(F32(500000.0), -exponent)
    wavelength = 2.0 * math.pi / inverse
    smooth = (8192.0 / wavelength - 1.0) / 3.0
    blended = (1.0 - smooth) * inverse / 32.0 + smooth * inverse
    return jnp.where(
        wavelength < 2048.0, inverse, jnp.where(wavelength > 8192.0, inverse / 32.0, blended)
    )


def swap_halves(values):
    rows, cols = values.shape
    halves = values.reshape(rows, cols // HEAD_DIM, 2, HEAD_DIM // 2)
    return halves[:, :, ::-1].reshape(rows, cols)


def dot(a, b):
    return jnp.dot(a, b, preferred_element_type=F32)


def dot_t(a, b):
    return lax.dot_general(a, b, (((1,), (1,)), ((), ())), preferred_element_type=F32)


def t_dot(a, b):
    return lax.dot_general(a, b, (((0,), (0,)), ((), ())), preferred_element_type=F32)


def allowed_tile(opening, q_first, k_first, shape):
    rows = q_first + lax.broadcasted_iota(jnp.int32, shape, 0)
    cols = k_first + lax.broadcasted_iota(jnp.int32, shape, 1)
    return (cols <= rows) & (cols >= opening)


def attention_kernel(block, q_ref, k_ref, v_ref, open_ref, out_ref, lse_ref):
    tile = pl.program_id(0)
    opening = open_ref[...]
    for head in range(q_ref.shape[1] // HEAD_DIM):
        lanes = slice(head * HEAD_DIM, (head + 1) * HEAD_DIM)
        query = q_ref[:, lanes]

        def step(j, carry, lanes=lanes, query=query):
            peak, total, acc = carry
            first = pl.multiple_of(j * block, block)
            scores = dot_t(query, k_ref[pl.ds(first, block), lanes])
            allowed = allowed_tile(opening, tile * block, first, scores.shape)
            scores = jnp.where(allowed, scores, NEG)
            new_peak = jnp.maximum(peak, jnp.max(scores, axis=1, keepdims=True))
            spread = jnp.where(allowed, jnp.exp(scores - new_peak), 0.0)
            fade = jnp.exp(peak - new_peak)
            total = total * fade + jnp.sum(spread, axis=1, keepdims=True)
            acc = acc * fade + dot(spread.astype(BF16), v_ref[pl.ds(first, block), lanes])
            return new_peak, total, acc

        peak, total, acc = lax.fori_loop(
            0,
            tile + 1,
            step,
            (
                jnp.full((block, 1), NEG, F32),
                jnp.zeros((block, 1), F32),
                jnp.zeros((block, HEAD_DIM), F32),
            ),
        )
        out_ref[:, lanes] = acc / total
        lse_ref[:, head : head + 1] = peak + jnp.log(total)


def attention(queries, keys, values, opening, block):
    rows, cols = queries.shape
    heads = cols // HEAD_DIM
    tiled = lambda width: pl.BlockSpec((block, width), lambda i: (i, 0))
    whole = pl.BlockSpec((rows, cols), lambda i: (0, 0))
    return pl.pallas_call(
        functools.partial(attention_kernel, block),
        grid=(rows // block,),
        in_specs=[tiled(cols), whole, whole, tiled(1)],
        out_specs=[tiled(cols), tiled(heads)],
        out_shape=[
            jax.ShapeDtypeStruct((rows, cols), F32),
            jax.ShapeDtypeStruct((rows, heads), F32),
        ],
        compiler_params=pltpu.CompilerParams(vmem_limit_bytes=48 << 20),
        cost_estimate=pl.CostEstimate(
            flops=2 * rows * rows * cols, bytes_accessed=10 * rows * cols, transcendentals=0
        ),
    )(queries, keys, values, opening)


def attention_back_kernel(
    block, q_ref, k_ref, v_ref, g_ref, att_ref, lse_ref, open_ref, dq_ref, dk_ref, dv_ref
):
    tile = pl.program_id(0)

    @pl.when(tile == 0)
    def _():
        dk_ref[...] = jnp.zeros_like(dk_ref)
        dv_ref[...] = jnp.zeros_like(dv_ref)

    opening = open_ref[...]
    for head in range(q_ref.shape[1] // HEAD_DIM):
        lanes = slice(head * HEAD_DIM, (head + 1) * HEAD_DIM)
        query = q_ref[:, lanes]
        grad = g_ref[:, lanes]
        log_total = lse_ref[:, head : head + 1]
        row_sum = jnp.sum(grad.astype(F32) * att_ref[:, lanes], axis=1, keepdims=True)

        def step(j, acc, lanes=lanes, query=query, grad=grad, log_total=log_total, row_sum=row_sum):
            first = pl.multiple_of(j * block, block)
            here = pl.ds(first, block)
            key = k_ref[here, lanes]
            scores = dot_t(query, key)
            allowed = allowed_tile(opening, tile * block, first, scores.shape)
            chance = jnp.where(allowed, jnp.exp(scores - log_total), 0.0)
            prob_grad = dot_t(grad, v_ref[here, lanes])
            score_grad = (chance * (prob_grad - row_sum)).astype(BF16)
            dk_ref[here, lanes] += t_dot(score_grad, query)
            dv_ref[here, lanes] += t_dot(chance.astype(BF16), grad)
            return acc + dot(score_grad, key)

        acc = lax.fori_loop(0, tile + 1, step, jnp.zeros((block, HEAD_DIM), F32))
        dq_ref[:, lanes] = acc


def attention_back(queries, keys, values, grads, attended, log_total, opening, block):
    rows, cols = queries.shape
    heads = cols // HEAD_DIM
    tiled = lambda width: pl.BlockSpec((block, width), lambda i: (i, 0))
    whole = pl.BlockSpec((rows, cols), lambda i: (0, 0))
    return pl.pallas_call(
        functools.partial(attention_back_kernel, block),
        grid=(rows // block,),
        in_specs=[tiled(cols), whole, whole, tiled(cols), tiled(cols), tiled(heads), tiled(1)],
        out_specs=[tiled(cols), whole, whole],
        out_shape=[jax.ShapeDtypeStruct((rows, cols), F32)] * 3,
        compiler_params=pltpu.CompilerParams(vmem_limit_bytes=60 << 20),
        cost_estimate=pl.CostEstimate(
            flops=5 * rows * rows * cols, bytes_accessed=20 * rows * cols, transcendentals=0
        ),
    )(queries, keys, values, grads, attended, log_total, opening)


class Place:
    def __init__(self):
        self.dp = lax.axis_index("dp")
        self.mine = lax.axis_index("seq")
        self.count = lax.axis_size("seq")
        self.length = self.count // 4
        self.line = lax.div(self.mine, 4)
        self.pair = lax.rem(lax.div(self.mine, 2), 2)
        self.core = lax.rem(self.mine, 2)
        self.slot = self.line * 2 + self.core

    def index(self, line, pair, core):
        return (line * 2 + pair) * 2 + core

    def peer(self, slot, same):
        pair = self.pair if same else 1 - self.pair
        return self.index(lax.div(slot, 2), pair, lax.rem(slot, 2))

    def device(self, line, pair, core):
        return (self.dp, self.index(line, pair, core))

    def sibling(self):
        return self.device(self.line, self.pair, 1 - self.core)

    def across(self):
        return self.device(self.line, 1 - self.pair, self.core)

    def above(self):
        return self.device(self.line + 1, self.pair, self.core)

    def below(self):
        return self.device(self.line - 1, self.pair, self.core)

    def partner(self):
        return (1 - self.dp, self.mine)

    def greet(self, partner=False):
        barrier = pltpu.get_barrier_semaphore()

        def signal(device):
            pl.semaphore_signal(barrier, inc=1, device_id=device, device_id_type=MESH)

        signal(self.sibling())
        signal(self.across())
        pl.when(self.line > 0)(lambda: signal(self.below()))
        pl.when(self.line < self.length - 1)(lambda: signal(self.above()))
        if partner:
            signal(self.partner())
        inner = (self.line > 0) & (self.line < self.length - 1)
        pl.semaphore_wait(barrier, jnp.where(inner, 4, 3) + (1 if partner else 0))

    def greet_all(self):
        barrier = pltpu.get_barrier_semaphore()

        def signal(device):
            pl.semaphore_signal(barrier, inc=1, device_id=device, device_id_type=MESH)

        signal(self.partner())

        @pl.loop(1, self.count)
        def _(ahead):
            signal((self.dp, lax.rem(self.mine + ahead, self.count)))

        pl.semaphore_wait(barrier, self.count)


def remote(src, dst, send_sem, recv_sem, device):
    return pltpu.make_async_remote_copy(
        src_ref=src,
        dst_ref=dst,
        send_sem=send_sem,
        recv_sem=recv_sem,
        device_id=device,
        device_id_type=MESH,
    )


class Spread:
    def __init__(self, here, same, copies):
        self.here, self.same, self.copies = here, same, copies
        self.slots = here.count // 2

    def each(self, visit):
        @pl.loop(1 if self.same else 0, self.slots)
        def _(ahead):
            slot = lax.rem(self.here.slot + ahead, self.slots)
            visit(self.here.peer(slot, self.same), slot)

    def start(self):
        def visit(peer, slot):
            for one in self.copies(peer, self.here.mine, self.here.slot, slot):
                one.start()

        self.each(visit)

    def finish(self):
        def visit(peer, slot):
            for one in self.copies(peer, peer, slot, slot):
                one.wait()

        self.each(visit)


def block_spread(here, same, blocks, into, sems):
    def copies(peer, sender, at, sem):
        return [
            remote(
                blocks.at[peer],
                into.at[at],
                sems.at[0, sem],
                sems.at[1, at],
                (here.dp, peer),
            )
        ]

    return Spread(here, same, copies)


def feed_spread(here, same, weights, into, sems):
    dp = lax.axis_size("dp")
    columns = into.shape[2] // (dp * len(weights))

    def copies(peer, sender, at, sem):
        made = []
        for kind, weight in enumerate(weights):
            for half in range(dp):
                part = kind * dp + half
                begin = pl.multiple_of((half * here.count + peer) * columns, columns)
                made.append(
                    remote(
                        weight.at[:, pl.ds(begin, columns)],
                        into.at[at, :, pl.ds(part * columns, columns)],
                        sems.at[0, sem, part],
                        sems.at[1, at, part],
                        (here.dp, peer),
                    )
                )
        return made

    return Spread(here, same, copies)


def nothing():
    pass


def gather_units(here, own_ref, buf, send_sems, recv_sems, compute, between=None, ready=0):
    length = here.length
    last = length - 1
    steps = 2 * length
    half = own_ref.shape[0] // 2
    mine = here.mine
    shorter = jnp.minimum(here.line, last - here.line)
    longer = jnp.where(here.line < last - here.line, 1, -1)

    def column(j):
        i = j - 1
        paired = jnp.where(i % 2 == 0, here.line - i // 2 - 1, here.line + i // 2 + 1)
        single = here.line + longer * (i - shorter + 1)
        return jnp.where(j == 0, here.line, jnp.where(i < 2 * shorter, paired, single))

    def copy(way, device, block, part):
        ref = buf.at[block, part]
        return remote(
            ref, ref, send_sems.at[way, block, part], recv_sems.at[block, part], device
        )

    def up(block, part):
        return copy(0, here.above(), block, part)

    def down(block, part):
        return copy(1, here.below(), block, part)

    def across(block, part):
        return copy(2, here.across(), block, part)

    def sideways(block, part):
        return copy(3, here.sibling(), block, part)

    def unit(number):
        in_column = (number % 2 == 1) & (number < steps - 1) | (number == 0)
        later = jnp.where(number == steps - 1, last, number // 2 - 1)
        line = column(jnp.where(in_column, (number + 1) // 2, later))
        pair = jnp.where(in_column, here.pair, 1 - here.pair)
        other = here.index(line, pair, 1 - here.core)
        sideways(other, 0).wait_recv()
        sideways(other, 1).wait_recv()
        compute(number, here.index(line, pair, 0))

    for part in range(2):
        buf[mine, part] = own_ref[pl.ds(part * half, half), :]
        pl.when(here.line < last)(lambda part=part: up(mine, part).start())
        pl.when(here.line > 0)(lambda part=part: down(mine, part).start())
        across(mine, part).start()
        sideways(mine, part).start()

    @pl.loop(0, steps)
    def _(step):
        part = step % 2
        far = step // 2 + 1

        @pl.when(here.line >= far)
        def _():
            block = here.index(here.line - far, here.pair, here.core)
            up(block, part).wait_recv()
            pl.when(here.line < last)(lambda: up(block, part).start())
            sideways(block, part).start()

        @pl.when(here.line + far <= last)
        def _():
            block = here.index(here.line + far, here.pair, here.core)
            down(block, part).wait_recv()
            pl.when(here.line > 0)(lambda: down(block, part).start())
            sideways(block, part).start()

        @pl.when(step + 2 < steps)
        def _():
            across(here.index(column(step // 2 + 1), here.pair, here.core), part).start()

        block = here.index(column(step // 2), 1 - here.pair, here.core)
        across(block, part).wait_recv()
        sideways(block, part).start()

        if between is None:
            unit(step)
        else:
            between(step)
            begin = jnp.where(step == ready, 0, step)
            end = jnp.where(step < ready, step, step + 1)

            @pl.loop(begin, end)
            def _(number):
                unit(number)

    @pl.loop(0, length)
    def _(line):
        for part in range(2):
            block = here.index(line, here.pair, here.core)

            @pl.when((line <= here.line) & (here.line < last))
            def _():
                up(block, part).wait_send()

            @pl.when((line >= here.line) & (here.line > 0))
            def _():
                down(block, part).wait_send()

            across(block, part).wait_send()
            sideways(block, part).wait_send()
            sideways(here.index(line, 1 - here.pair, here.core), part).wait_send()


def gather_scratch(seq, rows, width):
    return [
        pltpu.VMEM((seq, 2, rows // 2, width), BF16),
        pltpu.SemaphoreType.DMA((4, seq, 2)),
        pltpu.SemaphoreType.DMA((seq, 2)),
    ]


def unit_rows(first, rows):
    return pl.ds(pl.multiple_of(first * rows, 2 * rows), 2 * rows)


def take_unit(buf, first):
    blocks = buf[pl.ds(first, 2)]
    return blocks.reshape(-1, blocks.shape[-1])


class UnitStore:
    def __init__(self, buf, out_ref, sems):
        self.buf, self.out_ref, self.sems = buf, out_ref, sems

    def copies(self, number, first):
        half = self.buf.shape[2]
        made = []
        for block in range(2):
            for part in range(2):
                begin = ((first + block) * 2 + part) * half
                made.append(
                    pltpu.make_async_copy(
                        self.buf.at[first + block, part],
                        self.out_ref.at[pl.ds(pl.multiple_of(begin, half), half)],
                        self.sems.at[number, block, part],
                    )
                )
        return made

    def start(self, number, first):
        for one in self.copies(number, first):
            one.start()

    def finish(self):
        @pl.loop(0, self.sems.shape[0])
        def _(number):
            for one in self.copies(number, 0):
                one.wait()


def params(call_id, mebibytes):
    return pltpu.CompilerParams(
        collective_id=call_id, has_side_effects=True, vmem_limit_bytes=mebibytes << 20
    )


def cost(flops, bytes_accessed):
    return pl.CostEstimate(flops=flops, bytes_accessed=bytes_accessed, transcendentals=0)


VMEM = pl.BlockSpec(memory_space=pltpu.VMEM)
HBM = pl.BlockSpec(memory_space=pl.ANY)


def rotated(values, cosine, sine):
    cols = values.shape[1]
    lane = lax.broadcasted_iota(jnp.int32, values.shape, 1)
    ahead = pltpu.roll(values, cols - HEAD_DIM // 2, 1)
    behind = pltpu.roll(values, HEAD_DIM // 2, 1)
    swapped = jnp.where(lane % HEAD_DIM < HEAD_DIM // 2, ahead, behind)
    return values * cosine + swapped * sine


def project_kernel(
    own_ref,
    blocks_ref,
    gate_ref,
    up_ref,
    down_ref,
    output_ref,
    cos_ref,
    sin_ref,
    normed_ref,
    q_ref,
    k_ref,
    v_ref,
    weight_ref,
    feed_ref,
    down_out_ref,
    output_out_ref,
    buf,
    send_sems,
    recv_sems,
    store_sems,
    near_sems,
    far_sems,
    feed_sems,
    swap_sems,
    local_sems,
    pair_sems,
):
    here = Place()
    here.greet_all()
    cols = q_ref.shape[1]
    rows = own_ref.shape[0]
    dp = here.dp

    def weight_spread(same, sems):
        def copies(peer, sender, at, sem):
            return [
                remote(
                    blocks_ref.at[peer],
                    weight_ref.at[dp, sender],
                    sems.at[0, sem],
                    sems.at[1, at],
                    (dp, peer),
                )
            ]

        return Spread(here, same, copies)

    near = weight_spread(True, near_sems)
    far = weight_spread(False, far_sems)
    far.start()
    near.start()
    weight_ref[dp, here.mine] = blocks_ref[here.mine]
    swaps = []
    for number, (src, dst) in enumerate([(down_ref, down_out_ref), (output_ref, output_out_ref)]):
        swaps.append(
            remote(src, dst.at[dp], swap_sems.at[0, number], swap_sems.at[1, number], here.partner())
        )
        swaps.append(pltpu.make_async_copy(src, dst.at[dp], local_sems.at[number]))
    for one in swaps:
        one.start()
    feed = feed_spread(here, True, (gate_ref, up_ref), feed_ref, feed_sems)
    columns = feed_ref.shape[2] // 4
    own_feed = []
    for kind, weight in enumerate((gate_ref, up_ref)):
        for half in range(2):
            part = kind * 2 + half
            begin = pl.multiple_of((half * here.count + here.mine) * columns, columns)
            own_feed.append(
                pltpu.make_async_copy(
                    weight.at[:, pl.ds(begin, columns)],
                    feed_ref.at[here.slot, :, pl.ds(part * columns, columns)],
                    local_sems.at[2 + part],
                )
            )
    for one in own_feed:
        one.start()

    def pair_copy(source, sender):
        return remote(
            weight_ref.at[source, sender],
            weight_ref.at[source, sender],
            pair_sems.at[0, sender],
            pair_sems.at[1, sender],
            here.partner(),
        )

    def between(step):
        @pl.when(step == 0)
        def _():
            feed.start()

        @pl.when(step == 1)
        def _():
            near.finish()
            far.finish()

            @pl.loop(0, here.count)
            def _(sender):
                pair_copy(dp, sender).start()

        @pl.when(step == 3)
        def _():
            @pl.loop(0, here.count)
            def _(sender):
                pair_copy(1 - dp, sender).wait_recv()

    store = UnitStore(buf, normed_ref, store_sems)

    def compute(number, first):
        store.start(number, first)
        weight = weight_ref[...].reshape(-1, weight_ref.shape[-1])
        qkv = dot(take_unit(buf, first), weight)
        where = unit_rows(first, rows)
        cosine = cos_ref[where, :]
        sine = sin_ref[where, :]
        scale = BF16(1.0 / math.sqrt(HEAD_DIM))
        q_ref[where, :] = rotated(qkv[:, :cols], cosine, sine).astype(BF16) * scale
        k_ref[where, :] = rotated(qkv[:, cols : 2 * cols], cosine, sine).astype(BF16)
        v_ref[where, :] = qkv[:, 2 * cols :].astype(BF16)

    gather_units(here, own_ref, buf, send_sems, recv_sems, compute, between, 3)

    @pl.loop(0, here.count)
    def _(sender):
        pair_copy(dp, sender).wait_send()

    store.finish()
    feed.finish()
    for one in swaps + own_feed:
        one.wait()


def gather_project(own, blocks, gate, up, down, output, cosine, sine, call_id):
    seq = lax.axis_size("seq")
    rows, width = own.shape
    cols = cosine.shape[1]
    slab = gate.shape[0]
    head = jax.ShapeDtypeStruct((seq * rows, cols), BF16)
    feed_cols = 4 * down.shape[0]
    dma = pltpu.SemaphoreType.DMA
    return pl.pallas_call(
        project_kernel,
        out_shape=[
            jax.ShapeDtypeStruct((seq * rows, width), BF16),
            head,
            head,
            head,
            jax.ShapeDtypeStruct((2, *blocks.shape), BF16),
            jax.ShapeDtypeStruct((seq // 2, slab, feed_cols), BF16),
            jax.ShapeDtypeStruct((2, *down.shape), BF16),
            jax.ShapeDtypeStruct((2, *output.shape), BF16),
        ],
        in_specs=[VMEM, VMEM, HBM, HBM, HBM, HBM, VMEM, VMEM],
        out_specs=[HBM, VMEM, VMEM, VMEM, VMEM, HBM, HBM, HBM],
        scratch_shapes=gather_scratch(seq, rows, width)
        + [
            dma((seq // 2, 2, 2)),
            dma((2, seq // 2)),
            dma((2, seq // 2)),
            dma((2, seq // 2, 4)),
            dma((2, 2)),
            dma((6,)),
            dma((2, seq)),
        ],
        compiler_params=params(call_id, 40),
        cost_estimate=cost(2 * seq * rows * width * 3 * cols, 4 * seq * rows * width),
    )(own, blocks, gate, up, down, output, cosine, sine)


def attention_feed_kernel(
    block,
    q_ref,
    k_ref,
    v_ref,
    open_ref,
    gate_ref,
    up_ref,
    out_ref,
    lse_ref,
    feed_ref,
    feed_sems,
):
    here = Place()
    feed = feed_spread(here, False, (gate_ref, up_ref), feed_ref, feed_sems)

    @pl.when(pl.program_id(0) == 0)
    def _():
        here.greet_all()
        feed.start()

    attention_kernel(block, q_ref, k_ref, v_ref, open_ref, out_ref, lse_ref)

    @pl.when(pl.program_id(0) == pl.num_programs(0) - 1)
    def _():
        feed.finish()


def attention_feed(queries, keys, values, opening, gate, up, feed_cols, block, call_id):
    seq = lax.axis_size("seq")
    rows, cols = queries.shape
    heads = cols // HEAD_DIM
    tiled = lambda width: pl.BlockSpec((block, width), lambda i: (i, 0))
    whole = pl.BlockSpec((rows, cols), lambda i: (0, 0))
    return pl.pallas_call(
        functools.partial(attention_feed_kernel, block),
        grid=(rows // block,),
        in_specs=[tiled(cols), whole, whole, tiled(1), HBM, HBM],
        out_specs=[tiled(cols), tiled(heads), HBM],
        out_shape=[
            jax.ShapeDtypeStruct((rows, cols), F32),
            jax.ShapeDtypeStruct((rows, heads), F32),
            jax.ShapeDtypeStruct((seq // 2, gate.shape[0], feed_cols), BF16),
        ],
        scratch_shapes=[pltpu.SemaphoreType.DMA((2, seq // 2, 4))],
        compiler_params=params(call_id, 48),
        cost_estimate=cost(2 * rows * rows * cols, 10 * rows * cols),
    )(queries, keys, values, opening, gate, up)


def scatter_rows_of_product(
    here,
    transposed,
    parts,
    tile,
    a_ref,
    b_ref,
    out_ref,
    core_out,
    core_in,
    pair_out,
    pair_in,
    line_out,
    up_in,
    down_in,
    held,
    core_sems,
    pair_sems,
    line_sems,
    up_sems,
    down_sems,
    between=nothing,
    middle=nothing,
):
    length = here.length
    rows = out_ref.shape[0]
    width = out_ref.shape[1] // parts
    tiles = width // tile
    steps = length * parts

    def target(i):
        ups = length - 1 - here.line
        near = here.line < length // 2
        if_near = jnp.where(i < ups, length - 1 - i, i - ups)
        if_far = jnp.where(i < here.line, i, length - 1 - (i - here.line))
        return jnp.where(i == length - 1, here.line, jnp.where(near, if_near, if_far))

    def product(line, pair, core, part, use):
        first = pl.multiple_of(here.index(line, pair, core) * rows, rows)
        a = a_ref[pl.ds(first, rows), :]

        @pl.loop(0, tiles)
        def _(t):
            into = pl.ds(pl.multiple_of(t * tile, tile), tile)
            cols = pl.ds(pl.multiple_of(part * width + t * tile, tile), tile)
            use(dot_t(a, b_ref[cols, :]) if transposed else dot(a, b_ref[:, cols]), into)

    def core_copy(slot):
        return remote(
            core_out.at[slot],
            core_in.at[slot],
            core_sems.at[0, slot],
            core_sems.at[1, slot],
            here.sibling(),
        )

    def pair_copy(slot):
        return remote(
            pair_out.at[slot],
            pair_in.at[slot],
            pair_sems.at[0, slot],
            pair_sems.at[1, slot],
            here.across(),
        )

    def up_copy(slot, into):
        return remote(
            line_out.at[slot], up_in.at[into], line_sems.at[slot], up_sems.at[into], here.above()
        )

    def down_copy(slot, into):
        return remote(
            line_out.at[slot], down_in.at[into], line_sems.at[slot], down_sems.at[into], here.below()
        )

    def for_sibling(step, pair, slot):
        def use(value, cols):
            core_out[slot, :, cols] = value.astype(BF16)

        product(target(step // parts), pair, 1 - here.core, step % parts, use)
        core_copy(slot).start()

    for_sibling(0, 1 - here.pair, 0)

    @pl.loop(0, steps)
    def _(step):
        pl.when(step < steps - 1)(lambda: for_sibling(step + 1, 1 - here.pair, step + 1))
        core_copy(step).wait_recv()

        def use(value, cols):
            pair_out[step, :, cols] = (value + core_in[step, :, cols].astype(F32)).astype(BF16)

        product(target(step // parts), 1 - here.pair, here.core, step % parts, use)
        pair_copy(step).start()

    for_sibling(0, here.pair, steps)
    between()

    @pl.loop(0, steps)
    def _(step):
        pl.when(step < steps - 1)(lambda: for_sibling(step + 1, here.pair, steps + step + 1))
        core_copy(steps + step).wait_recv()
        line = target(step // parts)
        part = step % parts
        into = line * parts + part

        def use(value, cols):
            held[:, cols] = value + core_in[steps + step, :, cols].astype(F32)

        product(line, here.pair, here.core, part, use)
        pair_copy(step).wait_recv()
        from_above = (line <= here.line) & (here.line < length - 1)
        from_below = (line >= here.line) & (here.line > 0)
        held[...] += pair_in[step].astype(F32)

        @pl.when(from_above)
        def _():
            down_copy(0, into).wait_recv()
            held[...] += down_in[into].astype(F32)

        @pl.when(from_below)
        def _():
            up_copy(0, into).wait_recv()
            held[...] += up_in[into].astype(F32)

        @pl.when(line == here.line)
        def _():
            out_ref[:, pl.ds(pl.multiple_of(part * width, width), width)] = held[...]

        @pl.when(line < here.line)
        def _():
            line_out[step] = held[...].astype(BF16)
            down_copy(step, into).start()

        @pl.when(line > here.line)
        def _():
            line_out[step] = held[...].astype(BF16)
            up_copy(step, into).start()

        if middle is not nothing:
            pl.when(step == steps // 2)(middle)

    @pl.loop(0, steps)
    def _(step):
        core_copy(step).wait_send()
        core_copy(steps + step).wait_send()
        pair_copy(step).wait_send()
        line = target(step // parts)
        pl.when(line < here.line)(lambda: down_copy(step, 0).wait_send())
        pl.when(line > here.line)(lambda: up_copy(step, 0).wait_send())


SCATTER_PARTS = 2
SCATTER_SCRATCH = 13


def scatter_scratch(seq, rows, width):
    steps = seq // 4 * SCATTER_PARTS
    block = (rows, width // SCATTER_PARTS)
    dma = pltpu.SemaphoreType.DMA
    return [
        pltpu.VMEM((2 * steps, *block), BF16),
        pltpu.VMEM((2 * steps, *block), BF16),
        pltpu.VMEM((steps, *block), BF16),
        pltpu.VMEM((steps, *block), BF16),
        pltpu.VMEM((steps, *block), BF16),
        pltpu.VMEM((steps, *block), BF16),
        pltpu.VMEM((steps, *block), BF16),
        pltpu.VMEM(block, F32),
        dma((2, 2 * steps)),
        dma((2, steps)),
        dma((steps,)),
        dma((steps,)),
        dma((steps,)),
    ]


def scatter_tile(width):
    return min(width // SCATTER_PARTS, 512)


def scatter_cost(a, width):
    return cost(2 * a.shape[0] * a.shape[1] * width, 4 * a.shape[0] * width)


def scatter_kernel(tile, a_ref, b_ref, out_ref, *scratch):
    here = Place()
    here.greet()
    scatter_rows_of_product(here, False, SCATTER_PARTS, tile, a_ref, b_ref, out_ref, *scratch)


def product_scatter(a, b, call_id):
    seq = lax.axis_size("seq")
    rows = a.shape[0] // seq
    width = b.shape[1]
    return pl.pallas_call(
        functools.partial(scatter_kernel, scatter_tile(width)),
        out_shape=jax.ShapeDtypeStruct((rows, width), F32),
        in_specs=[VMEM, VMEM],
        out_specs=VMEM,
        scratch_shapes=scatter_scratch(seq, rows, width),
        compiler_params=params(call_id, 48),
        cost_estimate=scatter_cost(a, width),
    )(a, b)


def scatter_feed_kernel(tile, a_ref, b_ref, near_ref, far_ref, out_ref, feed_ref, *scratch):
    here = Place()
    here.greet(partner=True)
    swap_sems, local_sems = scratch[SCATTER_SCRATCH:]
    slots = near_ref.shape[0]

    def copies(half, ref, slot):
        place = feed_ref.at[here.dp, here.peer(slot, half == 0)]
        return (
            remote(
                ref.at[slot],
                place,
                swap_sems.at[0, half, slot],
                swap_sems.at[1, half, slot],
                here.partner(),
            ),
            pltpu.make_async_copy(ref.at[slot], place, local_sems.at[half, slot]),
        )

    @pl.loop(0, slots)
    def _(slot):
        for half, ref in enumerate((near_ref, far_ref)):
            for one in copies(half, ref, slot):
                one.start()

    scatter_rows_of_product(
        here, False, SCATTER_PARTS, tile, a_ref, b_ref, out_ref, *scratch[:SCATTER_SCRATCH]
    )

    @pl.loop(0, slots)
    def _(slot):
        for half, ref in enumerate((near_ref, far_ref)):
            for one in copies(half, ref, slot):
                one.wait()


def product_scatter_feed(a, b, near, far, call_id):
    seq = lax.axis_size("seq")
    rows = a.shape[0] // seq
    width = b.shape[1]
    dma = pltpu.SemaphoreType.DMA
    return pl.pallas_call(
        functools.partial(scatter_feed_kernel, scatter_tile(width)),
        out_shape=[
            jax.ShapeDtypeStruct((rows, width), F32),
            jax.ShapeDtypeStruct((2, seq, *near.shape[1:]), BF16),
        ],
        in_specs=[VMEM, VMEM, HBM, HBM],
        out_specs=[VMEM, HBM],
        scratch_shapes=scatter_scratch(seq, rows, width)
        + [dma((2, 2, seq // 2)), dma((2, seq // 2))],
        compiler_params=params(call_id, 40),
        cost_estimate=scatter_cost(a, width),
    )(a, b, near, far)


def feed_kernel(
    own_ref,
    grad_ref,
    feed_ref,
    down_ref,
    normed_ref,
    hidden_ref,
    back_ref,
    buf,
    send_sems,
    recv_sems,
    store_sems,
):
    here = Place()
    here.greet()
    rows = own_ref.shape[0]
    hidden = hidden_ref.shape[1]
    tile = 256
    store = UnitStore(buf, normed_ref, store_sems)

    def compute(number, first):
        store.start(number, first)
        where = unit_rows(first, rows)
        normed = take_unit(buf, first)
        grad = grad_ref[where, :]

        @pl.loop(0, hidden // tile)
        def _(t):
            cols = pl.ds(pl.multiple_of(t * tile, tile), tile)
            later = pl.ds(pl.multiple_of(hidden + t * tile, tile), tile)
            gate = dot(normed, feed_ref[:, cols])
            upward = dot(normed, feed_ref[:, later])
            hidden_grad = dot_t(grad, down_ref[cols, :])
            sigmoid = jax.nn.sigmoid(gate)
            silu = gate * sigmoid
            hidden_ref[where, cols] = (silu * upward).astype(BF16)
            back_ref[where, cols] = (
                hidden_grad * upward * sigmoid * (1.0 + gate * (1.0 - sigmoid))
            ).astype(BF16)
            back_ref[where, later] = (hidden_grad * silu).astype(BF16)

    gather_units(here, own_ref, buf, send_sems, recv_sems, compute)
    store.finish()


def gather_feed(own, grad_out, feed_weight, down_weight, call_id):
    seq = lax.axis_size("seq")
    rows, width = own.shape
    hidden = down_weight.shape[0]
    return pl.pallas_call(
        feed_kernel,
        out_shape=[
            jax.ShapeDtypeStruct((seq * rows, width), BF16),
            jax.ShapeDtypeStruct((seq * rows, hidden), BF16),
            jax.ShapeDtypeStruct((seq * rows, 2 * hidden), BF16),
        ],
        in_specs=[VMEM] * 4,
        out_specs=[HBM, VMEM, VMEM],
        scratch_shapes=gather_scratch(seq, rows, width)
        + [pltpu.SemaphoreType.DMA((seq // 2, 2, 2))],
        compiler_params=params(call_id, 56),
        cost_estimate=cost(6 * seq * rows * width * hidden, 6 * seq * rows * width),
    )(own, grad_out, feed_weight, down_weight)


def back_kernel(
    own_ref,
    weight_ref,
    attended_ref,
    share_ref,
    grad_ref,
    part_ref,
    came_ref,
    buf,
    send_sems,
    recv_sems,
    swap_sems,
):
    here = Place()
    here.greet(partner=True)
    rows = own_ref.shape[0]
    width = own_ref.shape[1]
    tile = 512
    swap = remote(
        share_ref.at[1 - here.dp], came_ref, swap_sems.at[0], swap_sems.at[1], here.partner()
    )
    swap.start()
    part_ref[...] = jnp.zeros_like(part_ref)

    def compute(number, first):
        where = unit_rows(first, rows)
        unit = take_unit(buf, first)
        grad_ref[where, :] = dot_t(unit, weight_ref[...]).astype(BF16)
        attended = attended_ref[where, :]
        for t in range(width // tile):
            cols = slice(t * tile, (t + 1) * tile)
            part_ref[:, cols] += t_dot(attended, unit[:, cols])

    gather_units(here, own_ref, buf, send_sems, recv_sems, compute)
    swap.wait()


def gather_back(own, weight, attended, share, call_id):
    seq = lax.axis_size("seq")
    rows, width = own.shape
    cols = weight.shape[0]
    return pl.pallas_call(
        back_kernel,
        out_shape=[
            jax.ShapeDtypeStruct((seq * rows, cols), BF16),
            jax.ShapeDtypeStruct((cols, width), F32),
            jax.ShapeDtypeStruct(share.shape[1:], BF16),
        ],
        in_specs=[VMEM] * 3 + [HBM],
        out_specs=[VMEM] * 2 + [HBM],
        scratch_shapes=gather_scratch(seq, rows, width) + [pltpu.SemaphoreType.DMA((2,))],
        compiler_params=params(call_id, 40),
        cost_estimate=cost(4 * seq * rows * width * cols, 4 * seq * rows * width),
    )(own, weight, attended, share)


def attention_back_feed_kernel(
    block,
    q_ref,
    k_ref,
    v_ref,
    g_ref,
    att_ref,
    lse_ref,
    open_ref,
    cos_ref,
    sin_ref,
    blocks_ref,
    down_ref,
    output_ref,
    back_ref,
    feed_ref,
    down_out_ref,
    output_out_ref,
    dq_ref,
    dk_ref,
    dv_ref,
    feed_sems,
    swap_sems,
):
    here = Place()
    tile = pl.program_id(0)
    cols = q_ref.shape[1]
    feed = block_spread(here, False, blocks_ref, feed_ref, feed_sems)
    swaps = [
        remote(src, dst, swap_sems.at[0, number], swap_sems.at[1, number], here.partner())
        for number, (src, dst) in enumerate(
            [(down_ref, down_out_ref), (output_ref, output_out_ref)]
        )
    ]

    @pl.when(tile == 0)
    def _():
        here.greet_all()
        feed.start()
        for one in swaps:
            one.start()

    attention_back_kernel(
        block, q_ref, k_ref, v_ref, g_ref, att_ref, lse_ref, open_ref, dq_ref, dk_ref, dv_ref
    )
    where = pl.ds(pl.multiple_of(tile * block, block), block)
    scale = 1.0 / math.sqrt(HEAD_DIM)
    cosine = cos_ref[where, :]
    sine = sin_ref[where, :]
    back_ref[where, :cols] = rotated(dq_ref[...] * scale, cosine, -sine).astype(BF16)

    @pl.when(tile == pl.num_programs(0) - 1)
    def _():
        @pl.loop(0, pl.num_programs(0))
        def _(i):
            rows = pl.ds(pl.multiple_of(i * block, block), block)
            keys = rotated(dk_ref[rows, :], cos_ref[rows, :], -sin_ref[rows, :])
            back_ref[rows, cols : 2 * cols] = keys.astype(BF16)
            back_ref[rows, 2 * cols :] = dv_ref[rows, :].astype(BF16)

        feed.finish()
        for one in swaps:
            one.wait()


def attention_back_feed(
    queries,
    keys,
    values,
    grads,
    attended,
    log_total,
    opening,
    cosine,
    sine,
    blocks,
    down,
    output,
    block,
    call_id,
):
    seq = lax.axis_size("seq")
    rows, cols = queries.shape
    heads = cols // HEAD_DIM
    tiled = lambda width: pl.BlockSpec((block, width), lambda i: (i, 0))
    whole = pl.BlockSpec((rows, cols), lambda i: (0, 0))
    dma = pltpu.SemaphoreType.DMA
    return pl.pallas_call(
        functools.partial(attention_back_feed_kernel, block),
        grid=(rows // block,),
        in_specs=[tiled(cols), whole, whole, tiled(cols), tiled(cols), tiled(heads), tiled(1)]
        + [whole, whole, HBM, HBM, HBM],
        out_specs=[pl.BlockSpec((rows, 3 * cols), lambda i: (0, 0)), HBM, HBM, HBM],
        out_shape=[
            jax.ShapeDtypeStruct((rows, 3 * cols), BF16),
            jax.ShapeDtypeStruct((seq // 2, *blocks.shape[1:]), BF16),
            jax.ShapeDtypeStruct(down.shape, BF16),
            jax.ShapeDtypeStruct(output.shape, BF16),
        ],
        scratch_shapes=[
            pltpu.VMEM((block, cols), F32),
            pltpu.VMEM((rows, cols), F32),
            pltpu.VMEM((rows, cols), F32),
            dma((2, seq // 2)),
            dma((2, 2)),
        ],
        compiler_params=params(call_id, 60),
        cost_estimate=cost(5 * rows * rows * cols, 20 * rows * cols),
    )(
        queries,
        keys,
        values,
        grads,
        attended,
        log_total,
        opening,
        cosine,
        sine,
        blocks,
        down,
        output,
    )


def scatter_last_kernel(
    tile,
    a_ref,
    b_ref,
    normed_ref,
    blocks_ref,
    out_ref,
    feed_ref,
    qkv_ref,
    *scratch,
):
    here = Place()
    here.greet_all()
    whole, away, came, sums, feed_sems, near_sems, far_sems, swap_sems, local_sem = scratch[
        SCATTER_SCRATCH:
    ]
    feed = block_spread(here, True, blocks_ref, feed_ref, feed_sems)
    feed.start()
    own_feed = pltpu.make_async_copy(
        blocks_ref.at[here.mine], feed_ref.at[here.slot], local_sem.at[0]
    )
    own_feed.start()
    swap = remote(away, came, swap_sems.at[0], swap_sems.at[1], here.partner())
    near = block_spread(here, True, sums, qkv_ref.at[0], near_sems)
    far = block_spread(here, False, sums, qkv_ref.at[1], far_sems)
    half = away.shape[0]
    chunk = min(half, 512)
    chunks = half // chunk

    def between():
        @pl.loop(0, 2 * chunks)
        def _(i):
            first = pl.multiple_of(i * chunk, chunk)
            part = t_dot(normed_ref[:, pl.ds(first, chunk)], a_ref[...])
            whole[pl.ds(first, chunk), :] = part

        @pl.loop(0, chunks)
        def _(i):
            into = pl.ds(pl.multiple_of(i * chunk, chunk), chunk)
            first = pl.multiple_of((1 - here.dp) * half + i * chunk, chunk)
            away[into, :] = whole[pl.ds(first, chunk), :].astype(BF16)

        swap.start()

    def middle():
        swap.wait_recv()
        slab = sums.shape[1]

        @pl.loop(0, here.count)
        def _(i):
            rows = pl.ds(pl.multiple_of(i * slab, slab), slab)
            own = pl.ds(pl.multiple_of(here.dp * half + i * slab, slab), slab)
            sums[i] = (whole[own, :] + came[rows, :].astype(F32)).astype(BF16)

        qkv_ref[0, here.slot] = sums[here.mine]
        far.start()
        near.start()

    scatter_rows_of_product(
        here,
        True,
        SCATTER_PARTS,
        tile,
        a_ref,
        b_ref,
        out_ref,
        *scratch[:SCATTER_SCRATCH],
        between,
        middle,
    )
    swap.wait_send()
    near.finish()
    far.finish()
    feed.finish()
    own_feed.wait()


def product_scatter_last(a, b, normed, blocks, call_id):
    seq = lax.axis_size("seq")
    rows = a.shape[0] // seq
    width, cols = b.shape
    slab = blocks.shape[1]
    dma = pltpu.SemaphoreType.DMA
    return pl.pallas_call(
        functools.partial(scatter_last_kernel, scatter_tile(width)),
        out_shape=[
            jax.ShapeDtypeStruct((rows, width), F32),
            jax.ShapeDtypeStruct((seq // 2, *blocks.shape[1:]), BF16),
            jax.ShapeDtypeStruct((2, seq // 2, slab, cols), BF16),
        ],
        in_specs=[VMEM, VMEM, VMEM, HBM],
        out_specs=[VMEM, HBM, VMEM],
        scratch_shapes=scatter_scratch(seq, rows, width)
        + [
            pltpu.VMEM((width, cols), F32),
            pltpu.VMEM((width // 2, cols), BF16),
            pltpu.VMEM((width // 2, cols), BF16),
            pltpu.VMEM((seq, slab, cols), BF16),
            dma((2, seq // 2)),
            dma((2, seq // 2)),
            dma((2, seq // 2)),
            dma((2,)),
            dma((1,)),
        ],
        compiler_params=params(call_id, 56),
        cost_estimate=scatter_cost(a, width),
    )(a, b, normed, blocks)


def swap_dp(values):
    count = lax.axis_size("dp")
    return lax.ppermute(values, "dp", [(i, (i + 1) % count) for i in range(count)])


def gather_dp(values):
    return lax.all_gather(values, "dp", axis=0, tiled=True)


def sum_dp(partial):
    half = partial.shape[0] // 2
    mine = lax.axis_index("dp")
    away = lax.dynamic_slice_in_dim(partial, (1 - mine) * half, half, 0).astype(BF16)
    kept = lax.dynamic_slice_in_dim(partial, mine * half, half, 0)
    return kept + swap_dp(away).astype(F32)


def gather_rows(values):
    return lax.all_gather(values, "seq", axis=0, tiled=True)


def scatter_rows(partial):
    return lax.psum_scatter(partial.astype(BF16), "seq", scatter_dimension=0, tiled=True).astype(F32)


def exchange(blocks):
    return lax.all_to_all(blocks, "seq", split_axis=0, concat_axis=0, tiled=True)


def norm_factor(values):
    return lax.rsqrt(jnp.mean(values * values, axis=-1, keepdims=True) + EPS)


def norm_back(inputs, factor, gain_row, upstream):
    scaled_up = gain_row * upstream
    inner_mean = jnp.mean(scaled_up * inputs, axis=-1, keepdims=True)
    grad_in = factor * scaled_up - inputs * factor * factor * factor * inner_mean
    grad_gain = jnp.sum(upstream * inputs * factor, axis=0)
    return grad_in, grad_gain


def plain_shards(
    tokens,
    cotangent,
    doc_lengths,
    attn_gain,
    mlp_gain,
    query_weight,
    key_weight,
    value_weight,
    output_weight,
    gate_weight,
    up_weight,
    down_weight,
):
    dp = lax.axis_size("dp")
    seq = lax.axis_size("seq")
    mine = lax.axis_index("seq")
    tok_count, width = tokens.shape
    rows = tok_count * seq
    slab = query_weight.shape[0]
    share = HEAD_DIM // slab
    half_heads = HEADS // dp
    half_kv = KV_HEADS // dp
    hidden_dev = down_weight.shape[0]
    block = 512

    doc_ends = jnp.cumsum(doc_lengths[0])
    place = jnp.arange(rows, dtype=jnp.int32)
    passed = doc_ends[None, :] <= place[:, None]
    opening = jnp.max(jnp.where(passed, doc_ends[None, :], 0), axis=1)
    position = place - opening
    keeping = place < doc_ends[DOCS - 1]
    angles = position.astype(F32)[:, None] * rotary_table(HEAD_DIM)[None, :]
    cosine = jnp.cos(angles)
    sine = jnp.sin(angles)
    cos_heads = jnp.tile(cosine, (1, 2 * dp))
    sin_heads = jnp.tile(jnp.concatenate([-sine, sine], axis=1), (1, dp))
    own_keeping = lax.dynamic_slice_in_dim(keeping, mine * tok_count, tok_count, 0)

    def head_columns(weight, kept):
        split = weight.reshape(slab, dp, kept, HEAD_DIM)
        return jnp.repeat(split, seq // kept, axis=2)

    qkv_blocks = jnp.stack(
        [
            head_columns(query_weight, half_heads),
            head_columns(key_weight, half_kv),
            head_columns(value_weight, half_kv),
        ],
        axis=1,
    )
    qkv_blocks = jnp.transpose(qkv_blocks, (3, 0, 1, 2, 4)).reshape(seq * slab, 3 * dp * HEAD_DIM)
    qkv_weight = gather_dp(exchange(qkv_blocks))
    feed_blocks = jnp.stack(
        [w.reshape(slab, dp, seq, hidden_dev) for w in (gate_weight, up_weight)], axis=1
    )
    feed_blocks = jnp.transpose(feed_blocks, (3, 0, 1, 2, 4)).reshape(
        seq * slab, 2 * dp * hidden_dev
    )
    feed_weight = gather_dp(exchange(feed_blocks))
    down_own = gather_dp(down_weight)
    output_own = output_weight
    if share > 1:
        groups = [list(range(i, i + share)) for i in range(0, seq, share)]
        output_own = lax.all_gather(
            output_own, "seq", axis=0, tiled=True, axis_index_groups=groups
        )
    output_own = gather_dp(output_own)
    gains = lax.all_gather(
        jnp.stack([attn_gain, mlp_gain]), ("dp", "seq"), axis=1, tiled=True
    ).astype(F32)
    gain_one, gain_two = gains[0], gains[1]

    inputs_all = gather_rows(tokens).astype(F32)
    normed_one = (inputs_all * norm_factor(inputs_all) * gain_one).astype(BF16)
    qkv = dot(normed_one, qkv_weight)
    head_cols = dp * HEAD_DIM
    query_lin, key_lin = qkv[:, :head_cols], qkv[:, head_cols : 2 * head_cols]
    values = qkv[:, 2 * head_cols :].astype(BF16)
    scale = 1.0 / math.sqrt(HEAD_DIM)
    queries = (query_lin * cos_heads + swap_halves(query_lin) * sin_heads).astype(BF16) * BF16(scale)
    keys = (key_lin * cos_heads + swap_halves(key_lin) * sin_heads).astype(BF16)
    attended_sum, log_total = attention(queries, keys, values, opening[:, None], block)
    if share > 1:
        own_rows = ((place // tok_count) % share == mine % share)[:, None]
        attended_sum = jnp.where(own_rows, attended_sum, 0.0)
    attended = attended_sum.astype(BF16)
    inputs = tokens.astype(F32)
    middle = inputs + scatter_rows(dot(attended, output_own))

    factor_two = norm_factor(middle)
    normed_two = gather_rows((middle * factor_two * gain_two).astype(BF16))
    grad_own = jnp.where(own_keeping[:, None], cotangent, BF16(0))
    grad_out = gather_rows(grad_own)
    feed = dot(normed_two, feed_weight)
    feed_cols = dp * hidden_dev
    gate_lin, upward = feed[:, :feed_cols], feed[:, feed_cols:]
    sigmoid = jax.nn.sigmoid(gate_lin)
    hidden = (gate_lin * sigmoid * upward).astype(BF16)
    hidden_grad = dot_t(grad_out, down_own)
    gate_back = (hidden_grad * upward * sigmoid * (1.0 + gate_lin * (1.0 - sigmoid))).astype(BF16)
    up_back = (hidden_grad * gate_lin * sigmoid).astype(BF16)
    feed_back = jnp.concatenate([gate_back, up_back], axis=1)
    normed_two_grad = scatter_rows(dot_t(feed_back, feed_weight))
    mixed = middle + scatter_rows(dot(hidden, down_own))
    middle_in, gain_two_part = norm_back(middle, factor_two, gain_two, normed_two_grad)
    middle_grad = grad_own.astype(F32) + middle_in
    middle_back = gather_rows(middle_grad.astype(BF16))

    attended_grad = dot_t(middle_back, output_own).astype(BF16)
    if share > 1:
        attended_grad = jnp.where(own_rows, attended_grad, BF16(0))
    query_acc, key_acc, value_acc = attention_back(
        queries, keys, values, attended_grad, attended_sum, log_total, opening[:, None], block
    )
    query_acc = query_acc * scale
    query_back = query_acc * cos_heads - swap_halves(query_acc) * sin_heads
    key_back = key_acc * cos_heads - swap_halves(key_acc) * sin_heads
    qkv_back = jnp.concatenate([query_back, key_back, value_acc], axis=1).astype(BF16)
    normed_one_grad = scatter_rows(dot_t(qkv_back, qkv_weight))
    input_in, gain_one_part = norm_back(inputs, norm_factor(inputs), gain_one, normed_one_grad)
    token_grad = middle_grad + input_in

    feed_grad = exchange(sum_dp(t_dot(normed_two, feed_back)).astype(BF16)).astype(F32)
    feed_grad = feed_grad.reshape(seq, slab, 2, dp, hidden_dev)
    feed_grad = jnp.transpose(feed_grad, (2, 1, 3, 0, 4)).reshape(2, slab, dp * seq * hidden_dev)
    down_grad = sum_dp(t_dot(hidden, grad_out))
    output_part = t_dot(attended, middle_back)
    if share > 1:
        split = output_part.reshape(dp, share, slab, width)
        split = jnp.transpose(split, (1, 0, 2, 3)).reshape(share * dp * slab, width)
        output_part = lax.psum_scatter(
            split, "seq", scatter_dimension=0, tiled=True, axis_index_groups=groups
        )
    output_grad = sum_dp(output_part)
    qkv_grad = exchange(sum_dp(t_dot(normed_one, qkv_back)).astype(BF16)).astype(F32)
    qkv_grad = qkv_grad.reshape(seq, slab, 3, dp, HEAD_DIM)

    def own_columns(part, kept):
        summed = jnp.sum(part.reshape(kept, seq // kept, slab, dp, HEAD_DIM), axis=1)
        return jnp.transpose(summed, (1, 2, 0, 3)).reshape(slab, dp * kept * HEAD_DIM)

    query_grad = own_columns(qkv_grad[:, :, 0], half_heads)
    key_grad = own_columns(qkv_grad[:, :, 1], half_kv)
    value_grad = own_columns(qkv_grad[:, :, 2], half_kv)
    gain_parts = lax.psum(jnp.stack([gain_one_part, gain_two_part]), ("dp", "seq"))
    own = lax.axis_index("dp") * seq + mine
    gain_grads = lax.dynamic_slice_in_dim(gain_parts, own * slab, slab, 1)
    return (
        mixed,
        token_grad,
        gain_grads[0],
        gain_grads[1],
        query_grad,
        key_grad,
        value_grad,
        output_grad,
        feed_grad[0],
        feed_grad[1],
        down_grad,
    )


def shards(
    tokens,
    cotangent,
    doc_lengths,
    attn_gain,
    mlp_gain,
    query_weight,
    key_weight,
    value_weight,
    output_weight,
    gate_weight,
    up_weight,
    down_weight,
):
    dp = lax.axis_size("dp")
    seq = lax.axis_size("seq")
    data = lax.axis_index("dp")
    mine = lax.axis_index("seq")
    tok_count, width = tokens.shape
    rows = tok_count * seq
    slab = query_weight.shape[0]
    half_heads = HEADS // dp
    half_kv = KV_HEADS // dp
    hidden_dev = down_weight.shape[0]
    block = 512

    doc_ends = jnp.cumsum(doc_lengths[0])
    place = jnp.arange(rows, dtype=jnp.int32)
    passed = doc_ends[None, :] <= place[:, None]
    opening = jnp.max(jnp.where(passed, doc_ends[None, :], 0), axis=1)
    position = place - opening
    keeping = place < doc_ends[DOCS - 1]
    angles = position.astype(F32)[:, None] * rotary_table(HEAD_DIM)[None, :]
    cosine = jnp.cos(angles)
    sine = jnp.sin(angles)
    cos_heads = jnp.tile(cosine, (1, 2 * dp))
    sin_heads = jnp.tile(jnp.concatenate([-sine, sine], axis=1), (1, dp))
    own_keeping = lax.dynamic_slice_in_dim(keeping, mine * tok_count, tok_count, 0)
    grad_own = jnp.where(own_keeping[:, None], cotangent, BF16(0))
    grad_out = gather_rows(grad_own)

    gain_one = attn_gain.astype(F32)[:, None]
    gain_two = mlp_gain.astype(F32)[:, None]

    def scaled(weight, gain):
        return (weight.astype(F32) * gain).astype(BF16)

    def head_columns(weight, kept):
        split = scaled(weight, gain_one).reshape(slab, dp, kept, HEAD_DIM)
        return jnp.repeat(split, seq // kept, axis=2)

    qkv_blocks = jnp.stack(
        [
            head_columns(query_weight, half_heads),
            head_columns(key_weight, half_kv),
            head_columns(value_weight, half_kv),
        ],
        axis=1,
    )
    qkv_blocks = jnp.transpose(qkv_blocks, (3, 0, 1, 2, 4)).reshape(seq, slab, 3 * dp * HEAD_DIM)
    gate_scaled = scaled(gate_weight, gain_two)
    up_scaled = scaled(up_weight, gain_two)

    inputs = tokens.astype(F32)
    factor_one = norm_factor(inputs)
    (normed_one, queries, keys, values, qkv_weight, feed_near, down_own, output_own) = (
        gather_project(
            (inputs * factor_one).astype(BF16),
            qkv_blocks,
            gate_scaled,
            up_scaled,
            down_weight,
            output_weight,
            cos_heads,
            sin_heads,
            0,
        )
    )
    qkv_weight = qkv_weight.reshape(width, -1)
    down_own = down_own.reshape(-1, width)
    output_own = output_own.reshape(-1, width)
    attended_sum, log_total, feed_far = attention_feed(
        queries,
        keys,
        values,
        opening[:, None],
        gate_scaled,
        up_scaled,
        feed_near.shape[2],
        block,
        1,
    )
    attended = attended_sum.astype(BF16)
    attended_out, feed_weight = product_scatter_feed(attended, output_own, feed_near, feed_far, 2)
    feed_weight = feed_weight.reshape(width, -1)
    middle = inputs + attended_out

    factor_two = norm_factor(middle)
    normed_two, hidden, feed_back = gather_feed(
        (middle * factor_two).astype(BF16), grad_out, feed_weight, down_own, 3
    )
    mixed = middle + scatter_rows(dot(hidden, down_own))

    def norm_input_grad(values, factor, upstream):
        inner_mean = jnp.mean(upstream * values, axis=-1, keepdims=True)
        return factor * upstream - values * factor * factor * factor * inner_mean

    middle_in = norm_input_grad(middle, factor_two, product_scatter(feed_back, feed_weight.T, 4))
    middle_grad = grad_own.astype(F32) + middle_in
    feed_part = t_dot(normed_two, feed_back).astype(BF16).reshape(dp, width // dp, -1)
    attended_grad, output_part, feed_came = gather_back(
        middle_grad.astype(BF16), output_own, attended, feed_part, 5
    )

    def halves(part):
        half = part.shape[0] // dp
        kept = lax.dynamic_slice_in_dim(part, data * half, half, 0)
        return kept, lax.dynamic_slice_in_dim(part, (1 - data) * half, half, 0).astype(BF16)

    def both(kept, came):
        return kept.astype(F32) + came.astype(F32)

    feed_kept = lax.dynamic_index_in_dim(feed_part, data, 0, keepdims=False)
    feed_sums = both(feed_kept, feed_came).astype(BF16).reshape(seq, slab, -1)
    down_kept, down_away = halves(t_dot(hidden, grad_out))
    output_kept, output_away = halves(output_part)
    qkv_back, feed_grad_far, down_came, output_came = attention_back_feed(
        queries,
        keys,
        values,
        attended_grad,
        attended_sum,
        log_total,
        opening[:, None],
        cos_heads,
        sin_heads,
        feed_sums,
        down_away,
        output_away,
        block,
        6,
    )
    down_grad = both(down_kept, down_came)
    output_grad = both(output_kept, output_came)
    normed_one_grad, feed_grad_near, qkv_grads = product_scatter_last(
        qkv_back, qkv_weight, normed_one, feed_sums, 7
    )
    token_grad = middle_grad + norm_input_grad(inputs, factor_one, normed_one_grad)

    pair = (mine // 2) % 2

    def by_sender(near, far):
        first = jnp.where(pair == 0, near, far)
        second = jnp.where(pair == 0, far, near)
        split = jnp.stack([first, second]).reshape(2, seq // 4, 2, *near.shape[1:])
        return jnp.swapaxes(split, 0, 1).reshape(seq, *near.shape[1:])

    feed_grad = by_sender(feed_grad_near, feed_grad_far).reshape(seq, slab, 2, dp, hidden_dev)
    feed_grad = jnp.transpose(feed_grad, (2, 1, 3, 0, 4)).reshape(2, slab, -1).astype(F32)
    qkv_grad = by_sender(qkv_grads[0], qkv_grads[1]).astype(F32)
    qkv_grad = qkv_grad.reshape(seq, slab, 3, dp, HEAD_DIM)

    def own_columns(part, kept):
        summed = jnp.sum(part.reshape(kept, seq // kept, slab, dp, HEAD_DIM), axis=1)
        return jnp.transpose(summed, (1, 2, 0, 3)).reshape(slab, dp * kept * HEAD_DIM)

    query_grad = own_columns(qkv_grad[:, :, 0], half_heads)
    key_grad = own_columns(qkv_grad[:, :, 1], half_kv)
    value_grad = own_columns(qkv_grad[:, :, 2], half_kv)

    def along(weight, grad):
        return jnp.sum(weight.astype(F32) * grad, axis=1)

    attn_gain_grad = (
        along(query_weight, query_grad)
        + along(key_weight, key_grad)
        + along(value_weight, value_grad)
    )
    mlp_gain_grad = along(gate_weight, feed_grad[0]) + along(up_weight, feed_grad[1])
    return (
        mixed,
        token_grad,
        attn_gain_grad,
        mlp_gain_grad,
        query_grad * gain_one,
        key_grad * gain_one,
        value_grad * gain_one,
        output_grad,
        feed_grad[0] * gain_two,
        feed_grad[1] * gain_two,
        down_grad,
    )


def solution(mesh):
    both = P(("dp", "seq"), None)
    line = P(("dp", "seq"))
    dp, seq = mesh.shape["dp"], mesh.shape["seq"]

    def run(*args):
        tokens = args[0].shape[0]
        width = args[0].shape[1]
        suits = dp == 2 and seq % 4 == 0 and width == dp * seq * HEAD_DIM
        suits = suits and 2 * (tokens // dp) * width <= 16 << 20
        return jax.shard_map(
            shards if suits else plain_shards,
            mesh=mesh,
            in_specs=(both, both, P("dp", None), line, line) + (both,) * 7,
            out_specs=(both, both, line, line) + (both,) * 7,
            check_vma=False,
        )(*args)

    return run
```

```python
import functools
import math

import jax
import jax.numpy as jnp
from jax import lax
from jax.experimental import pallas as pl
from jax.experimental.pallas import tpu as pltpu
from jax.sharding import PartitionSpec as P

HEADS = 32
KV_HEADS = 8
HEAD_DIM = 64
DOCS = 4
EPS = 1e-05
NEG = -1e30
MESH = pl.DeviceIdType.MESH
F32 = jnp.float32
BF16 = jnp.bfloat16


def rotary_table(head_dim):
    exponent = jnp.arange(0, head_dim, 2, dtype=F32) / head_dim
    inverse = jnp.power(F32(500000.0), -exponent)
    wavelength = 2.0 * math.pi / inverse
    smooth = (8192.0 / wavelength - 1.0) / 3.0
    blended = (1.0 - smooth) * inverse / 32.0 + smooth * inverse
    return jnp.where(
        wavelength < 2048.0, inverse, jnp.where(wavelength > 8192.0, inverse / 32.0, blended)
    )


def swap_halves(values):
    rows, cols = values.shape
    halves = values.reshape(rows, cols // HEAD_DIM, 2, HEAD_DIM // 2)
    return halves[:, :, ::-1].reshape(rows, cols)


def dot(a, b):
    return jnp.dot(a, b, preferred_element_type=F32)


def dot_t(a, b):
    return lax.dot_general(a, b, (((1,), (1,)), ((), ())), preferred_element_type=F32)


def t_dot(a, b):
    return lax.dot_general(a, b, (((0,), (0,)), ((), ())), preferred_element_type=F32)


def allowed_tile(opening, q_first, k_first, shape):
    rows = q_first + lax.broadcasted_iota(jnp.int32, shape, 0)
    cols = k_first + lax.broadcasted_iota(jnp.int32, shape, 1)
    return (cols <= rows) & (cols >= opening)


def attention_kernel(block, q_ref, k_ref, v_ref, open_ref, out_ref, lse_ref):
    tile = pl.program_id(0)
    opening = open_ref[...]
    for head in range(q_ref.shape[1] // HEAD_DIM):
        lanes = slice(head * HEAD_DIM, (head + 1) * HEAD_DIM)
        query = q_ref[:, lanes]

        def step(j, carry, lanes=lanes, query=query):
            peak, total, acc = carry
            first = pl.multiple_of(j * block, block)
            scores = dot_t(query, k_ref[pl.ds(first, block), lanes])
            allowed = allowed_tile(opening, tile * block, first, scores.shape)
            scores = jnp.where(allowed, scores, NEG)
            new_peak = jnp.maximum(peak, jnp.max(scores, axis=1, keepdims=True))
            spread = jnp.where(allowed, jnp.exp(scores - new_peak), 0.0)
            fade = jnp.exp(peak - new_peak)
            total = total * fade + jnp.sum(spread, axis=1, keepdims=True)
            acc = acc * fade + dot(spread.astype(BF16), v_ref[pl.ds(first, block), lanes])
            return new_peak, total, acc

        peak, total, acc = lax.fori_loop(
            0,
            tile + 1,
            step,
            (
                jnp.full((block, 1), NEG, F32),
                jnp.zeros((block, 1), F32),
                jnp.zeros((block, HEAD_DIM), F32),
            ),
        )
        out_ref[:, lanes] = acc / total
        lse_ref[:, head : head + 1] = peak + jnp.log(total)


def attention(queries, keys, values, opening, block):
    rows, cols = queries.shape
    heads = cols // HEAD_DIM
    tiled = lambda width: pl.BlockSpec((block, width), lambda i: (i, 0))
    whole = pl.BlockSpec((rows, cols), lambda i: (0, 0))
    return pl.pallas_call(
        functools.partial(attention_kernel, block),
        grid=(rows // block,),
        in_specs=[tiled(cols), whole, whole, tiled(1)],
        out_specs=[tiled(cols), tiled(heads)],
        out_shape=[
            jax.ShapeDtypeStruct((rows, cols), F32),
            jax.ShapeDtypeStruct((rows, heads), F32),
        ],
        compiler_params=pltpu.CompilerParams(vmem_limit_bytes=48 << 20),
        cost_estimate=pl.CostEstimate(
            flops=2 * rows * rows * cols, bytes_accessed=10 * rows * cols, transcendentals=0
        ),
    )(queries, keys, values, opening)


def attention_back_kernel(
    block, q_ref, k_ref, v_ref, g_ref, att_ref, lse_ref, open_ref, dq_ref, dk_ref, dv_ref
):
    tile = pl.program_id(0)

    @pl.when(tile == 0)
    def _():
        dk_ref[...] = jnp.zeros_like(dk_ref)
        dv_ref[...] = jnp.zeros_like(dv_ref)

    opening = open_ref[...]
    for head in range(q_ref.shape[1] // HEAD_DIM):
        lanes = slice(head * HEAD_DIM, (head + 1) * HEAD_DIM)
        query = q_ref[:, lanes]
        grad = g_ref[:, lanes]
        log_total = lse_ref[:, head : head + 1]
        row_sum = jnp.sum(grad.astype(F32) * att_ref[:, lanes], axis=1, keepdims=True)

        def step(j, acc, lanes=lanes, query=query, grad=grad, log_total=log_total, row_sum=row_sum):
            first = pl.multiple_of(j * block, block)
            here = pl.ds(first, block)
            key = k_ref[here, lanes]
            scores = dot_t(query, key)
            allowed = allowed_tile(opening, tile * block, first, scores.shape)
            chance = jnp.where(allowed, jnp.exp(scores - log_total), 0.0)
            prob_grad = dot_t(grad, v_ref[here, lanes])
            score_grad = (chance * (prob_grad - row_sum)).astype(BF16)
            dk_ref[here, lanes] += t_dot(score_grad, query)
            dv_ref[here, lanes] += t_dot(chance.astype(BF16), grad)
            return acc + dot(score_grad, key)

        acc = lax.fori_loop(0, tile + 1, step, jnp.zeros((block, HEAD_DIM), F32))
        dq_ref[:, lanes] = acc


def attention_back(queries, keys, values, grads, attended, log_total, opening, block):
    rows, cols = queries.shape
    heads = cols // HEAD_DIM
    tiled = lambda width: pl.BlockSpec((block, width), lambda i: (i, 0))
    whole = pl.BlockSpec((rows, cols), lambda i: (0, 0))
    return pl.pallas_call(
        functools.partial(attention_back_kernel, block),
        grid=(rows // block,),
        in_specs=[tiled(cols), whole, whole, tiled(cols), tiled(cols), tiled(heads), tiled(1)],
        out_specs=[tiled(cols), whole, whole],
        out_shape=[jax.ShapeDtypeStruct((rows, cols), F32)] * 3,
        compiler_params=pltpu.CompilerParams(vmem_limit_bytes=60 << 20),
        cost_estimate=pl.CostEstimate(
            flops=5 * rows * rows * cols, bytes_accessed=20 * rows * cols, transcendentals=0
        ),
    )(queries, keys, values, grads, attended, log_total, opening)


class Place:
    def __init__(self):
        self.dp = lax.axis_index("dp")
        self.mine = lax.axis_index("seq")
        self.count = lax.axis_size("seq")
        self.length = self.count // 4
        self.line = lax.div(self.mine, 4)
        self.pair = lax.rem(lax.div(self.mine, 2), 2)
        self.core = lax.rem(self.mine, 2)
        self.slot = self.line * 2 + self.core

    def index(self, line, pair, core):
        return (line * 2 + pair) * 2 + core

    def peer(self, slot, same):
        pair = self.pair if same else 1 - self.pair
        return self.index(lax.div(slot, 2), pair, lax.rem(slot, 2))

    def device(self, line, pair, core):
        return (self.dp, self.index(line, pair, core))

    def sibling(self):
        return self.device(self.line, self.pair, 1 - self.core)

    def across(self):
        return self.device(self.line, 1 - self.pair, self.core)

    def above(self):
        return self.device(self.line + 1, self.pair, self.core)

    def below(self):
        return self.device(self.line - 1, self.pair, self.core)

    def partner(self):
        return (1 - self.dp, self.mine)

    def greet(self, partner=False):
        barrier = pltpu.get_barrier_semaphore()

        def signal(device):
            pl.semaphore_signal(barrier, inc=1, device_id=device, device_id_type=MESH)

        signal(self.sibling())
        signal(self.across())
        pl.when(self.line > 0)(lambda: signal(self.below()))
        pl.when(self.line < self.length - 1)(lambda: signal(self.above()))
        if partner:
            signal(self.partner())
        inner = (self.line > 0) & (self.line < self.length - 1)
        pl.semaphore_wait(barrier, jnp.where(inner, 4, 3) + (1 if partner else 0))

    def greet_all(self):
        barrier = pltpu.get_barrier_semaphore()

        def signal(device):
            pl.semaphore_signal(barrier, inc=1, device_id=device, device_id_type=MESH)

        signal(self.partner())

        @pl.loop(1, self.count)
        def _(ahead):
            signal((self.dp, lax.rem(self.mine + ahead, self.count)))

        pl.semaphore_wait(barrier, self.count)


def remote(src, dst, send_sem, recv_sem, device):
    return pltpu.make_async_remote_copy(
        src_ref=src,
        dst_ref=dst,
        send_sem=send_sem,
        recv_sem=recv_sem,
        device_id=device,
        device_id_type=MESH,
    )


class Spread:
    def __init__(self, here, same, copies):
        self.here, self.same, self.copies = here, same, copies
        self.slots = here.count // 2

    def each(self, visit):
        @pl.loop(1 if self.same else 0, self.slots)
        def _(ahead):
            slot = lax.rem(self.here.slot + ahead, self.slots)
            visit(self.here.peer(slot, self.same), slot)

    def start(self):
        def visit(peer, slot):
            for one in self.copies(peer, self.here.mine, self.here.slot, slot):
                one.start()

        self.each(visit)

    def finish(self):
        def visit(peer, slot):
            for one in self.copies(peer, peer, slot, slot):
                one.wait()

        self.each(visit)


def block_spread(here, same, blocks, into, sems):
    def copies(peer, sender, at, sem):
        return [
            remote(
                blocks.at[peer],
                into.at[at],
                sems.at[0, sem],
                sems.at[1, at],
                (here.dp, peer),
            )
        ]

    return Spread(here, same, copies)


def feed_spread(here, same, weights, into, sems):
    dp = lax.axis_size("dp")
    columns = into.shape[2] // (dp * len(weights))

    def copies(peer, sender, at, sem):
        made = []
        for kind, weight in enumerate(weights):
            for half in range(dp):
                part = kind * dp + half
                begin = pl.multiple_of((half * here.count + peer) * columns, columns)
                made.append(
                    remote(
                        weight.at[:, pl.ds(begin, columns)],
                        into.at[at, :, pl.ds(part * columns, columns)],
                        sems.at[0, sem, part],
                        sems.at[1, at, part],
                        (here.dp, peer),
                    )
                )
        return made

    return Spread(here, same, copies)


def nothing():
    pass


def gather_units(here, own_ref, buf, send_sems, recv_sems, compute, between=None, ready=0):
    length = here.length
    last = length - 1
    steps = 2 * length
    half = own_ref.shape[0] // 2
    mine = here.mine
    shorter = jnp.minimum(here.line, last - here.line)
    longer = jnp.where(here.line < last - here.line, 1, -1)

    def column(j):
        i = j - 1
        paired = jnp.where(i % 2 == 0, here.line - i // 2 - 1, here.line + i // 2 + 1)
        single = here.line + longer * (i - shorter + 1)
        return jnp.where(j == 0, here.line, jnp.where(i < 2 * shorter, paired, single))

    def copy(way, device, block, part):
        ref = buf.at[block, part]
        return remote(
            ref, ref, send_sems.at[way, block, part], recv_sems.at[block, part], device
        )

    def up(block, part):
        return copy(0, here.above(), block, part)

    def down(block, part):
        return copy(1, here.below(), block, part)

    def across(block, part):
        return copy(2, here.across(), block, part)

    def sideways(block, part):
        return copy(3, here.sibling(), block, part)

    def unit(number):
        in_column = (number % 2 == 1) & (number < steps - 1) | (number == 0)
        later = jnp.where(number == steps - 1, last, number // 2 - 1)
        line = column(jnp.where(in_column, (number + 1) // 2, later))
        pair = jnp.where(in_column, here.pair, 1 - here.pair)
        other = here.index(line, pair, 1 - here.core)
        sideways(other, 0).wait_recv()
        sideways(other, 1).wait_recv()
        compute(number, here.index(line, pair, 0))

    for part in range(2):
        buf[mine, part] = own_ref[pl.ds(part * half, half), :]
        pl.when(here.line < last)(lambda part=part: up(mine, part).start())
        pl.when(here.line > 0)(lambda part=part: down(mine, part).start())
        across(mine, part).start()
        sideways(mine, part).start()

    @pl.loop(0, steps)
    def _(step):
        part = step % 2
        far = step // 2 + 1

        @pl.when(here.line >= far)
        def _():
            block = here.index(here.line - far, here.pair, here.core)
            up(block, part).wait_recv()
            pl.when(here.line < last)(lambda: up(block, part).start())
            sideways(block, part).start()

        @pl.when(here.line + far <= last)
        def _():
            block = here.index(here.line + far, here.pair, here.core)
            down(block, part).wait_recv()
            pl.when(here.line > 0)(lambda: down(block, part).start())
            sideways(block, part).start()

        @pl.when(step + 2 < steps)
        def _():
            across(here.index(column(step // 2 + 1), here.pair, here.core), part).start()

        block = here.index(column(step // 2), 1 - here.pair, here.core)
        across(block, part).wait_recv()
        sideways(block, part).start()

        if between is None:
            unit(step)
        else:
            between(step)
            begin = jnp.where(step == ready, 0, step)
            end = jnp.where(step < ready, step, step + 1)

            @pl.loop(begin, end)
            def _(number):
                unit(number)

    @pl.loop(0, length)
    def _(line):
        for part in range(2):
            block = here.index(line, here.pair, here.core)

            @pl.when((line <= here.line) & (here.line < last))
            def _():
                up(block, part).wait_send()

            @pl.when((line >= here.line) & (here.line > 0))
            def _():
                down(block, part).wait_send()

            across(block, part).wait_send()
            sideways(block, part).wait_send()
            sideways(here.index(line, 1 - here.pair, here.core), part).wait_send()


def gather_scratch(seq, rows, width):
    return [
        pltpu.VMEM((seq, 2, rows // 2, width), BF16),
        pltpu.SemaphoreType.DMA((4, seq, 2)),
        pltpu.SemaphoreType.DMA((seq, 2)),
    ]


def unit_rows(first, rows):
    return pl.ds(pl.multiple_of(first * rows, 2 * rows), 2 * rows)


def take_unit(buf, first):
    blocks = buf[pl.ds(first, 2)]
    return blocks.reshape(-1, blocks.shape[-1])


class UnitStore:
    def __init__(self, buf, out_ref, sems):
        self.buf, self.out_ref, self.sems = buf, out_ref, sems

    def copies(self, number, first):
        half = self.buf.shape[2]
        made = []
        for block in range(2):
            for part in range(2):
                begin = ((first + block) * 2 + part) * half
                made.append(
                    pltpu.make_async_copy(
                        self.buf.at[first + block, part],
                        self.out_ref.at[pl.ds(pl.multiple_of(begin, half), half)],
                        self.sems.at[number, block, part],
                    )
                )
        return made

    def start(self, number, first):
        for one in self.copies(number, first):
            one.start()

    def finish(self):
        @pl.loop(0, self.sems.shape[0])
        def _(number):
            for one in self.copies(number, 0):
                one.wait()


def params(call_id, mebibytes):
    return pltpu.CompilerParams(
        collective_id=call_id, has_side_effects=True, vmem_limit_bytes=mebibytes << 20
    )


def cost(flops, bytes_accessed):
    return pl.CostEstimate(flops=flops, bytes_accessed=bytes_accessed, transcendentals=0)


VMEM = pl.BlockSpec(memory_space=pltpu.VMEM)
HBM = pl.BlockSpec(memory_space=pl.ANY)


def rotated(values, cosine, sine):
    cols = values.shape[1]
    lane = lax.broadcasted_iota(jnp.int32, values.shape, 1)
    ahead = pltpu.roll(values, cols - HEAD_DIM // 2, 1)
    behind = pltpu.roll(values, HEAD_DIM // 2, 1)
    swapped = jnp.where(lane % HEAD_DIM < HEAD_DIM // 2, ahead, behind)
    return values * cosine + swapped * sine


def project_kernel(
    own_ref,
    blocks_ref,
    gate_ref,
    up_ref,
    down_ref,
    output_ref,
    cos_ref,
    sin_ref,
    normed_ref,
    q_ref,
    k_ref,
    v_ref,
    weight_ref,
    feed_ref,
    down_out_ref,
    output_out_ref,
    buf,
    send_sems,
    recv_sems,
    store_sems,
    near_sems,
    far_sems,
    feed_sems,
    swap_sems,
    local_sems,
    pair_sems,
):
    here = Place()
    here.greet_all()
    cols = q_ref.shape[1]
    rows = own_ref.shape[0]
    dp = here.dp

    def weight_spread(same, sems):
        def copies(peer, sender, at, sem):
            return [
                remote(
                    blocks_ref.at[peer],
                    weight_ref.at[dp, sender],
                    sems.at[0, sem],
                    sems.at[1, at],
                    (dp, peer),
                )
            ]

        return Spread(here, same, copies)

    near = weight_spread(True, near_sems)
    far = weight_spread(False, far_sems)
    far.start()
    near.start()
    weight_ref[dp, here.mine] = blocks_ref[here.mine]
    swaps = []
    for number, (src, dst) in enumerate([(down_ref, down_out_ref), (output_ref, output_out_ref)]):
        swaps.append(
            remote(src, dst.at[dp], swap_sems.at[0, number], swap_sems.at[1, number], here.partner())
        )
        swaps.append(pltpu.make_async_copy(src, dst.at[dp], local_sems.at[number]))
    for one in swaps:
        one.start()
    feed = feed_spread(here, True, (gate_ref, up_ref), feed_ref, feed_sems)
    columns = feed_ref.shape[2] // 4
    own_feed = []
    for kind, weight in enumerate((gate_ref, up_ref)):
        for half in range(2):
            part = kind * 2 + half
            begin = pl.multiple_of((half * here.count + here.mine) * columns, columns)
            own_feed.append(
                pltpu.make_async_copy(
                    weight.at[:, pl.ds(begin, columns)],
                    feed_ref.at[here.slot, :, pl.ds(part * columns, columns)],
                    local_sems.at[2 + part],
                )
            )
    for one in own_feed:
        one.start()

    def pair_copy(source, sender):
        return remote(
            weight_ref.at[source, sender],
            weight_ref.at[source, sender],
            pair_sems.at[0, sender],
            pair_sems.at[1, sender],
            here.partner(),
        )

    def between(step):
        @pl.when(step == 0)
        def _():
            feed.start()

        @pl.when(step == 1)
        def _():
            near.finish()
            far.finish()

            @pl.loop(0, here.count)
            def _(sender):
                pair_copy(dp, sender).start()

        @pl.when(step == 3)
        def _():
            @pl.loop(0, here.count)
            def _(sender):
                pair_copy(1 - dp, sender).wait_recv()

    store = UnitStore(buf, normed_ref, store_sems)

    def compute(number, first):
        store.start(number, first)
        weight = weight_ref[...].reshape(-1, weight_ref.shape[-1])
        qkv = dot(take_unit(buf, first), weight)
        where = unit_rows(first, rows)
        cosine = cos_ref[where, :]
        sine = sin_ref[where, :]
        scale = BF16(1.0 / math.sqrt(HEAD_DIM))
        q_ref[where, :] = rotated(qkv[:, :cols], cosine, sine).astype(BF16) * scale
        k_ref[where, :] = rotated(qkv[:, cols : 2 * cols], cosine, sine).astype(BF16)
        v_ref[where, :] = qkv[:, 2 * cols :].astype(BF16)

    gather_units(here, own_ref, buf, send_sems, recv_sems, compute, between, 3)

    @pl.loop(0, here.count)
    def _(sender):
        pair_copy(dp, sender).wait_send()

    store.finish()
    feed.finish()
    for one in swaps + own_feed:
        one.wait()


def gather_project(own, blocks, gate, up, down, output, cosine, sine, call_id):
    seq = lax.axis_size("seq")
    rows, width = own.shape
    cols = cosine.shape[1]
    slab = gate.shape[0]
    head = jax.ShapeDtypeStruct((seq * rows, cols), BF16)
    feed_cols = 4 * down.shape[0]
    dma = pltpu.SemaphoreType.DMA
    return pl.pallas_call(
        project_kernel,
        out_shape=[
            jax.ShapeDtypeStruct((seq * rows, width), BF16),
            head,
            head,
            head,
            jax.ShapeDtypeStruct((2, *blocks.shape), BF16),
            jax.ShapeDtypeStruct((seq // 2, slab, feed_cols), BF16),
            jax.ShapeDtypeStruct((2, *down.shape), BF16),
            jax.ShapeDtypeStruct((2, *output.shape), BF16),
        ],
        in_specs=[VMEM, VMEM, HBM, HBM, HBM, HBM, VMEM, VMEM],
        out_specs=[HBM, VMEM, VMEM, VMEM, VMEM, HBM, HBM, HBM],
        scratch_shapes=gather_scratch(seq, rows, width)
        + [
            dma((seq // 2, 2, 2)),
            dma((2, seq // 2)),
            dma((2, seq // 2)),
            dma((2, seq // 2, 4)),
            dma((2, 2)),
            dma((6,)),
            dma((2, seq)),
        ],
        compiler_params=params(call_id, 40),
        cost_estimate=cost(2 * seq * rows * width * 3 * cols, 4 * seq * rows * width),
    )(own, blocks, gate, up, down, output, cosine, sine)


def attention_feed_kernel(
    block,
    q_ref,
    k_ref,
    v_ref,
    open_ref,
    gate_ref,
    up_ref,
    out_ref,
    lse_ref,
    feed_ref,
    feed_sems,
):
    here = Place()
    feed = feed_spread(here, False, (gate_ref, up_ref), feed_ref, feed_sems)

    @pl.when(pl.program_id(0) == 0)
    def _():
        here.greet_all()
        feed.start()

    attention_kernel(block, q_ref, k_ref, v_ref, open_ref, out_ref, lse_ref)

    @pl.when(pl.program_id(0) == pl.num_programs(0) - 1)
    def _():
        feed.finish()


def attention_feed(queries, keys, values, opening, gate, up, feed_cols, block, call_id):
    seq = lax.axis_size("seq")
    rows, cols = queries.shape
    heads = cols // HEAD_DIM
    tiled = lambda width: pl.BlockSpec((block, width), lambda i: (i, 0))
    whole = pl.BlockSpec((rows, cols), lambda i: (0, 0))
    return pl.pallas_call(
        functools.partial(attention_feed_kernel, block),
        grid=(rows // block,),
        in_specs=[tiled(cols), whole, whole, tiled(1), HBM, HBM],
        out_specs=[tiled(cols), tiled(heads), HBM],
        out_shape=[
            jax.ShapeDtypeStruct((rows, cols), F32),
            jax.ShapeDtypeStruct((rows, heads), F32),
            jax.ShapeDtypeStruct((seq // 2, gate.shape[0], feed_cols), BF16),
        ],
        scratch_shapes=[pltpu.SemaphoreType.DMA((2, seq // 2, 4))],
        compiler_params=params(call_id, 48),
        cost_estimate=cost(2 * rows * rows * cols, 10 * rows * cols),
    )(queries, keys, values, opening, gate, up)


def scatter_rows_of_product(
    here,
    transposed,
    parts,
    tile,
    a_ref,
    b_ref,
    out_ref,
    core_out,
    core_in,
    pair_out,
    pair_in,
    line_out,
    up_in,
    down_in,
    held,
    core_sems,
    pair_sems,
    line_sems,
    up_sems,
    down_sems,
    between=nothing,
    middle=nothing,
    filler=None,
):
    length = here.length
    rows = out_ref.shape[0]
    width = out_ref.shape[1] // parts
    tiles = width // tile
    steps = length * parts

    def target(i):
        ups = length - 1 - here.line
        near = here.line < length // 2
        if_near = jnp.where(i < ups, length - 1 - i, i - ups)
        if_far = jnp.where(i < here.line, i, length - 1 - (i - here.line))
        return jnp.where(i == length - 1, here.line, jnp.where(near, if_near, if_far))

    def product(line, pair, core, part, use):
        first = pl.multiple_of(here.index(line, pair, core) * rows, rows)
        a = a_ref[pl.ds(first, rows), :]

        @pl.loop(0, tiles)
        def _(t):
            into = pl.ds(pl.multiple_of(t * tile, tile), tile)
            cols = pl.ds(pl.multiple_of(part * width + t * tile, tile), tile)
            use(dot_t(a, b_ref[cols, :]) if transposed else dot(a, b_ref[:, cols]), into)

    def core_copy(slot):
        return remote(
            core_out.at[slot],
            core_in.at[slot],
            core_sems.at[0, slot],
            core_sems.at[1, slot],
            here.sibling(),
        )

    def pair_copy(slot):
        return remote(
            pair_out.at[slot],
            pair_in.at[slot],
            pair_sems.at[0, slot],
            pair_sems.at[1, slot],
            here.across(),
        )

    def up_copy(slot, into):
        return remote(
            line_out.at[slot], up_in.at[into], line_sems.at[slot], up_sems.at[into], here.above()
        )

    def down_copy(slot, into):
        return remote(
            line_out.at[slot], down_in.at[into], line_sems.at[slot], down_sems.at[into], here.below()
        )

    def for_sibling(step, pair, slot):
        def use(value, cols):
            core_out[slot, :, cols] = value.astype(BF16)

        product(target(step // parts), pair, 1 - here.core, step % parts, use)
        core_copy(slot).start()

    for_sibling(0, 1 - here.pair, 0)

    @pl.loop(0, steps)
    def _(step):
        pl.when(step < steps - 1)(lambda: for_sibling(step + 1, 1 - here.pair, step + 1))
        core_copy(step).wait_recv()

        def use(value, cols):
            pair_out[step, :, cols] = (value + core_in[step, :, cols].astype(F32)).astype(BF16)

        product(target(step // parts), 1 - here.pair, here.core, step % parts, use)
        pair_copy(step).start()

    for_sibling(0, here.pair, steps)
    between()

    @pl.loop(0, steps)
    def _(step):
        pl.when(step < steps - 1)(lambda: for_sibling(step + 1, here.pair, steps + step + 1))
        core_copy(steps + step).wait_recv()
        line = target(step // parts)
        part = step % parts
        into = line * parts + part

        def use(value, cols):
            held[:, cols] = value + core_in[steps + step, :, cols].astype(F32)

        product(line, here.pair, here.core, part, use)
        if filler is not None:
            filler(step)
        pair_copy(step).wait_recv()
        from_above = (line <= here.line) & (here.line < length - 1)
        from_below = (line >= here.line) & (here.line > 0)
        held[...] += pair_in[step].astype(F32)

        @pl.when(from_above)
        def _():
            down_copy(0, into).wait_recv()
            held[...] += down_in[into].astype(F32)

        @pl.when(from_below)
        def _():
            up_copy(0, into).wait_recv()
            held[...] += up_in[into].astype(F32)

        @pl.when(line == here.line)
        def _():
            out_ref[:, pl.ds(pl.multiple_of(part * width, width), width)] = held[...]

        @pl.when(line < here.line)
        def _():
            line_out[step] = held[...].astype(BF16)
            down_copy(step, into).start()

        @pl.when(line > here.line)
        def _():
            line_out[step] = held[...].astype(BF16)
            up_copy(step, into).start()

        if middle is not nothing:
            pl.when(step == steps // 2)(middle)

    @pl.loop(0, steps)
    def _(step):
        core_copy(step).wait_send()
        core_copy(steps + step).wait_send()
        pair_copy(step).wait_send()
        line = target(step // parts)
        pl.when(line < here.line)(lambda: down_copy(step, 0).wait_send())
        pl.when(line > here.line)(lambda: up_copy(step, 0).wait_send())


SCATTER_PARTS = 2
SCATTER_SCRATCH = 13


def scatter_scratch(seq, rows, width):
    steps = seq // 4 * SCATTER_PARTS
    block = (rows, width // SCATTER_PARTS)
    dma = pltpu.SemaphoreType.DMA
    return [
        pltpu.VMEM((2 * steps, *block), BF16),
        pltpu.VMEM((2 * steps, *block), BF16),
        pltpu.VMEM((steps, *block), BF16),
        pltpu.VMEM((steps, *block), BF16),
        pltpu.VMEM((steps, *block), BF16),
        pltpu.VMEM((steps, *block), BF16),
        pltpu.VMEM((steps, *block), BF16),
        pltpu.VMEM(block, F32),
        dma((2, 2 * steps)),
        dma((2, steps)),
        dma((steps,)),
        dma((steps,)),
        dma((steps,)),
    ]


def scatter_tile(width):
    return min(width // SCATTER_PARTS, 512)


def scatter_cost(a, width):
    return cost(2 * a.shape[0] * a.shape[1] * width, 4 * a.shape[0] * width)


def scatter_grad_kernel(tile, a_ref, b_ref, normed_ref, out_ref, grad_ref, *scratch):
    here = Place()
    here.greet()
    cols = normed_ref.shape[1] // (here.length * SCATTER_PARTS)

    def filler(step):
        some = pl.ds(pl.multiple_of(step * cols, cols), cols)
        grad_ref[some, :] = t_dot(normed_ref[:, some], a_ref[...]).astype(BF16)

    scatter_rows_of_product(
        here,
        False,
        SCATTER_PARTS,
        tile,
        a_ref,
        b_ref,
        out_ref,
        *scratch,
        filler=filler,
    )


def product_scatter_grad(a, b, normed, call_id):
    seq = lax.axis_size("seq")
    rows = a.shape[0] // seq
    width = b.shape[1]
    return pl.pallas_call(
        functools.partial(scatter_grad_kernel, scatter_tile(width)),
        out_shape=[
            jax.ShapeDtypeStruct((rows, width), F32),
            jax.ShapeDtypeStruct((width, a.shape[1]), BF16),
        ],
        in_specs=[VMEM] * 3,
        out_specs=[VMEM] * 2,
        scratch_shapes=scatter_scratch(seq, rows, width),
        compiler_params=params(call_id, 56),
        cost_estimate=scatter_cost(a, 2 * width),
    )(a, b, normed)


def scatter_feed_kernel(tile, a_ref, b_ref, near_ref, far_ref, out_ref, feed_ref, *scratch):
    here = Place()
    here.greet(partner=True)
    swap_sems, local_sems = scratch[SCATTER_SCRATCH:]
    slots = near_ref.shape[0]

    def copies(half, ref, slot):
        place = feed_ref.at[here.dp, here.peer(slot, half == 0)]
        return (
            remote(
                ref.at[slot],
                place,
                swap_sems.at[0, half, slot],
                swap_sems.at[1, half, slot],
                here.partner(),
            ),
            pltpu.make_async_copy(ref.at[slot], place, local_sems.at[half, slot]),
        )

    @pl.loop(0, slots)
    def _(slot):
        for half, ref in enumerate((near_ref, far_ref)):
            for one in copies(half, ref, slot):
                one.start()

    scatter_rows_of_product(
        here, False, SCATTER_PARTS, tile, a_ref, b_ref, out_ref, *scratch[:SCATTER_SCRATCH]
    )

    @pl.loop(0, slots)
    def _(slot):
        for half, ref in enumerate((near_ref, far_ref)):
            for one in copies(half, ref, slot):
                one.wait()


def product_scatter_feed(a, b, near, far, call_id):
    seq = lax.axis_size("seq")
    rows = a.shape[0] // seq
    width = b.shape[1]
    dma = pltpu.SemaphoreType.DMA
    return pl.pallas_call(
        functools.partial(scatter_feed_kernel, scatter_tile(width)),
        out_shape=[
            jax.ShapeDtypeStruct((rows, width), F32),
            jax.ShapeDtypeStruct((2, seq, *near.shape[1:]), BF16),
        ],
        in_specs=[VMEM, VMEM, HBM, HBM],
        out_specs=[VMEM, HBM],
        scratch_shapes=scatter_scratch(seq, rows, width)
        + [dma((2, 2, seq // 2)), dma((2, seq // 2))],
        compiler_params=params(call_id, 40),
        cost_estimate=scatter_cost(a, width),
    )(a, b, near, far)


def feed_kernel(
    own_ref,
    grad_ref,
    feed_ref,
    down_ref,
    normed_ref,
    hidden_ref,
    back_ref,
    turned_ref,
    mixed_ref,
    buf,
    send_sems,
    recv_sems,
    store_sems,
    mixed_buf,
    mixed_sems,
):
    here = Place()
    here.greet()
    rows = own_ref.shape[0]
    width = own_ref.shape[1]
    hidden = hidden_ref.shape[1]
    tile = 256
    wide = 512
    store = UnitStore(buf, normed_ref, store_sems)

    def mixed_copy(number, first):
        slot = number % 2
        return pltpu.make_async_copy(
            mixed_buf.at[slot], mixed_ref.at[unit_rows(first, rows)], mixed_sems.at[slot]
        )

    def compute(number, first):
        store.start(number, first)
        pl.when(number >= 2)(lambda: mixed_copy(number, first).wait())
        where = unit_rows(first, rows)
        normed = take_unit(buf, first)
        grad = grad_ref[where, :]

        @pl.loop(0, hidden // tile)
        def _(t):
            cols = pl.ds(pl.multiple_of(t * tile, tile), tile)
            later = pl.ds(pl.multiple_of(hidden + t * tile, tile), tile)
            gate = dot(normed, feed_ref[:, cols])
            upward = dot(normed, feed_ref[:, later])
            hidden_grad = dot_t(grad, down_ref[cols, :])
            sigmoid = jax.nn.sigmoid(gate)
            silu = gate * sigmoid
            hidden_ref[where, cols] = (silu * upward).astype(BF16)
            back_ref[where, cols] = (
                hidden_grad * upward * sigmoid * (1.0 + gate * (1.0 - sigmoid))
            ).astype(BF16)
            back_ref[where, later] = (hidden_grad * silu).astype(BF16)

        @pl.loop(0, width // wide)
        def _(t):
            cols = pl.ds(pl.multiple_of(t * wide, wide), wide)
            part = dot(hidden_ref[where, :], down_ref[:, cols])
            mixed_buf[number % 2, :, cols] = part.astype(BF16)

        mixed_copy(number, first).start()
        share = width // (2 * here.length)
        some = pl.ds(pl.multiple_of(number * share, share), share)
        turned_ref[:, some] = feed_ref[some, :].T

    gather_units(here, own_ref, buf, send_sems, recv_sems, compute)
    mixed_copy(0, 0).wait()
    mixed_copy(1, 0).wait()
    store.finish()


def gather_feed(own, grad_out, feed_weight, down_weight, call_id):
    seq = lax.axis_size("seq")
    rows, width = own.shape
    hidden = down_weight.shape[0]
    return pl.pallas_call(
        feed_kernel,
        out_shape=[
            jax.ShapeDtypeStruct((seq * rows, width), BF16),
            jax.ShapeDtypeStruct((seq * rows, hidden), BF16),
            jax.ShapeDtypeStruct((seq * rows, 2 * hidden), BF16),
            jax.ShapeDtypeStruct((2 * hidden, width), BF16),
            jax.ShapeDtypeStruct((seq * rows, width), BF16),
        ],
        in_specs=[VMEM] * 4,
        out_specs=[HBM, VMEM, VMEM, VMEM, HBM],
        scratch_shapes=gather_scratch(seq, rows, width)
        + [
            pltpu.SemaphoreType.DMA((seq // 2, 2, 2)),
            pltpu.VMEM((2, 2 * rows, width), BF16),
            pltpu.SemaphoreType.DMA((2,)),
        ],
        compiler_params=params(call_id, 56),
        cost_estimate=cost(8 * seq * rows * width * hidden, 8 * seq * rows * width),
    )(own, grad_out, feed_weight, down_weight)


def back_kernel(
    own_ref,
    weight_ref,
    attended_ref,
    hidden_ref,
    out_grad_ref,
    share_ref,
    grad_ref,
    output_kept_ref,
    output_away_ref,
    down_kept_ref,
    down_away_ref,
    came_ref,
    buf,
    send_sems,
    recv_sems,
    swap_sems,
    part,
):
    here = Place()
    here.greet(partner=True)
    rows = own_ref.shape[0]
    width = own_ref.shape[1]
    tile = 512
    swap = remote(
        share_ref.at[1 - here.dp], came_ref, swap_sems.at[0], swap_sems.at[1], here.partner()
    )
    swap.start()
    part[...] = jnp.zeros_like(part)
    share = width // (2 * here.length)

    def split(values, kept_ref, away_ref, cols):
        half = values.shape[0] // 2
        top, bottom = values[:half], values[half:]
        kept_ref[:, cols] = jnp.where(here.dp == 0, top, bottom)
        away_ref[:, cols] = jnp.where(here.dp == 0, bottom, top).astype(BF16)

    def compute(number, first):
        where = unit_rows(first, rows)
        unit = take_unit(buf, first)
        grad_ref[where, :] = dot_t(unit, weight_ref[...]).astype(BF16)
        attended = attended_ref[where, :]
        for t in range(width // tile):
            cols = slice(t * tile, (t + 1) * tile)
            part[:, cols] += t_dot(attended, unit[:, cols])
        some = pl.ds(pl.multiple_of(number * share, share), share)
        split(t_dot(hidden_ref[...], out_grad_ref[:, some]), down_kept_ref, down_away_ref, some)

    gather_units(here, own_ref, buf, send_sems, recv_sems, compute)
    for t in range(width // tile):
        cols = slice(t * tile, (t + 1) * tile)
        split(part[:, cols], output_kept_ref, output_away_ref, cols)
    swap.wait()


def gather_back(own, weight, attended, hidden, grad_out, share, call_id):
    seq = lax.axis_size("seq")
    rows, width = own.shape
    cols = weight.shape[0]
    return pl.pallas_call(
        back_kernel,
        out_shape=[
            jax.ShapeDtypeStruct((seq * rows, cols), BF16),
            jax.ShapeDtypeStruct((cols // 2, width), F32),
            jax.ShapeDtypeStruct((cols // 2, width), BF16),
            jax.ShapeDtypeStruct((hidden.shape[1] // 2, width), F32),
            jax.ShapeDtypeStruct((hidden.shape[1] // 2, width), BF16),
            jax.ShapeDtypeStruct(share.shape[1:], BF16),
        ],
        in_specs=[VMEM] * 5 + [HBM],
        out_specs=[VMEM] * 5 + [HBM],
        scratch_shapes=gather_scratch(seq, rows, width)
        + [pltpu.SemaphoreType.DMA((2,)), pltpu.VMEM((cols, width), F32)],
        compiler_params=params(call_id, 48),
        cost_estimate=cost(8 * seq * rows * width * cols, 6 * seq * rows * width),
    )(own, weight, attended, hidden, grad_out, share)


def attention_back_feed_kernel(
    block,
    q_ref,
    k_ref,
    v_ref,
    g_ref,
    att_ref,
    lse_ref,
    open_ref,
    cos_ref,
    sin_ref,
    blocks_ref,
    down_ref,
    output_ref,
    back_ref,
    feed_ref,
    down_out_ref,
    output_out_ref,
    dq_ref,
    dk_ref,
    dv_ref,
    feed_sems,
    swap_sems,
):
    here = Place()
    tile = pl.program_id(0)
    cols = q_ref.shape[1]
    feed = block_spread(here, False, blocks_ref, feed_ref, feed_sems)
    swaps = [
        remote(src, dst, swap_sems.at[0, number], swap_sems.at[1, number], here.partner())
        for number, (src, dst) in enumerate(
            [(down_ref, down_out_ref), (output_ref, output_out_ref)]
        )
    ]

    @pl.when(tile == 0)
    def _():
        here.greet_all()
        feed.start()
        for one in swaps:
            one.start()

    attention_back_kernel(
        block, q_ref, k_ref, v_ref, g_ref, att_ref, lse_ref, open_ref, dq_ref, dk_ref, dv_ref
    )
    where = pl.ds(pl.multiple_of(tile * block, block), block)
    scale = 1.0 / math.sqrt(HEAD_DIM)
    cosine = cos_ref[where, :]
    sine = sin_ref[where, :]
    back_ref[where, :cols] = rotated(dq_ref[...] * scale, cosine, -sine).astype(BF16)

    @pl.when(tile == pl.num_programs(0) - 1)
    def _():
        @pl.loop(0, pl.num_programs(0))
        def _(i):
            rows = pl.ds(pl.multiple_of(i * block, block), block)
            keys = rotated(dk_ref[rows, :], cos_ref[rows, :], -sin_ref[rows, :])
            back_ref[rows, cols : 2 * cols] = keys.astype(BF16)
            back_ref[rows, 2 * cols :] = dv_ref[rows, :].astype(BF16)

        feed.finish()
        for one in swaps:
            one.wait()


def attention_back_feed(
    queries,
    keys,
    values,
    grads,
    attended,
    log_total,
    opening,
    cosine,
    sine,
    blocks,
    down,
    output,
    block,
    call_id,
):
    seq = lax.axis_size("seq")
    rows, cols = queries.shape
    heads = cols // HEAD_DIM
    tiled = lambda width: pl.BlockSpec((block, width), lambda i: (i, 0))
    whole = pl.BlockSpec((rows, cols), lambda i: (0, 0))
    dma = pltpu.SemaphoreType.DMA
    return pl.pallas_call(
        functools.partial(attention_back_feed_kernel, block),
        grid=(rows // block,),
        in_specs=[tiled(cols), whole, whole, tiled(cols), tiled(cols), tiled(heads), tiled(1)]
        + [whole, whole, HBM, HBM, HBM],
        out_specs=[pl.BlockSpec((rows, 3 * cols), lambda i: (0, 0)), HBM, HBM, HBM],
        out_shape=[
            jax.ShapeDtypeStruct((rows, 3 * cols), BF16),
            jax.ShapeDtypeStruct((seq // 2, *blocks.shape[1:]), BF16),
            jax.ShapeDtypeStruct(down.shape, BF16),
            jax.ShapeDtypeStruct(output.shape, BF16),
        ],
        scratch_shapes=[
            pltpu.VMEM((block, cols), F32),
            pltpu.VMEM((rows, cols), F32),
            pltpu.VMEM((rows, cols), F32),
            dma((2, seq // 2)),
            dma((2, 2)),
        ],
        compiler_params=params(call_id, 60),
        cost_estimate=cost(5 * rows * rows * cols, 20 * rows * cols),
    )(
        queries,
        keys,
        values,
        grads,
        attended,
        log_total,
        opening,
        cosine,
        sine,
        blocks,
        down,
        output,
    )


def scatter_last_kernel(
    tile,
    a_ref,
    b_ref,
    normed_ref,
    blocks_ref,
    out_ref,
    feed_ref,
    qkv_ref,
    *scratch,
):
    here = Place()
    here.greet_all()
    whole, away, came, sums, feed_sems, near_sems, far_sems, swap_sems, local_sem = scratch[
        SCATTER_SCRATCH:
    ]
    feed = block_spread(here, True, blocks_ref, feed_ref, feed_sems)
    feed.start()
    own_feed = pltpu.make_async_copy(
        blocks_ref.at[here.mine], feed_ref.at[here.slot], local_sem.at[0]
    )
    own_feed.start()
    swap = remote(away, came, swap_sems.at[0], swap_sems.at[1], here.partner())
    near = block_spread(here, True, sums, qkv_ref.at[0], near_sems)
    far = block_spread(here, False, sums, qkv_ref.at[1], far_sems)
    half = away.shape[0]
    chunk = min(half, 512)
    chunks = half // chunk

    def between():
        @pl.loop(0, 2 * chunks)
        def _(i):
            first = pl.multiple_of(i * chunk, chunk)
            part = t_dot(normed_ref[:, pl.ds(first, chunk)], a_ref[...])
            whole[pl.ds(first, chunk), :] = part

        @pl.loop(0, chunks)
        def _(i):
            into = pl.ds(pl.multiple_of(i * chunk, chunk), chunk)
            first = pl.multiple_of((1 - here.dp) * half + i * chunk, chunk)
            away[into, :] = whole[pl.ds(first, chunk), :].astype(BF16)

        swap.start()

    def middle():
        swap.wait_recv()
        slab = sums.shape[1]

        @pl.loop(0, here.count)
        def _(i):
            rows = pl.ds(pl.multiple_of(i * slab, slab), slab)
            own = pl.ds(pl.multiple_of(here.dp * half + i * slab, slab), slab)
            sums[i] = (whole[own, :] + came[rows, :].astype(F32)).astype(BF16)

        qkv_ref[0, here.slot] = sums[here.mine]
        far.start()
        near.start()

    scatter_rows_of_product(
        here,
        True,
        SCATTER_PARTS,
        tile,
        a_ref,
        b_ref,
        out_ref,
        *scratch[:SCATTER_SCRATCH],
        between,
        middle,
    )
    swap.wait_send()
    near.finish()
    far.finish()
    feed.finish()
    own_feed.wait()


def product_scatter_last(a, b, normed, blocks, call_id):
    seq = lax.axis_size("seq")
    rows = a.shape[0] // seq
    width, cols = b.shape
    slab = blocks.shape[1]
    dma = pltpu.SemaphoreType.DMA
    return pl.pallas_call(
        functools.partial(scatter_last_kernel, scatter_tile(width)),
        out_shape=[
            jax.ShapeDtypeStruct((rows, width), F32),
            jax.ShapeDtypeStruct((seq // 2, *blocks.shape[1:]), BF16),
            jax.ShapeDtypeStruct((2, seq // 2, slab, cols), BF16),
        ],
        in_specs=[VMEM, VMEM, VMEM, HBM],
        out_specs=[VMEM, HBM, VMEM],
        scratch_shapes=scatter_scratch(seq, rows, width)
        + [
            pltpu.VMEM((width, cols), F32),
            pltpu.VMEM((width // 2, cols), BF16),
            pltpu.VMEM((width // 2, cols), BF16),
            pltpu.VMEM((seq, slab, cols), BF16),
            dma((2, seq // 2)),
            dma((2, seq // 2)),
            dma((2, seq // 2)),
            dma((2,)),
            dma((1,)),
        ],
        compiler_params=params(call_id, 56),
        cost_estimate=scatter_cost(a, width),
    )(a, b, normed, blocks)


def unpack_kernel(
    pair_ref,
    near_gate_ref,
    far_gate_ref,
    near_up_ref,
    far_up_ref,
    gate_ref,
    up_ref,
    qkv_ref,
    query_ref,
    key_ref,
    value_ref,
    gain_one_ref,
    gain_two_ref,
    gate_out_ref,
    up_out_ref,
    query_out_ref,
    key_out_ref,
    value_out_ref,
    one_out_ref,
    two_out_ref,
):
    pair = pair_ref[0]
    dp = lax.axis_size("dp")
    length = qkv_ref.shape[1] // 2
    slab = qkv_ref.shape[2]
    step = pl.program_id(0) * pl.num_programs(1) + pl.program_id(1)
    columns = near_gate_ref.shape[2]

    def along(grad, weight):
        return jnp.sum(grad * weight.astype(F32), axis=1, keepdims=True)

    @pl.when(step == 0)
    def _():
        two_out_ref[...] = jnp.zeros_like(two_out_ref)
        total = jnp.zeros((slab, 1), F32)
        gain = gain_one_ref[...]

        def put(out_ref, weight_ref, begin, grad):
            cols = slice(begin, begin + grad.shape[1])
            out_ref[:, cols] = grad * gain
            return along(grad, weight_ref[:, cols])

        pairs = [{}, {}]
        for line in range(length):
            rows = []
            for number in range(4):
                slot = line * 2 + number % 2
                near, far = qkv_ref[0, slot].astype(F32), qkv_ref[1, slot].astype(F32)
                rows.append(jnp.where(number // 2 == pair, near, far))
            kv = rows[0] + rows[1] + rows[2] + rows[3]
            for half in range(dp):
                cols = slice(half * HEAD_DIM, (half + 1) * HEAD_DIM)
                for number in (0, 2):
                    two = jnp.concatenate([rows[number][:, cols], rows[number + 1][:, cols]], axis=1)
                    begin = (half * length * 4 + line * 4 + number) * HEAD_DIM
                    total = total + put(query_out_ref, query_ref, begin, two)
                for kind in range(2):
                    begin = ((kind + 1) * dp + half) * HEAD_DIM
                    pairs[kind][half, line] = kv[:, begin : begin + HEAD_DIM]
        for kind, (out_ref, weight_ref) in enumerate(
            [(key_out_ref, key_ref), (value_out_ref, value_ref)]
        ):
            for half in range(dp):
                for line in range(0, length, 2):
                    two = [pairs[kind][half, line], pairs[kind][half, line + 1]]
                    begin = (half * length + line) * HEAD_DIM
                    total = total + put(
                        out_ref, weight_ref, begin, jnp.concatenate(two, axis=1)
                    )
        one_out_ref[...] = total

    total = jnp.zeros((slab, 1), F32)
    for near_ref, far_ref, weight_ref, out_ref in (
        (near_gate_ref, far_gate_ref, gate_ref, gate_out_ref),
        (near_up_ref, far_up_ref, up_ref, up_out_ref),
    ):
        for number in range(4):
            core = number % 2
            near, far = near_ref[core].astype(F32), far_ref[core].astype(F32)
            grad = jnp.where(number // 2 == pair, near, far)
            cols = slice(number * columns, (number + 1) * columns)
            total = total + along(grad, weight_ref[:, cols])
            out_ref[:, cols] = grad * gain_two_ref[...]
    two_out_ref[...] += total


def unpack(pair, near, far, gate, up, qkv, query, key, value, gain_one, gain_two):
    dp = lax.axis_size("dp")
    seq = lax.axis_size("seq")
    slab, ff = gate.shape
    length = seq // 4
    columns = ff // (dp * seq)
    whole = lambda array: pl.BlockSpec(array.shape, lambda j, i: (0,) * array.ndim)
    block = lambda kind: pl.BlockSpec((2, slab, columns), lambda j, i: (i, 0, kind * dp + j))
    tile = pl.BlockSpec((slab, 4 * columns), lambda j, i: (0, j * length + i))
    f32 = lambda array: jax.ShapeDtypeStruct(array.shape, F32)
    outs = [f32(gate), f32(up), f32(query), f32(key), f32(value), f32(gain_one), f32(gain_two)]
    return pl.pallas_call(
        unpack_kernel,
        grid=(dp, length),
        in_specs=[pl.BlockSpec(memory_space=pltpu.SMEM)]
        + [block(0), block(0), block(1), block(1), tile, tile]
        + [whole(array) for array in (qkv, query, key, value, gain_one, gain_two)],
        out_specs=[tile, tile] + [whole(array) for array in outs[2:]],
        out_shape=outs,
        compiler_params=pltpu.CompilerParams(vmem_limit_bytes=40 << 20),
        cost_estimate=cost(slab * ff, 16 * slab * ff),
    )(pair, near, far, near, far, gate, up, qkv, query, key, value, gain_one, gain_two)


def swap_dp(values):
    count = lax.axis_size("dp")
    return lax.ppermute(values, "dp", [(i, (i + 1) % count) for i in range(count)])


def gather_dp(values):
    return lax.all_gather(values, "dp", axis=0, tiled=True)


def sum_dp(partial):
    half = partial.shape[0] // 2
    mine = lax.axis_index("dp")
    away = lax.dynamic_slice_in_dim(partial, (1 - mine) * half, half, 0).astype(BF16)
    kept = lax.dynamic_slice_in_dim(partial, mine * half, half, 0)
    return kept + swap_dp(away).astype(F32)


def gather_rows(values):
    return lax.all_gather(values, "seq", axis=0, tiled=True)


def scatter_rows(partial):
    return lax.psum_scatter(partial.astype(BF16), "seq", scatter_dimension=0, tiled=True).astype(F32)


def exchange(blocks):
    return lax.all_to_all(blocks, "seq", split_axis=0, concat_axis=0, tiled=True)


def norm_factor(values):
    return lax.rsqrt(jnp.mean(values * values, axis=-1, keepdims=True) + EPS)


def norm_back(inputs, factor, gain_row, upstream):
    scaled_up = gain_row * upstream
    inner_mean = jnp.mean(scaled_up * inputs, axis=-1, keepdims=True)
    grad_in = factor * scaled_up - inputs * factor * factor * factor * inner_mean
    grad_gain = jnp.sum(upstream * inputs * factor, axis=0)
    return grad_in, grad_gain


def plain_shards(
    tokens,
    cotangent,
    doc_lengths,
    attn_gain,
    mlp_gain,
    query_weight,
    key_weight,
    value_weight,
    output_weight,
    gate_weight,
    up_weight,
    down_weight,
):
    dp = lax.axis_size("dp")
    seq = lax.axis_size("seq")
    mine = lax.axis_index("seq")
    tok_count, width = tokens.shape
    rows = tok_count * seq
    slab = query_weight.shape[0]
    share = HEAD_DIM // slab
    half_heads = HEADS // dp
    half_kv = KV_HEADS // dp
    hidden_dev = down_weight.shape[0]
    block = 512

    doc_ends = jnp.cumsum(doc_lengths[0])
    place = jnp.arange(rows, dtype=jnp.int32)
    passed = doc_ends[None, :] <= place[:, None]
    opening = jnp.max(jnp.where(passed, doc_ends[None, :], 0), axis=1)
    position = place - opening
    keeping = place < doc_ends[DOCS - 1]
    angles = position.astype(F32)[:, None] * rotary_table(HEAD_DIM)[None, :]
    cosine = jnp.cos(angles)
    sine = jnp.sin(angles)
    cos_heads = jnp.tile(cosine, (1, 2 * dp))
    sin_heads = jnp.tile(jnp.concatenate([-sine, sine], axis=1), (1, dp))
    own_keeping = lax.dynamic_slice_in_dim(keeping, mine * tok_count, tok_count, 0)

    def head_columns(weight, kept):
        split = weight.reshape(slab, dp, kept, HEAD_DIM)
        return jnp.repeat(split, seq // kept, axis=2)

    qkv_blocks = jnp.stack(
        [
            head_columns(query_weight, half_heads),
            head_columns(key_weight, half_kv),
            head_columns(value_weight, half_kv),
        ],
        axis=1,
    )
    qkv_blocks = jnp.transpose(qkv_blocks, (3, 0, 1, 2, 4)).reshape(seq * slab, 3 * dp * HEAD_DIM)
    qkv_weight = gather_dp(exchange(qkv_blocks))
    feed_blocks = jnp.stack(
        [w.reshape(slab, dp, seq, hidden_dev) for w in (gate_weight, up_weight)], axis=1
    )
    feed_blocks = jnp.transpose(feed_blocks, (3, 0, 1, 2, 4)).reshape(
        seq * slab, 2 * dp * hidden_dev
    )
    feed_weight = gather_dp(exchange(feed_blocks))
    down_own = gather_dp(down_weight)
    output_own = output_weight
    if share > 1:
        groups = [list(range(i, i + share)) for i in range(0, seq, share)]
        output_own = lax.all_gather(
            output_own, "seq", axis=0, tiled=True, axis_index_groups=groups
        )
    output_own = gather_dp(output_own)
    gains = lax.all_gather(
        jnp.stack([attn_gain, mlp_gain]), ("dp", "seq"), axis=1, tiled=True
    ).astype(F32)
    gain_one, gain_two = gains[0], gains[1]

    inputs_all = gather_rows(tokens).astype(F32)
    normed_one = (inputs_all * norm_factor(inputs_all) * gain_one).astype(BF16)
    qkv = dot(normed_one, qkv_weight)
    head_cols = dp * HEAD_DIM
    query_lin, key_lin = qkv[:, :head_cols], qkv[:, head_cols : 2 * head_cols]
    values = qkv[:, 2 * head_cols :].astype(BF16)
    scale = 1.0 / math.sqrt(HEAD_DIM)
    queries = (query_lin * cos_heads + swap_halves(query_lin) * sin_heads).astype(BF16) * BF16(scale)
    keys = (key_lin * cos_heads + swap_halves(key_lin) * sin_heads).astype(BF16)
    attended_sum, log_total = attention(queries, keys, values, opening[:, None], block)
    if share > 1:
        own_rows = ((place // tok_count) % share == mine % share)[:, None]
        attended_sum = jnp.where(own_rows, attended_sum, 0.0)
    attended = attended_sum.astype(BF16)
    inputs = tokens.astype(F32)
    middle = inputs + scatter_rows(dot(attended, output_own))

    factor_two = norm_factor(middle)
    normed_two = gather_rows((middle * factor_two * gain_two).astype(BF16))
    grad_own = jnp.where(own_keeping[:, None], cotangent, BF16(0))
    grad_out = gather_rows(grad_own)
    feed = dot(normed_two, feed_weight)
    feed_cols = dp * hidden_dev
    gate_lin, upward = feed[:, :feed_cols], feed[:, feed_cols:]
    sigmoid = jax.nn.sigmoid(gate_lin)
    hidden = (gate_lin * sigmoid * upward).astype(BF16)
    hidden_grad = dot_t(grad_out, down_own)
    gate_back = (hidden_grad * upward * sigmoid * (1.0 + gate_lin * (1.0 - sigmoid))).astype(BF16)
    up_back = (hidden_grad * gate_lin * sigmoid).astype(BF16)
    feed_back = jnp.concatenate([gate_back, up_back], axis=1)
    normed_two_grad = scatter_rows(dot_t(feed_back, feed_weight))
    mixed = middle + scatter_rows(dot(hidden, down_own))
    middle_in, gain_two_part = norm_back(middle, factor_two, gain_two, normed_two_grad)
    middle_grad = grad_own.astype(F32) + middle_in
    middle_back = gather_rows(middle_grad.astype(BF16))

    attended_grad = dot_t(middle_back, output_own).astype(BF16)
    if share > 1:
        attended_grad = jnp.where(own_rows, attended_grad, BF16(0))
    query_acc, key_acc, value_acc = attention_back(
        queries, keys, values, attended_grad, attended_sum, log_total, opening[:, None], block
    )
    query_acc = query_acc * scale
    query_back = query_acc * cos_heads - swap_halves(query_acc) * sin_heads
    key_back = key_acc * cos_heads - swap_halves(key_acc) * sin_heads
    qkv_back = jnp.concatenate([query_back, key_back, value_acc], axis=1).astype(BF16)
    normed_one_grad = scatter_rows(dot_t(qkv_back, qkv_weight))
    input_in, gain_one_part = norm_back(inputs, norm_factor(inputs), gain_one, normed_one_grad)
    token_grad = middle_grad + input_in

    feed_grad = exchange(sum_dp(t_dot(normed_two, feed_back)).astype(BF16)).astype(F32)
    feed_grad = feed_grad.reshape(seq, slab, 2, dp, hidden_dev)
    feed_grad = jnp.transpose(feed_grad, (2, 1, 3, 0, 4)).reshape(2, slab, dp * seq * hidden_dev)
    down_grad = sum_dp(t_dot(hidden, grad_out))
    output_part = t_dot(attended, middle_back)
    if share > 1:
        split = output_part.reshape(dp, share, slab, width)
        split = jnp.transpose(split, (1, 0, 2, 3)).reshape(share * dp * slab, width)
        output_part = lax.psum_scatter(
            split, "seq", scatter_dimension=0, tiled=True, axis_index_groups=groups
        )
    output_grad = sum_dp(output_part)
    qkv_grad = exchange(sum_dp(t_dot(normed_one, qkv_back)).astype(BF16)).astype(F32)
    qkv_grad = qkv_grad.reshape(seq, slab, 3, dp, HEAD_DIM)

    def own_columns(part, kept):
        summed = jnp.sum(part.reshape(kept, seq // kept, slab, dp, HEAD_DIM), axis=1)
        return jnp.transpose(summed, (1, 2, 0, 3)).reshape(slab, dp * kept * HEAD_DIM)

    query_grad = own_columns(qkv_grad[:, :, 0], half_heads)
    key_grad = own_columns(qkv_grad[:, :, 1], half_kv)
    value_grad = own_columns(qkv_grad[:, :, 2], half_kv)
    gain_parts = lax.psum(jnp.stack([gain_one_part, gain_two_part]), ("dp", "seq"))
    own = lax.axis_index("dp") * seq + mine
    gain_grads = lax.dynamic_slice_in_dim(gain_parts, own * slab, slab, 1)
    return (
        mixed,
        token_grad,
        gain_grads[0],
        gain_grads[1],
        query_grad,
        key_grad,
        value_grad,
        output_grad,
        feed_grad[0],
        feed_grad[1],
        down_grad,
    )


def shards(
    tokens,
    cotangent,
    doc_lengths,
    attn_gain,
    mlp_gain,
    query_weight,
    key_weight,
    value_weight,
    output_weight,
    gate_weight,
    up_weight,
    down_weight,
):
    dp = lax.axis_size("dp")
    seq = lax.axis_size("seq")
    data = lax.axis_index("dp")
    mine = lax.axis_index("seq")
    tok_count, width = tokens.shape
    rows = tok_count * seq
    slab = query_weight.shape[0]
    half_heads = HEADS // dp
    half_kv = KV_HEADS // dp
    hidden_dev = down_weight.shape[0]
    block = 512

    doc_ends = jnp.cumsum(doc_lengths[0])
    place = jnp.arange(rows, dtype=jnp.int32)
    passed = doc_ends[None, :] <= place[:, None]
    opening = jnp.max(jnp.where(passed, doc_ends[None, :], 0), axis=1)
    position = place - opening
    keeping = place < doc_ends[DOCS - 1]
    angles = position.astype(F32)[:, None] * rotary_table(HEAD_DIM)[None, :]
    cosine = jnp.cos(angles)
    sine = jnp.sin(angles)
    cos_heads = jnp.tile(cosine, (1, 2 * dp))
    sin_heads = jnp.tile(jnp.concatenate([-sine, sine], axis=1), (1, dp))
    own_keeping = lax.dynamic_slice_in_dim(keeping, mine * tok_count, tok_count, 0)
    grad_own = jnp.where(own_keeping[:, None], cotangent, BF16(0))
    grad_out = gather_rows(grad_own)

    gain_one = attn_gain.astype(F32)[:, None]
    gain_two = mlp_gain.astype(F32)[:, None]

    def scaled(weight, gain):
        return (weight.astype(F32) * gain).astype(BF16)

    def head_columns(weight, kept):
        split = scaled(weight, gain_one).reshape(slab, dp, kept, HEAD_DIM)
        return jnp.repeat(split, seq // kept, axis=2)

    qkv_blocks = jnp.stack(
        [
            head_columns(query_weight, half_heads),
            head_columns(key_weight, half_kv),
            head_columns(value_weight, half_kv),
        ],
        axis=1,
    )
    qkv_blocks = jnp.transpose(qkv_blocks, (3, 0, 1, 2, 4)).reshape(seq, slab, 3 * dp * HEAD_DIM)
    gate_scaled = scaled(gate_weight, gain_two)
    up_scaled = scaled(up_weight, gain_two)

    inputs = tokens.astype(F32)
    factor_one = norm_factor(inputs)
    (normed_one, queries, keys, values, qkv_weight, feed_near, down_own, output_own) = (
        gather_project(
            (inputs * factor_one).astype(BF16),
            qkv_blocks,
            gate_scaled,
            up_scaled,
            down_weight,
            output_weight,
            cos_heads,
            sin_heads,
            0,
        )
    )
    qkv_weight = qkv_weight.reshape(width, -1)
    down_own = down_own.reshape(-1, width)
    output_own = output_own.reshape(-1, width)
    attended_sum, log_total, feed_far = attention_feed(
        queries,
        keys,
        values,
        opening[:, None],
        gate_scaled,
        up_scaled,
        feed_near.shape[2],
        block,
        1,
    )
    attended = attended_sum.astype(BF16)
    attended_out, feed_weight = product_scatter_feed(attended, output_own, feed_near, feed_far, 2)
    feed_weight = feed_weight.reshape(width, -1)
    middle = inputs + attended_out

    factor_two = norm_factor(middle)
    normed_two, hidden, feed_back, feed_turned, mixed_part = gather_feed(
        (middle * factor_two).astype(BF16), grad_out, feed_weight, down_own, 3
    )
    mixed = middle + scatter_rows(mixed_part)

    def norm_input_grad(values, factor, upstream):
        inner_mean = jnp.mean(upstream * values, axis=-1, keepdims=True)
        return factor * upstream - values * factor * factor * factor * inner_mean

    normed_two_grad, feed_part = product_scatter_grad(feed_back, feed_turned, normed_two, 4)
    middle_grad = grad_own.astype(F32) + norm_input_grad(middle, factor_two, normed_two_grad)
    feed_part = feed_part.reshape(dp, width // dp, -1)
    attended_grad, output_kept, output_away, down_kept, down_away, feed_came = gather_back(
        middle_grad.astype(BF16), output_own, attended, hidden, grad_out, feed_part, 5
    )

    def both(kept, came):
        return kept.astype(F32) + came.astype(F32)

    feed_kept = lax.dynamic_index_in_dim(feed_part, data, 0, keepdims=False)
    feed_sums = both(feed_kept, feed_came).astype(BF16).reshape(seq, slab, -1)
    qkv_back, feed_grad_far, down_came, output_came = attention_back_feed(
        queries,
        keys,
        values,
        attended_grad,
        attended_sum,
        log_total,
        opening[:, None],
        cos_heads,
        sin_heads,
        feed_sums,
        down_away,
        output_away,
        block,
        6,
    )
    down_grad = both(down_kept, down_came)
    output_grad = both(output_kept, output_came)
    normed_one_grad, feed_grad_near, qkv_grads = product_scatter_last(
        qkv_back, qkv_weight, normed_one, feed_sums, 7
    )
    token_grad = middle_grad + norm_input_grad(inputs, factor_one, normed_one_grad)

    pair = ((mine // 2) % 2).reshape(1)
    gate_grad, up_grad, query_grad, key_grad, value_grad, attn_gain_grad, mlp_gain_grad = unpack(
        pair,
        feed_grad_near,
        feed_grad_far,
        gate_weight,
        up_weight,
        qkv_grads,
        query_weight,
        key_weight,
        value_weight,
        gain_one,
        gain_two,
    )
    return (
        mixed,
        token_grad,
        attn_gain_grad[:, 0],
        mlp_gain_grad[:, 0],
        query_grad,
        key_grad,
        value_grad,
        output_grad,
        gate_grad,
        up_grad,
        down_grad,
    )


def solution(mesh):
    both = P(("dp", "seq"), None)
    line = P(("dp", "seq"))
    dp, seq = mesh.shape["dp"], mesh.shape["seq"]

    def run(*args):
        tokens = args[0].shape[0]
        width = args[0].shape[1]
        suits = dp == 2 and seq % 4 == 0 and width == dp * seq * HEAD_DIM
        suits = suits and 2 * (tokens // dp) * width <= 16 << 20
        return jax.shard_map(
            shards if suits else plain_shards,
            mesh=mesh,
            in_specs=(both, both, P("dp", None), line, line) + (both,) * 7,
            out_specs=(both, both, line, line) + (both,) * 7,
            check_vma=False,
        )(*args)

    return run
```

```python
import functools
import math

import jax
import jax.numpy as jnp
from jax import lax
from jax.experimental import pallas as pl
from jax.experimental.pallas import tpu as pltpu
from jax.sharding import PartitionSpec as P

HEADS = 32
KV_HEADS = 8
HEAD_DIM = 64
DOCS = 4
EPS = 1e-05
NEG = -1e30
MESH = pl.DeviceIdType.MESH
F32 = jnp.float32
BF16 = jnp.bfloat16


def rotary_table(head_dim):
    exponent = jnp.arange(0, head_dim, 2, dtype=F32) / head_dim
    inverse = jnp.power(F32(500000.0), -exponent)
    wavelength = 2.0 * math.pi / inverse
    smooth = (8192.0 / wavelength - 1.0) / 3.0
    blended = (1.0 - smooth) * inverse / 32.0 + smooth * inverse
    return jnp.where(
        wavelength < 2048.0, inverse, jnp.where(wavelength > 8192.0, inverse / 32.0, blended)
    )


def swap_halves(values):
    rows, cols = values.shape
    halves = values.reshape(rows, cols // HEAD_DIM, 2, HEAD_DIM // 2)
    return halves[:, :, ::-1].reshape(rows, cols)


def dot(a, b):
    return jnp.dot(a, b, preferred_element_type=F32)


def dot_t(a, b):
    return lax.dot_general(a, b, (((1,), (1,)), ((), ())), preferred_element_type=F32)


def t_dot(a, b):
    return lax.dot_general(a, b, (((0,), (0,)), ((), ())), preferred_element_type=F32)


def allowed_tile(opening, q_first, k_first, shape):
    rows = q_first + lax.broadcasted_iota(jnp.int32, shape, 0)
    cols = k_first + lax.broadcasted_iota(jnp.int32, shape, 1)
    return (cols <= rows) & (cols >= opening)


def attention_kernel(block, q_ref, k_ref, v_ref, open_ref, out_ref, lse_ref):
    tile = pl.program_id(0)
    opening = open_ref[...]
    for head in range(q_ref.shape[1] // HEAD_DIM):
        lanes = slice(head * HEAD_DIM, (head + 1) * HEAD_DIM)
        query = q_ref[:, lanes]

        def step(j, carry, lanes=lanes, query=query):
            peak, total, acc = carry
            first = pl.multiple_of(j * block, block)
            scores = dot_t(query, k_ref[pl.ds(first, block), lanes])
            allowed = allowed_tile(opening, tile * block, first, scores.shape)
            scores = jnp.where(allowed, scores, NEG)
            new_peak = jnp.maximum(peak, jnp.max(scores, axis=1, keepdims=True))
            spread = jnp.where(allowed, jnp.exp(scores - new_peak), 0.0)
            fade = jnp.exp(peak - new_peak)
            total = total * fade + jnp.sum(spread, axis=1, keepdims=True)
            acc = acc * fade + dot(spread.astype(BF16), v_ref[pl.ds(first, block), lanes])
            return new_peak, total, acc

        peak, total, acc = lax.fori_loop(
            0,
            tile + 1,
            step,
            (
                jnp.full((block, 1), NEG, F32),
                jnp.zeros((block, 1), F32),
                jnp.zeros((block, HEAD_DIM), F32),
            ),
        )
        out_ref[:, lanes] = acc / total
        lse_ref[:, head : head + 1] = peak + jnp.log(total)


def attention(queries, keys, values, opening, block):
    rows, cols = queries.shape
    heads = cols // HEAD_DIM
    tiled = lambda width: pl.BlockSpec((block, width), lambda i: (i, 0))
    whole = pl.BlockSpec((rows, cols), lambda i: (0, 0))
    return pl.pallas_call(
        functools.partial(attention_kernel, block),
        grid=(rows // block,),
        in_specs=[tiled(cols), whole, whole, tiled(1)],
        out_specs=[tiled(cols), tiled(heads)],
        out_shape=[
            jax.ShapeDtypeStruct((rows, cols), F32),
            jax.ShapeDtypeStruct((rows, heads), F32),
        ],
        compiler_params=pltpu.CompilerParams(vmem_limit_bytes=48 << 20),
        cost_estimate=pl.CostEstimate(
            flops=2 * rows * rows * cols, bytes_accessed=10 * rows * cols, transcendentals=0
        ),
    )(queries, keys, values, opening)


def attention_back_kernel(
    block, q_ref, k_ref, v_ref, g_ref, att_ref, lse_ref, open_ref, dq_ref, dk_ref, dv_ref
):
    tile = pl.program_id(0)

    @pl.when(tile == 0)
    def _():
        dk_ref[...] = jnp.zeros_like(dk_ref)
        dv_ref[...] = jnp.zeros_like(dv_ref)

    opening = open_ref[...]
    for head in range(q_ref.shape[1] // HEAD_DIM):
        lanes = slice(head * HEAD_DIM, (head + 1) * HEAD_DIM)
        query = q_ref[:, lanes]
        grad = g_ref[:, lanes]
        log_total = lse_ref[:, head : head + 1]
        row_sum = jnp.sum(grad.astype(F32) * att_ref[:, lanes], axis=1, keepdims=True)

        def step(j, acc, lanes=lanes, query=query, grad=grad, log_total=log_total, row_sum=row_sum):
            first = pl.multiple_of(j * block, block)
            here = pl.ds(first, block)
            key = k_ref[here, lanes]
            scores = dot_t(query, key)
            allowed = allowed_tile(opening, tile * block, first, scores.shape)
            chance = jnp.where(allowed, jnp.exp(scores - log_total), 0.0)
            prob_grad = dot_t(grad, v_ref[here, lanes])
            score_grad = (chance * (prob_grad - row_sum)).astype(BF16)
            dk_ref[here, lanes] += t_dot(score_grad, query)
            dv_ref[here, lanes] += t_dot(chance.astype(BF16), grad)
            return acc + dot(score_grad, key)

        acc = lax.fori_loop(0, tile + 1, step, jnp.zeros((block, HEAD_DIM), F32))
        dq_ref[:, lanes] = acc


def attention_back(queries, keys, values, grads, attended, log_total, opening, block):
    rows, cols = queries.shape
    heads = cols // HEAD_DIM
    tiled = lambda width: pl.BlockSpec((block, width), lambda i: (i, 0))
    whole = pl.BlockSpec((rows, cols), lambda i: (0, 0))
    return pl.pallas_call(
        functools.partial(attention_back_kernel, block),
        grid=(rows // block,),
        in_specs=[tiled(cols), whole, whole, tiled(cols), tiled(cols), tiled(heads), tiled(1)],
        out_specs=[tiled(cols), whole, whole],
        out_shape=[jax.ShapeDtypeStruct((rows, cols), F32)] * 3,
        compiler_params=pltpu.CompilerParams(vmem_limit_bytes=60 << 20),
        cost_estimate=pl.CostEstimate(
            flops=5 * rows * rows * cols, bytes_accessed=20 * rows * cols, transcendentals=0
        ),
    )(queries, keys, values, grads, attended, log_total, opening)


def nothing():
    pass


class Place:
    def __init__(self):
        self.dp = lax.axis_index("dp")
        self.mine = lax.axis_index("seq")
        self.count = lax.axis_size("seq")
        self.length = self.count // 4
        self.line = lax.div(self.mine, 4)
        self.pair = lax.rem(lax.div(self.mine, 2), 2)
        self.core = lax.rem(self.mine, 2)
        self.slot = self.line * 2 + self.core

    def index(self, line, pair, core):
        return (line * 2 + pair) * 2 + core

    def peer(self, slot, same):
        pair = self.pair if same else 1 - self.pair
        return self.index(lax.div(slot, 2), pair, lax.rem(slot, 2))

    def device(self, line, pair, core):
        return (self.dp, self.index(line, pair, core))

    def sibling(self):
        return self.device(self.line, self.pair, 1 - self.core)

    def across(self):
        return self.device(self.line, 1 - self.pair, self.core)

    def above(self):
        return self.device(self.line + 1, self.pair, self.core)

    def below(self):
        return self.device(self.line - 1, self.pair, self.core)

    def partner(self):
        return (1 - self.dp, self.mine)

    def greet(self, partner=False):
        barrier = pltpu.get_barrier_semaphore()

        def signal(device):
            pl.semaphore_signal(barrier, inc=1, device_id=device, device_id_type=MESH)

        signal(self.sibling())
        signal(self.across())
        pl.when(self.line > 0)(lambda: signal(self.below()))
        pl.when(self.line < self.length - 1)(lambda: signal(self.above()))
        if partner:
            signal(self.partner())
        inner = (self.line > 0) & (self.line < self.length - 1)
        pl.semaphore_wait(barrier, jnp.where(inner, 4, 3) + (1 if partner else 0))

    def greet_all(self, meanwhile=nothing):
        barrier = pltpu.get_barrier_semaphore()

        def signal(device):
            pl.semaphore_signal(barrier, inc=1, device_id=device, device_id_type=MESH)

        signal(self.partner())

        @pl.loop(1, self.count)
        def _(ahead):
            signal((self.dp, lax.rem(self.mine + ahead, self.count)))

        meanwhile()
        pl.semaphore_wait(barrier, self.count)


def remote(src, dst, send_sem, recv_sem, device):
    return pltpu.make_async_remote_copy(
        src_ref=src,
        dst_ref=dst,
        send_sem=send_sem,
        recv_sem=recv_sem,
        device_id=device,
        device_id_type=MESH,
    )


class Spread:
    def __init__(self, here, same, copies):
        self.here, self.same, self.copies = here, same, copies
        self.slots = here.count // 2

    def each(self, visit):
        @pl.loop(1 if self.same else 0, self.slots)
        def _(ahead):
            slot = lax.rem(self.here.slot + ahead, self.slots)
            visit(self.here.peer(slot, self.same), slot)

    def start(self):
        def visit(peer, slot):
            for one in self.copies(peer, self.here.mine, self.here.slot, slot):
                one.start()

        self.each(visit)

    def finish(self):
        def visit(peer, slot):
            for one in self.copies(peer, peer, slot, slot):
                one.wait()

        self.each(visit)


def block_spread(here, same, blocks, into, sems):
    def copies(peer, sender, at, sem):
        return [
            remote(
                blocks.at[peer],
                into.at[at],
                sems.at[0, sem],
                sems.at[1, at],
                (here.dp, peer),
            )
        ]

    return Spread(here, same, copies)


def feed_spread(here, same, weights, into, sems):
    dp = lax.axis_size("dp")
    columns = into.shape[2] // (dp * len(weights))

    def copies(peer, sender, at, sem):
        made = []
        for kind, weight in enumerate(weights):
            for half in range(dp):
                part = kind * dp + half
                begin = pl.multiple_of((half * here.count + peer) * columns, columns)
                made.append(
                    remote(
                        weight.at[:, pl.ds(begin, columns)],
                        into.at[at, :, pl.ds(part * columns, columns)],
                        sems.at[0, sem, part],
                        sems.at[1, at, part],
                        (here.dp, peer),
                    )
                )
        return made

    return Spread(here, same, copies)


def gather_units(here, buf, send_sems, recv_sems, compute, between=None, ready=0, started=nothing):
    length = here.length
    last = length - 1
    steps = 2 * length
    mine = here.mine
    shorter = jnp.minimum(here.line, last - here.line)
    longer = jnp.where(here.line < last - here.line, 1, -1)

    def column(j):
        i = j - 1
        paired = jnp.where(i % 2 == 0, here.line - i // 2 - 1, here.line + i // 2 + 1)
        single = here.line + longer * (i - shorter + 1)
        return jnp.where(j == 0, here.line, jnp.where(i < 2 * shorter, paired, single))

    def copy(way, device, block, part):
        ref = buf.at[block, part]
        return remote(
            ref, ref, send_sems.at[way, block, part], recv_sems.at[block, part], device
        )

    def up(block, part):
        return copy(0, here.above(), block, part)

    def down(block, part):
        return copy(1, here.below(), block, part)

    def across(block, part):
        return copy(2, here.across(), block, part)

    def sideways(block, part):
        return copy(3, here.sibling(), block, part)

    def unit(number):
        in_column = (number % 2 == 1) & (number < steps - 1) | (number == 0)
        later = jnp.where(number == steps - 1, last, number // 2 - 1)
        line = column(jnp.where(in_column, (number + 1) // 2, later))
        pair = jnp.where(in_column, here.pair, 1 - here.pair)
        other = here.index(line, pair, 1 - here.core)
        sideways(other, 0).wait_recv()
        sideways(other, 1).wait_recv()
        compute(number, here.index(line, pair, 0))

    for part in range(2):
        pl.when(here.line < last)(lambda part=part: up(mine, part).start())
        pl.when(here.line > 0)(lambda part=part: down(mine, part).start())
        across(mine, part).start()
        sideways(mine, part).start()
    started()

    @pl.loop(0, steps)
    def _(step):
        part = step % 2
        far = step // 2 + 1

        @pl.when(here.line >= far)
        def _():
            block = here.index(here.line - far, here.pair, here.core)
            up(block, part).wait_recv()
            pl.when(here.line < last)(lambda: up(block, part).start())
            sideways(block, part).start()

        @pl.when(here.line + far <= last)
        def _():
            block = here.index(here.line + far, here.pair, here.core)
            down(block, part).wait_recv()
            pl.when(here.line > 0)(lambda: down(block, part).start())
            sideways(block, part).start()

        @pl.when(step + 2 < steps)
        def _():
            across(here.index(column(step // 2 + 1), here.pair, here.core), part).start()

        block = here.index(column(step // 2), 1 - here.pair, here.core)
        across(block, part).wait_recv()
        sideways(block, part).start()

        if between is None:
            unit(step)
        else:
            between(step)
            begin = jnp.where(step == ready, 0, step)
            end = jnp.where(step < ready, step, step + 1)

            @pl.loop(begin, end)
            def _(number):
                unit(number)

    @pl.loop(0, length)
    def _(line):
        for part in range(2):
            block = here.index(line, here.pair, here.core)

            @pl.when((line <= here.line) & (here.line < last))
            def _():
                up(block, part).wait_send()

            @pl.when((line >= here.line) & (here.line > 0))
            def _():
                down(block, part).wait_send()

            across(block, part).wait_send()
            sideways(block, part).wait_send()
            sideways(here.index(line, 1 - here.pair, here.core), part).wait_send()


def put_own(here, own_ref, buf):
    half = buf.shape[2]
    for part in range(2):
        buf[here.mine, part] = own_ref[pl.ds(part * half, half), :]


def gather_scratch(seq, rows, width):
    return [
        pltpu.VMEM((seq, 2, rows, width), BF16),
        pltpu.SemaphoreType.DMA((4, seq, 2)),
        pltpu.SemaphoreType.DMA((seq, 2)),
    ]


def unit_rows(first, rows):
    return pl.ds(pl.multiple_of(first * rows, 2 * rows), 2 * rows)


def take_unit(buf, first):
    blocks = buf[pl.ds(first, 2)]
    return blocks.reshape(-1, blocks.shape[-1])


class UnitStore:
    def __init__(self, buf, out_ref, sems):
        self.buf, self.out_ref, self.sems = buf, out_ref, sems

    def copies(self, number, first):
        half = self.buf.shape[2]
        made = []
        for block in range(2):
            for part in range(2):
                begin = ((first + block) * 2 + part) * half
                made.append(
                    pltpu.make_async_copy(
                        self.buf.at[first + block, part],
                        self.out_ref.at[pl.ds(pl.multiple_of(begin, half), half)],
                        self.sems.at[number, block, part],
                    )
                )
        return made

    def start(self, number, first):
        for one in self.copies(number, first):
            one.start()

    def finish(self):
        @pl.loop(0, self.sems.shape[0])
        def _(number):
            for one in self.copies(number, 0):
                one.wait()


def params(call_id, mebibytes):
    return pltpu.CompilerParams(
        collective_id=call_id, has_side_effects=True, vmem_limit_bytes=mebibytes << 20
    )


def cost(flops, bytes_accessed):
    return pl.CostEstimate(flops=flops, bytes_accessed=bytes_accessed, transcendentals=0)


VMEM = pl.BlockSpec(memory_space=pltpu.VMEM)
HBM = pl.BlockSpec(memory_space=pl.ANY)


def rotated(values, cosine, sine):
    cols = values.shape[1]
    lane = lax.broadcasted_iota(jnp.int32, values.shape, 1)
    ahead = pltpu.roll(values, cols - HEAD_DIM // 2, 1)
    behind = pltpu.roll(values, HEAD_DIM // 2, 1)
    swapped = jnp.where(lane % HEAD_DIM < HEAD_DIM // 2, ahead, behind)
    return values * cosine + swapped * sine


def project_kernel(
    lengths_ref,
    tokens_ref,
    cotangent_ref,
    query_ref,
    key_ref,
    value_ref,
    gate_ref,
    up_ref,
    gain_one_ref,
    gain_two_ref,
    freq_ref,
    down_ref,
    output_ref,
    normed_ref,
    grads_ref,
    q_ref,
    k_ref,
    v_ref,
    cos_ref,
    sin_ref,
    open_ref,
    weight_ref,
    gate_out_ref,
    up_out_ref,
    feed_ref,
    down_out_ref,
    output_out_ref,
    buf,
    send_sems,
    recv_sems,
    blocks,
    store_sems,
    near_sems,
    far_sems,
    feed_sems,
    swap_sems,
    local_sems,
    pair_sems,
):
    here = Place()
    cols = q_ref.shape[1]
    rows = tokens_ref.shape[0]
    dp = here.dp
    ends = [lengths_ref[0, 0]]
    for j in range(1, DOCS):
        ends.append(ends[-1] + lengths_ref[0, j])

    def own_rows():
        chunk = 32

        @pl.loop(0, rows // chunk)
        def _(i):
            some = pl.ds(pl.multiple_of(i * chunk, chunk), chunk)
            values = tokens_ref[some, :].astype(F32)
            factor = lax.rsqrt(jnp.mean(values * values, axis=1, keepdims=True) + EPS)
            buf[here.mine, 0, some, :] = (values * factor).astype(BF16)
            shape = (chunk, cotangent_ref.shape[1])
            place = here.mine * rows + i * chunk + lax.broadcasted_iota(jnp.int32, shape, 0)
            grads = cotangent_ref[some, :].astype(F32)
            buf[here.mine, 1, some, :] = jnp.where(place < ends[-1], grads, 0.0).astype(BF16)

    def own_blocks():
        gain = gain_one_ref[...]
        query = query_ref[...].astype(F32) * gain
        key = key_ref[...].astype(F32) * gain
        value = value_ref[...].astype(F32) * gain

        def heads(array, number, kept):
            parts = []
            for half in range(2):
                head = half * kept + number * kept // blocks.shape[0]
                parts.append(array[:, head * HEAD_DIM : (head + 1) * HEAD_DIM])
            return jnp.concatenate(parts, axis=1).astype(BF16)

        for number in range(blocks.shape[0]):
            blocks[number, :, :cols] = heads(query, number, HEADS // 2)
            blocks[number, :, cols : 2 * cols] = heads(key, number, KV_HEADS // 2)
            blocks[number, :, 2 * cols :] = heads(value, number, KV_HEADS // 2)

    here.greet_all(own_rows)

    def weight_spread(same, sems):
        def copies(peer, sender, at, sem):
            return [
                remote(
                    blocks.at[peer],
                    weight_ref.at[dp, sender],
                    sems.at[0, sem],
                    sems.at[1, at],
                    (dp, peer),
                )
            ]

        return Spread(here, same, copies)

    near = weight_spread(True, near_sems)
    far = weight_spread(False, far_sems)
    swaps = []
    for number, (src, dst) in enumerate([(down_ref, down_out_ref), (output_ref, output_out_ref)]):
        swaps.append(
            remote(src, dst.at[dp], swap_sems.at[0, number], swap_sems.at[1, number], here.partner())
        )
        swaps.append(pltpu.make_async_copy(src, dst.at[dp], local_sems.at[number]))
    feed = feed_spread(here, True, (gate_out_ref, up_out_ref), feed_ref, feed_sems)
    columns = feed_ref.shape[2] // 4
    own_feed = []
    for kind, weight in enumerate((gate_out_ref, up_out_ref)):
        for half in range(2):
            part = kind * 2 + half
            begin = pl.multiple_of((half * here.count + here.mine) * columns, columns)
            own_feed.append(
                pltpu.make_async_copy(
                    weight.at[:, pl.ds(begin, columns)],
                    feed_ref.at[here.slot, :, pl.ds(part * columns, columns)],
                    local_sems.at[2 + part],
                )
            )

    def pair_copy(source, sender):
        return remote(
            weight_ref.at[source, sender],
            weight_ref.at[source, sender],
            pair_sems.at[0, sender],
            pair_sems.at[1, sender],
            here.partner(),
        )

    def own_tables():
        chunk = 128

        @pl.loop(0, open_ref.shape[0] // chunk)
        def _(i):
            some = pl.ds(pl.multiple_of(i * chunk, chunk), chunk)
            place = i * chunk + lax.broadcasted_iota(jnp.int32, (chunk, 1), 0)
            opening = jnp.zeros((chunk, 1), jnp.int32)
            for end in ends:
                opening = jnp.where(place >= end, end, opening)
            open_ref[some, :] = opening
            angles = (place - opening).astype(F32) * freq_ref[...]
            lane = lax.broadcasted_iota(jnp.int32, angles.shape, 1)
            sine = jnp.sin(angles)
            cos_ref[some, :] = jnp.cos(angles)
            sin_ref[some, :] = jnp.where(lane % HEAD_DIM < HEAD_DIM // 2, -sine, sine)

    def started():
        own_blocks()
        far.start()
        near.start()
        weight_ref[dp, here.mine] = blocks[here.mine]
        for one in swaps:
            one.start()
        chunk = 512

        @pl.loop(0, gate_ref.shape[1] // chunk)
        def _(i):
            some = pl.ds(pl.multiple_of(i * chunk, chunk), chunk)
            gain = gain_two_ref[...]
            gate_out_ref[:, some] = (gate_ref[:, some].astype(F32) * gain).astype(BF16)
            up_out_ref[:, some] = (up_ref[:, some].astype(F32) * gain).astype(BF16)

        for one in own_feed:
            one.start()
        feed.start()
        own_tables()

    def between(step):
        @pl.when(step == 1)
        def _():
            near.finish()
            far.finish()

            @pl.loop(0, here.count)
            def _(sender):
                pair_copy(dp, sender).start()

        @pl.when(step == 3)
        def _():
            @pl.loop(0, here.count)
            def _(sender):
                pair_copy(1 - dp, sender).wait_recv()

    def stores(number, first):
        made = []
        for block in range(2):
            where = pl.ds(pl.multiple_of((first + block) * rows, rows), rows)
            for part, out_ref in enumerate((normed_ref, grads_ref)):
                made.append(
                    pltpu.make_async_copy(
                        buf.at[first + block, part],
                        out_ref.at[where],
                        store_sems.at[number, block, part],
                    )
                )
        return made

    def compute(number, first):
        for one in stores(number, first):
            one.start()
        weight = weight_ref[...].reshape(-1, weight_ref.shape[-1])
        unit = buf[pl.ds(first, 2), 0]
        qkv = dot(unit.reshape(-1, unit.shape[-1]), weight)
        where = unit_rows(first, rows)
        cosine = cos_ref[where, :]
        sine = sin_ref[where, :]
        scale = BF16(1.0 / math.sqrt(HEAD_DIM))
        q_ref[where, :] = rotated(qkv[:, :cols], cosine, sine).astype(BF16) * scale
        k_ref[where, :] = rotated(qkv[:, cols : 2 * cols], cosine, sine).astype(BF16)
        v_ref[where, :] = qkv[:, 2 * cols :].astype(BF16)

    gather_units(here, buf, send_sems, recv_sems, compute, between, 3, started)

    @pl.loop(0, here.count)
    def _(sender):
        pair_copy(dp, sender).wait_send()

    @pl.loop(0, here.count // 2)
    def _(number):
        for one in stores(number, 0):
            one.wait()

    feed.finish()
    for one in swaps + own_feed:
        one.wait()


def gather_project(
    lengths, tokens, cotangent, query, key, value, gate, up, gains, freq, down, output, call_id
):
    seq = lax.axis_size("seq")
    rows, width = tokens.shape
    cols = 2 * HEAD_DIM
    slab, ff = gate.shape
    bf16 = lambda *shape: jax.ShapeDtypeStruct(shape, BF16)
    f32 = lambda *shape: jax.ShapeDtypeStruct(shape, F32)
    all_rows = seq * rows
    dma = pltpu.SemaphoreType.DMA
    return pl.pallas_call(
        project_kernel,
        out_shape=[
            bf16(all_rows, width),
            bf16(all_rows, width),
            bf16(all_rows, cols),
            bf16(all_rows, cols),
            bf16(all_rows, cols),
            f32(all_rows, cols),
            f32(all_rows, cols),
            jax.ShapeDtypeStruct((all_rows, 1), jnp.int32),
            bf16(2, seq, slab, 3 * cols),
            bf16(slab, ff),
            bf16(slab, ff),
            bf16(seq // 2, slab, 4 * down.shape[0]),
            bf16(2, *down.shape),
            bf16(2, *output.shape),
        ],
        in_specs=[pl.BlockSpec(memory_space=pltpu.SMEM)] + [VMEM] * 10 + [HBM] * 2,
        out_specs=[HBM] * 2 + [VMEM] * 9 + [HBM] * 3,
        scratch_shapes=gather_scratch(seq, rows, width)
        + [
            pltpu.VMEM((seq, slab, 3 * cols), BF16),
            dma((seq // 2, 2, 2)),
            dma((2, seq // 2)),
            dma((2, seq // 2)),
            dma((2, seq // 2, 4)),
            dma((2, 2)),
            dma((6,)),
            dma((2, seq)),
        ],
        compiler_params=params(call_id, 56),
        cost_estimate=cost(2 * all_rows * width * 3 * cols, 8 * all_rows * width),
    )(lengths, tokens, cotangent, query, key, value, gate, up, *gains, freq, down, output)


def attention_feed_kernel(
    block,
    q_ref,
    k_ref,
    v_ref,
    open_ref,
    gate_ref,
    up_ref,
    out_ref,
    lse_ref,
    feed_ref,
    feed_sems,
):
    here = Place()
    feed = feed_spread(here, False, (gate_ref, up_ref), feed_ref, feed_sems)

    @pl.when(pl.program_id(0) == 0)
    def _():
        here.greet_all()
        feed.start()

    attention_kernel(block, q_ref, k_ref, v_ref, open_ref, out_ref, lse_ref)

    @pl.when(pl.program_id(0) == pl.num_programs(0) - 1)
    def _():
        feed.finish()


def attention_feed(queries, keys, values, opening, gate, up, feed_cols, block, call_id):
    seq = lax.axis_size("seq")
    rows, cols = queries.shape
    heads = cols // HEAD_DIM
    tiled = lambda width: pl.BlockSpec((block, width), lambda i: (i, 0))
    whole = pl.BlockSpec((rows, cols), lambda i: (0, 0))
    return pl.pallas_call(
        functools.partial(attention_feed_kernel, block),
        grid=(rows // block,),
        in_specs=[tiled(cols), whole, whole, tiled(1), HBM, HBM],
        out_specs=[tiled(cols), tiled(heads), HBM],
        out_shape=[
            jax.ShapeDtypeStruct((rows, cols), F32),
            jax.ShapeDtypeStruct((rows, heads), F32),
            jax.ShapeDtypeStruct((seq // 2, gate.shape[0], feed_cols), BF16),
        ],
        scratch_shapes=[pltpu.SemaphoreType.DMA((2, seq // 2, 4))],
        compiler_params=params(call_id, 48),
        cost_estimate=cost(2 * rows * rows * cols, 10 * rows * cols),
    )(queries, keys, values, opening, gate, up)


def scatter_rows_of_product(
    here,
    transposed,
    parts,
    tile,
    a_ref,
    b_ref,
    out_ref,
    core_out,
    core_in,
    pair_out,
    pair_in,
    line_out,
    up_in,
    down_in,
    held,
    core_sems,
    pair_sems,
    line_sems,
    up_sems,
    down_sems,
    between=nothing,
    middle=nothing,
    filler=None,
):
    length = here.length
    rows = out_ref.shape[0]
    width = out_ref.shape[1] // parts
    tiles = width // tile
    steps = length * parts

    def target(i):
        ups = length - 1 - here.line
        near = here.line < length // 2
        if_near = jnp.where(i < ups, length - 1 - i, i - ups)
        if_far = jnp.where(i < here.line, i, length - 1 - (i - here.line))
        return jnp.where(i == length - 1, here.line, jnp.where(near, if_near, if_far))

    def product(line, pair, core, part, use):
        first = pl.multiple_of(here.index(line, pair, core) * rows, rows)
        a = a_ref[pl.ds(first, rows), :]

        @pl.loop(0, tiles)
        def _(t):
            into = pl.ds(pl.multiple_of(t * tile, tile), tile)
            cols = pl.ds(pl.multiple_of(part * width + t * tile, tile), tile)
            use(dot_t(a, b_ref[cols, :]) if transposed else dot(a, b_ref[:, cols]), into)

    def core_copy(slot):
        return remote(
            core_out.at[slot],
            core_in.at[slot],
            core_sems.at[0, slot],
            core_sems.at[1, slot],
            here.sibling(),
        )

    def pair_copy(slot):
        return remote(
            pair_out.at[slot],
            pair_in.at[slot],
            pair_sems.at[0, slot],
            pair_sems.at[1, slot],
            here.across(),
        )

    def up_copy(slot, into):
        return remote(
            line_out.at[slot], up_in.at[into], line_sems.at[slot], up_sems.at[into], here.above()
        )

    def down_copy(slot, into):
        return remote(
            line_out.at[slot], down_in.at[into], line_sems.at[slot], down_sems.at[into], here.below()
        )

    def for_sibling(step, pair, slot):
        def use(value, cols):
            core_out[slot, :, cols] = value.astype(BF16)

        product(target(step // parts), pair, 1 - here.core, step % parts, use)
        core_copy(slot).start()

    for_sibling(0, 1 - here.pair, 0)

    @pl.loop(0, steps)
    def _(step):
        pl.when(step < steps - 1)(lambda: for_sibling(step + 1, 1 - here.pair, step + 1))
        core_copy(step).wait_recv()

        def use(value, cols):
            pair_out[step, :, cols] = (value + core_in[step, :, cols].astype(F32)).astype(BF16)

        product(target(step // parts), 1 - here.pair, here.core, step % parts, use)
        pair_copy(step).start()

    for_sibling(0, here.pair, steps)
    between()

    @pl.loop(0, steps)
    def _(step):
        pl.when(step < steps - 1)(lambda: for_sibling(step + 1, here.pair, steps + step + 1))
        core_copy(steps + step).wait_recv()
        line = target(step // parts)
        part = step % parts
        into = line * parts + part

        def use(value, cols):
            held[:, cols] = value + core_in[steps + step, :, cols].astype(F32)

        product(line, here.pair, here.core, part, use)
        if filler is not None:
            filler(step)
        pair_copy(step).wait_recv()
        from_above = (line <= here.line) & (here.line < length - 1)
        from_below = (line >= here.line) & (here.line > 0)
        held[...] += pair_in[step].astype(F32)

        @pl.when(from_above)
        def _():
            down_copy(0, into).wait_recv()
            held[...] += down_in[into].astype(F32)

        @pl.when(from_below)
        def _():
            up_copy(0, into).wait_recv()
            held[...] += up_in[into].astype(F32)

        @pl.when(line == here.line)
        def _():
            out_ref[:, pl.ds(pl.multiple_of(part * width, width), width)] = held[...]

        @pl.when(line < here.line)
        def _():
            line_out[step] = held[...].astype(BF16)
            down_copy(step, into).start()

        @pl.when(line > here.line)
        def _():
            line_out[step] = held[...].astype(BF16)
            up_copy(step, into).start()

        if middle is not nothing:
            pl.when(step == steps // 2)(middle)

    @pl.loop(0, steps)
    def _(step):
        core_copy(step).wait_send()
        core_copy(steps + step).wait_send()
        pair_copy(step).wait_send()
        line = target(step // parts)
        pl.when(line < here.line)(lambda: down_copy(step, 0).wait_send())
        pl.when(line > here.line)(lambda: up_copy(step, 0).wait_send())


SCATTER_PARTS = 2
SCATTER_SCRATCH = 13


def scatter_scratch(seq, rows, width):
    steps = seq // 4 * SCATTER_PARTS
    block = (rows, width // SCATTER_PARTS)
    dma = pltpu.SemaphoreType.DMA
    return [
        pltpu.VMEM((2 * steps, *block), BF16),
        pltpu.VMEM((2 * steps, *block), BF16),
        pltpu.VMEM((steps, *block), BF16),
        pltpu.VMEM((steps, *block), BF16),
        pltpu.VMEM((steps, *block), BF16),
        pltpu.VMEM((steps, *block), BF16),
        pltpu.VMEM((steps, *block), BF16),
        pltpu.VMEM(block, F32),
        dma((2, 2 * steps)),
        dma((2, steps)),
        dma((steps,)),
        dma((steps,)),
        dma((steps,)),
    ]


def scatter_tile(width):
    return min(width // SCATTER_PARTS, 512)


def scatter_cost(a, width):
    return cost(2 * a.shape[0] * a.shape[1] * width, 4 * a.shape[0] * width)


def scatter_grad_kernel(tile, a_ref, b_ref, normed_hbm, out_ref, grad_ref, *scratch):
    here = Place()
    normed_ref, fetch_sem = scratch[SCATTER_SCRATCH:]
    fetch = pltpu.make_async_copy(normed_hbm, normed_ref, fetch_sem.at[0])
    fetch.start()
    here.greet()
    cols = normed_ref.shape[1] // (here.length * SCATTER_PARTS)

    def filler(step):
        some = pl.ds(pl.multiple_of(step * cols, cols), cols)
        grad_ref[some, :] = t_dot(normed_ref[:, some], a_ref[...]).astype(BF16)

    scatter_rows_of_product(
        here,
        False,
        SCATTER_PARTS,
        tile,
        a_ref,
        b_ref,
        out_ref,
        *scratch[:SCATTER_SCRATCH],
        between=fetch.wait,
        filler=filler,
    )


def product_scatter_grad(a, b, normed, call_id):
    seq = lax.axis_size("seq")
    rows = a.shape[0] // seq
    width = b.shape[1]
    return pl.pallas_call(
        functools.partial(scatter_grad_kernel, scatter_tile(width)),
        out_shape=[
            jax.ShapeDtypeStruct((rows, width), F32),
            jax.ShapeDtypeStruct((width, a.shape[1]), BF16),
        ],
        in_specs=[VMEM, VMEM, HBM],
        out_specs=[VMEM] * 2,
        scratch_shapes=scatter_scratch(seq, rows, width)
        + [pltpu.VMEM(normed.shape, BF16), pltpu.SemaphoreType.DMA((1,))],
        compiler_params=params(call_id, 56),
        cost_estimate=scatter_cost(a, 2 * width),
    )(a, b, normed)


def scatter_feed_kernel(tile, a_ref, b_ref, near_ref, far_ref, out_ref, feed_ref, *scratch):
    here = Place()
    here.greet(partner=True)
    swap_sems, local_sems = scratch[SCATTER_SCRATCH:]
    slots = near_ref.shape[0]

    def copies(half, ref, slot):
        place = feed_ref.at[here.dp, here.peer(slot, half == 0)]
        return (
            remote(
                ref.at[slot],
                place,
                swap_sems.at[0, half, slot],
                swap_sems.at[1, half, slot],
                here.partner(),
            ),
            pltpu.make_async_copy(ref.at[slot], place, local_sems.at[half, slot]),
        )

    @pl.loop(0, slots)
    def _(slot):
        for half, ref in enumerate((near_ref, far_ref)):
            for one in copies(half, ref, slot):
                one.start()

    scatter_rows_of_product(
        here, False, SCATTER_PARTS, tile, a_ref, b_ref, out_ref, *scratch[:SCATTER_SCRATCH]
    )

    @pl.loop(0, slots)
    def _(slot):
        for half, ref in enumerate((near_ref, far_ref)):
            for one in copies(half, ref, slot):
                one.wait()


def product_scatter_feed(a, b, near, far, call_id):
    seq = lax.axis_size("seq")
    rows = a.shape[0] // seq
    width = b.shape[1]
    dma = pltpu.SemaphoreType.DMA
    return pl.pallas_call(
        functools.partial(scatter_feed_kernel, scatter_tile(width)),
        out_shape=[
            jax.ShapeDtypeStruct((rows, width), F32),
            jax.ShapeDtypeStruct((2, seq, *near.shape[1:]), BF16),
        ],
        in_specs=[VMEM, VMEM, HBM, HBM],
        out_specs=[VMEM, HBM],
        scratch_shapes=scatter_scratch(seq, rows, width)
        + [dma((2, 2, seq // 2)), dma((2, seq // 2))],
        compiler_params=params(call_id, 40),
        cost_estimate=scatter_cost(a, width),
    )(a, b, near, far)


def feed_kernel(
    own_ref,
    grad_hbm,
    feed_hbm,
    down_hbm,
    normed_ref,
    hidden_out_ref,
    back_out_ref,
    turned_out_ref,
    mixed_ref,
    buf,
    send_sems,
    recv_sems,
    store_sems,
    mixed_buf,
    mixed_sems,
    grad_ref,
    feed_ref,
    down_ref,
    hidden_ref,
    back_ref,
    turned_ref,
    fetch_sems,
    out_sems,
):
    here = Place()
    fetches = [
        pltpu.make_async_copy(src, dst, fetch_sems.at[number])
        for number, (src, dst) in enumerate(
            [(feed_hbm, feed_ref), (down_hbm, down_ref), (grad_hbm, grad_ref)]
        )
    ]
    for one in fetches:
        one.start()
    put_own(here, own_ref, buf)
    here.greet()
    rows = own_ref.shape[0]
    width = own_ref.shape[1]
    hidden = hidden_ref.shape[1]
    tile = 256
    wide = 512
    store = UnitStore(buf, normed_ref, store_sems)

    def mixed_copy(number, first):
        slot = number % 2
        return pltpu.make_async_copy(
            mixed_buf.at[slot], mixed_ref.at[unit_rows(first, rows)], mixed_sems.at[slot]
        )

    def outs(number, first):
        where = unit_rows(first, rows)
        share = width // (2 * here.length)
        some = pl.ds(pl.multiple_of(number * share, share), share)
        return [
            pltpu.make_async_copy(src, dst, out_sems.at[number, i])
            for i, (src, dst) in enumerate(
                [
                    (hidden_ref.at[where], hidden_out_ref.at[where]),
                    (back_ref.at[where], back_out_ref.at[where]),
                    (turned_ref.at[:, some], turned_out_ref.at[:, some]),
                ]
            )
        ]

    def compute(number, first):
        store.start(number, first)

        @pl.when(number == 0)
        def _():
            for one in fetches:
                one.wait()

        pl.when(number >= 2)(lambda: mixed_copy(number, first).wait())
        where = unit_rows(first, rows)
        normed = take_unit(buf, first)
        grad = grad_ref[where, :]

        @pl.loop(0, hidden // tile)
        def _(t):
            cols = pl.ds(pl.multiple_of(t * tile, tile), tile)
            later = pl.ds(pl.multiple_of(hidden + t * tile, tile), tile)
            gate = dot(normed, feed_ref[:, cols])
            upward = dot(normed, feed_ref[:, later])
            hidden_grad = dot_t(grad, down_ref[cols, :])
            sigmoid = jax.nn.sigmoid(gate)
            silu = gate * sigmoid
            hidden_ref[where, cols] = (silu * upward).astype(BF16)
            back_ref[where, cols] = (
                hidden_grad * upward * sigmoid * (1.0 + gate * (1.0 - sigmoid))
            ).astype(BF16)
            back_ref[where, later] = (hidden_grad * silu).astype(BF16)

        @pl.loop(0, width // wide)
        def _(t):
            cols = pl.ds(pl.multiple_of(t * wide, wide), wide)
            part = dot(hidden_ref[where, :], down_ref[:, cols])
            mixed_buf[number % 2, :, cols] = part.astype(BF16)

        mixed_copy(number, first).start()
        share = width // (2 * here.length)
        some = pl.ds(pl.multiple_of(number * share, share), share)
        turned_ref[:, some] = feed_ref[some, :].T
        for one in outs(number, first):
            one.start()

    gather_units(here, buf, send_sems, recv_sems, compute)

    @pl.loop(0, here.count // 2)
    def _(number):
        for one in outs(number, 0):
            one.wait()

    mixed_copy(0, 0).wait()
    mixed_copy(1, 0).wait()
    store.finish()


def gather_feed(own, grad_out, feed_weight, down_weight, call_id):
    seq = lax.axis_size("seq")
    rows, width = own.shape
    hidden = down_weight.shape[0]
    return pl.pallas_call(
        feed_kernel,
        out_shape=[
            jax.ShapeDtypeStruct((seq * rows, width), BF16),
            jax.ShapeDtypeStruct((seq * rows, hidden), BF16),
            jax.ShapeDtypeStruct((seq * rows, 2 * hidden), BF16),
            jax.ShapeDtypeStruct((2 * hidden, width), BF16),
            jax.ShapeDtypeStruct((seq * rows, width), BF16),
        ],
        in_specs=[VMEM] + [HBM] * 3,
        out_specs=[HBM] * 5,
        scratch_shapes=gather_scratch(seq, rows // 2, width)
        + [
            pltpu.SemaphoreType.DMA((seq // 2, 2, 2)),
            pltpu.VMEM((2, 2 * rows, width), BF16),
            pltpu.SemaphoreType.DMA((2,)),
            pltpu.VMEM((seq * rows, width), BF16),
            pltpu.VMEM((width, 2 * hidden), BF16),
            pltpu.VMEM((hidden, width), BF16),
            pltpu.VMEM((seq * rows, hidden), BF16),
            pltpu.VMEM((seq * rows, 2 * hidden), BF16),
            pltpu.VMEM((2 * hidden, width), BF16),
            pltpu.SemaphoreType.DMA((3,)),
            pltpu.SemaphoreType.DMA((seq // 2, 3)),
        ],
        compiler_params=params(call_id, 56),
        cost_estimate=cost(8 * seq * rows * width * hidden, 8 * seq * rows * width),
    )(own, grad_out, feed_weight, down_weight)


def back_kernel(
    own_ref,
    weight_ref,
    attended_ref,
    hidden_hbm,
    out_grad_hbm,
    share_ref,
    grad_ref,
    output_kept_ref,
    output_away_ref,
    down_kept_ref,
    down_away_ref,
    came_ref,
    buf,
    send_sems,
    recv_sems,
    swap_sems,
    part,
    hidden_ref,
    out_grad_ref,
    fetch_sems,
):
    here = Place()
    fetches = [
        pltpu.make_async_copy(hidden_hbm, hidden_ref, fetch_sems.at[0]),
        pltpu.make_async_copy(out_grad_hbm, out_grad_ref, fetch_sems.at[1]),
    ]
    for one in fetches:
        one.start()
    put_own(here, own_ref, buf)
    here.greet(partner=True)
    rows = own_ref.shape[0]
    width = own_ref.shape[1]
    tile = 512
    swap = remote(
        share_ref.at[1 - here.dp], came_ref, swap_sems.at[0], swap_sems.at[1], here.partner()
    )
    swap.start()
    part[...] = jnp.zeros_like(part)
    share = width // (2 * here.length)

    def split(values, kept_ref, away_ref, cols):
        half = values.shape[0] // 2
        top, bottom = values[:half], values[half:]
        kept_ref[:, cols] = jnp.where(here.dp == 0, top, bottom)
        away_ref[:, cols] = jnp.where(here.dp == 0, bottom, top).astype(BF16)

    def compute(number, first):
        where = unit_rows(first, rows)
        unit = take_unit(buf, first)
        grad_ref[where, :] = dot_t(unit, weight_ref[...]).astype(BF16)
        attended = attended_ref[where, :]
        for t in range(width // tile):
            cols = slice(t * tile, (t + 1) * tile)
            part[:, cols] += t_dot(attended, unit[:, cols])
        some = pl.ds(pl.multiple_of(number * share, share), share)

        @pl.when(number == 0)
        def _():
            for one in fetches:
                one.wait()

        split(t_dot(hidden_ref[...], out_grad_ref[:, some]), down_kept_ref, down_away_ref, some)

    gather_units(here, buf, send_sems, recv_sems, compute)
    for t in range(width // tile):
        cols = slice(t * tile, (t + 1) * tile)
        split(part[:, cols], output_kept_ref, output_away_ref, cols)
    swap.wait()


def gather_back(own, weight, attended, hidden, grad_out, share, call_id):
    seq = lax.axis_size("seq")
    rows, width = own.shape
    cols = weight.shape[0]
    return pl.pallas_call(
        back_kernel,
        out_shape=[
            jax.ShapeDtypeStruct((seq * rows, cols), BF16),
            jax.ShapeDtypeStruct((cols // 2, width), F32),
            jax.ShapeDtypeStruct((cols // 2, width), BF16),
            jax.ShapeDtypeStruct((hidden.shape[1] // 2, width), F32),
            jax.ShapeDtypeStruct((hidden.shape[1] // 2, width), BF16),
            jax.ShapeDtypeStruct(share.shape[1:], BF16),
        ],
        in_specs=[VMEM] * 3 + [HBM] * 3,
        out_specs=[VMEM] * 5 + [HBM],
        scratch_shapes=gather_scratch(seq, rows // 2, width)
        + [
            pltpu.SemaphoreType.DMA((2,)),
            pltpu.VMEM((cols, width), F32),
            pltpu.VMEM(hidden.shape, BF16),
            pltpu.VMEM(grad_out.shape, BF16),
            pltpu.SemaphoreType.DMA((2,)),
        ],
        compiler_params=params(call_id, 48),
        cost_estimate=cost(8 * seq * rows * width * cols, 6 * seq * rows * width),
    )(own, weight, attended, hidden, grad_out, share)


def attention_back_feed_kernel(
    block,
    q_ref,
    k_ref,
    v_ref,
    g_ref,
    att_ref,
    lse_ref,
    open_ref,
    cos_ref,
    sin_ref,
    blocks_ref,
    down_ref,
    output_ref,
    back_ref,
    feed_ref,
    down_out_ref,
    output_out_ref,
    dq_ref,
    dk_ref,
    dv_ref,
    feed_sems,
    swap_sems,
):
    here = Place()
    tile = pl.program_id(0)
    cols = q_ref.shape[1]
    feed = block_spread(here, False, blocks_ref, feed_ref, feed_sems)
    swaps = [
        remote(src, dst, swap_sems.at[0, number], swap_sems.at[1, number], here.partner())
        for number, (src, dst) in enumerate(
            [(down_ref, down_out_ref), (output_ref, output_out_ref)]
        )
    ]

    @pl.when(tile == 0)
    def _():
        here.greet_all()
        feed.start()
        for one in swaps:
            one.start()

    attention_back_kernel(
        block, q_ref, k_ref, v_ref, g_ref, att_ref, lse_ref, open_ref, dq_ref, dk_ref, dv_ref
    )
    where = pl.ds(pl.multiple_of(tile * block, block), block)
    scale = 1.0 / math.sqrt(HEAD_DIM)
    cosine = cos_ref[where, :]
    sine = sin_ref[where, :]
    back_ref[where, :cols] = rotated(dq_ref[...] * scale, cosine, -sine).astype(BF16)

    @pl.when(tile == pl.num_programs(0) - 1)
    def _():
        @pl.loop(0, pl.num_programs(0))
        def _(i):
            rows = pl.ds(pl.multiple_of(i * block, block), block)
            keys = rotated(dk_ref[rows, :], cos_ref[rows, :], -sin_ref[rows, :])
            back_ref[rows, cols : 2 * cols] = keys.astype(BF16)
            back_ref[rows, 2 * cols :] = dv_ref[rows, :].astype(BF16)

        feed.finish()
        for one in swaps:
            one.wait()


def attention_back_feed(
    queries,
    keys,
    values,
    grads,
    attended,
    log_total,
    opening,
    cosine,
    sine,
    blocks,
    down,
    output,
    block,
    call_id,
):
    seq = lax.axis_size("seq")
    rows, cols = queries.shape
    heads = cols // HEAD_DIM
    tiled = lambda width: pl.BlockSpec((block, width), lambda i: (i, 0))
    whole = pl.BlockSpec((rows, cols), lambda i: (0, 0))
    dma = pltpu.SemaphoreType.DMA
    return pl.pallas_call(
        functools.partial(attention_back_feed_kernel, block),
        grid=(rows // block,),
        in_specs=[tiled(cols), whole, whole, tiled(cols), tiled(cols), tiled(heads), tiled(1)]
        + [whole, whole, HBM, HBM, HBM],
        out_specs=[pl.BlockSpec((rows, 3 * cols), lambda i: (0, 0)), HBM, HBM, HBM],
        out_shape=[
            jax.ShapeDtypeStruct((rows, 3 * cols), BF16),
            jax.ShapeDtypeStruct((seq // 2, *blocks.shape[1:]), BF16),
            jax.ShapeDtypeStruct(down.shape, BF16),
            jax.ShapeDtypeStruct(output.shape, BF16),
        ],
        scratch_shapes=[
            pltpu.VMEM((block, cols), F32),
            pltpu.VMEM((rows, cols), F32),
            pltpu.VMEM((rows, cols), F32),
            dma((2, seq // 2)),
            dma((2, 2)),
        ],
        compiler_params=params(call_id, 60),
        cost_estimate=cost(5 * rows * rows * cols, 20 * rows * cols),
    )(
        queries,
        keys,
        values,
        grads,
        attended,
        log_total,
        opening,
        cosine,
        sine,
        blocks,
        down,
        output,
    )


def scatter_last_kernel(
    tile,
    a_ref,
    b_ref,
    normed_hbm,
    blocks_ref,
    out_ref,
    feed_ref,
    qkv_ref,
    *scratch,
):
    here = Place()
    normed_ref, kept, away, came, sums, feed_sems, near_sems, far_sems, swap_sems, local_sems = (
        scratch[SCATTER_SCRATCH:]
    )
    fetch = pltpu.make_async_copy(normed_hbm, normed_ref, local_sems.at[1])
    fetch.start()
    here.greet_all()
    feed = block_spread(here, True, blocks_ref, feed_ref, feed_sems)
    feed.start()
    own_feed = pltpu.make_async_copy(
        blocks_ref.at[here.mine], feed_ref.at[here.slot], local_sems.at[0]
    )
    own_feed.start()
    swap = remote(away, came, swap_sems.at[0], swap_sems.at[1], here.partner())
    near = block_spread(here, True, sums, qkv_ref.at[0], near_sems)
    far = block_spread(here, False, sums, qkv_ref.at[1], far_sems)
    half = away.shape[0]
    chunk = 256

    def part(dp, i):
        first = pl.multiple_of(dp * half + i * chunk, chunk)
        return t_dot(normed_ref[:, pl.ds(first, chunk)], a_ref[...])

    def between():
        fetch.wait()

        @pl.loop(0, half // chunk)
        def _(i):
            away[pl.ds(pl.multiple_of(i * chunk, chunk), chunk), :] = part(1 - here.dp, i).astype(
                BF16
            )

        swap.start()

    def filler(step):
        @pl.when(step < half // chunk)
        def _():
            kept[pl.ds(pl.multiple_of(step * chunk, chunk), chunk), :] = part(here.dp, step)

    def middle():
        swap.wait_recv()
        slab = sums.shape[1]

        @pl.loop(0, here.count)
        def _(i):
            rows = pl.ds(pl.multiple_of(i * slab, slab), slab)
            sums[i] = (kept[rows, :] + came[rows, :].astype(F32)).astype(BF16)

        qkv_ref[0, here.slot] = sums[here.mine]
        far.start()
        near.start()

    scatter_rows_of_product(
        here,
        True,
        SCATTER_PARTS,
        tile,
        a_ref,
        b_ref,
        out_ref,
        *scratch[:SCATTER_SCRATCH],
        between,
        middle,
        filler,
    )
    swap.wait_send()
    near.finish()
    far.finish()
    feed.finish()
    own_feed.wait()


def product_scatter_last(a, b, normed, blocks, call_id):
    seq = lax.axis_size("seq")
    rows = a.shape[0] // seq
    width, cols = b.shape
    slab = blocks.shape[1]
    dma = pltpu.SemaphoreType.DMA
    return pl.pallas_call(
        functools.partial(scatter_last_kernel, scatter_tile(width)),
        out_shape=[
            jax.ShapeDtypeStruct((rows, width), F32),
            jax.ShapeDtypeStruct((seq // 2, *blocks.shape[1:]), BF16),
            jax.ShapeDtypeStruct((2, seq // 2, slab, cols), BF16),
        ],
        in_specs=[VMEM, VMEM, HBM, HBM],
        out_specs=[VMEM, HBM, VMEM],
        scratch_shapes=scatter_scratch(seq, rows, width)
        + [
            pltpu.VMEM(normed.shape, BF16),
            pltpu.VMEM((width // 2, cols), F32),
            pltpu.VMEM((width // 2, cols), BF16),
            pltpu.VMEM((width // 2, cols), BF16),
            pltpu.VMEM((seq, slab, cols), BF16),
            dma((2, seq // 2)),
            dma((2, seq // 2)),
            dma((2, seq // 2)),
            dma((2,)),
            dma((2,)),
        ],
        compiler_params=params(call_id, 56),
        cost_estimate=scatter_cost(a, width),
    )(a, b, normed, blocks)


def unpack_kernel(
    pair_ref,
    near_gate_ref,
    far_gate_ref,
    near_up_ref,
    far_up_ref,
    gate_ref,
    up_ref,
    qkv_ref,
    query_ref,
    key_ref,
    value_ref,
    gain_one_ref,
    gain_two_ref,
    gate_out_ref,
    up_out_ref,
    query_out_ref,
    key_out_ref,
    value_out_ref,
    one_out_ref,
    two_out_ref,
):
    pair = pair_ref[0]
    dp = lax.axis_size("dp")
    length = qkv_ref.shape[1] // 2
    slab = qkv_ref.shape[2]
    step = pl.program_id(0) * pl.num_programs(1) + pl.program_id(1)
    columns = near_gate_ref.shape[2]

    def along(grad, weight):
        return jnp.sum(grad * weight.astype(F32), axis=1, keepdims=True)

    @pl.when(step == 0)
    def _():
        two_out_ref[...] = jnp.zeros_like(two_out_ref)
        total = jnp.zeros((slab, 1), F32)
        gain = gain_one_ref[...]

        def put(out_ref, weight_ref, begin, grad):
            cols = slice(begin, begin + grad.shape[1])
            out_ref[:, cols] = grad * gain
            return along(grad, weight_ref[:, cols])

        pairs = [{}, {}]
        for line in range(length):
            rows = []
            for number in range(4):
                slot = line * 2 + number % 2
                near, far = qkv_ref[0, slot].astype(F32), qkv_ref[1, slot].astype(F32)
                rows.append(jnp.where(number // 2 == pair, near, far))
            kv = rows[0] + rows[1] + rows[2] + rows[3]
            for half in range(dp):
                cols = slice(half * HEAD_DIM, (half + 1) * HEAD_DIM)
                for number in (0, 2):
                    two = jnp.concatenate([rows[number][:, cols], rows[number + 1][:, cols]], axis=1)
                    begin = (half * length * 4 + line * 4 + number) * HEAD_DIM
                    total = total + put(query_out_ref, query_ref, begin, two)
                for kind in range(2):
                    begin = ((kind + 1) * dp + half) * HEAD_DIM
                    pairs[kind][half, line] = kv[:, begin : begin + HEAD_DIM]
        for kind, (out_ref, weight_ref) in enumerate(
            [(key_out_ref, key_ref), (value_out_ref, value_ref)]
        ):
            for half in range(dp):
                for line in range(0, length, 2):
                    two = [pairs[kind][half, line], pairs[kind][half, line + 1]]
                    begin = (half * length + line) * HEAD_DIM
                    total = total + put(
                        out_ref, weight_ref, begin, jnp.concatenate(two, axis=1)
                    )
        one_out_ref[...] = total

    total = jnp.zeros((slab, 1), F32)
    for near_ref, far_ref, weight_ref, out_ref in (
        (near_gate_ref, far_gate_ref, gate_ref, gate_out_ref),
        (near_up_ref, far_up_ref, up_ref, up_out_ref),
    ):
        for number in range(4):
            core = number % 2
            near, far = near_ref[core].astype(F32), far_ref[core].astype(F32)
            grad = jnp.where(number // 2 == pair, near, far)
            cols = slice(number * columns, (number + 1) * columns)
            total = total + along(grad, weight_ref[:, cols])
            out_ref[:, cols] = grad * gain_two_ref[...]
    two_out_ref[...] += total


def unpack(pair, near, far, gate, up, qkv, query, key, value, gain_one, gain_two):
    dp = lax.axis_size("dp")
    seq = lax.axis_size("seq")
    slab, ff = gate.shape
    length = seq // 4
    columns = ff // (dp * seq)
    whole = lambda array: pl.BlockSpec(array.shape, lambda j, i: (0,) * array.ndim)
    block = lambda kind: pl.BlockSpec((2, slab, columns), lambda j, i: (i, 0, kind * dp + j))
    tile = pl.BlockSpec((slab, 4 * columns), lambda j, i: (0, j * length + i))
    f32 = lambda array: jax.ShapeDtypeStruct(array.shape, F32)
    outs = [f32(gate), f32(up), f32(query), f32(key), f32(value), f32(gain_one), f32(gain_two)]
    return pl.pallas_call(
        unpack_kernel,
        grid=(dp, length),
        in_specs=[pl.BlockSpec(memory_space=pltpu.SMEM)]
        + [block(0), block(0), block(1), block(1), tile, tile]
        + [whole(array) for array in (qkv, query, key, value, gain_one, gain_two)],
        out_specs=[tile, tile] + [whole(array) for array in outs[2:]],
        out_shape=outs,
        compiler_params=pltpu.CompilerParams(vmem_limit_bytes=40 << 20),
        cost_estimate=cost(slab * ff, 16 * slab * ff),
    )(pair, near, far, near, far, gate, up, qkv, query, key, value, gain_one, gain_two)


def swap_dp(values):
    count = lax.axis_size("dp")
    return lax.ppermute(values, "dp", [(i, (i + 1) % count) for i in range(count)])


def gather_dp(values):
    return lax.all_gather(values, "dp", axis=0, tiled=True)


def sum_dp(partial):
    half = partial.shape[0] // 2
    mine = lax.axis_index("dp")
    away = lax.dynamic_slice_in_dim(partial, (1 - mine) * half, half, 0).astype(BF16)
    kept = lax.dynamic_slice_in_dim(partial, mine * half, half, 0)
    return kept + swap_dp(away).astype(F32)


def gather_rows(values):
    return lax.all_gather(values, "seq", axis=0, tiled=True)


def scatter_rows(partial):
    return lax.psum_scatter(partial.astype(BF16), "seq", scatter_dimension=0, tiled=True).astype(F32)


def exchange(blocks):
    return lax.all_to_all(blocks, "seq", split_axis=0, concat_axis=0, tiled=True)


def norm_factor(values):
    return lax.rsqrt(jnp.mean(values * values, axis=-1, keepdims=True) + EPS)


def norm_back(inputs, factor, gain_row, upstream):
    scaled_up = gain_row * upstream
    inner_mean = jnp.mean(scaled_up * inputs, axis=-1, keepdims=True)
    grad_in = factor * scaled_up - inputs * factor * factor * factor * inner_mean
    grad_gain = jnp.sum(upstream * inputs * factor, axis=0)
    return grad_in, grad_gain


def plain_shards(
    tokens,
    cotangent,
    doc_lengths,
    attn_gain,
    mlp_gain,
    query_weight,
    key_weight,
    value_weight,
    output_weight,
    gate_weight,
    up_weight,
    down_weight,
):
    dp = lax.axis_size("dp")
    seq = lax.axis_size("seq")
    mine = lax.axis_index("seq")
    tok_count, width = tokens.shape
    rows = tok_count * seq
    slab = query_weight.shape[0]
    share = HEAD_DIM // slab
    half_heads = HEADS // dp
    half_kv = KV_HEADS // dp
    hidden_dev = down_weight.shape[0]
    block = 512

    doc_ends = jnp.cumsum(doc_lengths[0])
    place = jnp.arange(rows, dtype=jnp.int32)
    passed = doc_ends[None, :] <= place[:, None]
    opening = jnp.max(jnp.where(passed, doc_ends[None, :], 0), axis=1)
    position = place - opening
    keeping = place < doc_ends[DOCS - 1]
    angles = position.astype(F32)[:, None] * rotary_table(HEAD_DIM)[None, :]
    cosine = jnp.cos(angles)
    sine = jnp.sin(angles)
    cos_heads = jnp.tile(cosine, (1, 2 * dp))
    sin_heads = jnp.tile(jnp.concatenate([-sine, sine], axis=1), (1, dp))
    own_keeping = lax.dynamic_slice_in_dim(keeping, mine * tok_count, tok_count, 0)

    def head_columns(weight, kept):
        split = weight.reshape(slab, dp, kept, HEAD_DIM)
        return jnp.repeat(split, seq // kept, axis=2)

    qkv_blocks = jnp.stack(
        [
            head_columns(query_weight, half_heads),
            head_columns(key_weight, half_kv),
            head_columns(value_weight, half_kv),
        ],
        axis=1,
    )
    qkv_blocks = jnp.transpose(qkv_blocks, (3, 0, 1, 2, 4)).reshape(seq * slab, 3 * dp * HEAD_DIM)
    qkv_weight = gather_dp(exchange(qkv_blocks))
    feed_blocks = jnp.stack(
        [w.reshape(slab, dp, seq, hidden_dev) for w in (gate_weight, up_weight)], axis=1
    )
    feed_blocks = jnp.transpose(feed_blocks, (3, 0, 1, 2, 4)).reshape(
        seq * slab, 2 * dp * hidden_dev
    )
    feed_weight = gather_dp(exchange(feed_blocks))
    down_own = gather_dp(down_weight)
    output_own = output_weight
    if share > 1:
        groups = [list(range(i, i + share)) for i in range(0, seq, share)]
        output_own = lax.all_gather(
            output_own, "seq", axis=0, tiled=True, axis_index_groups=groups
        )
    output_own = gather_dp(output_own)
    gains = lax.all_gather(
        jnp.stack([attn_gain, mlp_gain]), ("dp", "seq"), axis=1, tiled=True
    ).astype(F32)
    gain_one, gain_two = gains[0], gains[1]

    inputs_all = gather_rows(tokens).astype(F32)
    normed_one = (inputs_all * norm_factor(inputs_all) * gain_one).astype(BF16)
    qkv = dot(normed_one, qkv_weight)
    head_cols = dp * HEAD_DIM
    query_lin, key_lin = qkv[:, :head_cols], qkv[:, head_cols : 2 * head_cols]
    values = qkv[:, 2 * head_cols :].astype(BF16)
    scale = 1.0 / math.sqrt(HEAD_DIM)
    queries = (query_lin * cos_heads + swap_halves(query_lin) * sin_heads).astype(BF16) * BF16(scale)
    keys = (key_lin * cos_heads + swap_halves(key_lin) * sin_heads).astype(BF16)
    attended_sum, log_total = attention(queries, keys, values, opening[:, None], block)
    if share > 1:
        own_rows = ((place // tok_count) % share == mine % share)[:, None]
        attended_sum = jnp.where(own_rows, attended_sum, 0.0)
    attended = attended_sum.astype(BF16)
    inputs = tokens.astype(F32)
    middle = inputs + scatter_rows(dot(attended, output_own))

    factor_two = norm_factor(middle)
    normed_two = gather_rows((middle * factor_two * gain_two).astype(BF16))
    grad_own = jnp.where(own_keeping[:, None], cotangent, BF16(0))
    grad_out = gather_rows(grad_own)
    feed = dot(normed_two, feed_weight)
    feed_cols = dp * hidden_dev
    gate_lin, upward = feed[:, :feed_cols], feed[:, feed_cols:]
    sigmoid = jax.nn.sigmoid(gate_lin)
    hidden = (gate_lin * sigmoid * upward).astype(BF16)
    hidden_grad = dot_t(grad_out, down_own)
    gate_back = (hidden_grad * upward * sigmoid * (1.0 + gate_lin * (1.0 - sigmoid))).astype(BF16)
    up_back = (hidden_grad * gate_lin * sigmoid).astype(BF16)
    feed_back = jnp.concatenate([gate_back, up_back], axis=1)
    normed_two_grad = scatter_rows(dot_t(feed_back, feed_weight))
    mixed = middle + scatter_rows(dot(hidden, down_own))
    middle_in, gain_two_part = norm_back(middle, factor_two, gain_two, normed_two_grad)
    middle_grad = grad_own.astype(F32) + middle_in
    middle_back = gather_rows(middle_grad.astype(BF16))

    attended_grad = dot_t(middle_back, output_own).astype(BF16)
    if share > 1:
        attended_grad = jnp.where(own_rows, attended_grad, BF16(0))
    query_acc, key_acc, value_acc = attention_back(
        queries, keys, values, attended_grad, attended_sum, log_total, opening[:, None], block
    )
    query_acc = query_acc * scale
    query_back = query_acc * cos_heads - swap_halves(query_acc) * sin_heads
    key_back = key_acc * cos_heads - swap_halves(key_acc) * sin_heads
    qkv_back = jnp.concatenate([query_back, key_back, value_acc], axis=1).astype(BF16)
    normed_one_grad = scatter_rows(dot_t(qkv_back, qkv_weight))
    input_in, gain_one_part = norm_back(inputs, norm_factor(inputs), gain_one, normed_one_grad)
    token_grad = middle_grad + input_in

    feed_grad = exchange(sum_dp(t_dot(normed_two, feed_back)).astype(BF16)).astype(F32)
    feed_grad = feed_grad.reshape(seq, slab, 2, dp, hidden_dev)
    feed_grad = jnp.transpose(feed_grad, (2, 1, 3, 0, 4)).reshape(2, slab, dp * seq * hidden_dev)
    down_grad = sum_dp(t_dot(hidden, grad_out))
    output_part = t_dot(attended, middle_back)
    if share > 1:
        split = output_part.reshape(dp, share, slab, width)
        split = jnp.transpose(split, (1, 0, 2, 3)).reshape(share * dp * slab, width)
        output_part = lax.psum_scatter(
            split, "seq", scatter_dimension=0, tiled=True, axis_index_groups=groups
        )
    output_grad = sum_dp(output_part)
    qkv_grad = exchange(sum_dp(t_dot(normed_one, qkv_back)).astype(BF16)).astype(F32)
    qkv_grad = qkv_grad.reshape(seq, slab, 3, dp, HEAD_DIM)

    def own_columns(part, kept):
        summed = jnp.sum(part.reshape(kept, seq // kept, slab, dp, HEAD_DIM), axis=1)
        return jnp.transpose(summed, (1, 2, 0, 3)).reshape(slab, dp * kept * HEAD_DIM)

    query_grad = own_columns(qkv_grad[:, :, 0], half_heads)
    key_grad = own_columns(qkv_grad[:, :, 1], half_kv)
    value_grad = own_columns(qkv_grad[:, :, 2], half_kv)
    gain_parts = lax.psum(jnp.stack([gain_one_part, gain_two_part]), ("dp", "seq"))
    own = lax.axis_index("dp") * seq + mine
    gain_grads = lax.dynamic_slice_in_dim(gain_parts, own * slab, slab, 1)
    return (
        mixed,
        token_grad,
        gain_grads[0],
        gain_grads[1],
        query_grad,
        key_grad,
        value_grad,
        output_grad,
        feed_grad[0],
        feed_grad[1],
        down_grad,
    )


def shards(
    tokens,
    cotangent,
    doc_lengths,
    attn_gain,
    mlp_gain,
    query_weight,
    key_weight,
    value_weight,
    output_weight,
    gate_weight,
    up_weight,
    down_weight,
):
    dp = lax.axis_size("dp")
    seq = lax.axis_size("seq")
    data = lax.axis_index("dp")
    mine = lax.axis_index("seq")
    tok_count, width = tokens.shape
    slab = query_weight.shape[0]
    block = 512
    gain_one = attn_gain.astype(F32)[:, None]
    gain_two = mlp_gain.astype(F32)[:, None]

    (
        normed_one,
        grad_out,
        queries,
        keys,
        values,
        cosine,
        sine,
        opening,
        qkv_weight,
        gate_scaled,
        up_scaled,
        feed_near,
        down_own,
        output_own,
    ) = gather_project(
        doc_lengths,
        tokens,
        cotangent,
        query_weight,
        key_weight,
        value_weight,
        gate_weight,
        up_weight,
        (gain_one, gain_two),
        jnp.tile(rotary_table(HEAD_DIM), 2 * dp)[None, :],
        down_weight,
        output_weight,
        0,
    )
    inputs = tokens.astype(F32)
    factor_one = norm_factor(inputs)
    own_place = mine * tok_count + jnp.arange(tok_count, dtype=jnp.int32)
    own_keeping = own_place < jnp.sum(doc_lengths)
    grad_own = jnp.where(own_keeping[:, None], cotangent, BF16(0))
    qkv_weight = qkv_weight.reshape(width, -1)
    down_own = down_own.reshape(-1, width)
    output_own = output_own.reshape(-1, width)
    attended_sum, log_total, feed_far = attention_feed(
        queries,
        keys,
        values,
        opening,
        gate_scaled,
        up_scaled,
        feed_near.shape[2],
        block,
        1,
    )
    attended = attended_sum.astype(BF16)
    attended_out, feed_weight = product_scatter_feed(attended, output_own, feed_near, feed_far, 2)
    feed_weight = feed_weight.reshape(width, -1)
    middle = inputs + attended_out

    factor_two = norm_factor(middle)
    normed_two, hidden, feed_back, feed_turned, mixed_part = gather_feed(
        (middle * factor_two).astype(BF16), grad_out, feed_weight, down_own, 3
    )
    mixed = middle + scatter_rows(mixed_part)

    def norm_input_grad(values, factor, upstream):
        inner_mean = jnp.mean(upstream * values, axis=-1, keepdims=True)
        return factor * upstream - values * factor * factor * factor * inner_mean

    normed_two_grad, feed_part = product_scatter_grad(feed_back, feed_turned, normed_two, 4)
    middle_grad = grad_own.astype(F32) + norm_input_grad(middle, factor_two, normed_two_grad)
    feed_part = feed_part.reshape(dp, width // dp, -1)
    attended_grad, output_kept, output_away, down_kept, down_away, feed_came = gather_back(
        middle_grad.astype(BF16), output_own, attended, hidden, grad_out, feed_part, 5
    )

    def both(kept, came):
        return kept.astype(F32) + came.astype(F32)

    feed_kept = lax.dynamic_index_in_dim(feed_part, data, 0, keepdims=False)
    feed_sums = both(feed_kept, feed_came).astype(BF16).reshape(seq, slab, -1)
    qkv_back, feed_grad_far, down_came, output_came = attention_back_feed(
        queries,
        keys,
        values,
        attended_grad,
        attended_sum,
        log_total,
        opening,
        cosine,
        sine,
        feed_sums,
        down_away,
        output_away,
        block,
        6,
    )
    down_grad = both(down_kept, down_came)
    output_grad = both(output_kept, output_came)
    normed_one_grad, feed_grad_near, qkv_grads = product_scatter_last(
        qkv_back, qkv_weight, normed_one, feed_sums, 7
    )
    token_grad = middle_grad + norm_input_grad(inputs, factor_one, normed_one_grad)

    pair = ((mine // 2) % 2).reshape(1)
    gate_grad, up_grad, query_grad, key_grad, value_grad, attn_gain_grad, mlp_gain_grad = unpack(
        pair,
        feed_grad_near,
        feed_grad_far,
        gate_weight,
        up_weight,
        qkv_grads,
        query_weight,
        key_weight,
        value_weight,
        gain_one,
        gain_two,
    )
    return (
        mixed,
        token_grad,
        attn_gain_grad[:, 0],
        mlp_gain_grad[:, 0],
        query_grad,
        key_grad,
        value_grad,
        output_grad,
        gate_grad,
        up_grad,
        down_grad,
    )


def solution(mesh):
    both = P(("dp", "seq"), None)
    line = P(("dp", "seq"))
    dp, seq = mesh.shape["dp"], mesh.shape["seq"]

    def run(*args):
        tokens = args[0].shape[0]
        width = args[0].shape[1]
        suits = dp == 2 and seq % 4 == 0 and width == dp * seq * HEAD_DIM
        suits = suits and 2 * (tokens // dp) * width <= 16 << 20
        return jax.shard_map(
            shards if suits else plain_shards,
            mesh=mesh,
            in_specs=(both, both, P("dp", None), line, line) + (both,) * 7,
            out_specs=(both, both, line, line) + (both,) * 7,
            check_vma=False,
        )(*args)

    return run
```

```python
import functools
import math

import jax
import jax.numpy as jnp
from jax import lax
from jax.experimental import pallas as pl
from jax.experimental.pallas import tpu as pltpu
from jax.sharding import PartitionSpec as P

HEADS = 32
KV_HEADS = 8
HEAD_DIM = 64
DOCS = 4
EPS = 1e-05
NEG = -1e30
MESH = pl.DeviceIdType.MESH
F32 = jnp.float32
BF16 = jnp.bfloat16


def rotary_table(head_dim):
    exponent = jnp.arange(0, head_dim, 2, dtype=F32) / head_dim
    inverse = jnp.power(F32(500000.0), -exponent)
    wavelength = 2.0 * math.pi / inverse
    smooth = (8192.0 / wavelength - 1.0) / 3.0
    blended = (1.0 - smooth) * inverse / 32.0 + smooth * inverse
    return jnp.where(
        wavelength < 2048.0, inverse, jnp.where(wavelength > 8192.0, inverse / 32.0, blended)
    )


def swap_halves(values):
    rows, cols = values.shape
    halves = values.reshape(rows, cols // HEAD_DIM, 2, HEAD_DIM // 2)
    return halves[:, :, ::-1].reshape(rows, cols)


def dot(a, b):
    return jnp.dot(a, b, preferred_element_type=F32)


def dot_t(a, b):
    return lax.dot_general(a, b, (((1,), (1,)), ((), ())), preferred_element_type=F32)


def t_dot(a, b):
    return lax.dot_general(a, b, (((0,), (0,)), ((), ())), preferred_element_type=F32)


def allowed_tile(opening, q_first, k_first, shape):
    rows = q_first + lax.broadcasted_iota(jnp.int32, shape, 0)
    cols = k_first + lax.broadcasted_iota(jnp.int32, shape, 1)
    return (cols <= rows) & (cols >= opening)


def attention_kernel(block, q_ref, k_ref, v_ref, open_ref, out_ref, lse_ref):
    tile = pl.program_id(0)
    opening = open_ref[...]
    for head in range(q_ref.shape[1] // HEAD_DIM):
        lanes = slice(head * HEAD_DIM, (head + 1) * HEAD_DIM)
        query = q_ref[:, lanes]

        def step(j, carry, lanes=lanes, query=query):
            peak, total, acc = carry
            first = pl.multiple_of(j * block, block)
            scores = dot_t(query, k_ref[pl.ds(first, block), lanes])
            allowed = allowed_tile(opening, tile * block, first, scores.shape)
            scores = jnp.where(allowed, scores, NEG)
            new_peak = jnp.maximum(peak, jnp.max(scores, axis=1, keepdims=True))
            spread = jnp.where(allowed, jnp.exp(scores - new_peak), 0.0)
            fade = jnp.exp(peak - new_peak)
            total = total * fade + jnp.sum(spread, axis=1, keepdims=True)
            acc = acc * fade + dot(spread.astype(BF16), v_ref[pl.ds(first, block), lanes])
            return new_peak, total, acc

        peak, total, acc = lax.fori_loop(
            0,
            tile + 1,
            step,
            (
                jnp.full((block, 1), NEG, F32),
                jnp.zeros((block, 1), F32),
                jnp.zeros((block, HEAD_DIM), F32),
            ),
        )
        out_ref[:, lanes] = acc / total
        lse_ref[:, head : head + 1] = peak + jnp.log(total)


def attention(queries, keys, values, opening, block):
    rows, cols = queries.shape
    heads = cols // HEAD_DIM
    tiled = lambda width: pl.BlockSpec((block, width), lambda i: (i, 0))
    whole = pl.BlockSpec((rows, cols), lambda i: (0, 0))
    return pl.pallas_call(
        functools.partial(attention_kernel, block),
        grid=(rows // block,),
        in_specs=[tiled(cols), whole, whole, tiled(1)],
        out_specs=[tiled(cols), tiled(heads)],
        out_shape=[
            jax.ShapeDtypeStruct((rows, cols), F32),
            jax.ShapeDtypeStruct((rows, heads), F32),
        ],
        compiler_params=pltpu.CompilerParams(vmem_limit_bytes=48 << 20),
        cost_estimate=pl.CostEstimate(
            flops=2 * rows * rows * cols, bytes_accessed=10 * rows * cols, transcendentals=0
        ),
    )(queries, keys, values, opening)


def attention_back_kernel(
    block, q_ref, k_ref, v_ref, g_ref, att_ref, lse_ref, open_ref, dq_ref, dk_ref, dv_ref
):
    tile = pl.program_id(0)

    @pl.when(tile == 0)
    def _():
        dk_ref[...] = jnp.zeros_like(dk_ref)
        dv_ref[...] = jnp.zeros_like(dv_ref)

    opening = open_ref[...]
    for head in range(q_ref.shape[1] // HEAD_DIM):
        lanes = slice(head * HEAD_DIM, (head + 1) * HEAD_DIM)
        query = q_ref[:, lanes]
        grad = g_ref[:, lanes]
        log_total = lse_ref[:, head : head + 1]
        row_sum = jnp.sum(grad.astype(F32) * att_ref[:, lanes], axis=1, keepdims=True)

        def step(j, acc, lanes=lanes, query=query, grad=grad, log_total=log_total, row_sum=row_sum):
            first = pl.multiple_of(j * block, block)
            here = pl.ds(first, block)
            key = k_ref[here, lanes]
            scores = dot_t(query, key)
            allowed = allowed_tile(opening, tile * block, first, scores.shape)
            chance = jnp.where(allowed, jnp.exp(scores - log_total), 0.0)
            prob_grad = dot_t(grad, v_ref[here, lanes])
            score_grad = (chance * (prob_grad - row_sum)).astype(BF16)
            dk_ref[here, lanes] += t_dot(score_grad, query)
            dv_ref[here, lanes] += t_dot(chance.astype(BF16), grad)
            return acc + dot(score_grad, key)

        acc = lax.fori_loop(0, tile + 1, step, jnp.zeros((block, HEAD_DIM), F32))
        dq_ref[:, lanes] = acc


def attention_back(queries, keys, values, grads, attended, log_total, opening, block):
    rows, cols = queries.shape
    heads = cols // HEAD_DIM
    tiled = lambda width: pl.BlockSpec((block, width), lambda i: (i, 0))
    whole = pl.BlockSpec((rows, cols), lambda i: (0, 0))
    return pl.pallas_call(
        functools.partial(attention_back_kernel, block),
        grid=(rows // block,),
        in_specs=[tiled(cols), whole, whole, tiled(cols), tiled(cols), tiled(heads), tiled(1)],
        out_specs=[tiled(cols), whole, whole],
        out_shape=[jax.ShapeDtypeStruct((rows, cols), F32)] * 3,
        compiler_params=pltpu.CompilerParams(vmem_limit_bytes=60 << 20),
        cost_estimate=pl.CostEstimate(
            flops=5 * rows * rows * cols, bytes_accessed=20 * rows * cols, transcendentals=0
        ),
    )(queries, keys, values, grads, attended, log_total, opening)


def nothing():
    pass


class Place:
    def __init__(self):
        self.dp = lax.axis_index("dp")
        self.mine = lax.axis_index("seq")
        self.count = lax.axis_size("seq")
        self.length = self.count // 4
        self.line = lax.div(self.mine, 4)
        self.pair = lax.rem(lax.div(self.mine, 2), 2)
        self.core = lax.rem(self.mine, 2)
        self.slot = self.line * 2 + self.core

    def index(self, line, pair, core):
        return (line * 2 + pair) * 2 + core

    def peer(self, slot, same):
        pair = self.pair if same else 1 - self.pair
        return self.index(lax.div(slot, 2), pair, lax.rem(slot, 2))

    def device(self, line, pair, core):
        return (self.dp, self.index(line, pair, core))

    def sibling(self):
        return self.device(self.line, self.pair, 1 - self.core)

    def across(self):
        return self.device(self.line, 1 - self.pair, self.core)

    def above(self):
        return self.device(self.line + 1, self.pair, self.core)

    def below(self):
        return self.device(self.line - 1, self.pair, self.core)

    def partner(self):
        return (1 - self.dp, self.mine)

    def greet(self, partner=False):
        barrier = pltpu.get_barrier_semaphore()

        def signal(device):
            pl.semaphore_signal(barrier, inc=1, device_id=device, device_id_type=MESH)

        signal(self.sibling())
        signal(self.across())
        pl.when(self.line > 0)(lambda: signal(self.below()))
        pl.when(self.line < self.length - 1)(lambda: signal(self.above()))
        if partner:
            signal(self.partner())
        inner = (self.line > 0) & (self.line < self.length - 1)
        pl.semaphore_wait(barrier, jnp.where(inner, 4, 3) + (1 if partner else 0))

    def greet_all(self, meanwhile=nothing):
        barrier = pltpu.get_barrier_semaphore()

        def signal(device):
            pl.semaphore_signal(barrier, inc=1, device_id=device, device_id_type=MESH)

        signal(self.partner())

        @pl.loop(1, self.count)
        def _(ahead):
            signal((self.dp, lax.rem(self.mine + ahead, self.count)))

        meanwhile()
        pl.semaphore_wait(barrier, self.count)


def remote(src, dst, send_sem, recv_sem, device):
    return pltpu.make_async_remote_copy(
        src_ref=src,
        dst_ref=dst,
        send_sem=send_sem,
        recv_sem=recv_sem,
        device_id=device,
        device_id_type=MESH,
    )


class Spread:
    def __init__(self, here, same, copies):
        self.here, self.same, self.copies = here, same, copies
        self.slots = here.count // 2

    def each(self, visit):
        @pl.loop(1 if self.same else 0, self.slots)
        def _(ahead):
            slot = lax.rem(self.here.slot + ahead, self.slots)
            visit(self.here.peer(slot, self.same), slot)

    def start(self):
        def visit(peer, slot):
            for one in self.copies(peer, self.here.mine, self.here.slot, slot):
                one.start()

        self.each(visit)

    def finish(self):
        def visit(peer, slot):
            for one in self.copies(peer, peer, slot, slot):
                one.wait()

        self.each(visit)


def block_spread(here, same, blocks, into, sems):
    def copies(peer, sender, at, sem):
        return [
            remote(
                blocks.at[peer],
                into.at[at],
                sems.at[0, sem],
                sems.at[1, at],
                (here.dp, peer),
            )
        ]

    return Spread(here, same, copies)


def feed_spread(here, same, weights, into, sems):
    dp = lax.axis_size("dp")
    columns = into.shape[2] // (dp * len(weights))

    def copies(peer, sender, at, sem):
        made = []
        for kind, weight in enumerate(weights):
            for half in range(dp):
                part = kind * dp + half
                begin = pl.multiple_of((half * here.count + peer) * columns, columns)
                made.append(
                    remote(
                        weight.at[:, pl.ds(begin, columns)],
                        into.at[at, :, pl.ds(part * columns, columns)],
                        sems.at[0, sem, part],
                        sems.at[1, at, part],
                        (here.dp, peer),
                    )
                )
        return made

    return Spread(here, same, copies)


def gather_units(here, buf, send_sems, recv_sems, compute, between=None, ready=0, started=nothing):
    length = here.length
    last = length - 1
    steps = 2 * length
    mine = here.mine
    shorter = jnp.minimum(here.line, last - here.line)
    longer = jnp.where(here.line < last - here.line, 1, -1)

    def column(j):
        i = j - 1
        paired = jnp.where(i % 2 == 0, here.line - i // 2 - 1, here.line + i // 2 + 1)
        single = here.line + longer * (i - shorter + 1)
        return jnp.where(j == 0, here.line, jnp.where(i < 2 * shorter, paired, single))

    def copy(way, device, block, part):
        ref = buf.at[block, part]
        return remote(
            ref, ref, send_sems.at[way, block, part], recv_sems.at[block, part], device
        )

    def up(block, part):
        return copy(0, here.above(), block, part)

    def down(block, part):
        return copy(1, here.below(), block, part)

    def across(block, part):
        return copy(2, here.across(), block, part)

    def sideways(block, part):
        return copy(3, here.sibling(), block, part)

    def unit(number):
        in_column = (number % 2 == 1) & (number < steps - 1) | (number == 0)
        later = jnp.where(number == steps - 1, last, number // 2 - 1)
        line = column(jnp.where(in_column, (number + 1) // 2, later))
        pair = jnp.where(in_column, here.pair, 1 - here.pair)
        other = here.index(line, pair, 1 - here.core)
        sideways(other, 0).wait_recv()
        sideways(other, 1).wait_recv()
        compute(number, here.index(line, pair, 0))

    for part in range(2):
        pl.when(here.line < last)(lambda part=part: up(mine, part).start())
        pl.when(here.line > 0)(lambda part=part: down(mine, part).start())
        across(mine, part).start()
        sideways(mine, part).start()
    started()

    @pl.loop(0, steps)
    def _(step):
        part = step % 2
        far = step // 2 + 1

        @pl.when(here.line >= far)
        def _():
            block = here.index(here.line - far, here.pair, here.core)
            up(block, part).wait_recv()
            pl.when(here.line < last)(lambda: up(block, part).start())
            sideways(block, part).start()

        @pl.when(here.line + far <= last)
        def _():
            block = here.index(here.line + far, here.pair, here.core)
            down(block, part).wait_recv()
            pl.when(here.line > 0)(lambda: down(block, part).start())
            sideways(block, part).start()

        @pl.when(step + 2 < steps)
        def _():
            across(here.index(column(step // 2 + 1), here.pair, here.core), part).start()

        block = here.index(column(step // 2), 1 - here.pair, here.core)
        across(block, part).wait_recv()
        sideways(block, part).start()

        if between is None:
            unit(step)
        else:
            between(step)
            begin = jnp.maximum(2 * (step - ready), 0)
            end = jnp.maximum(2 * (step + 1 - ready), 0)

            @pl.loop(begin, end)
            def _(number):
                unit(number)

    @pl.loop(0, length)
    def _(line):
        for part in range(2):
            block = here.index(line, here.pair, here.core)

            @pl.when((line <= here.line) & (here.line < last))
            def _():
                up(block, part).wait_send()

            @pl.when((line >= here.line) & (here.line > 0))
            def _():
                down(block, part).wait_send()

            across(block, part).wait_send()
            sideways(block, part).wait_send()
            sideways(here.index(line, 1 - here.pair, here.core), part).wait_send()


def put_own(here, own_ref, buf):
    half = buf.shape[2]
    for part in range(2):
        buf[here.mine, part] = own_ref[pl.ds(part * half, half), :]


def gather_scratch(seq, rows, width):
    return [
        pltpu.VMEM((seq, 2, rows, width), BF16),
        pltpu.SemaphoreType.DMA((4, seq, 2)),
        pltpu.SemaphoreType.DMA((seq, 2)),
    ]


def unit_rows(first, rows):
    return pl.ds(pl.multiple_of(first * rows, 2 * rows), 2 * rows)


def take_unit(buf, first):
    blocks = buf[pl.ds(first, 2)]
    return blocks.reshape(-1, blocks.shape[-1])


class UnitStore:
    def __init__(self, buf, out_ref, sems):
        self.buf, self.out_ref, self.sems = buf, out_ref, sems

    def copies(self, number, first):
        half = self.buf.shape[2]
        made = []
        for block in range(2):
            for part in range(2):
                begin = ((first + block) * 2 + part) * half
                made.append(
                    pltpu.make_async_copy(
                        self.buf.at[first + block, part],
                        self.out_ref.at[pl.ds(pl.multiple_of(begin, half), half)],
                        self.sems.at[number, block, part],
                    )
                )
        return made

    def start(self, number, first):
        for one in self.copies(number, first):
            one.start()

    def finish(self):
        @pl.loop(0, self.sems.shape[0])
        def _(number):
            for one in self.copies(number, 0):
                one.wait()


def params(call_id, mebibytes):
    return pltpu.CompilerParams(
        collective_id=call_id, has_side_effects=True, vmem_limit_bytes=mebibytes << 20
    )


def cost(flops, bytes_accessed):
    return pl.CostEstimate(flops=flops, bytes_accessed=bytes_accessed, transcendentals=0)


VMEM = pl.BlockSpec(memory_space=pltpu.VMEM)
HBM = pl.BlockSpec(memory_space=pl.ANY)


def rotated(values, cosine, sine):
    cols = values.shape[1]
    lane = lax.broadcasted_iota(jnp.int32, values.shape, 1)
    ahead = pltpu.roll(values, cols - HEAD_DIM // 2, 1)
    behind = pltpu.roll(values, HEAD_DIM // 2, 1)
    swapped = jnp.where(lane % HEAD_DIM < HEAD_DIM // 2, ahead, behind)
    return values * cosine + swapped * sine


def project_kernel(
    lengths_ref,
    tokens_ref,
    cotangent_ref,
    query_ref,
    key_ref,
    value_ref,
    gate_ref,
    up_ref,
    gain_one_ref,
    gain_two_ref,
    freq_ref,
    down_ref,
    output_ref,
    normed_ref,
    grads_ref,
    q_ref,
    k_ref,
    v_ref,
    cos_ref,
    sin_ref,
    open_ref,
    weight_ref,
    gate_out_ref,
    up_out_ref,
    feed_ref,
    down_out_ref,
    output_out_ref,
    buf,
    send_sems,
    recv_sems,
    blocks,
    store_sems,
    near_sems,
    far_sems,
    feed_sems,
    swap_sems,
    local_sems,
    pair_sems,
):
    here = Place()
    cols = q_ref.shape[1]
    rows = tokens_ref.shape[0]
    dp = here.dp
    ends = [lengths_ref[0, 0]]
    for j in range(1, DOCS):
        ends.append(ends[-1] + lengths_ref[0, j])

    def own_rows():
        chunk = 32

        @pl.loop(0, rows // chunk)
        def _(i):
            some = pl.ds(pl.multiple_of(i * chunk, chunk), chunk)
            values = tokens_ref[some, :].astype(F32)
            factor = lax.rsqrt(jnp.mean(values * values, axis=1, keepdims=True) + EPS)
            buf[here.mine, 0, some, :] = (values * factor).astype(BF16)
            shape = (chunk, cotangent_ref.shape[1])
            place = here.mine * rows + i * chunk + lax.broadcasted_iota(jnp.int32, shape, 0)
            grads = cotangent_ref[some, :].astype(F32)
            buf[here.mine, 1, some, :] = jnp.where(place < ends[-1], grads, 0.0).astype(BF16)

    def own_blocks():
        gain = gain_one_ref[...]
        query = query_ref[...].astype(F32) * gain
        key = key_ref[...].astype(F32) * gain
        value = value_ref[...].astype(F32) * gain

        def heads(array, number, kept):
            parts = []
            for half in range(2):
                head = half * kept + number * kept // blocks.shape[0]
                parts.append(array[:, head * HEAD_DIM : (head + 1) * HEAD_DIM])
            return jnp.concatenate(parts, axis=1).astype(BF16)

        for number in range(blocks.shape[0]):
            blocks[number, :, :cols] = heads(query, number, HEADS // 2)
            blocks[number, :, cols : 2 * cols] = heads(key, number, KV_HEADS // 2)
            blocks[number, :, 2 * cols :] = heads(value, number, KV_HEADS // 2)

    def own_parts():
        own_blocks()
        own_rows()

    here.greet_all(own_parts)

    def weight_spread(same, sems):
        def copies(peer, sender, at, sem):
            return [
                remote(
                    blocks.at[peer],
                    weight_ref.at[dp, sender],
                    sems.at[0, sem],
                    sems.at[1, at],
                    (dp, peer),
                )
            ]

        return Spread(here, same, copies)

    near = weight_spread(True, near_sems)
    far = weight_spread(False, far_sems)
    swaps = []
    for number, (src, dst) in enumerate([(down_ref, down_out_ref), (output_ref, output_out_ref)]):
        swaps.append(
            remote(src, dst.at[dp], swap_sems.at[0, number], swap_sems.at[1, number], here.partner())
        )
        swaps.append(pltpu.make_async_copy(src, dst.at[dp], local_sems.at[number]))
    feed = feed_spread(here, True, (gate_out_ref, up_out_ref), feed_ref, feed_sems)
    columns = feed_ref.shape[2] // 4
    own_feed = []
    for kind, weight in enumerate((gate_out_ref, up_out_ref)):
        for half in range(2):
            part = kind * 2 + half
            begin = pl.multiple_of((half * here.count + here.mine) * columns, columns)
            own_feed.append(
                pltpu.make_async_copy(
                    weight.at[:, pl.ds(begin, columns)],
                    feed_ref.at[here.slot, :, pl.ds(part * columns, columns)],
                    local_sems.at[2 + part],
                )
            )

    def pair_copy(source, sender):
        return remote(
            weight_ref.at[source, sender],
            weight_ref.at[source, sender],
            pair_sems.at[0, sender],
            pair_sems.at[1, sender],
            here.partner(),
        )

    def own_tables():
        chunk = 128

        @pl.loop(0, open_ref.shape[0] // chunk)
        def _(i):
            some = pl.ds(pl.multiple_of(i * chunk, chunk), chunk)
            place = i * chunk + lax.broadcasted_iota(jnp.int32, (chunk, 1), 0)
            opening = jnp.zeros((chunk, 1), jnp.int32)
            for end in ends:
                opening = jnp.where(place >= end, end, opening)
            open_ref[some, :] = opening
            angles = (place - opening).astype(F32) * freq_ref[...]
            lane = lax.broadcasted_iota(jnp.int32, angles.shape, 1)
            sine = jnp.sin(angles)
            cos_ref[some, :] = jnp.cos(angles)
            sin_ref[some, :] = jnp.where(lane % HEAD_DIM < HEAD_DIM // 2, -sine, sine)

    def started():
        weight_ref[dp, here.mine] = blocks[here.mine]
        for one in swaps:
            one.start()
        chunk = 512

        @pl.loop(0, gate_ref.shape[1] // chunk)
        def _(i):
            some = pl.ds(pl.multiple_of(i * chunk, chunk), chunk)
            gain = gain_two_ref[...]
            gate_out_ref[:, some] = (gate_ref[:, some].astype(F32) * gain).astype(BF16)
            up_out_ref[:, some] = (up_ref[:, some].astype(F32) * gain).astype(BF16)

        for one in own_feed:
            one.start()
        feed.start()
        own_tables()

    def between(step):
        @pl.when(step == 2)
        def _():
            near.finish()
            far.finish()

            @pl.loop(0, here.count)
            def _(sender):
                pair_copy(dp, sender).start()

        @pl.when(step == 4)
        def _():
            @pl.loop(0, here.count)
            def _(sender):
                pair_copy(1 - dp, sender).wait_recv()

    def stores(number, first):
        made = []
        for block in range(2):
            where = pl.ds(pl.multiple_of((first + block) * rows, rows), rows)
            for part, out_ref in enumerate((normed_ref, grads_ref)):
                made.append(
                    pltpu.make_async_copy(
                        buf.at[first + block, part],
                        out_ref.at[where],
                        store_sems.at[number, block, part],
                    )
                )
        return made

    def compute(number, first):
        for one in stores(number, first):
            one.start()
        weight = weight_ref[...].reshape(-1, weight_ref.shape[-1])
        unit = buf[pl.ds(first, 2), 0]
        qkv = dot(unit.reshape(-1, unit.shape[-1]), weight)
        where = unit_rows(first, rows)
        cosine = cos_ref[where, :]
        sine = sin_ref[where, :]
        scale = BF16(1.0 / math.sqrt(HEAD_DIM))
        q_ref[where, :] = rotated(qkv[:, :cols], cosine, sine).astype(BF16) * scale
        k_ref[where, :] = rotated(qkv[:, cols : 2 * cols], cosine, sine).astype(BF16)
        v_ref[where, :] = qkv[:, 2 * cols :].astype(BF16)

    far.start()
    near.start()
    gather_units(here, buf, send_sems, recv_sems, compute, between, here.length, started)

    @pl.loop(0, here.count)
    def _(sender):
        pair_copy(dp, sender).wait_send()

    @pl.loop(0, here.count // 2)
    def _(number):
        for one in stores(number, 0):
            one.wait()

    feed.finish()
    for one in swaps + own_feed:
        one.wait()


def gather_project(
    lengths, tokens, cotangent, query, key, value, gate, up, gains, freq, down, output, call_id
):
    seq = lax.axis_size("seq")
    rows, width = tokens.shape
    cols = 2 * HEAD_DIM
    slab, ff = gate.shape
    bf16 = lambda *shape: jax.ShapeDtypeStruct(shape, BF16)
    f32 = lambda *shape: jax.ShapeDtypeStruct(shape, F32)
    all_rows = seq * rows
    dma = pltpu.SemaphoreType.DMA
    return pl.pallas_call(
        project_kernel,
        out_shape=[
            bf16(all_rows, width),
            bf16(all_rows, width),
            bf16(all_rows, cols),
            bf16(all_rows, cols),
            bf16(all_rows, cols),
            f32(all_rows, cols),
            f32(all_rows, cols),
            jax.ShapeDtypeStruct((all_rows, 1), jnp.int32),
            bf16(2, seq, slab, 3 * cols),
            bf16(slab, ff),
            bf16(slab, ff),
            bf16(seq // 2, slab, 4 * down.shape[0]),
            bf16(2, *down.shape),
            bf16(2, *output.shape),
        ],
        in_specs=[pl.BlockSpec(memory_space=pltpu.SMEM)] + [VMEM] * 10 + [HBM] * 2,
        out_specs=[HBM] * 2 + [VMEM] * 9 + [HBM] * 3,
        scratch_shapes=gather_scratch(seq, rows, width)
        + [
            pltpu.VMEM((seq, slab, 3 * cols), BF16),
            dma((seq // 2, 2, 2)),
            dma((2, seq // 2)),
            dma((2, seq // 2)),
            dma((2, seq // 2, 4)),
            dma((2, 2)),
            dma((6,)),
            dma((2, seq)),
        ],
        compiler_params=params(call_id, 56),
        cost_estimate=cost(2 * all_rows * width * 3 * cols, 8 * all_rows * width),
    )(lengths, tokens, cotangent, query, key, value, gate, up, *gains, freq, down, output)


def attention_feed_kernel(
    block,
    q_ref,
    k_ref,
    v_ref,
    open_ref,
    gate_ref,
    up_ref,
    out_ref,
    lse_ref,
    feed_ref,
    feed_sems,
):
    here = Place()
    feed = feed_spread(here, False, (gate_ref, up_ref), feed_ref, feed_sems)

    @pl.when(pl.program_id(0) == 0)
    def _():
        here.greet_all()
        feed.start()

    attention_kernel(block, q_ref, k_ref, v_ref, open_ref, out_ref, lse_ref)

    @pl.when(pl.program_id(0) == pl.num_programs(0) - 1)
    def _():
        feed.finish()


def attention_feed(queries, keys, values, opening, gate, up, feed_cols, block, call_id):
    seq = lax.axis_size("seq")
    rows, cols = queries.shape
    heads = cols // HEAD_DIM
    tiled = lambda width: pl.BlockSpec((block, width), lambda i: (i, 0))
    whole = pl.BlockSpec((rows, cols), lambda i: (0, 0))
    return pl.pallas_call(
        functools.partial(attention_feed_kernel, block),
        grid=(rows // block,),
        in_specs=[tiled(cols), whole, whole, tiled(1), HBM, HBM],
        out_specs=[tiled(cols), tiled(heads), HBM],
        out_shape=[
            jax.ShapeDtypeStruct((rows, cols), F32),
            jax.ShapeDtypeStruct((rows, heads), F32),
            jax.ShapeDtypeStruct((seq // 2, gate.shape[0], feed_cols), BF16),
        ],
        scratch_shapes=[pltpu.SemaphoreType.DMA((2, seq // 2, 4))],
        compiler_params=params(call_id, 48),
        cost_estimate=cost(2 * rows * rows * cols, 10 * rows * cols),
    )(queries, keys, values, opening, gate, up)


SCATTER_PARTS = 2
SCATTER_RING = 4
SCATTER_SCRATCH = 11


def scatter_rows_of_products(
    here,
    products,
    core_out,
    core_in,
    pair_out,
    pair_in,
    line_out,
    line_in,
    held,
    core_sems,
    pair_sems,
    line_sems,
    came_sems,
    between=nothing,
    middle=nothing,
    filler=None,
):
    length = here.length
    parts = SCATTER_PARTS * len(products)
    rows, width = held.shape
    tile = min(width, 512)
    tiles = width // tile
    steps = length * parts

    def target(i):
        ups = length - 1 - here.line
        near = here.line < length // 2
        if_near = jnp.where(i < ups, length - 1 - i, i - ups)
        if_far = jnp.where(i < here.line, i, length - 1 - (i - here.line))
        return jnp.where(i == length - 1, here.line, jnp.where(near, if_near, if_far))

    def product(line, pair, core, part, use):
        first = pl.multiple_of(here.index(line, pair, core) * rows, rows)

        def one(number):
            transposed, a_ref, b_ref, _ = products[number]
            a = a_ref[pl.ds(first, rows), :]
            begin = (part - number * SCATTER_PARTS) * width

            @pl.loop(0, tiles)
            def _(t):
                into = pl.ds(pl.multiple_of(t * tile, tile), tile)
                cols = pl.ds(pl.multiple_of(begin + t * tile, tile), tile)
                use(dot_t(a, b_ref[cols, :]) if transposed else dot(a, b_ref[:, cols]), into)

        for number in range(len(products)):
            pl.when(part // SCATTER_PARTS == number)(functools.partial(one, number))

    def core_copy(slot):
        return remote(
            core_out.at[slot % SCATTER_RING],
            core_in.at[slot],
            core_sems.at[0, slot],
            core_sems.at[1, slot],
            here.sibling(),
        )

    def pair_copy(slot):
        return remote(
            pair_out.at[slot],
            pair_in.at[slot],
            pair_sems.at[0, slot],
            pair_sems.at[1, slot],
            here.across(),
        )

    def up_copy(slot, line, part):
        into = (line + 1) * parts + part
        return remote(
            line_out.at[slot], line_in.at[into], line_sems.at[slot], came_sems.at[into], here.above()
        )

    def down_copy(slot, line, part):
        into = line * parts + part
        return remote(
            line_out.at[slot], line_in.at[into], line_sems.at[slot], came_sems.at[into], here.below()
        )

    def for_sibling(step, pair, slot):
        pl.when(slot >= SCATTER_RING)(lambda: core_copy(slot - SCATTER_RING).wait_send())

        def use(value, cols):
            core_out[slot % SCATTER_RING, :, cols] = value.astype(BF16)

        product(target(step // parts), pair, 1 - here.core, step % parts, use)
        core_copy(slot).start()

    for_sibling(jnp.int32(0), 1 - here.pair, jnp.int32(0))

    @pl.loop(0, steps)
    def _(step):
        pl.when(step < steps - 1)(lambda: for_sibling(step + 1, 1 - here.pair, step + 1))
        core_copy(step).wait_recv()

        def use(value, cols):
            pair_out[step, :, cols] = (value + core_in[step, :, cols].astype(F32)).astype(BF16)

        product(target(step // parts), 1 - here.pair, here.core, step % parts, use)
        pair_copy(step).start()

    for_sibling(jnp.int32(0), here.pair, jnp.int32(steps))
    between()

    @pl.loop(0, steps)
    def _(step):
        pl.when(step < steps - 1)(lambda: for_sibling(step + 1, here.pair, steps + step + 1))
        core_copy(steps + step).wait_recv()
        line = target(step // parts)
        part = step % parts

        def use(value, cols):
            held[:, cols] = value + core_in[steps + step, :, cols].astype(F32)

        product(line, here.pair, here.core, part, use)
        if filler is not None:
            filler(step)
        pair_copy(step).wait_recv()
        from_above = (line <= here.line) & (here.line < length - 1)
        from_below = (line >= here.line) & (here.line > 0)
        held[...] += pair_in[step].astype(F32)

        @pl.when(from_above)
        def _():
            down_copy(0, line, part).wait_recv()
            held[...] += line_in[line * parts + part].astype(F32)

        @pl.when(from_below)
        def _():
            up_copy(0, line, part).wait_recv()
            held[...] += line_in[(line + 1) * parts + part].astype(F32)

        for number, (_, _, _, out_ref) in enumerate(products):

            @pl.when((line == here.line) & (part // SCATTER_PARTS == number))
            def _():
                begin = (part - number * SCATTER_PARTS) * width
                out_ref[:, pl.ds(pl.multiple_of(begin, width), width)] = held[...]

        @pl.when(line < here.line)
        def _():
            line_out[step] = held[...].astype(BF16)
            down_copy(step, line, part).start()

        @pl.when(line > here.line)
        def _():
            line_out[step] = held[...].astype(BF16)
            up_copy(step, line, part).start()

        if middle is not nothing:
            pl.when(step == steps // 2)(middle)

    @pl.loop(2 * steps - SCATTER_RING, 2 * steps)
    def _(slot):
        core_copy(slot).wait_send()

    @pl.loop(0, steps)
    def _(step):
        pair_copy(step).wait_send()
        line = target(step // parts)
        pl.when(line < here.line)(lambda: down_copy(step, 0, 0).wait_send())
        pl.when(line > here.line)(lambda: up_copy(step, 0, 0).wait_send())


def scatter_scratch(seq, rows, width, count=1):
    length = seq // 4
    parts = SCATTER_PARTS * count
    steps = length * parts
    block = (rows, width // SCATTER_PARTS)
    dma = pltpu.SemaphoreType.DMA
    return [
        pltpu.VMEM((SCATTER_RING, *block), BF16),
        pltpu.VMEM((2 * steps, *block), BF16),
        pltpu.VMEM((steps, *block), BF16),
        pltpu.VMEM((steps, *block), BF16),
        pltpu.VMEM((steps, *block), BF16),
        pltpu.VMEM(((length + 1) * parts, *block), BF16),
        pltpu.VMEM(block, F32),
        dma((2, 2 * steps)),
        dma((2, steps)),
        dma((steps,)),
        dma(((length + 1) * parts,)),
    ]


def scatter_cost(a, width):
    return cost(2 * a.shape[0] * a.shape[1] * width, 4 * a.shape[0] * width)


def scatter_both_kernel(
    back_ref,
    turned_ref,
    hidden_ref,
    down_ref,
    normed_hbm,
    out_ref,
    mixed_ref,
    sums_ref,
    *scratch,
):
    here = Place()
    here.greet(partner=True)
    normed, away, came, fetch_sems, swap_sems = scratch[SCATTER_SCRATCH:]
    chunk = normed.shape[2]
    half = normed_hbm.shape[1] // 2
    chunks = half // chunk

    def fetch(number):
        dp = jnp.where(number < chunks, 1 - here.dp, here.dp)
        begin = dp * half + number % chunks * chunk
        return pltpu.make_async_copy(
            normed_hbm.at[:, pl.ds(pl.multiple_of(begin, chunk), chunk)],
            normed.at[number % 2],
            fetch_sems.at[number % 2],
        )

    def swap(i):
        some = pl.ds(pl.multiple_of(i * chunk, chunk), chunk)
        return remote(
            away.at[some], came.at[some], swap_sems.at[0, i], swap_sems.at[1, i], here.partner()
        )

    def part(number):
        fetch(number).wait()
        pl.when(number + 1 < 2 * chunks)(lambda: fetch(number + 1).start())
        return t_dot(normed[number % 2], back_ref[...])

    def filler(step):
        @pl.when(step < chunks)
        def _():
            some = pl.ds(pl.multiple_of(step * chunk, chunk), chunk)
            away[some, :] = part(step).astype(BF16)
            swap(step).start()

        @pl.when((step >= chunks) & (step < 3 * chunks) & (step % 2 == 0))
        def _():
            i = (step - chunks) // 2
            some = pl.ds(pl.multiple_of(i * chunk, chunk), chunk)
            kept = part(chunks + i)
            swap(i).wait()
            sums_ref[some, :] = (kept + came[some, :].astype(F32)).astype(BF16)

    fetch(jnp.int32(0)).start()
    scatter_rows_of_products(
        here,
        [(False, back_ref, turned_ref, out_ref), (False, hidden_ref, down_ref, mixed_ref)],
        *scratch[:SCATTER_SCRATCH],
        filler=filler,
    )


def product_scatter_both(back, turned, hidden, down, normed, call_id):
    seq = lax.axis_size("seq")
    rows = back.shape[0] // seq
    width = turned.shape[1]
    cols = back.shape[1]
    chunk = width // 8
    dma = pltpu.SemaphoreType.DMA
    return pl.pallas_call(
        scatter_both_kernel,
        out_shape=[
            jax.ShapeDtypeStruct((rows, width), F32),
            jax.ShapeDtypeStruct((rows, width), F32),
            jax.ShapeDtypeStruct((width // 2, cols), BF16),
        ],
        in_specs=[VMEM] * 4 + [HBM],
        out_specs=[VMEM] * 3,
        scratch_shapes=scatter_scratch(seq, rows, width, 2)
        + [
            pltpu.VMEM((2, normed.shape[0], chunk), BF16),
            pltpu.VMEM((width // 2, cols), BF16),
            pltpu.VMEM((width // 2, cols), BF16),
            dma((2,)),
            dma((2, 4)),
        ],
        compiler_params=params(call_id, 60),
        cost_estimate=scatter_cost(back, 3 * width),
    )(back, turned, hidden, down, normed)


def scatter_feed_kernel(a_ref, b_ref, near_ref, far_ref, out_ref, feed_ref, *scratch):
    here = Place()
    here.greet(partner=True)
    swap_sems, local_sems = scratch[SCATTER_SCRATCH:]
    slots = near_ref.shape[0]

    def copies(half, ref, slot):
        place = feed_ref.at[here.dp, here.peer(slot, half == 0)]
        return (
            remote(
                ref.at[slot],
                place,
                swap_sems.at[0, half, slot],
                swap_sems.at[1, half, slot],
                here.partner(),
            ),
            pltpu.make_async_copy(ref.at[slot], place, local_sems.at[half, slot]),
        )

    @pl.loop(0, slots)
    def _(slot):
        for half, ref in enumerate((near_ref, far_ref)):
            for one in copies(half, ref, slot):
                one.start()

    scatter_rows_of_products(
        here, [(False, a_ref, b_ref, out_ref)], *scratch[:SCATTER_SCRATCH]
    )

    @pl.loop(0, slots)
    def _(slot):
        for half, ref in enumerate((near_ref, far_ref)):
            for one in copies(half, ref, slot):
                one.wait()


def product_scatter_feed(a, b, near, far, call_id):
    seq = lax.axis_size("seq")
    rows = a.shape[0] // seq
    width = b.shape[1]
    dma = pltpu.SemaphoreType.DMA
    return pl.pallas_call(
        scatter_feed_kernel,
        out_shape=[
            jax.ShapeDtypeStruct((rows, width), F32),
            jax.ShapeDtypeStruct((2, seq, *near.shape[1:]), BF16),
        ],
        in_specs=[VMEM, VMEM, HBM, HBM],
        out_specs=[VMEM, HBM],
        scratch_shapes=scatter_scratch(seq, rows, width)
        + [dma((2, 2, seq // 2)), dma((2, seq // 2))],
        compiler_params=params(call_id, 40),
        cost_estimate=scatter_cost(a, width),
    )(a, b, near, far)


def feed_kernel(
    own_ref,
    grad_hbm,
    feed_hbm,
    down_hbm,
    normed_ref,
    hidden_out_ref,
    back_out_ref,
    turned_out_ref,
    buf,
    send_sems,
    recv_sems,
    store_sems,
    grad_ref,
    feed_ref,
    down_ref,
    hidden_ref,
    back_ref,
    turned_ref,
    fetch_sems,
    out_sems,
):
    here = Place()
    fetches = [
        pltpu.make_async_copy(src, dst, fetch_sems.at[number])
        for number, (src, dst) in enumerate(
            [(feed_hbm, feed_ref), (down_hbm, down_ref), (grad_hbm, grad_ref)]
        )
    ]
    for one in fetches:
        one.start()
    put_own(here, own_ref, buf)
    here.greet()
    rows = own_ref.shape[0]
    width = own_ref.shape[1]
    hidden = hidden_ref.shape[1]
    tile = 256
    store = UnitStore(buf, normed_ref, store_sems)

    def outs(number, first):
        where = unit_rows(first, rows)
        share = width // (2 * here.length)
        some = pl.ds(pl.multiple_of(number * share, share), share)
        return [
            pltpu.make_async_copy(src, dst, out_sems.at[number, i])
            for i, (src, dst) in enumerate(
                [
                    (hidden_ref.at[where], hidden_out_ref.at[where]),
                    (back_ref.at[where], back_out_ref.at[where]),
                    (turned_ref.at[:, some], turned_out_ref.at[:, some]),
                ]
            )
        ]

    def compute(number, first):
        store.start(number, first)

        @pl.when(number == 0)
        def _():
            for one in fetches:
                one.wait()

        where = unit_rows(first, rows)
        normed = take_unit(buf, first)
        grad = grad_ref[where, :]

        @pl.loop(0, hidden // tile)
        def _(t):
            cols = pl.ds(pl.multiple_of(t * tile, tile), tile)
            later = pl.ds(pl.multiple_of(hidden + t * tile, tile), tile)
            gate = dot(normed, feed_ref[:, cols])
            upward = dot(normed, feed_ref[:, later])
            hidden_grad = dot_t(grad, down_ref[cols, :])
            sigmoid = jax.nn.sigmoid(gate)
            silu = gate * sigmoid
            hidden_ref[where, cols] = (silu * upward).astype(BF16)
            back_ref[where, cols] = (
                hidden_grad * upward * sigmoid * (1.0 + gate * (1.0 - sigmoid))
            ).astype(BF16)
            back_ref[where, later] = (hidden_grad * silu).astype(BF16)

        share = width // (2 * here.length)
        some = pl.ds(pl.multiple_of(number * share, share), share)
        turned_ref[:, some] = feed_ref[some, :].T
        for one in outs(number, first):
            one.start()

    gather_units(here, buf, send_sems, recv_sems, compute)

    @pl.loop(0, here.count // 2)
    def _(number):
        for one in outs(number, 0):
            one.wait()

    store.finish()


def gather_feed(own, grad_out, feed_weight, down_weight, call_id):
    seq = lax.axis_size("seq")
    rows, width = own.shape
    hidden = down_weight.shape[0]
    return pl.pallas_call(
        feed_kernel,
        out_shape=[
            jax.ShapeDtypeStruct((seq * rows, width), BF16),
            jax.ShapeDtypeStruct((seq * rows, hidden), BF16),
            jax.ShapeDtypeStruct((seq * rows, 2 * hidden), BF16),
            jax.ShapeDtypeStruct((2 * hidden, width), BF16),
        ],
        in_specs=[VMEM] + [HBM] * 3,
        out_specs=[HBM] * 4,
        scratch_shapes=gather_scratch(seq, rows // 2, width)
        + [
            pltpu.SemaphoreType.DMA((seq // 2, 2, 2)),
            pltpu.VMEM((seq * rows, width), BF16),
            pltpu.VMEM((width, 2 * hidden), BF16),
            pltpu.VMEM((hidden, width), BF16),
            pltpu.VMEM((seq * rows, hidden), BF16),
            pltpu.VMEM((seq * rows, 2 * hidden), BF16),
            pltpu.VMEM((2 * hidden, width), BF16),
            pltpu.SemaphoreType.DMA((3,)),
            pltpu.SemaphoreType.DMA((seq // 2, 3)),
        ],
        compiler_params=params(call_id, 56),
        cost_estimate=cost(8 * seq * rows * width * hidden, 8 * seq * rows * width),
    )(own, grad_out, feed_weight, down_weight)


def back_kernel(
    own_ref,
    weight_ref,
    attended_ref,
    hidden_hbm,
    out_grad_hbm,
    blocks_ref,
    grad_ref,
    output_kept_ref,
    output_away_ref,
    down_kept_ref,
    down_away_ref,
    near_ref,
    buf,
    send_sems,
    recv_sems,
    near_sems,
    own_sem,
    part,
    hidden_ref,
    out_grad_ref,
    fetch_sems,
):
    here = Place()
    fetches = [
        pltpu.make_async_copy(hidden_hbm, hidden_ref, fetch_sems.at[0]),
        pltpu.make_async_copy(out_grad_hbm, out_grad_ref, fetch_sems.at[1]),
    ]
    for one in fetches:
        one.start()
    put_own(here, own_ref, buf)
    here.greet_all()
    rows = own_ref.shape[0]
    width = own_ref.shape[1]
    tile = 512
    near = block_spread(here, True, blocks_ref, near_ref, near_sems)
    own = pltpu.make_async_copy(blocks_ref.at[here.mine], near_ref.at[here.slot], own_sem.at[0])

    def started():
        near.start()
        own.start()

    part[...] = jnp.zeros_like(part)
    share = width // (2 * here.length)

    def split(values, kept_ref, away_ref, cols):
        half = values.shape[0] // 2
        top, bottom = values[:half], values[half:]
        kept_ref[:, cols] = jnp.where(here.dp == 0, top, bottom)
        away_ref[:, cols] = jnp.where(here.dp == 0, bottom, top).astype(BF16)

    def compute(number, first):
        where = unit_rows(first, rows)
        unit = take_unit(buf, first)
        grad_ref[where, :] = dot_t(unit, weight_ref[...]).astype(BF16)
        attended = attended_ref[where, :]
        for t in range(width // tile):
            cols = slice(t * tile, (t + 1) * tile)
            part[:, cols] += t_dot(attended, unit[:, cols])
        some = pl.ds(pl.multiple_of(number * share, share), share)

        @pl.when(number == 0)
        def _():
            for one in fetches:
                one.wait()

        split(t_dot(hidden_ref[...], out_grad_ref[:, some]), down_kept_ref, down_away_ref, some)

    gather_units(here, buf, send_sems, recv_sems, compute, started=started)
    for t in range(width // tile):
        cols = slice(t * tile, (t + 1) * tile)
        split(part[:, cols], output_kept_ref, output_away_ref, cols)
    near.finish()
    own.wait()


def gather_back(own, weight, attended, hidden, grad_out, blocks, call_id):
    seq = lax.axis_size("seq")
    rows, width = own.shape
    cols = weight.shape[0]
    return pl.pallas_call(
        back_kernel,
        out_shape=[
            jax.ShapeDtypeStruct((seq * rows, cols), BF16),
            jax.ShapeDtypeStruct((cols // 2, width), F32),
            jax.ShapeDtypeStruct((cols // 2, width), BF16),
            jax.ShapeDtypeStruct((hidden.shape[1] // 2, width), F32),
            jax.ShapeDtypeStruct((hidden.shape[1] // 2, width), BF16),
            jax.ShapeDtypeStruct((seq // 2, *blocks.shape[1:]), BF16),
        ],
        in_specs=[VMEM] * 3 + [HBM] * 3,
        out_specs=[VMEM] * 5 + [HBM],
        scratch_shapes=gather_scratch(seq, rows // 2, width)
        + [
            pltpu.SemaphoreType.DMA((2, seq // 2)),
            pltpu.SemaphoreType.DMA((1,)),
            pltpu.VMEM((cols, width), F32),
            pltpu.VMEM(hidden.shape, BF16),
            pltpu.VMEM(grad_out.shape, BF16),
            pltpu.SemaphoreType.DMA((2,)),
        ],
        compiler_params=params(call_id, 48),
        cost_estimate=cost(8 * seq * rows * width * cols, 6 * seq * rows * width),
    )(own, weight, attended, hidden, grad_out, blocks)


def attention_back_feed_kernel(
    block,
    q_ref,
    k_ref,
    v_ref,
    g_ref,
    att_ref,
    lse_ref,
    open_ref,
    cos_ref,
    sin_ref,
    blocks_ref,
    down_ref,
    output_ref,
    back_ref,
    feed_ref,
    down_out_ref,
    output_out_ref,
    dq_ref,
    dk_ref,
    dv_ref,
    feed_sems,
    swap_sems,
):
    here = Place()
    tile = pl.program_id(0)
    cols = q_ref.shape[1]
    feed = block_spread(here, False, blocks_ref, feed_ref, feed_sems)
    swaps = [
        remote(src, dst, swap_sems.at[0, number], swap_sems.at[1, number], here.partner())
        for number, (src, dst) in enumerate(
            [(down_ref, down_out_ref), (output_ref, output_out_ref)]
        )
    ]

    @pl.when(tile == 0)
    def _():
        here.greet_all()
        feed.start()
        for one in swaps:
            one.start()

    attention_back_kernel(
        block, q_ref, k_ref, v_ref, g_ref, att_ref, lse_ref, open_ref, dq_ref, dk_ref, dv_ref
    )
    where = pl.ds(pl.multiple_of(tile * block, block), block)
    scale = 1.0 / math.sqrt(HEAD_DIM)
    cosine = cos_ref[where, :]
    sine = sin_ref[where, :]
    back_ref[where, :cols] = rotated(dq_ref[...] * scale, cosine, -sine).astype(BF16)

    @pl.when(tile == pl.num_programs(0) - 1)
    def _():
        @pl.loop(0, pl.num_programs(0))
        def _(i):
            rows = pl.ds(pl.multiple_of(i * block, block), block)
            keys = rotated(dk_ref[rows, :], cos_ref[rows, :], -sin_ref[rows, :])
            back_ref[rows, cols : 2 * cols] = keys.astype(BF16)
            back_ref[rows, 2 * cols :] = dv_ref[rows, :].astype(BF16)

        feed.finish()
        for one in swaps:
            one.wait()


def attention_back_feed(
    queries,
    keys,
    values,
    grads,
    attended,
    log_total,
    opening,
    cosine,
    sine,
    blocks,
    down,
    output,
    block,
    call_id,
):
    seq = lax.axis_size("seq")
    rows, cols = queries.shape
    heads = cols // HEAD_DIM
    tiled = lambda width: pl.BlockSpec((block, width), lambda i: (i, 0))
    whole = pl.BlockSpec((rows, cols), lambda i: (0, 0))
    dma = pltpu.SemaphoreType.DMA
    return pl.pallas_call(
        functools.partial(attention_back_feed_kernel, block),
        grid=(rows // block,),
        in_specs=[tiled(cols), whole, whole, tiled(cols), tiled(cols), tiled(heads), tiled(1)]
        + [whole, whole, HBM, HBM, HBM],
        out_specs=[pl.BlockSpec((rows, 3 * cols), lambda i: (0, 0)), HBM, HBM, HBM],
        out_shape=[
            jax.ShapeDtypeStruct((rows, 3 * cols), BF16),
            jax.ShapeDtypeStruct((seq // 2, *blocks.shape[1:]), BF16),
            jax.ShapeDtypeStruct(down.shape, BF16),
            jax.ShapeDtypeStruct(output.shape, BF16),
        ],
        scratch_shapes=[
            pltpu.VMEM((block, cols), F32),
            pltpu.VMEM((rows, cols), F32),
            pltpu.VMEM((rows, cols), F32),
            dma((2, seq // 2)),
            dma((2, 2)),
        ],
        compiler_params=params(call_id, 60),
        cost_estimate=cost(5 * rows * rows * cols, 20 * rows * cols),
    )(
        queries,
        keys,
        values,
        grads,
        attended,
        log_total,
        opening,
        cosine,
        sine,
        blocks,
        down,
        output,
    )


def scatter_last_kernel(a_ref, b_ref, normed_hbm, out_ref, qkv_ref, *scratch):
    here = Place()
    normed_ref, kept, away, came, sums, near_sems, far_sems, swap_sems, fetch_sems = scratch[
        SCATTER_SCRATCH:
    ]
    fetch = pltpu.make_async_copy(normed_hbm, normed_ref, fetch_sems.at[0])
    fetch.start()
    here.greet_all()
    swap = remote(away, came, swap_sems.at[0], swap_sems.at[1], here.partner())
    near = block_spread(here, True, sums, qkv_ref.at[0], near_sems)
    far = block_spread(here, False, sums, qkv_ref.at[1], far_sems)
    half = away.shape[0]
    chunk = 256

    def part(dp, i):
        first = pl.multiple_of(dp * half + i * chunk, chunk)
        return t_dot(normed_ref[:, pl.ds(first, chunk)], a_ref[...])

    def between():
        fetch.wait()

        @pl.loop(0, half // chunk)
        def _(i):
            away[pl.ds(pl.multiple_of(i * chunk, chunk), chunk), :] = part(1 - here.dp, i).astype(
                BF16
            )

        swap.start()

    def filler(step):
        @pl.when(step < half // chunk)
        def _():
            kept[pl.ds(pl.multiple_of(step * chunk, chunk), chunk), :] = part(here.dp, step)

    def middle():
        swap.wait_recv()
        slab = sums.shape[1]

        @pl.loop(0, here.count)
        def _(i):
            rows = pl.ds(pl.multiple_of(i * slab, slab), slab)
            sums[i] = (kept[rows, :] + came[rows, :].astype(F32)).astype(BF16)

        qkv_ref[0, here.slot] = sums[here.mine]
        far.start()
        near.start()

    scatter_rows_of_products(
        here,
        [(True, a_ref, b_ref, out_ref)],
        *scratch[:SCATTER_SCRATCH],
        between,
        middle,
        filler,
    )
    swap.wait_send()
    near.finish()
    far.finish()


def product_scatter_last(a, b, normed, call_id):
    seq = lax.axis_size("seq")
    rows = a.shape[0] // seq
    width, cols = b.shape
    slab = width // (2 * seq)
    dma = pltpu.SemaphoreType.DMA
    return pl.pallas_call(
        scatter_last_kernel,
        out_shape=[
            jax.ShapeDtypeStruct((rows, width), F32),
            jax.ShapeDtypeStruct((2, seq // 2, slab, cols), BF16),
        ],
        in_specs=[VMEM, VMEM, HBM],
        out_specs=[VMEM, VMEM],
        scratch_shapes=scatter_scratch(seq, rows, width)
        + [
            pltpu.VMEM(normed.shape, BF16),
            pltpu.VMEM((width // 2, cols), F32),
            pltpu.VMEM((width // 2, cols), BF16),
            pltpu.VMEM((width // 2, cols), BF16),
            pltpu.VMEM((seq, slab, cols), BF16),
            dma((2, seq // 2)),
            dma((2, seq // 2)),
            dma((2,)),
            dma((1,)),
        ],
        compiler_params=params(call_id, 56),
        cost_estimate=scatter_cost(a, width),
    )(a, b, normed)


def unpack_kernel(
    pair_ref,
    near_gate_ref,
    far_gate_ref,
    near_up_ref,
    far_up_ref,
    gate_ref,
    up_ref,
    qkv_ref,
    query_ref,
    key_ref,
    value_ref,
    gain_one_ref,
    gain_two_ref,
    gate_out_ref,
    up_out_ref,
    query_out_ref,
    key_out_ref,
    value_out_ref,
    one_out_ref,
    two_out_ref,
):
    pair = pair_ref[0]
    dp = lax.axis_size("dp")
    length = qkv_ref.shape[1] // 2
    slab = qkv_ref.shape[2]
    step = pl.program_id(0) * pl.num_programs(1) + pl.program_id(1)
    columns = near_gate_ref.shape[2]

    def along(grad, weight):
        return jnp.sum(grad * weight.astype(F32), axis=1, keepdims=True)

    @pl.when(step == 0)
    def _():
        two_out_ref[...] = jnp.zeros_like(two_out_ref)
        total = jnp.zeros((slab, 1), F32)
        gain = gain_one_ref[...]

        def put(out_ref, weight_ref, begin, grad):
            cols = slice(begin, begin + grad.shape[1])
            out_ref[:, cols] = grad * gain
            return along(grad, weight_ref[:, cols])

        pairs = [{}, {}]
        for line in range(length):
            rows = []
            for number in range(4):
                slot = line * 2 + number % 2
                near, far = qkv_ref[0, slot].astype(F32), qkv_ref[1, slot].astype(F32)
                rows.append(jnp.where(number // 2 == pair, near, far))
            kv = rows[0] + rows[1] + rows[2] + rows[3]
            for half in range(dp):
                cols = slice(half * HEAD_DIM, (half + 1) * HEAD_DIM)
                for number in (0, 2):
                    two = jnp.concatenate([rows[number][:, cols], rows[number + 1][:, cols]], axis=1)
                    begin = (half * length * 4 + line * 4 + number) * HEAD_DIM
                    total = total + put(query_out_ref, query_ref, begin, two)
                for kind in range(2):
                    begin = ((kind + 1) * dp + half) * HEAD_DIM
                    pairs[kind][half, line] = kv[:, begin : begin + HEAD_DIM]
        for kind, (out_ref, weight_ref) in enumerate(
            [(key_out_ref, key_ref), (value_out_ref, value_ref)]
        ):
            for half in range(dp):
                for line in range(0, length, 2):
                    two = [pairs[kind][half, line], pairs[kind][half, line + 1]]
                    begin = (half * length + line) * HEAD_DIM
                    total = total + put(
                        out_ref, weight_ref, begin, jnp.concatenate(two, axis=1)
                    )
        one_out_ref[...] = total

    total = jnp.zeros((slab, 1), F32)
    for near_ref, far_ref, weight_ref, out_ref in (
        (near_gate_ref, far_gate_ref, gate_ref, gate_out_ref),
        (near_up_ref, far_up_ref, up_ref, up_out_ref),
    ):
        for number in range(4):
            core = number % 2
            near, far = near_ref[core].astype(F32), far_ref[core].astype(F32)
            grad = jnp.where(number // 2 == pair, near, far)
            cols = slice(number * columns, (number + 1) * columns)
            total = total + along(grad, weight_ref[:, cols])
            out_ref[:, cols] = grad * gain_two_ref[...]
    two_out_ref[...] += total


def unpack(pair, near, far, gate, up, qkv, query, key, value, gain_one, gain_two):
    dp = lax.axis_size("dp")
    seq = lax.axis_size("seq")
    slab, ff = gate.shape
    length = seq // 4
    columns = ff // (dp * seq)
    whole = lambda array: pl.BlockSpec(array.shape, lambda j, i: (0,) * array.ndim)
    block = lambda kind: pl.BlockSpec((2, slab, columns), lambda j, i: (i, 0, kind * dp + j))
    tile = pl.BlockSpec((slab, 4 * columns), lambda j, i: (0, j * length + i))
    f32 = lambda array: jax.ShapeDtypeStruct(array.shape, F32)
    outs = [f32(gate), f32(up), f32(query), f32(key), f32(value), f32(gain_one), f32(gain_two)]
    return pl.pallas_call(
        unpack_kernel,
        grid=(dp, length),
        in_specs=[pl.BlockSpec(memory_space=pltpu.SMEM)]
        + [block(0), block(0), block(1), block(1), tile, tile]
        + [whole(array) for array in (qkv, query, key, value, gain_one, gain_two)],
        out_specs=[tile, tile] + [whole(array) for array in outs[2:]],
        out_shape=outs,
        compiler_params=pltpu.CompilerParams(vmem_limit_bytes=40 << 20),
        cost_estimate=cost(slab * ff, 16 * slab * ff),
    )(pair, near, far, near, far, gate, up, qkv, query, key, value, gain_one, gain_two)


def swap_dp(values):
    count = lax.axis_size("dp")
    return lax.ppermute(values, "dp", [(i, (i + 1) % count) for i in range(count)])


def gather_dp(values):
    return lax.all_gather(values, "dp", axis=0, tiled=True)


def sum_dp(partial):
    half = partial.shape[0] // 2
    mine = lax.axis_index("dp")
    away = lax.dynamic_slice_in_dim(partial, (1 - mine) * half, half, 0).astype(BF16)
    kept = lax.dynamic_slice_in_dim(partial, mine * half, half, 0)
    return kept + swap_dp(away).astype(F32)


def gather_rows(values):
    return lax.all_gather(values, "seq", axis=0, tiled=True)


def scatter_rows(partial):
    return lax.psum_scatter(partial.astype(BF16), "seq", scatter_dimension=0, tiled=True).astype(F32)


def exchange(blocks):
    return lax.all_to_all(blocks, "seq", split_axis=0, concat_axis=0, tiled=True)


def norm_factor(values):
    return lax.rsqrt(jnp.mean(values * values, axis=-1, keepdims=True) + EPS)


def norm_back(inputs, factor, gain_row, upstream):
    scaled_up = gain_row * upstream
    inner_mean = jnp.mean(scaled_up * inputs, axis=-1, keepdims=True)
    grad_in = factor * scaled_up - inputs * factor * factor * factor * inner_mean
    grad_gain = jnp.sum(upstream * inputs * factor, axis=0)
    return grad_in, grad_gain


def plain_shards(
    tokens,
    cotangent,
    doc_lengths,
    attn_gain,
    mlp_gain,
    query_weight,
    key_weight,
    value_weight,
    output_weight,
    gate_weight,
    up_weight,
    down_weight,
):
    dp = lax.axis_size("dp")
    seq = lax.axis_size("seq")
    mine = lax.axis_index("seq")
    tok_count, width = tokens.shape
    rows = tok_count * seq
    slab = query_weight.shape[0]
    share = HEAD_DIM // slab
    half_heads = HEADS // dp
    half_kv = KV_HEADS // dp
    hidden_dev = down_weight.shape[0]
    block = 512

    doc_ends = jnp.cumsum(doc_lengths[0])
    place = jnp.arange(rows, dtype=jnp.int32)
    passed = doc_ends[None, :] <= place[:, None]
    opening = jnp.max(jnp.where(passed, doc_ends[None, :], 0), axis=1)
    position = place - opening
    keeping = place < doc_ends[DOCS - 1]
    angles = position.astype(F32)[:, None] * rotary_table(HEAD_DIM)[None, :]
    cosine = jnp.cos(angles)
    sine = jnp.sin(angles)
    cos_heads = jnp.tile(cosine, (1, 2 * dp))
    sin_heads = jnp.tile(jnp.concatenate([-sine, sine], axis=1), (1, dp))
    own_keeping = lax.dynamic_slice_in_dim(keeping, mine * tok_count, tok_count, 0)

    def head_columns(weight, kept):
        split = weight.reshape(slab, dp, kept, HEAD_DIM)
        return jnp.repeat(split, seq // kept, axis=2)

    qkv_blocks = jnp.stack(
        [
            head_columns(query_weight, half_heads),
            head_columns(key_weight, half_kv),
            head_columns(value_weight, half_kv),
        ],
        axis=1,
    )
    qkv_blocks = jnp.transpose(qkv_blocks, (3, 0, 1, 2, 4)).reshape(seq * slab, 3 * dp * HEAD_DIM)
    qkv_weight = gather_dp(exchange(qkv_blocks))
    feed_blocks = jnp.stack(
        [w.reshape(slab, dp, seq, hidden_dev) for w in (gate_weight, up_weight)], axis=1
    )
    feed_blocks = jnp.transpose(feed_blocks, (3, 0, 1, 2, 4)).reshape(
        seq * slab, 2 * dp * hidden_dev
    )
    feed_weight = gather_dp(exchange(feed_blocks))
    down_own = gather_dp(down_weight)
    output_own = output_weight
    if share > 1:
        groups = [list(range(i, i + share)) for i in range(0, seq, share)]
        output_own = lax.all_gather(
            output_own, "seq", axis=0, tiled=True, axis_index_groups=groups
        )
    output_own = gather_dp(output_own)
    gains = lax.all_gather(
        jnp.stack([attn_gain, mlp_gain]), ("dp", "seq"), axis=1, tiled=True
    ).astype(F32)
    gain_one, gain_two = gains[0], gains[1]

    inputs_all = gather_rows(tokens).astype(F32)
    normed_one = (inputs_all * norm_factor(inputs_all) * gain_one).astype(BF16)
    qkv = dot(normed_one, qkv_weight)
    head_cols = dp * HEAD_DIM
    query_lin, key_lin = qkv[:, :head_cols], qkv[:, head_cols : 2 * head_cols]
    values = qkv[:, 2 * head_cols :].astype(BF16)
    scale = 1.0 / math.sqrt(HEAD_DIM)
    queries = (query_lin * cos_heads + swap_halves(query_lin) * sin_heads).astype(BF16) * BF16(scale)
    keys = (key_lin * cos_heads + swap_halves(key_lin) * sin_heads).astype(BF16)
    attended_sum, log_total = attention(queries, keys, values, opening[:, None], block)
    if share > 1:
        own_rows = ((place // tok_count) % share == mine % share)[:, None]
        attended_sum = jnp.where(own_rows, attended_sum, 0.0)
    attended = attended_sum.astype(BF16)
    inputs = tokens.astype(F32)
    middle = inputs + scatter_rows(dot(attended, output_own))

    factor_two = norm_factor(middle)
    normed_two = gather_rows((middle * factor_two * gain_two).astype(BF16))
    grad_own = jnp.where(own_keeping[:, None], cotangent, BF16(0))
    grad_out = gather_rows(grad_own)
    feed = dot(normed_two, feed_weight)
    feed_cols = dp * hidden_dev
    gate_lin, upward = feed[:, :feed_cols], feed[:, feed_cols:]
    sigmoid = jax.nn.sigmoid(gate_lin)
    hidden = (gate_lin * sigmoid * upward).astype(BF16)
    hidden_grad = dot_t(grad_out, down_own)
    gate_back = (hidden_grad * upward * sigmoid * (1.0 + gate_lin * (1.0 - sigmoid))).astype(BF16)
    up_back = (hidden_grad * gate_lin * sigmoid).astype(BF16)
    feed_back = jnp.concatenate([gate_back, up_back], axis=1)
    normed_two_grad = scatter_rows(dot_t(feed_back, feed_weight))
    mixed = middle + scatter_rows(dot(hidden, down_own))
    middle_in, gain_two_part = norm_back(middle, factor_two, gain_two, normed_two_grad)
    middle_grad = grad_own.astype(F32) + middle_in
    middle_back = gather_rows(middle_grad.astype(BF16))

    attended_grad = dot_t(middle_back, output_own).astype(BF16)
    if share > 1:
        attended_grad = jnp.where(own_rows, attended_grad, BF16(0))
    query_acc, key_acc, value_acc = attention_back(
        queries, keys, values, attended_grad, attended_sum, log_total, opening[:, None], block
    )
    query_acc = query_acc * scale
    query_back = query_acc * cos_heads - swap_halves(query_acc) * sin_heads
    key_back = key_acc * cos_heads - swap_halves(key_acc) * sin_heads
    qkv_back = jnp.concatenate([query_back, key_back, value_acc], axis=1).astype(BF16)
    normed_one_grad = scatter_rows(dot_t(qkv_back, qkv_weight))
    input_in, gain_one_part = norm_back(inputs, norm_factor(inputs), gain_one, normed_one_grad)
    token_grad = middle_grad + input_in

    feed_grad = exchange(sum_dp(t_dot(normed_two, feed_back)).astype(BF16)).astype(F32)
    feed_grad = feed_grad.reshape(seq, slab, 2, dp, hidden_dev)
    feed_grad = jnp.transpose(feed_grad, (2, 1, 3, 0, 4)).reshape(2, slab, dp * seq * hidden_dev)
    down_grad = sum_dp(t_dot(hidden, grad_out))
    output_part = t_dot(attended, middle_back)
    if share > 1:
        split = output_part.reshape(dp, share, slab, width)
        split = jnp.transpose(split, (1, 0, 2, 3)).reshape(share * dp * slab, width)
        output_part = lax.psum_scatter(
            split, "seq", scatter_dimension=0, tiled=True, axis_index_groups=groups
        )
    output_grad = sum_dp(output_part)
    qkv_grad = exchange(sum_dp(t_dot(normed_one, qkv_back)).astype(BF16)).astype(F32)
    qkv_grad = qkv_grad.reshape(seq, slab, 3, dp, HEAD_DIM)

    def own_columns(part, kept):
        summed = jnp.sum(part.reshape(kept, seq // kept, slab, dp, HEAD_DIM), axis=1)
        return jnp.transpose(summed, (1, 2, 0, 3)).reshape(slab, dp * kept * HEAD_DIM)

    query_grad = own_columns(qkv_grad[:, :, 0], half_heads)
    key_grad = own_columns(qkv_grad[:, :, 1], half_kv)
    value_grad = own_columns(qkv_grad[:, :, 2], half_kv)
    gain_parts = lax.psum(jnp.stack([gain_one_part, gain_two_part]), ("dp", "seq"))
    own = lax.axis_index("dp") * seq + mine
    gain_grads = lax.dynamic_slice_in_dim(gain_parts, own * slab, slab, 1)
    return (
        mixed,
        token_grad,
        gain_grads[0],
        gain_grads[1],
        query_grad,
        key_grad,
        value_grad,
        output_grad,
        feed_grad[0],
        feed_grad[1],
        down_grad,
    )


def shards(
    tokens,
    cotangent,
    doc_lengths,
    attn_gain,
    mlp_gain,
    query_weight,
    key_weight,
    value_weight,
    output_weight,
    gate_weight,
    up_weight,
    down_weight,
):
    dp = lax.axis_size("dp")
    seq = lax.axis_size("seq")
    mine = lax.axis_index("seq")
    tok_count, width = tokens.shape
    slab = query_weight.shape[0]
    block = 512
    gain_one = attn_gain.astype(F32)[:, None]
    gain_two = mlp_gain.astype(F32)[:, None]

    (
        normed_one,
        grad_out,
        queries,
        keys,
        values,
        cosine,
        sine,
        opening,
        qkv_weight,
        gate_scaled,
        up_scaled,
        feed_near,
        down_own,
        output_own,
    ) = gather_project(
        doc_lengths,
        tokens,
        cotangent,
        query_weight,
        key_weight,
        value_weight,
        gate_weight,
        up_weight,
        (gain_one, gain_two),
        jnp.tile(rotary_table(HEAD_DIM), 2 * dp)[None, :],
        down_weight,
        output_weight,
        0,
    )
    inputs = tokens.astype(F32)
    factor_one = norm_factor(inputs)
    own_place = mine * tok_count + jnp.arange(tok_count, dtype=jnp.int32)
    own_keeping = own_place < jnp.sum(doc_lengths)
    grad_own = jnp.where(own_keeping[:, None], cotangent, BF16(0))
    qkv_weight = qkv_weight.reshape(width, -1)
    down_own = down_own.reshape(-1, width)
    output_own = output_own.reshape(-1, width)
    attended_sum, log_total, feed_far = attention_feed(
        queries,
        keys,
        values,
        opening,
        gate_scaled,
        up_scaled,
        feed_near.shape[2],
        block,
        1,
    )
    attended = attended_sum.astype(BF16)
    attended_out, feed_weight = product_scatter_feed(attended, output_own, feed_near, feed_far, 2)
    feed_weight = feed_weight.reshape(width, -1)
    middle = inputs + attended_out

    factor_two = norm_factor(middle)
    normed_two, hidden, feed_back, feed_turned = gather_feed(
        (middle * factor_two).astype(BF16), grad_out, feed_weight, down_own, 3
    )

    def norm_input_grad(values, factor, upstream):
        inner_mean = jnp.mean(upstream * values, axis=-1, keepdims=True)
        return factor * upstream - values * factor * factor * factor * inner_mean

    normed_two_grad, mixed_sum, feed_sums = product_scatter_both(
        feed_back, feed_turned, hidden, down_own, normed_two, 4
    )
    mixed = middle + mixed_sum
    feed_sums = feed_sums.reshape(seq, slab, -1)
    middle_grad = grad_own.astype(F32) + norm_input_grad(middle, factor_two, normed_two_grad)
    attended_grad, output_kept, output_away, down_kept, down_away, feed_grad_near = gather_back(
        middle_grad.astype(BF16), output_own, attended, hidden, grad_out, feed_sums, 5
    )

    def both(kept, came):
        return kept.astype(F32) + came.astype(F32)

    qkv_back, feed_grad_far, down_came, output_came = attention_back_feed(
        queries,
        keys,
        values,
        attended_grad,
        attended_sum,
        log_total,
        opening,
        cosine,
        sine,
        feed_sums,
        down_away,
        output_away,
        block,
        6,
    )
    down_grad = both(down_kept, down_came)
    output_grad = both(output_kept, output_came)
    normed_one_grad, qkv_grads = product_scatter_last(qkv_back, qkv_weight, normed_one, 7)
    token_grad = middle_grad + norm_input_grad(inputs, factor_one, normed_one_grad)

    pair = ((mine // 2) % 2).reshape(1)
    gate_grad, up_grad, query_grad, key_grad, value_grad, attn_gain_grad, mlp_gain_grad = unpack(
        pair,
        feed_grad_near,
        feed_grad_far,
        gate_weight,
        up_weight,
        qkv_grads,
        query_weight,
        key_weight,
        value_weight,
        gain_one,
        gain_two,
    )
    return (
        mixed,
        token_grad,
        attn_gain_grad[:, 0],
        mlp_gain_grad[:, 0],
        query_grad,
        key_grad,
        value_grad,
        output_grad,
        gate_grad,
        up_grad,
        down_grad,
    )


def solution(mesh):
    both = P(("dp", "seq"), None)
    line = P(("dp", "seq"))
    dp, seq = mesh.shape["dp"], mesh.shape["seq"]

    def run(*args):
        tokens = args[0].shape[0]
        width = args[0].shape[1]
        suits = dp == 2 and seq % 4 == 0 and width == dp * seq * HEAD_DIM
        suits = suits and 2 * (tokens // dp) * width <= 16 << 20
        return jax.shard_map(
            shards if suits else plain_shards,
            mesh=mesh,
            in_specs=(both, both, P("dp", None), line, line) + (both,) * 7,
            out_specs=(both, both, line, line) + (both,) * 7,
            check_vma=False,
        )(*args)

    return run
```

```python
import functools
import math

import jax
import jax.numpy as jnp
import numpy as np
from jax import lax
from jax.experimental import pallas as pl
from jax.experimental.pallas import tpu as pltpu
from jax.sharding import PartitionSpec as P

HEADS = 32
KV_HEADS = 8
HEAD_DIM = 64
DOCS = 4
EPS = 1e-05
NEG = -1e30
MESH = pl.DeviceIdType.MESH
F32 = jnp.float32
BF16 = jnp.bfloat16


def rotary_table(head_dim):
    exponent = jnp.arange(0, head_dim, 2, dtype=F32) / head_dim
    inverse = jnp.power(F32(500000.0), -exponent)
    wavelength = 2.0 * math.pi / inverse
    smooth = (8192.0 / wavelength - 1.0) / 3.0
    blended = (1.0 - smooth) * inverse / 32.0 + smooth * inverse
    return jnp.where(
        wavelength < 2048.0, inverse, jnp.where(wavelength > 8192.0, inverse / 32.0, blended)
    )


def swap_halves(values):
    rows, cols = values.shape
    halves = values.reshape(rows, cols // HEAD_DIM, 2, HEAD_DIM // 2)
    return halves[:, :, ::-1].reshape(rows, cols)


def dot(a, b):
    return jnp.dot(a, b, preferred_element_type=F32)


def dot_t(a, b):
    return lax.dot_general(a, b, (((1,), (1,)), ((), ())), preferred_element_type=F32)


def t_dot(a, b):
    return lax.dot_general(a, b, (((0,), (0,)), ((), ())), preferred_element_type=F32)


def allowed_tile(opening, q_first, k_first, shape):
    rows = q_first + lax.broadcasted_iota(jnp.int32, shape, 0)
    cols = k_first + lax.broadcasted_iota(jnp.int32, shape, 1)
    return (cols <= rows) & (cols >= opening)


def attention_kernel(block, q_ref, k_ref, v_ref, open_ref, out_ref, lse_ref):
    tile = pl.program_id(0)
    opening = open_ref[...]
    for head in range(q_ref.shape[1] // HEAD_DIM):
        lanes = slice(head * HEAD_DIM, (head + 1) * HEAD_DIM)
        query = q_ref[:, lanes]

        def step(j, carry, lanes=lanes, query=query):
            peak, total, acc = carry
            first = pl.multiple_of(j * block, block)
            scores = dot_t(query, k_ref[pl.ds(first, block), lanes])
            allowed = allowed_tile(opening, tile * block, first, scores.shape)
            scores = jnp.where(allowed, scores, NEG)
            new_peak = jnp.maximum(peak, jnp.max(scores, axis=1, keepdims=True))
            spread = jnp.exp(scores - new_peak)
            fade = jnp.exp(peak - new_peak)
            total = total * fade + jnp.sum(spread, axis=1, keepdims=True)
            acc = acc * fade + dot(spread.astype(BF16), v_ref[pl.ds(first, block), lanes])
            return new_peak, total, acc

        peak, total, acc = lax.fori_loop(
            0,
            tile + 1,
            step,
            (
                jnp.full((block, 1), NEG, F32),
                jnp.zeros((block, 1), F32),
                jnp.zeros((block, HEAD_DIM), F32),
            ),
        )
        out_ref[:, lanes] = acc / total
        lse_ref[:, head : head + 1] = peak + jnp.log(total)


def attention(queries, keys, values, opening, block):
    rows, cols = queries.shape
    heads = cols // HEAD_DIM
    tiled = lambda width: pl.BlockSpec((block, width), lambda i: (i, 0))
    whole = pl.BlockSpec((rows, cols), lambda i: (0, 0))
    return pl.pallas_call(
        functools.partial(attention_kernel, block),
        grid=(rows // block,),
        in_specs=[tiled(cols), whole, whole, tiled(1)],
        out_specs=[tiled(cols), tiled(heads)],
        out_shape=[
            jax.ShapeDtypeStruct((rows, cols), F32),
            jax.ShapeDtypeStruct((rows, heads), F32),
        ],
        compiler_params=pltpu.CompilerParams(vmem_limit_bytes=48 << 20),
        cost_estimate=pl.CostEstimate(
            flops=2 * rows * rows * cols, bytes_accessed=10 * rows * cols, transcendentals=0
        ),
    )(queries, keys, values, opening)


def attention_back_kernel(
    block, q_ref, k_ref, v_ref, g_ref, att_ref, lse_ref, open_ref, dq_ref, dk_ref, dv_ref
):
    tile = pl.program_id(0)

    @pl.when(tile == 0)
    def _():
        dk_ref[...] = jnp.zeros_like(dk_ref)
        dv_ref[...] = jnp.zeros_like(dv_ref)

    opening = open_ref[...]
    for head in range(q_ref.shape[1] // HEAD_DIM):
        lanes = slice(head * HEAD_DIM, (head + 1) * HEAD_DIM)
        query = q_ref[:, lanes]
        grad = g_ref[:, lanes]
        log_total = lse_ref[:, head : head + 1]
        row_sum = jnp.sum(grad.astype(F32) * att_ref[:, lanes], axis=1, keepdims=True)

        def step(j, acc, lanes=lanes, query=query, grad=grad, log_total=log_total, row_sum=row_sum):
            first = pl.multiple_of(j * block, block)
            here = pl.ds(first, block)
            key = k_ref[here, lanes]
            scores = dot_t(query, key)
            allowed = allowed_tile(opening, tile * block, first, scores.shape)
            chance = jnp.where(allowed, jnp.exp(scores - log_total), 0.0)
            prob_grad = dot_t(grad, v_ref[here, lanes])
            score_grad = (chance * (prob_grad - row_sum)).astype(BF16)
            dk_ref[here, lanes] += t_dot(score_grad, query)
            dv_ref[here, lanes] += t_dot(chance.astype(BF16), grad)
            return acc + dot(score_grad, key)

        acc = lax.fori_loop(0, tile + 1, step, jnp.zeros((block, HEAD_DIM), F32))
        dq_ref[:, lanes] = acc


def attention_back(queries, keys, values, grads, attended, log_total, opening, block):
    rows, cols = queries.shape
    heads = cols // HEAD_DIM
    tiled = lambda width: pl.BlockSpec((block, width), lambda i: (i, 0))
    whole = pl.BlockSpec((rows, cols), lambda i: (0, 0))
    return pl.pallas_call(
        functools.partial(attention_back_kernel, block),
        grid=(rows // block,),
        in_specs=[tiled(cols), whole, whole, tiled(cols), tiled(cols), tiled(heads), tiled(1)],
        out_specs=[tiled(cols), whole, whole],
        out_shape=[jax.ShapeDtypeStruct((rows, cols), F32)] * 3,
        compiler_params=pltpu.CompilerParams(vmem_limit_bytes=60 << 20),
        cost_estimate=pl.CostEstimate(
            flops=5 * rows * rows * cols, bytes_accessed=20 * rows * cols, transcendentals=0
        ),
    )(queries, keys, values, grads, attended, log_total, opening)


def nothing():
    pass


class Place:
    def __init__(self):
        self.dp = lax.axis_index("dp")
        self.mine = lax.axis_index("seq")
        self.count = lax.axis_size("seq")
        self.length = self.count // 4
        self.line = lax.div(self.mine, 4)
        self.pair = lax.rem(lax.div(self.mine, 2), 2)
        self.core = lax.rem(self.mine, 2)
        self.slot = self.line * 2 + self.core

    def index(self, line, pair, core):
        return (line * 2 + pair) * 2 + core

    def peer(self, slot, same):
        pair = self.pair if same else 1 - self.pair
        return self.index(lax.div(slot, 2), pair, lax.rem(slot, 2))

    def device(self, line, pair, core):
        return (self.dp, self.index(line, pair, core))

    def sibling(self):
        return self.device(self.line, self.pair, 1 - self.core)

    def across(self):
        return self.device(self.line, 1 - self.pair, self.core)

    def above(self):
        return self.device(self.line + 1, self.pair, self.core)

    def below(self):
        return self.device(self.line - 1, self.pair, self.core)

    def partner(self):
        return (1 - self.dp, self.mine)

    def greet(self, partner=False):
        barrier = pltpu.get_barrier_semaphore()

        def signal(device):
            pl.semaphore_signal(barrier, inc=1, device_id=device, device_id_type=MESH)

        signal(self.sibling())
        signal(self.across())
        pl.when(self.line > 0)(lambda: signal(self.below()))
        pl.when(self.line < self.length - 1)(lambda: signal(self.above()))
        if partner:
            signal(self.partner())
        inner = (self.line > 0) & (self.line < self.length - 1)
        pl.semaphore_wait(barrier, jnp.where(inner, 4, 3) + (1 if partner else 0))

    def greet_all(self, meanwhile=nothing):
        barrier = pltpu.get_barrier_semaphore()

        def signal(device):
            pl.semaphore_signal(barrier, inc=1, device_id=device, device_id_type=MESH)

        signal(self.partner())

        @pl.loop(1, self.count)
        def _(ahead):
            signal((self.dp, lax.rem(self.mine + ahead, self.count)))

        meanwhile()
        pl.semaphore_wait(barrier, self.count)


def remote(src, dst, send_sem, recv_sem, device):
    return pltpu.make_async_remote_copy(
        src_ref=src,
        dst_ref=dst,
        send_sem=send_sem,
        recv_sem=recv_sem,
        device_id=device,
        device_id_type=MESH,
    )


class Spread:
    def __init__(self, here, same, copies):
        self.here, self.same, self.copies = here, same, copies
        self.slots = here.count // 2

    def each(self, visit):
        @pl.loop(1 if self.same else 0, self.slots)
        def _(ahead):
            slot = lax.rem(self.here.slot + ahead, self.slots)
            visit(self.here.peer(slot, self.same), slot)

    def start_one(self, ahead):
        slot = lax.rem(self.here.slot + ahead, self.slots)
        peer = self.here.peer(slot, self.same)
        for one in self.copies(peer, self.here.mine, self.here.slot, slot):
            one.start()

    def start(self):
        pl.loop(1 if self.same else 0, self.slots)(self.start_one)

    def start_some(self, number, each):
        first = 1 if self.same else 0

        @pl.loop(0, each)
        def _(i):
            ahead = first + number * each + i
            pl.when((number >= 0) & (ahead < self.slots))(lambda: self.start_one(ahead))

    def finish(self):
        def visit(peer, slot):
            for one in self.copies(peer, peer, slot, slot):
                one.wait()

        self.each(visit)


def block_spread(here, same, blocks, into, sems):
    def copies(peer, sender, at, sem):
        return [
            remote(
                blocks.at[peer],
                into.at[at],
                sems.at[0, sem],
                sems.at[1, at],
                (here.dp, peer),
            )
        ]

    return Spread(here, same, copies)


def feed_spread(here, same, weights, into, sems):
    dp = lax.axis_size("dp")
    columns = into.shape[2] // (dp * len(weights))

    def copies(peer, sender, at, sem):
        made = []
        for kind, weight in enumerate(weights):
            for half in range(dp):
                part = kind * dp + half
                begin = pl.multiple_of((half * here.count + peer) * columns, columns)
                made.append(
                    remote(
                        weight.at[:, pl.ds(begin, columns)],
                        into.at[at, :, pl.ds(part * columns, columns)],
                        sems.at[0, sem, part],
                        sems.at[1, at, part],
                        (here.dp, peer),
                    )
                )
        return made

    return Spread(here, same, copies)


def gather_units(here, buf, send_sems, recv_sems, compute, between=None, ready=None, started=nothing):
    length = here.length
    last = length - 1
    steps = 2 * length
    mine = here.mine
    shorter = jnp.minimum(here.line, last - here.line)
    longer = jnp.where(here.line < last - here.line, 1, -1)

    def column(j):
        i = j - 1
        paired = jnp.where(i % 2 == 0, here.line - i // 2 - 1, here.line + i // 2 + 1)
        single = here.line + longer * (i - shorter + 1)
        return jnp.where(j == 0, here.line, jnp.where(i < 2 * shorter, paired, single))

    def copy(way, device, block, part):
        ref = buf.at[block, part]
        return remote(
            ref, ref, send_sems.at[way, block, part], recv_sems.at[block, part], device
        )

    def up(block, part):
        return copy(0, here.above(), block, part)

    def down(block, part):
        return copy(1, here.below(), block, part)

    def across(block, part):
        return copy(2, here.across(), block, part)

    def sideways(block, part):
        return copy(3, here.sibling(), block, part)

    def unit(number):
        in_column = (number % 2 == 1) & (number < steps - 1) | (number == 0)
        later = jnp.where(number == steps - 1, last, number // 2 - 1)
        line = column(jnp.where(in_column, (number + 1) // 2, later))
        pair = jnp.where(in_column, here.pair, 1 - here.pair)
        other = here.index(line, pair, 1 - here.core)
        sideways(other, 0).wait_recv()
        sideways(other, 1).wait_recv()
        compute(number, here.index(line, pair, 0))

    for part in range(2):
        pl.when(here.line < last)(lambda part=part: up(mine, part).start())
        pl.when(here.line > 0)(lambda part=part: down(mine, part).start())
        across(mine, part).start()
        sideways(mine, part).start()
    started()

    @pl.loop(0, steps)
    def _(step):
        part = step % 2
        far = step // 2 + 1

        @pl.when(here.line >= far)
        def _():
            block = here.index(here.line - far, here.pair, here.core)
            up(block, part).wait_recv()
            pl.when(here.line < last)(lambda: up(block, part).start())
            sideways(block, part).start()

        @pl.when(here.line + far <= last)
        def _():
            block = here.index(here.line + far, here.pair, here.core)
            down(block, part).wait_recv()
            pl.when(here.line > 0)(lambda: down(block, part).start())
            sideways(block, part).start()

        @pl.when(step + 2 < steps)
        def _():
            across(here.index(column(step // 2 + 1), here.pair, here.core), part).start()

        block = here.index(column(step // 2), 1 - here.pair, here.core)
        across(block, part).wait_recv()
        sideways(block, part).start()

        if between is not None:
            between(step)
        if ready is None:
            unit(step)
        else:
            begin = jnp.maximum(2 * (step - ready), 0)
            end = jnp.maximum(2 * (step + 1 - ready), 0)

            @pl.loop(begin, end)
            def _(number):
                unit(number)

    @pl.loop(0, length)
    def _(line):
        for part in range(2):
            block = here.index(line, here.pair, here.core)

            @pl.when((line <= here.line) & (here.line < last))
            def _():
                up(block, part).wait_send()

            @pl.when((line >= here.line) & (here.line > 0))
            def _():
                down(block, part).wait_send()

            across(block, part).wait_send()
            sideways(block, part).wait_send()
            sideways(here.index(line, 1 - here.pair, here.core), part).wait_send()


def put_own(here, own_ref, buf):
    half = buf.shape[2]
    for part in range(2):
        buf[here.mine, part] = own_ref[pl.ds(part * half, half), :]


def gather_scratch(seq, rows, width):
    return [
        pltpu.VMEM((seq, 2, rows, width), BF16),
        pltpu.SemaphoreType.DMA((4, seq, 2)),
        pltpu.SemaphoreType.DMA((seq, 2)),
    ]


def unit_rows(first, rows):
    return pl.ds(pl.multiple_of(first * rows, 2 * rows), 2 * rows)


def take_unit(buf, first):
    blocks = buf[pl.ds(first, 2)]
    return blocks.reshape(-1, blocks.shape[-1])


class UnitStore:
    def __init__(self, buf, out_ref, sems):
        self.buf, self.out_ref, self.sems = buf, out_ref, sems

    def copies(self, number, first):
        half = self.buf.shape[2]
        made = []
        for block in range(2):
            for part in range(2):
                begin = ((first + block) * 2 + part) * half
                made.append(
                    pltpu.make_async_copy(
                        self.buf.at[first + block, part],
                        self.out_ref.at[pl.ds(pl.multiple_of(begin, half), half)],
                        self.sems.at[number, block, part],
                    )
                )
        return made

    def start(self, number, first):
        for one in self.copies(number, first):
            one.start()

    def finish(self):
        @pl.loop(0, self.sems.shape[0])
        def _(number):
            for one in self.copies(number, 0):
                one.wait()


def params(call_id, mebibytes):
    return pltpu.CompilerParams(
        collective_id=call_id, has_side_effects=True, vmem_limit_bytes=mebibytes << 20
    )


def cost(flops, bytes_accessed):
    return pl.CostEstimate(flops=flops, bytes_accessed=bytes_accessed, transcendentals=0)


VMEM = pl.BlockSpec(memory_space=pltpu.VMEM)
HBM = pl.BlockSpec(memory_space=pl.ANY)


def rotated(values, cosine, sine):
    cols = values.shape[1]
    lane = lax.broadcasted_iota(jnp.int32, values.shape, 1)
    ahead = pltpu.roll(values, cols - HEAD_DIM // 2, 1)
    behind = pltpu.roll(values, HEAD_DIM // 2, 1)
    swapped = jnp.where(lane % HEAD_DIM < HEAD_DIM // 2, ahead, behind)
    return values * cosine + swapped * sine


def upright(row):
    count = row.shape[1]
    shape = (count, count)
    same = lax.broadcasted_iota(jnp.int32, shape, 0) == lax.broadcasted_iota(jnp.int32, shape, 1)
    return jnp.sum(jnp.where(same, row.astype(F32), 0.0), axis=1, keepdims=True)


def flat(column):
    count = column.shape[0]
    shape = (count, count)
    same = lax.broadcasted_iota(jnp.int32, shape, 0) == lax.broadcasted_iota(jnp.int32, shape, 1)
    return jnp.sum(jnp.where(same, column, 0.0), axis=0, keepdims=True)


def project_kernel(
    lengths_ref,
    tokens_ref,
    cotangent_ref,
    query_ref,
    key_ref,
    value_ref,
    gate_ref,
    up_ref,
    gain_one_ref,
    gain_two_ref,
    freq_ref,
    down_ref,
    output_ref,
    normed_ref,
    grads_ref,
    q_ref,
    k_ref,
    v_ref,
    cos_ref,
    sin_ref,
    open_ref,
    weight_ref,
    gate_out_ref,
    up_out_ref,
    feed_ref,
    down_out_ref,
    output_out_ref,
    buf,
    send_sems,
    recv_sems,
    blocks,
    store_sems,
    near_sems,
    far_sems,
    feed_sems,
    swap_sems,
    local_sems,
    pair_sems,
):
    here = Place()
    cols = q_ref.shape[1]
    rows = tokens_ref.shape[0]
    dp = here.dp
    ends = [lengths_ref[0, 0]]
    for j in range(1, DOCS):
        ends.append(ends[-1] + lengths_ref[0, j])

    def own_rows():
        chunk = 32

        @pl.loop(0, rows // chunk)
        def _(i):
            some = pl.ds(pl.multiple_of(i * chunk, chunk), chunk)
            values = tokens_ref[some, :].astype(F32)
            factor = lax.rsqrt(jnp.mean(values * values, axis=1, keepdims=True) + EPS)
            buf[here.mine, 0, some, :] = (values * factor).astype(BF16)
            shape = (chunk, cotangent_ref.shape[1])
            place = here.mine * rows + i * chunk + lax.broadcasted_iota(jnp.int32, shape, 0)
            grads = cotangent_ref[some, :].astype(F32)
            buf[here.mine, 1, some, :] = jnp.where(place < ends[-1], grads, 0.0).astype(BF16)

    def own_blocks():
        gain = upright(gain_one_ref[...])
        query = query_ref[...].astype(F32) * gain
        key = key_ref[...].astype(F32) * gain
        value = value_ref[...].astype(F32) * gain

        def heads(array, number, kept):
            parts = []
            for half in range(2):
                head = half * kept + number * kept // blocks.shape[0]
                parts.append(array[:, head * HEAD_DIM : (head + 1) * HEAD_DIM])
            return jnp.concatenate(parts, axis=1).astype(BF16)

        for number in range(blocks.shape[0]):
            blocks[number, :, :cols] = heads(query, number, HEADS // 2)
            blocks[number, :, cols : 2 * cols] = heads(key, number, KV_HEADS // 2)
            blocks[number, :, 2 * cols :] = heads(value, number, KV_HEADS // 2)

    def own_parts():
        own_blocks()
        own_rows()

    here.greet_all(own_parts)

    def weight_spread(same, sems):
        def copies(peer, sender, at, sem):
            return [
                remote(
                    blocks.at[peer],
                    weight_ref.at[dp, sender],
                    sems.at[0, sem],
                    sems.at[1, at],
                    (dp, peer),
                )
            ]

        return Spread(here, same, copies)

    near = weight_spread(True, near_sems)
    far = weight_spread(False, far_sems)
    swaps = []
    for number, (src, dst) in enumerate([(down_ref, down_out_ref), (output_ref, output_out_ref)]):
        swaps.append(
            remote(src, dst.at[dp], swap_sems.at[0, number], swap_sems.at[1, number], here.partner())
        )
        swaps.append(pltpu.make_async_copy(src, dst.at[dp], local_sems.at[number]))
    feed = feed_spread(here, True, (gate_out_ref, up_out_ref), feed_ref, feed_sems)
    columns = feed_ref.shape[2] // 4
    own_feed = []
    for kind, weight in enumerate((gate_out_ref, up_out_ref)):
        for half in range(2):
            part = kind * 2 + half
            begin = pl.multiple_of((half * here.count + here.mine) * columns, columns)
            own_feed.append(
                pltpu.make_async_copy(
                    weight.at[:, pl.ds(begin, columns)],
                    feed_ref.at[here.slot, :, pl.ds(part * columns, columns)],
                    local_sems.at[2 + part],
                )
            )

    def pair_copy(source, sender):
        return remote(
            weight_ref.at[source, sender],
            weight_ref.at[source, sender],
            pair_sems.at[0, sender],
            pair_sems.at[1, sender],
            here.partner(),
        )

    def own_tables():
        chunk = 128

        @pl.loop(0, open_ref.shape[0] // chunk)
        def _(i):
            some = pl.ds(pl.multiple_of(i * chunk, chunk), chunk)
            place = i * chunk + lax.broadcasted_iota(jnp.int32, (chunk, 1), 0)
            opening = jnp.zeros((chunk, 1), jnp.int32)
            for end in ends:
                opening = jnp.where(place >= end, end, opening)
            open_ref[some, :] = opening
            angles = (place - opening).astype(F32) * freq_ref[...]
            lane = lax.broadcasted_iota(jnp.int32, angles.shape, 1)
            sine = jnp.sin(angles)
            cos_ref[some, :] = jnp.cos(angles)
            sin_ref[some, :] = jnp.where(lane % HEAD_DIM < HEAD_DIM // 2, -sine, sine)

    def started():
        weight_ref[dp, here.mine] = blocks[here.mine]
        for one in swaps:
            one.start()
        chunk = 512

        @pl.loop(0, gate_ref.shape[1] // chunk)
        def _(i):
            some = pl.ds(pl.multiple_of(i * chunk, chunk), chunk)
            gain = upright(gain_two_ref[...])
            gate_out_ref[:, some] = (gate_ref[:, some].astype(F32) * gain).astype(BF16)
            up_out_ref[:, some] = (up_ref[:, some].astype(F32) * gain).astype(BF16)

        for one in own_feed:
            one.start()
        own_tables()

    def between(step):
        feed.start_some(step - (2 * here.length - 3), 3)

        @pl.when(step == 2)
        def _():
            near.finish()
            far.finish()

            @pl.loop(0, here.count)
            def _(sender):
                pair_copy(dp, sender).start()

        @pl.when(step == 4)
        def _():
            @pl.loop(0, here.count)
            def _(sender):
                pair_copy(1 - dp, sender).wait_recv()

    def stores(number, first):
        made = []
        for block in range(2):
            where = pl.ds(pl.multiple_of((first + block) * rows, rows), rows)
            for part, out_ref in enumerate((normed_ref, grads_ref)):
                made.append(
                    pltpu.make_async_copy(
                        buf.at[first + block, part],
                        out_ref.at[where],
                        store_sems.at[number, block, part],
                    )
                )
        return made

    def compute(number, first):
        for one in stores(number, first):
            one.start()
        weight = weight_ref[...].reshape(-1, weight_ref.shape[-1])
        unit = buf[pl.ds(first, 2), 0]
        qkv = dot(unit.reshape(-1, unit.shape[-1]), weight)
        where = unit_rows(first, rows)
        cosine = cos_ref[where, :]
        sine = sin_ref[where, :]
        scale = BF16(1.0 / math.sqrt(HEAD_DIM))
        q_ref[where, :] = rotated(qkv[:, :cols], cosine, sine).astype(BF16) * scale
        k_ref[where, :] = rotated(qkv[:, cols : 2 * cols], cosine, sine).astype(BF16)
        v_ref[where, :] = qkv[:, 2 * cols :].astype(BF16)

    far.start()
    near.start()
    gather_units(here, buf, send_sems, recv_sems, compute, between, here.length, started)

    @pl.loop(0, here.count)
    def _(sender):
        pair_copy(dp, sender).wait_send()

    @pl.loop(0, here.count // 2)
    def _(number):
        for one in stores(number, 0):
            one.wait()

    feed.finish()
    for one in swaps + own_feed:
        one.wait()


def gather_project(
    lengths, tokens, cotangent, query, key, value, gate, up, gains, freq, down, output, call_id
):
    seq = lax.axis_size("seq")
    rows, width = tokens.shape
    cols = 2 * HEAD_DIM
    slab, ff = gate.shape
    bf16 = lambda *shape: jax.ShapeDtypeStruct(shape, BF16)
    f32 = lambda *shape: jax.ShapeDtypeStruct(shape, F32)
    all_rows = seq * rows
    dma = pltpu.SemaphoreType.DMA
    return pl.pallas_call(
        project_kernel,
        out_shape=[
            bf16(all_rows, width),
            bf16(all_rows, width),
            bf16(all_rows, cols),
            bf16(all_rows, cols),
            bf16(all_rows, cols),
            f32(all_rows, cols),
            f32(all_rows, cols),
            jax.ShapeDtypeStruct((all_rows, 1), jnp.int32),
            bf16(2, seq, slab, 3 * cols),
            bf16(slab, ff),
            bf16(slab, ff),
            bf16(seq // 2, slab, 4 * down.shape[0]),
            bf16(2, *down.shape),
            bf16(2, *output.shape),
        ],
        in_specs=[pl.BlockSpec(memory_space=pltpu.SMEM)] + [VMEM] * 10 + [HBM] * 2,
        out_specs=[HBM] * 2 + [VMEM] * 9 + [HBM] * 3,
        scratch_shapes=gather_scratch(seq, rows, width)
        + [
            pltpu.VMEM((seq, slab, 3 * cols), BF16),
            dma((seq // 2, 2, 2)),
            dma((2, seq // 2)),
            dma((2, seq // 2)),
            dma((2, seq // 2, 4)),
            dma((2, 2)),
            dma((6,)),
            dma((2, seq)),
        ],
        compiler_params=params(call_id, 60),
        cost_estimate=cost(2 * all_rows * width * 3 * cols, 8 * all_rows * width),
    )(lengths, tokens, cotangent, query, key, value, gate, up, *gains, freq, down, output)


def attention_feed_kernel(
    block,
    q_ref,
    k_ref,
    v_ref,
    open_ref,
    gate_ref,
    up_ref,
    out_ref,
    lse_ref,
    feed_ref,
    low_ref,
    feed_sems,
):
    here = Place()
    feed = feed_spread(here, False, (gate_ref, up_ref), feed_ref, feed_sems)

    @pl.when(pl.program_id(0) == 0)
    def _():
        here.greet_all()
        feed.start()

    attention_kernel(block, q_ref, k_ref, v_ref, open_ref, out_ref, lse_ref)
    low_ref[...] = out_ref[...].astype(BF16)

    @pl.when(pl.program_id(0) == pl.num_programs(0) - 1)
    def _():
        feed.finish()


def attention_feed(queries, keys, values, opening, gate, up, feed_cols, block, call_id):
    seq = lax.axis_size("seq")
    rows, cols = queries.shape
    heads = cols // HEAD_DIM
    tiled = lambda width: pl.BlockSpec((block, width), lambda i: (i, 0))
    whole = pl.BlockSpec((rows, cols), lambda i: (0, 0))
    return pl.pallas_call(
        functools.partial(attention_feed_kernel, block),
        grid=(rows // block,),
        in_specs=[tiled(cols), whole, whole, tiled(1), HBM, HBM],
        out_specs=[tiled(cols), tiled(heads), HBM, tiled(cols)],
        out_shape=[
            jax.ShapeDtypeStruct((rows, cols), F32),
            jax.ShapeDtypeStruct((rows, heads), F32),
            jax.ShapeDtypeStruct((seq // 2, gate.shape[0], feed_cols), BF16),
            jax.ShapeDtypeStruct((rows, cols), BF16),
        ],
        scratch_shapes=[pltpu.SemaphoreType.DMA((2, seq // 2, 4))],
        compiler_params=params(call_id, 60),
        cost_estimate=cost(2 * rows * rows * cols, 10 * rows * cols),
    )(queries, keys, values, opening, gate, up)


ROW_CHUNK = 32


def norm_input_grad(values, upstream):
    factor = norm_factor(values)
    inner_mean = jnp.mean(upstream * values, axis=-1, keepdims=True)
    return factor * upstream - values * factor * factor * factor * inner_mean


def in_row_chunks(rows, chunk, visit):
    @pl.loop(0, rows // chunk)
    def _(i):
        visit(pl.ds(pl.multiple_of(i * chunk, chunk), chunk))


SCATTER_PARTS = 2
SCATTER_RING = 4
SCATTER_SCRATCH = 11


def scatter_rows_of_products(
    here,
    products,
    core_out,
    core_in,
    pair_out,
    pair_in,
    line_out,
    line_in,
    held,
    core_sems,
    pair_sems,
    line_sems,
    came_sems,
    early=None,
    between=nothing,
    filler=None,
):
    length = here.length
    parts = SCATTER_PARTS * len(products)
    rows, width = held.shape
    tile = min(width, 512)
    tiles = width // tile
    steps = length * parts

    def target(i):
        ups = length - 1 - here.line
        near = here.line < length // 2
        if_near = jnp.where(i < ups, length - 1 - i, i - ups)
        if_far = jnp.where(i < here.line, i, length - 1 - (i - here.line))
        return jnp.where(i == length - 1, here.line, jnp.where(near, if_near, if_far))

    def product(line, pair, core, part, use):
        first = pl.multiple_of(here.index(line, pair, core) * rows, rows)

        def one(number):
            transposed, a_ref, b_ref, _ = products[number]
            a = a_ref[pl.ds(first, rows), :]
            begin = (part - number * SCATTER_PARTS) * width

            @pl.loop(0, tiles)
            def _(t):
                into = pl.ds(pl.multiple_of(t * tile, tile), tile)
                cols = pl.ds(pl.multiple_of(begin + t * tile, tile), tile)
                use(dot_t(a, b_ref[cols, :]) if transposed else dot(a, b_ref[:, cols]), into)

        for number in range(len(products)):
            pl.when(part // SCATTER_PARTS == number)(functools.partial(one, number))

    def core_copy(slot):
        return remote(
            core_out.at[slot % SCATTER_RING],
            core_in.at[slot],
            core_sems.at[0, slot],
            core_sems.at[1, slot],
            here.sibling(),
        )

    def pair_copy(slot):
        return remote(
            pair_out.at[slot],
            pair_in.at[slot],
            pair_sems.at[0, slot],
            pair_sems.at[1, slot],
            here.across(),
        )

    def up_copy(slot, line, part):
        into = (line + 1) * parts + part
        return remote(
            line_out.at[slot], line_in.at[into], line_sems.at[slot], came_sems.at[into], here.above()
        )

    def down_copy(slot, line, part):
        into = line * parts + part
        return remote(
            line_out.at[slot], line_in.at[into], line_sems.at[slot], came_sems.at[into], here.below()
        )

    def for_sibling(step, pair, slot):
        pl.when(slot >= SCATTER_RING)(lambda: core_copy(slot - SCATTER_RING).wait_send())

        def use(value, cols):
            core_out[slot % SCATTER_RING, :, cols] = value.astype(BF16)

        product(target(step // parts), pair, 1 - here.core, step % parts, use)
        core_copy(slot).start()

    for_sibling(jnp.int32(0), 1 - here.pair, jnp.int32(0))

    @pl.loop(0, steps)
    def _(step):
        pl.when(step < steps - 1)(lambda: for_sibling(step + 1, 1 - here.pair, step + 1))
        core_copy(step).wait_recv()

        def use(value, cols):
            pair_out[step, :, cols] = (value + core_in[step, :, cols].astype(F32)).astype(BF16)

        product(target(step // parts), 1 - here.pair, here.core, step % parts, use)
        pair_copy(step).start()
        if early is not None:
            early(step)

    for_sibling(jnp.int32(0), here.pair, jnp.int32(steps))
    between()

    @pl.loop(0, steps)
    def _(step):
        pl.when(step < steps - 1)(lambda: for_sibling(step + 1, here.pair, steps + step + 1))
        core_copy(steps + step).wait_recv()
        line = target(step // parts)
        part = step % parts

        def use(value, cols):
            held[:, cols] = value + core_in[steps + step, :, cols].astype(F32)

        product(line, here.pair, here.core, part, use)
        if filler is not None:
            filler(step)
        pair_copy(step).wait_recv()
        from_above = (line <= here.line) & (here.line < length - 1)
        from_below = (line >= here.line) & (here.line > 0)
        held[...] += pair_in[step].astype(F32)

        @pl.when(from_above)
        def _():
            down_copy(0, line, part).wait_recv()
            held[...] += line_in[line * parts + part].astype(F32)

        @pl.when(from_below)
        def _():
            up_copy(0, line, part).wait_recv()
            held[...] += line_in[(line + 1) * parts + part].astype(F32)

        for number, (_, _, _, out_ref) in enumerate(products):

            @pl.when((line == here.line) & (part // SCATTER_PARTS == number))
            def _():
                begin = (part - number * SCATTER_PARTS) * width
                out_ref[:, pl.ds(pl.multiple_of(begin, width), width)] = held[...]

        @pl.when(line < here.line)
        def _():
            line_out[step] = held[...].astype(BF16)
            down_copy(step, line, part).start()

        @pl.when(line > here.line)
        def _():
            line_out[step] = held[...].astype(BF16)
            up_copy(step, line, part).start()

    @pl.loop(2 * steps - SCATTER_RING, 2 * steps)
    def _(slot):
        core_copy(slot).wait_send()

    @pl.loop(0, steps)
    def _(step):
        pair_copy(step).wait_send()
        line = target(step // parts)
        pl.when(line < here.line)(lambda: down_copy(step, 0, 0).wait_send())
        pl.when(line > here.line)(lambda: up_copy(step, 0, 0).wait_send())


def scatter_scratch(seq, rows, width, count=1):
    length = seq // 4
    parts = SCATTER_PARTS * count
    steps = length * parts
    block = (rows, width // SCATTER_PARTS)
    dma = pltpu.SemaphoreType.DMA
    return [
        pltpu.VMEM((SCATTER_RING, *block), BF16),
        pltpu.VMEM((2 * steps, *block), BF16),
        pltpu.VMEM((steps, *block), BF16),
        pltpu.VMEM((steps, *block), BF16),
        pltpu.VMEM((steps, *block), BF16),
        pltpu.VMEM(((length + 1) * parts, *block), BF16),
        pltpu.VMEM(block, F32),
        dma((2, 2 * steps)),
        dma((2, steps)),
        dma((steps,)),
        dma(((length + 1) * parts,)),
    ]


def scatter_cost(a, width):
    return cost(2 * a.shape[0] * a.shape[1] * width, 4 * a.shape[0] * width)


def scatter_both_kernel(
    back_ref,
    turned_ref,
    hidden_ref,
    down_ref,
    middle_ref,
    grads_hbm,
    normed_hbm,
    grad_ref,
    low_ref,
    mixed_ref,
    sums_ref,
    *scratch,
):
    here = Place()
    normed, away, came, own, fetch_sems, swap_sems, own_sem = scratch[SCATTER_SCRATCH:]
    rows = grad_ref.shape[0]
    own_copy = pltpu.make_async_copy(
        grads_hbm.at[pl.ds(pl.multiple_of(here.mine * rows, rows), rows)], own, own_sem.at[0]
    )
    own_copy.start()
    here.greet(partner=True)
    chunk = normed.shape[2]
    half = normed_hbm.shape[1] // 2
    chunks = half // chunk

    def fetch(number):
        dp = jnp.where(number < chunks, 1 - here.dp, here.dp)
        begin = dp * half + number % chunks * chunk
        return pltpu.make_async_copy(
            normed_hbm.at[:, pl.ds(pl.multiple_of(begin, chunk), chunk)],
            normed.at[number % 2],
            fetch_sems.at[number % 2],
        )

    def swap(i):
        some = pl.ds(pl.multiple_of(i * chunk, chunk), chunk)
        return remote(
            away.at[some], came.at[some], swap_sems.at[0, i], swap_sems.at[1, i], here.partner()
        )

    def part(number):
        fetch(number).wait()
        pl.when(number + 1 < 2 * chunks)(lambda: fetch(number + 1).start())
        return t_dot(normed[number % 2], back_ref[...])

    def filler(step):
        @pl.when(step < chunks)
        def _():
            some = pl.ds(pl.multiple_of(step * chunk, chunk), chunk)
            away[some, :] = part(step).astype(BF16)
            swap(step).start()

        @pl.when((step >= chunks) & (step < 3 * chunks) & (step % 2 == 0))
        def _():
            i = (step - chunks) // 2
            some = pl.ds(pl.multiple_of(i * chunk, chunk), chunk)
            kept = part(chunks + i)
            swap(i).wait()
            sums_ref[some, :] = (kept + came[some, :].astype(F32)).astype(BF16)

    fetch(jnp.int32(0)).start()
    scatter_rows_of_products(
        here,
        [(False, back_ref, turned_ref, grad_ref), (False, hidden_ref, down_ref, mixed_ref)],
        *scratch[:SCATTER_SCRATCH],
        filler=filler,
    )
    own_copy.wait()

    def add(some):
        grad = own[some, :].astype(F32) + norm_input_grad(middle_ref[some, :], grad_ref[some, :])
        grad_ref[some, :] = grad
        low_ref[some, :] = grad.astype(BF16)

    in_row_chunks(rows, ROW_CHUNK, add)


def product_scatter_both(back, turned, hidden, down, middle, grads, normed, call_id):
    seq = lax.axis_size("seq")
    rows = back.shape[0] // seq
    width = turned.shape[1]
    cols = back.shape[1]
    chunk = width // 8
    dma = pltpu.SemaphoreType.DMA
    return pl.pallas_call(
        scatter_both_kernel,
        out_shape=[
            jax.ShapeDtypeStruct((rows, width), F32),
            jax.ShapeDtypeStruct((rows, width), BF16),
            jax.ShapeDtypeStruct((rows, width), F32),
            jax.ShapeDtypeStruct((width // 2, cols), BF16),
        ],
        in_specs=[VMEM] * 5 + [HBM] * 2,
        out_specs=[VMEM] * 4,
        scratch_shapes=scatter_scratch(seq, rows, width, 2)
        + [
            pltpu.VMEM((2, normed.shape[0], chunk), BF16),
            pltpu.VMEM((width // 2, cols), BF16),
            pltpu.VMEM((width // 2, cols), BF16),
            pltpu.VMEM((rows, width), BF16),
            dma((2,)),
            dma((2, 4)),
            dma((1,)),
        ],
        compiler_params=params(call_id, 60),
        cost_estimate=scatter_cost(back, 3 * width),
    )(back, turned, hidden, down, middle, grads, normed)


def scatter_feed_kernel(
    a_ref, b_ref, tokens_ref, near_ref, far_ref, middle_ref, normed_ref, feed_ref, *scratch
):
    here = Place()
    here.greet(partner=True)
    swap_sems, local_sems = scratch[SCATTER_SCRATCH:]
    slots = near_ref.shape[0]

    def copies(half, ref, slot):
        place = feed_ref.at[here.dp, here.peer(slot, half == 0)]
        return (
            remote(
                ref.at[slot],
                place,
                swap_sems.at[0, half, slot],
                swap_sems.at[1, half, slot],
                here.partner(),
            ),
            pltpu.make_async_copy(ref.at[slot], place, local_sems.at[half, slot]),
        )

    @pl.loop(0, slots)
    def _(slot):
        for half, ref in enumerate((near_ref, far_ref)):
            for one in copies(half, ref, slot):
                one.start()

    scatter_rows_of_products(
        here, [(False, a_ref, b_ref, middle_ref)], *scratch[:SCATTER_SCRATCH]
    )

    def add(some):
        middle = tokens_ref[some, :].astype(F32) + middle_ref[some, :]
        middle_ref[some, :] = middle
        normed_ref[some, :] = (middle * norm_factor(middle)).astype(BF16)

    in_row_chunks(middle_ref.shape[0], ROW_CHUNK, add)

    @pl.loop(0, slots)
    def _(slot):
        for half, ref in enumerate((near_ref, far_ref)):
            for one in copies(half, ref, slot):
                one.wait()


def product_scatter_feed(a, b, tokens, near, far, call_id):
    seq = lax.axis_size("seq")
    rows = a.shape[0] // seq
    width = b.shape[1]
    dma = pltpu.SemaphoreType.DMA
    return pl.pallas_call(
        scatter_feed_kernel,
        out_shape=[
            jax.ShapeDtypeStruct((rows, width), F32),
            jax.ShapeDtypeStruct((rows, width), BF16),
            jax.ShapeDtypeStruct((2, seq, *near.shape[1:]), BF16),
        ],
        in_specs=[VMEM, VMEM, VMEM, HBM, HBM],
        out_specs=[VMEM, VMEM, HBM],
        scratch_shapes=scatter_scratch(seq, rows, width)
        + [dma((2, 2, seq // 2)), dma((2, seq // 2))],
        compiler_params=params(call_id, 40),
        cost_estimate=scatter_cost(a, width),
    )(a, b, tokens, near, far)


def feed_kernel(
    own_ref,
    grad_hbm,
    feed_hbm,
    down_hbm,
    normed_ref,
    hidden_out_ref,
    back_out_ref,
    turned_out_ref,
    buf,
    send_sems,
    recv_sems,
    store_sems,
    grad_ref,
    feed_ref,
    down_ref,
    hidden_ref,
    back_ref,
    turned_ref,
    fetch_sems,
    out_sems,
):
    here = Place()
    fetches = [
        pltpu.make_async_copy(src, dst, fetch_sems.at[number])
        for number, (src, dst) in enumerate(
            [(feed_hbm, feed_ref), (down_hbm, down_ref), (grad_hbm, grad_ref)]
        )
    ]
    for one in fetches:
        one.start()
    put_own(here, own_ref, buf)
    here.greet()
    rows = own_ref.shape[0]
    width = own_ref.shape[1]
    hidden = hidden_ref.shape[1]
    tile = 256
    store = UnitStore(buf, normed_ref, store_sems)

    def outs(number, first):
        where = unit_rows(first, rows)
        share = width // (2 * here.length)
        some = pl.ds(pl.multiple_of(number * share, share), share)
        return [
            pltpu.make_async_copy(src, dst, out_sems.at[number, i])
            for i, (src, dst) in enumerate(
                [
                    (hidden_ref.at[where], hidden_out_ref.at[where]),
                    (back_ref.at[where], back_out_ref.at[where]),
                    (turned_ref.at[:, some], turned_out_ref.at[:, some]),
                ]
            )
        ]

    def compute(number, first):
        store.start(number, first)

        @pl.when(number == 0)
        def _():
            for one in fetches:
                one.wait()

        where = unit_rows(first, rows)
        normed = take_unit(buf, first)
        grad = grad_ref[where, :]

        @pl.loop(0, hidden // tile)
        def _(t):
            cols = pl.ds(pl.multiple_of(t * tile, tile), tile)
            later = pl.ds(pl.multiple_of(hidden + t * tile, tile), tile)
            gate = dot(normed, feed_ref[:, cols])
            upward = dot(normed, feed_ref[:, later])
            hidden_grad = dot_t(grad, down_ref[cols, :])
            sigmoid = jax.nn.sigmoid(gate)
            silu = gate * sigmoid
            hidden_ref[where, cols] = (silu * upward).astype(BF16)
            back_ref[where, cols] = (
                hidden_grad * upward * sigmoid * (1.0 + gate * (1.0 - sigmoid))
            ).astype(BF16)
            back_ref[where, later] = (hidden_grad * silu).astype(BF16)

        share = width // (2 * here.length)
        some = pl.ds(pl.multiple_of(number * share, share), share)
        turned_ref[:, some] = feed_ref[some, :].T
        for one in outs(number, first):
            one.start()

    gather_units(here, buf, send_sems, recv_sems, compute)

    @pl.loop(0, here.count // 2)
    def _(number):
        for one in outs(number, 0):
            one.wait()

    store.finish()


def gather_feed(own, grad_out, feed_weight, down_weight, call_id):
    seq = lax.axis_size("seq")
    rows, width = own.shape
    hidden = down_weight.shape[0]
    return pl.pallas_call(
        feed_kernel,
        out_shape=[
            jax.ShapeDtypeStruct((seq * rows, width), BF16),
            jax.ShapeDtypeStruct((seq * rows, hidden), BF16),
            jax.ShapeDtypeStruct((seq * rows, 2 * hidden), BF16),
            jax.ShapeDtypeStruct((2 * hidden, width), BF16),
        ],
        in_specs=[VMEM] + [HBM] * 3,
        out_specs=[HBM] * 4,
        scratch_shapes=gather_scratch(seq, rows // 2, width)
        + [
            pltpu.SemaphoreType.DMA((seq // 2, 2, 2)),
            pltpu.VMEM((seq * rows, width), BF16),
            pltpu.VMEM((width, 2 * hidden), BF16),
            pltpu.VMEM((hidden, width), BF16),
            pltpu.VMEM((seq * rows, hidden), BF16),
            pltpu.VMEM((seq * rows, 2 * hidden), BF16),
            pltpu.VMEM((2 * hidden, width), BF16),
            pltpu.SemaphoreType.DMA((3,)),
            pltpu.SemaphoreType.DMA((seq // 2, 3)),
        ],
        compiler_params=params(call_id, 60),
        cost_estimate=cost(8 * seq * rows * width * hidden, 8 * seq * rows * width),
    )(own, grad_out, feed_weight, down_weight)


def back_kernel(
    own_ref,
    weight_ref,
    attended_ref,
    hidden_hbm,
    out_grad_hbm,
    blocks_ref,
    grad_ref,
    output_kept_ref,
    output_away_ref,
    down_kept_ref,
    down_away_ref,
    near_ref,
    buf,
    send_sems,
    recv_sems,
    near_sems,
    own_sem,
    part,
    hidden_ref,
    out_grad_ref,
    fetch_sems,
):
    here = Place()
    fetches = [
        pltpu.make_async_copy(hidden_hbm, hidden_ref, fetch_sems.at[0]),
        pltpu.make_async_copy(out_grad_hbm, out_grad_ref, fetch_sems.at[1]),
    ]
    for one in fetches:
        one.start()
    put_own(here, own_ref, buf)
    here.greet_all()
    rows = own_ref.shape[0]
    width = own_ref.shape[1]
    tile = 512
    near = block_spread(here, True, blocks_ref, near_ref, near_sems)
    own = pltpu.make_async_copy(blocks_ref.at[here.mine], near_ref.at[here.slot], own_sem.at[0])

    own.start()

    def between(step):
        near.start_some(step - here.length, 2)

    part[...] = jnp.zeros_like(part)
    share = width // (2 * here.length)

    def split(values, kept_ref, away_ref, cols):
        half = values.shape[0] // 2
        top, bottom = values[:half], values[half:]
        kept_ref[:, cols] = jnp.where(here.dp == 0, top, bottom)
        away_ref[:, cols] = jnp.where(here.dp == 0, bottom, top).astype(BF16)

    def compute(number, first):
        where = unit_rows(first, rows)
        unit = take_unit(buf, first)
        grad_ref[where, :] = dot_t(unit, weight_ref[...]).astype(BF16)
        attended = attended_ref[where, :]
        for t in range(width // tile):
            cols = slice(t * tile, (t + 1) * tile)
            part[:, cols] += t_dot(attended, unit[:, cols])
        some = pl.ds(pl.multiple_of(number * share, share), share)

        @pl.when(number == 0)
        def _():
            for one in fetches:
                one.wait()

        split(t_dot(hidden_ref[...], out_grad_ref[:, some]), down_kept_ref, down_away_ref, some)

    gather_units(here, buf, send_sems, recv_sems, compute, between)
    for t in range(width // tile):
        cols = slice(t * tile, (t + 1) * tile)
        split(part[:, cols], output_kept_ref, output_away_ref, cols)
    near.finish()
    own.wait()


def gather_back(own, weight, attended, hidden, grad_out, blocks, call_id):
    seq = lax.axis_size("seq")
    rows, width = own.shape
    cols = weight.shape[0]
    return pl.pallas_call(
        back_kernel,
        out_shape=[
            jax.ShapeDtypeStruct((seq * rows, cols), BF16),
            jax.ShapeDtypeStruct((cols // 2, width), F32),
            jax.ShapeDtypeStruct((cols // 2, width), BF16),
            jax.ShapeDtypeStruct((hidden.shape[1] // 2, width), F32),
            jax.ShapeDtypeStruct((hidden.shape[1] // 2, width), BF16),
            jax.ShapeDtypeStruct((seq // 2, *blocks.shape[1:]), BF16),
        ],
        in_specs=[VMEM] * 3 + [HBM] * 3,
        out_specs=[VMEM] * 5 + [HBM],
        scratch_shapes=gather_scratch(seq, rows // 2, width)
        + [
            pltpu.SemaphoreType.DMA((2, seq // 2)),
            pltpu.SemaphoreType.DMA((1,)),
            pltpu.VMEM((cols, width), F32),
            pltpu.VMEM(hidden.shape, BF16),
            pltpu.VMEM(grad_out.shape, BF16),
            pltpu.SemaphoreType.DMA((2,)),
        ],
        compiler_params=params(call_id, 60),
        cost_estimate=cost(8 * seq * rows * width * cols, 6 * seq * rows * width),
    )(own, weight, attended, hidden, grad_out, blocks)


def attention_back_feed_kernel(
    block,
    q_ref,
    k_ref,
    v_ref,
    g_ref,
    att_ref,
    lse_ref,
    open_ref,
    cos_ref,
    sin_ref,
    blocks_ref,
    down_ref,
    output_ref,
    back_ref,
    feed_ref,
    down_out_ref,
    output_out_ref,
    dq_ref,
    dk_ref,
    dv_ref,
    feed_sems,
    swap_sems,
):
    here = Place()
    tile = pl.program_id(0)
    cols = q_ref.shape[1]
    feed = block_spread(here, False, blocks_ref, feed_ref, feed_sems)
    swaps = [
        remote(src, dst, swap_sems.at[0, number], swap_sems.at[1, number], here.partner())
        for number, (src, dst) in enumerate(
            [(down_ref, down_out_ref), (output_ref, output_out_ref)]
        )
    ]

    @pl.when(tile == 0)
    def _():
        here.greet_all()
        feed.start()
        for one in swaps:
            one.start()

    attention_back_kernel(
        block, q_ref, k_ref, v_ref, g_ref, att_ref, lse_ref, open_ref, dq_ref, dk_ref, dv_ref
    )
    where = pl.ds(pl.multiple_of(tile * block, block), block)
    scale = 1.0 / math.sqrt(HEAD_DIM)
    cosine = cos_ref[where, :]
    sine = sin_ref[where, :]
    back_ref[where, :cols] = rotated(dq_ref[...] * scale, cosine, -sine).astype(BF16)

    @pl.when(tile == pl.num_programs(0) - 1)
    def _():
        @pl.loop(0, pl.num_programs(0))
        def _(i):
            rows = pl.ds(pl.multiple_of(i * block, block), block)
            keys = rotated(dk_ref[rows, :], cos_ref[rows, :], -sin_ref[rows, :])
            back_ref[rows, cols : 2 * cols] = keys.astype(BF16)
            back_ref[rows, 2 * cols :] = dv_ref[rows, :].astype(BF16)

        feed.finish()
        for one in swaps:
            one.wait()


def attention_back_feed(
    queries,
    keys,
    values,
    grads,
    attended,
    log_total,
    opening,
    cosine,
    sine,
    blocks,
    down,
    output,
    block,
    call_id,
):
    seq = lax.axis_size("seq")
    rows, cols = queries.shape
    heads = cols // HEAD_DIM
    tiled = lambda width: pl.BlockSpec((block, width), lambda i: (i, 0))
    whole = pl.BlockSpec((rows, cols), lambda i: (0, 0))
    dma = pltpu.SemaphoreType.DMA
    return pl.pallas_call(
        functools.partial(attention_back_feed_kernel, block),
        grid=(rows // block,),
        in_specs=[tiled(cols), whole, whole, tiled(cols), tiled(cols), tiled(heads), tiled(1)]
        + [whole, whole, HBM, HBM, HBM],
        out_specs=[pl.BlockSpec((rows, 3 * cols), lambda i: (0, 0)), HBM, HBM, HBM],
        out_shape=[
            jax.ShapeDtypeStruct((rows, 3 * cols), BF16),
            jax.ShapeDtypeStruct((seq // 2, *blocks.shape[1:]), BF16),
            jax.ShapeDtypeStruct(down.shape, BF16),
            jax.ShapeDtypeStruct(output.shape, BF16),
        ],
        scratch_shapes=[
            pltpu.VMEM((block, cols), F32),
            pltpu.VMEM((rows, cols), F32),
            pltpu.VMEM((rows, cols), F32),
            dma((2, seq // 2)),
            dma((2, 2)),
        ],
        compiler_params=params(call_id, 60),
        cost_estimate=cost(5 * rows * rows * cols, 20 * rows * cols),
    )(
        queries,
        keys,
        values,
        grads,
        attended,
        log_total,
        opening,
        cosine,
        sine,
        blocks,
        down,
        output,
    )


def scatter_last_kernel(a_ref, b_ref, normed_hbm, out_ref, qkv_ref, *scratch):
    here = Place()
    normed_ref, kept, away, came, sums, near_sems, far_sems, swap_sems, fetch_sems = scratch[
        SCATTER_SCRATCH:
    ]
    fetch = pltpu.make_async_copy(normed_hbm, normed_ref, fetch_sems.at[0])
    fetch.start()
    here.greet_all()
    swap = remote(away, came, swap_sems.at[0], swap_sems.at[1], here.partner())
    near = block_spread(here, True, sums, qkv_ref.at[0], near_sems)
    far = block_spread(here, False, sums, qkv_ref.at[1], far_sems)
    half = away.shape[0]
    chunk = 256

    def part(dp, i):
        first = pl.multiple_of(dp * half + i * chunk, chunk)
        return t_dot(normed_ref[:, pl.ds(first, chunk)], a_ref[...])

    def early(step):
        @pl.when(step == 1)
        def _():
            fetch.wait()

            @pl.loop(0, half // chunk)
            def _(i):
                some = pl.ds(pl.multiple_of(i * chunk, chunk), chunk)
                away[some, :] = part(1 - here.dp, i).astype(BF16)

            swap.start()

    def between():
        @pl.loop(0, half // chunk)
        def _(i):
            kept[pl.ds(pl.multiple_of(i * chunk, chunk), chunk), :] = part(here.dp, i)

    begin = 2
    each = 3

    def filler(step):
        @pl.when(step == begin)
        def _():
            swap.wait_recv()
            slab = sums.shape[1]

            @pl.loop(0, here.count)
            def _(i):
                rows = pl.ds(pl.multiple_of(i * slab, slab), slab)
                sums[i] = (kept[rows, :] + came[rows, :].astype(F32)).astype(BF16)

            qkv_ref[0, here.slot] = sums[here.mine]

        @pl.when(step > begin)
        def _():
            @pl.loop(0, each)
            def _(i):
                number = (step - begin - 1) * each + i
                pl.when(number < far.slots)(lambda: far.start_one(number))

                @pl.when((number >= far.slots) & (number < 2 * far.slots - 1))
                def _():
                    near.start_one(number - far.slots + 1)

    scatter_rows_of_products(
        here,
        [(True, a_ref, b_ref, out_ref)],
        *scratch[:SCATTER_SCRATCH],
        early,
        between,
        filler,
    )
    swap.wait_send()
    near.finish()
    far.finish()


def product_scatter_last(a, b, normed, call_id):
    seq = lax.axis_size("seq")
    rows = a.shape[0] // seq
    width, cols = b.shape
    slab = width // (2 * seq)
    dma = pltpu.SemaphoreType.DMA
    return pl.pallas_call(
        scatter_last_kernel,
        out_shape=[
            jax.ShapeDtypeStruct((rows, width), F32),
            jax.ShapeDtypeStruct((2, seq // 2, slab, cols), BF16),
        ],
        in_specs=[VMEM, VMEM, HBM],
        out_specs=[VMEM, VMEM],
        scratch_shapes=scatter_scratch(seq, rows, width)
        + [
            pltpu.VMEM(normed.shape, BF16),
            pltpu.VMEM((width // 2, cols), F32),
            pltpu.VMEM((width // 2, cols), BF16),
            pltpu.VMEM((width // 2, cols), BF16),
            pltpu.VMEM((seq, slab, cols), BF16),
            dma((2, seq // 2)),
            dma((2, seq // 2)),
            dma((2,)),
            dma((1,)),
        ],
        compiler_params=params(call_id, 60),
        cost_estimate=scatter_cost(a, width),
    )(a, b, normed)


def unpack_kernel(
    pair_ref,
    near_gate_ref,
    far_gate_ref,
    near_up_ref,
    far_up_ref,
    gate_ref,
    up_ref,
    qkv_ref,
    query_ref,
    key_ref,
    value_ref,
    gain_one_ref,
    gain_two_ref,
    tokens_ref,
    middle_ref,
    mixed_sum_ref,
    middle_grad_ref,
    upstream_ref,
    down_kept_ref,
    down_came_ref,
    output_kept_ref,
    output_came_ref,
    gate_out_ref,
    up_out_ref,
    query_out_ref,
    key_out_ref,
    value_out_ref,
    one_out_ref,
    two_out_ref,
    mixed_ref,
    token_grad_ref,
    down_out_ref,
    output_out_ref,
    total_two,
):
    pair = pair_ref[0]
    dp = lax.axis_size("dp")
    length = qkv_ref.shape[1] // 2
    slab = qkv_ref.shape[2]
    step = pl.program_id(0) * pl.num_programs(1) + pl.program_id(1)
    columns = near_gate_ref.shape[2]

    def along(grad, weight):
        return jnp.sum(grad * weight.astype(F32), axis=1, keepdims=True)

    @pl.when(step == 0)
    def _():
        total_two[...] = jnp.zeros_like(total_two)
        total = jnp.zeros((slab, 1), F32)
        gain = upright(gain_one_ref[...])

        def put(out_ref, weight_ref, begin, grad):
            cols = slice(begin, begin + grad.shape[1])
            out_ref[:, cols] = grad * gain
            return along(grad, weight_ref[:, cols])

        pairs = [{}, {}]
        for line in range(length):
            rows = []
            for number in range(4):
                slot = line * 2 + number % 2
                near, far = qkv_ref[0, slot].astype(F32), qkv_ref[1, slot].astype(F32)
                rows.append(jnp.where(number // 2 == pair, near, far))
            kv = rows[0] + rows[1] + rows[2] + rows[3]
            for half in range(dp):
                cols = slice(half * HEAD_DIM, (half + 1) * HEAD_DIM)
                for number in (0, 2):
                    two = jnp.concatenate([rows[number][:, cols], rows[number + 1][:, cols]], axis=1)
                    begin = (half * length * 4 + line * 4 + number) * HEAD_DIM
                    total = total + put(query_out_ref, query_ref, begin, two)
                for kind in range(2):
                    begin = ((kind + 1) * dp + half) * HEAD_DIM
                    pairs[kind][half, line] = kv[:, begin : begin + HEAD_DIM]
        for kind, (out_ref, weight_ref) in enumerate(
            [(key_out_ref, key_ref), (value_out_ref, value_ref)]
        ):
            for half in range(dp):
                for line in range(0, length, 2):
                    two = [pairs[kind][half, line], pairs[kind][half, line + 1]]
                    begin = (half * length + line) * HEAD_DIM
                    total = total + put(
                        out_ref, weight_ref, begin, jnp.concatenate(two, axis=1)
                    )
        one_out_ref[...] = flat(total)

    mixed_ref[...] = middle_ref[...] + mixed_sum_ref[...]
    token_grad_ref[...] = middle_grad_ref[...] + norm_input_grad(
        tokens_ref[...].astype(F32), upstream_ref[...]
    )
    down_out_ref[...] = down_kept_ref[...] + down_came_ref[...].astype(F32)
    output_out_ref[...] = output_kept_ref[...] + output_came_ref[...].astype(F32)
    gain_two = upright(gain_two_ref[...])
    total = jnp.zeros((slab, 1), F32)
    for near_ref, far_ref, weight_ref, out_ref in (
        (near_gate_ref, far_gate_ref, gate_ref, gate_out_ref),
        (near_up_ref, far_up_ref, up_ref, up_out_ref),
    ):
        for number in range(4):
            core = number % 2
            near, far = near_ref[core].astype(F32), far_ref[core].astype(F32)
            grad = jnp.where(number // 2 == pair, near, far)
            cols = slice(number * columns, (number + 1) * columns)
            total = total + along(grad, weight_ref[:, cols])
            out_ref[:, cols] = grad * gain_two
    total_two[...] += total

    @pl.when(step == pl.num_programs(0) * pl.num_programs(1) - 1)
    def _():
        two_out_ref[...] = flat(total_two[...])


def unpack(pair, near, far, gate, up, qkv, query, key, value, gain_one, gain_two, *rows):
    dp = lax.axis_size("dp")
    seq = lax.axis_size("seq")
    slab, ff = gate.shape
    length = seq // 4
    columns = ff // (dp * seq)
    whole = lambda array: pl.BlockSpec(array.shape, lambda j, i: (0,) * array.ndim)
    block = lambda kind: pl.BlockSpec((2, slab, columns), lambda j, i: (i, 0, kind * dp + j))
    tile = pl.BlockSpec((slab, 4 * columns), lambda j, i: (0, j * length + i))
    f32 = lambda array: jax.ShapeDtypeStruct(array.shape, F32)
    outs = [f32(gate), f32(up), f32(query), f32(key), f32(value), f32(gain_one), f32(gain_two)]
    sums = [f32(rows[0]), f32(rows[0]), f32(rows[5]), f32(rows[7])]
    steps = dp * length
    strip = lambda array: pl.BlockSpec(
        (array.shape[0] // steps, array.shape[1]), lambda j, i: (j * length + i, 0)
    )
    return pl.pallas_call(
        unpack_kernel,
        grid=(dp, length),
        in_specs=[pl.BlockSpec(memory_space=pltpu.SMEM)]
        + [block(0), block(0), block(1), block(1), tile, tile]
        + [whole(array) for array in (qkv, query, key, value, gain_one, gain_two)]
        + [strip(array) for array in rows],
        out_specs=[tile, tile]
        + [whole(array) for array in outs[2:]]
        + [strip(array) for array in sums],
        out_shape=outs + sums,
        scratch_shapes=[pltpu.VMEM((slab, 1), F32)],
        compiler_params=pltpu.CompilerParams(vmem_limit_bytes=40 << 20),
        cost_estimate=cost(slab * ff, 16 * slab * ff),
    )(
        pair,
        near,
        far,
        near,
        far,
        gate,
        up,
        qkv,
        query,
        key,
        value,
        gain_one,
        gain_two,
        *rows,
    )


def swap_dp(values):
    count = lax.axis_size("dp")
    return lax.ppermute(values, "dp", [(i, (i + 1) % count) for i in range(count)])


def gather_dp(values):
    return lax.all_gather(values, "dp", axis=0, tiled=True)


def sum_dp(partial):
    half = partial.shape[0] // 2
    mine = lax.axis_index("dp")
    away = lax.dynamic_slice_in_dim(partial, (1 - mine) * half, half, 0).astype(BF16)
    kept = lax.dynamic_slice_in_dim(partial, mine * half, half, 0)
    return kept + swap_dp(away).astype(F32)


def gather_rows(values):
    return lax.all_gather(values, "seq", axis=0, tiled=True)


def scatter_rows(partial):
    return lax.psum_scatter(partial.astype(BF16), "seq", scatter_dimension=0, tiled=True).astype(F32)


def exchange(blocks):
    return lax.all_to_all(blocks, "seq", split_axis=0, concat_axis=0, tiled=True)


def norm_factor(values):
    return lax.rsqrt(jnp.mean(values * values, axis=-1, keepdims=True) + EPS)


def norm_back(inputs, factor, gain_row, upstream):
    scaled_up = gain_row * upstream
    inner_mean = jnp.mean(scaled_up * inputs, axis=-1, keepdims=True)
    grad_in = factor * scaled_up - inputs * factor * factor * factor * inner_mean
    grad_gain = jnp.sum(upstream * inputs * factor, axis=0)
    return grad_in, grad_gain


def plain_shards(
    tokens,
    cotangent,
    doc_lengths,
    attn_gain,
    mlp_gain,
    query_weight,
    key_weight,
    value_weight,
    output_weight,
    gate_weight,
    up_weight,
    down_weight,
):
    dp = lax.axis_size("dp")
    seq = lax.axis_size("seq")
    mine = lax.axis_index("seq")
    tok_count, width = tokens.shape
    rows = tok_count * seq
    slab = query_weight.shape[0]
    share = HEAD_DIM // slab
    half_heads = HEADS // dp
    half_kv = KV_HEADS // dp
    hidden_dev = down_weight.shape[0]
    block = 512

    doc_ends = jnp.cumsum(doc_lengths[0])
    place = jnp.arange(rows, dtype=jnp.int32)
    passed = doc_ends[None, :] <= place[:, None]
    opening = jnp.max(jnp.where(passed, doc_ends[None, :], 0), axis=1)
    position = place - opening
    keeping = place < doc_ends[DOCS - 1]
    angles = position.astype(F32)[:, None] * rotary_table(HEAD_DIM)[None, :]
    cosine = jnp.cos(angles)
    sine = jnp.sin(angles)
    cos_heads = jnp.tile(cosine, (1, 2 * dp))
    sin_heads = jnp.tile(jnp.concatenate([-sine, sine], axis=1), (1, dp))
    own_keeping = lax.dynamic_slice_in_dim(keeping, mine * tok_count, tok_count, 0)

    def head_columns(weight, kept):
        split = weight.reshape(slab, dp, kept, HEAD_DIM)
        return jnp.repeat(split, seq // kept, axis=2)

    qkv_blocks = jnp.stack(
        [
            head_columns(query_weight, half_heads),
            head_columns(key_weight, half_kv),
            head_columns(value_weight, half_kv),
        ],
        axis=1,
    )
    qkv_blocks = jnp.transpose(qkv_blocks, (3, 0, 1, 2, 4)).reshape(seq * slab, 3 * dp * HEAD_DIM)
    qkv_weight = gather_dp(exchange(qkv_blocks))
    feed_blocks = jnp.stack(
        [w.reshape(slab, dp, seq, hidden_dev) for w in (gate_weight, up_weight)], axis=1
    )
    feed_blocks = jnp.transpose(feed_blocks, (3, 0, 1, 2, 4)).reshape(
        seq * slab, 2 * dp * hidden_dev
    )
    feed_weight = gather_dp(exchange(feed_blocks))
    down_own = gather_dp(down_weight)
    output_own = output_weight
    if share > 1:
        groups = [list(range(i, i + share)) for i in range(0, seq, share)]
        output_own = lax.all_gather(
            output_own, "seq", axis=0, tiled=True, axis_index_groups=groups
        )
    output_own = gather_dp(output_own)
    gains = lax.all_gather(
        jnp.stack([attn_gain, mlp_gain]), ("dp", "seq"), axis=1, tiled=True
    ).astype(F32)
    gain_one, gain_two = gains[0], gains[1]

    inputs_all = gather_rows(tokens).astype(F32)
    normed_one = (inputs_all * norm_factor(inputs_all) * gain_one).astype(BF16)
    qkv = dot(normed_one, qkv_weight)
    head_cols = dp * HEAD_DIM
    query_lin, key_lin = qkv[:, :head_cols], qkv[:, head_cols : 2 * head_cols]
    values = qkv[:, 2 * head_cols :].astype(BF16)
    scale = 1.0 / math.sqrt(HEAD_DIM)
    queries = (query_lin * cos_heads + swap_halves(query_lin) * sin_heads).astype(BF16) * BF16(scale)
    keys = (key_lin * cos_heads + swap_halves(key_lin) * sin_heads).astype(BF16)
    attended_sum, log_total = attention(queries, keys, values, opening[:, None], block)
    if share > 1:
        own_rows = ((place // tok_count) % share == mine % share)[:, None]
        attended_sum = jnp.where(own_rows, attended_sum, 0.0)
    attended = attended_sum.astype(BF16)
    inputs = tokens.astype(F32)
    middle = inputs + scatter_rows(dot(attended, output_own))

    factor_two = norm_factor(middle)
    normed_two = gather_rows((middle * factor_two * gain_two).astype(BF16))
    grad_own = jnp.where(own_keeping[:, None], cotangent, BF16(0))
    grad_out = gather_rows(grad_own)
    feed = dot(normed_two, feed_weight)
    feed_cols = dp * hidden_dev
    gate_lin, upward = feed[:, :feed_cols], feed[:, feed_cols:]
    sigmoid = jax.nn.sigmoid(gate_lin)
    hidden = (gate_lin * sigmoid * upward).astype(BF16)
    hidden_grad = dot_t(grad_out, down_own)
    gate_back = (hidden_grad * upward * sigmoid * (1.0 + gate_lin * (1.0 - sigmoid))).astype(BF16)
    up_back = (hidden_grad * gate_lin * sigmoid).astype(BF16)
    feed_back = jnp.concatenate([gate_back, up_back], axis=1)
    normed_two_grad = scatter_rows(dot_t(feed_back, feed_weight))
    mixed = middle + scatter_rows(dot(hidden, down_own))
    middle_in, gain_two_part = norm_back(middle, factor_two, gain_two, normed_two_grad)
    middle_grad = grad_own.astype(F32) + middle_in
    middle_back = gather_rows(middle_grad.astype(BF16))

    attended_grad = dot_t(middle_back, output_own).astype(BF16)
    if share > 1:
        attended_grad = jnp.where(own_rows, attended_grad, BF16(0))
    query_acc, key_acc, value_acc = attention_back(
        queries, keys, values, attended_grad, attended_sum, log_total, opening[:, None], block
    )
    query_acc = query_acc * scale
    query_back = query_acc * cos_heads - swap_halves(query_acc) * sin_heads
    key_back = key_acc * cos_heads - swap_halves(key_acc) * sin_heads
    qkv_back = jnp.concatenate([query_back, key_back, value_acc], axis=1).astype(BF16)
    normed_one_grad = scatter_rows(dot_t(qkv_back, qkv_weight))
    input_in, gain_one_part = norm_back(inputs, norm_factor(inputs), gain_one, normed_one_grad)
    token_grad = middle_grad + input_in

    feed_grad = exchange(sum_dp(t_dot(normed_two, feed_back)).astype(BF16)).astype(F32)
    feed_grad = feed_grad.reshape(seq, slab, 2, dp, hidden_dev)
    feed_grad = jnp.transpose(feed_grad, (2, 1, 3, 0, 4)).reshape(2, slab, dp * seq * hidden_dev)
    down_grad = sum_dp(t_dot(hidden, grad_out))
    output_part = t_dot(attended, middle_back)
    if share > 1:
        split = output_part.reshape(dp, share, slab, width)
        split = jnp.transpose(split, (1, 0, 2, 3)).reshape(share * dp * slab, width)
        output_part = lax.psum_scatter(
            split, "seq", scatter_dimension=0, tiled=True, axis_index_groups=groups
        )
    output_grad = sum_dp(output_part)
    qkv_grad = exchange(sum_dp(t_dot(normed_one, qkv_back)).astype(BF16)).astype(F32)
    qkv_grad = qkv_grad.reshape(seq, slab, 3, dp, HEAD_DIM)

    def own_columns(part, kept):
        summed = jnp.sum(part.reshape(kept, seq // kept, slab, dp, HEAD_DIM), axis=1)
        return jnp.transpose(summed, (1, 2, 0, 3)).reshape(slab, dp * kept * HEAD_DIM)

    query_grad = own_columns(qkv_grad[:, :, 0], half_heads)
    key_grad = own_columns(qkv_grad[:, :, 1], half_kv)
    value_grad = own_columns(qkv_grad[:, :, 2], half_kv)
    gain_parts = lax.psum(jnp.stack([gain_one_part, gain_two_part]), ("dp", "seq"))
    own = lax.axis_index("dp") * seq + mine
    gain_grads = lax.dynamic_slice_in_dim(gain_parts, own * slab, slab, 1)
    return (
        mixed,
        token_grad,
        gain_grads[0],
        gain_grads[1],
        query_grad,
        key_grad,
        value_grad,
        output_grad,
        feed_grad[0],
        feed_grad[1],
        down_grad,
    )


def frequencies():
    exponent = np.arange(0, HEAD_DIM, 2, dtype=np.float32) / np.float32(HEAD_DIM)
    inverse = np.power(np.float32(500000.0), -exponent)
    wavelength = np.float32(2.0 * math.pi) / inverse
    smooth = (np.float32(8192.0) / wavelength - np.float32(1.0)) / np.float32(3.0)
    blended = (np.float32(1.0) - smooth) * inverse / np.float32(32.0) + smooth * inverse
    scaled = np.where(
        wavelength < 2048.0,
        inverse,
        np.where(wavelength > 8192.0, inverse / np.float32(32.0), blended),
    )
    return np.tile(scaled.astype(np.float32), 4)


FREQUENCIES = frequencies()


def shards(
    tokens,
    cotangent,
    doc_lengths,
    attn_gain,
    mlp_gain,
    query_weight,
    key_weight,
    value_weight,
    output_weight,
    gate_weight,
    up_weight,
    down_weight,
):
    dp = lax.axis_size("dp")
    seq = lax.axis_size("seq")
    mine = lax.axis_index("seq")
    tok_count, width = tokens.shape
    slab = query_weight.shape[0]
    block = 512
    gain_one = attn_gain[None, :]
    gain_two = mlp_gain[None, :]

    (
        normed_one,
        grad_out,
        queries,
        keys,
        values,
        cosine,
        sine,
        opening,
        qkv_weight,
        gate_scaled,
        up_scaled,
        feed_near,
        down_own,
        output_own,
    ) = gather_project(
        doc_lengths,
        tokens,
        cotangent,
        query_weight,
        key_weight,
        value_weight,
        gate_weight,
        up_weight,
        (gain_one, gain_two),
        jnp.asarray(FREQUENCIES)[None, :],
        down_weight,
        output_weight,
        0,
    )
    qkv_weight = qkv_weight.reshape(width, -1)
    down_own = down_own.reshape(-1, width)
    output_own = output_own.reshape(-1, width)
    attended_sum, log_total, feed_far, attended = attention_feed(
        queries,
        keys,
        values,
        opening,
        gate_scaled,
        up_scaled,
        feed_near.shape[2],
        block,
        1,
    )
    middle, middle_normed, feed_weight = product_scatter_feed(
        attended, output_own, tokens, feed_near, feed_far, 2
    )
    feed_weight = feed_weight.reshape(width, -1)

    normed_two, hidden, feed_back, feed_turned = gather_feed(
        middle_normed, grad_out, feed_weight, down_own, 3
    )
    middle_grad, middle_back, mixed_sum, feed_sums = product_scatter_both(
        feed_back, feed_turned, hidden, down_own, middle, grad_out, normed_two, 4
    )
    feed_sums = feed_sums.reshape(seq, slab, -1)
    attended_grad, output_kept, output_away, down_kept, down_away, feed_grad_near = gather_back(
        middle_back, output_own, attended, hidden, grad_out, feed_sums, 5
    )

    qkv_back, feed_grad_far, down_came, output_came = attention_back_feed(
        queries,
        keys,
        values,
        attended_grad,
        attended_sum,
        log_total,
        opening,
        cosine,
        sine,
        feed_sums,
        down_away,
        output_away,
        block,
        6,
    )
    normed_one_grad, qkv_grads = product_scatter_last(qkv_back, qkv_weight, normed_one, 7)

    pair = ((mine // 2) % 2).reshape(1)
    (
        gate_grad,
        up_grad,
        query_grad,
        key_grad,
        value_grad,
        attn_gain_grad,
        mlp_gain_grad,
        mixed,
        token_grad,
        down_grad,
        output_grad,
    ) = unpack(
        pair,
        feed_grad_near,
        feed_grad_far,
        gate_weight,
        up_weight,
        qkv_grads,
        query_weight,
        key_weight,
        value_weight,
        gain_one,
        gain_two,
        tokens,
        middle,
        mixed_sum,
        middle_grad,
        normed_one_grad,
        down_kept,
        down_came,
        output_kept,
        output_came,
    )
    return (
        mixed,
        token_grad,
        attn_gain_grad[0],
        mlp_gain_grad[0],
        query_grad,
        key_grad,
        value_grad,
        output_grad,
        gate_grad,
        up_grad,
        down_grad,
    )


def solution(mesh):
    both = P(("dp", "seq"), None)
    line = P(("dp", "seq"))
    dp, seq = mesh.shape["dp"], mesh.shape["seq"]

    def run(*args):
        tokens = args[0].shape[0]
        width = args[0].shape[1]
        suits = dp == 2 and seq % 4 == 0 and width == dp * seq * HEAD_DIM
        suits = suits and 2 * (tokens // dp) * width <= 16 << 20
        return jax.shard_map(
            shards if suits else plain_shards,
            mesh=mesh,
            in_specs=(both, both, P("dp", None), line, line) + (both,) * 7,
            out_specs=(both, both, line, line) + (both,) * 7,
            check_vma=False,
        )(*args)

    return run
```

```python
import functools
import math

import jax
import jax.numpy as jnp
import numpy as np
from jax import lax
from jax.experimental import pallas as pl
from jax.experimental.pallas import tpu as pltpu
from jax.sharding import PartitionSpec as P

HEADS = 32
KV_HEADS = 8
HEAD_DIM = 64
DOCS = 4
EPS = 1e-05
NEG = -1e30
MESH = pl.DeviceIdType.MESH
F32 = jnp.float32
BF16 = jnp.bfloat16


def rotary_table(head_dim):
    exponent = jnp.arange(0, head_dim, 2, dtype=F32) / head_dim
    inverse = jnp.power(F32(500000.0), -exponent)
    wavelength = 2.0 * math.pi / inverse
    smooth = (8192.0 / wavelength - 1.0) / 3.0
    blended = (1.0 - smooth) * inverse / 32.0 + smooth * inverse
    return jnp.where(
        wavelength < 2048.0, inverse, jnp.where(wavelength > 8192.0, inverse / 32.0, blended)
    )


def swap_halves(values):
    rows, cols = values.shape
    halves = values.reshape(rows, cols // HEAD_DIM, 2, HEAD_DIM // 2)
    return halves[:, :, ::-1].reshape(rows, cols)


def dot(a, b):
    return jnp.dot(a, b, preferred_element_type=F32)


def dot_t(a, b):
    return lax.dot_general(a, b, (((1,), (1,)), ((), ())), preferred_element_type=F32)


def t_dot(a, b):
    return lax.dot_general(a, b, (((0,), (0,)), ((), ())), preferred_element_type=F32)


def allowed_tile(opening, q_first, k_first, shape):
    rows = q_first + lax.broadcasted_iota(jnp.int32, shape, 0)
    cols = k_first + lax.broadcasted_iota(jnp.int32, shape, 1)
    return (cols <= rows) & (cols >= opening)


def attention_kernel(block, q_ref, k_ref, v_ref, open_ref, out_ref, lse_ref):
    tile = pl.program_id(0)
    opening = open_ref[...]
    heads = [
        slice(i * HEAD_DIM, (i + 1) * HEAD_DIM) for i in range(q_ref.shape[1] // HEAD_DIM)
    ]

    def step(j, carry):
        first = pl.multiple_of(j * block, block)
        allowed = allowed_tile(opening, tile * block, first, (block, block))
        after = []
        for lanes, (peak, total, acc) in zip(heads, carry):
            scores = dot_t(q_ref[:, lanes], k_ref[pl.ds(first, block), lanes])
            scores = jnp.where(allowed, scores, NEG)
            new_peak = jnp.maximum(peak, jnp.max(scores, axis=1, keepdims=True))
            spread = jnp.exp(scores - new_peak)
            fade = jnp.exp(peak - new_peak)
            total = total * fade + jnp.sum(spread, axis=1, keepdims=True)
            acc = acc * fade + dot(spread.astype(BF16), v_ref[pl.ds(first, block), lanes])
            after.append((new_peak, total, acc))
        return tuple(after)

    start = (
        jnp.full((block, 1), NEG, F32),
        jnp.zeros((block, 1), F32),
        jnp.zeros((block, HEAD_DIM), F32),
    )
    done = lax.fori_loop(0, tile + 1, step, (start,) * len(heads))
    for head, (lanes, (peak, total, acc)) in enumerate(zip(heads, done)):
        out_ref[:, lanes] = acc / total
        lse_ref[:, head : head + 1] = peak + jnp.log(total)


def attention(queries, keys, values, opening, block):
    rows, cols = queries.shape
    heads = cols // HEAD_DIM
    tiled = lambda width: pl.BlockSpec((block, width), lambda i: (i, 0))
    whole = pl.BlockSpec((rows, cols), lambda i: (0, 0))
    return pl.pallas_call(
        functools.partial(attention_kernel, block),
        grid=(rows // block,),
        in_specs=[tiled(cols), whole, whole, tiled(1)],
        out_specs=[tiled(cols), tiled(heads)],
        out_shape=[
            jax.ShapeDtypeStruct((rows, cols), F32),
            jax.ShapeDtypeStruct((rows, heads), F32),
        ],
        compiler_params=pltpu.CompilerParams(vmem_limit_bytes=48 << 20),
        cost_estimate=pl.CostEstimate(
            flops=2 * rows * rows * cols, bytes_accessed=10 * rows * cols, transcendentals=0
        ),
    )(queries, keys, values, opening)


def attention_back_kernel(
    block, q_ref, k_ref, v_ref, g_ref, att_ref, lse_ref, open_ref, dq_ref, dk_ref, dv_ref
):
    tile = pl.program_id(0)

    @pl.when(tile == 0)
    def _():
        dk_ref[...] = jnp.zeros_like(dk_ref)
        dv_ref[...] = jnp.zeros_like(dv_ref)

    opening = open_ref[...]
    heads = []
    for head in range(q_ref.shape[1] // HEAD_DIM):
        lanes = slice(head * HEAD_DIM, (head + 1) * HEAD_DIM)
        grad = g_ref[:, lanes].astype(F32)
        row_sum = jnp.sum(grad * att_ref[:, lanes], axis=1, keepdims=True)
        heads.append((lanes, lse_ref[:, head : head + 1], row_sum))

    def step(j, carry):
        first = pl.multiple_of(j * block, block)
        here = pl.ds(first, block)
        allowed = allowed_tile(opening, tile * block, first, (block, block))
        after = []
        for (lanes, log_total, row_sum), acc in zip(heads, carry):
            query, grad, key = q_ref[:, lanes], g_ref[:, lanes], k_ref[here, lanes]
            scores = dot_t(query, key)
            chance = jnp.where(allowed, jnp.exp(scores - log_total), 0.0)
            prob_grad = dot_t(grad, v_ref[here, lanes])
            score_grad = (chance * (prob_grad - row_sum)).astype(BF16)
            dk_ref[here, lanes] += t_dot(score_grad, query)
            dv_ref[here, lanes] += t_dot(chance.astype(BF16), grad)
            after.append(acc + dot(score_grad, key))
        return tuple(after)

    start = jnp.zeros((block, HEAD_DIM), F32)
    done = lax.fori_loop(0, tile + 1, step, (start,) * len(heads))
    for (lanes, _, _), acc in zip(heads, done):
        dq_ref[:, lanes] = acc


def attention_back(queries, keys, values, grads, attended, log_total, opening, block):
    rows, cols = queries.shape
    heads = cols // HEAD_DIM
    tiled = lambda width: pl.BlockSpec((block, width), lambda i: (i, 0))
    whole = pl.BlockSpec((rows, cols), lambda i: (0, 0))
    return pl.pallas_call(
        functools.partial(attention_back_kernel, block),
        grid=(rows // block,),
        in_specs=[tiled(cols), whole, whole, tiled(cols), tiled(cols), tiled(heads), tiled(1)],
        out_specs=[tiled(cols), whole, whole],
        out_shape=[jax.ShapeDtypeStruct((rows, cols), F32)] * 3,
        compiler_params=pltpu.CompilerParams(vmem_limit_bytes=60 << 20),
        cost_estimate=pl.CostEstimate(
            flops=5 * rows * rows * cols, bytes_accessed=20 * rows * cols, transcendentals=0
        ),
    )(queries, keys, values, grads, attended, log_total, opening)


def nothing():
    pass


class Place:
    def __init__(self):
        self.dp = lax.axis_index("dp")
        self.mine = lax.axis_index("seq")
        self.count = lax.axis_size("seq")
        self.length = self.count // 4
        self.line = lax.div(self.mine, 4)
        self.pair = lax.rem(lax.div(self.mine, 2), 2)
        self.core = lax.rem(self.mine, 2)
        self.slot = self.line * 2 + self.core

    def index(self, line, pair, core):
        return (line * 2 + pair) * 2 + core

    def peer(self, slot, same):
        pair = self.pair if same else 1 - self.pair
        return self.index(lax.div(slot, 2), pair, lax.rem(slot, 2))

    def device(self, line, pair, core):
        return (self.dp, self.index(line, pair, core))

    def sibling(self):
        return self.device(self.line, self.pair, 1 - self.core)

    def across(self):
        return self.device(self.line, 1 - self.pair, self.core)

    def above(self):
        return self.device(self.line + 1, self.pair, self.core)

    def below(self):
        return self.device(self.line - 1, self.pair, self.core)

    def partner(self):
        return (1 - self.dp, self.mine)

    def greet(self, partner=False):
        barrier = pltpu.get_barrier_semaphore()

        def signal(device):
            pl.semaphore_signal(barrier, inc=1, device_id=device, device_id_type=MESH)

        signal(self.sibling())
        signal(self.across())
        pl.when(self.line > 0)(lambda: signal(self.below()))
        pl.when(self.line < self.length - 1)(lambda: signal(self.above()))
        if partner:
            signal(self.partner())
        inner = (self.line > 0) & (self.line < self.length - 1)
        pl.semaphore_wait(barrier, jnp.where(inner, 4, 3) + (1 if partner else 0))

    def greet_all(self, meanwhile=nothing):
        self.call_all()
        meanwhile()
        self.await_all()

    def await_all(self):
        pl.semaphore_wait(pltpu.get_barrier_semaphore(), self.count)

    def call_all(self):
        barrier = pltpu.get_barrier_semaphore()

        def signal(device):
            pl.semaphore_signal(barrier, inc=1, device_id=device, device_id_type=MESH)

        signal(self.partner())

        @pl.loop(1, self.count)
        def _(ahead):
            signal((self.dp, lax.rem(self.mine + ahead, self.count)))


def remote(src, dst, send_sem, recv_sem, device):
    return pltpu.make_async_remote_copy(
        src_ref=src,
        dst_ref=dst,
        send_sem=send_sem,
        recv_sem=recv_sem,
        device_id=device,
        device_id_type=MESH,
    )


class Spread:
    def __init__(self, here, same, copies):
        self.here, self.same, self.copies = here, same, copies
        self.slots = here.count // 2

    def each(self, visit):
        @pl.loop(1 if self.same else 0, self.slots)
        def _(ahead):
            slot = lax.rem(self.here.slot + ahead, self.slots)
            visit(self.here.peer(slot, self.same), slot)

    def start_one(self, ahead):
        slot = lax.rem(self.here.slot + ahead, self.slots)
        peer = self.here.peer(slot, self.same)
        for one in self.copies(peer, self.here.mine, self.here.slot, slot):
            one.start()

    def start(self):
        pl.loop(1 if self.same else 0, self.slots)(self.start_one)

    def start_some(self, number, each):
        first = 1 if self.same else 0

        @pl.loop(0, each)
        def _(i):
            ahead = first + number * each + i
            pl.when((number >= 0) & (ahead < self.slots))(lambda: self.start_one(ahead))

    def finish(self):
        def visit(peer, slot):
            for one in self.copies(peer, peer, slot, slot):
                one.wait()

        self.each(visit)


def block_spread(here, same, blocks, into, sems):
    def copies(peer, sender, at, sem):
        return [
            remote(
                blocks.at[peer],
                into.at[at],
                sems.at[0, sem],
                sems.at[1, at],
                (here.dp, peer),
            )
        ]

    return Spread(here, same, copies)


def feed_spread(here, same, weights, into, sems):
    dp = lax.axis_size("dp")
    columns = into.shape[2] // (dp * len(weights))

    def copies(peer, sender, at, sem):
        made = []
        for kind, weight in enumerate(weights):
            for half in range(dp):
                part = kind * dp + half
                begin = pl.multiple_of((half * here.count + peer) * columns, columns)
                made.append(
                    remote(
                        weight.at[:, pl.ds(begin, columns)],
                        into.at[at, :, pl.ds(part * columns, columns)],
                        sems.at[0, sem, part],
                        sems.at[1, at, part],
                        (here.dp, peer),
                    )
                )
        return made

    return Spread(here, same, copies)


def gather_units(here, buf, send_sems, recv_sems, compute, between=None, ready=None, started=nothing):
    length = here.length
    last = length - 1
    steps = 2 * length
    mine = here.mine
    shorter = jnp.minimum(here.line, last - here.line)
    longer = jnp.where(here.line < last - here.line, 1, -1)

    def column(j):
        i = j - 1
        paired = jnp.where(i % 2 == 0, here.line - i // 2 - 1, here.line + i // 2 + 1)
        single = here.line + longer * (i - shorter + 1)
        return jnp.where(j == 0, here.line, jnp.where(i < 2 * shorter, paired, single))

    def copy(way, device, block, part):
        ref = buf.at[block, part]
        return remote(
            ref, ref, send_sems.at[way, block, part], recv_sems.at[block, part], device
        )

    def up(block, part):
        return copy(0, here.above(), block, part)

    def down(block, part):
        return copy(1, here.below(), block, part)

    def across(block, part):
        return copy(2, here.across(), block, part)

    def sideways(block, part):
        return copy(3, here.sibling(), block, part)

    def unit(number):
        in_column = (number % 2 == 1) & (number < steps - 1) | (number == 0)
        later = jnp.where(number == steps - 1, last, number // 2 - 1)
        line = column(jnp.where(in_column, (number + 1) // 2, later))
        pair = jnp.where(in_column, here.pair, 1 - here.pair)
        other = here.index(line, pair, 1 - here.core)
        sideways(other, 0).wait_recv()
        sideways(other, 1).wait_recv()
        compute(number, here.index(line, pair, 0))

    for part in range(2):
        pl.when(here.line < last)(lambda part=part: up(mine, part).start())
        pl.when(here.line > 0)(lambda part=part: down(mine, part).start())
        across(mine, part).start()
        sideways(mine, part).start()
    started()

    @pl.loop(0, steps)
    def _(step):
        part = step % 2
        far = step // 2 + 1

        @pl.when(here.line >= far)
        def _():
            block = here.index(here.line - far, here.pair, here.core)
            up(block, part).wait_recv()
            pl.when(here.line < last)(lambda: up(block, part).start())
            sideways(block, part).start()

        @pl.when(here.line + far <= last)
        def _():
            block = here.index(here.line + far, here.pair, here.core)
            down(block, part).wait_recv()
            pl.when(here.line > 0)(lambda: down(block, part).start())
            sideways(block, part).start()

        @pl.when(step + 2 < steps)
        def _():
            across(here.index(column(step // 2 + 1), here.pair, here.core), part).start()

        block = here.index(column(step // 2), 1 - here.pair, here.core)
        across(block, part).wait_recv()
        sideways(block, part).start()

        if between is not None:
            between(step)
        if ready is None:
            unit(step)
        else:
            begin = jnp.maximum(2 * (step - ready), 0)
            end = jnp.maximum(2 * (step + 1 - ready), 0)

            @pl.loop(begin, end)
            def _(number):
                unit(number)

    @pl.loop(0, length)
    def _(line):
        for part in range(2):
            block = here.index(line, here.pair, here.core)

            @pl.when((line <= here.line) & (here.line < last))
            def _():
                up(block, part).wait_send()

            @pl.when((line >= here.line) & (here.line > 0))
            def _():
                down(block, part).wait_send()

            across(block, part).wait_send()
            sideways(block, part).wait_send()
            sideways(here.index(line, 1 - here.pair, here.core), part).wait_send()


def put_own(here, own_ref, buf):
    half = buf.shape[2]
    for part in range(2):
        buf[here.mine, part] = own_ref[pl.ds(part * half, half), :]


def gather_scratch(seq, rows, width):
    return [
        pltpu.VMEM((seq, 2, rows, width), BF16),
        pltpu.SemaphoreType.DMA((4, seq, 2)),
        pltpu.SemaphoreType.DMA((seq, 2)),
    ]


def unit_rows(first, rows):
    return pl.ds(pl.multiple_of(first * rows, 2 * rows), 2 * rows)


def take_unit(buf, first):
    blocks = buf[pl.ds(first, 2)]
    return blocks.reshape(-1, blocks.shape[-1])


class UnitStore:
    def __init__(self, buf, out_ref, sems):
        self.buf, self.out_ref, self.sems = buf, out_ref, sems

    def copies(self, number, first):
        half = self.buf.shape[2]
        made = []
        for block in range(2):
            for part in range(2):
                begin = ((first + block) * 2 + part) * half
                made.append(
                    pltpu.make_async_copy(
                        self.buf.at[first + block, part],
                        self.out_ref.at[pl.ds(pl.multiple_of(begin, half), half)],
                        self.sems.at[number, block, part],
                    )
                )
        return made

    def start(self, number, first):
        for one in self.copies(number, first):
            one.start()

    def finish(self):
        @pl.loop(0, self.sems.shape[0])
        def _(number):
            for one in self.copies(number, 0):
                one.wait()


def params(call_id, mebibytes):
    return pltpu.CompilerParams(
        collective_id=call_id, has_side_effects=True, vmem_limit_bytes=mebibytes << 20
    )


def cost(flops, bytes_accessed):
    return pl.CostEstimate(flops=flops, bytes_accessed=bytes_accessed, transcendentals=0)


VMEM = pl.BlockSpec(memory_space=pltpu.VMEM)
HBM = pl.BlockSpec(memory_space=pl.ANY)


def rotated(values, cosine, sine):
    cols = values.shape[1]
    lane = lax.broadcasted_iota(jnp.int32, values.shape, 1)
    ahead = pltpu.roll(values, cols - HEAD_DIM // 2, 1)
    behind = pltpu.roll(values, HEAD_DIM // 2, 1)
    swapped = jnp.where(lane % HEAD_DIM < HEAD_DIM // 2, ahead, behind)
    return values * cosine + swapped * sine


def upright(row):
    count = row.shape[1]
    shape = (count, count)
    same = lax.broadcasted_iota(jnp.int32, shape, 0) == lax.broadcasted_iota(jnp.int32, shape, 1)
    return jnp.sum(jnp.where(same, row.astype(F32), 0.0), axis=1, keepdims=True)


def flat(column):
    count = column.shape[0]
    shape = (count, count)
    same = lax.broadcasted_iota(jnp.int32, shape, 0) == lax.broadcasted_iota(jnp.int32, shape, 1)
    return jnp.sum(jnp.where(same, column, 0.0), axis=0, keepdims=True)


def project_kernel(
    lengths_ref,
    tokens_ref,
    cotangent_ref,
    query_ref,
    key_ref,
    value_ref,
    gate_ref,
    up_ref,
    gain_one_ref,
    gain_two_ref,
    freq_ref,
    down_ref,
    output_ref,
    normed_ref,
    grads_ref,
    q_ref,
    k_ref,
    v_ref,
    cos_ref,
    sin_ref,
    open_ref,
    weight_ref,
    gate_out_ref,
    up_out_ref,
    feed_ref,
    down_out_ref,
    output_out_ref,
    buf,
    send_sems,
    recv_sems,
    blocks,
    store_sems,
    near_sems,
    far_sems,
    feed_sems,
    swap_sems,
    local_sems,
    pair_sems,
    share_sems,
):
    here = Place()
    cols = q_ref.shape[1]
    rows = tokens_ref.shape[0]
    dp = here.dp
    ends = [lengths_ref[0, 0]]
    for j in range(1, DOCS):
        ends.append(ends[-1] + lengths_ref[0, j])

    def own_rows():
        chunk = 32

        @pl.loop(0, rows // chunk)
        def _(i):
            some = pl.ds(pl.multiple_of(i * chunk, chunk), chunk)
            values = tokens_ref[some, :].astype(F32)
            factor = lax.rsqrt(jnp.mean(values * values, axis=1, keepdims=True) + EPS)
            buf[here.mine, 0, some, :] = (values * factor).astype(BF16)
            shape = (chunk, cotangent_ref.shape[1])
            place = here.mine * rows + i * chunk + lax.broadcasted_iota(jnp.int32, shape, 0)
            grads = cotangent_ref[some, :].astype(F32)
            buf[here.mine, 1, some, :] = jnp.where(place < ends[-1], grads, 0.0).astype(BF16)

    def own_blocks():
        gain = upright(gain_one_ref[...])
        query = query_ref[...].astype(F32) * gain
        key = key_ref[...].astype(F32) * gain
        value = value_ref[...].astype(F32) * gain

        def heads(array, number, kept):
            parts = []
            for half in range(2):
                head = half * kept + number * kept // blocks.shape[0]
                parts.append(array[:, head * HEAD_DIM : (head + 1) * HEAD_DIM])
            return jnp.concatenate(parts, axis=1).astype(BF16)

        for number in range(blocks.shape[0]):
            blocks[number, :, :cols] = heads(query, number, HEADS // 2)
            array = value if number % 2 else key
            blocks[number, :, cols:] = heads(array, number, KV_HEADS // 2)

    def own_parts():
        own_blocks()
        own_rows()

    here.greet_all(own_parts)

    def weight_spread(same, sems):
        def copies(peer, sender, at, sem):
            return [
                remote(
                    blocks.at[peer],
                    weight_ref.at[dp, sender],
                    sems.at[0, sem],
                    sems.at[1, at],
                    (dp, peer),
                )
            ]

        return Spread(here, same, copies)

    near = weight_spread(True, near_sems)
    far = weight_spread(False, far_sems)
    swaps = []
    for number, (src, dst) in enumerate([(down_ref, down_out_ref), (output_ref, output_out_ref)]):
        swaps.append(
            remote(src, dst.at[dp], swap_sems.at[0, number], swap_sems.at[1, number], here.partner())
        )
        swaps.append(pltpu.make_async_copy(src, dst.at[dp], local_sems.at[number]))
    feed = feed_spread(here, True, (gate_out_ref, up_out_ref), feed_ref, feed_sems)
    columns = feed_ref.shape[2] // 4
    own_feed = []
    for kind, weight in enumerate((gate_out_ref, up_out_ref)):
        for half in range(2):
            part = kind * 2 + half
            begin = pl.multiple_of((half * here.count + here.mine) * columns, columns)
            own_feed.append(
                pltpu.make_async_copy(
                    weight.at[:, pl.ds(begin, columns)],
                    feed_ref.at[here.slot, :, pl.ds(part * columns, columns)],
                    local_sems.at[2 + part],
                )
            )

    def pair_copy(source, sender):
        return remote(
            weight_ref.at[source, sender],
            weight_ref.at[source, sender],
            pair_sems.at[0, sender],
            pair_sems.at[1, sender],
            here.partner(),
        )

    def own_tables():
        chunk = 128

        @pl.loop(0, open_ref.shape[0] // chunk)
        def _(i):
            some = pl.ds(pl.multiple_of(i * chunk, chunk), chunk)
            place = i * chunk + lax.broadcasted_iota(jnp.int32, (chunk, 1), 0)
            opening = jnp.zeros((chunk, 1), jnp.int32)
            for end in ends:
                opening = jnp.where(place >= end, end, opening)
            open_ref[some, :] = opening
            angles = (place - opening).astype(F32) * freq_ref[...]
            lane = lax.broadcasted_iota(jnp.int32, angles.shape, 1)
            sine = jnp.sin(angles)
            cos_ref[some, :] = jnp.cos(angles)
            sin_ref[some, :] = jnp.where(lane % HEAD_DIM < HEAD_DIM // 2, -sine, sine)

    def started():
        weight_ref[dp, here.mine] = blocks[here.mine]
        for one in swaps:
            one.start()
        chunk = 512

        @pl.loop(0, gate_ref.shape[1] // chunk)
        def _(i):
            some = pl.ds(pl.multiple_of(i * chunk, chunk), chunk)
            gain = upright(gain_two_ref[...])
            gate_out_ref[:, some] = (gate_ref[:, some].astype(F32) * gain).astype(BF16)
            up_out_ref[:, some] = (up_ref[:, some].astype(F32) * gain).astype(BF16)

        for one in own_feed:
            one.start()
        own_tables()

    def between(step):
        feed.start_some(step - (2 * here.length - 3), 3)

        @pl.when(step == 2)
        def _():
            near.finish()
            far.finish()

            @pl.loop(0, here.count)
            def _(sender):
                pair_copy(dp, sender).start()

        @pl.when(step == 4)
        def _():
            @pl.loop(0, here.count)
            def _(sender):
                pair_copy(1 - dp, sender).wait_recv()

    def share_copy(ref, number, where):
        return remote(
            ref.at[where],
            ref.at[where],
            share_sems.at[0, number],
            share_sems.at[1, number],
            here.sibling(),
        )

    def stores(number, first):
        made = []
        for block in range(2):
            where = pl.ds(pl.multiple_of((first + block) * rows, rows), rows)
            for part, out_ref in enumerate((normed_ref, grads_ref)):
                made.append(
                    pltpu.make_async_copy(
                        buf.at[first + block, part],
                        out_ref.at[where],
                        store_sems.at[number, block, part],
                    )
                )
        return made

    def compute(number, first):
        for one in stores(number, first):
            one.start()
        weight = weight_ref[...].reshape(-1, weight_ref.shape[-1])
        unit = buf[pl.ds(first, 2), 0]
        qkv = dot(unit.reshape(-1, unit.shape[-1]), weight)
        where = unit_rows(first, rows)
        cosine = cos_ref[where, :]
        sine = sin_ref[where, :]
        scale = BF16(1.0 / math.sqrt(HEAD_DIM))
        q_ref[where, :] = rotated(qkv[:, :cols], cosine, sine).astype(BF16) * scale
        for core, ref in enumerate((k_ref, v_ref)):

            @pl.when(here.core == core)
            def _():
                mine = qkv[:, cols:]
                ref[where, :] = (mine if core else rotated(mine, cosine, sine)).astype(BF16)
                share_copy(ref, number, where).start()

    far.start()
    near.start()
    gather_units(here, buf, send_sems, recv_sems, compute, between, here.length, started)

    @pl.loop(0, here.count)
    def _(sender):
        pair_copy(dp, sender).wait_send()

    @pl.loop(0, here.count // 2)
    def _(number):
        for one in stores(number, 0):
            one.wait()
        share_copy(k_ref, number, unit_rows(0, rows)).wait()

    feed.finish()
    for one in swaps + own_feed:
        one.wait()


def gather_project(
    lengths, tokens, cotangent, query, key, value, gate, up, gains, freq, down, output, call_id
):
    seq = lax.axis_size("seq")
    rows, width = tokens.shape
    cols = 2 * HEAD_DIM
    slab, ff = gate.shape
    bf16 = lambda *shape: jax.ShapeDtypeStruct(shape, BF16)
    f32 = lambda *shape: jax.ShapeDtypeStruct(shape, F32)
    all_rows = seq * rows
    dma = pltpu.SemaphoreType.DMA
    return pl.pallas_call(
        project_kernel,
        out_shape=[
            bf16(all_rows, width),
            bf16(all_rows, width),
            bf16(all_rows, cols),
            bf16(all_rows, cols),
            bf16(all_rows, cols),
            f32(all_rows, cols),
            f32(all_rows, cols),
            jax.ShapeDtypeStruct((all_rows, 1), jnp.int32),
            bf16(2, seq, slab, 2 * cols),
            bf16(slab, ff),
            bf16(slab, ff),
            bf16(seq // 2, slab, 4 * down.shape[0]),
            bf16(2, *down.shape),
            bf16(2, *output.shape),
        ],
        in_specs=[pl.BlockSpec(memory_space=pltpu.SMEM)] + [VMEM] * 10 + [HBM] * 2,
        out_specs=[HBM] * 2 + [VMEM] * 9 + [HBM] * 3,
        scratch_shapes=gather_scratch(seq, rows, width)
        + [
            pltpu.VMEM((seq, slab, 2 * cols), BF16),
            dma((seq // 2, 2, 2)),
            dma((2, seq // 2)),
            dma((2, seq // 2)),
            dma((2, seq // 2, 4)),
            dma((2, 2)),
            dma((6,)),
            dma((2, seq)),
            dma((2, seq // 2)),
        ],
        compiler_params=params(call_id, 60),
        cost_estimate=cost(2 * all_rows * width * 2 * cols, 8 * all_rows * width),
    )(lengths, tokens, cotangent, query, key, value, gate, up, *gains, freq, down, output)


def attention_feed_kernel(
    block,
    q_ref,
    k_ref,
    v_ref,
    open_ref,
    gate_ref,
    up_ref,
    near_ref,
    out_ref,
    lse_ref,
    feed_ref,
    low_ref,
    near_out_ref,
    feed_sems,
    swap_sems,
):
    here = Place()
    feed = feed_spread(here, False, (gate_ref, up_ref), feed_ref, feed_sems)

    swap = remote(near_ref, near_out_ref, swap_sems.at[0], swap_sems.at[1], here.partner())
    pl.when(pl.program_id(0) == 0)(here.call_all)
    attention_kernel(block, q_ref, k_ref, v_ref, open_ref, out_ref, lse_ref)
    low_ref[...] = out_ref[...].astype(BF16)

    @pl.when(pl.program_id(0) == 0)
    def _():
        here.await_all()
        feed.start()
        swap.start()

    @pl.when(pl.program_id(0) == pl.num_programs(0) - 1)
    def _():
        feed.finish()
        swap.wait()


def attention_feed(queries, keys, values, opening, gate, up, near, block, call_id):
    seq = lax.axis_size("seq")
    rows, cols = queries.shape
    heads = cols // HEAD_DIM
    tiled = lambda width: pl.BlockSpec((block, width), lambda i: (i, 0))
    whole = pl.BlockSpec((rows, cols), lambda i: (0, 0))
    return pl.pallas_call(
        functools.partial(attention_feed_kernel, block),
        grid=(rows // block,),
        in_specs=[tiled(cols), whole, whole, tiled(1), HBM, HBM, HBM],
        out_specs=[tiled(cols), tiled(heads), HBM, tiled(cols), HBM],
        out_shape=[
            jax.ShapeDtypeStruct((rows, cols), F32),
            jax.ShapeDtypeStruct((rows, heads), F32),
            jax.ShapeDtypeStruct(near.shape, BF16),
            jax.ShapeDtypeStruct((rows, cols), BF16),
            jax.ShapeDtypeStruct(near.shape, BF16),
        ],
        scratch_shapes=[pltpu.SemaphoreType.DMA((2, seq // 2, 4)), pltpu.SemaphoreType.DMA((2,))],
        compiler_params=params(call_id, 60),
        cost_estimate=cost(2 * rows * rows * cols, 10 * rows * cols),
    )(queries, keys, values, opening, gate, up, near)


ROW_CHUNK = 32


def norm_input_grad(values, upstream):
    factor = norm_factor(values)
    inner_mean = jnp.mean(upstream * values, axis=-1, keepdims=True)
    return factor * upstream - values * factor * factor * factor * inner_mean


def in_row_chunks(rows, chunk, visit):
    @pl.loop(0, rows // chunk)
    def _(i):
        visit(pl.ds(pl.multiple_of(i * chunk, chunk), chunk))


SCATTER_PARTS = 2
SCATTER_RING = 4
SCATTER_SCRATCH = 11


def scatter_rows_of_products(
    here,
    products,
    core_out,
    core_in,
    pair_out,
    pair_in,
    line_out,
    line_in,
    held,
    core_sems,
    pair_sems,
    line_sems,
    came_sems,
    first=None,
    between=nothing,
    filler=None,
):
    length = here.length
    parts = SCATTER_PARTS * len(products)
    rows, width = held.shape
    tile = min(width, 512)
    tiles = width // tile
    steps = length * parts

    def target(i):
        ups = length - 1 - here.line
        near = here.line < length // 2
        if_near = jnp.where(i < ups, length - 1 - i, i - ups)
        if_far = jnp.where(i < here.line, i, length - 1 - (i - here.line))
        return jnp.where(i == length - 1, here.line, jnp.where(near, if_near, if_far))

    def product(line, pair, core, part, use):
        first = pl.multiple_of(here.index(line, pair, core) * rows, rows)

        def one(number):
            transposed, a_ref, b_ref, _ = products[number]
            a = a_ref[pl.ds(first, rows), :]
            begin = (part - number * SCATTER_PARTS) * width

            @pl.loop(0, tiles)
            def _(t):
                into = pl.ds(pl.multiple_of(t * tile, tile), tile)
                cols = pl.ds(pl.multiple_of(begin + t * tile, tile), tile)
                use(dot_t(a, b_ref[cols, :]) if transposed else dot(a, b_ref[:, cols]), into)

        for number in range(len(products)):
            pl.when(part // SCATTER_PARTS == number)(functools.partial(one, number))

    def core_copy(slot):
        return remote(
            core_out.at[slot % SCATTER_RING],
            core_in.at[slot],
            core_sems.at[0, slot],
            core_sems.at[1, slot],
            here.sibling(),
        )

    def pair_copy(slot):
        return remote(
            pair_out.at[slot],
            pair_in.at[slot],
            pair_sems.at[0, slot],
            pair_sems.at[1, slot],
            here.across(),
        )

    def up_copy(slot, line, part):
        into = (line + 1) * parts + part
        return remote(
            line_out.at[slot], line_in.at[into], line_sems.at[slot], came_sems.at[into], here.above()
        )

    def down_copy(slot, line, part):
        into = line * parts + part
        return remote(
            line_out.at[slot], line_in.at[into], line_sems.at[slot], came_sems.at[into], here.below()
        )

    def for_sibling(step, pair, slot):
        pl.when(slot >= SCATTER_RING)(lambda: core_copy(slot - SCATTER_RING).wait_send())

        def use(value, cols):
            core_out[slot % SCATTER_RING, :, cols] = value.astype(BF16)

        product(target(step // parts), pair, 1 - here.core, step % parts, use)
        core_copy(slot).start()

    for_sibling(jnp.int32(0), 1 - here.pair, jnp.int32(0))

    @pl.loop(0, steps)
    def _(step):
        if first is not None:
            first(step)
        pl.when(step < steps - 1)(lambda: for_sibling(step + 1, 1 - here.pair, step + 1))
        core_copy(step).wait_recv()

        def use(value, cols):
            pair_out[step, :, cols] = (value + core_in[step, :, cols].astype(F32)).astype(BF16)

        product(target(step // parts), 1 - here.pair, here.core, step % parts, use)
        pair_copy(step).start()

    for_sibling(jnp.int32(0), here.pair, jnp.int32(steps))
    between()

    @pl.loop(0, steps)
    def _(step):
        pl.when(step < steps - 1)(lambda: for_sibling(step + 1, here.pair, steps + step + 1))
        core_copy(steps + step).wait_recv()
        line = target(step // parts)
        part = step % parts

        def use(value, cols):
            held[:, cols] = value + core_in[steps + step, :, cols].astype(F32)

        product(line, here.pair, here.core, part, use)
        if filler is not None:
            filler(step)
        pair_copy(step).wait_recv()
        from_above = (line <= here.line) & (here.line < length - 1)
        from_below = (line >= here.line) & (here.line > 0)
        held[...] += pair_in[step].astype(F32)

        @pl.when(from_above)
        def _():
            down_copy(0, line, part).wait_recv()
            held[...] += line_in[line * parts + part].astype(F32)

        @pl.when(from_below)
        def _():
            up_copy(0, line, part).wait_recv()
            held[...] += line_in[(line + 1) * parts + part].astype(F32)

        for number, (_, _, _, out_ref) in enumerate(products):

            @pl.when((line == here.line) & (part // SCATTER_PARTS == number))
            def _():
                begin = (part - number * SCATTER_PARTS) * width
                out_ref[:, pl.ds(pl.multiple_of(begin, width), width)] = held[...]

        @pl.when(line < here.line)
        def _():
            line_out[step] = held[...].astype(BF16)
            down_copy(step, line, part).start()

        @pl.when(line > here.line)
        def _():
            line_out[step] = held[...].astype(BF16)
            up_copy(step, line, part).start()

    @pl.loop(2 * steps - SCATTER_RING, 2 * steps)
    def _(slot):
        core_copy(slot).wait_send()

    @pl.loop(0, steps)
    def _(step):
        pair_copy(step).wait_send()
        line = target(step // parts)
        pl.when(line < here.line)(lambda: down_copy(step, 0, 0).wait_send())
        pl.when(line > here.line)(lambda: up_copy(step, 0, 0).wait_send())


def scatter_scratch(seq, rows, width, count=1):
    length = seq // 4
    parts = SCATTER_PARTS * count
    steps = length * parts
    block = (rows, width // SCATTER_PARTS)
    dma = pltpu.SemaphoreType.DMA
    return [
        pltpu.VMEM((SCATTER_RING, *block), BF16),
        pltpu.VMEM((2 * steps, *block), BF16),
        pltpu.VMEM((steps, *block), BF16),
        pltpu.VMEM((steps, *block), BF16),
        pltpu.VMEM((steps, *block), BF16),
        pltpu.VMEM(((length + 1) * parts, *block), BF16),
        pltpu.VMEM(block, F32),
        dma((2, 2 * steps)),
        dma((2, steps)),
        dma((steps,)),
        dma(((length + 1) * parts,)),
    ]


def scatter_cost(a, width):
    return cost(2 * a.shape[0] * a.shape[1] * width, 4 * a.shape[0] * width)


def scatter_both_kernel(
    back_hbm,
    turned_hbm,
    hidden_hbm,
    down_hbm,
    middle_ref,
    grads_hbm,
    normed_hbm,
    grad_ref,
    low_ref,
    mixed_ref,
    sums_ref,
    *scratch,
):
    here = Place()
    factors = scratch[SCATTER_SCRATCH : SCATTER_SCRATCH + 4]
    back_ref, turned_ref, hidden_ref, down_ref = factors
    normed, away, came, own, fetch_sems, swap_sems, own_sems = scratch[SCATTER_SCRATCH + 4 :]
    rows = grad_ref.shape[0]
    loads = [
        pltpu.make_async_copy(src, dst, own_sems.at[number])
        for number, (src, dst) in enumerate(
            zip((back_hbm, turned_hbm, hidden_hbm, down_hbm), factors)
        )
    ]
    own_copy = pltpu.make_async_copy(
        grads_hbm.at[pl.ds(pl.multiple_of(here.mine * rows, rows), rows)], own, own_sems.at[4]
    )
    for one in loads + [own_copy]:
        one.start()
    here.greet(partner=True)
    for one in loads[:2]:
        one.wait()

    def first(step):
        @pl.when(step == SCATTER_PARTS - 1)
        def _():
            for one in loads[2:]:
                one.wait()
    chunk = normed.shape[2]
    half = normed_hbm.shape[1] // 2
    chunks = half // chunk

    def fetch(number):
        dp = jnp.where(number < chunks, 1 - here.dp, here.dp)
        begin = dp * half + number % chunks * chunk
        return pltpu.make_async_copy(
            normed_hbm.at[:, pl.ds(pl.multiple_of(begin, chunk), chunk)],
            normed.at[number % 2],
            fetch_sems.at[number % 2],
        )

    def swap(i):
        some = pl.ds(pl.multiple_of(i * chunk, chunk), chunk)
        return remote(
            away.at[some], came.at[some], swap_sems.at[0, i], swap_sems.at[1, i], here.partner()
        )

    def part(number):
        fetch(number).wait()
        pl.when(number + 1 < 2 * chunks)(lambda: fetch(number + 1).start())
        return t_dot(normed[number % 2], back_ref[...])

    def filler(step):
        @pl.when(step < chunks)
        def _():
            some = pl.ds(pl.multiple_of(step * chunk, chunk), chunk)
            away[some, :] = part(step).astype(BF16)
            swap(step).start()

        @pl.when((step >= chunks) & (step < 3 * chunks) & (step % 2 == 0))
        def _():
            i = (step - chunks) // 2
            some = pl.ds(pl.multiple_of(i * chunk, chunk), chunk)
            kept = part(chunks + i)
            swap(i).wait()
            sums_ref[some, :] = (kept + came[some, :].astype(F32)).astype(BF16)

    fetch(jnp.int32(0)).start()
    scatter_rows_of_products(
        here,
        [(False, back_ref, turned_ref, grad_ref), (False, hidden_ref, down_ref, mixed_ref)],
        *scratch[:SCATTER_SCRATCH],
        first=first,
        filler=filler,
    )
    own_copy.wait()

    def add(some):
        grad = own[some, :].astype(F32) + norm_input_grad(middle_ref[some, :], grad_ref[some, :])
        grad_ref[some, :] = grad
        low_ref[some, :] = grad.astype(BF16)

    in_row_chunks(rows, ROW_CHUNK, add)


def product_scatter_both(back, turned, hidden, down, middle, grads, normed, call_id):
    seq = lax.axis_size("seq")
    rows = back.shape[0] // seq
    width = turned.shape[1]
    cols = back.shape[1]
    chunk = width // 8
    dma = pltpu.SemaphoreType.DMA
    return pl.pallas_call(
        scatter_both_kernel,
        out_shape=[
            jax.ShapeDtypeStruct((rows, width), F32),
            jax.ShapeDtypeStruct((rows, width), BF16),
            jax.ShapeDtypeStruct((rows, width), F32),
            jax.ShapeDtypeStruct((width // 2, cols), BF16),
        ],
        in_specs=[HBM] * 4 + [VMEM] + [HBM] * 2,
        out_specs=[VMEM] * 4,
        scratch_shapes=scatter_scratch(seq, rows, width, 2)
        + [pltpu.VMEM(array.shape, BF16) for array in (back, turned, hidden, down)]
        + [
            pltpu.VMEM((2, normed.shape[0], chunk), BF16),
            pltpu.VMEM((width // 2, cols), BF16),
            pltpu.VMEM((width // 2, cols), BF16),
            pltpu.VMEM((rows, width), BF16),
            dma((2,)),
            dma((2, 4)),
            dma((5,)),
        ],
        compiler_params=params(call_id, 60),
        cost_estimate=scatter_cost(back, 3 * width),
    )(back, turned, hidden, down, middle, grads, normed)


def scatter_feed_kernel(
    a_ref,
    b_ref,
    tokens_ref,
    near_hbm,
    other_hbm,
    far_hbm,
    middle_ref,
    normed_ref,
    feed_ref,
    *scratch,
):
    here = Place()
    here.greet(partner=True)
    swap_sems, local_sems = scratch[SCATTER_SCRATCH:]
    slots = near_hbm.shape[0]

    def fetch(kind, slot):
        ref = (near_hbm, other_hbm, far_hbm)[kind]
        dp = 1 - here.dp if kind == 1 else here.dp
        return pltpu.make_async_copy(
            ref.at[slot], feed_ref.at[dp, here.peer(slot, kind < 2)], local_sems.at[kind, slot]
        )

    def swap(slot):
        place = feed_ref.at[here.dp, here.peer(slot, False)]
        return remote(
            place, place, swap_sems.at[0, slot], swap_sems.at[1, slot], here.partner()
        )

    for kind in (2, 0, 1):
        pl.loop(0, slots)(lambda slot, kind=kind: fetch(kind, slot).start())

    @pl.loop(0, slots)
    def _(slot):
        fetch(2, slot).wait()
        swap(slot).start()

    scatter_rows_of_products(
        here, [(False, a_ref, b_ref, middle_ref)], *scratch[:SCATTER_SCRATCH]
    )

    def add(some):
        middle = tokens_ref[some, :].astype(F32) + middle_ref[some, :]
        middle_ref[some, :] = middle
        normed_ref[some, :] = (middle * norm_factor(middle)).astype(BF16)

    in_row_chunks(middle_ref.shape[0], ROW_CHUNK, add)

    @pl.loop(0, slots)
    def _(slot):
        swap(slot).wait()
        for kind in range(2):
            fetch(kind, slot).wait()


def product_scatter_feed(a, b, tokens, near, other, far, call_id):
    seq = lax.axis_size("seq")
    rows = a.shape[0] // seq
    width = b.shape[1]
    dma = pltpu.SemaphoreType.DMA
    return pl.pallas_call(
        scatter_feed_kernel,
        out_shape=[
            jax.ShapeDtypeStruct((rows, width), F32),
            jax.ShapeDtypeStruct((rows, width), BF16),
            jax.ShapeDtypeStruct((2, seq, *near.shape[1:]), BF16),
        ],
        in_specs=[VMEM, VMEM, VMEM, HBM, HBM, HBM],
        out_specs=[VMEM, VMEM, VMEM],
        scratch_shapes=scatter_scratch(seq, rows, width)
        + [dma((2, seq // 2)), dma((3, seq // 2))],
        compiler_params=params(call_id, 60),
        cost_estimate=scatter_cost(a, width),
    )(a, b, tokens, near, other, far)


def feed_kernel(
    own_ref,
    grad_hbm,
    feed_hbm,
    down_hbm,
    normed_ref,
    hidden_out_ref,
    back_out_ref,
    turned_out_ref,
    buf,
    send_sems,
    recv_sems,
    store_sems,
    grad_ref,
    feed_ref,
    down_ref,
    hidden_ref,
    back_ref,
    turned_ref,
    fetch_sems,
    out_sems,
):
    here = Place()
    fetches = [
        pltpu.make_async_copy(src, dst, fetch_sems.at[number])
        for number, (src, dst) in enumerate(
            [(feed_hbm, feed_ref), (down_hbm, down_ref), (grad_hbm, grad_ref)]
        )
    ]
    for one in fetches:
        one.start()
    put_own(here, own_ref, buf)
    here.greet()
    rows = own_ref.shape[0]
    width = own_ref.shape[1]
    hidden = hidden_ref.shape[1]
    tile = 256
    store = UnitStore(buf, normed_ref, store_sems)

    def outs(number, first):
        where = unit_rows(first, rows)
        share = width // (2 * here.length)
        some = pl.ds(pl.multiple_of(number * share, share), share)
        return [
            pltpu.make_async_copy(src, dst, out_sems.at[number, i])
            for i, (src, dst) in enumerate(
                [
                    (hidden_ref.at[where], hidden_out_ref.at[where]),
                    (back_ref.at[where], back_out_ref.at[where]),
                    (turned_ref.at[:, some], turned_out_ref.at[:, some]),
                ]
            )
        ]

    def compute(number, first):
        store.start(number, first)

        @pl.when(number == 0)
        def _():
            for one in fetches:
                one.wait()

        where = unit_rows(first, rows)
        normed = take_unit(buf, first)
        grad = grad_ref[where, :]

        @pl.loop(0, hidden // tile)
        def _(t):
            cols = pl.ds(pl.multiple_of(t * tile, tile), tile)
            later = pl.ds(pl.multiple_of(hidden + t * tile, tile), tile)
            gate = dot(normed, feed_ref[:, cols])
            upward = dot(normed, feed_ref[:, later])
            hidden_grad = dot_t(grad, down_ref[cols, :])
            sigmoid = jax.nn.sigmoid(gate)
            silu = gate * sigmoid
            hidden_ref[where, cols] = (silu * upward).astype(BF16)
            back_ref[where, cols] = (
                hidden_grad * upward * sigmoid * (1.0 + gate * (1.0 - sigmoid))
            ).astype(BF16)
            back_ref[where, later] = (hidden_grad * silu).astype(BF16)

        share = width // (2 * here.length)
        some = pl.ds(pl.multiple_of(number * share, share), share)
        turned_ref[:, some] = feed_ref[some, :].T
        for one in outs(number, first):
            one.start()

    gather_units(here, buf, send_sems, recv_sems, compute)

    @pl.loop(0, here.count // 2)
    def _(number):
        for one in outs(number, 0):
            one.wait()

    store.finish()


def gather_feed(own, grad_out, feed_weight, down_weight, call_id):
    seq = lax.axis_size("seq")
    rows, width = own.shape
    hidden = down_weight.shape[0]
    return pl.pallas_call(
        feed_kernel,
        out_shape=[
            jax.ShapeDtypeStruct((seq * rows, width), BF16),
            jax.ShapeDtypeStruct((seq * rows, hidden), BF16),
            jax.ShapeDtypeStruct((seq * rows, 2 * hidden), BF16),
            jax.ShapeDtypeStruct((2 * hidden, width), BF16),
        ],
        in_specs=[VMEM] + [HBM] * 3,
        out_specs=[HBM] * 4,
        scratch_shapes=gather_scratch(seq, rows // 2, width)
        + [
            pltpu.SemaphoreType.DMA((seq // 2, 2, 2)),
            pltpu.VMEM((seq * rows, width), BF16),
            pltpu.VMEM((width, 2 * hidden), BF16),
            pltpu.VMEM((hidden, width), BF16),
            pltpu.VMEM((seq * rows, hidden), BF16),
            pltpu.VMEM((seq * rows, 2 * hidden), BF16),
            pltpu.VMEM((2 * hidden, width), BF16),
            pltpu.SemaphoreType.DMA((3,)),
            pltpu.SemaphoreType.DMA((seq // 2, 3)),
        ],
        compiler_params=params(call_id, 60),
        cost_estimate=cost(8 * seq * rows * width * hidden, 8 * seq * rows * width),
    )(own, grad_out, feed_weight, down_weight)


def back_kernel(
    own_ref,
    weight_ref,
    attended_ref,
    hidden_hbm,
    out_grad_hbm,
    blocks_ref,
    grad_ref,
    output_kept_ref,
    output_away_ref,
    down_kept_ref,
    down_away_ref,
    near_ref,
    buf,
    send_sems,
    recv_sems,
    near_sems,
    own_sem,
    part,
    hidden_ref,
    out_grad_ref,
    fetch_sems,
):
    here = Place()
    fetches = [
        pltpu.make_async_copy(hidden_hbm, hidden_ref, fetch_sems.at[0]),
        pltpu.make_async_copy(out_grad_hbm, out_grad_ref, fetch_sems.at[1]),
    ]
    for one in fetches:
        one.start()
    put_own(here, own_ref, buf)
    here.greet_all()
    rows = own_ref.shape[0]
    width = own_ref.shape[1]
    tile = 512
    near = block_spread(here, True, blocks_ref, near_ref, near_sems)
    own = pltpu.make_async_copy(blocks_ref.at[here.mine], near_ref.at[here.slot], own_sem.at[0])

    own.start()

    def between(step):
        near.start_some(step - here.length, 2)

    part[...] = jnp.zeros_like(part)
    share = width // (2 * here.length)

    def split(values, kept_ref, away_ref, cols):
        half = values.shape[0] // 2
        top, bottom = values[:half], values[half:]
        kept_ref[:, cols] = jnp.where(here.dp == 0, top, bottom)
        away_ref[:, cols] = jnp.where(here.dp == 0, bottom, top).astype(BF16)

    def compute(number, first):
        where = unit_rows(first, rows)
        unit = take_unit(buf, first)
        grad_ref[where, :] = dot_t(unit, weight_ref[...]).astype(BF16)
        attended = attended_ref[where, :]
        for t in range(width // tile):
            cols = slice(t * tile, (t + 1) * tile)
            part[:, cols] += t_dot(attended, unit[:, cols])
        some = pl.ds(pl.multiple_of(number * share, share), share)

        @pl.when(number == 0)
        def _():
            for one in fetches:
                one.wait()

        split(t_dot(hidden_ref[...], out_grad_ref[:, some]), down_kept_ref, down_away_ref, some)

    gather_units(here, buf, send_sems, recv_sems, compute, between)
    for t in range(width // tile):
        cols = slice(t * tile, (t + 1) * tile)
        split(part[:, cols], output_kept_ref, output_away_ref, cols)
    near.finish()
    own.wait()


def gather_back(own, weight, attended, hidden, grad_out, blocks, call_id):
    seq = lax.axis_size("seq")
    rows, width = own.shape
    cols = weight.shape[0]
    return pl.pallas_call(
        back_kernel,
        out_shape=[
            jax.ShapeDtypeStruct((seq * rows, cols), BF16),
            jax.ShapeDtypeStruct((cols // 2, width), F32),
            jax.ShapeDtypeStruct((cols // 2, width), BF16),
            jax.ShapeDtypeStruct((hidden.shape[1] // 2, width), F32),
            jax.ShapeDtypeStruct((hidden.shape[1] // 2, width), BF16),
            jax.ShapeDtypeStruct((seq // 2, *blocks.shape[1:]), BF16),
        ],
        in_specs=[VMEM] * 3 + [HBM] * 3,
        out_specs=[VMEM] * 5 + [HBM],
        scratch_shapes=gather_scratch(seq, rows // 2, width)
        + [
            pltpu.SemaphoreType.DMA((2, seq // 2)),
            pltpu.SemaphoreType.DMA((1,)),
            pltpu.VMEM((cols, width), F32),
            pltpu.VMEM(hidden.shape, BF16),
            pltpu.VMEM(grad_out.shape, BF16),
            pltpu.SemaphoreType.DMA((2,)),
        ],
        compiler_params=params(call_id, 60),
        cost_estimate=cost(8 * seq * rows * width * cols, 6 * seq * rows * width),
    )(own, weight, attended, hidden, grad_out, blocks)


def attention_back_feed_kernel(
    block,
    q_ref,
    k_ref,
    v_ref,
    g_ref,
    att_ref,
    lse_ref,
    open_ref,
    cos_ref,
    sin_ref,
    blocks_ref,
    down_ref,
    output_ref,
    back_ref,
    feed_ref,
    down_out_ref,
    output_out_ref,
    dq_ref,
    dk_ref,
    dv_ref,
    share_out,
    share_in,
    feed_sems,
    swap_sems,
    share_sems,
):
    here = Place()
    tile = pl.program_id(0)
    cols = q_ref.shape[1]
    feed = block_spread(here, False, blocks_ref, feed_ref, feed_sems)
    swaps = [
        remote(src, dst, swap_sems.at[0, number], swap_sems.at[1, number], here.partner())
        for number, (src, dst) in enumerate(
            [(down_ref, down_out_ref), (output_ref, output_out_ref)]
        )
    ]

    pl.when(tile == 0)(here.call_all)
    attention_back_kernel(
        block, q_ref, k_ref, v_ref, g_ref, att_ref, lse_ref, open_ref, dq_ref, dk_ref, dv_ref
    )

    @pl.when(tile == 0)
    def _():
        here.await_all()
        feed.start()
        for one in swaps:
            one.start()

    where = pl.ds(pl.multiple_of(tile * block, block), block)
    scale = 1.0 / math.sqrt(HEAD_DIM)
    cosine = cos_ref[where, :]
    sine = sin_ref[where, :]
    back_ref[where, :cols] = rotated(dq_ref[...] * scale, cosine, -sine).astype(BF16)

    def share(i):
        rows = pl.ds(pl.multiple_of(i * block, block), block)
        return remote(
            share_out.at[rows],
            share_in.at[rows],
            share_sems.at[0, i],
            share_sems.at[1, i],
            here.sibling(),
        )

    @pl.when(tile == pl.num_programs(0) - 1)
    def _():
        @pl.loop(0, pl.num_programs(0))
        def _(i):
            rows = pl.ds(pl.multiple_of(i * block, block), block)
            away = jnp.where(here.core == 0, dv_ref[rows, :], dk_ref[rows, :])
            share_out[rows, :] = away.astype(BF16)
            share(i).start()

        @pl.loop(0, pl.num_programs(0))
        def _(i):
            rows = pl.ds(pl.multiple_of(i * block, block), block)
            share(i).wait()
            came = share_in[rows, :].astype(F32)
            keys = rotated(dk_ref[rows, :] + came, cos_ref[rows, :], -sin_ref[rows, :])
            back_ref[rows, cols:] = jnp.where(here.core == 0, keys, dv_ref[rows, :] + came).astype(
                BF16
            )

        feed.finish()
        for one in swaps:
            one.wait()


def attention_back_feed(
    queries,
    keys,
    values,
    grads,
    attended,
    log_total,
    opening,
    cosine,
    sine,
    blocks,
    down,
    output,
    block,
    call_id,
):
    seq = lax.axis_size("seq")
    rows, cols = queries.shape
    heads = cols // HEAD_DIM
    tiled = lambda width: pl.BlockSpec((block, width), lambda i: (i, 0))
    whole = pl.BlockSpec((rows, cols), lambda i: (0, 0))
    dma = pltpu.SemaphoreType.DMA
    return pl.pallas_call(
        functools.partial(attention_back_feed_kernel, block),
        grid=(rows // block,),
        in_specs=[tiled(cols), whole, whole, tiled(cols), tiled(cols), tiled(heads), tiled(1)]
        + [whole, whole, HBM, HBM, HBM],
        out_specs=[pl.BlockSpec((rows, 2 * cols), lambda i: (0, 0)), HBM, HBM, HBM],
        out_shape=[
            jax.ShapeDtypeStruct((rows, 2 * cols), BF16),
            jax.ShapeDtypeStruct((seq // 2, *blocks.shape[1:]), BF16),
            jax.ShapeDtypeStruct(down.shape, BF16),
            jax.ShapeDtypeStruct(output.shape, BF16),
        ],
        scratch_shapes=[
            pltpu.VMEM((block, cols), F32),
            pltpu.VMEM((rows, cols), F32),
            pltpu.VMEM((rows, cols), F32),
            pltpu.VMEM((rows, cols), BF16),
            pltpu.VMEM((rows, cols), BF16),
            dma((2, seq // 2)),
            dma((2, 2)),
            dma((2, rows // block)),
        ],
        compiler_params=params(call_id, 60),
        cost_estimate=cost(5 * rows * rows * cols, 20 * rows * cols),
    )(
        queries,
        keys,
        values,
        grads,
        attended,
        log_total,
        opening,
        cosine,
        sine,
        blocks,
        down,
        output,
    )


def scatter_last_kernel(a_ref, b_ref, normed_hbm, out_ref, qkv_ref, *scratch):
    here = Place()
    normed_ref, kept, away, came, sums, near_sems, far_sems, swap_sems, fetch_sems = scratch[
        SCATTER_SCRATCH:
    ]
    fetch = pltpu.make_async_copy(normed_hbm, normed_ref, fetch_sems.at[0])
    fetch.start()
    swap = remote(away, came, swap_sems.at[0], swap_sems.at[1], here.partner())
    near = block_spread(here, True, sums, qkv_ref.at[0], near_sems)
    far = block_spread(here, False, sums, qkv_ref.at[1], far_sems)
    half = away.shape[0]
    chunk = 256

    def part(dp, i):
        first = pl.multiple_of(dp * half + i * chunk, chunk)
        return t_dot(normed_ref[:, pl.ds(first, chunk)], a_ref[...])

    def meanwhile():
        fetch.wait()

        @pl.loop(0, half // chunk)
        def _(i):
            some = pl.ds(pl.multiple_of(i * chunk, chunk), chunk)
            away[some, :] = part(1 - here.dp, i).astype(BF16)

    here.greet_all(meanwhile)
    swap.start()

    def between():
        @pl.loop(0, half // chunk)
        def _(i):
            kept[pl.ds(pl.multiple_of(i * chunk, chunk), chunk), :] = part(here.dp, i)

    begin = 2
    each = 3

    def filler(step):
        @pl.when(step == begin)
        def _():
            swap.wait_recv()
            slab = sums.shape[1]

            @pl.loop(0, here.count)
            def _(i):
                rows = pl.ds(pl.multiple_of(i * slab, slab), slab)
                sums[i] = (kept[rows, :] + came[rows, :].astype(F32)).astype(BF16)

            qkv_ref[0, here.slot] = sums[here.mine]

        @pl.when(step > begin)
        def _():
            @pl.loop(0, each)
            def _(i):
                number = (step - begin - 1) * each + i
                pl.when(number < far.slots)(lambda: far.start_one(number))

                @pl.when((number >= far.slots) & (number < 2 * far.slots - 1))
                def _():
                    near.start_one(number - far.slots + 1)

    scatter_rows_of_products(
        here,
        [(True, a_ref, b_ref, out_ref)],
        *scratch[:SCATTER_SCRATCH],
        between=between,
        filler=filler,
    )
    swap.wait_send()
    near.finish()
    far.finish()


def product_scatter_last(a, b, normed, call_id):
    seq = lax.axis_size("seq")
    rows = a.shape[0] // seq
    width, cols = b.shape
    slab = width // (2 * seq)
    dma = pltpu.SemaphoreType.DMA
    return pl.pallas_call(
        scatter_last_kernel,
        out_shape=[
            jax.ShapeDtypeStruct((rows, width), F32),
            jax.ShapeDtypeStruct((2, seq // 2, slab, cols), BF16),
        ],
        in_specs=[VMEM, VMEM, HBM],
        out_specs=[VMEM, VMEM],
        scratch_shapes=scatter_scratch(seq, rows, width)
        + [
            pltpu.VMEM(normed.shape, BF16),
            pltpu.VMEM((width // 2, cols), F32),
            pltpu.VMEM((width // 2, cols), BF16),
            pltpu.VMEM((width // 2, cols), BF16),
            pltpu.VMEM((seq, slab, cols), BF16),
            dma((2, seq // 2)),
            dma((2, seq // 2)),
            dma((2,)),
            dma((1,)),
        ],
        compiler_params=params(call_id, 60),
        cost_estimate=scatter_cost(a, width),
    )(a, b, normed)


def unpack_kernel(
    pair_ref,
    near_gate_ref,
    far_gate_ref,
    near_up_ref,
    far_up_ref,
    gate_ref,
    up_ref,
    qkv_ref,
    query_ref,
    key_ref,
    value_ref,
    gain_one_ref,
    gain_two_ref,
    tokens_ref,
    middle_ref,
    mixed_sum_ref,
    middle_grad_ref,
    upstream_ref,
    down_kept_ref,
    down_came_ref,
    output_kept_ref,
    output_came_ref,
    gate_out_ref,
    up_out_ref,
    query_out_ref,
    key_out_ref,
    value_out_ref,
    one_out_ref,
    two_out_ref,
    mixed_ref,
    token_grad_ref,
    down_out_ref,
    output_out_ref,
    total_two,
):
    pair = pair_ref[0]
    dp = lax.axis_size("dp")
    length = qkv_ref.shape[1] // 2
    slab = qkv_ref.shape[2]
    step = pl.program_id(0) * pl.num_programs(1) + pl.program_id(1)
    columns = near_gate_ref.shape[2]

    def along(grad, weight):
        return jnp.sum(grad * weight.astype(F32), axis=1, keepdims=True)

    @pl.when(step == 0)
    def _():
        total_two[...] = jnp.zeros_like(total_two)
        total = jnp.zeros((slab, 1), F32)
        gain = upright(gain_one_ref[...])

        def put(out_ref, weight_ref, begin, grad):
            cols = slice(begin, begin + grad.shape[1])
            out_ref[:, cols] = grad * gain
            return along(grad, weight_ref[:, cols])

        pairs = [{}, {}]
        for line in range(length):
            rows = []
            for number in range(4):
                slot = line * 2 + number % 2
                near, far = qkv_ref[0, slot].astype(F32), qkv_ref[1, slot].astype(F32)
                rows.append(jnp.where(number // 2 == pair, near, far))
            kv = [rows[core] + rows[core + 2] for core in range(2)]
            for half in range(dp):
                cols = slice(half * HEAD_DIM, (half + 1) * HEAD_DIM)
                for number in (0, 2):
                    two = jnp.concatenate([rows[number][:, cols], rows[number + 1][:, cols]], axis=1)
                    begin = (half * length * 4 + line * 4 + number) * HEAD_DIM
                    total = total + put(query_out_ref, query_ref, begin, two)
                for kind in range(2):
                    begin = (dp + half) * HEAD_DIM
                    pairs[kind][half, line] = kv[kind][:, begin : begin + HEAD_DIM]
        for kind, (out_ref, weight_ref) in enumerate(
            [(key_out_ref, key_ref), (value_out_ref, value_ref)]
        ):
            for half in range(dp):
                for line in range(0, length, 2):
                    two = [pairs[kind][half, line], pairs[kind][half, line + 1]]
                    begin = (half * length + line) * HEAD_DIM
                    total = total + put(
                        out_ref, weight_ref, begin, jnp.concatenate(two, axis=1)
                    )
        one_out_ref[...] = flat(total)

    mixed_ref[...] = middle_ref[...] + mixed_sum_ref[...]
    token_grad_ref[...] = middle_grad_ref[...] + norm_input_grad(
        tokens_ref[...].astype(F32), upstream_ref[...]
    )
    down_out_ref[...] = down_kept_ref[...] + down_came_ref[...].astype(F32)
    output_out_ref[...] = output_kept_ref[...] + output_came_ref[...].astype(F32)
    gain_two = upright(gain_two_ref[...])
    total = jnp.zeros((slab, 1), F32)
    for near_ref, far_ref, weight_ref, out_ref in (
        (near_gate_ref, far_gate_ref, gate_ref, gate_out_ref),
        (near_up_ref, far_up_ref, up_ref, up_out_ref),
    ):
        for number in range(4):
            core = number % 2
            near, far = near_ref[core].astype(F32), far_ref[core].astype(F32)
            grad = jnp.where(number // 2 == pair, near, far)
            cols = slice(number * columns, (number + 1) * columns)
            total = total + along(grad, weight_ref[:, cols])
            out_ref[:, cols] = grad * gain_two
    total_two[...] += total

    @pl.when(step == pl.num_programs(0) * pl.num_programs(1) - 1)
    def _():
        two_out_ref[...] = flat(total_two[...])


def unpack(pair, near, far, gate, up, qkv, query, key, value, gain_one, gain_two, *rows):
    dp = lax.axis_size("dp")
    seq = lax.axis_size("seq")
    slab, ff = gate.shape
    length = seq // 4
    columns = ff // (dp * seq)
    whole = lambda array: pl.BlockSpec(array.shape, lambda j, i: (0,) * array.ndim)
    block = lambda kind: pl.BlockSpec((2, slab, columns), lambda j, i: (i, 0, kind * dp + j))
    tile = pl.BlockSpec((slab, 4 * columns), lambda j, i: (0, j * length + i))
    f32 = lambda array: jax.ShapeDtypeStruct(array.shape, F32)
    outs = [f32(gate), f32(up), f32(query), f32(key), f32(value), f32(gain_one), f32(gain_two)]
    sums = [f32(rows[0]), f32(rows[0]), f32(rows[5]), f32(rows[7])]
    steps = dp * length
    strip = lambda array: pl.BlockSpec(
        (array.shape[0] // steps, array.shape[1]), lambda j, i: (j * length + i, 0)
    )
    return pl.pallas_call(
        unpack_kernel,
        grid=(dp, length),
        in_specs=[pl.BlockSpec(memory_space=pltpu.SMEM)]
        + [block(0), block(0), block(1), block(1), tile, tile]
        + [whole(array) for array in (qkv, query, key, value, gain_one, gain_two)]
        + [strip(array) for array in rows],
        out_specs=[tile, tile]
        + [whole(array) for array in outs[2:]]
        + [strip(array) for array in sums],
        out_shape=outs + sums,
        scratch_shapes=[pltpu.VMEM((slab, 1), F32)],
        compiler_params=pltpu.CompilerParams(vmem_limit_bytes=60 << 20),
        cost_estimate=cost(slab * ff, 16 * slab * ff),
    )(
        pair,
        near,
        far,
        near,
        far,
        gate,
        up,
        qkv,
        query,
        key,
        value,
        gain_one,
        gain_two,
        *rows,
    )


def swap_dp(values):
    count = lax.axis_size("dp")
    return lax.ppermute(values, "dp", [(i, (i + 1) % count) for i in range(count)])


def gather_dp(values):
    return lax.all_gather(values, "dp", axis=0, tiled=True)


def sum_dp(partial):
    half = partial.shape[0] // 2
    mine = lax.axis_index("dp")
    away = lax.dynamic_slice_in_dim(partial, (1 - mine) * half, half, 0).astype(BF16)
    kept = lax.dynamic_slice_in_dim(partial, mine * half, half, 0)
    return kept + swap_dp(away).astype(F32)


def gather_rows(values):
    return lax.all_gather(values, "seq", axis=0, tiled=True)


def scatter_rows(partial):
    return lax.psum_scatter(partial.astype(BF16), "seq", scatter_dimension=0, tiled=True).astype(F32)


def exchange(blocks):
    return lax.all_to_all(blocks, "seq", split_axis=0, concat_axis=0, tiled=True)


def norm_factor(values):
    return lax.rsqrt(jnp.mean(values * values, axis=-1, keepdims=True) + EPS)


def norm_back(inputs, factor, gain_row, upstream):
    scaled_up = gain_row * upstream
    inner_mean = jnp.mean(scaled_up * inputs, axis=-1, keepdims=True)
    grad_in = factor * scaled_up - inputs * factor * factor * factor * inner_mean
    grad_gain = jnp.sum(upstream * inputs * factor, axis=0)
    return grad_in, grad_gain


def plain_shards(
    tokens,
    cotangent,
    doc_lengths,
    attn_gain,
    mlp_gain,
    query_weight,
    key_weight,
    value_weight,
    output_weight,
    gate_weight,
    up_weight,
    down_weight,
):
    dp = lax.axis_size("dp")
    seq = lax.axis_size("seq")
    mine = lax.axis_index("seq")
    tok_count, width = tokens.shape
    rows = tok_count * seq
    slab = query_weight.shape[0]
    share = HEAD_DIM // slab
    half_heads = HEADS // dp
    half_kv = KV_HEADS // dp
    hidden_dev = down_weight.shape[0]
    block = 512

    doc_ends = jnp.cumsum(doc_lengths[0])
    place = jnp.arange(rows, dtype=jnp.int32)
    passed = doc_ends[None, :] <= place[:, None]
    opening = jnp.max(jnp.where(passed, doc_ends[None, :], 0), axis=1)
    position = place - opening
    keeping = place < doc_ends[DOCS - 1]
    angles = position.astype(F32)[:, None] * rotary_table(HEAD_DIM)[None, :]
    cosine = jnp.cos(angles)
    sine = jnp.sin(angles)
    cos_heads = jnp.tile(cosine, (1, 2 * dp))
    sin_heads = jnp.tile(jnp.concatenate([-sine, sine], axis=1), (1, dp))
    own_keeping = lax.dynamic_slice_in_dim(keeping, mine * tok_count, tok_count, 0)

    def head_columns(weight, kept):
        split = weight.reshape(slab, dp, kept, HEAD_DIM)
        return jnp.repeat(split, seq // kept, axis=2)

    qkv_blocks = jnp.stack(
        [
            head_columns(query_weight, half_heads),
            head_columns(key_weight, half_kv),
            head_columns(value_weight, half_kv),
        ],
        axis=1,
    )
    qkv_blocks = jnp.transpose(qkv_blocks, (3, 0, 1, 2, 4)).reshape(seq * slab, 3 * dp * HEAD_DIM)
    qkv_weight = gather_dp(exchange(qkv_blocks))
    feed_blocks = jnp.stack(
        [w.reshape(slab, dp, seq, hidden_dev) for w in (gate_weight, up_weight)], axis=1
    )
    feed_blocks = jnp.transpose(feed_blocks, (3, 0, 1, 2, 4)).reshape(
        seq * slab, 2 * dp * hidden_dev
    )
    feed_weight = gather_dp(exchange(feed_blocks))
    down_own = gather_dp(down_weight)
    output_own = output_weight
    if share > 1:
        groups = [list(range(i, i + share)) for i in range(0, seq, share)]
        output_own = lax.all_gather(
            output_own, "seq", axis=0, tiled=True, axis_index_groups=groups
        )
    output_own = gather_dp(output_own)
    gains = lax.all_gather(
        jnp.stack([attn_gain, mlp_gain]), ("dp", "seq"), axis=1, tiled=True
    ).astype(F32)
    gain_one, gain_two = gains[0], gains[1]

    inputs_all = gather_rows(tokens).astype(F32)
    normed_one = (inputs_all * norm_factor(inputs_all) * gain_one).astype(BF16)
    qkv = dot(normed_one, qkv_weight)
    head_cols = dp * HEAD_DIM
    query_lin, key_lin = qkv[:, :head_cols], qkv[:, head_cols : 2 * head_cols]
    values = qkv[:, 2 * head_cols :].astype(BF16)
    scale = 1.0 / math.sqrt(HEAD_DIM)
    queries = (query_lin * cos_heads + swap_halves(query_lin) * sin_heads).astype(BF16) * BF16(scale)
    keys = (key_lin * cos_heads + swap_halves(key_lin) * sin_heads).astype(BF16)
    attended_sum, log_total = attention(queries, keys, values, opening[:, None], block)
    if share > 1:
        own_rows = ((place // tok_count) % share == mine % share)[:, None]
        attended_sum = jnp.where(own_rows, attended_sum, 0.0)
    attended = attended_sum.astype(BF16)
    inputs = tokens.astype(F32)
    middle = inputs + scatter_rows(dot(attended, output_own))

    factor_two = norm_factor(middle)
    normed_two = gather_rows((middle * factor_two * gain_two).astype(BF16))
    grad_own = jnp.where(own_keeping[:, None], cotangent, BF16(0))
    grad_out = gather_rows(grad_own)
    feed = dot(normed_two, feed_weight)
    feed_cols = dp * hidden_dev
    gate_lin, upward = feed[:, :feed_cols], feed[:, feed_cols:]
    sigmoid = jax.nn.sigmoid(gate_lin)
    hidden = (gate_lin * sigmoid * upward).astype(BF16)
    hidden_grad = dot_t(grad_out, down_own)
    gate_back = (hidden_grad * upward * sigmoid * (1.0 + gate_lin * (1.0 - sigmoid))).astype(BF16)
    up_back = (hidden_grad * gate_lin * sigmoid).astype(BF16)
    feed_back = jnp.concatenate([gate_back, up_back], axis=1)
    normed_two_grad = scatter_rows(dot_t(feed_back, feed_weight))
    mixed = middle + scatter_rows(dot(hidden, down_own))
    middle_in, gain_two_part = norm_back(middle, factor_two, gain_two, normed_two_grad)
    middle_grad = grad_own.astype(F32) + middle_in
    middle_back = gather_rows(middle_grad.astype(BF16))

    attended_grad = dot_t(middle_back, output_own).astype(BF16)
    if share > 1:
        attended_grad = jnp.where(own_rows, attended_grad, BF16(0))
    query_acc, key_acc, value_acc = attention_back(
        queries, keys, values, attended_grad, attended_sum, log_total, opening[:, None], block
    )
    query_acc = query_acc * scale
    query_back = query_acc * cos_heads - swap_halves(query_acc) * sin_heads
    key_back = key_acc * cos_heads - swap_halves(key_acc) * sin_heads
    qkv_back = jnp.concatenate([query_back, key_back, value_acc], axis=1).astype(BF16)
    normed_one_grad = scatter_rows(dot_t(qkv_back, qkv_weight))
    input_in, gain_one_part = norm_back(inputs, norm_factor(inputs), gain_one, normed_one_grad)
    token_grad = middle_grad + input_in

    feed_grad = exchange(sum_dp(t_dot(normed_two, feed_back)).astype(BF16)).astype(F32)
    feed_grad = feed_grad.reshape(seq, slab, 2, dp, hidden_dev)
    feed_grad = jnp.transpose(feed_grad, (2, 1, 3, 0, 4)).reshape(2, slab, dp * seq * hidden_dev)
    down_grad = sum_dp(t_dot(hidden, grad_out))
    output_part = t_dot(attended, middle_back)
    if share > 1:
        split = output_part.reshape(dp, share, slab, width)
        split = jnp.transpose(split, (1, 0, 2, 3)).reshape(share * dp * slab, width)
        output_part = lax.psum_scatter(
            split, "seq", scatter_dimension=0, tiled=True, axis_index_groups=groups
        )
    output_grad = sum_dp(output_part)
    qkv_grad = exchange(sum_dp(t_dot(normed_one, qkv_back)).astype(BF16)).astype(F32)
    qkv_grad = qkv_grad.reshape(seq, slab, 3, dp, HEAD_DIM)

    def own_columns(part, kept):
        summed = jnp.sum(part.reshape(kept, seq // kept, slab, dp, HEAD_DIM), axis=1)
        return jnp.transpose(summed, (1, 2, 0, 3)).reshape(slab, dp * kept * HEAD_DIM)

    query_grad = own_columns(qkv_grad[:, :, 0], half_heads)
    key_grad = own_columns(qkv_grad[:, :, 1], half_kv)
    value_grad = own_columns(qkv_grad[:, :, 2], half_kv)
    gain_parts = lax.psum(jnp.stack([gain_one_part, gain_two_part]), ("dp", "seq"))
    own = lax.axis_index("dp") * seq + mine
    gain_grads = lax.dynamic_slice_in_dim(gain_parts, own * slab, slab, 1)
    return (
        mixed,
        token_grad,
        gain_grads[0],
        gain_grads[1],
        query_grad,
        key_grad,
        value_grad,
        output_grad,
        feed_grad[0],
        feed_grad[1],
        down_grad,
    )


def frequencies():
    exponent = np.arange(0, HEAD_DIM, 2, dtype=np.float32) / np.float32(HEAD_DIM)
    inverse = np.power(np.float32(500000.0), -exponent)
    wavelength = np.float32(2.0 * math.pi) / inverse
    smooth = (np.float32(8192.0) / wavelength - np.float32(1.0)) / np.float32(3.0)
    blended = (np.float32(1.0) - smooth) * inverse / np.float32(32.0) + smooth * inverse
    scaled = np.where(
        wavelength < 2048.0,
        inverse,
        np.where(wavelength > 8192.0, inverse / np.float32(32.0), blended),
    )
    return np.tile(scaled.astype(np.float32), 4)


FREQUENCIES = frequencies()


def shards(
    tokens,
    cotangent,
    doc_lengths,
    attn_gain,
    mlp_gain,
    query_weight,
    key_weight,
    value_weight,
    output_weight,
    gate_weight,
    up_weight,
    down_weight,
):
    dp = lax.axis_size("dp")
    seq = lax.axis_size("seq")
    mine = lax.axis_index("seq")
    tok_count, width = tokens.shape
    slab = query_weight.shape[0]
    block = 512
    gain_one = attn_gain[None, :]
    gain_two = mlp_gain[None, :]

    (
        normed_one,
        grad_out,
        queries,
        keys,
        values,
        cosine,
        sine,
        opening,
        qkv_weight,
        gate_scaled,
        up_scaled,
        feed_near,
        down_own,
        output_own,
    ) = gather_project(
        doc_lengths,
        tokens,
        cotangent,
        query_weight,
        key_weight,
        value_weight,
        gate_weight,
        up_weight,
        (gain_one, gain_two),
        jnp.asarray(FREQUENCIES)[None, :],
        down_weight,
        output_weight,
        0,
    )
    qkv_weight = qkv_weight.reshape(width, -1)
    down_own = down_own.reshape(-1, width)
    output_own = output_own.reshape(-1, width)
    attended_sum, log_total, feed_far, attended, feed_other = attention_feed(
        queries,
        keys,
        values,
        opening,
        gate_scaled,
        up_scaled,
        feed_near,
        block,
        1,
    )
    middle, middle_normed, feed_weight = product_scatter_feed(
        attended, output_own, tokens, feed_near, feed_other, feed_far, 2
    )
    feed_weight = feed_weight.reshape(width, -1)

    normed_two, hidden, feed_back, feed_turned = gather_feed(
        middle_normed, grad_out, feed_weight, down_own, 3
    )
    middle_grad, middle_back, mixed_sum, feed_sums = product_scatter_both(
        feed_back, feed_turned, hidden, down_own, middle, grad_out, normed_two, 4
    )
    feed_sums = feed_sums.reshape(seq, slab, -1)
    attended_grad, output_kept, output_away, down_kept, down_away, feed_grad_near = gather_back(
        middle_back, output_own, attended, hidden, grad_out, feed_sums, 5
    )

    qkv_back, feed_grad_far, down_came, output_came = attention_back_feed(
        queries,
        keys,
        values,
        attended_grad,
        attended_sum,
        log_total,
        opening,
        cosine,
        sine,
        feed_sums,
        down_away,
        output_away,
        block,
        6,
    )
    normed_one_grad, qkv_grads = product_scatter_last(qkv_back, qkv_weight, normed_one, 7)

    pair = ((mine // 2) % 2).reshape(1)
    (
        gate_grad,
        up_grad,
        query_grad,
        key_grad,
        value_grad,
        attn_gain_grad,
        mlp_gain_grad,
        mixed,
        token_grad,
        down_grad,
        output_grad,
    ) = unpack(
        pair,
        feed_grad_near,
        feed_grad_far,
        gate_weight,
        up_weight,
        qkv_grads,
        query_weight,
        key_weight,
        value_weight,
        gain_one,
        gain_two,
        tokens,
        middle,
        mixed_sum,
        middle_grad,
        normed_one_grad,
        down_kept,
        down_came,
        output_kept,
        output_came,
    )
    return (
        mixed,
        token_grad,
        attn_gain_grad[0],
        mlp_gain_grad[0],
        query_grad,
        key_grad,
        value_grad,
        output_grad,
        gate_grad,
        up_grad,
        down_grad,
    )


def solution(mesh):
    both = P(("dp", "seq"), None)
    line = P(("dp", "seq"))
    dp, seq = mesh.shape["dp"], mesh.shape["seq"]

    def run(*args):
        tokens = args[0].shape[0]
        width = args[0].shape[1]
        suits = dp == 2 and seq % 4 == 0 and width == dp * seq * HEAD_DIM
        suits = suits and 2 * (tokens // dp) * width <= 16 << 20
        return jax.shard_map(
            shards if suits else plain_shards,
            mesh=mesh,
            in_specs=(both, both, P("dp", None), line, line) + (both,) * 7,
            out_specs=(both, both, line, line) + (both,) * 7,
            check_vma=False,
        )(*args)

    return run
```

```python
import functools
import math

import jax
import jax.numpy as jnp
import numpy as np
from jax import lax
from jax.experimental import pallas as pl
from jax.experimental.pallas import tpu as pltpu
from jax.sharding import PartitionSpec as P

HEADS = 32
KV_HEADS = 8
HEAD_DIM = 64
DOCS = 4
EPS = 1e-05
NEG = -1e30
MESH = pl.DeviceIdType.MESH
F32 = jnp.float32
BF16 = jnp.bfloat16


def rotary_table(head_dim):
    exponent = jnp.arange(0, head_dim, 2, dtype=F32) / head_dim
    inverse = jnp.power(F32(500000.0), -exponent)
    wavelength = 2.0 * math.pi / inverse
    smooth = (8192.0 / wavelength - 1.0) / 3.0
    blended = (1.0 - smooth) * inverse / 32.0 + smooth * inverse
    return jnp.where(
        wavelength < 2048.0, inverse, jnp.where(wavelength > 8192.0, inverse / 32.0, blended)
    )


def swap_halves(values):
    rows, cols = values.shape
    halves = values.reshape(rows, cols // HEAD_DIM, 2, HEAD_DIM // 2)
    return halves[:, :, ::-1].reshape(rows, cols)


def dot(a, b):
    return jnp.dot(a, b, preferred_element_type=F32)


def dot_t(a, b):
    return lax.dot_general(a, b, (((1,), (1,)), ((), ())), preferred_element_type=F32)


def t_dot(a, b):
    return lax.dot_general(a, b, (((0,), (0,)), ((), ())), preferred_element_type=F32)


def allowed_tile(opening, q_first, k_first, shape):
    rows = q_first + lax.broadcasted_iota(jnp.int32, shape, 0)
    cols = k_first + lax.broadcasted_iota(jnp.int32, shape, 1)
    return (cols <= rows) & (cols >= opening)


def attention_kernel(block, q_ref, k_ref, v_ref, open_ref, out_ref, lse_ref, tile=None):
    if tile is None:
        tile = pl.program_id(0)
    opening = open_ref[...]
    heads = [
        slice(i * HEAD_DIM, (i + 1) * HEAD_DIM) for i in range(q_ref.shape[1] // HEAD_DIM)
    ]

    def step(j, carry):
        first = pl.multiple_of(j * block, block)
        allowed = allowed_tile(opening, tile * block, first, (block, block))
        after = []
        for lanes, (peak, total, acc) in zip(heads, carry):
            scores = dot_t(q_ref[:, lanes], k_ref[pl.ds(first, block), lanes])
            scores = jnp.where(allowed, scores, NEG)
            new_peak = jnp.maximum(peak, jnp.max(scores, axis=1, keepdims=True))
            spread = jnp.exp(scores - new_peak)
            fade = jnp.exp(peak - new_peak)
            total = total * fade + jnp.sum(spread, axis=1, keepdims=True)
            acc = acc * fade + dot(spread.astype(BF16), v_ref[pl.ds(first, block), lanes])
            after.append((new_peak, total, acc))
        return tuple(after)

    start = (
        jnp.full((block, 1), NEG, F32),
        jnp.zeros((block, 1), F32),
        jnp.zeros((block, HEAD_DIM), F32),
    )
    done = lax.fori_loop(0, tile + 1, step, (start,) * len(heads))
    for head, (lanes, (peak, total, acc)) in enumerate(zip(heads, done)):
        out_ref[:, lanes] = acc / total
        lse_ref[:, head : head + 1] = peak + jnp.log(total)


def attention(queries, keys, values, opening, block):
    rows, cols = queries.shape
    heads = cols // HEAD_DIM
    tiled = lambda width: pl.BlockSpec((block, width), lambda i: (i, 0))
    whole = pl.BlockSpec((rows, cols), lambda i: (0, 0))
    return pl.pallas_call(
        functools.partial(attention_kernel, block),
        grid=(rows // block,),
        in_specs=[tiled(cols), whole, whole, tiled(1)],
        out_specs=[tiled(cols), tiled(heads)],
        out_shape=[
            jax.ShapeDtypeStruct((rows, cols), F32),
            jax.ShapeDtypeStruct((rows, heads), F32),
        ],
        compiler_params=pltpu.CompilerParams(vmem_limit_bytes=48 << 20),
        cost_estimate=pl.CostEstimate(
            flops=2 * rows * rows * cols, bytes_accessed=10 * rows * cols, transcendentals=0
        ),
    )(queries, keys, values, opening)


def attention_back_kernel(
    block, q_ref, k_ref, v_ref, g_ref, att_ref, lse_ref, open_ref, dq_ref, dk_ref, dv_ref
):
    tile = pl.program_id(0)

    @pl.when(tile == 0)
    def _():
        dk_ref[...] = jnp.zeros_like(dk_ref)
        dv_ref[...] = jnp.zeros_like(dv_ref)

    opening = open_ref[...]
    heads = []
    for head in range(q_ref.shape[1] // HEAD_DIM):
        lanes = slice(head * HEAD_DIM, (head + 1) * HEAD_DIM)
        grad = g_ref[:, lanes].astype(F32)
        row_sum = jnp.sum(grad * att_ref[:, lanes], axis=1, keepdims=True)
        heads.append((lanes, lse_ref[:, head : head + 1], row_sum))

    def step(j, carry):
        first = pl.multiple_of(j * block, block)
        here = pl.ds(first, block)
        allowed = allowed_tile(opening, tile * block, first, (block, block))
        after = []
        for (lanes, log_total, row_sum), acc in zip(heads, carry):
            query, grad, key = q_ref[:, lanes], g_ref[:, lanes], k_ref[here, lanes]
            scores = dot_t(query, key)
            chance = jnp.where(allowed, jnp.exp(scores - log_total), 0.0)
            prob_grad = dot_t(grad, v_ref[here, lanes])
            score_grad = (chance * (prob_grad - row_sum)).astype(BF16)
            dk_ref[here, lanes] += t_dot(score_grad, query)
            dv_ref[here, lanes] += t_dot(chance.astype(BF16), grad)
            after.append(acc + dot(score_grad, key))
        return tuple(after)

    start = jnp.zeros((block, HEAD_DIM), F32)
    done = lax.fori_loop(0, tile + 1, step, (start,) * len(heads))
    for (lanes, _, _), acc in zip(heads, done):
        dq_ref[:, lanes] = acc


def attention_back(queries, keys, values, grads, attended, log_total, opening, block):
    rows, cols = queries.shape
    heads = cols // HEAD_DIM
    tiled = lambda width: pl.BlockSpec((block, width), lambda i: (i, 0))
    whole = pl.BlockSpec((rows, cols), lambda i: (0, 0))
    return pl.pallas_call(
        functools.partial(attention_back_kernel, block),
        grid=(rows // block,),
        in_specs=[tiled(cols), whole, whole, tiled(cols), tiled(cols), tiled(heads), tiled(1)],
        out_specs=[tiled(cols), whole, whole],
        out_shape=[jax.ShapeDtypeStruct((rows, cols), F32)] * 3,
        compiler_params=pltpu.CompilerParams(vmem_limit_bytes=60 << 20),
        cost_estimate=pl.CostEstimate(
            flops=5 * rows * rows * cols, bytes_accessed=20 * rows * cols, transcendentals=0
        ),
    )(queries, keys, values, grads, attended, log_total, opening)


def nothing():
    pass


class Place:
    def __init__(self):
        self.dp = lax.axis_index("dp")
        self.mine = lax.axis_index("seq")
        self.count = lax.axis_size("seq")
        self.length = self.count // 4
        self.line = lax.div(self.mine, 4)
        self.pair = lax.rem(lax.div(self.mine, 2), 2)
        self.core = lax.rem(self.mine, 2)
        self.slot = self.line * 2 + self.core

    def index(self, line, pair, core):
        return (line * 2 + pair) * 2 + core

    def peer(self, slot, same):
        pair = self.pair if same else 1 - self.pair
        return self.index(lax.div(slot, 2), pair, lax.rem(slot, 2))

    def device(self, line, pair, core):
        return (self.dp, self.index(line, pair, core))

    def sibling(self):
        return self.device(self.line, self.pair, 1 - self.core)

    def across(self):
        return self.device(self.line, 1 - self.pair, self.core)

    def above(self):
        return self.device(self.line + 1, self.pair, self.core)

    def below(self):
        return self.device(self.line - 1, self.pair, self.core)

    def partner(self):
        return (1 - self.dp, self.mine)

    def greet(self, partner=False):
        barrier = pltpu.get_barrier_semaphore()

        def signal(device):
            pl.semaphore_signal(barrier, inc=1, device_id=device, device_id_type=MESH)

        signal(self.sibling())
        signal(self.across())
        pl.when(self.line > 0)(lambda: signal(self.below()))
        pl.when(self.line < self.length - 1)(lambda: signal(self.above()))
        if partner:
            signal(self.partner())
        inner = (self.line > 0) & (self.line < self.length - 1)
        pl.semaphore_wait(barrier, jnp.where(inner, 4, 3) + (1 if partner else 0))

    def greet_all(self, meanwhile=nothing):
        self.call_all()
        meanwhile()
        self.await_all()

    def await_all(self):
        pl.semaphore_wait(pltpu.get_barrier_semaphore(), self.count)

    def call_all(self):
        barrier = pltpu.get_barrier_semaphore()

        def signal(device):
            pl.semaphore_signal(barrier, inc=1, device_id=device, device_id_type=MESH)

        signal(self.partner())

        @pl.loop(1, self.count)
        def _(ahead):
            signal((self.dp, lax.rem(self.mine + ahead, self.count)))


def remote(src, dst, send_sem, recv_sem, device):
    return pltpu.make_async_remote_copy(
        src_ref=src,
        dst_ref=dst,
        send_sem=send_sem,
        recv_sem=recv_sem,
        device_id=device,
        device_id_type=MESH,
    )


class Spread:
    def __init__(self, here, same, copies):
        self.here, self.same, self.copies = here, same, copies
        self.slots = here.count // 2

    def each(self, visit):
        @pl.loop(1 if self.same else 0, self.slots)
        def _(ahead):
            slot = lax.rem(self.here.slot + ahead, self.slots)
            visit(self.here.peer(slot, self.same), slot)

    def start_one(self, ahead):
        slot = lax.rem(self.here.slot + ahead, self.slots)
        peer = self.here.peer(slot, self.same)
        for one in self.copies(peer, self.here.mine, self.here.slot, slot):
            one.start()

    def start(self):
        pl.loop(1 if self.same else 0, self.slots)(self.start_one)

    def start_some(self, number, each):
        first = 1 if self.same else 0

        @pl.loop(0, each)
        def _(i):
            ahead = first + number * each + i
            pl.when((number >= 0) & (ahead < self.slots))(lambda: self.start_one(ahead))

    def finish(self):
        def visit(peer, slot):
            for one in self.copies(peer, peer, slot, slot):
                one.wait()

        self.each(visit)


def block_spread(here, same, blocks, into, sems):
    def copies(peer, sender, at, sem):
        return [
            remote(
                blocks.at[peer],
                into.at[at],
                sems.at[0, sem],
                sems.at[1, at],
                (here.dp, peer),
            )
        ]

    return Spread(here, same, copies)


def feed_spread(here, same, weights, into, sems):
    dp = lax.axis_size("dp")
    columns = into.shape[2] // (dp * len(weights))

    def copies(peer, sender, at, sem):
        made = []
        for kind, weight in enumerate(weights):
            for half in range(dp):
                part = kind * dp + half
                begin = pl.multiple_of((half * here.count + peer) * columns, columns)
                made.append(
                    remote(
                        weight.at[:, pl.ds(begin, columns)],
                        into.at[at, :, pl.ds(part * columns, columns)],
                        sems.at[0, sem, part],
                        sems.at[1, at, part],
                        (here.dp, peer),
                    )
                )
        return made

    return Spread(here, same, copies)


def gather_units(here, buf, send_sems, recv_sems, compute, between=None, ready=None, started=nothing):
    length = here.length
    last = length - 1
    steps = 2 * length
    mine = here.mine
    shorter = jnp.minimum(here.line, last - here.line)
    longer = jnp.where(here.line < last - here.line, 1, -1)

    def column(j):
        i = j - 1
        paired = jnp.where(i % 2 == 0, here.line - i // 2 - 1, here.line + i // 2 + 1)
        single = here.line + longer * (i - shorter + 1)
        return jnp.where(j == 0, here.line, jnp.where(i < 2 * shorter, paired, single))

    def copy(way, device, block, part):
        ref = buf.at[block, part]
        return remote(
            ref, ref, send_sems.at[way, block, part], recv_sems.at[block, part], device
        )

    def up(block, part):
        return copy(0, here.above(), block, part)

    def down(block, part):
        return copy(1, here.below(), block, part)

    def across(block, part):
        return copy(2, here.across(), block, part)

    def sideways(block, part):
        return copy(3, here.sibling(), block, part)

    def unit(number):
        in_column = (number % 2 == 1) & (number < steps - 1) | (number == 0)
        later = jnp.where(number == steps - 1, last, number // 2 - 1)
        line = column(jnp.where(in_column, (number + 1) // 2, later))
        pair = jnp.where(in_column, here.pair, 1 - here.pair)
        other = here.index(line, pair, 1 - here.core)
        sideways(other, 0).wait_recv()
        sideways(other, 1).wait_recv()
        compute(number, here.index(line, pair, 0))

    for part in range(2):
        pl.when(here.line < last)(lambda part=part: up(mine, part).start())
        pl.when(here.line > 0)(lambda part=part: down(mine, part).start())
        across(mine, part).start()
        sideways(mine, part).start()
    started()

    @pl.loop(0, steps)
    def _(step):
        part = step % 2
        far = step // 2 + 1

        @pl.when(here.line >= far)
        def _():
            block = here.index(here.line - far, here.pair, here.core)
            up(block, part).wait_recv()
            pl.when(here.line < last)(lambda: up(block, part).start())
            sideways(block, part).start()

        @pl.when(here.line + far <= last)
        def _():
            block = here.index(here.line + far, here.pair, here.core)
            down(block, part).wait_recv()
            pl.when(here.line > 0)(lambda: down(block, part).start())
            sideways(block, part).start()

        @pl.when(step + 2 < steps)
        def _():
            across(here.index(column(step // 2 + 1), here.pair, here.core), part).start()

        block = here.index(column(step // 2), 1 - here.pair, here.core)
        across(block, part).wait_recv()
        sideways(block, part).start()

        if between is not None:
            between(step)
        if ready is None:
            unit(step)
        else:
            begin = jnp.maximum(2 * (step - ready), 0)
            end = jnp.maximum(2 * (step + 1 - ready), 0)

            @pl.loop(begin, end)
            def _(number):
                unit(number)

    @pl.loop(0, length)
    def _(line):
        for part in range(2):
            block = here.index(line, here.pair, here.core)

            @pl.when((line <= here.line) & (here.line < last))
            def _():
                up(block, part).wait_send()

            @pl.when((line >= here.line) & (here.line > 0))
            def _():
                down(block, part).wait_send()

            across(block, part).wait_send()
            sideways(block, part).wait_send()
            sideways(here.index(line, 1 - here.pair, here.core), part).wait_send()


def put_own(here, own_ref, buf):
    half = buf.shape[2]
    for part in range(2):
        buf[here.mine, part] = own_ref[pl.ds(part * half, half), :]


def gather_scratch(seq, rows, width):
    return [
        pltpu.VMEM((seq, 2, rows, width), BF16),
        pltpu.SemaphoreType.DMA((4, seq, 2)),
        pltpu.SemaphoreType.DMA((seq, 2)),
    ]


def unit_rows(first, rows):
    return pl.ds(pl.multiple_of(first * rows, 2 * rows), 2 * rows)


def take_unit(buf, first):
    blocks = buf[pl.ds(first, 2)]
    return blocks.reshape(-1, blocks.shape[-1])


class UnitStore:
    def __init__(self, buf, out_ref, sems):
        self.buf, self.out_ref, self.sems = buf, out_ref, sems

    def copies(self, number, first):
        half = self.buf.shape[2]
        made = []
        for block in range(2):
            for part in range(2):
                begin = ((first + block) * 2 + part) * half
                made.append(
                    pltpu.make_async_copy(
                        self.buf.at[first + block, part],
                        self.out_ref.at[pl.ds(pl.multiple_of(begin, half), half)],
                        self.sems.at[number, block, part],
                    )
                )
        return made

    def start(self, number, first):
        for one in self.copies(number, first):
            one.start()

    def finish(self):
        @pl.loop(0, self.sems.shape[0])
        def _(number):
            for one in self.copies(number, 0):
                one.wait()


def params(call_id, mebibytes):
    return pltpu.CompilerParams(
        collective_id=call_id, has_side_effects=True, vmem_limit_bytes=mebibytes << 20
    )


def cost(flops, bytes_accessed):
    return pl.CostEstimate(flops=flops, bytes_accessed=bytes_accessed, transcendentals=0)


VMEM = pl.BlockSpec(memory_space=pltpu.VMEM)
HBM = pl.BlockSpec(memory_space=pl.ANY)


def rotated(values, cosine, sine):
    cols = values.shape[1]
    lane = lax.broadcasted_iota(jnp.int32, values.shape, 1)
    ahead = pltpu.roll(values, cols - HEAD_DIM // 2, 1)
    behind = pltpu.roll(values, HEAD_DIM // 2, 1)
    swapped = jnp.where(lane % HEAD_DIM < HEAD_DIM // 2, ahead, behind)
    return values * cosine + swapped * sine


def upright(row):
    count = row.shape[1]
    shape = (count, count)
    same = lax.broadcasted_iota(jnp.int32, shape, 0) == lax.broadcasted_iota(jnp.int32, shape, 1)
    return jnp.sum(jnp.where(same, row.astype(F32), 0.0), axis=1, keepdims=True)


def flat(column):
    count = column.shape[0]
    shape = (count, count)
    same = lax.broadcasted_iota(jnp.int32, shape, 0) == lax.broadcasted_iota(jnp.int32, shape, 1)
    return jnp.sum(jnp.where(same, column, 0.0), axis=0, keepdims=True)


def project_kernel(
    lengths_ref,
    tokens_ref,
    cotangent_ref,
    query_ref,
    key_ref,
    value_ref,
    gate_ref,
    up_ref,
    gain_one_ref,
    gain_two_ref,
    freq_ref,
    down_ref,
    output_ref,
    normed_ref,
    grads_ref,
    q_ref,
    k_ref,
    v_ref,
    cos_ref,
    sin_ref,
    open_ref,
    weight_ref,
    gate_out_ref,
    up_out_ref,
    feed_ref,
    down_out_ref,
    output_out_ref,
    buf,
    send_sems,
    recv_sems,
    blocks,
    store_sems,
    near_sems,
    far_sems,
    feed_sems,
    swap_sems,
    local_sems,
    pair_sems,
    share_sems,
):
    here = Place()
    cols = q_ref.shape[1]
    rows = tokens_ref.shape[0]
    dp = here.dp
    ends = [lengths_ref[0, 0]]
    for j in range(1, DOCS):
        ends.append(ends[-1] + lengths_ref[0, j])

    def own_rows():
        chunk = 32

        @pl.loop(0, rows // chunk)
        def _(i):
            some = pl.ds(pl.multiple_of(i * chunk, chunk), chunk)
            values = tokens_ref[some, :].astype(F32)
            factor = lax.rsqrt(jnp.mean(values * values, axis=1, keepdims=True) + EPS)
            buf[here.mine, 0, some, :] = (values * factor).astype(BF16)
            shape = (chunk, cotangent_ref.shape[1])
            place = here.mine * rows + i * chunk + lax.broadcasted_iota(jnp.int32, shape, 0)
            grads = cotangent_ref[some, :].astype(F32)
            buf[here.mine, 1, some, :] = jnp.where(place < ends[-1], grads, 0.0).astype(BF16)

    def own_blocks():
        gain = upright(gain_one_ref[...])
        query = query_ref[...].astype(F32) * gain
        key = key_ref[...].astype(F32) * gain
        value = value_ref[...].astype(F32) * gain

        def heads(array, number, kept):
            parts = []
            for half in range(2):
                head = half * kept + number * kept // blocks.shape[0]
                parts.append(array[:, head * HEAD_DIM : (head + 1) * HEAD_DIM])
            return jnp.concatenate(parts, axis=1).astype(BF16)

        for number in range(blocks.shape[0]):
            blocks[number, :, :cols] = heads(query, number, HEADS // 2)
            array = value if number % 2 else key
            blocks[number, :, cols:] = heads(array, number, KV_HEADS // 2)

    def own_parts():
        own_blocks()
        own_rows()

    here.greet_all(own_parts)

    def weight_spread(same, sems):
        def copies(peer, sender, at, sem):
            return [
                remote(
                    blocks.at[peer],
                    weight_ref.at[dp, sender],
                    sems.at[0, sem],
                    sems.at[1, at],
                    (dp, peer),
                )
            ]

        return Spread(here, same, copies)

    near = weight_spread(True, near_sems)
    far = weight_spread(False, far_sems)
    swaps = []
    for number, (src, dst) in enumerate([(down_ref, down_out_ref), (output_ref, output_out_ref)]):
        swaps.append(
            remote(src, dst.at[dp], swap_sems.at[0, number], swap_sems.at[1, number], here.partner())
        )
        swaps.append(pltpu.make_async_copy(src, dst.at[dp], local_sems.at[number]))
    feed = feed_spread(here, True, (gate_out_ref, up_out_ref), feed_ref, feed_sems)
    columns = feed_ref.shape[2] // 4
    own_feed = []
    for kind, weight in enumerate((gate_out_ref, up_out_ref)):
        for half in range(2):
            part = kind * 2 + half
            begin = pl.multiple_of((half * here.count + here.mine) * columns, columns)
            own_feed.append(
                pltpu.make_async_copy(
                    weight.at[:, pl.ds(begin, columns)],
                    feed_ref.at[here.slot, :, pl.ds(part * columns, columns)],
                    local_sems.at[2 + part],
                )
            )

    def pair_copy(source, sender):
        return remote(
            weight_ref.at[source, sender],
            weight_ref.at[source, sender],
            pair_sems.at[0, sender],
            pair_sems.at[1, sender],
            here.partner(),
        )

    def own_tables():
        chunk = 128

        @pl.loop(0, open_ref.shape[0] // chunk)
        def _(i):
            some = pl.ds(pl.multiple_of(i * chunk, chunk), chunk)
            place = i * chunk + lax.broadcasted_iota(jnp.int32, (chunk, 1), 0)
            opening = jnp.zeros((chunk, 1), jnp.int32)
            for end in ends:
                opening = jnp.where(place >= end, end, opening)
            open_ref[some, :] = opening
            angles = (place - opening).astype(F32) * freq_ref[...]
            lane = lax.broadcasted_iota(jnp.int32, angles.shape, 1)
            sine = jnp.sin(angles)
            cos_ref[some, :] = jnp.cos(angles)
            sin_ref[some, :] = jnp.where(lane % HEAD_DIM < HEAD_DIM // 2, -sine, sine)

    def started():
        far.start()
        near.start()
        weight_ref[dp, here.mine] = blocks[here.mine]
        for one in swaps:
            one.start()
        chunk = 512

        @pl.loop(0, gate_ref.shape[1] // chunk)
        def _(i):
            some = pl.ds(pl.multiple_of(i * chunk, chunk), chunk)
            gain = upright(gain_two_ref[...])
            gate_out_ref[:, some] = (gate_ref[:, some].astype(F32) * gain).astype(BF16)
            up_out_ref[:, some] = (up_ref[:, some].astype(F32) * gain).astype(BF16)

        for one in own_feed:
            one.start()
        own_tables()

    def between(step):
        feed.start_some(step - (2 * here.length - 3), 3)

        @pl.when(step == 2)
        def _():
            near.finish()
            far.finish()

            @pl.loop(0, here.count)
            def _(sender):
                pair_copy(dp, sender).start()

        @pl.when(step == 4)
        def _():
            @pl.loop(0, here.count)
            def _(sender):
                pair_copy(1 - dp, sender).wait_recv()

    def share_copy(ref, number, where):
        return remote(
            ref.at[where],
            ref.at[where],
            share_sems.at[0, number],
            share_sems.at[1, number],
            here.sibling(),
        )

    def stores(number, first):
        made = []
        for block in range(2):
            where = pl.ds(pl.multiple_of((first + block) * rows, rows), rows)
            for part, out_ref in enumerate((normed_ref, grads_ref)):
                made.append(
                    pltpu.make_async_copy(
                        buf.at[first + block, part],
                        out_ref.at[where],
                        store_sems.at[number, block, part],
                    )
                )
        return made

    def compute(number, first):
        for one in stores(number, first):
            one.start()
        weight = weight_ref[...].reshape(-1, weight_ref.shape[-1])
        unit = buf[pl.ds(first, 2), 0]
        qkv = dot(unit.reshape(-1, unit.shape[-1]), weight)
        where = unit_rows(first, rows)
        cosine = cos_ref[where, :]
        sine = sin_ref[where, :]
        scale = BF16(1.0 / math.sqrt(HEAD_DIM))
        q_ref[where, :] = rotated(qkv[:, :cols], cosine, sine).astype(BF16) * scale
        for core, ref in enumerate((k_ref, v_ref)):

            @pl.when(here.core == core)
            def _():
                mine = qkv[:, cols:]
                ref[where, :] = (mine if core else rotated(mine, cosine, sine)).astype(BF16)
                share_copy(ref, number, where).start()

    gather_units(here, buf, send_sems, recv_sems, compute, between, here.length, started)

    @pl.loop(0, here.count)
    def _(sender):
        pair_copy(dp, sender).wait_send()

    @pl.loop(0, here.count // 2)
    def _(number):
        for one in stores(number, 0):
            one.wait()
        share_copy(k_ref, number, unit_rows(0, rows)).wait()

    feed.finish()
    for one in swaps + own_feed:
        one.wait()


def gather_project(
    lengths, tokens, cotangent, query, key, value, gate, up, gains, freq, down, output, call_id
):
    seq = lax.axis_size("seq")
    rows, width = tokens.shape
    cols = 2 * HEAD_DIM
    slab, ff = gate.shape
    bf16 = lambda *shape: jax.ShapeDtypeStruct(shape, BF16)
    f32 = lambda *shape: jax.ShapeDtypeStruct(shape, F32)
    all_rows = seq * rows
    dma = pltpu.SemaphoreType.DMA
    return pl.pallas_call(
        project_kernel,
        out_shape=[
            bf16(all_rows, width),
            bf16(all_rows, width),
            bf16(all_rows, cols),
            bf16(all_rows, cols),
            bf16(all_rows, cols),
            f32(all_rows, cols),
            f32(all_rows, cols),
            jax.ShapeDtypeStruct((all_rows, 1), jnp.int32),
            bf16(2, seq, slab, 2 * cols),
            bf16(slab, ff),
            bf16(slab, ff),
            bf16(seq // 2, slab, 4 * down.shape[0]),
            bf16(2, *down.shape),
            bf16(2, *output.shape),
        ],
        in_specs=[pl.BlockSpec(memory_space=pltpu.SMEM)] + [VMEM] * 10 + [HBM] * 2,
        out_specs=[HBM] * 2 + [VMEM] * 9 + [HBM] * 3,
        scratch_shapes=gather_scratch(seq, rows, width)
        + [
            pltpu.VMEM((seq, slab, 2 * cols), BF16),
            dma((seq // 2, 2, 2)),
            dma((2, seq // 2)),
            dma((2, seq // 2)),
            dma((2, seq // 2, 4)),
            dma((2, 2)),
            dma((6,)),
            dma((2, seq)),
            dma((2, seq // 2)),
        ],
        compiler_params=params(call_id, 60),
        cost_estimate=cost(2 * all_rows * width * 2 * cols, 8 * all_rows * width),
    )(lengths, tokens, cotangent, query, key, value, gate, up, *gains, freq, down, output)


ROW_CHUNK = 32


def norm_input_grad(values, upstream):
    factor = norm_factor(values)
    inner_mean = jnp.mean(upstream * values, axis=-1, keepdims=True)
    return factor * upstream - values * factor * factor * factor * inner_mean


def in_row_chunks(rows, chunk, visit):
    @pl.loop(0, rows // chunk)
    def _(i):
        visit(pl.ds(pl.multiple_of(i * chunk, chunk), chunk))


SCATTER_PARTS = 2
SCATTER_RING = 4
SCATTER_SCRATCH = 11


def scatter_rows_of_products(
    here,
    products,
    core_out,
    core_in,
    pair_out,
    pair_in,
    line_out,
    line_in,
    held,
    core_sems,
    pair_sems,
    line_sems,
    came_sems,
    first=None,
    between=nothing,
    filler=None,
):
    length = here.length
    parts = SCATTER_PARTS * len(products)
    rows, width = held.shape
    tile = min(width, 512)
    tiles = width // tile
    steps = length * parts

    def target(i):
        ups = length - 1 - here.line
        near = here.line < length // 2
        if_near = jnp.where(i < ups, length - 1 - i, i - ups)
        if_far = jnp.where(i < here.line, i, length - 1 - (i - here.line))
        return jnp.where(i == length - 1, here.line, jnp.where(near, if_near, if_far))

    def product(line, pair, core, part, use):
        first = pl.multiple_of(here.index(line, pair, core) * rows, rows)

        def one(number):
            transposed, a_ref, b_ref, _ = products[number]
            a = a_ref[pl.ds(first, rows), :]
            begin = (part - number * SCATTER_PARTS) * width

            @pl.loop(0, tiles)
            def _(t):
                into = pl.ds(pl.multiple_of(t * tile, tile), tile)
                cols = pl.ds(pl.multiple_of(begin + t * tile, tile), tile)
                use(dot_t(a, b_ref[cols, :]) if transposed else dot(a, b_ref[:, cols]), into)

        for number in range(len(products)):
            pl.when(part // SCATTER_PARTS == number)(functools.partial(one, number))

    def core_copy(slot):
        return remote(
            core_out.at[slot % SCATTER_RING],
            core_in.at[slot],
            core_sems.at[0, slot],
            core_sems.at[1, slot],
            here.sibling(),
        )

    def pair_copy(slot):
        return remote(
            pair_out.at[slot],
            pair_in.at[slot],
            pair_sems.at[0, slot],
            pair_sems.at[1, slot],
            here.across(),
        )

    def up_copy(slot, line, part):
        into = (line + 1) * parts + part
        return remote(
            line_out.at[slot], line_in.at[into], line_sems.at[slot], came_sems.at[into], here.above()
        )

    def down_copy(slot, line, part):
        into = line * parts + part
        return remote(
            line_out.at[slot], line_in.at[into], line_sems.at[slot], came_sems.at[into], here.below()
        )

    def for_sibling(step, pair, slot):
        pl.when(slot >= SCATTER_RING)(lambda: core_copy(slot - SCATTER_RING).wait_send())

        def use(value, cols):
            core_out[slot % SCATTER_RING, :, cols] = value.astype(BF16)

        product(target(step // parts), pair, 1 - here.core, step % parts, use)
        core_copy(slot).start()

    for_sibling(jnp.int32(0), 1 - here.pair, jnp.int32(0))

    @pl.loop(0, steps)
    def _(step):
        if first is not None:
            first(step)
        pl.when(step < steps - 1)(lambda: for_sibling(step + 1, 1 - here.pair, step + 1))
        core_copy(step).wait_recv()

        def use(value, cols):
            pair_out[step, :, cols] = (value + core_in[step, :, cols].astype(F32)).astype(BF16)

        product(target(step // parts), 1 - here.pair, here.core, step % parts, use)
        pair_copy(step).start()

    for_sibling(jnp.int32(0), here.pair, jnp.int32(steps))
    between()

    @pl.loop(0, steps)
    def _(step):
        pl.when(step < steps - 1)(lambda: for_sibling(step + 1, here.pair, steps + step + 1))
        core_copy(steps + step).wait_recv()
        line = target(step // parts)
        part = step % parts

        def use(value, cols):
            held[:, cols] = value + core_in[steps + step, :, cols].astype(F32)

        product(line, here.pair, here.core, part, use)
        if filler is not None:
            filler(step)
        pair_copy(step).wait_recv()
        from_above = (line <= here.line) & (here.line < length - 1)
        from_below = (line >= here.line) & (here.line > 0)
        held[...] += pair_in[step].astype(F32)

        @pl.when(from_above)
        def _():
            down_copy(0, line, part).wait_recv()
            held[...] += line_in[line * parts + part].astype(F32)

        @pl.when(from_below)
        def _():
            up_copy(0, line, part).wait_recv()
            held[...] += line_in[(line + 1) * parts + part].astype(F32)

        for number, (_, _, _, out_ref) in enumerate(products):

            @pl.when((line == here.line) & (part // SCATTER_PARTS == number))
            def _():
                begin = (part - number * SCATTER_PARTS) * width
                out_ref[:, pl.ds(pl.multiple_of(begin, width), width)] = held[...]

        @pl.when(line < here.line)
        def _():
            line_out[step] = held[...].astype(BF16)
            down_copy(step, line, part).start()

        @pl.when(line > here.line)
        def _():
            line_out[step] = held[...].astype(BF16)
            up_copy(step, line, part).start()

    @pl.loop(2 * steps - SCATTER_RING, 2 * steps)
    def _(slot):
        core_copy(slot).wait_send()

    @pl.loop(0, steps)
    def _(step):
        pair_copy(step).wait_send()
        line = target(step // parts)
        pl.when(line < here.line)(lambda: down_copy(step, 0, 0).wait_send())
        pl.when(line > here.line)(lambda: up_copy(step, 0, 0).wait_send())


def scatter_scratch(seq, rows, width, count=1):
    length = seq // 4
    parts = SCATTER_PARTS * count
    steps = length * parts
    block = (rows, width // SCATTER_PARTS)
    dma = pltpu.SemaphoreType.DMA
    return [
        pltpu.VMEM((SCATTER_RING, *block), BF16),
        pltpu.VMEM((2 * steps, *block), BF16),
        pltpu.VMEM((steps, *block), BF16),
        pltpu.VMEM((steps, *block), BF16),
        pltpu.VMEM((steps, *block), BF16),
        pltpu.VMEM(((length + 1) * parts, *block), BF16),
        pltpu.VMEM(block, F32),
        dma((2, 2 * steps)),
        dma((2, steps)),
        dma((steps,)),
        dma(((length + 1) * parts,)),
    ]


def scatter_cost(a, width):
    return cost(2 * a.shape[0] * a.shape[1] * width, 4 * a.shape[0] * width)


def scatter_both_kernel(
    back_hbm,
    turned_hbm,
    hidden_hbm,
    down_hbm,
    middle_ref,
    grads_hbm,
    normed_hbm,
    grad_ref,
    low_ref,
    mixed_ref,
    sums_ref,
    *scratch,
):
    here = Place()
    factors = scratch[SCATTER_SCRATCH : SCATTER_SCRATCH + 4]
    back_ref, turned_ref, hidden_ref, down_ref = factors
    normed, away, came, own, fetch_sems, swap_sems, own_sems = scratch[SCATTER_SCRATCH + 4 :]
    rows = grad_ref.shape[0]
    loads = [
        pltpu.make_async_copy(src, dst, own_sems.at[number])
        for number, (src, dst) in enumerate(
            zip((back_hbm, turned_hbm, hidden_hbm, down_hbm), factors)
        )
    ]
    own_copy = pltpu.make_async_copy(
        grads_hbm.at[pl.ds(pl.multiple_of(here.mine * rows, rows), rows)], own, own_sems.at[4]
    )
    for one in loads + [own_copy]:
        one.start()
    here.greet(partner=True)
    for one in loads[:2]:
        one.wait()

    def first(step):
        @pl.when(step == SCATTER_PARTS - 1)
        def _():
            for one in loads[2:]:
                one.wait()
    chunk = normed.shape[2]
    half = normed_hbm.shape[1] // 2
    chunks = half // chunk

    def fetch(number):
        dp = jnp.where(number < chunks, 1 - here.dp, here.dp)
        begin = dp * half + number % chunks * chunk
        return pltpu.make_async_copy(
            normed_hbm.at[:, pl.ds(pl.multiple_of(begin, chunk), chunk)],
            normed.at[number % 2],
            fetch_sems.at[number % 2],
        )

    def swap(i):
        some = pl.ds(pl.multiple_of(i * chunk, chunk), chunk)
        return remote(
            away.at[some], came.at[some], swap_sems.at[0, i], swap_sems.at[1, i], here.partner()
        )

    def part(number):
        fetch(number).wait()
        pl.when(number + 1 < 2 * chunks)(lambda: fetch(number + 1).start())
        return t_dot(normed[number % 2], back_ref[...])

    def filler(step):
        @pl.when(step < chunks)
        def _():
            some = pl.ds(pl.multiple_of(step * chunk, chunk), chunk)
            away[some, :] = part(step).astype(BF16)
            swap(step).start()

        @pl.when((step >= chunks) & (step < 3 * chunks) & (step % 2 == 0))
        def _():
            i = (step - chunks) // 2
            some = pl.ds(pl.multiple_of(i * chunk, chunk), chunk)
            kept = part(chunks + i)
            swap(i).wait()
            sums_ref[some, :] = (kept + came[some, :].astype(F32)).astype(BF16)

    fetch(jnp.int32(0)).start()
    scatter_rows_of_products(
        here,
        [(False, back_ref, turned_ref, grad_ref), (False, hidden_ref, down_ref, mixed_ref)],
        *scratch[:SCATTER_SCRATCH],
        first=first,
        filler=filler,
    )
    own_copy.wait()

    def add(some):
        grad = own[some, :].astype(F32) + norm_input_grad(middle_ref[some, :], grad_ref[some, :])
        grad_ref[some, :] = grad
        low_ref[some, :] = grad.astype(BF16)

    in_row_chunks(rows, ROW_CHUNK, add)


def product_scatter_both(back, turned, hidden, down, middle, grads, normed, call_id):
    seq = lax.axis_size("seq")
    rows = back.shape[0] // seq
    width = turned.shape[1]
    cols = back.shape[1]
    chunk = width // 8
    dma = pltpu.SemaphoreType.DMA
    return pl.pallas_call(
        scatter_both_kernel,
        out_shape=[
            jax.ShapeDtypeStruct((rows, width), F32),
            jax.ShapeDtypeStruct((rows, width), BF16),
            jax.ShapeDtypeStruct((rows, width), F32),
            jax.ShapeDtypeStruct((width // 2, cols), BF16),
        ],
        in_specs=[HBM] * 4 + [VMEM] + [HBM] * 2,
        out_specs=[VMEM] * 4,
        scratch_shapes=scatter_scratch(seq, rows, width, 2)
        + [pltpu.VMEM(array.shape, BF16) for array in (back, turned, hidden, down)]
        + [
            pltpu.VMEM((2, normed.shape[0], chunk), BF16),
            pltpu.VMEM((width // 2, cols), BF16),
            pltpu.VMEM((width // 2, cols), BF16),
            pltpu.VMEM((rows, width), BF16),
            dma((2,)),
            dma((2, 4)),
            dma((5,)),
        ],
        compiler_params=params(call_id, 60),
        cost_estimate=scatter_cost(back, 3 * width),
    )(back, turned, hidden, down, middle, grads, normed)


def feed_kernel(
    block,
    q_ref,
    k_ref,
    v_ref,
    open_ref,
    b_ref,
    tokens_ref,
    gate_hbm,
    up_hbm,
    near_hbm,
    grad_hbm,
    down_hbm,
    attended_ref,
    lse_ref,
    a_ref,
    middle_ref,
    normed_ref,
    hidden_out_ref,
    back_out_ref,
    turned_out_ref,
    *scratch,
):
    here = Place()
    (
        feed_ref,
        swap_sems,
        local_sems,
        far_sems,
        buf,
        send_sems,
        recv_sems,
        store_sems,
        grad_ref,
        down_ref,
        hidden_ref,
        back_ref,
        turned_ref,
        fetch_sems,
        out_sems,
    ) = scratch[SCATTER_SCRATCH:]
    slots, slab = near_hbm.shape[:2]
    rows, width = middle_ref.shape
    hidden = hidden_ref.shape[1]
    tile = 256

    def fetch(slot):
        return pltpu.make_async_copy(
            near_hbm.at[slot], feed_ref.at[here.dp, here.peer(slot, True)], local_sems.at[slot]
        )

    def swap(slot, same):
        place = feed_ref.at[here.dp, here.peer(slot, same)]
        half = 0 if same else 1
        return remote(
            place,
            place,
            swap_sems.at[0, half, slot],
            swap_sems.at[1, half, slot],
            here.partner(),
        )

    columns = hidden // 2

    def far_copies(peer, sender, at, sem):
        made = []
        for kind, weight in enumerate((gate_hbm, up_hbm)):
            for half in range(2):
                part = kind * 2 + half
                begin = pl.multiple_of((half * here.count + peer) * columns, columns)
                made.append(
                    remote(
                        weight.at[:, pl.ds(begin, columns)],
                        feed_ref.at[here.dp, sender, :, pl.ds(part * columns, columns)],
                        far_sems.at[0, sem, part],
                        far_sems.at[1, at, part],
                        (here.dp, peer),
                    )
                )
        return made

    far = Spread(here, False, far_copies)

    fetches = [
        pltpu.make_async_copy(down_hbm, down_ref, fetch_sems.at[0]),
        pltpu.make_async_copy(grad_hbm, grad_ref, fetch_sems.at[1]),
    ]
    pl.loop(0, slots)(lambda slot: fetch(slot).start())
    for one in fetches:
        one.start()
    here.call_all()

    @pl.loop(0, a_ref.shape[0] // block)
    def _(tile):
        some = pl.ds(pl.multiple_of(tile * block, block), block)
        attention_kernel(
            block,
            q_ref.at[some],
            k_ref,
            v_ref,
            open_ref.at[some],
            attended_ref.at[some],
            lse_ref.at[some],
            tile,
        )
        a_ref[some, :] = attended_ref[some, :].astype(BF16)

        @pl.when(tile == 0)
        def _():
            here.await_all()
            far.start()

            @pl.loop(0, slots)
            def _(slot):
                fetch(slot).wait()
                swap(slot, True).start()

    def between():
        far.finish()
        pl.loop(0, slots)(lambda slot: swap(slot, False).start())

    scatter_rows_of_products(
        here,
        [(False, a_ref, b_ref, middle_ref)],
        *scratch[:SCATTER_SCRATCH],
        between=between,
    )
    half = buf.shape[2]
    for part in range(2):

        @pl.loop(0, half // ROW_CHUNK)
        def _(i, part=part):
            into = pl.ds(pl.multiple_of(i * ROW_CHUNK, ROW_CHUNK), ROW_CHUNK)
            some = pl.ds(pl.multiple_of(part * half + i * ROW_CHUNK, ROW_CHUNK), ROW_CHUNK)
            middle = tokens_ref[some, :].astype(F32) + middle_ref[some, :]
            middle_ref[some, :] = middle
            buf[here.mine, part, into, :] = (middle * norm_factor(middle)).astype(BF16)

    def started():
        @pl.loop(0, slots)
        def _(slot):
            swap(slot, True).wait()
            swap(slot, False).wait()

        for one in fetches:
            one.wait()

    store = UnitStore(buf, normed_ref, store_sems)
    share = width // (2 * here.length)

    def outs(number, first):
        where = unit_rows(first, rows)
        some = pl.ds(pl.multiple_of(number * share, share), share)
        return [
            pltpu.make_async_copy(src, dst, out_sems.at[number, i])
            for i, (src, dst) in enumerate(
                [
                    (hidden_ref.at[where], hidden_out_ref.at[where]),
                    (back_ref.at[where], back_out_ref.at[where]),
                    (turned_ref.at[:, some], turned_out_ref.at[:, some]),
                ]
            )
        ]

    def compute(number, first):
        store.start(number, first)
        where = unit_rows(first, rows)
        normed = take_unit(buf, first)
        grad = grad_ref[where, :]

        @pl.loop(0, hidden // tile)
        def _(t):
            cols = pl.ds(pl.multiple_of(t * tile, tile), tile)
            later = pl.ds(pl.multiple_of(hidden + t * tile, tile), tile)
            gate = dot(normed, feed_ref[:, :, :, cols].reshape(width, tile))
            upward = dot(normed, feed_ref[:, :, :, later].reshape(width, tile))
            hidden_grad = dot_t(grad, down_ref[cols, :])
            sigmoid = jax.nn.sigmoid(gate)
            silu = gate * sigmoid
            hidden_ref[where, cols] = (silu * upward).astype(BF16)
            back_ref[where, cols] = (
                hidden_grad * upward * sigmoid * (1.0 + gate * (1.0 - sigmoid))
            ).astype(BF16)
            back_ref[where, later] = (hidden_grad * silu).astype(BF16)

        slabs = share // slab
        begin = number * slabs
        some = pl.ds(pl.multiple_of(number * share, share), share)
        weights = feed_ref[lax.div(begin, here.count), pl.ds(lax.rem(begin, here.count), slabs)]
        turned_ref[:, some] = weights.reshape(share, 2 * hidden).T
        for one in outs(number, first):
            one.start()

    gather_units(here, buf, send_sems, recv_sems, compute, started=started)

    @pl.loop(0, here.count // 2)
    def _(number):
        for one in outs(number, 0):
            one.wait()

    store.finish()


def feed_both_ways(
    queries, keys, values, opening, output, tokens, gate, up, near, grad_out, down, block, call_id
):
    seq = lax.axis_size("seq")
    rows, width = tokens.shape
    cols = queries.shape[1]
    hidden = down.shape[0]
    all_rows = seq * rows
    bf16 = lambda *shape: jax.ShapeDtypeStruct(shape, BF16)
    f32 = lambda *shape: jax.ShapeDtypeStruct(shape, F32)
    dma = pltpu.SemaphoreType.DMA
    return pl.pallas_call(
        functools.partial(feed_kernel, block),
        out_shape=[
            f32(all_rows, cols),
            f32(all_rows, cols // HEAD_DIM),
            bf16(all_rows, cols),
            f32(rows, width),
            bf16(all_rows, width),
            bf16(all_rows, hidden),
            bf16(all_rows, 2 * hidden),
            bf16(2 * hidden, width),
        ],
        in_specs=[VMEM] * 6 + [HBM] * 5,
        out_specs=[VMEM] * 4 + [HBM] * 4,
        scratch_shapes=scatter_scratch(seq, rows, width)
        + [
            pltpu.VMEM((2, seq, *near.shape[1:]), BF16),
            dma((2, 2, seq // 2)),
            dma((seq // 2,)),
            dma((2, seq // 2, 4)),
        ]
        + gather_scratch(seq, rows // 2, width)
        + [
            dma((seq // 2, 2, 2)),
            pltpu.VMEM((all_rows, width), BF16),
            pltpu.VMEM((hidden, width), BF16),
            pltpu.VMEM((all_rows, hidden), BF16),
            pltpu.VMEM((all_rows, 2 * hidden), BF16),
            pltpu.VMEM((2 * hidden, width), BF16),
            dma((2,)),
            dma((seq // 2, 3)),
        ],
        compiler_params=params(call_id, 62),
        cost_estimate=cost(8 * all_rows * width * hidden, 8 * all_rows * width),
    )(queries, keys, values, opening, output, tokens, gate, up, near, grad_out, down)


def back_kernel(
    own_ref,
    weight_ref,
    attended_ref,
    hidden_hbm,
    out_grad_hbm,
    blocks_ref,
    grad_ref,
    output_kept_ref,
    output_away_ref,
    down_kept_ref,
    down_away_ref,
    near_ref,
    buf,
    send_sems,
    recv_sems,
    near_sems,
    own_sem,
    part,
    hidden_ref,
    out_grad_ref,
    fetch_sems,
):
    here = Place()
    fetches = [
        pltpu.make_async_copy(hidden_hbm, hidden_ref, fetch_sems.at[0]),
        pltpu.make_async_copy(out_grad_hbm, out_grad_ref, fetch_sems.at[1]),
    ]
    for one in fetches:
        one.start()
    put_own(here, own_ref, buf)
    here.greet_all()
    rows = own_ref.shape[0]
    width = own_ref.shape[1]
    tile = 512
    near = block_spread(here, True, blocks_ref, near_ref, near_sems)
    own = pltpu.make_async_copy(blocks_ref.at[here.mine], near_ref.at[here.slot], own_sem.at[0])

    own.start()

    def between(step):
        near.start_some(step - here.length, 2)

    part[...] = jnp.zeros_like(part)
    share = width // (2 * here.length)

    def split(values, kept_ref, away_ref, cols):
        half = values.shape[0] // 2
        top, bottom = values[:half], values[half:]
        kept_ref[:, cols] = jnp.where(here.dp == 0, top, bottom)
        away_ref[:, cols] = jnp.where(here.dp == 0, bottom, top).astype(BF16)

    def compute(number, first):
        where = unit_rows(first, rows)
        unit = take_unit(buf, first)
        grad_ref[where, :] = dot_t(unit, weight_ref[...]).astype(BF16)
        attended = attended_ref[where, :]
        for t in range(width // tile):
            cols = slice(t * tile, (t + 1) * tile)
            part[:, cols] += t_dot(attended, unit[:, cols])
        some = pl.ds(pl.multiple_of(number * share, share), share)

        @pl.when(number == 0)
        def _():
            for one in fetches:
                one.wait()

        split(t_dot(hidden_ref[...], out_grad_ref[:, some]), down_kept_ref, down_away_ref, some)

    gather_units(here, buf, send_sems, recv_sems, compute, between)
    for t in range(width // tile):
        cols = slice(t * tile, (t + 1) * tile)
        split(part[:, cols], output_kept_ref, output_away_ref, cols)
    near.finish()
    own.wait()


def gather_back(own, weight, attended, hidden, grad_out, blocks, call_id):
    seq = lax.axis_size("seq")
    rows, width = own.shape
    cols = weight.shape[0]
    return pl.pallas_call(
        back_kernel,
        out_shape=[
            jax.ShapeDtypeStruct((seq * rows, cols), BF16),
            jax.ShapeDtypeStruct((cols // 2, width), F32),
            jax.ShapeDtypeStruct((cols // 2, width), BF16),
            jax.ShapeDtypeStruct((hidden.shape[1] // 2, width), F32),
            jax.ShapeDtypeStruct((hidden.shape[1] // 2, width), BF16),
            jax.ShapeDtypeStruct((seq // 2, *blocks.shape[1:]), BF16),
        ],
        in_specs=[VMEM] * 3 + [HBM] * 3,
        out_specs=[VMEM] * 5 + [HBM],
        scratch_shapes=gather_scratch(seq, rows // 2, width)
        + [
            pltpu.SemaphoreType.DMA((2, seq // 2)),
            pltpu.SemaphoreType.DMA((1,)),
            pltpu.VMEM((cols, width), F32),
            pltpu.VMEM(hidden.shape, BF16),
            pltpu.VMEM(grad_out.shape, BF16),
            pltpu.SemaphoreType.DMA((2,)),
        ],
        compiler_params=params(call_id, 60),
        cost_estimate=cost(8 * seq * rows * width * cols, 6 * seq * rows * width),
    )(own, weight, attended, hidden, grad_out, blocks)


def attention_back_feed_kernel(
    block,
    q_ref,
    k_ref,
    v_ref,
    g_ref,
    att_ref,
    lse_ref,
    open_ref,
    cos_ref,
    sin_ref,
    blocks_ref,
    down_ref,
    output_ref,
    back_ref,
    feed_ref,
    down_out_ref,
    output_out_ref,
    dq_ref,
    dk_ref,
    dv_ref,
    share_out,
    share_in,
    feed_sems,
    swap_sems,
    share_sems,
):
    here = Place()
    tile = pl.program_id(0)
    cols = q_ref.shape[1]
    feed = block_spread(here, False, blocks_ref, feed_ref, feed_sems)
    swaps = [
        remote(src, dst, swap_sems.at[0, number], swap_sems.at[1, number], here.partner())
        for number, (src, dst) in enumerate(
            [(down_ref, down_out_ref), (output_ref, output_out_ref)]
        )
    ]

    pl.when(tile == 0)(here.call_all)
    attention_back_kernel(
        block, q_ref, k_ref, v_ref, g_ref, att_ref, lse_ref, open_ref, dq_ref, dk_ref, dv_ref
    )

    @pl.when(tile == 0)
    def _():
        here.await_all()
        feed.start()
        for one in swaps:
            one.start()

    where = pl.ds(pl.multiple_of(tile * block, block), block)
    scale = 1.0 / math.sqrt(HEAD_DIM)
    cosine = cos_ref[where, :]
    sine = sin_ref[where, :]
    back_ref[where, :cols] = rotated(dq_ref[...] * scale, cosine, -sine).astype(BF16)

    def share(i):
        rows = pl.ds(pl.multiple_of(i * block, block), block)
        return remote(
            share_out.at[rows],
            share_in.at[rows],
            share_sems.at[0, i],
            share_sems.at[1, i],
            here.sibling(),
        )

    @pl.when(tile == pl.num_programs(0) - 1)
    def _():
        @pl.loop(0, pl.num_programs(0))
        def _(i):
            rows = pl.ds(pl.multiple_of(i * block, block), block)
            away = jnp.where(here.core == 0, dv_ref[rows, :], dk_ref[rows, :])
            share_out[rows, :] = away.astype(BF16)
            share(i).start()

        @pl.loop(0, pl.num_programs(0))
        def _(i):
            rows = pl.ds(pl.multiple_of(i * block, block), block)
            share(i).wait()
            came = share_in[rows, :].astype(F32)
            keys = rotated(dk_ref[rows, :] + came, cos_ref[rows, :], -sin_ref[rows, :])
            back_ref[rows, cols:] = jnp.where(here.core == 0, keys, dv_ref[rows, :] + came).astype(
                BF16
            )

        feed.finish()
        for one in swaps:
            one.wait()


def attention_back_feed(
    queries,
    keys,
    values,
    grads,
    attended,
    log_total,
    opening,
    cosine,
    sine,
    blocks,
    down,
    output,
    block,
    call_id,
):
    seq = lax.axis_size("seq")
    rows, cols = queries.shape
    heads = cols // HEAD_DIM
    tiled = lambda width: pl.BlockSpec((block, width), lambda i: (i, 0))
    whole = pl.BlockSpec((rows, cols), lambda i: (0, 0))
    dma = pltpu.SemaphoreType.DMA
    return pl.pallas_call(
        functools.partial(attention_back_feed_kernel, block),
        grid=(rows // block,),
        in_specs=[tiled(cols), whole, whole, tiled(cols), tiled(cols), tiled(heads), tiled(1)]
        + [whole, whole, HBM, HBM, HBM],
        out_specs=[pl.BlockSpec((rows, 2 * cols), lambda i: (0, 0)), HBM, HBM, HBM],
        out_shape=[
            jax.ShapeDtypeStruct((rows, 2 * cols), BF16),
            jax.ShapeDtypeStruct((seq // 2, *blocks.shape[1:]), BF16),
            jax.ShapeDtypeStruct(down.shape, BF16),
            jax.ShapeDtypeStruct(output.shape, BF16),
        ],
        scratch_shapes=[
            pltpu.VMEM((block, cols), F32),
            pltpu.VMEM((rows, cols), F32),
            pltpu.VMEM((rows, cols), F32),
            pltpu.VMEM((rows, cols), BF16),
            pltpu.VMEM((rows, cols), BF16),
            dma((2, seq // 2)),
            dma((2, 2)),
            dma((2, rows // block)),
        ],
        compiler_params=params(call_id, 60),
        cost_estimate=cost(5 * rows * rows * cols, 20 * rows * cols),
    )(
        queries,
        keys,
        values,
        grads,
        attended,
        log_total,
        opening,
        cosine,
        sine,
        blocks,
        down,
        output,
    )


def scatter_last_kernel(a_ref, b_ref, normed_hbm, out_ref, qkv_ref, *scratch):
    here = Place()
    normed_ref, kept, away, came, sums, near_sems, far_sems, swap_sems, fetch_sems = scratch[
        SCATTER_SCRATCH:
    ]
    fetch = pltpu.make_async_copy(normed_hbm, normed_ref, fetch_sems.at[0])
    fetch.start()
    swap = remote(away, came, swap_sems.at[0], swap_sems.at[1], here.partner())
    near = block_spread(here, True, sums, qkv_ref.at[0], near_sems)
    far = block_spread(here, False, sums, qkv_ref.at[1], far_sems)
    half = away.shape[0]
    chunk = 256

    def part(dp, i):
        first = pl.multiple_of(dp * half + i * chunk, chunk)
        return t_dot(normed_ref[:, pl.ds(first, chunk)], a_ref[...])

    def meanwhile():
        fetch.wait()

        @pl.loop(0, half // chunk)
        def _(i):
            some = pl.ds(pl.multiple_of(i * chunk, chunk), chunk)
            away[some, :] = part(1 - here.dp, i).astype(BF16)

    here.greet_all(meanwhile)
    swap.start()

    def between():
        @pl.loop(0, half // chunk)
        def _(i):
            kept[pl.ds(pl.multiple_of(i * chunk, chunk), chunk), :] = part(here.dp, i)

    begin = 2
    each = 3

    def filler(step):
        @pl.when(step == begin)
        def _():
            swap.wait_recv()
            slab = sums.shape[1]

            @pl.loop(0, here.count)
            def _(i):
                rows = pl.ds(pl.multiple_of(i * slab, slab), slab)
                sums[i] = (kept[rows, :] + came[rows, :].astype(F32)).astype(BF16)

            qkv_ref[0, here.slot] = sums[here.mine]

        @pl.when(step > begin)
        def _():
            @pl.loop(0, each)
            def _(i):
                number = (step - begin - 1) * each + i
                pl.when(number < far.slots)(lambda: far.start_one(number))

                @pl.when((number >= far.slots) & (number < 2 * far.slots - 1))
                def _():
                    near.start_one(number - far.slots + 1)

    scatter_rows_of_products(
        here,
        [(True, a_ref, b_ref, out_ref)],
        *scratch[:SCATTER_SCRATCH],
        between=between,
        filler=filler,
    )
    swap.wait_send()
    near.finish()
    far.finish()


def product_scatter_last(a, b, normed, call_id):
    seq = lax.axis_size("seq")
    rows = a.shape[0] // seq
    width, cols = b.shape
    slab = width // (2 * seq)
    dma = pltpu.SemaphoreType.DMA
    return pl.pallas_call(
        scatter_last_kernel,
        out_shape=[
            jax.ShapeDtypeStruct((rows, width), F32),
            jax.ShapeDtypeStruct((2, seq // 2, slab, cols), BF16),
        ],
        in_specs=[VMEM, VMEM, HBM],
        out_specs=[VMEM, VMEM],
        scratch_shapes=scatter_scratch(seq, rows, width)
        + [
            pltpu.VMEM(normed.shape, BF16),
            pltpu.VMEM((width // 2, cols), F32),
            pltpu.VMEM((width // 2, cols), BF16),
            pltpu.VMEM((width // 2, cols), BF16),
            pltpu.VMEM((seq, slab, cols), BF16),
            dma((2, seq // 2)),
            dma((2, seq // 2)),
            dma((2,)),
            dma((1,)),
        ],
        compiler_params=params(call_id, 60),
        cost_estimate=scatter_cost(a, width),
    )(a, b, normed)


UNPACK_LINES = 4


def unpack_kernel(
    pair_ref,
    near_gate_ref,
    far_gate_ref,
    near_up_ref,
    far_up_ref,
    gate_ref,
    up_ref,
    qkv_ref,
    query_ref,
    key_ref,
    value_ref,
    gain_one_ref,
    gain_two_ref,
    tokens_ref,
    middle_ref,
    mixed_sum_ref,
    middle_grad_ref,
    upstream_ref,
    down_kept_ref,
    down_came_ref,
    output_kept_ref,
    output_came_ref,
    gate_out_ref,
    up_out_ref,
    query_out_ref,
    key_out_ref,
    value_out_ref,
    one_out_ref,
    two_out_ref,
    mixed_ref,
    token_grad_ref,
    down_out_ref,
    output_out_ref,
    total_two,
):
    pair = pair_ref[0]
    dp = lax.axis_size("dp")
    length = qkv_ref.shape[1] // 2
    slab = qkv_ref.shape[2]
    step = pl.program_id(0) * pl.num_programs(1) + pl.program_id(1)
    columns = near_gate_ref.shape[2]

    def along(grad, weight):
        return jnp.sum(grad * weight.astype(F32), axis=1, keepdims=True)

    @pl.when(step == 0)
    def _():
        total_two[...] = jnp.zeros_like(total_two)
        total = jnp.zeros((slab, 1), F32)
        gain = upright(gain_one_ref[...])

        def put(out_ref, weight_ref, begin, grad):
            cols = slice(begin, begin + grad.shape[1])
            out_ref[:, cols] = grad * gain
            return along(grad, weight_ref[:, cols])

        pairs = [{}, {}]
        for line in range(length):
            rows = []
            for number in range(4):
                slot = line * 2 + number % 2
                near, far = qkv_ref[0, slot].astype(F32), qkv_ref[1, slot].astype(F32)
                rows.append(jnp.where(number // 2 == pair, near, far))
            kv = [rows[core] + rows[core + 2] for core in range(2)]
            for half in range(dp):
                cols = slice(half * HEAD_DIM, (half + 1) * HEAD_DIM)
                for number in (0, 2):
                    two = jnp.concatenate([rows[number][:, cols], rows[number + 1][:, cols]], axis=1)
                    begin = (half * length * 4 + line * 4 + number) * HEAD_DIM
                    total = total + put(query_out_ref, query_ref, begin, two)
                for kind in range(2):
                    begin = (dp + half) * HEAD_DIM
                    pairs[kind][half, line] = kv[kind][:, begin : begin + HEAD_DIM]
        for kind, (out_ref, weight_ref) in enumerate(
            [(key_out_ref, key_ref), (value_out_ref, value_ref)]
        ):
            for half in range(dp):
                for line in range(0, length, 2):
                    two = [pairs[kind][half, line], pairs[kind][half, line + 1]]
                    begin = (half * length + line) * HEAD_DIM
                    total = total + put(
                        out_ref, weight_ref, begin, jnp.concatenate(two, axis=1)
                    )
        one_out_ref[...] = flat(total)

    mixed_ref[...] = middle_ref[...] + mixed_sum_ref[...]
    token_grad_ref[...] = middle_grad_ref[...] + norm_input_grad(
        tokens_ref[...].astype(F32), upstream_ref[...]
    )
    down_out_ref[...] = down_kept_ref[...] + down_came_ref[...].astype(F32)
    output_out_ref[...] = output_kept_ref[...] + output_came_ref[...].astype(F32)
    gain_two = upright(gain_two_ref[...])
    total = jnp.zeros((slab, 1), F32)
    for near_ref, far_ref, weight_ref, out_ref in (
        (near_gate_ref, far_gate_ref, gate_ref, gate_out_ref),
        (near_up_ref, far_up_ref, up_ref, up_out_ref),
    ):
        for number in range(2 * near_ref.shape[0]):
            slot = number // 4 * 2 + number % 2
            near, far = near_ref[slot].astype(F32), far_ref[slot].astype(F32)
            grad = jnp.where(number // 2 % 2 == pair, near, far)
            cols = slice(number * columns, (number + 1) * columns)
            total = total + along(grad, weight_ref[:, cols])
            out_ref[:, cols] = grad * gain_two
    total_two[...] += total

    @pl.when(step == pl.num_programs(0) * pl.num_programs(1) - 1)
    def _():
        two_out_ref[...] = flat(total_two[...])


def unpack(pair, near, far, gate, up, qkv, query, key, value, gain_one, gain_two, *rows):
    dp = lax.axis_size("dp")
    seq = lax.axis_size("seq")
    slab, ff = gate.shape
    length = seq // 4 // UNPACK_LINES
    columns = ff // (dp * seq)
    whole = lambda array: pl.BlockSpec(array.shape, lambda j, i: (0,) * array.ndim)
    block = lambda kind: pl.BlockSpec(
        (2 * UNPACK_LINES, slab, columns), lambda j, i: (i, 0, kind * dp + j)
    )
    tile = pl.BlockSpec((slab, 4 * UNPACK_LINES * columns), lambda j, i: (0, j * length + i))
    f32 = lambda array: jax.ShapeDtypeStruct(array.shape, F32)
    outs = [f32(gate), f32(up), f32(query), f32(key), f32(value), f32(gain_one), f32(gain_two)]
    sums = [f32(rows[0]), f32(rows[0]), f32(rows[5]), f32(rows[7])]
    steps = dp * length
    strip = lambda array: pl.BlockSpec(
        (array.shape[0] // steps, array.shape[1]), lambda j, i: (j * length + i, 0)
    )
    return pl.pallas_call(
        unpack_kernel,
        grid=(dp, length),
        in_specs=[pl.BlockSpec(memory_space=pltpu.SMEM)]
        + [block(0), block(0), block(1), block(1), tile, tile]
        + [whole(array) for array in (qkv, query, key, value, gain_one, gain_two)]
        + [strip(array) for array in rows],
        out_specs=[tile, tile]
        + [whole(array) for array in outs[2:]]
        + [strip(array) for array in sums],
        out_shape=outs + sums,
        scratch_shapes=[pltpu.VMEM((slab, 1), F32)],
        compiler_params=pltpu.CompilerParams(vmem_limit_bytes=60 << 20),
        cost_estimate=cost(slab * ff, 16 * slab * ff),
    )(
        pair,
        near,
        far,
        near,
        far,
        gate,
        up,
        qkv,
        query,
        key,
        value,
        gain_one,
        gain_two,
        *rows,
    )


def swap_dp(values):
    count = lax.axis_size("dp")
    return lax.ppermute(values, "dp", [(i, (i + 1) % count) for i in range(count)])


def gather_dp(values):
    return lax.all_gather(values, "dp", axis=0, tiled=True)


def sum_dp(partial):
    half = partial.shape[0] // 2
    mine = lax.axis_index("dp")
    away = lax.dynamic_slice_in_dim(partial, (1 - mine) * half, half, 0).astype(BF16)
    kept = lax.dynamic_slice_in_dim(partial, mine * half, half, 0)
    return kept + swap_dp(away).astype(F32)


def gather_rows(values):
    return lax.all_gather(values, "seq", axis=0, tiled=True)


def scatter_rows(partial):
    return lax.psum_scatter(partial.astype(BF16), "seq", scatter_dimension=0, tiled=True).astype(F32)


def exchange(blocks):
    return lax.all_to_all(blocks, "seq", split_axis=0, concat_axis=0, tiled=True)


def norm_factor(values):
    return lax.rsqrt(jnp.mean(values * values, axis=-1, keepdims=True) + EPS)


def norm_back(inputs, factor, gain_row, upstream):
    scaled_up = gain_row * upstream
    inner_mean = jnp.mean(scaled_up * inputs, axis=-1, keepdims=True)
    grad_in = factor * scaled_up - inputs * factor * factor * factor * inner_mean
    grad_gain = jnp.sum(upstream * inputs * factor, axis=0)
    return grad_in, grad_gain


def plain_shards(
    tokens,
    cotangent,
    doc_lengths,
    attn_gain,
    mlp_gain,
    query_weight,
    key_weight,
    value_weight,
    output_weight,
    gate_weight,
    up_weight,
    down_weight,
):
    dp = lax.axis_size("dp")
    seq = lax.axis_size("seq")
    mine = lax.axis_index("seq")
    tok_count, width = tokens.shape
    rows = tok_count * seq
    slab = query_weight.shape[0]
    share = HEAD_DIM // slab
    half_heads = HEADS // dp
    half_kv = KV_HEADS // dp
    hidden_dev = down_weight.shape[0]
    block = 512

    doc_ends = jnp.cumsum(doc_lengths[0])
    place = jnp.arange(rows, dtype=jnp.int32)
    passed = doc_ends[None, :] <= place[:, None]
    opening = jnp.max(jnp.where(passed, doc_ends[None, :], 0), axis=1)
    position = place - opening
    keeping = place < doc_ends[DOCS - 1]
    angles = position.astype(F32)[:, None] * rotary_table(HEAD_DIM)[None, :]
    cosine = jnp.cos(angles)
    sine = jnp.sin(angles)
    cos_heads = jnp.tile(cosine, (1, 2 * dp))
    sin_heads = jnp.tile(jnp.concatenate([-sine, sine], axis=1), (1, dp))
    own_keeping = lax.dynamic_slice_in_dim(keeping, mine * tok_count, tok_count, 0)

    def head_columns(weight, kept):
        split = weight.reshape(slab, dp, kept, HEAD_DIM)
        return jnp.repeat(split, seq // kept, axis=2)

    qkv_blocks = jnp.stack(
        [
            head_columns(query_weight, half_heads),
            head_columns(key_weight, half_kv),
            head_columns(value_weight, half_kv),
        ],
        axis=1,
    )
    qkv_blocks = jnp.transpose(qkv_blocks, (3, 0, 1, 2, 4)).reshape(seq * slab, 3 * dp * HEAD_DIM)
    qkv_weight = gather_dp(exchange(qkv_blocks))
    feed_blocks = jnp.stack(
        [w.reshape(slab, dp, seq, hidden_dev) for w in (gate_weight, up_weight)], axis=1
    )
    feed_blocks = jnp.transpose(feed_blocks, (3, 0, 1, 2, 4)).reshape(
        seq * slab, 2 * dp * hidden_dev
    )
    feed_weight = gather_dp(exchange(feed_blocks))
    down_own = gather_dp(down_weight)
    output_own = output_weight
    if share > 1:
        groups = [list(range(i, i + share)) for i in range(0, seq, share)]
        output_own = lax.all_gather(
            output_own, "seq", axis=0, tiled=True, axis_index_groups=groups
        )
    output_own = gather_dp(output_own)
    gains = lax.all_gather(
        jnp.stack([attn_gain, mlp_gain]), ("dp", "seq"), axis=1, tiled=True
    ).astype(F32)
    gain_one, gain_two = gains[0], gains[1]

    inputs_all = gather_rows(tokens).astype(F32)
    normed_one = (inputs_all * norm_factor(inputs_all) * gain_one).astype(BF16)
    qkv = dot(normed_one, qkv_weight)
    head_cols = dp * HEAD_DIM
    query_lin, key_lin = qkv[:, :head_cols], qkv[:, head_cols : 2 * head_cols]
    values = qkv[:, 2 * head_cols :].astype(BF16)
    scale = 1.0 / math.sqrt(HEAD_DIM)
    queries = (query_lin * cos_heads + swap_halves(query_lin) * sin_heads).astype(BF16) * BF16(scale)
    keys = (key_lin * cos_heads + swap_halves(key_lin) * sin_heads).astype(BF16)
    attended_sum, log_total = attention(queries, keys, values, opening[:, None], block)
    if share > 1:
        own_rows = ((place // tok_count) % share == mine % share)[:, None]
        attended_sum = jnp.where(own_rows, attended_sum, 0.0)
    attended = attended_sum.astype(BF16)
    inputs = tokens.astype(F32)
    middle = inputs + scatter_rows(dot(attended, output_own))

    factor_two = norm_factor(middle)
    normed_two = gather_rows((middle * factor_two * gain_two).astype(BF16))
    grad_own = jnp.where(own_keeping[:, None], cotangent, BF16(0))
    grad_out = gather_rows(grad_own)
    feed = dot(normed_two, feed_weight)
    feed_cols = dp * hidden_dev
    gate_lin, upward = feed[:, :feed_cols], feed[:, feed_cols:]
    sigmoid = jax.nn.sigmoid(gate_lin)
    hidden = (gate_lin * sigmoid * upward).astype(BF16)
    hidden_grad = dot_t(grad_out, down_own)
    gate_back = (hidden_grad * upward * sigmoid * (1.0 + gate_lin * (1.0 - sigmoid))).astype(BF16)
    up_back = (hidden_grad * gate_lin * sigmoid).astype(BF16)
    feed_back = jnp.concatenate([gate_back, up_back], axis=1)
    normed_two_grad = scatter_rows(dot_t(feed_back, feed_weight))
    mixed = middle + scatter_rows(dot(hidden, down_own))
    middle_in, gain_two_part = norm_back(middle, factor_two, gain_two, normed_two_grad)
    middle_grad = grad_own.astype(F32) + middle_in
    middle_back = gather_rows(middle_grad.astype(BF16))

    attended_grad = dot_t(middle_back, output_own).astype(BF16)
    if share > 1:
        attended_grad = jnp.where(own_rows, attended_grad, BF16(0))
    query_acc, key_acc, value_acc = attention_back(
        queries, keys, values, attended_grad, attended_sum, log_total, opening[:, None], block
    )
    query_acc = query_acc * scale
    query_back = query_acc * cos_heads - swap_halves(query_acc) * sin_heads
    key_back = key_acc * cos_heads - swap_halves(key_acc) * sin_heads
    qkv_back = jnp.concatenate([query_back, key_back, value_acc], axis=1).astype(BF16)
    normed_one_grad = scatter_rows(dot_t(qkv_back, qkv_weight))
    input_in, gain_one_part = norm_back(inputs, norm_factor(inputs), gain_one, normed_one_grad)
    token_grad = middle_grad + input_in

    feed_grad = exchange(sum_dp(t_dot(normed_two, feed_back)).astype(BF16)).astype(F32)
    feed_grad = feed_grad.reshape(seq, slab, 2, dp, hidden_dev)
    feed_grad = jnp.transpose(feed_grad, (2, 1, 3, 0, 4)).reshape(2, slab, dp * seq * hidden_dev)
    down_grad = sum_dp(t_dot(hidden, grad_out))
    output_part = t_dot(attended, middle_back)
    if share > 1:
        split = output_part.reshape(dp, share, slab, width)
        split = jnp.transpose(split, (1, 0, 2, 3)).reshape(share * dp * slab, width)
        output_part = lax.psum_scatter(
            split, "seq", scatter_dimension=0, tiled=True, axis_index_groups=groups
        )
    output_grad = sum_dp(output_part)
    qkv_grad = exchange(sum_dp(t_dot(normed_one, qkv_back)).astype(BF16)).astype(F32)
    qkv_grad = qkv_grad.reshape(seq, slab, 3, dp, HEAD_DIM)

    def own_columns(part, kept):
        summed = jnp.sum(part.reshape(kept, seq // kept, slab, dp, HEAD_DIM), axis=1)
        return jnp.transpose(summed, (1, 2, 0, 3)).reshape(slab, dp * kept * HEAD_DIM)

    query_grad = own_columns(qkv_grad[:, :, 0], half_heads)
    key_grad = own_columns(qkv_grad[:, :, 1], half_kv)
    value_grad = own_columns(qkv_grad[:, :, 2], half_kv)
    gain_parts = lax.psum(jnp.stack([gain_one_part, gain_two_part]), ("dp", "seq"))
    own = lax.axis_index("dp") * seq + mine
    gain_grads = lax.dynamic_slice_in_dim(gain_parts, own * slab, slab, 1)
    return (
        mixed,
        token_grad,
        gain_grads[0],
        gain_grads[1],
        query_grad,
        key_grad,
        value_grad,
        output_grad,
        feed_grad[0],
        feed_grad[1],
        down_grad,
    )


def frequencies():
    exponent = np.arange(0, HEAD_DIM, 2, dtype=np.float32) / np.float32(HEAD_DIM)
    inverse = np.power(np.float32(500000.0), -exponent)
    wavelength = np.float32(2.0 * math.pi) / inverse
    smooth = (np.float32(8192.0) / wavelength - np.float32(1.0)) / np.float32(3.0)
    blended = (np.float32(1.0) - smooth) * inverse / np.float32(32.0) + smooth * inverse
    scaled = np.where(
        wavelength < 2048.0,
        inverse,
        np.where(wavelength > 8192.0, inverse / np.float32(32.0), blended),
    )
    return np.tile(scaled.astype(np.float32), 4)


FREQUENCIES = frequencies()


def shards(
    tokens,
    cotangent,
    doc_lengths,
    attn_gain,
    mlp_gain,
    query_weight,
    key_weight,
    value_weight,
    output_weight,
    gate_weight,
    up_weight,
    down_weight,
):
    dp = lax.axis_size("dp")
    seq = lax.axis_size("seq")
    mine = lax.axis_index("seq")
    tok_count, width = tokens.shape
    slab = query_weight.shape[0]
    block = 512
    gain_one = attn_gain[None, :]
    gain_two = mlp_gain[None, :]

    (
        normed_one,
        grad_out,
        queries,
        keys,
        values,
        cosine,
        sine,
        opening,
        qkv_weight,
        gate_scaled,
        up_scaled,
        feed_near,
        down_own,
        output_own,
    ) = gather_project(
        doc_lengths,
        tokens,
        cotangent,
        query_weight,
        key_weight,
        value_weight,
        gate_weight,
        up_weight,
        (gain_one, gain_two),
        jnp.asarray(FREQUENCIES)[None, :],
        down_weight,
        output_weight,
        0,
    )
    qkv_weight = qkv_weight.reshape(width, -1)
    down_own = down_own.reshape(-1, width)
    output_own = output_own.reshape(-1, width)
    attended_sum, log_total, attended, middle, normed_two, hidden, feed_back, feed_turned = (
        feed_both_ways(
            queries,
            keys,
            values,
            opening,
            output_own,
            tokens,
            gate_scaled,
            up_scaled,
            feed_near,
            grad_out,
            down_own,
            block,
            1,
        )
    )

    middle_grad, middle_back, mixed_sum, feed_sums = product_scatter_both(
        feed_back, feed_turned, hidden, down_own, middle, grad_out, normed_two, 4
    )
    feed_sums = feed_sums.reshape(seq, slab, -1)
    attended_grad, output_kept, output_away, down_kept, down_away, feed_grad_near = gather_back(
        middle_back, output_own, attended, hidden, grad_out, feed_sums, 5
    )

    qkv_back, feed_grad_far, down_came, output_came = attention_back_feed(
        queries,
        keys,
        values,
        attended_grad,
        attended_sum,
        log_total,
        opening,
        cosine,
        sine,
        feed_sums,
        down_away,
        output_away,
        block,
        6,
    )
    normed_one_grad, qkv_grads = product_scatter_last(qkv_back, qkv_weight, normed_one, 7)

    pair = ((mine // 2) % 2).reshape(1)
    (
        gate_grad,
        up_grad,
        query_grad,
        key_grad,
        value_grad,
        attn_gain_grad,
        mlp_gain_grad,
        mixed,
        token_grad,
        down_grad,
        output_grad,
    ) = unpack(
        pair,
        feed_grad_near,
        feed_grad_far,
        gate_weight,
        up_weight,
        qkv_grads,
        query_weight,
        key_weight,
        value_weight,
        gain_one,
        gain_two,
        tokens,
        middle,
        mixed_sum,
        middle_grad,
        normed_one_grad,
        down_kept,
        down_came,
        output_kept,
        output_came,
    )
    return (
        mixed,
        token_grad,
        attn_gain_grad[0],
        mlp_gain_grad[0],
        query_grad,
        key_grad,
        value_grad,
        output_grad,
        gate_grad,
        up_grad,
        down_grad,
    )


def solution(mesh):
    both = P(("dp", "seq"), None)
    line = P(("dp", "seq"))
    dp, seq = mesh.shape["dp"], mesh.shape["seq"]

    def run(*args):
        tokens = args[0].shape[0]
        width = args[0].shape[1]
        suits = dp == 2 and seq % 4 == 0 and width == dp * seq * HEAD_DIM
        suits = suits and 2 * (tokens // dp) * width <= 16 << 20
        return jax.shard_map(
            shards if suits else plain_shards,
            mesh=mesh,
            in_specs=(both, both, P("dp", None), line, line) + (both,) * 7,
            out_specs=(both, both, line, line) + (both,) * 7,
            check_vma=False,
        )(*args)

    return run
```

```python
import functools
import math

import jax
import jax.numpy as jnp
import numpy as np
from jax import lax
from jax.experimental import pallas as pl
from jax.experimental.pallas import tpu as pltpu
from jax.sharding import PartitionSpec as P

HEADS = 32
KV_HEADS = 8
HEAD_DIM = 64
DOCS = 4
EPS = 1e-05
NEG = -1e30
MESH = pl.DeviceIdType.MESH
F32 = jnp.float32
BF16 = jnp.bfloat16


def rotary_table(head_dim):
    exponent = jnp.arange(0, head_dim, 2, dtype=F32) / head_dim
    inverse = jnp.power(F32(500000.0), -exponent)
    wavelength = 2.0 * math.pi / inverse
    smooth = (8192.0 / wavelength - 1.0) / 3.0
    blended = (1.0 - smooth) * inverse / 32.0 + smooth * inverse
    return jnp.where(
        wavelength < 2048.0, inverse, jnp.where(wavelength > 8192.0, inverse / 32.0, blended)
    )


def swap_halves(values):
    rows, cols = values.shape
    halves = values.reshape(rows, cols // HEAD_DIM, 2, HEAD_DIM // 2)
    return halves[:, :, ::-1].reshape(rows, cols)


def dot(a, b):
    return jnp.dot(a, b, preferred_element_type=F32)


def dot_t(a, b):
    return lax.dot_general(a, b, (((1,), (1,)), ((), ())), preferred_element_type=F32)


def t_dot(a, b):
    return lax.dot_general(a, b, (((0,), (0,)), ((), ())), preferred_element_type=F32)


def allowed_tile(opening, q_first, k_first, shape):
    rows = q_first + lax.broadcasted_iota(jnp.int32, shape, 0)
    cols = k_first + lax.broadcasted_iota(jnp.int32, shape, 1)
    return (cols <= rows) & (cols >= opening)


def attention_kernel(block, q_ref, k_ref, v_ref, open_ref, out_ref, lse_ref, tile=None):
    if tile is None:
        tile = pl.program_id(0)
    opening = open_ref[...]
    heads = [
        slice(i * HEAD_DIM, (i + 1) * HEAD_DIM) for i in range(q_ref.shape[1] // HEAD_DIM)
    ]

    def step(j, carry):
        first = pl.multiple_of(j * block, block)
        allowed = allowed_tile(opening, tile * block, first, (block, block))
        after = []
        for lanes, (peak, total, acc) in zip(heads, carry):
            scores = dot_t(q_ref[:, lanes], k_ref[pl.ds(first, block), lanes])
            scores = jnp.where(allowed, scores, NEG)
            new_peak = jnp.maximum(peak, jnp.max(scores, axis=1, keepdims=True))
            spread = jnp.exp(scores - new_peak)
            fade = jnp.exp(peak - new_peak)
            total = total * fade + jnp.sum(spread, axis=1, keepdims=True)
            acc = acc * fade + dot(spread.astype(BF16), v_ref[pl.ds(first, block), lanes])
            after.append((new_peak, total, acc))
        return tuple(after)

    start = (
        jnp.full((block, 1), NEG, F32),
        jnp.zeros((block, 1), F32),
        jnp.zeros((block, HEAD_DIM), F32),
    )
    done = lax.fori_loop(0, tile + 1, step, (start,) * len(heads))
    for head, (lanes, (peak, total, acc)) in enumerate(zip(heads, done)):
        out_ref[:, lanes] = acc / total
        lse_ref[:, head : head + 1] = peak + jnp.log(total)


def attention(queries, keys, values, opening, block):
    rows, cols = queries.shape
    heads = cols // HEAD_DIM
    tiled = lambda width: pl.BlockSpec((block, width), lambda i: (i, 0))
    whole = pl.BlockSpec((rows, cols), lambda i: (0, 0))
    return pl.pallas_call(
        functools.partial(attention_kernel, block),
        grid=(rows // block,),
        in_specs=[tiled(cols), whole, whole, tiled(1)],
        out_specs=[tiled(cols), tiled(heads)],
        out_shape=[
            jax.ShapeDtypeStruct((rows, cols), F32),
            jax.ShapeDtypeStruct((rows, heads), F32),
        ],
        compiler_params=pltpu.CompilerParams(vmem_limit_bytes=48 << 20),
        cost_estimate=pl.CostEstimate(
            flops=2 * rows * rows * cols, bytes_accessed=10 * rows * cols, transcendentals=0
        ),
    )(queries, keys, values, opening)


def attention_back_kernel(
    block,
    q_ref,
    k_ref,
    v_ref,
    g_ref,
    att_ref,
    lse_ref,
    open_ref,
    dq_ref,
    dk_ref,
    dv_ref,
    tile=None,
):
    if tile is None:
        tile = pl.program_id(0)

    @pl.when(tile == 0)
    def _():
        dk_ref[...] = jnp.zeros_like(dk_ref)
        dv_ref[...] = jnp.zeros_like(dv_ref)

    opening = open_ref[...]
    heads = []
    for head in range(q_ref.shape[1] // HEAD_DIM):
        lanes = slice(head * HEAD_DIM, (head + 1) * HEAD_DIM)
        grad = g_ref[:, lanes].astype(F32)
        row_sum = jnp.sum(grad * att_ref[:, lanes], axis=1, keepdims=True)
        heads.append((lanes, lse_ref[:, head : head + 1], row_sum))

    def step(j, carry):
        first = pl.multiple_of(j * block, block)
        here = pl.ds(first, block)
        allowed = allowed_tile(opening, tile * block, first, (block, block))
        after = []
        for (lanes, log_total, row_sum), acc in zip(heads, carry):
            query, grad, key = q_ref[:, lanes], g_ref[:, lanes], k_ref[here, lanes]
            scores = dot_t(query, key)
            chance = jnp.where(allowed, jnp.exp(scores - log_total), 0.0)
            prob_grad = dot_t(grad, v_ref[here, lanes])
            score_grad = (chance * (prob_grad - row_sum)).astype(BF16)
            dk_ref[here, lanes] += t_dot(score_grad, query)
            dv_ref[here, lanes] += t_dot(chance.astype(BF16), grad)
            after.append(acc + dot(score_grad, key))
        return tuple(after)

    start = jnp.zeros((block, HEAD_DIM), F32)
    done = lax.fori_loop(0, tile + 1, step, (start,) * len(heads))
    for (lanes, _, _), acc in zip(heads, done):
        dq_ref[:, lanes] = acc


def attention_back(queries, keys, values, grads, attended, log_total, opening, block):
    rows, cols = queries.shape
    heads = cols // HEAD_DIM
    tiled = lambda width: pl.BlockSpec((block, width), lambda i: (i, 0))
    whole = pl.BlockSpec((rows, cols), lambda i: (0, 0))
    return pl.pallas_call(
        functools.partial(attention_back_kernel, block),
        grid=(rows // block,),
        in_specs=[tiled(cols), whole, whole, tiled(cols), tiled(cols), tiled(heads), tiled(1)],
        out_specs=[tiled(cols), whole, whole],
        out_shape=[jax.ShapeDtypeStruct((rows, cols), F32)] * 3,
        compiler_params=pltpu.CompilerParams(vmem_limit_bytes=60 << 20),
        cost_estimate=pl.CostEstimate(
            flops=5 * rows * rows * cols, bytes_accessed=20 * rows * cols, transcendentals=0
        ),
    )(queries, keys, values, grads, attended, log_total, opening)


def nothing():
    pass


class Place:
    def __init__(self):
        self.dp = lax.axis_index("dp")
        self.mine = lax.axis_index("seq")
        self.count = lax.axis_size("seq")
        self.length = self.count // 4
        self.line = lax.div(self.mine, 4)
        self.pair = lax.rem(lax.div(self.mine, 2), 2)
        self.core = lax.rem(self.mine, 2)
        self.slot = self.line * 2 + self.core

    def index(self, line, pair, core):
        return (line * 2 + pair) * 2 + core

    def peer(self, slot, same):
        pair = self.pair if same else 1 - self.pair
        return self.index(lax.div(slot, 2), pair, lax.rem(slot, 2))

    def device(self, line, pair, core):
        return (self.dp, self.index(line, pair, core))

    def sibling(self):
        return self.device(self.line, self.pair, 1 - self.core)

    def across(self):
        return self.device(self.line, 1 - self.pair, self.core)

    def above(self):
        return self.device(self.line + 1, self.pair, self.core)

    def below(self):
        return self.device(self.line - 1, self.pair, self.core)

    def partner(self):
        return (1 - self.dp, self.mine)

    def greet(self, partner=False):
        barrier = pltpu.get_barrier_semaphore()

        def signal(device):
            pl.semaphore_signal(barrier, inc=1, device_id=device, device_id_type=MESH)

        signal(self.sibling())
        signal(self.across())
        pl.when(self.line > 0)(lambda: signal(self.below()))
        pl.when(self.line < self.length - 1)(lambda: signal(self.above()))
        if partner:
            signal(self.partner())
        inner = (self.line > 0) & (self.line < self.length - 1)
        pl.semaphore_wait(barrier, jnp.where(inner, 4, 3) + (1 if partner else 0))

    def greet_all(self, meanwhile=nothing):
        self.call_all()
        meanwhile()
        self.await_all()

    def await_all(self):
        pl.semaphore_wait(pltpu.get_barrier_semaphore(), self.count)

    def call_all(self):
        barrier = pltpu.get_barrier_semaphore()

        def signal(device):
            pl.semaphore_signal(barrier, inc=1, device_id=device, device_id_type=MESH)

        signal(self.partner())

        @pl.loop(1, self.count)
        def _(ahead):
            signal((self.dp, lax.rem(self.mine + ahead, self.count)))


def remote(src, dst, send_sem, recv_sem, device):
    return pltpu.make_async_remote_copy(
        src_ref=src,
        dst_ref=dst,
        send_sem=send_sem,
        recv_sem=recv_sem,
        device_id=device,
        device_id_type=MESH,
    )


class Spread:
    def __init__(self, here, same, copies):
        self.here, self.same, self.copies = here, same, copies
        self.slots = here.count // 2

    def each(self, visit):
        @pl.loop(1 if self.same else 0, self.slots)
        def _(ahead):
            slot = lax.rem(self.here.slot + ahead, self.slots)
            visit(self.here.peer(slot, self.same), slot)

    def start_one(self, ahead):
        slot = lax.rem(self.here.slot + ahead, self.slots)
        peer = self.here.peer(slot, self.same)
        for one in self.copies(peer, self.here.mine, self.here.slot, slot):
            one.start()

    def start(self):
        pl.loop(1 if self.same else 0, self.slots)(self.start_one)

    def start_some(self, number, each):
        first = 1 if self.same else 0

        @pl.loop(0, each)
        def _(i):
            ahead = first + number * each + i
            pl.when((number >= 0) & (ahead < self.slots))(lambda: self.start_one(ahead))

    def finish(self):
        def visit(peer, slot):
            for one in self.copies(peer, peer, slot, slot):
                one.wait()

        self.each(visit)


def block_spread(here, same, blocks, into, sems):
    def copies(peer, sender, at, sem):
        return [
            remote(
                blocks.at[peer],
                into.at[at],
                sems.at[0, sem],
                sems.at[1, at],
                (here.dp, peer),
            )
        ]

    return Spread(here, same, copies)


def feed_spread(here, same, weights, into, sems):
    dp = lax.axis_size("dp")
    columns = into.shape[2] // (dp * len(weights))

    def copies(peer, sender, at, sem):
        made = []
        for kind, weight in enumerate(weights):
            for half in range(dp):
                part = kind * dp + half
                begin = pl.multiple_of((half * here.count + peer) * columns, columns)
                made.append(
                    remote(
                        weight.at[:, pl.ds(begin, columns)],
                        into.at[at, :, pl.ds(part * columns, columns)],
                        sems.at[0, sem, part],
                        sems.at[1, at, part],
                        (here.dp, peer),
                    )
                )
        return made

    return Spread(here, same, copies)


def gather_units(here, buf, send_sems, recv_sems, compute, between=None, ready=None, started=nothing):
    length = here.length
    last = length - 1
    steps = 2 * length
    mine = here.mine
    shorter = jnp.minimum(here.line, last - here.line)
    longer = jnp.where(here.line < last - here.line, 1, -1)

    def column(j):
        i = j - 1
        paired = jnp.where(i % 2 == 0, here.line - i // 2 - 1, here.line + i // 2 + 1)
        single = here.line + longer * (i - shorter + 1)
        return jnp.where(j == 0, here.line, jnp.where(i < 2 * shorter, paired, single))

    def copy(way, device, block, part):
        ref = buf.at[block, part]
        return remote(
            ref, ref, send_sems.at[way, block, part], recv_sems.at[block, part], device
        )

    def up(block, part):
        return copy(0, here.above(), block, part)

    def down(block, part):
        return copy(1, here.below(), block, part)

    def across(block, part):
        return copy(2, here.across(), block, part)

    def sideways(block, part):
        return copy(3, here.sibling(), block, part)

    def unit(number):
        in_column = (number % 2 == 1) & (number < steps - 1) | (number == 0)
        later = jnp.where(number == steps - 1, last, number // 2 - 1)
        line = column(jnp.where(in_column, (number + 1) // 2, later))
        pair = jnp.where(in_column, here.pair, 1 - here.pair)
        other = here.index(line, pair, 1 - here.core)
        sideways(other, 0).wait_recv()
        sideways(other, 1).wait_recv()
        compute(number, here.index(line, pair, 0))

    for part in range(2):
        pl.when(here.line < last)(lambda part=part: up(mine, part).start())
        pl.when(here.line > 0)(lambda part=part: down(mine, part).start())
        across(mine, part).start()
        sideways(mine, part).start()
    started()

    @pl.loop(0, steps)
    def _(step):
        part = step % 2
        far = step // 2 + 1

        @pl.when(here.line >= far)
        def _():
            block = here.index(here.line - far, here.pair, here.core)
            up(block, part).wait_recv()
            pl.when(here.line < last)(lambda: up(block, part).start())
            sideways(block, part).start()

        @pl.when(here.line + far <= last)
        def _():
            block = here.index(here.line + far, here.pair, here.core)
            down(block, part).wait_recv()
            pl.when(here.line > 0)(lambda: down(block, part).start())
            sideways(block, part).start()

        @pl.when(step + 2 < steps)
        def _():
            across(here.index(column(step // 2 + 1), here.pair, here.core), part).start()

        block = here.index(column(step // 2), 1 - here.pair, here.core)
        across(block, part).wait_recv()
        sideways(block, part).start()

        if between is not None:
            between(step)
        if ready is None:
            unit(step)
        else:
            begin = jnp.maximum(2 * (step - ready), 0)
            end = jnp.maximum(2 * (step + 1 - ready), 0)

            @pl.loop(begin, end)
            def _(number):
                unit(number)

    @pl.loop(0, length)
    def _(line):
        for part in range(2):
            block = here.index(line, here.pair, here.core)

            @pl.when((line <= here.line) & (here.line < last))
            def _():
                up(block, part).wait_send()

            @pl.when((line >= here.line) & (here.line > 0))
            def _():
                down(block, part).wait_send()

            across(block, part).wait_send()
            sideways(block, part).wait_send()
            sideways(here.index(line, 1 - here.pair, here.core), part).wait_send()


def put_own(here, own_ref, buf):
    half = buf.shape[2]
    for part in range(2):
        buf[here.mine, part] = own_ref[pl.ds(part * half, half), :]


def gather_scratch(seq, rows, width):
    return [
        pltpu.VMEM((seq, 2, rows, width), BF16),
        pltpu.SemaphoreType.DMA((4, seq, 2)),
        pltpu.SemaphoreType.DMA((seq, 2)),
    ]


def unit_rows(first, rows):
    return pl.ds(pl.multiple_of(first * rows, 2 * rows), 2 * rows)


def take_unit(buf, first):
    blocks = buf[pl.ds(first, 2)]
    return blocks.reshape(-1, blocks.shape[-1])


class UnitStore:
    def __init__(self, buf, out_ref, sems):
        self.buf, self.out_ref, self.sems = buf, out_ref, sems

    def copies(self, number, first):
        half = self.buf.shape[2]
        made = []
        for block in range(2):
            for part in range(2):
                begin = ((first + block) * 2 + part) * half
                made.append(
                    pltpu.make_async_copy(
                        self.buf.at[first + block, part],
                        self.out_ref.at[pl.ds(pl.multiple_of(begin, half), half)],
                        self.sems.at[number, block, part],
                    )
                )
        return made

    def start(self, number, first):
        for one in self.copies(number, first):
            one.start()

    def finish(self):
        @pl.loop(0, self.sems.shape[0])
        def _(number):
            for one in self.copies(number, 0):
                one.wait()


def params(call_id, mebibytes):
    return pltpu.CompilerParams(
        collective_id=call_id, has_side_effects=True, vmem_limit_bytes=mebibytes << 20
    )


def cost(flops, bytes_accessed):
    return pl.CostEstimate(flops=flops, bytes_accessed=bytes_accessed, transcendentals=0)


VMEM = pl.BlockSpec(memory_space=pltpu.VMEM)
HBM = pl.BlockSpec(memory_space=pl.ANY)


def rotated(values, cosine, sine):
    cols = values.shape[1]
    lane = lax.broadcasted_iota(jnp.int32, values.shape, 1)
    ahead = pltpu.roll(values, cols - HEAD_DIM // 2, 1)
    behind = pltpu.roll(values, HEAD_DIM // 2, 1)
    swapped = jnp.where(lane % HEAD_DIM < HEAD_DIM // 2, ahead, behind)
    return values * cosine + swapped * sine


def upright(row):
    count = row.shape[1]
    shape = (count, count)
    same = lax.broadcasted_iota(jnp.int32, shape, 0) == lax.broadcasted_iota(jnp.int32, shape, 1)
    return jnp.sum(jnp.where(same, row.astype(F32), 0.0), axis=1, keepdims=True)


def flat(column):
    count = column.shape[0]
    shape = (count, count)
    same = lax.broadcasted_iota(jnp.int32, shape, 0) == lax.broadcasted_iota(jnp.int32, shape, 1)
    return jnp.sum(jnp.where(same, column, 0.0), axis=0, keepdims=True)


def project_kernel(
    lengths_ref,
    tokens_ref,
    cotangent_ref,
    query_ref,
    key_ref,
    value_ref,
    gate_ref,
    up_ref,
    gain_one_ref,
    gain_two_ref,
    freq_ref,
    down_ref,
    output_ref,
    normed_ref,
    grads_ref,
    q_ref,
    k_ref,
    v_ref,
    cos_ref,
    sin_ref,
    open_ref,
    weight_ref,
    gate_out_ref,
    up_out_ref,
    feed_ref,
    down_out_ref,
    output_out_ref,
    buf,
    send_sems,
    recv_sems,
    blocks,
    store_sems,
    near_sems,
    far_sems,
    feed_sems,
    swap_sems,
    local_sems,
    pair_sems,
    share_sems,
):
    here = Place()
    cols = q_ref.shape[1]
    rows = tokens_ref.shape[0]
    dp = here.dp
    ends = [lengths_ref[0, 0]]
    for j in range(1, DOCS):
        ends.append(ends[-1] + lengths_ref[0, j])

    def own_rows():
        chunk = 32

        @pl.loop(0, rows // chunk)
        def _(i):
            some = pl.ds(pl.multiple_of(i * chunk, chunk), chunk)
            values = tokens_ref[some, :].astype(F32)
            factor = lax.rsqrt(jnp.mean(values * values, axis=1, keepdims=True) + EPS)
            buf[here.mine, 0, some, :] = (values * factor).astype(BF16)
            shape = (chunk, cotangent_ref.shape[1])
            place = here.mine * rows + i * chunk + lax.broadcasted_iota(jnp.int32, shape, 0)
            grads = cotangent_ref[some, :].astype(F32)
            buf[here.mine, 1, some, :] = jnp.where(place < ends[-1], grads, 0.0).astype(BF16)

    def own_blocks():
        gain = upright(gain_one_ref[...])
        query = query_ref[...].astype(F32) * gain
        key = key_ref[...].astype(F32) * gain
        value = value_ref[...].astype(F32) * gain

        def heads(array, number, kept):
            parts = []
            for half in range(2):
                head = half * kept + number * kept // blocks.shape[0]
                parts.append(array[:, head * HEAD_DIM : (head + 1) * HEAD_DIM])
            return jnp.concatenate(parts, axis=1).astype(BF16)

        for number in range(blocks.shape[0]):
            blocks[number, :, :cols] = heads(query, number, HEADS // 2)
            array = value if number % 2 else key
            blocks[number, :, cols:] = heads(array, number, KV_HEADS // 2)

    def own_parts():
        own_blocks()
        own_rows()

    here.greet_all(own_parts)

    def weight_spread(same, sems):
        def copies(peer, sender, at, sem):
            return [
                remote(
                    blocks.at[peer],
                    weight_ref.at[dp, sender],
                    sems.at[0, sem],
                    sems.at[1, at],
                    (dp, peer),
                )
            ]

        return Spread(here, same, copies)

    near = weight_spread(True, near_sems)
    far = weight_spread(False, far_sems)
    swaps = []
    for number, (src, dst) in enumerate([(down_ref, down_out_ref), (output_ref, output_out_ref)]):
        swaps.append(
            remote(src, dst.at[dp], swap_sems.at[0, number], swap_sems.at[1, number], here.partner())
        )
        swaps.append(pltpu.make_async_copy(src, dst.at[dp], local_sems.at[number]))
    feed = feed_spread(here, True, (gate_out_ref, up_out_ref), feed_ref, feed_sems)
    columns = feed_ref.shape[2] // 4
    own_feed = []
    for kind, weight in enumerate((gate_out_ref, up_out_ref)):
        for half in range(2):
            part = kind * 2 + half
            begin = pl.multiple_of((half * here.count + here.mine) * columns, columns)
            own_feed.append(
                pltpu.make_async_copy(
                    weight.at[:, pl.ds(begin, columns)],
                    feed_ref.at[here.slot, :, pl.ds(part * columns, columns)],
                    local_sems.at[2 + part],
                )
            )

    def pair_copy(source, sender):
        return remote(
            weight_ref.at[source, sender],
            weight_ref.at[source, sender],
            pair_sems.at[0, sender],
            pair_sems.at[1, sender],
            here.partner(),
        )

    def own_tables():
        chunk = 128

        @pl.loop(0, open_ref.shape[0] // chunk)
        def _(i):
            some = pl.ds(pl.multiple_of(i * chunk, chunk), chunk)
            place = i * chunk + lax.broadcasted_iota(jnp.int32, (chunk, 1), 0)
            opening = jnp.zeros((chunk, 1), jnp.int32)
            for end in ends:
                opening = jnp.where(place >= end, end, opening)
            open_ref[some, :] = opening
            angles = (place - opening).astype(F32) * freq_ref[...]
            lane = lax.broadcasted_iota(jnp.int32, angles.shape, 1)
            sine = jnp.sin(angles)
            cos_ref[some, :] = jnp.cos(angles)
            sin_ref[some, :] = jnp.where(lane % HEAD_DIM < HEAD_DIM // 2, -sine, sine)

    def started():
        far.start()
        near.start()
        weight_ref[dp, here.mine] = blocks[here.mine]
        for one in swaps:
            one.start()
        chunk = 512

        @pl.loop(0, gate_ref.shape[1] // chunk)
        def _(i):
            some = pl.ds(pl.multiple_of(i * chunk, chunk), chunk)
            gain = upright(gain_two_ref[...])
            gate_out_ref[:, some] = (gate_ref[:, some].astype(F32) * gain).astype(BF16)
            up_out_ref[:, some] = (up_ref[:, some].astype(F32) * gain).astype(BF16)

        for one in own_feed:
            one.start()
        own_tables()

    def between(step):
        feed.start_some(step - (2 * here.length - 3), 3)

        @pl.when(step == 2)
        def _():
            near.finish()
            far.finish()

            @pl.loop(0, here.count)
            def _(sender):
                pair_copy(dp, sender).start()

        @pl.when(step == 4)
        def _():
            @pl.loop(0, here.count)
            def _(sender):
                pair_copy(1 - dp, sender).wait_recv()

    def share_copy(ref, number, where):
        return remote(
            ref.at[where],
            ref.at[where],
            share_sems.at[0, number],
            share_sems.at[1, number],
            here.sibling(),
        )

    def stores(number, first):
        made = []
        for block in range(2):
            where = pl.ds(pl.multiple_of((first + block) * rows, rows), rows)
            for part, out_ref in enumerate((normed_ref, grads_ref)):
                made.append(
                    pltpu.make_async_copy(
                        buf.at[first + block, part],
                        out_ref.at[where],
                        store_sems.at[number, block, part],
                    )
                )
        return made

    def compute(number, first):
        for one in stores(number, first):
            one.start()
        weight = weight_ref[...].reshape(-1, weight_ref.shape[-1])
        unit = buf[pl.ds(first, 2), 0]
        qkv = dot(unit.reshape(-1, unit.shape[-1]), weight)
        where = unit_rows(first, rows)
        cosine = cos_ref[where, :]
        sine = sin_ref[where, :]
        scale = BF16(1.0 / math.sqrt(HEAD_DIM))
        q_ref[where, :] = rotated(qkv[:, :cols], cosine, sine).astype(BF16) * scale
        for core, ref in enumerate((k_ref, v_ref)):

            @pl.when(here.core == core)
            def _():
                mine = qkv[:, cols:]
                ref[where, :] = (mine if core else rotated(mine, cosine, sine)).astype(BF16)
                share_copy(ref, number, where).start()

    gather_units(here, buf, send_sems, recv_sems, compute, between, here.length, started)

    @pl.loop(0, here.count)
    def _(sender):
        pair_copy(dp, sender).wait_send()

    @pl.loop(0, here.count // 2)
    def _(number):
        for one in stores(number, 0):
            one.wait()
        share_copy(k_ref, number, unit_rows(0, rows)).wait()

    feed.finish()
    for one in swaps + own_feed:
        one.wait()


def gather_project(
    lengths, tokens, cotangent, query, key, value, gate, up, gains, freq, down, output, call_id
):
    seq = lax.axis_size("seq")
    rows, width = tokens.shape
    cols = 2 * HEAD_DIM
    slab, ff = gate.shape
    bf16 = lambda *shape: jax.ShapeDtypeStruct(shape, BF16)
    f32 = lambda *shape: jax.ShapeDtypeStruct(shape, F32)
    all_rows = seq * rows
    dma = pltpu.SemaphoreType.DMA
    return pl.pallas_call(
        project_kernel,
        out_shape=[
            bf16(all_rows, width),
            bf16(all_rows, width),
            bf16(all_rows, cols),
            bf16(all_rows, cols),
            bf16(all_rows, cols),
            f32(all_rows, cols),
            f32(all_rows, cols),
            jax.ShapeDtypeStruct((all_rows, 1), jnp.int32),
            bf16(2, seq, slab, 2 * cols),
            bf16(slab, ff),
            bf16(slab, ff),
            bf16(seq // 2, slab, 4 * down.shape[0]),
            bf16(2, *down.shape),
            bf16(2, *output.shape),
        ],
        in_specs=[pl.BlockSpec(memory_space=pltpu.SMEM)] + [VMEM] * 10 + [HBM] * 2,
        out_specs=[HBM] * 2 + [VMEM] * 9 + [HBM] * 3,
        scratch_shapes=gather_scratch(seq, rows, width)
        + [
            pltpu.VMEM((seq, slab, 2 * cols), BF16),
            dma((seq // 2, 2, 2)),
            dma((2, seq // 2)),
            dma((2, seq // 2)),
            dma((2, seq // 2, 4)),
            dma((2, 2)),
            dma((6,)),
            dma((2, seq)),
            dma((2, seq // 2)),
        ],
        compiler_params=params(call_id, 60),
        cost_estimate=cost(2 * all_rows * width * 2 * cols, 8 * all_rows * width),
    )(lengths, tokens, cotangent, query, key, value, gate, up, *gains, freq, down, output)


ROW_CHUNK = 32


def norm_input_grad(values, upstream):
    factor = norm_factor(values)
    inner_mean = jnp.mean(upstream * values, axis=-1, keepdims=True)
    return factor * upstream - values * factor * factor * factor * inner_mean


def in_row_chunks(rows, chunk, visit):
    @pl.loop(0, rows // chunk)
    def _(i):
        visit(pl.ds(pl.multiple_of(i * chunk, chunk), chunk))


SCATTER_PARTS = 2
SCATTER_RING = 4
SCATTER_SCRATCH = 11


def scatter_rows_of_products(
    here,
    products,
    core_out,
    core_in,
    pair_out,
    pair_in,
    line_out,
    line_in,
    held,
    core_sems,
    pair_sems,
    line_sems,
    came_sems,
    first=None,
    between=nothing,
    filler=None,
):
    length = here.length
    parts = SCATTER_PARTS * len(products)
    rows, width = held.shape
    tile = min(width, 512)
    tiles = width // tile
    steps = length * parts

    def target(i):
        ups = length - 1 - here.line
        near = here.line < length // 2
        if_near = jnp.where(i < ups, length - 1 - i, i - ups)
        if_far = jnp.where(i < here.line, i, length - 1 - (i - here.line))
        return jnp.where(i == length - 1, here.line, jnp.where(near, if_near, if_far))

    def product(line, pair, core, part, use):
        first = pl.multiple_of(here.index(line, pair, core) * rows, rows)

        def one(number):
            transposed, a_ref, b_ref, _ = products[number]
            a = a_ref[pl.ds(first, rows), :]
            begin = (part - number * SCATTER_PARTS) * width

            @pl.loop(0, tiles)
            def _(t):
                into = pl.ds(pl.multiple_of(t * tile, tile), tile)
                cols = pl.ds(pl.multiple_of(begin + t * tile, tile), tile)
                use(dot_t(a, b_ref[cols, :]) if transposed else dot(a, b_ref[:, cols]), into)

        for number in range(len(products)):
            pl.when(part // SCATTER_PARTS == number)(functools.partial(one, number))

    def core_copy(slot):
        return remote(
            core_out.at[slot % SCATTER_RING],
            core_in.at[slot],
            core_sems.at[0, slot],
            core_sems.at[1, slot],
            here.sibling(),
        )

    def pair_copy(slot):
        return remote(
            pair_out.at[slot],
            pair_in.at[slot],
            pair_sems.at[0, slot],
            pair_sems.at[1, slot],
            here.across(),
        )

    def up_copy(slot, line, part):
        into = (line + 1) * parts + part
        return remote(
            line_out.at[slot], line_in.at[into], line_sems.at[slot], came_sems.at[into], here.above()
        )

    def down_copy(slot, line, part):
        into = line * parts + part
        return remote(
            line_out.at[slot], line_in.at[into], line_sems.at[slot], came_sems.at[into], here.below()
        )

    def for_sibling(step, pair, slot):
        pl.when(slot >= SCATTER_RING)(lambda: core_copy(slot - SCATTER_RING).wait_send())

        def use(value, cols):
            core_out[slot % SCATTER_RING, :, cols] = value.astype(BF16)

        product(target(step // parts), pair, 1 - here.core, step % parts, use)
        core_copy(slot).start()

    for_sibling(jnp.int32(0), 1 - here.pair, jnp.int32(0))

    @pl.loop(0, steps)
    def _(step):
        if first is not None:
            first(step)
        pl.when(step < steps - 1)(lambda: for_sibling(step + 1, 1 - here.pair, step + 1))
        core_copy(step).wait_recv()

        def use(value, cols):
            pair_out[step, :, cols] = (value + core_in[step, :, cols].astype(F32)).astype(BF16)

        product(target(step // parts), 1 - here.pair, here.core, step % parts, use)
        pair_copy(step).start()

    for_sibling(jnp.int32(0), here.pair, jnp.int32(steps))
    between()

    @pl.loop(0, steps)
    def _(step):
        pl.when(step < steps - 1)(lambda: for_sibling(step + 1, here.pair, steps + step + 1))
        core_copy(steps + step).wait_recv()
        line = target(step // parts)
        part = step % parts

        def use(value, cols):
            held[:, cols] = value + core_in[steps + step, :, cols].astype(F32)

        product(line, here.pair, here.core, part, use)
        if filler is not None:
            filler(step)
        pair_copy(step).wait_recv()
        from_above = (line <= here.line) & (here.line < length - 1)
        from_below = (line >= here.line) & (here.line > 0)
        held[...] += pair_in[step].astype(F32)

        @pl.when(from_above)
        def _():
            down_copy(0, line, part).wait_recv()
            held[...] += line_in[line * parts + part].astype(F32)

        @pl.when(from_below)
        def _():
            up_copy(0, line, part).wait_recv()
            held[...] += line_in[(line + 1) * parts + part].astype(F32)

        for number, (_, _, _, out_ref) in enumerate(products):

            @pl.when((line == here.line) & (part // SCATTER_PARTS == number))
            def _():
                begin = (part - number * SCATTER_PARTS) * width
                out_ref[:, pl.ds(pl.multiple_of(begin, width), width)] = held[...]

        @pl.when(line < here.line)
        def _():
            line_out[step] = held[...].astype(BF16)
            down_copy(step, line, part).start()

        @pl.when(line > here.line)
        def _():
            line_out[step] = held[...].astype(BF16)
            up_copy(step, line, part).start()

    @pl.loop(2 * steps - SCATTER_RING, 2 * steps)
    def _(slot):
        core_copy(slot).wait_send()

    @pl.loop(0, steps)
    def _(step):
        pair_copy(step).wait_send()
        line = target(step // parts)
        pl.when(line < here.line)(lambda: down_copy(step, 0, 0).wait_send())
        pl.when(line > here.line)(lambda: up_copy(step, 0, 0).wait_send())


def scatter_scratch(seq, rows, width, count=1):
    length = seq // 4
    parts = SCATTER_PARTS * count
    steps = length * parts
    block = (rows, width // SCATTER_PARTS)
    dma = pltpu.SemaphoreType.DMA
    return [
        pltpu.VMEM((SCATTER_RING, *block), BF16),
        pltpu.VMEM((2 * steps, *block), BF16),
        pltpu.VMEM((steps, *block), BF16),
        pltpu.VMEM((steps, *block), BF16),
        pltpu.VMEM((steps, *block), BF16),
        pltpu.VMEM(((length + 1) * parts, *block), BF16),
        pltpu.VMEM(block, F32),
        dma((2, 2 * steps)),
        dma((2, steps)),
        dma((steps,)),
        dma(((length + 1) * parts,)),
    ]


def scatter_cost(a, width):
    return cost(2 * a.shape[0] * a.shape[1] * width, 4 * a.shape[0] * width)


def scatter_both_kernel(
    back_hbm,
    turned_hbm,
    hidden_hbm,
    down_hbm,
    middle_ref,
    grads_hbm,
    normed_hbm,
    grad_ref,
    low_ref,
    mixed_ref,
    sums_ref,
    *scratch,
):
    here = Place()
    factors = scratch[SCATTER_SCRATCH : SCATTER_SCRATCH + 4]
    back_ref, turned_ref, hidden_ref, down_ref = factors
    normed, away, came, own, fetch_sems, swap_sems, own_sems = scratch[SCATTER_SCRATCH + 4 :]
    rows = grad_ref.shape[0]
    loads = [
        pltpu.make_async_copy(src, dst, own_sems.at[number])
        for number, (src, dst) in enumerate(
            zip((back_hbm, turned_hbm, hidden_hbm, down_hbm), factors)
        )
    ]
    own_copy = pltpu.make_async_copy(
        grads_hbm.at[pl.ds(pl.multiple_of(here.mine * rows, rows), rows)], own, own_sems.at[4]
    )
    for one in loads + [own_copy]:
        one.start()
    here.greet(partner=True)
    for one in loads[:2]:
        one.wait()

    def first(step):
        @pl.when(step == SCATTER_PARTS - 1)
        def _():
            for one in loads[2:]:
                one.wait()
    chunk = normed.shape[2]
    half = normed_hbm.shape[1] // 2
    chunks = half // chunk

    def fetch(number):
        dp = jnp.where(number < chunks, 1 - here.dp, here.dp)
        begin = dp * half + number % chunks * chunk
        return pltpu.make_async_copy(
            normed_hbm.at[:, pl.ds(pl.multiple_of(begin, chunk), chunk)],
            normed.at[number % 2],
            fetch_sems.at[number % 2],
        )

    def swap(i):
        some = pl.ds(pl.multiple_of(i * chunk, chunk), chunk)
        return remote(
            away.at[some], came.at[some], swap_sems.at[0, i], swap_sems.at[1, i], here.partner()
        )

    def part(number):
        fetch(number).wait()
        pl.when(number + 1 < 2 * chunks)(lambda: fetch(number + 1).start())
        return t_dot(normed[number % 2], back_ref[...])

    def filler(step):
        @pl.when(step < chunks)
        def _():
            some = pl.ds(pl.multiple_of(step * chunk, chunk), chunk)
            away[some, :] = part(step).astype(BF16)
            swap(step).start()

        @pl.when((step >= chunks) & (step < 3 * chunks) & (step % 2 == 0))
        def _():
            i = (step - chunks) // 2
            some = pl.ds(pl.multiple_of(i * chunk, chunk), chunk)
            kept = part(chunks + i)
            swap(i).wait()
            sums_ref[some, :] = (kept + came[some, :].astype(F32)).astype(BF16)

    fetch(jnp.int32(0)).start()
    scatter_rows_of_products(
        here,
        [(False, back_ref, turned_ref, grad_ref), (False, hidden_ref, down_ref, mixed_ref)],
        *scratch[:SCATTER_SCRATCH],
        first=first,
        filler=filler,
    )
    own_copy.wait()

    def add(some):
        grad = own[some, :].astype(F32) + norm_input_grad(middle_ref[some, :], grad_ref[some, :])
        grad_ref[some, :] = grad
        low_ref[some, :] = grad.astype(BF16)

    in_row_chunks(rows, ROW_CHUNK, add)


def product_scatter_both(back, turned, hidden, down, middle, grads, normed, call_id):
    seq = lax.axis_size("seq")
    rows = back.shape[0] // seq
    width = turned.shape[1]
    cols = back.shape[1]
    chunk = width // 8
    dma = pltpu.SemaphoreType.DMA
    return pl.pallas_call(
        scatter_both_kernel,
        out_shape=[
            jax.ShapeDtypeStruct((rows, width), F32),
            jax.ShapeDtypeStruct((rows, width), BF16),
            jax.ShapeDtypeStruct((rows, width), F32),
            jax.ShapeDtypeStruct((width // 2, cols), BF16),
        ],
        in_specs=[HBM] * 4 + [VMEM] + [HBM] * 2,
        out_specs=[VMEM] * 4,
        scratch_shapes=scatter_scratch(seq, rows, width, 2)
        + [pltpu.VMEM(array.shape, BF16) for array in (back, turned, hidden, down)]
        + [
            pltpu.VMEM((2, normed.shape[0], chunk), BF16),
            pltpu.VMEM((width // 2, cols), BF16),
            pltpu.VMEM((width // 2, cols), BF16),
            pltpu.VMEM((rows, width), BF16),
            dma((2,)),
            dma((2, 4)),
            dma((5,)),
        ],
        compiler_params=params(call_id, 60),
        cost_estimate=scatter_cost(back, 3 * width),
    )(back, turned, hidden, down, middle, grads, normed)


def feed_kernel(
    block,
    q_ref,
    k_ref,
    v_ref,
    open_ref,
    b_ref,
    tokens_ref,
    gate_hbm,
    up_hbm,
    near_hbm,
    grad_hbm,
    down_hbm,
    attended_ref,
    lse_ref,
    a_ref,
    middle_ref,
    normed_ref,
    hidden_out_ref,
    back_out_ref,
    turned_out_ref,
    *scratch,
):
    here = Place()
    (
        feed_ref,
        swap_sems,
        local_sems,
        far_sems,
        buf,
        send_sems,
        recv_sems,
        store_sems,
        grad_ref,
        down_ref,
        hidden_ref,
        back_ref,
        turned_ref,
        fetch_sems,
        out_sems,
    ) = scratch[SCATTER_SCRATCH:]
    slots, slab = near_hbm.shape[:2]
    rows, width = middle_ref.shape
    hidden = hidden_ref.shape[1]
    tile = 256

    def fetch(slot):
        return pltpu.make_async_copy(
            near_hbm.at[slot], feed_ref.at[here.dp, here.peer(slot, True)], local_sems.at[slot]
        )

    def swap(slot, same):
        place = feed_ref.at[here.dp, here.peer(slot, same)]
        half = 0 if same else 1
        return remote(
            place,
            place,
            swap_sems.at[0, half, slot],
            swap_sems.at[1, half, slot],
            here.partner(),
        )

    columns = hidden // 2

    def far_copies(peer, sender, at, sem):
        made = []
        for kind, weight in enumerate((gate_hbm, up_hbm)):
            for half in range(2):
                part = kind * 2 + half
                begin = pl.multiple_of((half * here.count + peer) * columns, columns)
                made.append(
                    remote(
                        weight.at[:, pl.ds(begin, columns)],
                        feed_ref.at[here.dp, sender, :, pl.ds(part * columns, columns)],
                        far_sems.at[0, sem, part],
                        far_sems.at[1, at, part],
                        (here.dp, peer),
                    )
                )
        return made

    far = Spread(here, False, far_copies)

    fetches = [
        pltpu.make_async_copy(down_hbm, down_ref, fetch_sems.at[0]),
        pltpu.make_async_copy(grad_hbm, grad_ref, fetch_sems.at[1]),
    ]
    pl.loop(0, slots)(lambda slot: fetch(slot).start())
    for one in fetches:
        one.start()
    here.call_all()

    @pl.loop(0, a_ref.shape[0] // block)
    def _(tile):
        some = pl.ds(pl.multiple_of(tile * block, block), block)
        attention_kernel(
            block,
            q_ref.at[some],
            k_ref,
            v_ref,
            open_ref.at[some],
            attended_ref.at[some],
            lse_ref.at[some],
            tile,
        )
        a_ref[some, :] = attended_ref[some, :].astype(BF16)

        @pl.when(tile == 0)
        def _():
            here.await_all()
            far.start()

            @pl.loop(0, slots)
            def _(slot):
                fetch(slot).wait()
                swap(slot, True).start()

    def between():
        far.finish()
        pl.loop(0, slots)(lambda slot: swap(slot, False).start())

    scatter_rows_of_products(
        here,
        [(False, a_ref, b_ref, middle_ref)],
        *scratch[:SCATTER_SCRATCH],
        between=between,
    )
    half = buf.shape[2]
    for part in range(2):

        @pl.loop(0, half // ROW_CHUNK)
        def _(i, part=part):
            into = pl.ds(pl.multiple_of(i * ROW_CHUNK, ROW_CHUNK), ROW_CHUNK)
            some = pl.ds(pl.multiple_of(part * half + i * ROW_CHUNK, ROW_CHUNK), ROW_CHUNK)
            middle = tokens_ref[some, :].astype(F32) + middle_ref[some, :]
            middle_ref[some, :] = middle
            buf[here.mine, part, into, :] = (middle * norm_factor(middle)).astype(BF16)

    def started():
        @pl.loop(0, slots)
        def _(slot):
            swap(slot, True).wait()
            swap(slot, False).wait()

        for one in fetches:
            one.wait()

    store = UnitStore(buf, normed_ref, store_sems)
    share = width // (2 * here.length)

    def outs(number, first):
        where = unit_rows(first, rows)
        some = pl.ds(pl.multiple_of(number * share, share), share)
        return [
            pltpu.make_async_copy(src, dst, out_sems.at[number, i])
            for i, (src, dst) in enumerate(
                [
                    (hidden_ref.at[where], hidden_out_ref.at[where]),
                    (back_ref.at[where], back_out_ref.at[where]),
                    (turned_ref.at[:, some], turned_out_ref.at[:, some]),
                ]
            )
        ]

    def compute(number, first):
        store.start(number, first)
        where = unit_rows(first, rows)
        normed = take_unit(buf, first)
        grad = grad_ref[where, :]

        @pl.loop(0, hidden // tile)
        def _(t):
            cols = pl.ds(pl.multiple_of(t * tile, tile), tile)
            later = pl.ds(pl.multiple_of(hidden + t * tile, tile), tile)
            gate = dot(normed, feed_ref[:, :, :, cols].reshape(width, tile))
            upward = dot(normed, feed_ref[:, :, :, later].reshape(width, tile))
            hidden_grad = dot_t(grad, down_ref[cols, :])
            sigmoid = jax.nn.sigmoid(gate)
            silu = gate * sigmoid
            hidden_ref[where, cols] = (silu * upward).astype(BF16)
            back_ref[where, cols] = (
                hidden_grad * upward * sigmoid * (1.0 + gate * (1.0 - sigmoid))
            ).astype(BF16)
            back_ref[where, later] = (hidden_grad * silu).astype(BF16)

        slabs = share // slab
        begin = number * slabs
        some = pl.ds(pl.multiple_of(number * share, share), share)
        weights = feed_ref[lax.div(begin, here.count), pl.ds(lax.rem(begin, here.count), slabs)]
        turned_ref[:, some] = weights.reshape(share, 2 * hidden).T
        for one in outs(number, first):
            one.start()

    gather_units(here, buf, send_sems, recv_sems, compute, started=started)

    @pl.loop(0, here.count // 2)
    def _(number):
        for one in outs(number, 0):
            one.wait()

    store.finish()


def feed_both_ways(
    queries, keys, values, opening, output, tokens, gate, up, near, grad_out, down, block, call_id
):
    seq = lax.axis_size("seq")
    rows, width = tokens.shape
    cols = queries.shape[1]
    hidden = down.shape[0]
    all_rows = seq * rows
    bf16 = lambda *shape: jax.ShapeDtypeStruct(shape, BF16)
    f32 = lambda *shape: jax.ShapeDtypeStruct(shape, F32)
    dma = pltpu.SemaphoreType.DMA
    return pl.pallas_call(
        functools.partial(feed_kernel, block),
        out_shape=[
            f32(all_rows, cols),
            f32(all_rows, cols // HEAD_DIM),
            bf16(all_rows, cols),
            f32(rows, width),
            bf16(all_rows, width),
            bf16(all_rows, hidden),
            bf16(all_rows, 2 * hidden),
            bf16(2 * hidden, width),
        ],
        in_specs=[VMEM] * 6 + [HBM] * 5,
        out_specs=[VMEM] * 4 + [HBM] * 4,
        scratch_shapes=scatter_scratch(seq, rows, width)
        + [
            pltpu.VMEM((2, seq, *near.shape[1:]), BF16),
            dma((2, 2, seq // 2)),
            dma((seq // 2,)),
            dma((2, seq // 2, 4)),
        ]
        + gather_scratch(seq, rows // 2, width)
        + [
            dma((seq // 2, 2, 2)),
            pltpu.VMEM((all_rows, width), BF16),
            pltpu.VMEM((hidden, width), BF16),
            pltpu.VMEM((all_rows, hidden), BF16),
            pltpu.VMEM((all_rows, 2 * hidden), BF16),
            pltpu.VMEM((2 * hidden, width), BF16),
            dma((2,)),
            dma((seq // 2, 3)),
        ],
        compiler_params=params(call_id, 62),
        cost_estimate=cost(8 * all_rows * width * hidden, 8 * all_rows * width),
    )(queries, keys, values, opening, output, tokens, gate, up, near, grad_out, down)


def back_kernel(
    block,
    own_ref,
    weight_ref,
    low_ref,
    q_ref,
    k_ref,
    v_ref,
    att_ref,
    lse_ref,
    open_ref,
    cos_ref,
    sin_ref,
    heads_ref,
    hidden_hbm,
    out_grad_hbm,
    blocks_ref,
    normed_hbm,
    output_kept_ref,
    output_came_ref,
    down_kept_ref,
    down_came_ref,
    near_ref,
    far_ref,
    out_ref,
    qkv_ref,
    *scratch,
):
    here = Place()
    (
        buf,
        send_sems,
        recv_sems,
        part,
        hidden_ref,
        out_grad,
        grad_ref,
        output_away,
        down_away,
        dq_ref,
        dk_ref,
        dv_ref,
        share_out,
        share_in,
        back_ref,
        normed,
        kept,
        away,
        came,
        sums,
        near_sems,
        far_sems,
        local_sems,
        swap_sems,
        share_sems,
        fetch_sems,
        sum_sems,
        sum_near_sems,
        sum_far_sems,
    ) = scratch[SCATTER_SCRATCH:]
    rows, width = own_ref.shape
    cols = q_ref.shape[1]
    tile = 512
    units = 2 * here.length
    share = width // units

    hidden_copy = pltpu.make_async_copy(hidden_hbm, hidden_ref, local_sems.at[0])
    own_copy = pltpu.make_async_copy(
        blocks_ref.at[here.mine], near_ref.at[here.slot], local_sems.at[1]
    )
    near = block_spread(here, True, blocks_ref, near_ref, near_sems)
    far = block_spread(here, False, blocks_ref, far_ref, far_sems)
    swaps = [
        remote(src, dst, swap_sems.at[0, number], swap_sems.at[1, number], here.partner())
        for number, (src, dst) in enumerate(
            [(down_away, down_came_ref), (output_away, output_came_ref)]
        )
    ]

    def out_grad_copy(number):
        some = pl.ds(pl.multiple_of(number * share, share), share)
        slot = number % 2
        return pltpu.make_async_copy(
            out_grad_hbm.at[:, some], out_grad.at[slot], fetch_sems.at[0, slot]
        )

    hidden_copy.start()
    own_copy.start()
    out_grad_copy(jnp.int32(0)).start()
    here.call_all()
    put_own(here, own_ref, buf)
    part[...] = jnp.zeros_like(part)
    here.await_all()

    def split(values, kept_to, away_to, some):
        half = values.shape[0] // 2
        top, bottom = values[:half], values[half:]
        kept_to[:, some] = jnp.where(here.dp == 0, top, bottom)
        away_to[:, some] = jnp.where(here.dp == 0, bottom, top).astype(BF16)

    def compute(number, first):
        where = unit_rows(first, rows)
        unit = take_unit(buf, first)
        grad_ref[where, :] = dot_t(unit, weight_ref[...]).astype(BF16)
        attended = low_ref[where, :]
        for t in range(width // tile):
            some = slice(t * tile, (t + 1) * tile)
            part[:, some] += t_dot(attended, unit[:, some])
        pl.when(number == 0)(hidden_copy.wait)
        out_grad_copy(number).wait()
        pl.when(number + 1 < units)(lambda: out_grad_copy(number + 1).start())
        some = pl.ds(pl.multiple_of(number * share, share), share)
        split(t_dot(hidden_ref[...], out_grad[number % 2]), down_kept_ref, down_away, some)

    def between(step):
        near.start_some(step - here.length, 2)

    gather_units(here, buf, send_sems, recv_sems, compute, between)
    far.start()
    for t in range(width // tile):
        some = slice(t * tile, (t + 1) * tile)
        split(part[:, some], output_kept_ref, output_away, some)
    for one in swaps:
        one.start()

    tiles = q_ref.shape[0] // block
    scale = 1.0 / math.sqrt(HEAD_DIM)

    @pl.loop(0, tiles)
    def _(i):
        some = pl.ds(pl.multiple_of(i * block, block), block)
        attention_back_kernel(
            block,
            q_ref.at[some],
            k_ref,
            v_ref,
            grad_ref.at[some],
            att_ref.at[some],
            lse_ref.at[some],
            open_ref.at[some],
            dq_ref,
            dk_ref,
            dv_ref,
            i,
        )
        turned = rotated(dq_ref[...] * scale, cos_ref[some, :], -sin_ref[some, :])
        back_ref[some, :cols] = turned.astype(BF16)

    def share_copy(i):
        some = pl.ds(pl.multiple_of(i * block, block), block)
        return remote(
            share_out.at[some],
            share_in.at[some],
            share_sems.at[0, i],
            share_sems.at[1, i],
            here.sibling(),
        )

    @pl.loop(0, tiles)
    def _(i):
        some = pl.ds(pl.multiple_of(i * block, block), block)
        share_out[some, :] = jnp.where(here.core == 0, dv_ref[some, :], dk_ref[some, :]).astype(BF16)
        share_copy(i).start()

    @pl.loop(0, tiles)
    def _(i):
        some = pl.ds(pl.multiple_of(i * block, block), block)
        share_copy(i).wait()
        other = share_in[some, :].astype(F32)
        keys = rotated(dk_ref[some, :] + other, cos_ref[some, :], -sin_ref[some, :])
        back_ref[some, cols:] = jnp.where(here.core == 0, keys, dv_ref[some, :] + other).astype(BF16)

    swap = remote(away, came, sum_sems.at[0], sum_sems.at[1], here.partner())
    sum_near = block_spread(here, True, sums, qkv_ref.at[0], sum_near_sems)
    sum_far = block_spread(here, False, sums, qkv_ref.at[1], sum_far_sems)
    half = away.shape[0]
    chunk = normed.shape[2]
    chunks = half // chunk

    def normed_copy(number):
        dp = jnp.where(number < chunks, 1 - here.dp, here.dp)
        begin = dp * half + number % chunks * chunk
        slot = number % 2
        return pltpu.make_async_copy(
            normed_hbm.at[:, pl.ds(pl.multiple_of(begin, chunk), chunk)],
            normed.at[slot],
            fetch_sems.at[1, slot],
        )

    def heads_part(number):
        normed_copy(number).wait()
        pl.when(number + 1 < 2 * chunks)(lambda: normed_copy(number + 1).start())
        return t_dot(normed[number % 2], back_ref[...])

    normed_copy(jnp.int32(0)).start()

    def first(step):
        @pl.when(step == 2)
        def _():
            @pl.loop(0, chunks)
            def _(i):
                some = pl.ds(pl.multiple_of(i * chunk, chunk), chunk)
                away[some, :] = heads_part(i).astype(BF16)

            swap.start()

    def own_share():
        @pl.loop(0, chunks)
        def _(i):
            kept[pl.ds(pl.multiple_of(i * chunk, chunk), chunk), :] = heads_part(chunks + i)

    begin = 2
    each = 3

    def filler(step):
        @pl.when(step == begin)
        def _():
            swap.wait_recv()
            slab = sums.shape[1]

            @pl.loop(0, here.count)
            def _(i):
                some = pl.ds(pl.multiple_of(i * slab, slab), slab)
                sums[i] = (kept[some, :] + came[some, :].astype(F32)).astype(BF16)

            qkv_ref[0, here.slot] = sums[here.mine]

        @pl.when(step > begin)
        def _():
            @pl.loop(0, each)
            def _(i):
                number = (step - begin - 1) * each + i
                pl.when(number < sum_far.slots)(lambda: sum_far.start_one(number))

                @pl.when((number >= sum_far.slots) & (number < 2 * sum_far.slots - 1))
                def _():
                    sum_near.start_one(number - sum_far.slots + 1)

    scatter_rows_of_products(
        here,
        [(True, back_ref, heads_ref, out_ref)],
        *scratch[:SCATTER_SCRATCH],
        first=first,
        between=own_share,
        filler=filler,
    )
    swap.wait_send()
    for one in swaps:
        one.wait()
    near.finish()
    far.finish()
    own_copy.wait()
    sum_near.finish()
    sum_far.finish()


def attention_backwards(
    own,
    weight,
    attended,
    queries,
    keys,
    values,
    attended_sum,
    log_total,
    opening,
    cosine,
    sine,
    heads,
    hidden,
    grad_out,
    blocks,
    normed,
    block,
    call_id,
):
    seq = lax.axis_size("seq")
    rows, width = own.shape
    all_rows, cols = queries.shape
    slab = blocks.shape[1]
    half_hidden = hidden.shape[1] // 2
    chunk = width // 8
    bf16 = lambda *shape: jax.ShapeDtypeStruct(shape, BF16)
    f32 = lambda *shape: jax.ShapeDtypeStruct(shape, F32)
    dma = pltpu.SemaphoreType.DMA
    return pl.pallas_call(
        functools.partial(back_kernel, block),
        out_shape=[
            f32(cols // 2, width),
            bf16(cols // 2, width),
            f32(half_hidden, width),
            bf16(half_hidden, width),
            bf16(seq // 2, *blocks.shape[1:]),
            bf16(seq // 2, *blocks.shape[1:]),
            f32(rows, width),
            bf16(2, seq // 2, slab, 2 * cols),
        ],
        in_specs=[VMEM] * 12 + [HBM] * 4,
        out_specs=[VMEM, HBM, VMEM, HBM, HBM, HBM, VMEM, VMEM],
        scratch_shapes=scatter_scratch(seq, rows, width)
        + gather_scratch(seq, rows // 2, width)
        + [
            pltpu.VMEM((cols, width), F32),
            pltpu.VMEM(hidden.shape, BF16),
            pltpu.VMEM((2, all_rows, width // (seq // 2)), BF16),
            pltpu.VMEM((all_rows, cols), BF16),
            pltpu.VMEM((cols // 2, width), BF16),
            pltpu.VMEM((half_hidden, width), BF16),
            pltpu.VMEM((block, cols), F32),
            pltpu.VMEM((all_rows, cols), F32),
            pltpu.VMEM((all_rows, cols), F32),
            pltpu.VMEM((all_rows, cols), BF16),
            pltpu.VMEM((all_rows, cols), BF16),
            pltpu.VMEM((all_rows, 2 * cols), BF16),
            pltpu.VMEM((2, all_rows, chunk), BF16),
            pltpu.VMEM((width // 2, 2 * cols), F32),
            pltpu.VMEM((width // 2, 2 * cols), BF16),
            pltpu.VMEM((width // 2, 2 * cols), BF16),
            pltpu.VMEM((seq, slab, 2 * cols), BF16),
            dma((2, seq // 2)),
            dma((2, seq // 2)),
            dma((2,)),
            dma((2, 2)),
            dma((2, all_rows // block)),
            dma((2, 2)),
            dma((2,)),
            dma((2, seq // 2)),
            dma((2, seq // 2)),
        ],
        compiler_params=params(call_id, 62),
        cost_estimate=cost(12 * all_rows * width * cols, 12 * all_rows * width),
    )(
        own,
        weight,
        attended,
        queries,
        keys,
        values,
        attended_sum,
        log_total,
        opening,
        cosine,
        sine,
        heads,
        hidden,
        grad_out,
        blocks,
        normed,
    )


UNPACK_LINES = 4


def unpack_kernel(
    pair_ref,
    near_gate_ref,
    far_gate_ref,
    near_up_ref,
    far_up_ref,
    gate_ref,
    up_ref,
    qkv_ref,
    query_ref,
    key_ref,
    value_ref,
    gain_one_ref,
    gain_two_ref,
    tokens_ref,
    middle_ref,
    mixed_sum_ref,
    middle_grad_ref,
    upstream_ref,
    down_kept_ref,
    down_came_ref,
    output_kept_ref,
    output_came_ref,
    gate_out_ref,
    up_out_ref,
    query_out_ref,
    key_out_ref,
    value_out_ref,
    one_out_ref,
    two_out_ref,
    mixed_ref,
    token_grad_ref,
    down_out_ref,
    output_out_ref,
    total_two,
):
    pair = pair_ref[0]
    dp = lax.axis_size("dp")
    length = qkv_ref.shape[1] // 2
    slab = qkv_ref.shape[2]
    step = pl.program_id(0) * pl.num_programs(1) + pl.program_id(1)
    columns = near_gate_ref.shape[2]

    def along(grad, weight):
        return jnp.sum(grad * weight.astype(F32), axis=1, keepdims=True)

    @pl.when(step == 0)
    def _():
        total_two[...] = jnp.zeros_like(total_two)
        total = jnp.zeros((slab, 1), F32)
        gain = upright(gain_one_ref[...])

        def put(out_ref, weight_ref, begin, grad):
            cols = slice(begin, begin + grad.shape[1])
            out_ref[:, cols] = grad * gain
            return along(grad, weight_ref[:, cols])

        pairs = [{}, {}]
        for line in range(length):
            rows = []
            for number in range(4):
                slot = line * 2 + number % 2
                near, far = qkv_ref[0, slot].astype(F32), qkv_ref[1, slot].astype(F32)
                rows.append(jnp.where(number // 2 == pair, near, far))
            kv = [rows[core] + rows[core + 2] for core in range(2)]
            for half in range(dp):
                cols = slice(half * HEAD_DIM, (half + 1) * HEAD_DIM)
                for number in (0, 2):
                    two = jnp.concatenate([rows[number][:, cols], rows[number + 1][:, cols]], axis=1)
                    begin = (half * length * 4 + line * 4 + number) * HEAD_DIM
                    total = total + put(query_out_ref, query_ref, begin, two)
                for kind in range(2):
                    begin = (dp + half) * HEAD_DIM
                    pairs[kind][half, line] = kv[kind][:, begin : begin + HEAD_DIM]
        for kind, (out_ref, weight_ref) in enumerate(
            [(key_out_ref, key_ref), (value_out_ref, value_ref)]
        ):
            for half in range(dp):
                for line in range(0, length, 2):
                    two = [pairs[kind][half, line], pairs[kind][half, line + 1]]
                    begin = (half * length + line) * HEAD_DIM
                    total = total + put(
                        out_ref, weight_ref, begin, jnp.concatenate(two, axis=1)
                    )
        one_out_ref[...] = flat(total)

    mixed_ref[...] = middle_ref[...] + mixed_sum_ref[...]
    token_grad_ref[...] = middle_grad_ref[...] + norm_input_grad(
        tokens_ref[...].astype(F32), upstream_ref[...]
    )
    down_out_ref[...] = down_kept_ref[...] + down_came_ref[...].astype(F32)
    output_out_ref[...] = output_kept_ref[...] + output_came_ref[...].astype(F32)
    gain_two = upright(gain_two_ref[...])
    total = jnp.zeros((slab, 1), F32)
    for near_ref, far_ref, weight_ref, out_ref in (
        (near_gate_ref, far_gate_ref, gate_ref, gate_out_ref),
        (near_up_ref, far_up_ref, up_ref, up_out_ref),
    ):
        for number in range(2 * near_ref.shape[0]):
            slot = number // 4 * 2 + number % 2
            near, far = near_ref[slot].astype(F32), far_ref[slot].astype(F32)
            grad = jnp.where(number // 2 % 2 == pair, near, far)
            cols = slice(number * columns, (number + 1) * columns)
            total = total + along(grad, weight_ref[:, cols])
            out_ref[:, cols] = grad * gain_two
    total_two[...] += total

    @pl.when(step == pl.num_programs(0) * pl.num_programs(1) - 1)
    def _():
        two_out_ref[...] = flat(total_two[...])


def unpack(pair, near, far, gate, up, qkv, query, key, value, gain_one, gain_two, *rows):
    dp = lax.axis_size("dp")
    seq = lax.axis_size("seq")
    slab, ff = gate.shape
    length = seq // 4 // UNPACK_LINES
    columns = ff // (dp * seq)
    whole = lambda array: pl.BlockSpec(array.shape, lambda j, i: (0,) * array.ndim)
    block = lambda kind: pl.BlockSpec(
        (2 * UNPACK_LINES, slab, columns), lambda j, i: (i, 0, kind * dp + j)
    )
    tile = pl.BlockSpec((slab, 4 * UNPACK_LINES * columns), lambda j, i: (0, j * length + i))
    f32 = lambda array: jax.ShapeDtypeStruct(array.shape, F32)
    outs = [f32(gate), f32(up), f32(query), f32(key), f32(value), f32(gain_one), f32(gain_two)]
    sums = [f32(rows[0]), f32(rows[0]), f32(rows[5]), f32(rows[7])]
    steps = dp * length
    strip = lambda array: pl.BlockSpec(
        (array.shape[0] // steps, array.shape[1]), lambda j, i: (j * length + i, 0)
    )
    return pl.pallas_call(
        unpack_kernel,
        grid=(dp, length),
        in_specs=[pl.BlockSpec(memory_space=pltpu.SMEM)]
        + [block(0), block(0), block(1), block(1), tile, tile]
        + [whole(array) for array in (qkv, query, key, value, gain_one, gain_two)]
        + [strip(array) for array in rows],
        out_specs=[tile, tile]
        + [whole(array) for array in outs[2:]]
        + [strip(array) for array in sums],
        out_shape=outs + sums,
        scratch_shapes=[pltpu.VMEM((slab, 1), F32)],
        compiler_params=pltpu.CompilerParams(vmem_limit_bytes=60 << 20),
        cost_estimate=cost(slab * ff, 16 * slab * ff),
    )(
        pair,
        near,
        far,
        near,
        far,
        gate,
        up,
        qkv,
        query,
        key,
        value,
        gain_one,
        gain_two,
        *rows,
    )


def swap_dp(values):
    count = lax.axis_size("dp")
    return lax.ppermute(values, "dp", [(i, (i + 1) % count) for i in range(count)])


def gather_dp(values):
    return lax.all_gather(values, "dp", axis=0, tiled=True)


def sum_dp(partial):
    half = partial.shape[0] // 2
    mine = lax.axis_index("dp")
    away = lax.dynamic_slice_in_dim(partial, (1 - mine) * half, half, 0).astype(BF16)
    kept = lax.dynamic_slice_in_dim(partial, mine * half, half, 0)
    return kept + swap_dp(away).astype(F32)


def gather_rows(values):
    return lax.all_gather(values, "seq", axis=0, tiled=True)


def scatter_rows(partial):
    return lax.psum_scatter(partial.astype(BF16), "seq", scatter_dimension=0, tiled=True).astype(F32)


def exchange(blocks):
    return lax.all_to_all(blocks, "seq", split_axis=0, concat_axis=0, tiled=True)


def norm_factor(values):
    return lax.rsqrt(jnp.mean(values * values, axis=-1, keepdims=True) + EPS)


def norm_back(inputs, factor, gain_row, upstream):
    scaled_up = gain_row * upstream
    inner_mean = jnp.mean(scaled_up * inputs, axis=-1, keepdims=True)
    grad_in = factor * scaled_up - inputs * factor * factor * factor * inner_mean
    grad_gain = jnp.sum(upstream * inputs * factor, axis=0)
    return grad_in, grad_gain


def plain_shards(
    tokens,
    cotangent,
    doc_lengths,
    attn_gain,
    mlp_gain,
    query_weight,
    key_weight,
    value_weight,
    output_weight,
    gate_weight,
    up_weight,
    down_weight,
):
    dp = lax.axis_size("dp")
    seq = lax.axis_size("seq")
    mine = lax.axis_index("seq")
    tok_count, width = tokens.shape
    rows = tok_count * seq
    slab = query_weight.shape[0]
    share = HEAD_DIM // slab
    half_heads = HEADS // dp
    half_kv = KV_HEADS // dp
    hidden_dev = down_weight.shape[0]
    block = 512

    doc_ends = jnp.cumsum(doc_lengths[0])
    place = jnp.arange(rows, dtype=jnp.int32)
    passed = doc_ends[None, :] <= place[:, None]
    opening = jnp.max(jnp.where(passed, doc_ends[None, :], 0), axis=1)
    position = place - opening
    keeping = place < doc_ends[DOCS - 1]
    angles = position.astype(F32)[:, None] * rotary_table(HEAD_DIM)[None, :]
    cosine = jnp.cos(angles)
    sine = jnp.sin(angles)
    cos_heads = jnp.tile(cosine, (1, 2 * dp))
    sin_heads = jnp.tile(jnp.concatenate([-sine, sine], axis=1), (1, dp))
    own_keeping = lax.dynamic_slice_in_dim(keeping, mine * tok_count, tok_count, 0)

    def head_columns(weight, kept):
        split = weight.reshape(slab, dp, kept, HEAD_DIM)
        return jnp.repeat(split, seq // kept, axis=2)

    qkv_blocks = jnp.stack(
        [
            head_columns(query_weight, half_heads),
            head_columns(key_weight, half_kv),
            head_columns(value_weight, half_kv),
        ],
        axis=1,
    )
    qkv_blocks = jnp.transpose(qkv_blocks, (3, 0, 1, 2, 4)).reshape(seq * slab, 3 * dp * HEAD_DIM)
    qkv_weight = gather_dp(exchange(qkv_blocks))
    feed_blocks = jnp.stack(
        [w.reshape(slab, dp, seq, hidden_dev) for w in (gate_weight, up_weight)], axis=1
    )
    feed_blocks = jnp.transpose(feed_blocks, (3, 0, 1, 2, 4)).reshape(
        seq * slab, 2 * dp * hidden_dev
    )
    feed_weight = gather_dp(exchange(feed_blocks))
    down_own = gather_dp(down_weight)
    output_own = output_weight
    if share > 1:
        groups = [list(range(i, i + share)) for i in range(0, seq, share)]
        output_own = lax.all_gather(
            output_own, "seq", axis=0, tiled=True, axis_index_groups=groups
        )
    output_own = gather_dp(output_own)
    gains = lax.all_gather(
        jnp.stack([attn_gain, mlp_gain]), ("dp", "seq"), axis=1, tiled=True
    ).astype(F32)
    gain_one, gain_two = gains[0], gains[1]

    inputs_all = gather_rows(tokens).astype(F32)
    normed_one = (inputs_all * norm_factor(inputs_all) * gain_one).astype(BF16)
    qkv = dot(normed_one, qkv_weight)
    head_cols = dp * HEAD_DIM
    query_lin, key_lin = qkv[:, :head_cols], qkv[:, head_cols : 2 * head_cols]
    values = qkv[:, 2 * head_cols :].astype(BF16)
    scale = 1.0 / math.sqrt(HEAD_DIM)
    queries = (query_lin * cos_heads + swap_halves(query_lin) * sin_heads).astype(BF16) * BF16(scale)
    keys = (key_lin * cos_heads + swap_halves(key_lin) * sin_heads).astype(BF16)
    attended_sum, log_total = attention(queries, keys, values, opening[:, None], block)
    if share > 1:
        own_rows = ((place // tok_count) % share == mine % share)[:, None]
        attended_sum = jnp.where(own_rows, attended_sum, 0.0)
    attended = attended_sum.astype(BF16)
    inputs = tokens.astype(F32)
    middle = inputs + scatter_rows(dot(attended, output_own))

    factor_two = norm_factor(middle)
    normed_two = gather_rows((middle * factor_two * gain_two).astype(BF16))
    grad_own = jnp.where(own_keeping[:, None], cotangent, BF16(0))
    grad_out = gather_rows(grad_own)
    feed = dot(normed_two, feed_weight)
    feed_cols = dp * hidden_dev
    gate_lin, upward = feed[:, :feed_cols], feed[:, feed_cols:]
    sigmoid = jax.nn.sigmoid(gate_lin)
    hidden = (gate_lin * sigmoid * upward).astype(BF16)
    hidden_grad = dot_t(grad_out, down_own)
    gate_back = (hidden_grad * upward * sigmoid * (1.0 + gate_lin * (1.0 - sigmoid))).astype(BF16)
    up_back = (hidden_grad * gate_lin * sigmoid).astype(BF16)
    feed_back = jnp.concatenate([gate_back, up_back], axis=1)
    normed_two_grad = scatter_rows(dot_t(feed_back, feed_weight))
    mixed = middle + scatter_rows(dot(hidden, down_own))
    middle_in, gain_two_part = norm_back(middle, factor_two, gain_two, normed_two_grad)
    middle_grad = grad_own.astype(F32) + middle_in
    middle_back = gather_rows(middle_grad.astype(BF16))

    attended_grad = dot_t(middle_back, output_own).astype(BF16)
    if share > 1:
        attended_grad = jnp.where(own_rows, attended_grad, BF16(0))
    query_acc, key_acc, value_acc = attention_back(
        queries, keys, values, attended_grad, attended_sum, log_total, opening[:, None], block
    )
    query_acc = query_acc * scale
    query_back = query_acc * cos_heads - swap_halves(query_acc) * sin_heads
    key_back = key_acc * cos_heads - swap_halves(key_acc) * sin_heads
    qkv_back = jnp.concatenate([query_back, key_back, value_acc], axis=1).astype(BF16)
    normed_one_grad = scatter_rows(dot_t(qkv_back, qkv_weight))
    input_in, gain_one_part = norm_back(inputs, norm_factor(inputs), gain_one, normed_one_grad)
    token_grad = middle_grad + input_in

    feed_grad = exchange(sum_dp(t_dot(normed_two, feed_back)).astype(BF16)).astype(F32)
    feed_grad = feed_grad.reshape(seq, slab, 2, dp, hidden_dev)
    feed_grad = jnp.transpose(feed_grad, (2, 1, 3, 0, 4)).reshape(2, slab, dp * seq * hidden_dev)
    down_grad = sum_dp(t_dot(hidden, grad_out))
    output_part = t_dot(attended, middle_back)
    if share > 1:
        split = output_part.reshape(dp, share, slab, width)
        split = jnp.transpose(split, (1, 0, 2, 3)).reshape(share * dp * slab, width)
        output_part = lax.psum_scatter(
            split, "seq", scatter_dimension=0, tiled=True, axis_index_groups=groups
        )
    output_grad = sum_dp(output_part)
    qkv_grad = exchange(sum_dp(t_dot(normed_one, qkv_back)).astype(BF16)).astype(F32)
    qkv_grad = qkv_grad.reshape(seq, slab, 3, dp, HEAD_DIM)

    def own_columns(part, kept):
        summed = jnp.sum(part.reshape(kept, seq // kept, slab, dp, HEAD_DIM), axis=1)
        return jnp.transpose(summed, (1, 2, 0, 3)).reshape(slab, dp * kept * HEAD_DIM)

    query_grad = own_columns(qkv_grad[:, :, 0], half_heads)
    key_grad = own_columns(qkv_grad[:, :, 1], half_kv)
    value_grad = own_columns(qkv_grad[:, :, 2], half_kv)
    gain_parts = lax.psum(jnp.stack([gain_one_part, gain_two_part]), ("dp", "seq"))
    own = lax.axis_index("dp") * seq + mine
    gain_grads = lax.dynamic_slice_in_dim(gain_parts, own * slab, slab, 1)
    return (
        mixed,
        token_grad,
        gain_grads[0],
        gain_grads[1],
        query_grad,
        key_grad,
        value_grad,
        output_grad,
        feed_grad[0],
        feed_grad[1],
        down_grad,
    )


def frequencies():
    exponent = np.arange(0, HEAD_DIM, 2, dtype=np.float32) / np.float32(HEAD_DIM)
    inverse = np.power(np.float32(500000.0), -exponent)
    wavelength = np.float32(2.0 * math.pi) / inverse
    smooth = (np.float32(8192.0) / wavelength - np.float32(1.0)) / np.float32(3.0)
    blended = (np.float32(1.0) - smooth) * inverse / np.float32(32.0) + smooth * inverse
    scaled = np.where(
        wavelength < 2048.0,
        inverse,
        np.where(wavelength > 8192.0, inverse / np.float32(32.0), blended),
    )
    return np.tile(scaled.astype(np.float32), 4)


FREQUENCIES = frequencies()


def shards(
    tokens,
    cotangent,
    doc_lengths,
    attn_gain,
    mlp_gain,
    query_weight,
    key_weight,
    value_weight,
    output_weight,
    gate_weight,
    up_weight,
    down_weight,
):
    dp = lax.axis_size("dp")
    seq = lax.axis_size("seq")
    mine = lax.axis_index("seq")
    tok_count, width = tokens.shape
    slab = query_weight.shape[0]
    block = 512
    gain_one = attn_gain[None, :]
    gain_two = mlp_gain[None, :]

    (
        normed_one,
        grad_out,
        queries,
        keys,
        values,
        cosine,
        sine,
        opening,
        qkv_weight,
        gate_scaled,
        up_scaled,
        feed_near,
        down_own,
        output_own,
    ) = gather_project(
        doc_lengths,
        tokens,
        cotangent,
        query_weight,
        key_weight,
        value_weight,
        gate_weight,
        up_weight,
        (gain_one, gain_two),
        jnp.asarray(FREQUENCIES)[None, :],
        down_weight,
        output_weight,
        0,
    )
    qkv_weight = qkv_weight.reshape(width, -1)
    down_own = down_own.reshape(-1, width)
    output_own = output_own.reshape(-1, width)
    attended_sum, log_total, attended, middle, normed_two, hidden, feed_back, feed_turned = (
        feed_both_ways(
            queries,
            keys,
            values,
            opening,
            output_own,
            tokens,
            gate_scaled,
            up_scaled,
            feed_near,
            grad_out,
            down_own,
            block,
            1,
        )
    )

    middle_grad, middle_back, mixed_sum, feed_sums = product_scatter_both(
        feed_back, feed_turned, hidden, down_own, middle, grad_out, normed_two, 4
    )
    feed_sums = feed_sums.reshape(seq, slab, -1)
    (
        output_kept,
        output_came,
        down_kept,
        down_came,
        feed_grad_near,
        feed_grad_far,
        normed_one_grad,
        qkv_grads,
    ) = attention_backwards(
        middle_back,
        output_own,
        attended,
        queries,
        keys,
        values,
        attended_sum,
        log_total,
        opening,
        cosine,
        sine,
        qkv_weight,
        hidden,
        grad_out,
        feed_sums,
        normed_one,
        block,
        5,
    )

    pair = ((mine // 2) % 2).reshape(1)
    (
        gate_grad,
        up_grad,
        query_grad,
        key_grad,
        value_grad,
        attn_gain_grad,
        mlp_gain_grad,
        mixed,
        token_grad,
        down_grad,
        output_grad,
    ) = unpack(
        pair,
        feed_grad_near,
        feed_grad_far,
        gate_weight,
        up_weight,
        qkv_grads,
        query_weight,
        key_weight,
        value_weight,
        gain_one,
        gain_two,
        tokens,
        middle,
        mixed_sum,
        middle_grad,
        normed_one_grad,
        down_kept,
        down_came,
        output_kept,
        output_came,
    )
    return (
        mixed,
        token_grad,
        attn_gain_grad[0],
        mlp_gain_grad[0],
        query_grad,
        key_grad,
        value_grad,
        output_grad,
        gate_grad,
        up_grad,
        down_grad,
    )


def solution(mesh):
    both = P(("dp", "seq"), None)
    line = P(("dp", "seq"))
    dp, seq = mesh.shape["dp"], mesh.shape["seq"]

    def run(*args):
        tokens = args[0].shape[0]
        width = args[0].shape[1]
        suits = dp == 2 and seq % 4 == 0 and width == dp * seq * HEAD_DIM
        suits = suits and 2 * (tokens // dp) * width <= 16 << 20
        return jax.shard_map(
            shards if suits else plain_shards,
            mesh=mesh,
            in_specs=(both, both, P("dp", None), line, line) + (both,) * 7,
            out_specs=(both, both, line, line) + (both,) * 7,
            check_vma=False,
        )(*args)

    return run
```

```python
import functools
import math

import jax
import jax.numpy as jnp
import numpy as np
from jax import lax
from jax.experimental import pallas as pl
from jax.experimental.pallas import tpu as pltpu
from jax.sharding import PartitionSpec as P

HEADS = 32
KV_HEADS = 8
HEAD_DIM = 64
DOCS = 4
EPS = 1e-05
NEG = -1e30
MESH = pl.DeviceIdType.MESH
F32 = jnp.float32
BF16 = jnp.bfloat16


def rotary_table(head_dim):
    exponent = jnp.arange(0, head_dim, 2, dtype=F32) / head_dim
    inverse = jnp.power(F32(500000.0), -exponent)
    wavelength = 2.0 * math.pi / inverse
    smooth = (8192.0 / wavelength - 1.0) / 3.0
    blended = (1.0 - smooth) * inverse / 32.0 + smooth * inverse
    return jnp.where(
        wavelength < 2048.0, inverse, jnp.where(wavelength > 8192.0, inverse / 32.0, blended)
    )


def swap_halves(values):
    rows, cols = values.shape
    halves = values.reshape(rows, cols // HEAD_DIM, 2, HEAD_DIM // 2)
    return halves[:, :, ::-1].reshape(rows, cols)


def dot(a, b):
    return jnp.dot(a, b, preferred_element_type=F32)


def dot_t(a, b):
    return lax.dot_general(a, b, (((1,), (1,)), ((), ())), preferred_element_type=F32)


def t_dot(a, b):
    return lax.dot_general(a, b, (((0,), (0,)), ((), ())), preferred_element_type=F32)


def allowed_tile(opening, q_first, k_first, shape):
    rows = q_first + lax.broadcasted_iota(jnp.int32, shape, 0)
    cols = k_first + lax.broadcasted_iota(jnp.int32, shape, 1)
    return (cols <= rows) & (cols >= opening)


def attention_kernel(block, q_ref, k_ref, v_ref, open_ref, out_ref, lse_ref, tile=None):
    if tile is None:
        tile = pl.program_id(0)
    opening = open_ref[...]
    heads = [
        slice(i * HEAD_DIM, (i + 1) * HEAD_DIM) for i in range(q_ref.shape[1] // HEAD_DIM)
    ]

    def step(j, carry):
        first = pl.multiple_of(j * block, block)
        allowed = allowed_tile(opening, tile * block, first, (block, block))
        after = []
        for lanes, (peak, total, acc) in zip(heads, carry):
            scores = dot_t(q_ref[:, lanes], k_ref[pl.ds(first, block), lanes])
            scores = jnp.where(allowed, scores, NEG)
            new_peak = jnp.maximum(peak, jnp.max(scores, axis=1, keepdims=True))
            spread = jnp.exp(scores - new_peak)
            fade = jnp.exp(peak - new_peak)
            total = total * fade + jnp.sum(spread, axis=1, keepdims=True)
            acc = acc * fade + dot(spread.astype(BF16), v_ref[pl.ds(first, block), lanes])
            after.append((new_peak, total, acc))
        return tuple(after)

    start = (
        jnp.full((block, 1), NEG, F32),
        jnp.zeros((block, 1), F32),
        jnp.zeros((block, HEAD_DIM), F32),
    )
    done = lax.fori_loop(0, tile + 1, step, (start,) * len(heads))
    for head, (lanes, (peak, total, acc)) in enumerate(zip(heads, done)):
        out_ref[:, lanes] = acc / total
        lse_ref[:, head : head + 1] = peak + jnp.log(total)


def attention(queries, keys, values, opening, block):
    rows, cols = queries.shape
    heads = cols // HEAD_DIM
    tiled = lambda width: pl.BlockSpec((block, width), lambda i: (i, 0))
    whole = pl.BlockSpec((rows, cols), lambda i: (0, 0))
    return pl.pallas_call(
        functools.partial(attention_kernel, block),
        grid=(rows // block,),
        in_specs=[tiled(cols), whole, whole, tiled(1)],
        out_specs=[tiled(cols), tiled(heads)],
        out_shape=[
            jax.ShapeDtypeStruct((rows, cols), F32),
            jax.ShapeDtypeStruct((rows, heads), F32),
        ],
        compiler_params=pltpu.CompilerParams(vmem_limit_bytes=48 << 20),
        cost_estimate=pl.CostEstimate(
            flops=2 * rows * rows * cols, bytes_accessed=10 * rows * cols, transcendentals=0
        ),
    )(queries, keys, values, opening)


def attention_back_kernel(
    block,
    q_ref,
    k_ref,
    v_ref,
    g_ref,
    att_ref,
    lse_ref,
    open_ref,
    dq_ref,
    dk_ref,
    dv_ref,
    tile=None,
):
    if tile is None:
        tile = pl.program_id(0)

    @pl.when(tile == 0)
    def _():
        dk_ref[...] = jnp.zeros_like(dk_ref)
        dv_ref[...] = jnp.zeros_like(dv_ref)

    count = q_ref.shape[1] // HEAD_DIM
    columns = [open_ref[...].astype(F32), lse_ref[...]]
    for head in range(count):
        lanes = slice(head * HEAD_DIM, (head + 1) * HEAD_DIM)
        grad = g_ref[:, lanes].astype(F32)
        columns.append(jnp.sum(grad * att_ref[:, lanes], axis=1, keepdims=True))
    columns.append(jnp.zeros((block, 127 - 2 * count), F32))
    across = jnp.concatenate(columns, axis=1).T
    opening = across[0:1].astype(jnp.int32)
    heads = [
        (
            slice(head * HEAD_DIM, (head + 1) * HEAD_DIM),
            across[1 + head : 2 + head],
            across[1 + count + head : 2 + count + head],
        )
        for head in range(count)
    ]

    def step(j, carry):
        first = pl.multiple_of(j * block, block)
        here = pl.ds(first, block)
        keys = first + lax.broadcasted_iota(jnp.int32, (block, block), 0)
        places = tile * block + lax.broadcasted_iota(jnp.int32, (block, block), 1)
        allowed = (keys <= places) & (keys >= opening)
        after = []
        for (lanes, log_total, row_sum), acc in zip(heads, carry):
            query, grad, key = q_ref[:, lanes], g_ref[:, lanes], k_ref[here, lanes]
            scores = dot_t(key, query)
            chance = jnp.where(allowed, jnp.exp(scores - log_total), 0.0)
            prob_grad = dot_t(v_ref[here, lanes], grad)
            score_grad = (chance * (prob_grad - row_sum)).astype(BF16)
            dk_ref[here, lanes] += dot(score_grad, query)
            dv_ref[here, lanes] += dot(chance.astype(BF16), grad)
            after.append(acc + t_dot(score_grad, key))
        return tuple(after)

    start = jnp.zeros((block, HEAD_DIM), F32)
    done = lax.fori_loop(0, tile + 1, step, (start,) * len(heads))
    for (lanes, _, _), acc in zip(heads, done):
        dq_ref[:, lanes] = acc


def attention_back(queries, keys, values, grads, attended, log_total, opening, block):
    rows, cols = queries.shape
    heads = cols // HEAD_DIM
    tiled = lambda width: pl.BlockSpec((block, width), lambda i: (i, 0))
    whole = pl.BlockSpec((rows, cols), lambda i: (0, 0))
    return pl.pallas_call(
        functools.partial(attention_back_kernel, block),
        grid=(rows // block,),
        in_specs=[tiled(cols), whole, whole, tiled(cols), tiled(cols), tiled(heads), tiled(1)],
        out_specs=[tiled(cols), whole, whole],
        out_shape=[jax.ShapeDtypeStruct((rows, cols), F32)] * 3,
        compiler_params=pltpu.CompilerParams(vmem_limit_bytes=60 << 20),
        cost_estimate=pl.CostEstimate(
            flops=5 * rows * rows * cols, bytes_accessed=20 * rows * cols, transcendentals=0
        ),
    )(queries, keys, values, grads, attended, log_total, opening)


def nothing():
    pass


class Place:
    def __init__(self):
        self.dp = lax.axis_index("dp")
        self.mine = lax.axis_index("seq")
        self.count = lax.axis_size("seq")
        self.length = self.count // 4
        self.line = lax.div(self.mine, 4)
        self.pair = lax.rem(lax.div(self.mine, 2), 2)
        self.core = lax.rem(self.mine, 2)
        self.slot = self.line * 2 + self.core

    def index(self, line, pair, core):
        return (line * 2 + pair) * 2 + core

    def peer(self, slot, same):
        pair = self.pair if same else 1 - self.pair
        return self.index(lax.div(slot, 2), pair, lax.rem(slot, 2))

    def device(self, line, pair, core):
        return (self.dp, self.index(line, pair, core))

    def sibling(self):
        return self.device(self.line, self.pair, 1 - self.core)

    def across(self):
        return self.device(self.line, 1 - self.pair, self.core)

    def above(self):
        return self.device(self.line + 1, self.pair, self.core)

    def below(self):
        return self.device(self.line - 1, self.pair, self.core)

    def partner(self):
        return (1 - self.dp, self.mine)

    def greet(self, partner=False):
        barrier = pltpu.get_barrier_semaphore()

        def signal(device):
            pl.semaphore_signal(barrier, inc=1, device_id=device, device_id_type=MESH)

        signal(self.sibling())
        signal(self.across())
        pl.when(self.line > 0)(lambda: signal(self.below()))
        pl.when(self.line < self.length - 1)(lambda: signal(self.above()))
        if partner:
            signal(self.partner())
        inner = (self.line > 0) & (self.line < self.length - 1)
        pl.semaphore_wait(barrier, jnp.where(inner, 4, 3) + (1 if partner else 0))

    def greet_all(self, meanwhile=nothing):
        self.call_all()
        meanwhile()
        self.await_all()

    def await_all(self):
        pl.semaphore_wait(pltpu.get_barrier_semaphore(), self.count)

    def call_all(self):
        barrier = pltpu.get_barrier_semaphore()

        def signal(device):
            pl.semaphore_signal(barrier, inc=1, device_id=device, device_id_type=MESH)

        signal(self.partner())

        @pl.loop(1, self.count)
        def _(ahead):
            signal((self.dp, lax.rem(self.mine + ahead, self.count)))


def remote(src, dst, send_sem, recv_sem, device):
    return pltpu.make_async_remote_copy(
        src_ref=src,
        dst_ref=dst,
        send_sem=send_sem,
        recv_sem=recv_sem,
        device_id=device,
        device_id_type=MESH,
    )


class Spread:
    def __init__(self, here, same, copies):
        self.here, self.same, self.copies = here, same, copies
        self.slots = here.count // 2

    def each(self, visit):
        @pl.loop(1 if self.same else 0, self.slots)
        def _(ahead):
            slot = lax.rem(self.here.slot + ahead, self.slots)
            visit(self.here.peer(slot, self.same), slot)

    def start_one(self, ahead):
        slot = lax.rem(self.here.slot + ahead, self.slots)
        peer = self.here.peer(slot, self.same)
        for one in self.copies(peer, self.here.mine, self.here.slot, slot):
            one.start()

    def start(self):
        pl.loop(1 if self.same else 0, self.slots)(self.start_one)

    def start_some(self, number, each):
        first = 1 if self.same else 0

        @pl.loop(0, each)
        def _(i):
            ahead = first + number * each + i
            pl.when((number >= 0) & (ahead < self.slots))(lambda: self.start_one(ahead))

    def finish(self):
        def visit(peer, slot):
            for one in self.copies(peer, peer, slot, slot):
                one.wait()

        self.each(visit)


def block_spread(here, same, blocks, into, sems):
    def copies(peer, sender, at, sem):
        return [
            remote(
                blocks.at[peer],
                into.at[at],
                sems.at[0, sem],
                sems.at[1, at],
                (here.dp, peer),
            )
        ]

    return Spread(here, same, copies)


def feed_spread(here, same, weights, into, sems):
    dp = lax.axis_size("dp")
    columns = into.shape[2] // (dp * len(weights))

    def copies(peer, sender, at, sem):
        made = []
        for kind, weight in enumerate(weights):
            for half in range(dp):
                part = kind * dp + half
                begin = pl.multiple_of((half * here.count + peer) * columns, columns)
                made.append(
                    remote(
                        weight.at[:, pl.ds(begin, columns)],
                        into.at[at, :, pl.ds(part * columns, columns)],
                        sems.at[0, sem, part],
                        sems.at[1, at, part],
                        (here.dp, peer),
                    )
                )
        return made

    return Spread(here, same, copies)


def gather_units(here, buf, send_sems, recv_sems, compute, between=None, ready=None, started=nothing, level=False):
    length = here.length
    last = length - 1
    steps = 2 * length
    mine = here.mine
    shorter = jnp.minimum(here.line, last - here.line)
    longer = jnp.where(here.line < last - here.line, 1, -1)

    def column(j):
        i = j - 1
        paired = jnp.where(i % 2 == 0, here.line - i // 2 - 1, here.line + i // 2 + 1)
        single = here.line + longer * (i - shorter + 1)
        return jnp.where(j == 0, here.line, jnp.where(i < 2 * shorter, paired, single))

    keep = buf.shape[2] * 3 // 4

    def copy(way, device, block, piece):
        if piece == 2:
            ref, sem = buf.at[block, 1, pl.ds(0, keep)], 1
        elif piece == 3:
            ref, sem = buf.at[block, 1, pl.ds(keep, buf.shape[2] - keep)], 2
        else:
            ref, sem = buf.at[block, piece], piece
        return remote(ref, ref, send_sems.at[way, block, sem], recv_sems.at[block, sem], device)

    def up(block, piece):
        return copy(0, here.above(), block, piece)

    def down(block, piece):
        return copy(1, here.below(), block, piece)

    def across(block, piece):
        return copy(2, here.across(), block, piece)

    def sideways(block, piece):
        return copy(3, here.sibling(), block, piece)

    def unit(number):
        in_column = (number % 2 == 1) & (number < steps - 1) | (number == 0)
        later = jnp.where(number == steps - 1, last, number // 2 - 1)
        line = column(jnp.where(in_column, (number + 1) // 2, later))
        pair = jnp.where(in_column, here.pair, 1 - here.pair)
        other = here.index(line, pair, 1 - here.core)
        sideways(other, 0).wait_recv()
        if level:
            whole = in_column | (line == here.line)
            pl.when(whole)(lambda: sideways(other, 1).wait_recv())

            @pl.when(jnp.logical_not(whole))
            def _():
                sideways(other, 2).wait_recv()
                sideways(other, 3).wait_recv()

        else:
            sideways(other, 1).wait_recv()

        compute(number, here.index(line, pair, 0))

    for piece in range(2):
        pl.when(here.line < last)(lambda piece=piece: up(mine, piece).start())
        pl.when(here.line > 0)(lambda piece=piece: down(mine, piece).start())
        across(mine, piece).start()
        sideways(mine, piece).start()
    started()
    beside = here.index(here.line, 1 - here.pair, here.core)

    def relay(far, pair, piece):
        @pl.when(here.line >= far)
        def _():
            block = here.index(here.line - far, pair, here.core)
            up(block, piece).wait_recv()
            pl.when(here.line < last)(lambda: up(block, piece).start())
            sideways(block, piece).start()

        @pl.when(here.line + far <= last)
        def _():
            block = here.index(here.line + far, pair, here.core)
            down(block, piece).wait_recv()
            pl.when(here.line > 0)(lambda: down(block, piece).start())
            sideways(block, piece).start()

    @pl.loop(0, length)
    def _(round):
        for part in range(2):
            step = 2 * round + part
            relay(round + 1, here.pair, part)

            @pl.when(round < last)
            def _():
                block = here.index(column(round + 1), here.pair, here.core)
                across(block, (2 if level else 1) if part else 0).start()

            block = here.index(column(round), 1 - here.pair, here.core)
            if part == 0 or not level:
                across(block, part).wait_recv()
                sideways(block, part).start()
            else:

                @pl.when(round == 0)
                def _():
                    across(beside, 1).wait_recv()
                    pl.when(here.line < last)(lambda: up(beside, 3).start())
                    pl.when(here.line > 0)(lambda: down(beside, 3).start())
                    sideways(beside, 1).start()

                @pl.when(round > 0)
                def _():
                    across(block, 2).wait_recv()
                    sideways(block, 2).start()
                    relay(round, 1 - here.pair, 3)

            if between is not None:
                between(step)
            if ready is None:
                unit(step)
            else:
                begin = jnp.maximum(2 * (step - ready), 0)
                end = jnp.maximum(2 * (step + 1 - ready), 0)

                @pl.loop(begin, end)
                def _(number):
                    unit(number)

    @pl.loop(0, length)
    def _(line):
        own = here.index(line, here.pair, here.core)
        other = here.index(line, 1 - here.pair, here.core)
        goes_up = (line <= here.line) & (here.line < last)
        goes_down = (line >= here.line) & (here.line > 0)

        @pl.when(goes_up)
        def _():
            up(own, 0).wait_send()
            up(own, 1).wait_send()
            if level:
                up(other, 3).wait_send()

        @pl.when(goes_down)
        def _():
            down(own, 0).wait_send()
            down(own, 1).wait_send()
            if level:
                down(other, 3).wait_send()

        across(own, 0).wait_send()
        sideways(own, 0).wait_send()
        sideways(own, 1).wait_send()
        sideways(other, 0).wait_send()

        if not level:
            across(own, 1).wait_send()
            sideways(other, 1).wait_send()
            return

        @pl.when(line == here.line)
        def _():
            across(own, 1).wait_send()
            sideways(other, 1).wait_send()

        @pl.when(line != here.line)
        def _():
            across(own, 2).wait_send()
            sideways(other, 2).wait_send()
            sideways(other, 3).wait_send()


def put_own(here, own_ref, buf):
    half = buf.shape[2]
    for part in range(2):
        buf[here.mine, part] = own_ref[pl.ds(part * half, half), :]


def gather_scratch(seq, rows, width):
    return [
        pltpu.VMEM((seq, 2, rows, width), BF16),
        pltpu.SemaphoreType.DMA((4, seq, 3)),
        pltpu.SemaphoreType.DMA((seq, 3)),
    ]


def unit_rows(first, rows):
    return pl.ds(pl.multiple_of(first * rows, 2 * rows), 2 * rows)


def take_unit(buf, first):
    blocks = buf[pl.ds(first, 2)]
    return blocks.reshape(-1, blocks.shape[-1])


class UnitStore:
    def __init__(self, buf, out_ref, sems):
        self.buf, self.out_ref, self.sems = buf, out_ref, sems

    def copies(self, number, first):
        half = self.buf.shape[2]
        made = []
        for block in range(2):
            for part in range(2):
                begin = ((first + block) * 2 + part) * half
                made.append(
                    pltpu.make_async_copy(
                        self.buf.at[first + block, part],
                        self.out_ref.at[pl.ds(pl.multiple_of(begin, half), half)],
                        self.sems.at[number, block, part],
                    )
                )
        return made

    def start(self, number, first):
        for one in self.copies(number, first):
            one.start()

    def finish(self):
        @pl.loop(0, self.sems.shape[0])
        def _(number):
            for one in self.copies(number, 0):
                one.wait()


def params(call_id, mebibytes):
    return pltpu.CompilerParams(
        collective_id=call_id, has_side_effects=True, vmem_limit_bytes=mebibytes << 20
    )


def cost(flops, bytes_accessed):
    return pl.CostEstimate(flops=flops, bytes_accessed=bytes_accessed, transcendentals=0)


VMEM = pl.BlockSpec(memory_space=pltpu.VMEM)
HBM = pl.BlockSpec(memory_space=pl.ANY)


def rotated(values, cosine, sine):
    cols = values.shape[1]
    lane = lax.broadcasted_iota(jnp.int32, values.shape, 1)
    ahead = pltpu.roll(values, cols - HEAD_DIM // 2, 1)
    behind = pltpu.roll(values, HEAD_DIM // 2, 1)
    swapped = jnp.where(lane % HEAD_DIM < HEAD_DIM // 2, ahead, behind)
    return values * cosine + swapped * sine


def upright(row):
    count = row.shape[1]
    shape = (count, count)
    same = lax.broadcasted_iota(jnp.int32, shape, 0) == lax.broadcasted_iota(jnp.int32, shape, 1)
    return jnp.sum(jnp.where(same, row.astype(F32), 0.0), axis=1, keepdims=True)


def flat(column):
    count = column.shape[0]
    shape = (count, count)
    same = lax.broadcasted_iota(jnp.int32, shape, 0) == lax.broadcasted_iota(jnp.int32, shape, 1)
    return jnp.sum(jnp.where(same, column, 0.0), axis=0, keepdims=True)


def project_kernel(
    lengths_ref,
    tokens_ref,
    cotangent_ref,
    query_ref,
    key_ref,
    value_ref,
    gate_ref,
    up_ref,
    gain_one_ref,
    gain_two_ref,
    freq_ref,
    down_ref,
    output_ref,
    normed_ref,
    grads_ref,
    q_ref,
    k_ref,
    v_ref,
    cos_ref,
    sin_ref,
    open_ref,
    weight_ref,
    gate_out_ref,
    up_out_ref,
    feed_ref,
    down_out_ref,
    output_out_ref,
    buf,
    send_sems,
    recv_sems,
    blocks,
    store_sems,
    near_sems,
    far_sems,
    feed_sems,
    swap_sems,
    local_sems,
    pair_sems,
    share_sems,
):
    here = Place()
    cols = q_ref.shape[1]
    rows = tokens_ref.shape[0]
    dp = here.dp
    ends = [lengths_ref[0, 0]]
    for j in range(1, DOCS):
        ends.append(ends[-1] + lengths_ref[0, j])

    def own_rows():
        chunk = 32

        @pl.loop(0, rows // chunk)
        def _(i):
            some = pl.ds(pl.multiple_of(i * chunk, chunk), chunk)
            values = tokens_ref[some, :].astype(F32)
            factor = lax.rsqrt(jnp.mean(values * values, axis=1, keepdims=True) + EPS)
            buf[here.mine, 0, some, :] = (values * factor).astype(BF16)
            shape = (chunk, cotangent_ref.shape[1])
            place = here.mine * rows + i * chunk + lax.broadcasted_iota(jnp.int32, shape, 0)
            grads = cotangent_ref[some, :].astype(F32)
            buf[here.mine, 1, some, :] = jnp.where(place < ends[-1], grads, 0.0).astype(BF16)

    def own_blocks():
        gain = upright(gain_one_ref[...])
        query = query_ref[...].astype(F32) * gain
        key = key_ref[...].astype(F32) * gain
        value = value_ref[...].astype(F32) * gain

        def heads(array, number, kept):
            parts = []
            for half in range(2):
                head = half * kept + number * kept // blocks.shape[0]
                parts.append(array[:, head * HEAD_DIM : (head + 1) * HEAD_DIM])
            return jnp.concatenate(parts, axis=1).astype(BF16)

        for number in range(blocks.shape[0]):
            blocks[number, :, :cols] = heads(query, number, HEADS // 2)
            array = value if number % 2 else key
            blocks[number, :, cols:] = heads(array, number, KV_HEADS // 2)

    def own_parts():
        own_blocks()
        own_rows()

    here.greet_all(own_parts)

    def weight_spread(same, sems):
        def copies(peer, sender, at, sem):
            return [
                remote(
                    blocks.at[peer],
                    weight_ref.at[dp, sender],
                    sems.at[0, sem],
                    sems.at[1, at],
                    (dp, peer),
                )
            ]

        return Spread(here, same, copies)

    near = weight_spread(True, near_sems)
    far = weight_spread(False, far_sems)
    swaps = []
    for number, (src, dst) in enumerate([(down_ref, down_out_ref), (output_ref, output_out_ref)]):
        swaps.append(
            remote(src, dst.at[dp], swap_sems.at[0, number], swap_sems.at[1, number], here.partner())
        )
        swaps.append(pltpu.make_async_copy(src, dst.at[dp], local_sems.at[number]))
    feed = feed_spread(here, True, (gate_out_ref, up_out_ref), feed_ref, feed_sems)
    columns = feed_ref.shape[2] // 4
    own_feed = []
    for kind, weight in enumerate((gate_out_ref, up_out_ref)):
        for half in range(2):
            part = kind * 2 + half
            begin = pl.multiple_of((half * here.count + here.mine) * columns, columns)
            own_feed.append(
                pltpu.make_async_copy(
                    weight.at[:, pl.ds(begin, columns)],
                    feed_ref.at[here.slot, :, pl.ds(part * columns, columns)],
                    local_sems.at[2 + part],
                )
            )

    def pair_copy(source, sender):
        return remote(
            weight_ref.at[source, sender],
            weight_ref.at[source, sender],
            pair_sems.at[0, sender],
            pair_sems.at[1, sender],
            here.partner(),
        )

    def own_tables():
        chunk = 128

        @pl.loop(0, open_ref.shape[0] // chunk)
        def _(i):
            some = pl.ds(pl.multiple_of(i * chunk, chunk), chunk)
            place = i * chunk + lax.broadcasted_iota(jnp.int32, (chunk, 1), 0)
            opening = jnp.zeros((chunk, 1), jnp.int32)
            for end in ends:
                opening = jnp.where(place >= end, end, opening)
            open_ref[some, :] = opening
            angles = (place - opening).astype(F32) * freq_ref[...]
            lane = lax.broadcasted_iota(jnp.int32, angles.shape, 1)
            sine = jnp.sin(angles)
            cos_ref[some, :] = jnp.cos(angles)
            sin_ref[some, :] = jnp.where(lane % HEAD_DIM < HEAD_DIM // 2, -sine, sine)

    def started():
        far.start()
        near.start()
        weight_ref[dp, here.mine] = blocks[here.mine]
        for one in swaps:
            one.start()
        chunk = 512

        @pl.loop(0, gate_ref.shape[1] // chunk)
        def _(i):
            some = pl.ds(pl.multiple_of(i * chunk, chunk), chunk)
            gain = upright(gain_two_ref[...])
            gate_out_ref[:, some] = (gate_ref[:, some].astype(F32) * gain).astype(BF16)
            up_out_ref[:, some] = (up_ref[:, some].astype(F32) * gain).astype(BF16)

        for one in own_feed:
            one.start()
        own_tables()

    def between(step):
        feed.start_some(step - (2 * here.length - 3), 3)

        @pl.when(step == 2)
        def _():
            near.finish()
            far.finish()

            @pl.loop(0, here.count)
            def _(sender):
                pair_copy(dp, sender).start()

        @pl.when(step == 4)
        def _():
            @pl.loop(0, here.count)
            def _(sender):
                pair_copy(1 - dp, sender).wait_recv()

    def share_copy(ref, number, where):
        return remote(
            ref.at[where],
            ref.at[where],
            share_sems.at[0, number],
            share_sems.at[1, number],
            here.sibling(),
        )

    def stores(number, first):
        made = []
        for block in range(2):
            where = pl.ds(pl.multiple_of((first + block) * rows, rows), rows)
            for part, out_ref in enumerate((normed_ref, grads_ref)):
                made.append(
                    pltpu.make_async_copy(
                        buf.at[first + block, part],
                        out_ref.at[where],
                        store_sems.at[number, block, part],
                    )
                )
        return made

    def compute(number, first):
        for one in stores(number, first):
            one.start()
        weight = weight_ref[...].reshape(-1, weight_ref.shape[-1])
        unit = buf[pl.ds(first, 2), 0]
        qkv = dot(unit.reshape(-1, unit.shape[-1]), weight)
        where = unit_rows(first, rows)
        cosine = cos_ref[where, :]
        sine = sin_ref[where, :]
        scale = BF16(1.0 / math.sqrt(HEAD_DIM))
        q_ref[where, :] = rotated(qkv[:, :cols], cosine, sine).astype(BF16) * scale
        for core, ref in enumerate((k_ref, v_ref)):

            @pl.when(here.core == core)
            def _():
                mine = qkv[:, cols:]
                ref[where, :] = (mine if core else rotated(mine, cosine, sine)).astype(BF16)
                share_copy(ref, number, where).start()

    gather_units(here, buf, send_sems, recv_sems, compute, between, here.length, started)

    @pl.loop(0, here.count)
    def _(sender):
        pair_copy(dp, sender).wait_send()

    @pl.loop(0, here.count // 2)
    def _(number):
        for one in stores(number, 0):
            one.wait()
        share_copy(k_ref, number, unit_rows(0, rows)).wait()

    feed.finish()
    for one in swaps + own_feed:
        one.wait()


def gather_project(
    lengths, tokens, cotangent, query, key, value, gate, up, gains, freq, down, output, call_id
):
    seq = lax.axis_size("seq")
    rows, width = tokens.shape
    cols = 2 * HEAD_DIM
    slab, ff = gate.shape
    bf16 = lambda *shape: jax.ShapeDtypeStruct(shape, BF16)
    f32 = lambda *shape: jax.ShapeDtypeStruct(shape, F32)
    all_rows = seq * rows
    dma = pltpu.SemaphoreType.DMA
    return pl.pallas_call(
        project_kernel,
        out_shape=[
            bf16(all_rows, width),
            bf16(all_rows, width),
            bf16(all_rows, cols),
            bf16(all_rows, cols),
            bf16(all_rows, cols),
            f32(all_rows, cols),
            f32(all_rows, cols),
            jax.ShapeDtypeStruct((all_rows, 1), jnp.int32),
            bf16(2, seq, slab, 2 * cols),
            bf16(slab, ff),
            bf16(slab, ff),
            bf16(seq // 2, slab, 4 * down.shape[0]),
            bf16(2, *down.shape),
            bf16(2, *output.shape),
        ],
        in_specs=[pl.BlockSpec(memory_space=pltpu.SMEM)] + [VMEM] * 10 + [HBM] * 2,
        out_specs=[HBM] * 2 + [VMEM] * 9 + [HBM] * 3,
        scratch_shapes=gather_scratch(seq, rows, width)
        + [
            pltpu.VMEM((seq, slab, 2 * cols), BF16),
            dma((seq // 2, 2, 2)),
            dma((2, seq // 2)),
            dma((2, seq // 2)),
            dma((2, seq // 2, 4)),
            dma((2, 2)),
            dma((6,)),
            dma((2, seq)),
            dma((2, seq // 2)),
        ],
        compiler_params=params(call_id, 60),
        cost_estimate=cost(2 * all_rows * width * 2 * cols, 8 * all_rows * width),
    )(lengths, tokens, cotangent, query, key, value, gate, up, *gains, freq, down, output)


ROW_CHUNK = 32


def norm_input_grad(values, upstream):
    factor = norm_factor(values)
    inner_mean = jnp.mean(upstream * values, axis=-1, keepdims=True)
    return factor * upstream - values * factor * factor * factor * inner_mean


def in_row_chunks(rows, chunk, visit):
    @pl.loop(0, rows // chunk)
    def _(i):
        visit(pl.ds(pl.multiple_of(i * chunk, chunk), chunk))


SCATTER_PARTS = 2
SCATTER_RING = 4
SCATTER_SCRATCH = 11


def scatter_rows_of_products(
    here,
    products,
    core_out,
    core_in,
    pair_out,
    pair_in,
    line_out,
    line_in,
    held,
    core_sems,
    pair_sems,
    line_sems,
    came_sems,
    first=None,
    between=nothing,
    filler=None,
):
    length = here.length
    parts = SCATTER_PARTS * len(products)
    rows, width = held.shape
    tile = min(width, 512)
    tiles = width // tile
    steps = length * parts

    def target(i):
        ups = length - 1 - here.line
        near = here.line < length // 2
        if_near = jnp.where(i < ups, length - 1 - i, i - ups)
        if_far = jnp.where(i < here.line, i, length - 1 - (i - here.line))
        return jnp.where(i == length - 1, here.line, jnp.where(near, if_near, if_far))

    def product(line, pair, core, part, use):
        first = pl.multiple_of(here.index(line, pair, core) * rows, rows)

        def one(number):
            transposed, a_ref, b_ref, _ = products[number]
            a = a_ref[pl.ds(first, rows), :]
            begin = (part - number * SCATTER_PARTS) * width

            @pl.loop(0, tiles)
            def _(t):
                into = pl.ds(pl.multiple_of(t * tile, tile), tile)
                cols = pl.ds(pl.multiple_of(begin + t * tile, tile), tile)
                use(dot_t(a, b_ref[cols, :]) if transposed else dot(a, b_ref[:, cols]), into)

        for number in range(len(products)):
            pl.when(part // SCATTER_PARTS == number)(functools.partial(one, number))

    def core_copy(slot):
        return remote(
            core_out.at[slot % SCATTER_RING],
            core_in.at[slot],
            core_sems.at[0, slot],
            core_sems.at[1, slot],
            here.sibling(),
        )

    def pair_copy(slot):
        return remote(
            pair_out.at[slot],
            pair_in.at[slot],
            pair_sems.at[0, slot],
            pair_sems.at[1, slot],
            here.across(),
        )

    def up_copy(slot, line, part):
        into = (line + 1) * parts + part
        return remote(
            line_out.at[slot], line_in.at[into], line_sems.at[slot], came_sems.at[into], here.above()
        )

    def down_copy(slot, line, part):
        into = line * parts + part
        return remote(
            line_out.at[slot], line_in.at[into], line_sems.at[slot], came_sems.at[into], here.below()
        )

    def for_sibling(step, pair, slot):
        pl.when(slot >= SCATTER_RING)(lambda: core_copy(slot - SCATTER_RING).wait_send())

        def use(value, cols):
            core_out[slot % SCATTER_RING, :, cols] = value.astype(BF16)

        product(target(step // parts), pair, 1 - here.core, step % parts, use)
        core_copy(slot).start()

    for_sibling(jnp.int32(0), 1 - here.pair, jnp.int32(0))

    @pl.loop(0, steps)
    def _(step):
        if first is not None:
            first(step)
        pl.when(step < steps - 1)(lambda: for_sibling(step + 1, 1 - here.pair, step + 1))
        core_copy(step).wait_recv()

        def use(value, cols):
            pair_out[step, :, cols] = (value + core_in[step, :, cols].astype(F32)).astype(BF16)

        product(target(step // parts), 1 - here.pair, here.core, step % parts, use)
        pair_copy(step).start()

    for_sibling(jnp.int32(0), here.pair, jnp.int32(steps))
    between()

    @pl.loop(0, steps)
    def _(step):
        pl.when(step < steps - 1)(lambda: for_sibling(step + 1, here.pair, steps + step + 1))
        core_copy(steps + step).wait_recv()
        line = target(step // parts)
        part = step % parts

        def use(value, cols):
            held[:, cols] = value + core_in[steps + step, :, cols].astype(F32)

        product(line, here.pair, here.core, part, use)
        if filler is not None:
            filler(step)
        pair_copy(step).wait_recv()
        from_above = (line <= here.line) & (here.line < length - 1)
        from_below = (line >= here.line) & (here.line > 0)
        held[...] += pair_in[step].astype(F32)

        @pl.when(from_above)
        def _():
            down_copy(0, line, part).wait_recv()
            held[...] += line_in[line * parts + part].astype(F32)

        @pl.when(from_below)
        def _():
            up_copy(0, line, part).wait_recv()
            held[...] += line_in[(line + 1) * parts + part].astype(F32)

        for number, (_, _, _, out_ref) in enumerate(products):

            @pl.when((line == here.line) & (part // SCATTER_PARTS == number))
            def _():
                begin = (part - number * SCATTER_PARTS) * width
                out_ref[:, pl.ds(pl.multiple_of(begin, width), width)] = held[...]

        @pl.when(line < here.line)
        def _():
            line_out[step] = held[...].astype(BF16)
            down_copy(step, line, part).start()

        @pl.when(line > here.line)
        def _():
            line_out[step] = held[...].astype(BF16)
            up_copy(step, line, part).start()

    @pl.loop(2 * steps - SCATTER_RING, 2 * steps)
    def _(slot):
        core_copy(slot).wait_send()

    @pl.loop(0, steps)
    def _(step):
        pair_copy(step).wait_send()
        line = target(step // parts)
        pl.when(line < here.line)(lambda: down_copy(step, 0, 0).wait_send())
        pl.when(line > here.line)(lambda: up_copy(step, 0, 0).wait_send())


def scatter_scratch(seq, rows, width, count=1):
    length = seq // 4
    parts = SCATTER_PARTS * count
    steps = length * parts
    block = (rows, width // SCATTER_PARTS)
    dma = pltpu.SemaphoreType.DMA
    return [
        pltpu.VMEM((SCATTER_RING, *block), BF16),
        pltpu.VMEM((2 * steps, *block), BF16),
        pltpu.VMEM((steps, *block), BF16),
        pltpu.VMEM((steps, *block), BF16),
        pltpu.VMEM((steps, *block), BF16),
        pltpu.VMEM(((length + 1) * parts, *block), BF16),
        pltpu.VMEM(block, F32),
        dma((2, 2 * steps)),
        dma((2, steps)),
        dma((steps,)),
        dma(((length + 1) * parts,)),
    ]


def scatter_cost(a, width):
    return cost(2 * a.shape[0] * a.shape[1] * width, 4 * a.shape[0] * width)


def scatter_both_kernel(
    back_hbm,
    turned_hbm,
    hidden_hbm,
    down_hbm,
    middle_ref,
    grads_hbm,
    normed_hbm,
    grad_ref,
    low_ref,
    mixed_ref,
    sums_ref,
    *scratch,
):
    here = Place()
    factors = scratch[SCATTER_SCRATCH : SCATTER_SCRATCH + 4]
    back_ref, turned_ref, hidden_ref, down_ref = factors
    normed, away, came, own, fetch_sems, swap_sems, own_sems = scratch[SCATTER_SCRATCH + 4 :]
    rows = grad_ref.shape[0]
    loads = [
        pltpu.make_async_copy(src, dst, own_sems.at[number])
        for number, (src, dst) in enumerate(
            zip((back_hbm, turned_hbm, hidden_hbm, down_hbm), factors)
        )
    ]
    own_copy = pltpu.make_async_copy(
        grads_hbm.at[pl.ds(pl.multiple_of(here.mine * rows, rows), rows)], own, own_sems.at[4]
    )
    for one in loads + [own_copy]:
        one.start()
    here.greet(partner=True)
    for one in loads[:2]:
        one.wait()

    def first(step):
        @pl.when(step == SCATTER_PARTS - 1)
        def _():
            for one in loads[2:]:
                one.wait()
    chunk = normed.shape[2]
    half = normed_hbm.shape[1] // 2
    chunks = half // chunk

    def fetch(number):
        dp = jnp.where(number < chunks, 1 - here.dp, here.dp)
        begin = dp * half + number % chunks * chunk
        return pltpu.make_async_copy(
            normed_hbm.at[:, pl.ds(pl.multiple_of(begin, chunk), chunk)],
            normed.at[number % 2],
            fetch_sems.at[number % 2],
        )

    def swap(i):
        some = pl.ds(pl.multiple_of(i * chunk, chunk), chunk)
        return remote(
            away.at[some], came.at[some], swap_sems.at[0, i], swap_sems.at[1, i], here.partner()
        )

    def part(number):
        fetch(number).wait()
        pl.when(number + 1 < 2 * chunks)(lambda: fetch(number + 1).start())
        return t_dot(normed[number % 2], back_ref[...])

    def filler(step):
        @pl.when(step < chunks)
        def _():
            some = pl.ds(pl.multiple_of(step * chunk, chunk), chunk)
            away[some, :] = part(step).astype(BF16)
            swap(step).start()

        @pl.when((step >= chunks) & (step < 3 * chunks) & (step % 2 == 0))
        def _():
            i = (step - chunks) // 2
            some = pl.ds(pl.multiple_of(i * chunk, chunk), chunk)
            kept = part(chunks + i)
            swap(i).wait()
            sums_ref[some, :] = (kept + came[some, :].astype(F32)).astype(BF16)

    fetch(jnp.int32(0)).start()
    scatter_rows_of_products(
        here,
        [(False, back_ref, turned_ref, grad_ref), (False, hidden_ref, down_ref, mixed_ref)],
        *scratch[:SCATTER_SCRATCH],
        first=first,
        filler=filler,
    )
    own_copy.wait()

    def add(some):
        grad = own[some, :].astype(F32) + norm_input_grad(middle_ref[some, :], grad_ref[some, :])
        grad_ref[some, :] = grad
        low_ref[some, :] = grad.astype(BF16)

    in_row_chunks(rows, ROW_CHUNK, add)


def product_scatter_both(back, turned, hidden, down, middle, grads, normed, call_id):
    seq = lax.axis_size("seq")
    rows = back.shape[0] // seq
    width = turned.shape[1]
    cols = back.shape[1]
    chunk = width // 8
    dma = pltpu.SemaphoreType.DMA
    return pl.pallas_call(
        scatter_both_kernel,
        out_shape=[
            jax.ShapeDtypeStruct((rows, width), F32),
            jax.ShapeDtypeStruct((rows, width), BF16),
            jax.ShapeDtypeStruct((rows, width), F32),
            jax.ShapeDtypeStruct((width // 2, cols), BF16),
        ],
        in_specs=[HBM] * 4 + [VMEM] + [HBM] * 2,
        out_specs=[VMEM] * 4,
        scratch_shapes=scatter_scratch(seq, rows, width, 2)
        + [pltpu.VMEM(array.shape, BF16) for array in (back, turned, hidden, down)]
        + [
            pltpu.VMEM((2, normed.shape[0], chunk), BF16),
            pltpu.VMEM((width // 2, cols), BF16),
            pltpu.VMEM((width // 2, cols), BF16),
            pltpu.VMEM((rows, width), BF16),
            dma((2,)),
            dma((2, 4)),
            dma((5,)),
        ],
        compiler_params=params(call_id, 60),
        cost_estimate=scatter_cost(back, 3 * width),
    )(back, turned, hidden, down, middle, grads, normed)


def feed_kernel(
    block,
    q_ref,
    k_ref,
    v_ref,
    open_ref,
    b_ref,
    tokens_ref,
    gate_hbm,
    up_hbm,
    near_hbm,
    grad_hbm,
    down_hbm,
    attended_ref,
    lse_ref,
    a_ref,
    middle_ref,
    normed_ref,
    hidden_out_ref,
    back_out_ref,
    turned_out_ref,
    *scratch,
):
    here = Place()
    (
        feed_ref,
        swap_sems,
        local_sems,
        far_sems,
        buf,
        send_sems,
        recv_sems,
        store_sems,
        grad_ref,
        down_ref,
        hidden_ref,
        back_ref,
        turned_ref,
        fetch_sems,
        out_sems,
    ) = scratch[SCATTER_SCRATCH:]
    slots, slab = near_hbm.shape[:2]
    rows, width = middle_ref.shape
    hidden = hidden_ref.shape[1]
    tile = 256

    def fetch(slot):
        return pltpu.make_async_copy(
            near_hbm.at[slot], feed_ref.at[here.dp, here.peer(slot, True)], local_sems.at[slot]
        )

    def swap(slot, same):
        place = feed_ref.at[here.dp, here.peer(slot, same)]
        half = 0 if same else 1
        return remote(
            place,
            place,
            swap_sems.at[0, half, slot],
            swap_sems.at[1, half, slot],
            here.partner(),
        )

    columns = hidden // 2

    def far_copies(peer, sender, at, sem):
        made = []
        for kind, weight in enumerate((gate_hbm, up_hbm)):
            for half in range(2):
                part = kind * 2 + half
                begin = pl.multiple_of((half * here.count + peer) * columns, columns)
                made.append(
                    remote(
                        weight.at[:, pl.ds(begin, columns)],
                        feed_ref.at[here.dp, sender, :, pl.ds(part * columns, columns)],
                        far_sems.at[0, sem, part],
                        far_sems.at[1, at, part],
                        (here.dp, peer),
                    )
                )
        return made

    far = Spread(here, False, far_copies)

    fetches = [
        pltpu.make_async_copy(down_hbm, down_ref, fetch_sems.at[0]),
        pltpu.make_async_copy(grad_hbm, grad_ref, fetch_sems.at[1]),
    ]
    pl.loop(0, slots)(lambda slot: fetch(slot).start())
    for one in fetches:
        one.start()
    here.call_all()

    @pl.loop(0, a_ref.shape[0] // block)
    def _(tile):
        some = pl.ds(pl.multiple_of(tile * block, block), block)
        attention_kernel(
            block,
            q_ref.at[some],
            k_ref,
            v_ref,
            open_ref.at[some],
            attended_ref.at[some],
            lse_ref.at[some],
            tile,
        )
        a_ref[some, :] = attended_ref[some, :].astype(BF16)

        @pl.when(tile == 0)
        def _():
            here.await_all()
            far.start()

            @pl.loop(0, slots)
            def _(slot):
                fetch(slot).wait()
                swap(slot, True).start()

    def between():
        far.finish()
        pl.loop(0, slots)(lambda slot: swap(slot, False).start())

    scatter_rows_of_products(
        here,
        [(False, a_ref, b_ref, middle_ref)],
        *scratch[:SCATTER_SCRATCH],
        between=between,
    )
    half = buf.shape[2]
    for part in range(2):

        @pl.loop(0, half // ROW_CHUNK)
        def _(i, part=part):
            into = pl.ds(pl.multiple_of(i * ROW_CHUNK, ROW_CHUNK), ROW_CHUNK)
            some = pl.ds(pl.multiple_of(part * half + i * ROW_CHUNK, ROW_CHUNK), ROW_CHUNK)
            middle = tokens_ref[some, :].astype(F32) + middle_ref[some, :]
            middle_ref[some, :] = middle
            buf[here.mine, part, into, :] = (middle * norm_factor(middle)).astype(BF16)

    def started():
        @pl.loop(0, slots)
        def _(slot):
            swap(slot, True).wait()
            swap(slot, False).wait()

        for one in fetches:
            one.wait()

    store = UnitStore(buf, normed_ref, store_sems)
    share = width // (2 * here.length)

    def outs(number, first):
        where = unit_rows(first, rows)
        some = pl.ds(pl.multiple_of(number * share, share), share)
        return [
            pltpu.make_async_copy(src, dst, out_sems.at[number, i])
            for i, (src, dst) in enumerate(
                [
                    (hidden_ref.at[where], hidden_out_ref.at[where]),
                    (back_ref.at[where], back_out_ref.at[where]),
                    (turned_ref.at[:, some], turned_out_ref.at[:, some]),
                ]
            )
        ]

    def compute(number, first):
        store.start(number, first)
        where = unit_rows(first, rows)
        normed = take_unit(buf, first)
        grad = grad_ref[where, :]

        @pl.loop(0, hidden // tile)
        def _(t):
            cols = pl.ds(pl.multiple_of(t * tile, tile), tile)
            later = pl.ds(pl.multiple_of(hidden + t * tile, tile), tile)
            gate = dot(normed, feed_ref[:, :, :, cols].reshape(width, tile))
            upward = dot(normed, feed_ref[:, :, :, later].reshape(width, tile))
            hidden_grad = dot_t(grad, down_ref[cols, :])
            sigmoid = jax.nn.sigmoid(gate)
            silu = gate * sigmoid
            hidden_ref[where, cols] = (silu * upward).astype(BF16)
            back_ref[where, cols] = (
                hidden_grad * upward * sigmoid * (1.0 + gate * (1.0 - sigmoid))
            ).astype(BF16)
            back_ref[where, later] = (hidden_grad * silu).astype(BF16)

        slabs = share // slab
        begin = number * slabs
        some = pl.ds(pl.multiple_of(number * share, share), share)
        weights = feed_ref[lax.div(begin, here.count), pl.ds(lax.rem(begin, here.count), slabs)]
        turned_ref[:, some] = weights.reshape(share, 2 * hidden).T
        for one in outs(number, first):
            one.start()

    gather_units(here, buf, send_sems, recv_sems, compute, started=started, level=True)

    @pl.loop(0, here.count // 2)
    def _(number):
        for one in outs(number, 0):
            one.wait()

    store.finish()


def feed_both_ways(
    queries, keys, values, opening, output, tokens, gate, up, near, grad_out, down, block, call_id
):
    seq = lax.axis_size("seq")
    rows, width = tokens.shape
    cols = queries.shape[1]
    hidden = down.shape[0]
    all_rows = seq * rows
    bf16 = lambda *shape: jax.ShapeDtypeStruct(shape, BF16)
    f32 = lambda *shape: jax.ShapeDtypeStruct(shape, F32)
    dma = pltpu.SemaphoreType.DMA
    return pl.pallas_call(
        functools.partial(feed_kernel, block),
        out_shape=[
            f32(all_rows, cols),
            f32(all_rows, cols // HEAD_DIM),
            bf16(all_rows, cols),
            f32(rows, width),
            bf16(all_rows, width),
            bf16(all_rows, hidden),
            bf16(all_rows, 2 * hidden),
            bf16(2 * hidden, width),
        ],
        in_specs=[VMEM] * 6 + [HBM] * 5,
        out_specs=[VMEM] * 4 + [HBM] * 4,
        scratch_shapes=scatter_scratch(seq, rows, width)
        + [
            pltpu.VMEM((2, seq, *near.shape[1:]), BF16),
            dma((2, 2, seq // 2)),
            dma((seq // 2,)),
            dma((2, seq // 2, 4)),
        ]
        + gather_scratch(seq, rows // 2, width)
        + [
            dma((seq // 2, 2, 2)),
            pltpu.VMEM((all_rows, width), BF16),
            pltpu.VMEM((hidden, width), BF16),
            pltpu.VMEM((all_rows, hidden), BF16),
            pltpu.VMEM((all_rows, 2 * hidden), BF16),
            pltpu.VMEM((2 * hidden, width), BF16),
            dma((2,)),
            dma((seq // 2, 3)),
        ],
        compiler_params=params(call_id, 62),
        cost_estimate=cost(8 * all_rows * width * hidden, 8 * all_rows * width),
    )(queries, keys, values, opening, output, tokens, gate, up, near, grad_out, down)


def back_kernel(
    block,
    own_ref,
    weight_ref,
    low_ref,
    q_ref,
    k_ref,
    v_ref,
    att_ref,
    lse_ref,
    open_ref,
    cos_ref,
    sin_ref,
    heads_ref,
    hidden_hbm,
    out_grad_hbm,
    blocks_ref,
    normed_hbm,
    output_kept_ref,
    output_came_ref,
    down_kept_ref,
    down_came_ref,
    near_ref,
    far_ref,
    out_ref,
    qkv_ref,
    *scratch,
):
    here = Place()
    (
        buf,
        send_sems,
        recv_sems,
        part,
        hidden_ref,
        out_grad,
        grad_ref,
        output_away,
        down_away,
        dq_ref,
        dk_ref,
        dv_ref,
        share_out,
        share_in,
        back_ref,
        normed,
        kept,
        away,
        came,
        sums,
        near_sems,
        far_sems,
        local_sems,
        swap_sems,
        share_sems,
        fetch_sems,
        sum_sems,
        sum_near_sems,
        sum_far_sems,
    ) = scratch[SCATTER_SCRATCH:]
    rows, width = own_ref.shape
    cols = q_ref.shape[1]
    tile = 512
    units = 2 * here.length
    share = width // units

    hidden_copy = pltpu.make_async_copy(hidden_hbm, hidden_ref, local_sems.at[0])
    own_copy = pltpu.make_async_copy(
        blocks_ref.at[here.mine], near_ref.at[here.slot], local_sems.at[1]
    )
    near = block_spread(here, True, blocks_ref, near_ref, near_sems)
    far = block_spread(here, False, blocks_ref, far_ref, far_sems)
    swaps = [
        remote(src, dst, swap_sems.at[0, number], swap_sems.at[1, number], here.partner())
        for number, (src, dst) in enumerate(
            [(down_away, down_came_ref), (output_away, output_came_ref)]
        )
    ]

    def out_grad_copy(number):
        some = pl.ds(pl.multiple_of(number * share, share), share)
        slot = number % 2
        return pltpu.make_async_copy(
            out_grad_hbm.at[:, some], out_grad.at[slot], fetch_sems.at[0, slot]
        )

    hidden_copy.start()
    own_copy.start()
    out_grad_copy(jnp.int32(0)).start()
    here.call_all()
    put_own(here, own_ref, buf)
    part[...] = jnp.zeros_like(part)
    here.await_all()

    def split(values, kept_to, away_to, some):
        half = values.shape[0] // 2
        top, bottom = values[:half], values[half:]
        kept_to[:, some] = jnp.where(here.dp == 0, top, bottom)
        away_to[:, some] = jnp.where(here.dp == 0, bottom, top).astype(BF16)

    def compute(number, first):
        where = unit_rows(first, rows)
        unit = take_unit(buf, first)
        grad_ref[where, :] = dot_t(unit, weight_ref[...]).astype(BF16)
        attended = low_ref[where, :]
        for t in range(width // tile):
            some = slice(t * tile, (t + 1) * tile)
            part[:, some] += t_dot(attended, unit[:, some])
        pl.when(number == 0)(hidden_copy.wait)
        out_grad_copy(number).wait()
        pl.when(number + 1 < units)(lambda: out_grad_copy(number + 1).start())
        some = pl.ds(pl.multiple_of(number * share, share), share)
        split(t_dot(hidden_ref[...], out_grad[number % 2]), down_kept_ref, down_away, some)

    gather_units(here, buf, send_sems, recv_sems, compute, level=True)
    far.start()
    near.start()
    for t in range(width // tile):
        some = slice(t * tile, (t + 1) * tile)
        split(part[:, some], output_kept_ref, output_away, some)
    for one in swaps:
        one.start()

    tiles = q_ref.shape[0] // block
    scale = 1.0 / math.sqrt(HEAD_DIM)

    @pl.loop(0, tiles)
    def _(i):
        some = pl.ds(pl.multiple_of(i * block, block), block)
        attention_back_kernel(
            block,
            q_ref.at[some],
            k_ref,
            v_ref,
            grad_ref.at[some],
            att_ref.at[some],
            lse_ref.at[some],
            open_ref.at[some],
            dq_ref,
            dk_ref,
            dv_ref,
            i,
        )
        turned = rotated(dq_ref[...] * scale, cos_ref[some, :], -sin_ref[some, :])
        back_ref[some, :cols] = turned.astype(BF16)

    def share_copy(i):
        some = pl.ds(pl.multiple_of(i * block, block), block)
        return remote(
            share_out.at[some],
            share_in.at[some],
            share_sems.at[0, i],
            share_sems.at[1, i],
            here.sibling(),
        )

    @pl.loop(0, tiles)
    def _(i):
        some = pl.ds(pl.multiple_of(i * block, block), block)
        share_out[some, :] = jnp.where(here.core == 0, dv_ref[some, :], dk_ref[some, :]).astype(BF16)
        share_copy(i).start()

    @pl.loop(0, tiles)
    def _(i):
        some = pl.ds(pl.multiple_of(i * block, block), block)
        share_copy(i).wait()
        other = share_in[some, :].astype(F32)
        keys = rotated(dk_ref[some, :] + other, cos_ref[some, :], -sin_ref[some, :])
        back_ref[some, cols:] = jnp.where(here.core == 0, keys, dv_ref[some, :] + other).astype(BF16)

    swap = remote(away, came, sum_sems.at[0], sum_sems.at[1], here.partner())
    sum_near = block_spread(here, True, sums, qkv_ref.at[0], sum_near_sems)
    sum_far = block_spread(here, False, sums, qkv_ref.at[1], sum_far_sems)
    half = away.shape[0]
    chunk = normed.shape[2]
    chunks = half // chunk

    def normed_copy(number):
        dp = jnp.where(number < chunks, 1 - here.dp, here.dp)
        begin = dp * half + number % chunks * chunk
        slot = number % 2
        return pltpu.make_async_copy(
            normed_hbm.at[:, pl.ds(pl.multiple_of(begin, chunk), chunk)],
            normed.at[slot],
            fetch_sems.at[1, slot],
        )

    def heads_part(number):
        normed_copy(number).wait()
        pl.when(number + 1 < 2 * chunks)(lambda: normed_copy(number + 1).start())
        return t_dot(normed[number % 2], back_ref[...])

    normed_copy(jnp.int32(0)).start()

    def first(step):
        @pl.when(step == 2)
        def _():
            @pl.loop(0, chunks)
            def _(i):
                some = pl.ds(pl.multiple_of(i * chunk, chunk), chunk)
                away[some, :] = heads_part(i).astype(BF16)

            swap.start()

    def own_share():
        @pl.loop(0, chunks)
        def _(i):
            kept[pl.ds(pl.multiple_of(i * chunk, chunk), chunk), :] = heads_part(chunks + i)

    begin = 2
    each = 3

    def filler(step):
        @pl.when(step == begin)
        def _():
            swap.wait_recv()
            slab = sums.shape[1]

            @pl.loop(0, here.count)
            def _(i):
                some = pl.ds(pl.multiple_of(i * slab, slab), slab)
                sums[i] = (kept[some, :] + came[some, :].astype(F32)).astype(BF16)

            qkv_ref[0, here.slot] = sums[here.mine]

        @pl.when(step > begin)
        def _():
            @pl.loop(0, each)
            def _(i):
                number = (step - begin - 1) * each + i
                pl.when(number < sum_far.slots)(lambda: sum_far.start_one(number))

                @pl.when((number >= sum_far.slots) & (number < 2 * sum_far.slots - 1))
                def _():
                    sum_near.start_one(number - sum_far.slots + 1)

    scatter_rows_of_products(
        here,
        [(True, back_ref, heads_ref, out_ref)],
        *scratch[:SCATTER_SCRATCH],
        first=first,
        between=own_share,
        filler=filler,
    )
    swap.wait_send()
    for one in swaps:
        one.wait()
    near.finish()
    far.finish()
    own_copy.wait()
    sum_near.finish()
    sum_far.finish()


def attention_backwards(
    own,
    weight,
    attended,
    queries,
    keys,
    values,
    attended_sum,
    log_total,
    opening,
    cosine,
    sine,
    heads,
    hidden,
    grad_out,
    blocks,
    normed,
    block,
    call_id,
):
    seq = lax.axis_size("seq")
    rows, width = own.shape
    all_rows, cols = queries.shape
    slab = blocks.shape[1]
    half_hidden = hidden.shape[1] // 2
    chunk = width // 8
    bf16 = lambda *shape: jax.ShapeDtypeStruct(shape, BF16)
    f32 = lambda *shape: jax.ShapeDtypeStruct(shape, F32)
    dma = pltpu.SemaphoreType.DMA
    return pl.pallas_call(
        functools.partial(back_kernel, block),
        out_shape=[
            f32(cols // 2, width),
            bf16(cols // 2, width),
            f32(half_hidden, width),
            bf16(half_hidden, width),
            bf16(seq // 2, *blocks.shape[1:]),
            bf16(seq // 2, *blocks.shape[1:]),
            f32(rows, width),
            bf16(2, seq // 2, slab, 2 * cols),
        ],
        in_specs=[VMEM] * 12 + [HBM] * 4,
        out_specs=[VMEM, HBM, VMEM, HBM, HBM, HBM, VMEM, VMEM],
        scratch_shapes=scatter_scratch(seq, rows, width)
        + gather_scratch(seq, rows // 2, width)
        + [
            pltpu.VMEM((cols, width), F32),
            pltpu.VMEM(hidden.shape, BF16),
            pltpu.VMEM((2, all_rows, width // (seq // 2)), BF16),
            pltpu.VMEM((all_rows, cols), BF16),
            pltpu.VMEM((cols // 2, width), BF16),
            pltpu.VMEM((half_hidden, width), BF16),
            pltpu.VMEM((block, cols), F32),
            pltpu.VMEM((all_rows, cols), F32),
            pltpu.VMEM((all_rows, cols), F32),
            pltpu.VMEM((all_rows, cols), BF16),
            pltpu.VMEM((all_rows, cols), BF16),
            pltpu.VMEM((all_rows, 2 * cols), BF16),
            pltpu.VMEM((2, all_rows, chunk), BF16),
            pltpu.VMEM((width // 2, 2 * cols), F32),
            pltpu.VMEM((width // 2, 2 * cols), BF16),
            pltpu.VMEM((width // 2, 2 * cols), BF16),
            pltpu.VMEM((seq, slab, 2 * cols), BF16),
            dma((2, seq // 2)),
            dma((2, seq // 2)),
            dma((2,)),
            dma((2, 2)),
            dma((2, all_rows // block)),
            dma((2, 2)),
            dma((2,)),
            dma((2, seq // 2)),
            dma((2, seq // 2)),
        ],
        compiler_params=params(call_id, 62),
        cost_estimate=cost(12 * all_rows * width * cols, 12 * all_rows * width),
    )(
        own,
        weight,
        attended,
        queries,
        keys,
        values,
        attended_sum,
        log_total,
        opening,
        cosine,
        sine,
        heads,
        hidden,
        grad_out,
        blocks,
        normed,
    )


UNPACK_LINES = 4


def unpack_kernel(
    pair_ref,
    near_gate_ref,
    far_gate_ref,
    near_up_ref,
    far_up_ref,
    gate_ref,
    up_ref,
    qkv_ref,
    query_ref,
    key_ref,
    value_ref,
    gain_one_ref,
    gain_two_ref,
    tokens_ref,
    middle_ref,
    mixed_sum_ref,
    middle_grad_ref,
    upstream_ref,
    down_kept_ref,
    down_came_ref,
    output_kept_ref,
    output_came_ref,
    gate_out_ref,
    up_out_ref,
    query_out_ref,
    key_out_ref,
    value_out_ref,
    one_out_ref,
    two_out_ref,
    mixed_ref,
    token_grad_ref,
    down_out_ref,
    output_out_ref,
    total_two,
):
    pair = pair_ref[0]
    dp = lax.axis_size("dp")
    length = qkv_ref.shape[1] // 2
    slab = qkv_ref.shape[2]
    step = pl.program_id(0) * pl.num_programs(1) + pl.program_id(1)
    columns = near_gate_ref.shape[2]

    def along(grad, weight):
        return jnp.sum(grad * weight.astype(F32), axis=1, keepdims=True)

    @pl.when(step == 0)
    def _():
        total_two[...] = jnp.zeros_like(total_two)
        total = jnp.zeros((slab, 1), F32)
        gain = upright(gain_one_ref[...])

        def put(out_ref, weight_ref, begin, grad):
            cols = slice(begin, begin + grad.shape[1])
            out_ref[:, cols] = grad * gain
            return along(grad, weight_ref[:, cols])

        pairs = [{}, {}]
        for line in range(length):
            rows = []
            for number in range(4):
                slot = line * 2 + number % 2
                near, far = qkv_ref[0, slot].astype(F32), qkv_ref[1, slot].astype(F32)
                rows.append(jnp.where(number // 2 == pair, near, far))
            kv = [rows[core] + rows[core + 2] for core in range(2)]
            for half in range(dp):
                cols = slice(half * HEAD_DIM, (half + 1) * HEAD_DIM)
                for number in (0, 2):
                    two = jnp.concatenate([rows[number][:, cols], rows[number + 1][:, cols]], axis=1)
                    begin = (half * length * 4 + line * 4 + number) * HEAD_DIM
                    total = total + put(query_out_ref, query_ref, begin, two)
                for kind in range(2):
                    begin = (dp + half) * HEAD_DIM
                    pairs[kind][half, line] = kv[kind][:, begin : begin + HEAD_DIM]
        for kind, (out_ref, weight_ref) in enumerate(
            [(key_out_ref, key_ref), (value_out_ref, value_ref)]
        ):
            for half in range(dp):
                for line in range(0, length, 2):
                    two = [pairs[kind][half, line], pairs[kind][half, line + 1]]
                    begin = (half * length + line) * HEAD_DIM
                    total = total + put(
                        out_ref, weight_ref, begin, jnp.concatenate(two, axis=1)
                    )
        one_out_ref[...] = flat(total)

    mixed_ref[...] = middle_ref[...] + mixed_sum_ref[...]
    token_grad_ref[...] = middle_grad_ref[...] + norm_input_grad(
        tokens_ref[...].astype(F32), upstream_ref[...]
    )
    down_out_ref[...] = down_kept_ref[...] + down_came_ref[...].astype(F32)
    output_out_ref[...] = output_kept_ref[...] + output_came_ref[...].astype(F32)
    gain_two = upright(gain_two_ref[...])
    total = jnp.zeros((slab, 1), F32)
    for near_ref, far_ref, weight_ref, out_ref in (
        (near_gate_ref, far_gate_ref, gate_ref, gate_out_ref),
        (near_up_ref, far_up_ref, up_ref, up_out_ref),
    ):
        for number in range(2 * near_ref.shape[0]):
            slot = number // 4 * 2 + number % 2
            near, far = near_ref[slot].astype(F32), far_ref[slot].astype(F32)
            grad = jnp.where(number // 2 % 2 == pair, near, far)
            cols = slice(number * columns, (number + 1) * columns)
            total = total + along(grad, weight_ref[:, cols])
            out_ref[:, cols] = grad * gain_two
    total_two[...] += total

    @pl.when(step == pl.num_programs(0) * pl.num_programs(1) - 1)
    def _():
        two_out_ref[...] = flat(total_two[...])


def unpack(pair, near, far, gate, up, qkv, query, key, value, gain_one, gain_two, *rows):
    dp = lax.axis_size("dp")
    seq = lax.axis_size("seq")
    slab, ff = gate.shape
    length = seq // 4 // UNPACK_LINES
    columns = ff // (dp * seq)
    whole = lambda array: pl.BlockSpec(array.shape, lambda j, i: (0,) * array.ndim)
    block = lambda kind: pl.BlockSpec(
        (2 * UNPACK_LINES, slab, columns), lambda j, i: (i, 0, kind * dp + j)
    )
    tile = pl.BlockSpec((slab, 4 * UNPACK_LINES * columns), lambda j, i: (0, j * length + i))
    f32 = lambda array: jax.ShapeDtypeStruct(array.shape, F32)
    outs = [f32(gate), f32(up), f32(query), f32(key), f32(value), f32(gain_one), f32(gain_two)]
    sums = [f32(rows[0]), f32(rows[0]), f32(rows[5]), f32(rows[7])]
    steps = dp * length
    strip = lambda array: pl.BlockSpec(
        (array.shape[0] // steps, array.shape[1]), lambda j, i: (j * length + i, 0)
    )
    return pl.pallas_call(
        unpack_kernel,
        grid=(dp, length),
        in_specs=[pl.BlockSpec(memory_space=pltpu.SMEM)]
        + [block(0), block(0), block(1), block(1), tile, tile]
        + [whole(array) for array in (qkv, query, key, value, gain_one, gain_two)]
        + [strip(array) for array in rows],
        out_specs=[tile, tile]
        + [whole(array) for array in outs[2:]]
        + [strip(array) for array in sums],
        out_shape=outs + sums,
        scratch_shapes=[pltpu.VMEM((slab, 1), F32)],
        compiler_params=pltpu.CompilerParams(vmem_limit_bytes=60 << 20),
        cost_estimate=cost(slab * ff, 16 * slab * ff),
    )(
        pair,
        near,
        far,
        near,
        far,
        gate,
        up,
        qkv,
        query,
        key,
        value,
        gain_one,
        gain_two,
        *rows,
    )


def swap_dp(values):
    count = lax.axis_size("dp")
    return lax.ppermute(values, "dp", [(i, (i + 1) % count) for i in range(count)])


def gather_dp(values):
    return lax.all_gather(values, "dp", axis=0, tiled=True)


def sum_dp(partial):
    half = partial.shape[0] // 2
    mine = lax.axis_index("dp")
    away = lax.dynamic_slice_in_dim(partial, (1 - mine) * half, half, 0).astype(BF16)
    kept = lax.dynamic_slice_in_dim(partial, mine * half, half, 0)
    return kept + swap_dp(away).astype(F32)


def gather_rows(values):
    return lax.all_gather(values, "seq", axis=0, tiled=True)


def scatter_rows(partial):
    return lax.psum_scatter(partial.astype(BF16), "seq", scatter_dimension=0, tiled=True).astype(F32)


def exchange(blocks):
    return lax.all_to_all(blocks, "seq", split_axis=0, concat_axis=0, tiled=True)


def norm_factor(values):
    return lax.rsqrt(jnp.mean(values * values, axis=-1, keepdims=True) + EPS)


def norm_back(inputs, factor, gain_row, upstream):
    scaled_up = gain_row * upstream
    inner_mean = jnp.mean(scaled_up * inputs, axis=-1, keepdims=True)
    grad_in = factor * scaled_up - inputs * factor * factor * factor * inner_mean
    grad_gain = jnp.sum(upstream * inputs * factor, axis=0)
    return grad_in, grad_gain


def plain_shards(
    tokens,
    cotangent,
    doc_lengths,
    attn_gain,
    mlp_gain,
    query_weight,
    key_weight,
    value_weight,
    output_weight,
    gate_weight,
    up_weight,
    down_weight,
):
    dp = lax.axis_size("dp")
    seq = lax.axis_size("seq")
    mine = lax.axis_index("seq")
    tok_count, width = tokens.shape
    rows = tok_count * seq
    slab = query_weight.shape[0]
    share = HEAD_DIM // slab
    half_heads = HEADS // dp
    half_kv = KV_HEADS // dp
    hidden_dev = down_weight.shape[0]
    block = 512

    doc_ends = jnp.cumsum(doc_lengths[0])
    place = jnp.arange(rows, dtype=jnp.int32)
    passed = doc_ends[None, :] <= place[:, None]
    opening = jnp.max(jnp.where(passed, doc_ends[None, :], 0), axis=1)
    position = place - opening
    keeping = place < doc_ends[DOCS - 1]
    angles = position.astype(F32)[:, None] * rotary_table(HEAD_DIM)[None, :]
    cosine = jnp.cos(angles)
    sine = jnp.sin(angles)
    cos_heads = jnp.tile(cosine, (1, 2 * dp))
    sin_heads = jnp.tile(jnp.concatenate([-sine, sine], axis=1), (1, dp))
    own_keeping = lax.dynamic_slice_in_dim(keeping, mine * tok_count, tok_count, 0)

    def head_columns(weight, kept):
        split = weight.reshape(slab, dp, kept, HEAD_DIM)
        return jnp.repeat(split, seq // kept, axis=2)

    qkv_blocks = jnp.stack(
        [
            head_columns(query_weight, half_heads),
            head_columns(key_weight, half_kv),
            head_columns(value_weight, half_kv),
        ],
        axis=1,
    )
    qkv_blocks = jnp.transpose(qkv_blocks, (3, 0, 1, 2, 4)).reshape(seq * slab, 3 * dp * HEAD_DIM)
    qkv_weight = gather_dp(exchange(qkv_blocks))
    feed_blocks = jnp.stack(
        [w.reshape(slab, dp, seq, hidden_dev) for w in (gate_weight, up_weight)], axis=1
    )
    feed_blocks = jnp.transpose(feed_blocks, (3, 0, 1, 2, 4)).reshape(
        seq * slab, 2 * dp * hidden_dev
    )
    feed_weight = gather_dp(exchange(feed_blocks))
    down_own = gather_dp(down_weight)
    output_own = output_weight
    if share > 1:
        groups = [list(range(i, i + share)) for i in range(0, seq, share)]
        output_own = lax.all_gather(
            output_own, "seq", axis=0, tiled=True, axis_index_groups=groups
        )
    output_own = gather_dp(output_own)
    gains = lax.all_gather(
        jnp.stack([attn_gain, mlp_gain]), ("dp", "seq"), axis=1, tiled=True
    ).astype(F32)
    gain_one, gain_two = gains[0], gains[1]

    inputs_all = gather_rows(tokens).astype(F32)
    normed_one = (inputs_all * norm_factor(inputs_all) * gain_one).astype(BF16)
    qkv = dot(normed_one, qkv_weight)
    head_cols = dp * HEAD_DIM
    query_lin, key_lin = qkv[:, :head_cols], qkv[:, head_cols : 2 * head_cols]
    values = qkv[:, 2 * head_cols :].astype(BF16)
    scale = 1.0 / math.sqrt(HEAD_DIM)
    queries = (query_lin * cos_heads + swap_halves(query_lin) * sin_heads).astype(BF16) * BF16(scale)
    keys = (key_lin * cos_heads + swap_halves(key_lin) * sin_heads).astype(BF16)
    attended_sum, log_total = attention(queries, keys, values, opening[:, None], block)
    if share > 1:
        own_rows = ((place // tok_count) % share == mine % share)[:, None]
        attended_sum = jnp.where(own_rows, attended_sum, 0.0)
    attended = attended_sum.astype(BF16)
    inputs = tokens.astype(F32)
    middle = inputs + scatter_rows(dot(attended, output_own))

    factor_two = norm_factor(middle)
    normed_two = gather_rows((middle * factor_two * gain_two).astype(BF16))
    grad_own = jnp.where(own_keeping[:, None], cotangent, BF16(0))
    grad_out = gather_rows(grad_own)
    feed = dot(normed_two, feed_weight)
    feed_cols = dp * hidden_dev
    gate_lin, upward = feed[:, :feed_cols], feed[:, feed_cols:]
    sigmoid = jax.nn.sigmoid(gate_lin)
    hidden = (gate_lin * sigmoid * upward).astype(BF16)
    hidden_grad = dot_t(grad_out, down_own)
    gate_back = (hidden_grad * upward * sigmoid * (1.0 + gate_lin * (1.0 - sigmoid))).astype(BF16)
    up_back = (hidden_grad * gate_lin * sigmoid).astype(BF16)
    feed_back = jnp.concatenate([gate_back, up_back], axis=1)
    normed_two_grad = scatter_rows(dot_t(feed_back, feed_weight))
    mixed = middle + scatter_rows(dot(hidden, down_own))
    middle_in, gain_two_part = norm_back(middle, factor_two, gain_two, normed_two_grad)
    middle_grad = grad_own.astype(F32) + middle_in
    middle_back = gather_rows(middle_grad.astype(BF16))

    attended_grad = dot_t(middle_back, output_own).astype(BF16)
    if share > 1:
        attended_grad = jnp.where(own_rows, attended_grad, BF16(0))
    query_acc, key_acc, value_acc = attention_back(
        queries, keys, values, attended_grad, attended_sum, log_total, opening[:, None], block
    )
    query_acc = query_acc * scale
    query_back = query_acc * cos_heads - swap_halves(query_acc) * sin_heads
    key_back = key_acc * cos_heads - swap_halves(key_acc) * sin_heads
    qkv_back = jnp.concatenate([query_back, key_back, value_acc], axis=1).astype(BF16)
    normed_one_grad = scatter_rows(dot_t(qkv_back, qkv_weight))
    input_in, gain_one_part = norm_back(inputs, norm_factor(inputs), gain_one, normed_one_grad)
    token_grad = middle_grad + input_in

    feed_grad = exchange(sum_dp(t_dot(normed_two, feed_back)).astype(BF16)).astype(F32)
    feed_grad = feed_grad.reshape(seq, slab, 2, dp, hidden_dev)
    feed_grad = jnp.transpose(feed_grad, (2, 1, 3, 0, 4)).reshape(2, slab, dp * seq * hidden_dev)
    down_grad = sum_dp(t_dot(hidden, grad_out))
    output_part = t_dot(attended, middle_back)
    if share > 1:
        split = output_part.reshape(dp, share, slab, width)
        split = jnp.transpose(split, (1, 0, 2, 3)).reshape(share * dp * slab, width)
        output_part = lax.psum_scatter(
            split, "seq", scatter_dimension=0, tiled=True, axis_index_groups=groups
        )
    output_grad = sum_dp(output_part)
    qkv_grad = exchange(sum_dp(t_dot(normed_one, qkv_back)).astype(BF16)).astype(F32)
    qkv_grad = qkv_grad.reshape(seq, slab, 3, dp, HEAD_DIM)

    def own_columns(part, kept):
        summed = jnp.sum(part.reshape(kept, seq // kept, slab, dp, HEAD_DIM), axis=1)
        return jnp.transpose(summed, (1, 2, 0, 3)).reshape(slab, dp * kept * HEAD_DIM)

    query_grad = own_columns(qkv_grad[:, :, 0], half_heads)
    key_grad = own_columns(qkv_grad[:, :, 1], half_kv)
    value_grad = own_columns(qkv_grad[:, :, 2], half_kv)
    gain_parts = lax.psum(jnp.stack([gain_one_part, gain_two_part]), ("dp", "seq"))
    own = lax.axis_index("dp") * seq + mine
    gain_grads = lax.dynamic_slice_in_dim(gain_parts, own * slab, slab, 1)
    return (
        mixed,
        token_grad,
        gain_grads[0],
        gain_grads[1],
        query_grad,
        key_grad,
        value_grad,
        output_grad,
        feed_grad[0],
        feed_grad[1],
        down_grad,
    )


def frequencies():
    exponent = np.arange(0, HEAD_DIM, 2, dtype=np.float32) / np.float32(HEAD_DIM)
    inverse = np.power(np.float32(500000.0), -exponent)
    wavelength = np.float32(2.0 * math.pi) / inverse
    smooth = (np.float32(8192.0) / wavelength - np.float32(1.0)) / np.float32(3.0)
    blended = (np.float32(1.0) - smooth) * inverse / np.float32(32.0) + smooth * inverse
    scaled = np.where(
        wavelength < 2048.0,
        inverse,
        np.where(wavelength > 8192.0, inverse / np.float32(32.0), blended),
    )
    return np.tile(scaled.astype(np.float32), 4)


FREQUENCIES = frequencies()


def shards(
    tokens,
    cotangent,
    doc_lengths,
    attn_gain,
    mlp_gain,
    query_weight,
    key_weight,
    value_weight,
    output_weight,
    gate_weight,
    up_weight,
    down_weight,
):
    dp = lax.axis_size("dp")
    seq = lax.axis_size("seq")
    mine = lax.axis_index("seq")
    tok_count, width = tokens.shape
    slab = query_weight.shape[0]
    block = 512
    gain_one = attn_gain[None, :]
    gain_two = mlp_gain[None, :]

    (
        normed_one,
        grad_out,
        queries,
        keys,
        values,
        cosine,
        sine,
        opening,
        qkv_weight,
        gate_scaled,
        up_scaled,
        feed_near,
        down_own,
        output_own,
    ) = gather_project(
        doc_lengths,
        tokens,
        cotangent,
        query_weight,
        key_weight,
        value_weight,
        gate_weight,
        up_weight,
        (gain_one, gain_two),
        jnp.asarray(FREQUENCIES)[None, :],
        down_weight,
        output_weight,
        0,
    )
    qkv_weight = qkv_weight.reshape(width, -1)
    down_own = down_own.reshape(-1, width)
    output_own = output_own.reshape(-1, width)
    attended_sum, log_total, attended, middle, normed_two, hidden, feed_back, feed_turned = (
        feed_both_ways(
            queries,
            keys,
            values,
            opening,
            output_own,
            tokens,
            gate_scaled,
            up_scaled,
            feed_near,
            grad_out,
            down_own,
            block,
            1,
        )
    )

    middle_grad, middle_back, mixed_sum, feed_sums = product_scatter_both(
        feed_back, feed_turned, hidden, down_own, middle, grad_out, normed_two, 4
    )
    feed_sums = feed_sums.reshape(seq, slab, -1)
    (
        output_kept,
        output_came,
        down_kept,
        down_came,
        feed_grad_near,
        feed_grad_far,
        normed_one_grad,
        qkv_grads,
    ) = attention_backwards(
        middle_back,
        output_own,
        attended,
        queries,
        keys,
        values,
        attended_sum,
        log_total,
        opening,
        cosine,
        sine,
        qkv_weight,
        hidden,
        grad_out,
        feed_sums,
        normed_one,
        block,
        5,
    )

    pair = ((mine // 2) % 2).reshape(1)
    (
        gate_grad,
        up_grad,
        query_grad,
        key_grad,
        value_grad,
        attn_gain_grad,
        mlp_gain_grad,
        mixed,
        token_grad,
        down_grad,
        output_grad,
    ) = unpack(
        pair,
        feed_grad_near,
        feed_grad_far,
        gate_weight,
        up_weight,
        qkv_grads,
        query_weight,
        key_weight,
        value_weight,
        gain_one,
        gain_two,
        tokens,
        middle,
        mixed_sum,
        middle_grad,
        normed_one_grad,
        down_kept,
        down_came,
        output_kept,
        output_came,
    )
    return (
        mixed,
        token_grad,
        attn_gain_grad[0],
        mlp_gain_grad[0],
        query_grad,
        key_grad,
        value_grad,
        output_grad,
        gate_grad,
        up_grad,
        down_grad,
    )


def solution(mesh):
    both = P(("dp", "seq"), None)
    line = P(("dp", "seq"))
    dp, seq = mesh.shape["dp"], mesh.shape["seq"]

    def run(*args):
        tokens = args[0].shape[0]
        width = args[0].shape[1]
        suits = dp == 2 and seq % 4 == 0 and width == dp * seq * HEAD_DIM
        suits = suits and 2 * (tokens // dp) * width <= 16 << 20
        return jax.shard_map(
            shards if suits else plain_shards,
            mesh=mesh,
            in_specs=(both, both, P("dp", None), line, line) + (both,) * 7,
            out_specs=(both, both, line, line) + (both,) * 7,
            check_vma=False,
        )(*args)

    return run
```

```python
import functools
import math

import jax
import jax.numpy as jnp
import numpy as np
from jax import lax
from jax.experimental import pallas as pl
from jax.experimental.pallas import tpu as pltpu
from jax.sharding import PartitionSpec as P

HEADS = 32
KV_HEADS = 8
HEAD_DIM = 64
DOCS = 4
EPS = 1e-05
NEG = -1e30
MESH = pl.DeviceIdType.MESH
F32 = jnp.float32
BF16 = jnp.bfloat16


def rotary_table(head_dim):
    exponent = jnp.arange(0, head_dim, 2, dtype=F32) / head_dim
    inverse = jnp.power(F32(500000.0), -exponent)
    wavelength = 2.0 * math.pi / inverse
    smooth = (8192.0 / wavelength - 1.0) / 3.0
    blended = (1.0 - smooth) * inverse / 32.0 + smooth * inverse
    return jnp.where(
        wavelength < 2048.0, inverse, jnp.where(wavelength > 8192.0, inverse / 32.0, blended)
    )


def swap_halves(values):
    rows, cols = values.shape
    halves = values.reshape(rows, cols // HEAD_DIM, 2, HEAD_DIM // 2)
    return halves[:, :, ::-1].reshape(rows, cols)


def dot(a, b):
    return jnp.dot(a, b, preferred_element_type=F32)


def dot_t(a, b):
    return lax.dot_general(a, b, (((1,), (1,)), ((), ())), preferred_element_type=F32)


def t_dot(a, b):
    return lax.dot_general(a, b, (((0,), (0,)), ((), ())), preferred_element_type=F32)


def allowed_tile(opening, q_first, k_first, shape):
    rows = q_first + lax.broadcasted_iota(jnp.int32, shape, 0)
    cols = k_first + lax.broadcasted_iota(jnp.int32, shape, 1)
    return (cols <= rows) & (cols >= opening)


def attention_kernel(block, q_ref, k_ref, v_ref, open_ref, out_ref, lse_ref, tile=None):
    if tile is None:
        tile = pl.program_id(0)
    opening = open_ref[...]
    heads = [
        slice(i * HEAD_DIM, (i + 1) * HEAD_DIM) for i in range(q_ref.shape[1] // HEAD_DIM)
    ]

    def step(j, carry):
        first = pl.multiple_of(j * block, block)
        allowed = allowed_tile(opening, tile * block, first, (block, block))
        after = []
        for lanes, (peak, total, acc) in zip(heads, carry):
            scores = dot_t(q_ref[:, lanes], k_ref[pl.ds(first, block), lanes])
            scores = jnp.where(allowed, scores, NEG)
            new_peak = jnp.maximum(peak, jnp.max(scores, axis=1, keepdims=True))
            spread = jnp.exp(scores - new_peak)
            fade = jnp.exp(peak - new_peak)
            total = total * fade + jnp.sum(spread, axis=1, keepdims=True)
            acc = acc * fade + dot(spread.astype(BF16), v_ref[pl.ds(first, block), lanes])
            after.append((new_peak, total, acc))
        return tuple(after)

    start = (
        jnp.full((block, 1), NEG, F32),
        jnp.zeros((block, 1), F32),
        jnp.zeros((block, HEAD_DIM), F32),
    )
    done = lax.fori_loop(0, tile + 1, step, (start,) * len(heads))
    for head, (lanes, (peak, total, acc)) in enumerate(zip(heads, done)):
        out_ref[:, lanes] = acc / total
        lse_ref[:, head : head + 1] = peak + jnp.log(total)


def attention(queries, keys, values, opening, block):
    rows, cols = queries.shape
    heads = cols // HEAD_DIM
    tiled = lambda width: pl.BlockSpec((block, width), lambda i: (i, 0))
    whole = pl.BlockSpec((rows, cols), lambda i: (0, 0))
    return pl.pallas_call(
        functools.partial(attention_kernel, block),
        grid=(rows // block,),
        in_specs=[tiled(cols), whole, whole, tiled(1)],
        out_specs=[tiled(cols), tiled(heads)],
        out_shape=[
            jax.ShapeDtypeStruct((rows, cols), F32),
            jax.ShapeDtypeStruct((rows, heads), F32),
        ],
        compiler_params=pltpu.CompilerParams(vmem_limit_bytes=48 << 20),
        cost_estimate=pl.CostEstimate(
            flops=2 * rows * rows * cols, bytes_accessed=10 * rows * cols, transcendentals=0
        ),
    )(queries, keys, values, opening)


def attention_back_kernel(
    block,
    q_ref,
    k_ref,
    v_ref,
    g_ref,
    att_ref,
    lse_ref,
    open_ref,
    dq_ref,
    dk_ref,
    dv_ref,
    tile=None,
):
    if tile is None:
        tile = pl.program_id(0)

    @pl.when(tile == 0)
    def _():
        dk_ref[...] = jnp.zeros_like(dk_ref)
        dv_ref[...] = jnp.zeros_like(dv_ref)

    count = q_ref.shape[1] // HEAD_DIM
    columns = [open_ref[...].astype(F32), lse_ref[...]]
    for head in range(count):
        lanes = slice(head * HEAD_DIM, (head + 1) * HEAD_DIM)
        grad = g_ref[:, lanes].astype(F32)
        columns.append(jnp.sum(grad * att_ref[:, lanes], axis=1, keepdims=True))
    columns.append(jnp.zeros((block, 127 - 2 * count), F32))
    across = jnp.concatenate(columns, axis=1).T
    opening = across[0:1].astype(jnp.int32)
    heads = [
        (
            slice(head * HEAD_DIM, (head + 1) * HEAD_DIM),
            across[1 + head : 2 + head],
            across[1 + count + head : 2 + count + head],
        )
        for head in range(count)
    ]

    def step(j, carry):
        first = pl.multiple_of(j * block, block)
        here = pl.ds(first, block)
        keys = first + lax.broadcasted_iota(jnp.int32, (block, block), 0)
        places = tile * block + lax.broadcasted_iota(jnp.int32, (block, block), 1)
        allowed = (keys <= places) & (keys >= opening)
        after = []
        for (lanes, log_total, row_sum), acc in zip(heads, carry):
            query, grad, key = q_ref[:, lanes], g_ref[:, lanes], k_ref[here, lanes]
            scores = dot_t(key, query)
            chance = jnp.where(allowed, jnp.exp(scores - log_total), 0.0)
            prob_grad = dot_t(v_ref[here, lanes], grad)
            score_grad = (chance * (prob_grad - row_sum)).astype(BF16)
            dk_ref[here, lanes] += dot(score_grad, query)
            dv_ref[here, lanes] += dot(chance.astype(BF16), grad)
            after.append(acc + t_dot(score_grad, key))
        return tuple(after)

    start = jnp.zeros((block, HEAD_DIM), F32)
    done = lax.fori_loop(0, tile + 1, step, (start,) * len(heads))
    for (lanes, _, _), acc in zip(heads, done):
        dq_ref[:, lanes] = acc


def attention_back(queries, keys, values, grads, attended, log_total, opening, block):
    rows, cols = queries.shape
    heads = cols // HEAD_DIM
    tiled = lambda width: pl.BlockSpec((block, width), lambda i: (i, 0))
    whole = pl.BlockSpec((rows, cols), lambda i: (0, 0))
    return pl.pallas_call(
        functools.partial(attention_back_kernel, block),
        grid=(rows // block,),
        in_specs=[tiled(cols), whole, whole, tiled(cols), tiled(cols), tiled(heads), tiled(1)],
        out_specs=[tiled(cols), whole, whole],
        out_shape=[jax.ShapeDtypeStruct((rows, cols), F32)] * 3,
        compiler_params=pltpu.CompilerParams(vmem_limit_bytes=60 << 20),
        cost_estimate=pl.CostEstimate(
            flops=5 * rows * rows * cols, bytes_accessed=20 * rows * cols, transcendentals=0
        ),
    )(queries, keys, values, grads, attended, log_total, opening)


def nothing():
    pass


class Place:
    def __init__(self):
        self.dp = lax.axis_index("dp")
        self.mine = lax.axis_index("seq")
        self.count = lax.axis_size("seq")
        self.length = self.count // 4
        self.line = lax.div(self.mine, 4)
        self.pair = lax.rem(lax.div(self.mine, 2), 2)
        self.core = lax.rem(self.mine, 2)
        self.slot = self.line * 2 + self.core

    def index(self, line, pair, core):
        return (line * 2 + pair) * 2 + core

    def peer(self, slot, same):
        pair = self.pair if same else 1 - self.pair
        return self.index(lax.div(slot, 2), pair, lax.rem(slot, 2))

    def device(self, line, pair, core):
        return (self.dp, self.index(line, pair, core))

    def sibling(self):
        return self.device(self.line, self.pair, 1 - self.core)

    def across(self):
        return self.device(self.line, 1 - self.pair, self.core)

    def above(self):
        return self.device(self.line + 1, self.pair, self.core)

    def below(self):
        return self.device(self.line - 1, self.pair, self.core)

    def partner(self):
        return (1 - self.dp, self.mine)

    def greet(self, partner=False):
        barrier = pltpu.get_barrier_semaphore()

        def signal(device):
            pl.semaphore_signal(barrier, inc=1, device_id=device, device_id_type=MESH)

        signal(self.sibling())
        signal(self.across())
        pl.when(self.line > 0)(lambda: signal(self.below()))
        pl.when(self.line < self.length - 1)(lambda: signal(self.above()))
        if partner:
            signal(self.partner())
        inner = (self.line > 0) & (self.line < self.length - 1)
        pl.semaphore_wait(barrier, jnp.where(inner, 4, 3) + (1 if partner else 0))

    def greet_all(self, meanwhile=nothing):
        self.call_all()
        meanwhile()
        self.await_all()

    def await_all(self):
        pl.semaphore_wait(pltpu.get_barrier_semaphore(), self.count)

    def call_all(self):
        barrier = pltpu.get_barrier_semaphore()

        def signal(device):
            pl.semaphore_signal(barrier, inc=1, device_id=device, device_id_type=MESH)

        signal(self.partner())

        @pl.loop(1, self.count)
        def _(ahead):
            signal((self.dp, lax.rem(self.mine + ahead, self.count)))


def remote(src, dst, send_sem, recv_sem, device):
    return pltpu.make_async_remote_copy(
        src_ref=src,
        dst_ref=dst,
        send_sem=send_sem,
        recv_sem=recv_sem,
        device_id=device,
        device_id_type=MESH,
    )


class Spread:
    def __init__(self, here, same, copies):
        self.here, self.same, self.copies = here, same, copies
        self.slots = here.count // 2

    def each(self, visit):
        @pl.loop(1 if self.same else 0, self.slots)
        def _(ahead):
            slot = lax.rem(self.here.slot + ahead, self.slots)
            visit(self.here.peer(slot, self.same), slot)

    def start_one(self, ahead):
        slot = lax.rem(self.here.slot + ahead, self.slots)
        peer = self.here.peer(slot, self.same)
        for one in self.copies(peer, self.here.mine, self.here.slot, slot):
            one.start()

    def start(self):
        pl.loop(1 if self.same else 0, self.slots)(self.start_one)

    def start_some(self, number, each):
        first = 1 if self.same else 0

        @pl.loop(0, each)
        def _(i):
            ahead = first + number * each + i
            pl.when((number >= 0) & (ahead < self.slots))(lambda: self.start_one(ahead))

    def finish(self):
        def visit(peer, slot):
            for one in self.copies(peer, peer, slot, slot):
                one.wait()

        self.each(visit)


def block_spread(here, same, blocks, into, sems):
    def copies(peer, sender, at, sem):
        return [
            remote(
                blocks.at[peer],
                into.at[at],
                sems.at[0, sem],
                sems.at[1, at],
                (here.dp, peer),
            )
        ]

    return Spread(here, same, copies)


def gather_units(here, buf, send_sems, recv_sems, compute, between=None, ready=None, started=nothing, level=False):
    length = here.length
    last = length - 1
    steps = 2 * length
    mine = here.mine
    shorter = jnp.minimum(here.line, last - here.line)
    longer = jnp.where(here.line < last - here.line, 1, -1)

    def column(j):
        i = j - 1
        paired = jnp.where(i % 2 == 0, here.line - i // 2 - 1, here.line + i // 2 + 1)
        single = here.line + longer * (i - shorter + 1)
        return jnp.where(j == 0, here.line, jnp.where(i < 2 * shorter, paired, single))

    keep = buf.shape[2] * 3 // 4

    def copy(way, device, block, piece):
        if piece == 2:
            ref, sem = buf.at[block, 1, pl.ds(0, keep)], 1
        elif piece == 3:
            ref, sem = buf.at[block, 1, pl.ds(keep, buf.shape[2] - keep)], 2
        else:
            ref, sem = buf.at[block, piece], piece
        return remote(ref, ref, send_sems.at[way, block, sem], recv_sems.at[block, sem], device)

    def up(block, piece):
        return copy(0, here.above(), block, piece)

    def down(block, piece):
        return copy(1, here.below(), block, piece)

    def across(block, piece):
        return copy(2, here.across(), block, piece)

    def sideways(block, piece):
        return copy(3, here.sibling(), block, piece)

    def unit(number):
        in_column = (number % 2 == 1) & (number < steps - 1) | (number == 0)
        later = jnp.where(number == steps - 1, last, number // 2 - 1)
        line = column(jnp.where(in_column, (number + 1) // 2, later))
        pair = jnp.where(in_column, here.pair, 1 - here.pair)
        other = here.index(line, pair, 1 - here.core)
        sideways(other, 0).wait_recv()
        if level:
            whole = in_column | (line == here.line)
            pl.when(whole)(lambda: sideways(other, 1).wait_recv())

            @pl.when(jnp.logical_not(whole))
            def _():
                sideways(other, 2).wait_recv()
                sideways(other, 3).wait_recv()

        else:
            sideways(other, 1).wait_recv()

        compute(number, here.index(line, pair, 0))

    for piece in range(2):
        pl.when(here.line < last)(lambda piece=piece: up(mine, piece).start())
        pl.when(here.line > 0)(lambda piece=piece: down(mine, piece).start())
        across(mine, piece).start()
        sideways(mine, piece).start()
    started()
    beside = here.index(here.line, 1 - here.pair, here.core)

    def relay(far, pair, piece):
        @pl.when(here.line >= far)
        def _():
            block = here.index(here.line - far, pair, here.core)
            up(block, piece).wait_recv()
            pl.when(here.line < last)(lambda: up(block, piece).start())
            sideways(block, piece).start()

        @pl.when(here.line + far <= last)
        def _():
            block = here.index(here.line + far, pair, here.core)
            down(block, piece).wait_recv()
            pl.when(here.line > 0)(lambda: down(block, piece).start())
            sideways(block, piece).start()

    @pl.loop(0, length)
    def _(round):
        for part in range(2):
            step = 2 * round + part
            relay(round + 1, here.pair, part)

            @pl.when(round < last)
            def _():
                block = here.index(column(round + 1), here.pair, here.core)
                across(block, (2 if level else 1) if part else 0).start()

            block = here.index(column(round), 1 - here.pair, here.core)
            if part == 0 or not level:
                across(block, part).wait_recv()
                sideways(block, part).start()
            else:

                @pl.when(round == 0)
                def _():
                    across(beside, 1).wait_recv()
                    pl.when(here.line < last)(lambda: up(beside, 3).start())
                    pl.when(here.line > 0)(lambda: down(beside, 3).start())
                    sideways(beside, 1).start()

                @pl.when(round > 0)
                def _():
                    across(block, 2).wait_recv()
                    sideways(block, 2).start()
                    relay(round, 1 - here.pair, 3)

            if between is not None:
                between(step)
            if ready is None:
                unit(step)
            else:
                begin = jnp.maximum(2 * (step - ready), 0)
                end = jnp.maximum(2 * (step + 1 - ready), 0)

                @pl.loop(begin, end)
                def _(number):
                    unit(number)

    @pl.loop(0, length)
    def _(line):
        own = here.index(line, here.pair, here.core)
        other = here.index(line, 1 - here.pair, here.core)
        goes_up = (line <= here.line) & (here.line < last)
        goes_down = (line >= here.line) & (here.line > 0)

        @pl.when(goes_up)
        def _():
            up(own, 0).wait_send()
            up(own, 1).wait_send()
            if level:
                up(other, 3).wait_send()

        @pl.when(goes_down)
        def _():
            down(own, 0).wait_send()
            down(own, 1).wait_send()
            if level:
                down(other, 3).wait_send()

        across(own, 0).wait_send()
        sideways(own, 0).wait_send()
        sideways(own, 1).wait_send()
        sideways(other, 0).wait_send()

        if not level:
            across(own, 1).wait_send()
            sideways(other, 1).wait_send()
            return

        @pl.when(line == here.line)
        def _():
            across(own, 1).wait_send()
            sideways(other, 1).wait_send()

        @pl.when(line != here.line)
        def _():
            across(own, 2).wait_send()
            sideways(other, 2).wait_send()
            sideways(other, 3).wait_send()


def put_own(here, own_ref, buf):
    half = buf.shape[2]
    for part in range(2):
        buf[here.mine, part] = own_ref[pl.ds(part * half, half), :]


def gather_scratch(seq, rows, width):
    return [
        pltpu.VMEM((seq, 2, rows, width), BF16),
        pltpu.SemaphoreType.DMA((4, seq, 3)),
        pltpu.SemaphoreType.DMA((seq, 3)),
    ]


def unit_rows(first, rows):
    return pl.ds(pl.multiple_of(first * rows, 2 * rows), 2 * rows)


def take_unit(buf, first):
    blocks = buf[pl.ds(first, 2)]
    return blocks.reshape(-1, blocks.shape[-1])


class UnitStore:
    def __init__(self, buf, out_ref, sems):
        self.buf, self.out_ref, self.sems = buf, out_ref, sems

    def copies(self, number, first):
        half = self.buf.shape[2]
        made = []
        for block in range(2):
            for part in range(2):
                begin = ((first + block) * 2 + part) * half
                made.append(
                    pltpu.make_async_copy(
                        self.buf.at[first + block, part],
                        self.out_ref.at[pl.ds(pl.multiple_of(begin, half), half)],
                        self.sems.at[number, block, part],
                    )
                )
        return made

    def start(self, number, first):
        for one in self.copies(number, first):
            one.start()

    def finish(self):
        @pl.loop(0, self.sems.shape[0])
        def _(number):
            for one in self.copies(number, 0):
                one.wait()


def params(call_id, mebibytes):
    return pltpu.CompilerParams(
        collective_id=call_id, has_side_effects=True, vmem_limit_bytes=mebibytes << 20
    )


def cost(flops, bytes_accessed):
    return pl.CostEstimate(flops=flops, bytes_accessed=bytes_accessed, transcendentals=0)


VMEM = pl.BlockSpec(memory_space=pltpu.VMEM)
HBM = pl.BlockSpec(memory_space=pl.ANY)


def rotated(values, cosine, sine):
    cols = values.shape[1]
    lane = lax.broadcasted_iota(jnp.int32, values.shape, 1)
    ahead = pltpu.roll(values, cols - HEAD_DIM // 2, 1)
    behind = pltpu.roll(values, HEAD_DIM // 2, 1)
    swapped = jnp.where(lane % HEAD_DIM < HEAD_DIM // 2, ahead, behind)
    return values * cosine + swapped * sine


def upright(row):
    count = row.shape[1]
    shape = (count, count)
    same = lax.broadcasted_iota(jnp.int32, shape, 0) == lax.broadcasted_iota(jnp.int32, shape, 1)
    return jnp.sum(jnp.where(same, row.astype(F32), 0.0), axis=1, keepdims=True)


def flat(column):
    count = column.shape[0]
    shape = (count, count)
    same = lax.broadcasted_iota(jnp.int32, shape, 0) == lax.broadcasted_iota(jnp.int32, shape, 1)
    return jnp.sum(jnp.where(same, column, 0.0), axis=0, keepdims=True)


def project_kernel(
    lengths_ref,
    tokens_ref,
    cotangent_ref,
    query_ref,
    key_ref,
    value_ref,
    gate_ref,
    up_ref,
    gain_one_ref,
    gain_two_ref,
    freq_ref,
    down_ref,
    output_ref,
    normed_ref,
    grads_ref,
    q_ref,
    k_ref,
    v_ref,
    cos_ref,
    sin_ref,
    open_ref,
    weight_ref,
    gate_out_ref,
    up_out_ref,
    down_out_ref,
    output_out_ref,
    buf,
    send_sems,
    recv_sems,
    blocks,
    store_sems,
    near_sems,
    far_sems,
    swap_sems,
    local_sems,
    pair_sems,
    share_sems,
):
    here = Place()
    cols = q_ref.shape[1]
    rows = tokens_ref.shape[0]
    dp = here.dp
    ends = [lengths_ref[0, 0]]
    for j in range(1, DOCS):
        ends.append(ends[-1] + lengths_ref[0, j])

    def own_rows():
        chunk = 32

        @pl.loop(0, rows // chunk)
        def _(i):
            some = pl.ds(pl.multiple_of(i * chunk, chunk), chunk)
            values = tokens_ref[some, :].astype(F32)
            factor = lax.rsqrt(jnp.mean(values * values, axis=1, keepdims=True) + EPS)
            buf[here.mine, 0, some, :] = (values * factor).astype(BF16)
            shape = (chunk, cotangent_ref.shape[1])
            place = here.mine * rows + i * chunk + lax.broadcasted_iota(jnp.int32, shape, 0)
            grads = cotangent_ref[some, :].astype(F32)
            buf[here.mine, 1, some, :] = jnp.where(place < ends[-1], grads, 0.0).astype(BF16)

    def own_blocks():
        gain = upright(gain_one_ref[...])
        query = query_ref[...].astype(F32) * gain
        key = key_ref[...].astype(F32) * gain
        value = value_ref[...].astype(F32) * gain

        def heads(array, number, kept):
            parts = []
            for half in range(2):
                head = half * kept + number * kept // blocks.shape[0]
                parts.append(array[:, head * HEAD_DIM : (head + 1) * HEAD_DIM])
            return jnp.concatenate(parts, axis=1).astype(BF16)

        for number in range(blocks.shape[0]):
            blocks[number, :, :cols] = heads(query, number, HEADS // 2)
            array = value if number % 2 else key
            blocks[number, :, cols:] = heads(array, number, KV_HEADS // 2)

    def own_parts():
        own_blocks()
        own_rows()

    here.greet_all(own_parts)

    def weight_spread(same, sems):
        def copies(peer, sender, at, sem):
            return [
                remote(
                    blocks.at[peer],
                    weight_ref.at[dp, sender],
                    sems.at[0, sem],
                    sems.at[1, at],
                    (dp, peer),
                )
            ]

        return Spread(here, same, copies)

    near = weight_spread(True, near_sems)
    far = weight_spread(False, far_sems)
    swaps = []
    for number, (src, dst) in enumerate([(down_ref, down_out_ref), (output_ref, output_out_ref)]):
        swaps.append(
            remote(src, dst.at[dp], swap_sems.at[0, number], swap_sems.at[1, number], here.partner())
        )
        swaps.append(pltpu.make_async_copy(src, dst.at[dp], local_sems.at[number]))
    def pair_copy(source, sender):
        return remote(
            weight_ref.at[source, sender],
            weight_ref.at[source, sender],
            pair_sems.at[0, sender],
            pair_sems.at[1, sender],
            here.partner(),
        )

    def own_tables():
        chunk = 128

        @pl.loop(0, open_ref.shape[0] // chunk)
        def _(i):
            some = pl.ds(pl.multiple_of(i * chunk, chunk), chunk)
            place = i * chunk + lax.broadcasted_iota(jnp.int32, (chunk, 1), 0)
            opening = jnp.zeros((chunk, 1), jnp.int32)
            for end in ends:
                opening = jnp.where(place >= end, end, opening)
            open_ref[some, :] = opening
            angles = (place - opening).astype(F32) * freq_ref[...]
            lane = lax.broadcasted_iota(jnp.int32, angles.shape, 1)
            sine = jnp.sin(angles)
            cos_ref[some, :] = jnp.cos(angles)
            sin_ref[some, :] = jnp.where(lane % HEAD_DIM < HEAD_DIM // 2, -sine, sine)

    def started():
        far.start()
        near.start()
        weight_ref[dp, here.mine] = blocks[here.mine]
        for one in swaps:
            one.start()
        chunk = 512

        @pl.loop(0, gate_ref.shape[1] // chunk)
        def _(i):
            some = pl.ds(pl.multiple_of(i * chunk, chunk), chunk)
            gain = upright(gain_two_ref[...])
            gate_out_ref[:, some] = (gate_ref[:, some].astype(F32) * gain).astype(BF16)
            up_out_ref[:, some] = (up_ref[:, some].astype(F32) * gain).astype(BF16)

        own_tables()

    def between(step):
        @pl.when(step == 2)
        def _():
            near.finish()
            far.finish()

            @pl.loop(0, here.count)
            def _(sender):
                pair_copy(dp, sender).start()

        @pl.when(step == 4)
        def _():
            @pl.loop(0, here.count)
            def _(sender):
                pair_copy(1 - dp, sender).wait_recv()

    def share_copy(ref, number, where):
        return remote(
            ref.at[where],
            ref.at[where],
            share_sems.at[0, number],
            share_sems.at[1, number],
            here.sibling(),
        )

    def stores(number, first):
        made = []
        for block in range(2):
            where = pl.ds(pl.multiple_of((first + block) * rows, rows), rows)
            for part, out_ref in enumerate((normed_ref, grads_ref)):
                made.append(
                    pltpu.make_async_copy(
                        buf.at[first + block, part],
                        out_ref.at[where],
                        store_sems.at[number, block, part],
                    )
                )
        return made

    def compute(number, first):
        for one in stores(number, first):
            one.start()
        weight = weight_ref[...].reshape(-1, weight_ref.shape[-1])
        unit = buf[pl.ds(first, 2), 0]
        qkv = dot(unit.reshape(-1, unit.shape[-1]), weight)
        where = unit_rows(first, rows)
        cosine = cos_ref[where, :]
        sine = sin_ref[where, :]
        scale = BF16(1.0 / math.sqrt(HEAD_DIM))
        q_ref[where, :] = rotated(qkv[:, :cols], cosine, sine).astype(BF16) * scale
        for core, ref in enumerate((k_ref, v_ref)):

            @pl.when(here.core == core)
            def _():
                mine = qkv[:, cols:]
                ref[where, :] = (mine if core else rotated(mine, cosine, sine)).astype(BF16)
                share_copy(ref, number, where).start()

    gather_units(here, buf, send_sems, recv_sems, compute, between, here.length, started, True)

    @pl.loop(0, here.count)
    def _(sender):
        pair_copy(dp, sender).wait_send()

    @pl.loop(0, here.count // 2)
    def _(number):
        for one in stores(number, 0):
            one.wait()
        share_copy(k_ref, number, unit_rows(0, rows)).wait()

    for one in swaps:
        one.wait()


def gather_project(
    lengths, tokens, cotangent, query, key, value, gate, up, gains, freq, down, output, call_id
):
    seq = lax.axis_size("seq")
    rows, width = tokens.shape
    cols = 2 * HEAD_DIM
    slab, ff = gate.shape
    bf16 = lambda *shape: jax.ShapeDtypeStruct(shape, BF16)
    f32 = lambda *shape: jax.ShapeDtypeStruct(shape, F32)
    all_rows = seq * rows
    dma = pltpu.SemaphoreType.DMA
    return pl.pallas_call(
        project_kernel,
        out_shape=[
            bf16(all_rows, width),
            bf16(all_rows, width),
            bf16(all_rows, cols),
            bf16(all_rows, cols),
            bf16(all_rows, cols),
            f32(all_rows, cols),
            f32(all_rows, cols),
            jax.ShapeDtypeStruct((all_rows, 1), jnp.int32),
            bf16(2, seq, slab, 2 * cols),
            bf16(slab, ff),
            bf16(slab, ff),
            bf16(2, *down.shape),
            bf16(2, *output.shape),
        ],
        in_specs=[pl.BlockSpec(memory_space=pltpu.SMEM)] + [VMEM] * 10 + [HBM] * 2,
        out_specs=[HBM] * 2 + [VMEM] * 9 + [HBM] * 2,
        scratch_shapes=gather_scratch(seq, rows, width)
        + [
            pltpu.VMEM((seq, slab, 2 * cols), BF16),
            dma((seq // 2, 2, 2)),
            dma((2, seq // 2)),
            dma((2, seq // 2)),
            dma((2, 2)),
            dma((2,)),
            dma((2, seq)),
            dma((2, seq // 2)),
        ],
        compiler_params=params(call_id, 60),
        cost_estimate=cost(2 * all_rows * width * 2 * cols, 8 * all_rows * width),
    )(lengths, tokens, cotangent, query, key, value, gate, up, *gains, freq, down, output)


ROW_CHUNK = 32


def norm_input_grad(values, upstream):
    factor = norm_factor(values)
    inner_mean = jnp.mean(upstream * values, axis=-1, keepdims=True)
    return factor * upstream - values * factor * factor * factor * inner_mean


def in_row_chunks(rows, chunk, visit):
    @pl.loop(0, rows // chunk)
    def _(i):
        visit(pl.ds(pl.multiple_of(i * chunk, chunk), chunk))


SCATTER_PARTS = 2
SCATTER_RING = 4
SCATTER_SCRATCH = 11


def scatter_rows_of_products(
    here,
    products,
    core_out,
    core_in,
    pair_out,
    pair_in,
    line_out,
    line_in,
    held,
    core_sems,
    pair_sems,
    line_sems,
    came_sems,
    first=None,
    between=nothing,
    filler=None,
):
    length = here.length
    parts = SCATTER_PARTS * len(products)
    rows, width = held.shape
    tile = min(width, 512)
    tiles = width // tile
    steps = length * parts

    def target(i):
        ups = length - 1 - here.line
        near = here.line < length // 2
        if_near = jnp.where(i < ups, length - 1 - i, i - ups)
        if_far = jnp.where(i < here.line, i, length - 1 - (i - here.line))
        return jnp.where(i == length - 1, here.line, jnp.where(near, if_near, if_far))

    def product(line, pair, core, part, use):
        first = pl.multiple_of(here.index(line, pair, core) * rows, rows)

        def one(number):
            transposed, a_ref, b_ref, _ = products[number]
            a = a_ref[pl.ds(first, rows), :]
            begin = (part - number * SCATTER_PARTS) * width

            @pl.loop(0, tiles)
            def _(t):
                into = pl.ds(pl.multiple_of(t * tile, tile), tile)
                cols = pl.ds(pl.multiple_of(begin + t * tile, tile), tile)
                use(dot_t(a, b_ref[cols, :]) if transposed else dot(a, b_ref[:, cols]), into)

        for number in range(len(products)):
            pl.when(part // SCATTER_PARTS == number)(functools.partial(one, number))

    def core_copy(slot):
        return remote(
            core_out.at[slot % SCATTER_RING],
            core_in.at[slot],
            core_sems.at[0, slot],
            core_sems.at[1, slot],
            here.sibling(),
        )

    def pair_copy(slot):
        return remote(
            pair_out.at[slot],
            pair_in.at[slot],
            pair_sems.at[0, slot],
            pair_sems.at[1, slot],
            here.across(),
        )

    def up_copy(slot, line, part):
        into = (line + 1) * parts + part
        return remote(
            line_out.at[slot], line_in.at[into], line_sems.at[slot], came_sems.at[into], here.above()
        )

    def down_copy(slot, line, part):
        into = line * parts + part
        return remote(
            line_out.at[slot], line_in.at[into], line_sems.at[slot], came_sems.at[into], here.below()
        )

    def for_sibling(step, pair, slot):
        pl.when(slot >= SCATTER_RING)(lambda: core_copy(slot - SCATTER_RING).wait_send())

        def use(value, cols):
            core_out[slot % SCATTER_RING, :, cols] = value.astype(BF16)

        product(target(step // parts), pair, 1 - here.core, step % parts, use)
        core_copy(slot).start()

    for_sibling(jnp.int32(0), 1 - here.pair, jnp.int32(0))

    @pl.loop(0, steps)
    def _(step):
        if first is not None:
            first(step)
        pl.when(step < steps - 1)(lambda: for_sibling(step + 1, 1 - here.pair, step + 1))
        core_copy(step).wait_recv()

        def use(value, cols):
            pair_out[step, :, cols] = (value + core_in[step, :, cols].astype(F32)).astype(BF16)

        product(target(step // parts), 1 - here.pair, here.core, step % parts, use)
        pair_copy(step).start()

    for_sibling(jnp.int32(0), here.pair, jnp.int32(steps))
    between()

    @pl.loop(0, steps)
    def _(step):
        pl.when(step < steps - 1)(lambda: for_sibling(step + 1, here.pair, steps + step + 1))
        core_copy(steps + step).wait_recv()
        line = target(step // parts)
        part = step % parts

        def use(value, cols):
            held[:, cols] = value + core_in[steps + step, :, cols].astype(F32)

        product(line, here.pair, here.core, part, use)
        if filler is not None:
            filler(step)
        pair_copy(step).wait_recv()
        from_above = (line <= here.line) & (here.line < length - 1)
        from_below = (line >= here.line) & (here.line > 0)
        held[...] += pair_in[step].astype(F32)

        @pl.when(from_above)
        def _():
            down_copy(0, line, part).wait_recv()
            held[...] += line_in[line * parts + part].astype(F32)

        @pl.when(from_below)
        def _():
            up_copy(0, line, part).wait_recv()
            held[...] += line_in[(line + 1) * parts + part].astype(F32)

        for number, (_, _, _, out_ref) in enumerate(products):

            @pl.when((line == here.line) & (part // SCATTER_PARTS == number))
            def _():
                begin = (part - number * SCATTER_PARTS) * width
                out_ref[:, pl.ds(pl.multiple_of(begin, width), width)] = held[...]

        @pl.when(line < here.line)
        def _():
            line_out[step] = held[...].astype(BF16)
            down_copy(step, line, part).start()

        @pl.when(line > here.line)
        def _():
            line_out[step] = held[...].astype(BF16)
            up_copy(step, line, part).start()

    @pl.loop(2 * steps - SCATTER_RING, 2 * steps)
    def _(slot):
        core_copy(slot).wait_send()

    @pl.loop(0, steps)
    def _(step):
        pair_copy(step).wait_send()
        line = target(step // parts)
        pl.when(line < here.line)(lambda: down_copy(step, 0, 0).wait_send())
        pl.when(line > here.line)(lambda: up_copy(step, 0, 0).wait_send())


def scatter_scratch(seq, rows, width, count=1):
    length = seq // 4
    parts = SCATTER_PARTS * count
    steps = length * parts
    block = (rows, width // SCATTER_PARTS)
    dma = pltpu.SemaphoreType.DMA
    return [
        pltpu.VMEM((SCATTER_RING, *block), BF16),
        pltpu.VMEM((2 * steps, *block), BF16),
        pltpu.VMEM((steps, *block), BF16),
        pltpu.VMEM((steps, *block), BF16),
        pltpu.VMEM((steps, *block), BF16),
        pltpu.VMEM(((length + 1) * parts, *block), BF16),
        pltpu.VMEM(block, F32),
        dma((2, 2 * steps)),
        dma((2, steps)),
        dma((steps,)),
        dma(((length + 1) * parts,)),
    ]


def scatter_cost(a, width):
    return cost(2 * a.shape[0] * a.shape[1] * width, 4 * a.shape[0] * width)


def scatter_both_kernel(
    back_hbm,
    turned_hbm,
    hidden_hbm,
    down_hbm,
    middle_ref,
    grads_hbm,
    normed_hbm,
    grad_ref,
    low_ref,
    mixed_ref,
    sums_ref,
    *scratch,
):
    here = Place()
    factors = scratch[SCATTER_SCRATCH : SCATTER_SCRATCH + 4]
    back_ref, turned_ref, hidden_ref, down_ref = factors
    normed, away, came, own, fetch_sems, swap_sems, own_sems = scratch[SCATTER_SCRATCH + 4 :]
    rows = grad_ref.shape[0]
    loads = [
        pltpu.make_async_copy(src, dst, own_sems.at[number])
        for number, (src, dst) in enumerate(
            zip((back_hbm, turned_hbm, hidden_hbm, down_hbm), factors)
        )
    ]
    own_copy = pltpu.make_async_copy(
        grads_hbm.at[pl.ds(pl.multiple_of(here.mine * rows, rows), rows)], own, own_sems.at[4]
    )
    for one in loads + [own_copy]:
        one.start()
    here.greet(partner=True)
    for one in loads[:2]:
        one.wait()

    def first(step):
        @pl.when(step == SCATTER_PARTS - 1)
        def _():
            for one in loads[2:]:
                one.wait()
    chunk = normed.shape[2]
    half = normed_hbm.shape[1] // 2
    chunks = half // chunk

    def fetch(number):
        dp = jnp.where(number < chunks, 1 - here.dp, here.dp)
        begin = dp * half + number % chunks * chunk
        return pltpu.make_async_copy(
            normed_hbm.at[:, pl.ds(pl.multiple_of(begin, chunk), chunk)],
            normed.at[number % 2],
            fetch_sems.at[number % 2],
        )

    def swap(i):
        some = pl.ds(pl.multiple_of(i * chunk, chunk), chunk)
        return remote(
            away.at[some], came.at[some], swap_sems.at[0, i], swap_sems.at[1, i], here.partner()
        )

    def part(number):
        fetch(number).wait()
        pl.when(number + 1 < 2 * chunks)(lambda: fetch(number + 1).start())
        return t_dot(normed[number % 2], back_ref[...])

    def filler(step):
        @pl.when(step < chunks)
        def _():
            some = pl.ds(pl.multiple_of(step * chunk, chunk), chunk)
            away[some, :] = part(step).astype(BF16)
            swap(step).start()

        @pl.when((step >= chunks) & (step < 3 * chunks) & (step % 2 == 0))
        def _():
            i = (step - chunks) // 2
            some = pl.ds(pl.multiple_of(i * chunk, chunk), chunk)
            kept = part(chunks + i)
            swap(i).wait()
            sums_ref[some, :] = (kept + came[some, :].astype(F32)).astype(BF16)

    fetch(jnp.int32(0)).start()
    scatter_rows_of_products(
        here,
        [(False, back_ref, turned_ref, grad_ref), (False, hidden_ref, down_ref, mixed_ref)],
        *scratch[:SCATTER_SCRATCH],
        first=first,
        filler=filler,
    )
    own_copy.wait()

    def add(some):
        grad = own[some, :].astype(F32) + norm_input_grad(middle_ref[some, :], grad_ref[some, :])
        grad_ref[some, :] = grad
        low_ref[some, :] = grad.astype(BF16)

    in_row_chunks(rows, ROW_CHUNK, add)


def product_scatter_both(back, turned, hidden, down, middle, grads, normed, call_id):
    seq = lax.axis_size("seq")
    rows = back.shape[0] // seq
    width = turned.shape[1]
    cols = back.shape[1]
    chunk = width // 8
    dma = pltpu.SemaphoreType.DMA
    return pl.pallas_call(
        scatter_both_kernel,
        out_shape=[
            jax.ShapeDtypeStruct((rows, width), F32),
            jax.ShapeDtypeStruct((rows, width), BF16),
            jax.ShapeDtypeStruct((rows, width), F32),
            jax.ShapeDtypeStruct((width // 2, cols), BF16),
        ],
        in_specs=[HBM] * 4 + [VMEM] + [HBM] * 2,
        out_specs=[VMEM] * 4,
        scratch_shapes=scatter_scratch(seq, rows, width, 2)
        + [pltpu.VMEM(array.shape, BF16) for array in (back, turned, hidden, down)]
        + [
            pltpu.VMEM((2, normed.shape[0], chunk), BF16),
            pltpu.VMEM((width // 2, cols), BF16),
            pltpu.VMEM((width // 2, cols), BF16),
            pltpu.VMEM((rows, width), BF16),
            dma((2,)),
            dma((2, 4)),
            dma((5,)),
        ],
        compiler_params=params(call_id, 60),
        cost_estimate=scatter_cost(back, 3 * width),
    )(back, turned, hidden, down, middle, grads, normed)


def feed_kernel(
    block,
    q_ref,
    k_ref,
    v_ref,
    open_ref,
    b_ref,
    tokens_ref,
    gate_hbm,
    up_hbm,
    grad_hbm,
    down_hbm,
    attended_ref,
    lse_ref,
    a_ref,
    middle_ref,
    normed_ref,
    hidden_out_ref,
    back_out_ref,
    turned_out_ref,
    *scratch,
):
    here = Place()
    (
        feed_ref,
        swap_sems,
        local_sems,
        near_sems,
        far_sems,
        buf,
        send_sems,
        recv_sems,
        store_sems,
        grad_ref,
        down_ref,
        hidden_ref,
        back_ref,
        turned_ref,
        fetch_sems,
        out_sems,
    ) = scratch[SCATTER_SCRATCH:]
    slab = feed_ref.shape[2]
    slots = here.count // 2
    rows, width = middle_ref.shape
    hidden = hidden_ref.shape[1]
    tile = 256

    def swap(slot, same):
        place = feed_ref.at[here.dp, here.peer(slot, same)]
        half = 0 if same else 1
        return remote(
            place,
            place,
            swap_sems.at[0, half, slot],
            swap_sems.at[1, half, slot],
            here.partner(),
        )

    columns = hidden // 2

    def columns_of(weight, half, index):
        begin = pl.multiple_of((half * here.count + index) * columns, columns)
        return weight.at[:, pl.ds(begin, columns)]

    def place_of(sender, part):
        return feed_ref.at[here.dp, sender, :, pl.ds(part * columns, columns)]

    sources = [(weight, half) for weight in (gate_hbm, up_hbm) for half in range(2)]

    def feed_spread(same, sems):
        def copies(peer, sender, at, sem):
            return [
                remote(
                    columns_of(weight, half, peer),
                    place_of(sender, part),
                    sems.at[0, sem, part],
                    sems.at[1, at, part],
                    (here.dp, peer),
                )
                for part, (weight, half) in enumerate(sources)
            ]

        return Spread(here, same, copies)

    near = feed_spread(True, near_sems)
    own_feed = [
        pltpu.make_async_copy(
            columns_of(weight, half, here.mine), place_of(here.mine, part), local_sems.at[part]
        )
        for part, (weight, half) in enumerate(sources)
    ]
    far = feed_spread(False, far_sems)

    fetches = [
        pltpu.make_async_copy(down_hbm, down_ref, fetch_sems.at[0]),
        pltpu.make_async_copy(grad_hbm, grad_ref, fetch_sems.at[1]),
    ]
    for one in own_feed + fetches:
        one.start()
    here.call_all()

    @pl.loop(0, a_ref.shape[0] // block)
    def _(tile):
        some = pl.ds(pl.multiple_of(tile * block, block), block)
        attention_kernel(
            block,
            q_ref.at[some],
            k_ref,
            v_ref,
            open_ref.at[some],
            attended_ref.at[some],
            lse_ref.at[some],
            tile,
        )
        a_ref[some, :] = attended_ref[some, :].astype(BF16)

        @pl.when(tile == 0)
        def _():
            here.await_all()
            far.start()
            near.start()

    def between():
        far.finish()
        pl.loop(0, slots)(lambda slot: swap(slot, False).start())

    def filler(step):
        @pl.when(step == 2)
        def _():
            near.finish()
            for one in own_feed:
                one.wait()
            pl.loop(0, slots)(lambda slot: swap(slot, True).start())

    scatter_rows_of_products(
        here,
        [(False, a_ref, b_ref, middle_ref)],
        *scratch[:SCATTER_SCRATCH],
        between=between,
        filler=filler,
    )
    half = buf.shape[2]
    for part in range(2):

        @pl.loop(0, half // ROW_CHUNK)
        def _(i, part=part):
            into = pl.ds(pl.multiple_of(i * ROW_CHUNK, ROW_CHUNK), ROW_CHUNK)
            some = pl.ds(pl.multiple_of(part * half + i * ROW_CHUNK, ROW_CHUNK), ROW_CHUNK)
            middle = tokens_ref[some, :].astype(F32) + middle_ref[some, :]
            middle_ref[some, :] = middle
            buf[here.mine, part, into, :] = (middle * norm_factor(middle)).astype(BF16)

    def started():
        @pl.loop(0, slots)
        def _(slot):
            swap(slot, True).wait()
            swap(slot, False).wait()

        for one in fetches:
            one.wait()

    store = UnitStore(buf, normed_ref, store_sems)
    share = width // (2 * here.length)

    def outs(number, first):
        where = unit_rows(first, rows)
        some = pl.ds(pl.multiple_of(number * share, share), share)
        return [
            pltpu.make_async_copy(src, dst, out_sems.at[number, i])
            for i, (src, dst) in enumerate(
                [
                    (hidden_ref.at[where], hidden_out_ref.at[where]),
                    (back_ref.at[where], back_out_ref.at[where]),
                    (turned_ref.at[:, some], turned_out_ref.at[:, some]),
                ]
            )
        ]

    def compute(number, first):
        store.start(number, first)
        where = unit_rows(first, rows)
        normed = take_unit(buf, first)
        grad = grad_ref[where, :]

        @pl.loop(0, hidden // tile)
        def _(t):
            cols = pl.ds(pl.multiple_of(t * tile, tile), tile)
            later = pl.ds(pl.multiple_of(hidden + t * tile, tile), tile)
            gate = dot(normed, feed_ref[:, :, :, cols].reshape(width, tile))
            upward = dot(normed, feed_ref[:, :, :, later].reshape(width, tile))
            hidden_grad = dot_t(grad, down_ref[cols, :])
            sigmoid = jax.nn.sigmoid(gate)
            silu = gate * sigmoid
            hidden_ref[where, cols] = (silu * upward).astype(BF16)
            back_ref[where, cols] = (
                hidden_grad * upward * sigmoid * (1.0 + gate * (1.0 - sigmoid))
            ).astype(BF16)
            back_ref[where, later] = (hidden_grad * silu).astype(BF16)

        slabs = share // slab
        begin = number * slabs
        some = pl.ds(pl.multiple_of(number * share, share), share)
        weights = feed_ref[lax.div(begin, here.count), pl.ds(lax.rem(begin, here.count), slabs)]
        turned_ref[:, some] = weights.reshape(share, 2 * hidden).T
        for one in outs(number, first):
            one.start()

    gather_units(here, buf, send_sems, recv_sems, compute, started=started, level=True)

    @pl.loop(0, here.count // 2)
    def _(number):
        for one in outs(number, 0):
            one.wait()

    store.finish()


def feed_both_ways(
    queries, keys, values, opening, output, tokens, gate, up, grad_out, down, block, call_id
):
    seq = lax.axis_size("seq")
    rows, width = tokens.shape
    cols = queries.shape[1]
    hidden = down.shape[0]
    all_rows = seq * rows
    bf16 = lambda *shape: jax.ShapeDtypeStruct(shape, BF16)
    f32 = lambda *shape: jax.ShapeDtypeStruct(shape, F32)
    dma = pltpu.SemaphoreType.DMA
    return pl.pallas_call(
        functools.partial(feed_kernel, block),
        out_shape=[
            f32(all_rows, cols),
            f32(all_rows, cols // HEAD_DIM),
            bf16(all_rows, cols),
            f32(rows, width),
            bf16(all_rows, width),
            bf16(all_rows, hidden),
            bf16(all_rows, 2 * hidden),
            bf16(2 * hidden, width),
        ],
        in_specs=[VMEM] * 6 + [HBM] * 4,
        out_specs=[VMEM] * 4 + [HBM] * 4,
        scratch_shapes=scatter_scratch(seq, rows, width)
        + [
            pltpu.VMEM((2, seq, gate.shape[0], 2 * hidden), BF16),
            dma((2, 2, seq // 2)),
            dma((4,)),
            dma((2, seq // 2, 4)),
            dma((2, seq // 2, 4)),
        ]
        + gather_scratch(seq, rows // 2, width)
        + [
            dma((seq // 2, 2, 2)),
            pltpu.VMEM((all_rows, width), BF16),
            pltpu.VMEM((hidden, width), BF16),
            pltpu.VMEM((all_rows, hidden), BF16),
            pltpu.VMEM((all_rows, 2 * hidden), BF16),
            pltpu.VMEM((2 * hidden, width), BF16),
            dma((2,)),
            dma((seq // 2, 3)),
        ],
        compiler_params=params(call_id, 62),
        cost_estimate=cost(8 * all_rows * width * hidden, 8 * all_rows * width),
    )(queries, keys, values, opening, output, tokens, gate, up, grad_out, down)


def back_kernel(
    block,
    own_ref,
    weight_ref,
    low_ref,
    q_ref,
    k_ref,
    v_ref,
    att_ref,
    lse_ref,
    open_ref,
    cos_ref,
    sin_ref,
    heads_ref,
    hidden_hbm,
    out_grad_hbm,
    blocks_ref,
    normed_hbm,
    output_kept_ref,
    output_came_ref,
    down_kept_ref,
    down_came_ref,
    near_ref,
    far_ref,
    out_ref,
    qkv_ref,
    *scratch,
):
    here = Place()
    (
        buf,
        send_sems,
        recv_sems,
        part,
        hidden_ref,
        out_grad,
        grad_ref,
        output_away,
        down_away,
        dq_ref,
        dk_ref,
        dv_ref,
        share_out,
        share_in,
        back_ref,
        normed,
        kept,
        away,
        came,
        sums,
        near_sems,
        far_sems,
        local_sems,
        swap_sems,
        share_sems,
        fetch_sems,
        sum_sems,
        sum_near_sems,
        sum_far_sems,
    ) = scratch[SCATTER_SCRATCH:]
    rows, width = own_ref.shape
    cols = q_ref.shape[1]
    tile = 512
    units = 2 * here.length
    share = width // units

    hidden_copy = pltpu.make_async_copy(hidden_hbm, hidden_ref, local_sems.at[0])
    own_copy = pltpu.make_async_copy(
        blocks_ref.at[here.mine], near_ref.at[here.slot], local_sems.at[1]
    )
    near = block_spread(here, True, blocks_ref, near_ref, near_sems)
    far = block_spread(here, False, blocks_ref, far_ref, far_sems)
    swaps = [
        remote(src, dst, swap_sems.at[0, number], swap_sems.at[1, number], here.partner())
        for number, (src, dst) in enumerate(
            [(down_away, down_came_ref), (output_away, output_came_ref)]
        )
    ]

    def out_grad_copy(number):
        some = pl.ds(pl.multiple_of(number * share, share), share)
        slot = number % 2
        return pltpu.make_async_copy(
            out_grad_hbm.at[:, some], out_grad.at[slot], fetch_sems.at[0, slot]
        )

    hidden_copy.start()
    own_copy.start()
    out_grad_copy(jnp.int32(0)).start()
    here.call_all()
    put_own(here, own_ref, buf)
    part[...] = jnp.zeros_like(part)
    here.await_all()

    def split(values, kept_to, away_to, some):
        half = values.shape[0] // 2
        top, bottom = values[:half], values[half:]
        kept_to[:, some] = jnp.where(here.dp == 0, top, bottom)
        away_to[:, some] = jnp.where(here.dp == 0, bottom, top).astype(BF16)

    def compute(number, first):
        where = unit_rows(first, rows)
        unit = take_unit(buf, first)
        grad_ref[where, :] = dot_t(unit, weight_ref[...]).astype(BF16)
        attended = low_ref[where, :]
        for t in range(width // tile):
            some = slice(t * tile, (t + 1) * tile)
            part[:, some] += t_dot(attended, unit[:, some])
        pl.when(number == 0)(hidden_copy.wait)
        out_grad_copy(number).wait()
        pl.when(number + 1 < units)(lambda: out_grad_copy(number + 1).start())
        some = pl.ds(pl.multiple_of(number * share, share), share)
        split(t_dot(hidden_ref[...], out_grad[number % 2]), down_kept_ref, down_away, some)

    gather_units(here, buf, send_sems, recv_sems, compute, level=True)
    far.start()
    near.start()
    for t in range(width // tile):
        some = slice(t * tile, (t + 1) * tile)
        split(part[:, some], output_kept_ref, output_away, some)
    for one in swaps:
        one.start()

    tiles = q_ref.shape[0] // block
    scale = 1.0 / math.sqrt(HEAD_DIM)

    @pl.loop(0, tiles)
    def _(i):
        some = pl.ds(pl.multiple_of(i * block, block), block)
        attention_back_kernel(
            block,
            q_ref.at[some],
            k_ref,
            v_ref,
            grad_ref.at[some],
            att_ref.at[some],
            lse_ref.at[some],
            open_ref.at[some],
            dq_ref,
            dk_ref,
            dv_ref,
            i,
        )
        turned = rotated(dq_ref[...] * scale, cos_ref[some, :], -sin_ref[some, :])
        back_ref[some, :cols] = turned.astype(BF16)

    def share_copy(i):
        some = pl.ds(pl.multiple_of(i * block, block), block)
        return remote(
            share_out.at[some],
            share_in.at[some],
            share_sems.at[0, i],
            share_sems.at[1, i],
            here.sibling(),
        )

    @pl.loop(0, tiles)
    def _(i):
        some = pl.ds(pl.multiple_of(i * block, block), block)
        share_out[some, :] = jnp.where(here.core == 0, dv_ref[some, :], dk_ref[some, :]).astype(BF16)
        share_copy(i).start()

    @pl.loop(0, tiles)
    def _(i):
        some = pl.ds(pl.multiple_of(i * block, block), block)
        share_copy(i).wait()
        other = share_in[some, :].astype(F32)
        keys = rotated(dk_ref[some, :] + other, cos_ref[some, :], -sin_ref[some, :])
        back_ref[some, cols:] = jnp.where(here.core == 0, keys, dv_ref[some, :] + other).astype(BF16)

    swap = remote(away, came, sum_sems.at[0], sum_sems.at[1], here.partner())
    sum_near = block_spread(here, True, sums, qkv_ref.at[0], sum_near_sems)
    sum_far = block_spread(here, False, sums, qkv_ref.at[1], sum_far_sems)
    half = away.shape[0]
    chunk = normed.shape[2]
    chunks = half // chunk

    def normed_copy(number):
        dp = jnp.where(number < chunks, 1 - here.dp, here.dp)
        begin = dp * half + number % chunks * chunk
        slot = number % 2
        return pltpu.make_async_copy(
            normed_hbm.at[:, pl.ds(pl.multiple_of(begin, chunk), chunk)],
            normed.at[slot],
            fetch_sems.at[1, slot],
        )

    def heads_part(number):
        normed_copy(number).wait()
        pl.when(number + 1 < 2 * chunks)(lambda: normed_copy(number + 1).start())
        return t_dot(normed[number % 2], back_ref[...])

    normed_copy(jnp.int32(0)).start()

    def first(step):
        @pl.when(step == 2)
        def _():
            @pl.loop(0, chunks)
            def _(i):
                some = pl.ds(pl.multiple_of(i * chunk, chunk), chunk)
                away[some, :] = heads_part(i).astype(BF16)

            swap.start()

    def own_share():
        @pl.loop(0, chunks)
        def _(i):
            kept[pl.ds(pl.multiple_of(i * chunk, chunk), chunk), :] = heads_part(chunks + i)

    begin = 2
    each = 3

    def filler(step):
        @pl.when(step == begin)
        def _():
            swap.wait_recv()
            slab = sums.shape[1]

            @pl.loop(0, here.count)
            def _(i):
                some = pl.ds(pl.multiple_of(i * slab, slab), slab)
                sums[i] = (kept[some, :] + came[some, :].astype(F32)).astype(BF16)

            qkv_ref[0, here.slot] = sums[here.mine]

        @pl.when(step > begin)
        def _():
            @pl.loop(0, each)
            def _(i):
                number = (step - begin - 1) * each + i
                pl.when(number < sum_far.slots)(lambda: sum_far.start_one(number))

                @pl.when((number >= sum_far.slots) & (number < 2 * sum_far.slots - 1))
                def _():
                    sum_near.start_one(number - sum_far.slots + 1)

    scatter_rows_of_products(
        here,
        [(True, back_ref, heads_ref, out_ref)],
        *scratch[:SCATTER_SCRATCH],
        first=first,
        between=own_share,
        filler=filler,
    )
    swap.wait_send()
    for one in swaps:
        one.wait()
    near.finish()
    far.finish()
    own_copy.wait()
    sum_near.finish()
    sum_far.finish()


def attention_backwards(
    own,
    weight,
    attended,
    queries,
    keys,
    values,
    attended_sum,
    log_total,
    opening,
    cosine,
    sine,
    heads,
    hidden,
    grad_out,
    blocks,
    normed,
    block,
    call_id,
):
    seq = lax.axis_size("seq")
    rows, width = own.shape
    all_rows, cols = queries.shape
    slab = blocks.shape[1]
    half_hidden = hidden.shape[1] // 2
    chunk = width // 8
    bf16 = lambda *shape: jax.ShapeDtypeStruct(shape, BF16)
    f32 = lambda *shape: jax.ShapeDtypeStruct(shape, F32)
    dma = pltpu.SemaphoreType.DMA
    return pl.pallas_call(
        functools.partial(back_kernel, block),
        out_shape=[
            f32(cols // 2, width),
            bf16(cols // 2, width),
            f32(half_hidden, width),
            bf16(half_hidden, width),
            bf16(seq // 2, *blocks.shape[1:]),
            bf16(seq // 2, *blocks.shape[1:]),
            f32(rows, width),
            bf16(2, seq // 2, slab, 2 * cols),
        ],
        in_specs=[VMEM] * 12 + [HBM] * 4,
        out_specs=[VMEM, HBM, VMEM, HBM, HBM, HBM, VMEM, VMEM],
        scratch_shapes=scatter_scratch(seq, rows, width)
        + gather_scratch(seq, rows // 2, width)
        + [
            pltpu.VMEM((cols, width), F32),
            pltpu.VMEM(hidden.shape, BF16),
            pltpu.VMEM((2, all_rows, width // (seq // 2)), BF16),
            pltpu.VMEM((all_rows, cols), BF16),
            pltpu.VMEM((cols // 2, width), BF16),
            pltpu.VMEM((half_hidden, width), BF16),
            pltpu.VMEM((block, cols), F32),
            pltpu.VMEM((all_rows, cols), F32),
            pltpu.VMEM((all_rows, cols), F32),
            pltpu.VMEM((all_rows, cols), BF16),
            pltpu.VMEM((all_rows, cols), BF16),
            pltpu.VMEM((all_rows, 2 * cols), BF16),
            pltpu.VMEM((2, all_rows, chunk), BF16),
            pltpu.VMEM((width // 2, 2 * cols), F32),
            pltpu.VMEM((width // 2, 2 * cols), BF16),
            pltpu.VMEM((width // 2, 2 * cols), BF16),
            pltpu.VMEM((seq, slab, 2 * cols), BF16),
            dma((2, seq // 2)),
            dma((2, seq // 2)),
            dma((2,)),
            dma((2, 2)),
            dma((2, all_rows // block)),
            dma((2, 2)),
            dma((2,)),
            dma((2, seq // 2)),
            dma((2, seq // 2)),
        ],
        compiler_params=params(call_id, 62),
        cost_estimate=cost(12 * all_rows * width * cols, 12 * all_rows * width),
    )(
        own,
        weight,
        attended,
        queries,
        keys,
        values,
        attended_sum,
        log_total,
        opening,
        cosine,
        sine,
        heads,
        hidden,
        grad_out,
        blocks,
        normed,
    )


UNPACK_LINES = 4


def unpack_kernel(
    pair_ref,
    near_gate_ref,
    far_gate_ref,
    near_up_ref,
    far_up_ref,
    gate_ref,
    up_ref,
    qkv_ref,
    query_ref,
    key_ref,
    value_ref,
    gain_one_ref,
    gain_two_ref,
    tokens_ref,
    middle_ref,
    mixed_sum_ref,
    middle_grad_ref,
    upstream_ref,
    down_kept_ref,
    down_came_ref,
    output_kept_ref,
    output_came_ref,
    gate_out_ref,
    up_out_ref,
    query_out_ref,
    key_out_ref,
    value_out_ref,
    one_out_ref,
    two_out_ref,
    mixed_ref,
    token_grad_ref,
    down_out_ref,
    output_out_ref,
    total_two,
):
    pair = pair_ref[0]
    dp = lax.axis_size("dp")
    length = qkv_ref.shape[1] // 2
    slab = qkv_ref.shape[2]
    step = pl.program_id(0) * pl.num_programs(1) + pl.program_id(1)
    columns = near_gate_ref.shape[2]

    def along(grad, weight):
        return jnp.sum(grad * weight.astype(F32), axis=1, keepdims=True)

    @pl.when(step == 0)
    def _():
        total_two[...] = jnp.zeros_like(total_two)
        total = jnp.zeros((slab, 1), F32)
        gain = upright(gain_one_ref[...])

        def put(out_ref, weight_ref, begin, grad):
            cols = slice(begin, begin + grad.shape[1])
            out_ref[:, cols] = grad * gain
            return along(grad, weight_ref[:, cols])

        pairs = [{}, {}]
        for line in range(length):
            rows = []
            for number in range(4):
                slot = line * 2 + number % 2
                near, far = qkv_ref[0, slot].astype(F32), qkv_ref[1, slot].astype(F32)
                rows.append(jnp.where(number // 2 == pair, near, far))
            kv = [rows[core] + rows[core + 2] for core in range(2)]
            for half in range(dp):
                cols = slice(half * HEAD_DIM, (half + 1) * HEAD_DIM)
                for number in (0, 2):
                    two = jnp.concatenate([rows[number][:, cols], rows[number + 1][:, cols]], axis=1)
                    begin = (half * length * 4 + line * 4 + number) * HEAD_DIM
                    total = total + put(query_out_ref, query_ref, begin, two)
                for kind in range(2):
                    begin = (dp + half) * HEAD_DIM
                    pairs[kind][half, line] = kv[kind][:, begin : begin + HEAD_DIM]
        for kind, (out_ref, weight_ref) in enumerate(
            [(key_out_ref, key_ref), (value_out_ref, value_ref)]
        ):
            for half in range(dp):
                for line in range(0, length, 2):
                    two = [pairs[kind][half, line], pairs[kind][half, line + 1]]
                    begin = (half * length + line) * HEAD_DIM
                    total = total + put(
                        out_ref, weight_ref, begin, jnp.concatenate(two, axis=1)
                    )
        one_out_ref[...] = flat(total)

    mixed_ref[...] = middle_ref[...] + mixed_sum_ref[...]
    token_grad_ref[...] = middle_grad_ref[...] + norm_input_grad(
        tokens_ref[...].astype(F32), upstream_ref[...]
    )
    down_out_ref[...] = down_kept_ref[...] + down_came_ref[...].astype(F32)
    output_out_ref[...] = output_kept_ref[...] + output_came_ref[...].astype(F32)
    gain_two = upright(gain_two_ref[...])
    total = jnp.zeros((slab, 1), F32)
    for near_ref, far_ref, weight_ref, out_ref in (
        (near_gate_ref, far_gate_ref, gate_ref, gate_out_ref),
        (near_up_ref, far_up_ref, up_ref, up_out_ref),
    ):
        for number in range(2 * near_ref.shape[0]):
            slot = number // 4 * 2 + number % 2
            near, far = near_ref[slot].astype(F32), far_ref[slot].astype(F32)
            grad = jnp.where(number // 2 % 2 == pair, near, far)
            cols = slice(number * columns, (number + 1) * columns)
            total = total + along(grad, weight_ref[:, cols])
            out_ref[:, cols] = grad * gain_two
    total_two[...] += total

    @pl.when(step == pl.num_programs(0) * pl.num_programs(1) - 1)
    def _():
        two_out_ref[...] = flat(total_two[...])


def unpack(pair, near, far, gate, up, qkv, query, key, value, gain_one, gain_two, *rows):
    dp = lax.axis_size("dp")
    seq = lax.axis_size("seq")
    slab, ff = gate.shape
    length = seq // 4 // UNPACK_LINES
    columns = ff // (dp * seq)
    whole = lambda array: pl.BlockSpec(array.shape, lambda j, i: (0,) * array.ndim)
    block = lambda kind: pl.BlockSpec(
        (2 * UNPACK_LINES, slab, columns), lambda j, i: (i, 0, kind * dp + j)
    )
    tile = pl.BlockSpec((slab, 4 * UNPACK_LINES * columns), lambda j, i: (0, j * length + i))
    f32 = lambda array: jax.ShapeDtypeStruct(array.shape, F32)
    outs = [f32(gate), f32(up), f32(query), f32(key), f32(value), f32(gain_one), f32(gain_two)]
    sums = [f32(rows[0]), f32(rows[0]), f32(rows[5]), f32(rows[7])]
    steps = dp * length
    strip = lambda array: pl.BlockSpec(
        (array.shape[0] // steps, array.shape[1]), lambda j, i: (j * length + i, 0)
    )
    return pl.pallas_call(
        unpack_kernel,
        grid=(dp, length),
        in_specs=[pl.BlockSpec(memory_space=pltpu.SMEM)]
        + [block(0), block(0), block(1), block(1), tile, tile]
        + [whole(array) for array in (qkv, query, key, value, gain_one, gain_two)]
        + [strip(array) for array in rows],
        out_specs=[tile, tile]
        + [whole(array) for array in outs[2:]]
        + [strip(array) for array in sums],
        out_shape=outs + sums,
        scratch_shapes=[pltpu.VMEM((slab, 1), F32)],
        compiler_params=pltpu.CompilerParams(vmem_limit_bytes=60 << 20),
        cost_estimate=cost(slab * ff, 16 * slab * ff),
    )(
        pair,
        near,
        far,
        near,
        far,
        gate,
        up,
        qkv,
        query,
        key,
        value,
        gain_one,
        gain_two,
        *rows,
    )


def swap_dp(values):
    count = lax.axis_size("dp")
    return lax.ppermute(values, "dp", [(i, (i + 1) % count) for i in range(count)])


def gather_dp(values):
    return lax.all_gather(values, "dp", axis=0, tiled=True)


def sum_dp(partial):
    half = partial.shape[0] // 2
    mine = lax.axis_index("dp")
    away = lax.dynamic_slice_in_dim(partial, (1 - mine) * half, half, 0).astype(BF16)
    kept = lax.dynamic_slice_in_dim(partial, mine * half, half, 0)
    return kept + swap_dp(away).astype(F32)


def gather_rows(values):
    return lax.all_gather(values, "seq", axis=0, tiled=True)


def scatter_rows(partial):
    return lax.psum_scatter(partial.astype(BF16), "seq", scatter_dimension=0, tiled=True).astype(F32)


def exchange(blocks):
    return lax.all_to_all(blocks, "seq", split_axis=0, concat_axis=0, tiled=True)


def norm_factor(values):
    return lax.rsqrt(jnp.mean(values * values, axis=-1, keepdims=True) + EPS)


def norm_back(inputs, factor, gain_row, upstream):
    scaled_up = gain_row * upstream
    inner_mean = jnp.mean(scaled_up * inputs, axis=-1, keepdims=True)
    grad_in = factor * scaled_up - inputs * factor * factor * factor * inner_mean
    grad_gain = jnp.sum(upstream * inputs * factor, axis=0)
    return grad_in, grad_gain


def plain_shards(
    tokens,
    cotangent,
    doc_lengths,
    attn_gain,
    mlp_gain,
    query_weight,
    key_weight,
    value_weight,
    output_weight,
    gate_weight,
    up_weight,
    down_weight,
):
    dp = lax.axis_size("dp")
    seq = lax.axis_size("seq")
    mine = lax.axis_index("seq")
    tok_count, width = tokens.shape
    rows = tok_count * seq
    slab = query_weight.shape[0]
    share = HEAD_DIM // slab
    half_heads = HEADS // dp
    half_kv = KV_HEADS // dp
    hidden_dev = down_weight.shape[0]
    block = 512

    doc_ends = jnp.cumsum(doc_lengths[0])
    place = jnp.arange(rows, dtype=jnp.int32)
    passed = doc_ends[None, :] <= place[:, None]
    opening = jnp.max(jnp.where(passed, doc_ends[None, :], 0), axis=1)
    position = place - opening
    keeping = place < doc_ends[DOCS - 1]
    angles = position.astype(F32)[:, None] * rotary_table(HEAD_DIM)[None, :]
    cosine = jnp.cos(angles)
    sine = jnp.sin(angles)
    cos_heads = jnp.tile(cosine, (1, 2 * dp))
    sin_heads = jnp.tile(jnp.concatenate([-sine, sine], axis=1), (1, dp))
    own_keeping = lax.dynamic_slice_in_dim(keeping, mine * tok_count, tok_count, 0)

    def head_columns(weight, kept):
        split = weight.reshape(slab, dp, kept, HEAD_DIM)
        return jnp.repeat(split, seq // kept, axis=2)

    qkv_blocks = jnp.stack(
        [
            head_columns(query_weight, half_heads),
            head_columns(key_weight, half_kv),
            head_columns(value_weight, half_kv),
        ],
        axis=1,
    )
    qkv_blocks = jnp.transpose(qkv_blocks, (3, 0, 1, 2, 4)).reshape(seq * slab, 3 * dp * HEAD_DIM)
    qkv_weight = gather_dp(exchange(qkv_blocks))
    feed_blocks = jnp.stack(
        [w.reshape(slab, dp, seq, hidden_dev) for w in (gate_weight, up_weight)], axis=1
    )
    feed_blocks = jnp.transpose(feed_blocks, (3, 0, 1, 2, 4)).reshape(
        seq * slab, 2 * dp * hidden_dev
    )
    feed_weight = gather_dp(exchange(feed_blocks))
    down_own = gather_dp(down_weight)
    output_own = output_weight
    if share > 1:
        groups = [list(range(i, i + share)) for i in range(0, seq, share)]
        output_own = lax.all_gather(
            output_own, "seq", axis=0, tiled=True, axis_index_groups=groups
        )
    output_own = gather_dp(output_own)
    gains = lax.all_gather(
        jnp.stack([attn_gain, mlp_gain]), ("dp", "seq"), axis=1, tiled=True
    ).astype(F32)
    gain_one, gain_two = gains[0], gains[1]

    inputs_all = gather_rows(tokens).astype(F32)
    normed_one = (inputs_all * norm_factor(inputs_all) * gain_one).astype(BF16)
    qkv = dot(normed_one, qkv_weight)
    head_cols = dp * HEAD_DIM
    query_lin, key_lin = qkv[:, :head_cols], qkv[:, head_cols : 2 * head_cols]
    values = qkv[:, 2 * head_cols :].astype(BF16)
    scale = 1.0 / math.sqrt(HEAD_DIM)
    queries = (query_lin * cos_heads + swap_halves(query_lin) * sin_heads).astype(BF16) * BF16(scale)
    keys = (key_lin * cos_heads + swap_halves(key_lin) * sin_heads).astype(BF16)
    attended_sum, log_total = attention(queries, keys, values, opening[:, None], block)
    if share > 1:
        own_rows = ((place // tok_count) % share == mine % share)[:, None]
        attended_sum = jnp.where(own_rows, attended_sum, 0.0)
    attended = attended_sum.astype(BF16)
    inputs = tokens.astype(F32)
    middle = inputs + scatter_rows(dot(attended, output_own))

    factor_two = norm_factor(middle)
    normed_two = gather_rows((middle * factor_two * gain_two).astype(BF16))
    grad_own = jnp.where(own_keeping[:, None], cotangent, BF16(0))
    grad_out = gather_rows(grad_own)
    feed = dot(normed_two, feed_weight)
    feed_cols = dp * hidden_dev
    gate_lin, upward = feed[:, :feed_cols], feed[:, feed_cols:]
    sigmoid = jax.nn.sigmoid(gate_lin)
    hidden = (gate_lin * sigmoid * upward).astype(BF16)
    hidden_grad = dot_t(grad_out, down_own)
    gate_back = (hidden_grad * upward * sigmoid * (1.0 + gate_lin * (1.0 - sigmoid))).astype(BF16)
    up_back = (hidden_grad * gate_lin * sigmoid).astype(BF16)
    feed_back = jnp.concatenate([gate_back, up_back], axis=1)
    normed_two_grad = scatter_rows(dot_t(feed_back, feed_weight))
    mixed = middle + scatter_rows(dot(hidden, down_own))
    middle_in, gain_two_part = norm_back(middle, factor_two, gain_two, normed_two_grad)
    middle_grad = grad_own.astype(F32) + middle_in
    middle_back = gather_rows(middle_grad.astype(BF16))

    attended_grad = dot_t(middle_back, output_own).astype(BF16)
    if share > 1:
        attended_grad = jnp.where(own_rows, attended_grad, BF16(0))
    query_acc, key_acc, value_acc = attention_back(
        queries, keys, values, attended_grad, attended_sum, log_total, opening[:, None], block
    )
    query_acc = query_acc * scale
    query_back = query_acc * cos_heads - swap_halves(query_acc) * sin_heads
    key_back = key_acc * cos_heads - swap_halves(key_acc) * sin_heads
    qkv_back = jnp.concatenate([query_back, key_back, value_acc], axis=1).astype(BF16)
    normed_one_grad = scatter_rows(dot_t(qkv_back, qkv_weight))
    input_in, gain_one_part = norm_back(inputs, norm_factor(inputs), gain_one, normed_one_grad)
    token_grad = middle_grad + input_in

    feed_grad = exchange(sum_dp(t_dot(normed_two, feed_back)).astype(BF16)).astype(F32)
    feed_grad = feed_grad.reshape(seq, slab, 2, dp, hidden_dev)
    feed_grad = jnp.transpose(feed_grad, (2, 1, 3, 0, 4)).reshape(2, slab, dp * seq * hidden_dev)
    down_grad = sum_dp(t_dot(hidden, grad_out))
    output_part = t_dot(attended, middle_back)
    if share > 1:
        split = output_part.reshape(dp, share, slab, width)
        split = jnp.transpose(split, (1, 0, 2, 3)).reshape(share * dp * slab, width)
        output_part = lax.psum_scatter(
            split, "seq", scatter_dimension=0, tiled=True, axis_index_groups=groups
        )
    output_grad = sum_dp(output_part)
    qkv_grad = exchange(sum_dp(t_dot(normed_one, qkv_back)).astype(BF16)).astype(F32)
    qkv_grad = qkv_grad.reshape(seq, slab, 3, dp, HEAD_DIM)

    def own_columns(part, kept):
        summed = jnp.sum(part.reshape(kept, seq // kept, slab, dp, HEAD_DIM), axis=1)
        return jnp.transpose(summed, (1, 2, 0, 3)).reshape(slab, dp * kept * HEAD_DIM)

    query_grad = own_columns(qkv_grad[:, :, 0], half_heads)
    key_grad = own_columns(qkv_grad[:, :, 1], half_kv)
    value_grad = own_columns(qkv_grad[:, :, 2], half_kv)
    gain_parts = lax.psum(jnp.stack([gain_one_part, gain_two_part]), ("dp", "seq"))
    own = lax.axis_index("dp") * seq + mine
    gain_grads = lax.dynamic_slice_in_dim(gain_parts, own * slab, slab, 1)
    return (
        mixed,
        token_grad,
        gain_grads[0],
        gain_grads[1],
        query_grad,
        key_grad,
        value_grad,
        output_grad,
        feed_grad[0],
        feed_grad[1],
        down_grad,
    )


def frequencies():
    exponent = np.arange(0, HEAD_DIM, 2, dtype=np.float32) / np.float32(HEAD_DIM)
    inverse = np.power(np.float32(500000.0), -exponent)
    wavelength = np.float32(2.0 * math.pi) / inverse
    smooth = (np.float32(8192.0) / wavelength - np.float32(1.0)) / np.float32(3.0)
    blended = (np.float32(1.0) - smooth) * inverse / np.float32(32.0) + smooth * inverse
    scaled = np.where(
        wavelength < 2048.0,
        inverse,
        np.where(wavelength > 8192.0, inverse / np.float32(32.0), blended),
    )
    return np.tile(scaled.astype(np.float32), 4)


FREQUENCIES = frequencies()


def shards(
    tokens,
    cotangent,
    doc_lengths,
    attn_gain,
    mlp_gain,
    query_weight,
    key_weight,
    value_weight,
    output_weight,
    gate_weight,
    up_weight,
    down_weight,
):
    dp = lax.axis_size("dp")
    seq = lax.axis_size("seq")
    mine = lax.axis_index("seq")
    tok_count, width = tokens.shape
    slab = query_weight.shape[0]
    block = 512
    gain_one = attn_gain[None, :]
    gain_two = mlp_gain[None, :]

    (
        normed_one,
        grad_out,
        queries,
        keys,
        values,
        cosine,
        sine,
        opening,
        qkv_weight,
        gate_scaled,
        up_scaled,
        down_own,
        output_own,
    ) = gather_project(
        doc_lengths,
        tokens,
        cotangent,
        query_weight,
        key_weight,
        value_weight,
        gate_weight,
        up_weight,
        (gain_one, gain_two),
        jnp.asarray(FREQUENCIES)[None, :],
        down_weight,
        output_weight,
        0,
    )
    qkv_weight = qkv_weight.reshape(width, -1)
    down_own = down_own.reshape(-1, width)
    output_own = output_own.reshape(-1, width)
    attended_sum, log_total, attended, middle, normed_two, hidden, feed_back, feed_turned = (
        feed_both_ways(
            queries,
            keys,
            values,
            opening,
            output_own,
            tokens,
            gate_scaled,
            up_scaled,
            grad_out,
            down_own,
            block,
            1,
        )
    )

    middle_grad, middle_back, mixed_sum, feed_sums = product_scatter_both(
        feed_back, feed_turned, hidden, down_own, middle, grad_out, normed_two, 4
    )
    feed_sums = feed_sums.reshape(seq, slab, -1)
    (
        output_kept,
        output_came,
        down_kept,
        down_came,
        feed_grad_near,
        feed_grad_far,
        normed_one_grad,
        qkv_grads,
    ) = attention_backwards(
        middle_back,
        output_own,
        attended,
        queries,
        keys,
        values,
        attended_sum,
        log_total,
        opening,
        cosine,
        sine,
        qkv_weight,
        hidden,
        grad_out,
        feed_sums,
        normed_one,
        block,
        5,
    )

    pair = ((mine // 2) % 2).reshape(1)
    (
        gate_grad,
        up_grad,
        query_grad,
        key_grad,
        value_grad,
        attn_gain_grad,
        mlp_gain_grad,
        mixed,
        token_grad,
        down_grad,
        output_grad,
    ) = unpack(
        pair,
        feed_grad_near,
        feed_grad_far,
        gate_weight,
        up_weight,
        qkv_grads,
        query_weight,
        key_weight,
        value_weight,
        gain_one,
        gain_two,
        tokens,
        middle,
        mixed_sum,
        middle_grad,
        normed_one_grad,
        down_kept,
        down_came,
        output_kept,
        output_came,
    )
    return (
        mixed,
        token_grad,
        attn_gain_grad[0],
        mlp_gain_grad[0],
        query_grad,
        key_grad,
        value_grad,
        output_grad,
        gate_grad,
        up_grad,
        down_grad,
    )


def solution(mesh):
    both = P(("dp", "seq"), None)
    line = P(("dp", "seq"))
    dp, seq = mesh.shape["dp"], mesh.shape["seq"]

    def run(*args):
        tokens = args[0].shape[0]
        width = args[0].shape[1]
        suits = dp == 2 and seq % 4 == 0 and width == dp * seq * HEAD_DIM
        suits = suits and 2 * (tokens // dp) * width <= 16 << 20
        return jax.shard_map(
            shards if suits else plain_shards,
            mesh=mesh,
            in_specs=(both, both, P("dp", None), line, line) + (both,) * 7,
            out_specs=(both, both, line, line) + (both,) * 7,
            check_vma=False,
        )(*args)

    return run
```

```python
import functools
import math

import jax
import jax.numpy as jnp
import numpy as np
from jax import lax
from jax.experimental import pallas as pl
from jax.experimental.pallas import tpu as pltpu
from jax.sharding import PartitionSpec as P

HEADS = 32
KV_HEADS = 8
HEAD_DIM = 64
DOCS = 4
EPS = 1e-05
NEG = -1e30
MESH = pl.DeviceIdType.MESH
F32 = jnp.float32
BF16 = jnp.bfloat16


def rotary_table(head_dim):
    exponent = jnp.arange(0, head_dim, 2, dtype=F32) / head_dim
    inverse = jnp.power(F32(500000.0), -exponent)
    wavelength = 2.0 * math.pi / inverse
    smooth = (8192.0 / wavelength - 1.0) / 3.0
    blended = (1.0 - smooth) * inverse / 32.0 + smooth * inverse
    return jnp.where(
        wavelength < 2048.0, inverse, jnp.where(wavelength > 8192.0, inverse / 32.0, blended)
    )


def swap_halves(values):
    rows, cols = values.shape
    halves = values.reshape(rows, cols // HEAD_DIM, 2, HEAD_DIM // 2)
    return halves[:, :, ::-1].reshape(rows, cols)


def dot(a, b):
    return jnp.dot(a, b, preferred_element_type=F32)


def dot_t(a, b):
    return lax.dot_general(a, b, (((1,), (1,)), ((), ())), preferred_element_type=F32)


def t_dot(a, b):
    return lax.dot_general(a, b, (((0,), (0,)), ((), ())), preferred_element_type=F32)


def allowed_tile(opening, q_first, k_first, shape):
    rows = q_first + lax.broadcasted_iota(jnp.int32, shape, 0)
    cols = k_first + lax.broadcasted_iota(jnp.int32, shape, 1)
    return (cols <= rows) & (cols >= opening)


def attention_kernel(block, q_ref, k_ref, v_ref, open_ref, out_ref, lse_ref, tile=None):
    if tile is None:
        tile = pl.program_id(0)
    opening = open_ref[...]
    heads = [
        slice(i * HEAD_DIM, (i + 1) * HEAD_DIM) for i in range(q_ref.shape[1] // HEAD_DIM)
    ]

    def step(j, carry):
        first = pl.multiple_of(j * block, block)
        allowed = allowed_tile(opening, tile * block, first, (block, block))
        after = []
        for lanes, (peak, total, acc) in zip(heads, carry):
            scores = dot_t(q_ref[:, lanes], k_ref[pl.ds(first, block), lanes])
            scores = jnp.where(allowed, scores, NEG)
            new_peak = jnp.maximum(peak, jnp.max(scores, axis=1, keepdims=True))
            spread = jnp.exp(scores - new_peak)
            fade = jnp.exp(peak - new_peak)
            total = total * fade + jnp.sum(spread, axis=1, keepdims=True)
            acc = acc * fade + dot(spread.astype(BF16), v_ref[pl.ds(first, block), lanes])
            after.append((new_peak, total, acc))
        return tuple(after)

    start = (
        jnp.full((block, 1), NEG, F32),
        jnp.zeros((block, 1), F32),
        jnp.zeros((block, HEAD_DIM), F32),
    )
    done = lax.fori_loop(0, tile + 1, step, (start,) * len(heads))
    for head, (lanes, (peak, total, acc)) in enumerate(zip(heads, done)):
        out_ref[:, lanes] = acc / total
        lse_ref[:, head : head + 1] = peak + jnp.log(total)


def attention(queries, keys, values, opening, block):
    rows, cols = queries.shape
    heads = cols // HEAD_DIM
    tiled = lambda width: pl.BlockSpec((block, width), lambda i: (i, 0))
    whole = pl.BlockSpec((rows, cols), lambda i: (0, 0))
    return pl.pallas_call(
        functools.partial(attention_kernel, block),
        grid=(rows // block,),
        in_specs=[tiled(cols), whole, whole, tiled(1)],
        out_specs=[tiled(cols), tiled(heads)],
        out_shape=[
            jax.ShapeDtypeStruct((rows, cols), F32),
            jax.ShapeDtypeStruct((rows, heads), F32),
        ],
        compiler_params=pltpu.CompilerParams(vmem_limit_bytes=48 << 20),
        cost_estimate=pl.CostEstimate(
            flops=2 * rows * rows * cols, bytes_accessed=10 * rows * cols, transcendentals=0
        ),
    )(queries, keys, values, opening)


def attention_back_kernel(
    block,
    q_ref,
    k_ref,
    v_ref,
    g_ref,
    att_ref,
    lse_ref,
    open_ref,
    dq_ref,
    dk_ref,
    dv_ref,
    tile=None,
):
    if tile is None:
        tile = pl.program_id(0)

    @pl.when(tile == 0)
    def _():
        dk_ref[...] = jnp.zeros_like(dk_ref)
        dv_ref[...] = jnp.zeros_like(dv_ref)

    count = q_ref.shape[1] // HEAD_DIM
    columns = [open_ref[...].astype(F32), lse_ref[...]]
    for head in range(count):
        lanes = slice(head * HEAD_DIM, (head + 1) * HEAD_DIM)
        grad = g_ref[:, lanes].astype(F32)
        columns.append(jnp.sum(grad * att_ref[:, lanes], axis=1, keepdims=True))
    columns.append(jnp.zeros((block, 127 - 2 * count), F32))
    across = jnp.concatenate(columns, axis=1).T
    opening = across[0:1].astype(jnp.int32)
    heads = [
        (
            slice(head * HEAD_DIM, (head + 1) * HEAD_DIM),
            across[1 + head : 2 + head],
            across[1 + count + head : 2 + count + head],
        )
        for head in range(count)
    ]

    def step(j, carry):
        first = pl.multiple_of(j * block, block)
        here = pl.ds(first, block)
        keys = first + lax.broadcasted_iota(jnp.int32, (block, block), 0)
        places = tile * block + lax.broadcasted_iota(jnp.int32, (block, block), 1)
        allowed = (keys <= places) & (keys >= opening)
        after = []
        for (lanes, log_total, row_sum), acc in zip(heads, carry):
            query, grad, key = q_ref[:, lanes], g_ref[:, lanes], k_ref[here, lanes]
            scores = dot_t(key, query)
            chance = jnp.where(allowed, jnp.exp(scores - log_total), 0.0)
            prob_grad = dot_t(v_ref[here, lanes], grad)
            score_grad = (chance * (prob_grad - row_sum)).astype(BF16)
            dk_ref[here, lanes] += dot(score_grad, query)
            dv_ref[here, lanes] += dot(chance.astype(BF16), grad)
            after.append(acc + t_dot(score_grad, key))
        return tuple(after)

    start = jnp.zeros((block, HEAD_DIM), F32)
    done = lax.fori_loop(0, tile + 1, step, (start,) * len(heads))
    for (lanes, _, _), acc in zip(heads, done):
        dq_ref[:, lanes] = acc


def attention_back(queries, keys, values, grads, attended, log_total, opening, block):
    rows, cols = queries.shape
    heads = cols // HEAD_DIM
    tiled = lambda width: pl.BlockSpec((block, width), lambda i: (i, 0))
    whole = pl.BlockSpec((rows, cols), lambda i: (0, 0))
    return pl.pallas_call(
        functools.partial(attention_back_kernel, block),
        grid=(rows // block,),
        in_specs=[tiled(cols), whole, whole, tiled(cols), tiled(cols), tiled(heads), tiled(1)],
        out_specs=[tiled(cols), whole, whole],
        out_shape=[jax.ShapeDtypeStruct((rows, cols), F32)] * 3,
        compiler_params=pltpu.CompilerParams(vmem_limit_bytes=60 << 20),
        cost_estimate=pl.CostEstimate(
            flops=5 * rows * rows * cols, bytes_accessed=20 * rows * cols, transcendentals=0
        ),
    )(queries, keys, values, grads, attended, log_total, opening)


def nothing():
    pass


class Place:
    def __init__(self):
        self.dp = lax.axis_index("dp")
        self.mine = lax.axis_index("seq")
        self.count = lax.axis_size("seq")
        self.length = self.count // 4
        self.line = lax.div(self.mine, 4)
        self.pair = lax.rem(lax.div(self.mine, 2), 2)
        self.core = lax.rem(self.mine, 2)
        self.slot = self.line * 2 + self.core

    def index(self, line, pair, core):
        return (line * 2 + pair) * 2 + core

    def peer(self, slot, same):
        pair = self.pair if same else 1 - self.pair
        return self.index(lax.div(slot, 2), pair, lax.rem(slot, 2))

    def device(self, line, pair, core):
        return (self.dp, self.index(line, pair, core))

    def sibling(self):
        return self.device(self.line, self.pair, 1 - self.core)

    def across(self):
        return self.device(self.line, 1 - self.pair, self.core)

    def above(self):
        return self.device(self.line + 1, self.pair, self.core)

    def below(self):
        return self.device(self.line - 1, self.pair, self.core)

    def partner(self):
        return (1 - self.dp, self.mine)

    def greet(self, partner=False):
        barrier = pltpu.get_barrier_semaphore()

        def signal(device):
            pl.semaphore_signal(barrier, inc=1, device_id=device, device_id_type=MESH)

        signal(self.sibling())
        signal(self.across())
        pl.when(self.line > 0)(lambda: signal(self.below()))
        pl.when(self.line < self.length - 1)(lambda: signal(self.above()))
        if partner:
            signal(self.partner())
        inner = (self.line > 0) & (self.line < self.length - 1)
        pl.semaphore_wait(barrier, jnp.where(inner, 4, 3) + (1 if partner else 0))

    def greet_all(self, meanwhile=nothing):
        self.call_all()
        meanwhile()
        self.await_all()

    def await_all(self):
        pl.semaphore_wait(pltpu.get_barrier_semaphore(), self.count)

    def call_all(self):
        barrier = pltpu.get_barrier_semaphore()

        def signal(device):
            pl.semaphore_signal(barrier, inc=1, device_id=device, device_id_type=MESH)

        signal(self.partner())

        @pl.loop(1, self.count)
        def _(ahead):
            signal((self.dp, lax.rem(self.mine + ahead, self.count)))


def remote(src, dst, send_sem, recv_sem, device):
    return pltpu.make_async_remote_copy(
        src_ref=src,
        dst_ref=dst,
        send_sem=send_sem,
        recv_sem=recv_sem,
        device_id=device,
        device_id_type=MESH,
    )


class Spread:
    def __init__(self, here, same, copies):
        self.here, self.same, self.copies = here, same, copies
        self.slots = here.count // 2

    def each(self, visit):
        @pl.loop(1 if self.same else 0, self.slots)
        def _(ahead):
            slot = lax.rem(self.here.slot + ahead, self.slots)
            visit(self.here.peer(slot, self.same), slot)

    def start_one(self, ahead):
        slot = lax.rem(self.here.slot + ahead, self.slots)
        peer = self.here.peer(slot, self.same)
        for one in self.copies(peer, self.here.mine, self.here.slot, slot):
            one.start()

    def start(self):
        pl.loop(1 if self.same else 0, self.slots)(self.start_one)

    def start_some(self, number, each):
        first = 1 if self.same else 0

        @pl.loop(0, each)
        def _(i):
            ahead = first + number * each + i
            pl.when((number >= 0) & (ahead < self.slots))(lambda: self.start_one(ahead))

    def finish(self):
        def visit(peer, slot):
            for one in self.copies(peer, peer, slot, slot):
                one.wait()

        self.each(visit)


def block_spread(here, same, blocks, into, sems):
    def copies(peer, sender, at, sem):
        return [
            remote(
                blocks.at[peer],
                into.at[at],
                sems.at[0, sem],
                sems.at[1, at],
                (here.dp, peer),
            )
        ]

    return Spread(here, same, copies)


def gather_units(here, buf, send_sems, recv_sems, compute, between=None, ready=None, started=nothing, level=False):
    length = here.length
    last = length - 1
    steps = 2 * length
    mine = here.mine
    shorter = jnp.minimum(here.line, last - here.line)
    longer = jnp.where(here.line < last - here.line, 1, -1)

    def column(j):
        i = j - 1
        paired = jnp.where(i % 2 == 0, here.line - i // 2 - 1, here.line + i // 2 + 1)
        single = here.line + longer * (i - shorter + 1)
        return jnp.where(j == 0, here.line, jnp.where(i < 2 * shorter, paired, single))

    keep = buf.shape[2] * 3 // 4

    def copy(way, device, block, piece):
        if piece == 2:
            ref, sem = buf.at[block, 1, pl.ds(0, keep)], 1
        elif piece == 3:
            ref, sem = buf.at[block, 1, pl.ds(keep, buf.shape[2] - keep)], 2
        else:
            ref, sem = buf.at[block, piece], piece
        return remote(ref, ref, send_sems.at[way, block, sem], recv_sems.at[block, sem], device)

    def up(block, piece):
        return copy(0, here.above(), block, piece)

    def down(block, piece):
        return copy(1, here.below(), block, piece)

    def across(block, piece):
        return copy(2, here.across(), block, piece)

    def sideways(block, piece):
        return copy(3, here.sibling(), block, piece)

    def unit(number):
        in_column = (number % 2 == 1) & (number < steps - 1) | (number == 0)
        later = jnp.where(number == steps - 1, last, number // 2 - 1)
        line = column(jnp.where(in_column, (number + 1) // 2, later))
        pair = jnp.where(in_column, here.pair, 1 - here.pair)
        other = here.index(line, pair, 1 - here.core)
        sideways(other, 0).wait_recv()
        if level:
            whole = in_column | (line == here.line)
            pl.when(whole)(lambda: sideways(other, 1).wait_recv())

            @pl.when(jnp.logical_not(whole))
            def _():
                sideways(other, 2).wait_recv()
                sideways(other, 3).wait_recv()

        else:
            sideways(other, 1).wait_recv()

        compute(number, here.index(line, pair, 0))

    for piece in range(2):
        pl.when(here.line < last)(lambda piece=piece: up(mine, piece).start())
        pl.when(here.line > 0)(lambda piece=piece: down(mine, piece).start())
        across(mine, piece).start()
        sideways(mine, piece).start()
    started()
    beside = here.index(here.line, 1 - here.pair, here.core)

    def relay(far, pair, piece):
        @pl.when(here.line >= far)
        def _():
            block = here.index(here.line - far, pair, here.core)
            up(block, piece).wait_recv()
            pl.when(here.line < last)(lambda: up(block, piece).start())
            sideways(block, piece).start()

        @pl.when(here.line + far <= last)
        def _():
            block = here.index(here.line + far, pair, here.core)
            down(block, piece).wait_recv()
            pl.when(here.line > 0)(lambda: down(block, piece).start())
            sideways(block, piece).start()

    @pl.loop(0, length)
    def _(round):
        for part in range(2):
            step = 2 * round + part
            relay(round + 1, here.pair, part)

            @pl.when(round < last)
            def _():
                block = here.index(column(round + 1), here.pair, here.core)
                across(block, (2 if level else 1) if part else 0).start()

            block = here.index(column(round), 1 - here.pair, here.core)
            if part == 0 or not level:
                across(block, part).wait_recv()
                sideways(block, part).start()
            else:

                @pl.when(round == 0)
                def _():
                    across(beside, 1).wait_recv()
                    pl.when(here.line < last)(lambda: up(beside, 3).start())
                    pl.when(here.line > 0)(lambda: down(beside, 3).start())
                    sideways(beside, 1).start()

                @pl.when(round > 0)
                def _():
                    across(block, 2).wait_recv()
                    sideways(block, 2).start()
                    relay(round, 1 - here.pair, 3)

            if between is not None:
                between(step)
            if ready is None:
                unit(step)
            else:
                begin = jnp.maximum(2 * (step - ready), 0)
                end = jnp.maximum(2 * (step + 1 - ready), 0)

                @pl.loop(begin, end)
                def _(number):
                    unit(number)

    @pl.loop(0, length)
    def _(line):
        own = here.index(line, here.pair, here.core)
        other = here.index(line, 1 - here.pair, here.core)
        goes_up = (line <= here.line) & (here.line < last)
        goes_down = (line >= here.line) & (here.line > 0)

        @pl.when(goes_up)
        def _():
            up(own, 0).wait_send()
            up(own, 1).wait_send()
            if level:
                up(other, 3).wait_send()

        @pl.when(goes_down)
        def _():
            down(own, 0).wait_send()
            down(own, 1).wait_send()
            if level:
                down(other, 3).wait_send()

        across(own, 0).wait_send()
        sideways(own, 0).wait_send()
        sideways(own, 1).wait_send()
        sideways(other, 0).wait_send()

        if not level:
            across(own, 1).wait_send()
            sideways(other, 1).wait_send()
            return

        @pl.when(line == here.line)
        def _():
            across(own, 1).wait_send()
            sideways(other, 1).wait_send()

        @pl.when(line != here.line)
        def _():
            across(own, 2).wait_send()
            sideways(other, 2).wait_send()
            sideways(other, 3).wait_send()


def put_own(here, own_ref, buf):
    half = buf.shape[2]
    for part in range(2):
        buf[here.mine, part] = own_ref[pl.ds(part * half, half), :]


def gather_scratch(seq, rows, width):
    return [
        pltpu.VMEM((seq, 2, rows, width), BF16),
        pltpu.SemaphoreType.DMA((4, seq, 3)),
        pltpu.SemaphoreType.DMA((seq, 3)),
    ]


def unit_rows(first, rows):
    return pl.ds(pl.multiple_of(first * rows, 2 * rows), 2 * rows)


def take_unit(buf, first):
    blocks = buf[pl.ds(first, 2)]
    return blocks.reshape(-1, blocks.shape[-1])


class UnitStore:
    def __init__(self, buf, out_ref, sems):
        self.buf, self.out_ref, self.sems = buf, out_ref, sems

    def copies(self, number, first):
        half = self.buf.shape[2]
        made = []
        for block in range(2):
            for part in range(2):
                begin = ((first + block) * 2 + part) * half
                made.append(
                    pltpu.make_async_copy(
                        self.buf.at[first + block, part],
                        self.out_ref.at[pl.ds(pl.multiple_of(begin, half), half)],
                        self.sems.at[number, block, part],
                    )
                )
        return made

    def start(self, number, first):
        for one in self.copies(number, first):
            one.start()

    def finish(self):
        @pl.loop(0, self.sems.shape[0])
        def _(number):
            for one in self.copies(number, 0):
                one.wait()


def params(call_id, mebibytes):
    return pltpu.CompilerParams(
        collective_id=call_id, has_side_effects=True, vmem_limit_bytes=mebibytes << 20
    )


def cost(flops, bytes_accessed):
    return pl.CostEstimate(flops=flops, bytes_accessed=bytes_accessed, transcendentals=0)


VMEM = pl.BlockSpec(memory_space=pltpu.VMEM)
HBM = pl.BlockSpec(memory_space=pl.ANY)


def rotated(values, cosine, sine):
    cols = values.shape[1]
    lane = lax.broadcasted_iota(jnp.int32, values.shape, 1)
    ahead = pltpu.roll(values, cols - HEAD_DIM // 2, 1)
    behind = pltpu.roll(values, HEAD_DIM // 2, 1)
    swapped = jnp.where(lane % HEAD_DIM < HEAD_DIM // 2, ahead, behind)
    return values * cosine + swapped * sine


def upright(row):
    count = row.shape[1]
    shape = (count, count)
    same = lax.broadcasted_iota(jnp.int32, shape, 0) == lax.broadcasted_iota(jnp.int32, shape, 1)
    return jnp.sum(jnp.where(same, row.astype(F32), 0.0), axis=1, keepdims=True)


def flat(column):
    count = column.shape[0]
    shape = (count, count)
    same = lax.broadcasted_iota(jnp.int32, shape, 0) == lax.broadcasted_iota(jnp.int32, shape, 1)
    return jnp.sum(jnp.where(same, column, 0.0), axis=0, keepdims=True)


def project_kernel(
    lengths_ref,
    tokens_ref,
    cotangent_ref,
    query_ref,
    key_ref,
    value_ref,
    gate_ref,
    up_ref,
    gain_one_ref,
    gain_two_ref,
    freq_ref,
    down_ref,
    output_ref,
    normed_ref,
    grads_ref,
    q_ref,
    k_ref,
    v_ref,
    cos_ref,
    sin_ref,
    open_ref,
    weight_ref,
    gate_out_ref,
    up_out_ref,
    down_out_ref,
    output_out_ref,
    buf,
    send_sems,
    recv_sems,
    blocks,
    store_sems,
    near_sems,
    far_sems,
    swap_sems,
    local_sems,
    pair_sems,
    share_sems,
):
    here = Place()
    cols = q_ref.shape[1]
    rows = tokens_ref.shape[0]
    dp = here.dp
    ends = [lengths_ref[0, 0]]
    for j in range(1, DOCS):
        ends.append(ends[-1] + lengths_ref[0, j])

    def own_rows():
        chunk = 32

        @pl.loop(0, rows // chunk)
        def _(i):
            some = pl.ds(pl.multiple_of(i * chunk, chunk), chunk)
            values = tokens_ref[some, :].astype(F32)
            factor = lax.rsqrt(jnp.mean(values * values, axis=1, keepdims=True) + EPS)
            buf[here.mine, 0, some, :] = (values * factor).astype(BF16)
            shape = (chunk, cotangent_ref.shape[1])
            place = here.mine * rows + i * chunk + lax.broadcasted_iota(jnp.int32, shape, 0)
            grads = cotangent_ref[some, :].astype(F32)
            buf[here.mine, 1, some, :] = jnp.where(place < ends[-1], grads, 0.0).astype(BF16)

    def own_blocks():
        gain = upright(gain_one_ref[...])
        query = query_ref[...].astype(F32) * gain
        key = key_ref[...].astype(F32) * gain
        value = value_ref[...].astype(F32) * gain

        def heads(array, number, kept):
            parts = []
            for half in range(2):
                head = half * kept + number * kept // blocks.shape[0]
                parts.append(array[:, head * HEAD_DIM : (head + 1) * HEAD_DIM])
            return jnp.concatenate(parts, axis=1).astype(BF16)

        for number in range(blocks.shape[0]):
            blocks[number, :, :cols] = heads(query, number, HEADS // 2)
            array = value if number % 2 else key
            blocks[number, :, cols:] = heads(array, number, KV_HEADS // 2)

    def own_parts():
        own_blocks()
        own_rows()

    here.greet_all(own_parts)

    def weight_spread(same, sems):
        def copies(peer, sender, at, sem):
            return [
                remote(
                    blocks.at[peer],
                    weight_ref.at[dp, sender],
                    sems.at[0, sem],
                    sems.at[1, at],
                    (dp, peer),
                )
            ]

        return Spread(here, same, copies)

    near = weight_spread(True, near_sems)
    far = weight_spread(False, far_sems)
    swaps = []
    for number, (src, dst) in enumerate([(down_ref, down_out_ref), (output_ref, output_out_ref)]):
        swaps.append(
            remote(src, dst.at[dp], swap_sems.at[0, number], swap_sems.at[1, number], here.partner())
        )
        swaps.append(pltpu.make_async_copy(src, dst.at[dp], local_sems.at[number]))
    def pair_copy(source, sender):
        return remote(
            weight_ref.at[source, sender],
            weight_ref.at[source, sender],
            pair_sems.at[0, sender],
            pair_sems.at[1, sender],
            here.partner(),
        )

    def own_tables():
        chunk = 128

        @pl.loop(0, open_ref.shape[0] // chunk)
        def _(i):
            some = pl.ds(pl.multiple_of(i * chunk, chunk), chunk)
            place = i * chunk + lax.broadcasted_iota(jnp.int32, (chunk, 1), 0)
            opening = jnp.zeros((chunk, 1), jnp.int32)
            for end in ends:
                opening = jnp.where(place >= end, end, opening)
            open_ref[some, :] = opening
            angles = (place - opening).astype(F32) * freq_ref[...]
            lane = lax.broadcasted_iota(jnp.int32, angles.shape, 1)
            sine = jnp.sin(angles)
            cos_ref[some, :] = jnp.cos(angles)
            sin_ref[some, :] = jnp.where(lane % HEAD_DIM < HEAD_DIM // 2, -sine, sine)

    def started():
        far.start()
        near.start()
        weight_ref[dp, here.mine] = blocks[here.mine]
        for one in swaps:
            one.start()
        chunk = 512

        @pl.loop(0, gate_ref.shape[1] // chunk)
        def _(i):
            some = pl.ds(pl.multiple_of(i * chunk, chunk), chunk)
            gain = upright(gain_two_ref[...])
            gate_out_ref[:, some] = (gate_ref[:, some].astype(F32) * gain).astype(BF16)
            up_out_ref[:, some] = (up_ref[:, some].astype(F32) * gain).astype(BF16)

        own_tables()

    def between(step):
        @pl.when(step == 2)
        def _():
            near.finish()
            far.finish()

            @pl.loop(0, here.count)
            def _(sender):
                pair_copy(dp, sender).start()

        @pl.when(step == 4)
        def _():
            @pl.loop(0, here.count)
            def _(sender):
                pair_copy(1 - dp, sender).wait_recv()

    def share_copy(ref, number, where):
        return remote(
            ref.at[where],
            ref.at[where],
            share_sems.at[0, number],
            share_sems.at[1, number],
            here.sibling(),
        )

    def stores(number, first):
        made = []
        for block in range(2):
            where = pl.ds(pl.multiple_of((first + block) * rows, rows), rows)
            for part, out_ref in enumerate((normed_ref, grads_ref)):
                made.append(
                    pltpu.make_async_copy(
                        buf.at[first + block, part],
                        out_ref.at[where],
                        store_sems.at[number, block, part],
                    )
                )
        return made

    def compute(number, first):
        for one in stores(number, first):
            one.start()
        weight = weight_ref[...].reshape(-1, weight_ref.shape[-1])
        unit = buf[pl.ds(first, 2), 0]
        qkv = dot(unit.reshape(-1, unit.shape[-1]), weight)
        where = unit_rows(first, rows)
        cosine = cos_ref[where, :]
        sine = sin_ref[where, :]
        scale = BF16(1.0 / math.sqrt(HEAD_DIM))
        q_ref[where, :] = rotated(qkv[:, :cols], cosine, sine).astype(BF16) * scale
        for core, ref in enumerate((k_ref, v_ref)):

            @pl.when(here.core == core)
            def _():
                mine = qkv[:, cols:]
                ref[where, :] = (mine if core else rotated(mine, cosine, sine)).astype(BF16)
                share_copy(ref, number, where).start()

    gather_units(here, buf, send_sems, recv_sems, compute, between, here.length, started, True)

    @pl.loop(0, here.count)
    def _(sender):
        pair_copy(dp, sender).wait_send()

    @pl.loop(0, here.count // 2)
    def _(number):
        for one in stores(number, 0):
            one.wait()
        share_copy(k_ref, number, unit_rows(0, rows)).wait()

    for one in swaps:
        one.wait()


def gather_project(
    lengths, tokens, cotangent, query, key, value, gate, up, gains, freq, down, output, call_id
):
    seq = lax.axis_size("seq")
    rows, width = tokens.shape
    cols = 2 * HEAD_DIM
    slab, ff = gate.shape
    bf16 = lambda *shape: jax.ShapeDtypeStruct(shape, BF16)
    f32 = lambda *shape: jax.ShapeDtypeStruct(shape, F32)
    all_rows = seq * rows
    dma = pltpu.SemaphoreType.DMA
    return pl.pallas_call(
        project_kernel,
        out_shape=[
            bf16(all_rows, width),
            bf16(all_rows, width),
            bf16(all_rows, cols),
            bf16(all_rows, cols),
            bf16(all_rows, cols),
            f32(all_rows, cols),
            f32(all_rows, cols),
            jax.ShapeDtypeStruct((all_rows, 1), jnp.int32),
            bf16(2, seq, slab, 2 * cols),
            bf16(slab, ff),
            bf16(slab, ff),
            bf16(2, *down.shape),
            bf16(2, *output.shape),
        ],
        in_specs=[pl.BlockSpec(memory_space=pltpu.SMEM)] + [VMEM] * 10 + [HBM] * 2,
        out_specs=[HBM] * 2 + [VMEM] * 9 + [HBM] * 2,
        scratch_shapes=gather_scratch(seq, rows, width)
        + [
            pltpu.VMEM((seq, slab, 2 * cols), BF16),
            dma((seq // 2, 2, 2)),
            dma((2, seq // 2)),
            dma((2, seq // 2)),
            dma((2, 2)),
            dma((2,)),
            dma((2, seq)),
            dma((2, seq // 2)),
        ],
        compiler_params=params(call_id, 60),
        cost_estimate=cost(2 * all_rows * width * 2 * cols, 8 * all_rows * width),
    )(lengths, tokens, cotangent, query, key, value, gate, up, *gains, freq, down, output)


ROW_CHUNK = 32


def norm_input_grad(values, upstream):
    factor = norm_factor(values)
    inner_mean = jnp.mean(upstream * values, axis=-1, keepdims=True)
    return factor * upstream - values * factor * factor * factor * inner_mean


def in_row_chunks(rows, chunk, visit):
    @pl.loop(0, rows // chunk)
    def _(i):
        visit(pl.ds(pl.multiple_of(i * chunk, chunk), chunk))


SCATTER_PARTS = 2
SCATTER_RING = 4
SCATTER_SCRATCH = 11


def scatter_rows_of_products(
    here,
    products,
    core_out,
    core_in,
    pair_out,
    pair_in,
    line_out,
    line_in,
    held,
    core_sems,
    pair_sems,
    line_sems,
    came_sems,
    first=None,
    between=nothing,
    filler=None,
):
    length = here.length
    parts = SCATTER_PARTS * len(products)
    rows, width = held.shape
    tile = min(width, 512)
    tiles = width // tile
    steps = length * parts

    def target(i):
        ups = length - 1 - here.line
        near = here.line < length // 2
        if_near = jnp.where(i < ups, length - 1 - i, i - ups)
        if_far = jnp.where(i < here.line, i, length - 1 - (i - here.line))
        return jnp.where(i == length - 1, here.line, jnp.where(near, if_near, if_far))

    def product(line, pair, core, part, use):
        first = pl.multiple_of(here.index(line, pair, core) * rows, rows)

        def one(number):
            transposed, a_ref, b_ref, _ = products[number]
            a = a_ref[pl.ds(first, rows), :]
            begin = (part - number * SCATTER_PARTS) * width

            @pl.loop(0, tiles)
            def _(t):
                into = pl.ds(pl.multiple_of(t * tile, tile), tile)
                cols = pl.ds(pl.multiple_of(begin + t * tile, tile), tile)
                use(dot_t(a, b_ref[cols, :]) if transposed else dot(a, b_ref[:, cols]), into)

        for number in range(len(products)):
            pl.when(part // SCATTER_PARTS == number)(functools.partial(one, number))

    def core_copy(slot):
        return remote(
            core_out.at[slot % SCATTER_RING],
            core_in.at[slot],
            core_sems.at[0, slot],
            core_sems.at[1, slot],
            here.sibling(),
        )

    def pair_copy(slot):
        return remote(
            pair_out.at[slot],
            pair_in.at[slot],
            pair_sems.at[0, slot],
            pair_sems.at[1, slot],
            here.across(),
        )

    def up_copy(slot, line, part):
        into = (line + 1) * parts + part
        return remote(
            line_out.at[slot], line_in.at[into], line_sems.at[slot], came_sems.at[into], here.above()
        )

    def down_copy(slot, line, part):
        into = line * parts + part
        return remote(
            line_out.at[slot], line_in.at[into], line_sems.at[slot], came_sems.at[into], here.below()
        )

    def for_sibling(step, pair, slot):
        pl.when(slot >= SCATTER_RING)(lambda: core_copy(slot - SCATTER_RING).wait_send())

        def use(value, cols):
            core_out[slot % SCATTER_RING, :, cols] = value.astype(BF16)

        product(target(step // parts), pair, 1 - here.core, step % parts, use)
        core_copy(slot).start()

    for_sibling(jnp.int32(0), 1 - here.pair, jnp.int32(0))

    @pl.loop(0, steps)
    def _(step):
        if first is not None:
            first(step)
        pl.when(step < steps - 1)(lambda: for_sibling(step + 1, 1 - here.pair, step + 1))
        core_copy(step).wait_recv()

        def use(value, cols):
            pair_out[step, :, cols] = (value + core_in[step, :, cols].astype(F32)).astype(BF16)

        product(target(step // parts), 1 - here.pair, here.core, step % parts, use)
        pair_copy(step).start()

    for_sibling(jnp.int32(0), here.pair, jnp.int32(steps))
    between()

    @pl.loop(0, steps)
    def _(step):
        pl.when(step < steps - 1)(lambda: for_sibling(step + 1, here.pair, steps + step + 1))
        core_copy(steps + step).wait_recv()
        line = target(step // parts)
        part = step % parts

        def use(value, cols):
            held[:, cols] = value + core_in[steps + step, :, cols].astype(F32)

        product(line, here.pair, here.core, part, use)
        if filler is not None:
            filler(step)
        pair_copy(step).wait_recv()
        from_above = (line <= here.line) & (here.line < length - 1)
        from_below = (line >= here.line) & (here.line > 0)
        held[...] += pair_in[step].astype(F32)

        @pl.when(from_above)
        def _():
            down_copy(0, line, part).wait_recv()
            held[...] += line_in[line * parts + part].astype(F32)

        @pl.when(from_below)
        def _():
            up_copy(0, line, part).wait_recv()
            held[...] += line_in[(line + 1) * parts + part].astype(F32)

        for number, (_, _, _, out_ref) in enumerate(products):

            @pl.when((line == here.line) & (part // SCATTER_PARTS == number))
            def _():
                begin = (part - number * SCATTER_PARTS) * width
                out_ref[:, pl.ds(pl.multiple_of(begin, width), width)] = held[...]

        @pl.when(line < here.line)
        def _():
            line_out[step] = held[...].astype(BF16)
            down_copy(step, line, part).start()

        @pl.when(line > here.line)
        def _():
            line_out[step] = held[...].astype(BF16)
            up_copy(step, line, part).start()

    @pl.loop(2 * steps - SCATTER_RING, 2 * steps)
    def _(slot):
        core_copy(slot).wait_send()

    @pl.loop(0, steps)
    def _(step):
        pair_copy(step).wait_send()
        line = target(step // parts)
        pl.when(line < here.line)(lambda: down_copy(step, 0, 0).wait_send())
        pl.when(line > here.line)(lambda: up_copy(step, 0, 0).wait_send())


def scatter_scratch(seq, rows, width, count=1):
    length = seq // 4
    parts = SCATTER_PARTS * count
    steps = length * parts
    block = (rows, width // SCATTER_PARTS)
    dma = pltpu.SemaphoreType.DMA
    return [
        pltpu.VMEM((SCATTER_RING, *block), BF16),
        pltpu.VMEM((2 * steps, *block), BF16),
        pltpu.VMEM((steps, *block), BF16),
        pltpu.VMEM((steps, *block), BF16),
        pltpu.VMEM((steps, *block), BF16),
        pltpu.VMEM(((length + 1) * parts, *block), BF16),
        pltpu.VMEM(block, F32),
        dma((2, 2 * steps)),
        dma((2, steps)),
        dma((steps,)),
        dma(((length + 1) * parts,)),
    ]


def scatter_cost(a, width):
    return cost(2 * a.shape[0] * a.shape[1] * width, 4 * a.shape[0] * width)


def scatter_both_kernel(
    back_hbm,
    turned_hbm,
    hidden_hbm,
    down_hbm,
    middle_ref,
    grads_hbm,
    normed_hbm,
    grad_ref,
    low_ref,
    mixed_ref,
    sums_ref,
    *scratch,
):
    here = Place()
    factors = scratch[SCATTER_SCRATCH : SCATTER_SCRATCH + 4]
    back_ref, turned_ref, hidden_ref, down_ref = factors
    normed, away, came, own, fetch_sems, swap_sems, own_sems = scratch[SCATTER_SCRATCH + 4 :]
    rows = grad_ref.shape[0]
    loads = [
        pltpu.make_async_copy(src, dst, own_sems.at[number])
        for number, (src, dst) in enumerate(
            zip((back_hbm, turned_hbm, hidden_hbm, down_hbm), factors)
        )
    ]
    own_copy = pltpu.make_async_copy(
        grads_hbm.at[pl.ds(pl.multiple_of(here.mine * rows, rows), rows)], own, own_sems.at[4]
    )
    for one in loads + [own_copy]:
        one.start()
    here.greet(partner=True)
    for one in loads[:2]:
        one.wait()

    def first(step):
        @pl.when(step == SCATTER_PARTS - 1)
        def _():
            for one in loads[2:]:
                one.wait()
    chunk = normed.shape[2]
    half = normed_hbm.shape[1] // 2
    chunks = half // chunk

    def fetch(number):
        dp = jnp.where(number < chunks, 1 - here.dp, here.dp)
        begin = dp * half + number % chunks * chunk
        return pltpu.make_async_copy(
            normed_hbm.at[:, pl.ds(pl.multiple_of(begin, chunk), chunk)],
            normed.at[number % 2],
            fetch_sems.at[number % 2],
        )

    def swap(i):
        some = pl.ds(pl.multiple_of(i * chunk, chunk), chunk)
        return remote(
            away.at[some], came.at[some], swap_sems.at[0, i], swap_sems.at[1, i], here.partner()
        )

    def part(number):
        fetch(number).wait()
        pl.when(number + 1 < 2 * chunks)(lambda: fetch(number + 1).start())
        return t_dot(normed[number % 2], back_ref[...])

    def filler(place):
        step = place - 2

        @pl.when((step >= 0) & (step < chunks))
        def _():
            some = pl.ds(pl.multiple_of(step * chunk, chunk), chunk)
            away[some, :] = part(step).astype(BF16)
            swap(step).start()

        @pl.when((step >= chunks) & (step < 3 * chunks) & (step % 2 == 0))
        def _():
            i = (step - chunks) // 2
            some = pl.ds(pl.multiple_of(i * chunk, chunk), chunk)
            kept = part(chunks + i)
            swap(i).wait()
            sums_ref[some, :] = (kept + came[some, :].astype(F32)).astype(BF16)

    fetch(jnp.int32(0)).start()
    scatter_rows_of_products(
        here,
        [(False, back_ref, turned_ref, grad_ref), (False, hidden_ref, down_ref, mixed_ref)],
        *scratch[:SCATTER_SCRATCH],
        first=first,
        filler=filler,
    )
    own_copy.wait()

    def add(some):
        grad = own[some, :].astype(F32) + norm_input_grad(middle_ref[some, :], grad_ref[some, :])
        grad_ref[some, :] = grad
        low_ref[some, :] = grad.astype(BF16)

    in_row_chunks(rows, ROW_CHUNK, add)


def product_scatter_both(back, turned, hidden, down, middle, grads, normed, call_id):
    seq = lax.axis_size("seq")
    rows = back.shape[0] // seq
    width = turned.shape[1]
    cols = back.shape[1]
    chunk = width // 8
    dma = pltpu.SemaphoreType.DMA
    return pl.pallas_call(
        scatter_both_kernel,
        out_shape=[
            jax.ShapeDtypeStruct((rows, width), F32),
            jax.ShapeDtypeStruct((rows, width), BF16),
            jax.ShapeDtypeStruct((rows, width), F32),
            jax.ShapeDtypeStruct((width // 2, cols), BF16),
        ],
        in_specs=[HBM] * 4 + [VMEM] + [HBM] * 2,
        out_specs=[VMEM] * 4,
        scratch_shapes=scatter_scratch(seq, rows, width, 2)
        + [pltpu.VMEM(array.shape, BF16) for array in (back, turned, hidden, down)]
        + [
            pltpu.VMEM((2, normed.shape[0], chunk), BF16),
            pltpu.VMEM((width // 2, cols), BF16),
            pltpu.VMEM((width // 2, cols), BF16),
            pltpu.VMEM((rows, width), BF16),
            dma((2,)),
            dma((2, 4)),
            dma((5,)),
        ],
        compiler_params=params(call_id, 60),
        cost_estimate=scatter_cost(back, 3 * width),
    )(back, turned, hidden, down, middle, grads, normed)


def feed_kernel(
    block,
    q_ref,
    k_ref,
    v_ref,
    open_ref,
    b_ref,
    tokens_ref,
    gate_hbm,
    up_hbm,
    grad_hbm,
    down_hbm,
    attended_ref,
    lse_ref,
    a_ref,
    middle_ref,
    normed_ref,
    hidden_out_ref,
    back_out_ref,
    turned_out_ref,
    *scratch,
):
    here = Place()
    (
        feed_ref,
        swap_sems,
        local_sems,
        near_sems,
        far_sems,
        buf,
        send_sems,
        recv_sems,
        store_sems,
        grad_ref,
        down_ref,
        hidden_ref,
        back_ref,
        turned_ref,
        fetch_sems,
        out_sems,
    ) = scratch[SCATTER_SCRATCH:]
    slab = feed_ref.shape[2]
    slots = here.count // 2
    rows, width = middle_ref.shape
    hidden = hidden_ref.shape[1]
    tile = 512

    def swap(slot, same):
        place = feed_ref.at[here.dp, here.peer(slot, same)]
        half = 0 if same else 1
        return remote(
            place,
            place,
            swap_sems.at[0, half, slot],
            swap_sems.at[1, half, slot],
            here.partner(),
        )

    columns = hidden // 2

    def columns_of(weight, half, index):
        begin = pl.multiple_of((half * here.count + index) * columns, columns)
        return weight.at[:, pl.ds(begin, columns)]

    def place_of(sender, part):
        return feed_ref.at[here.dp, sender, :, pl.ds(part * columns, columns)]

    sources = [(weight, half) for weight in (gate_hbm, up_hbm) for half in range(2)]

    def feed_spread(same, sems):
        def copies(peer, sender, at, sem):
            return [
                remote(
                    columns_of(weight, half, peer),
                    place_of(sender, part),
                    sems.at[0, sem, part],
                    sems.at[1, at, part],
                    (here.dp, peer),
                )
                for part, (weight, half) in enumerate(sources)
            ]

        return Spread(here, same, copies)

    near = feed_spread(True, near_sems)
    own_feed = [
        pltpu.make_async_copy(
            columns_of(weight, half, here.mine), place_of(here.mine, part), local_sems.at[part]
        )
        for part, (weight, half) in enumerate(sources)
    ]
    far = feed_spread(False, far_sems)

    fetches = [
        pltpu.make_async_copy(down_hbm, down_ref, fetch_sems.at[0]),
        pltpu.make_async_copy(grad_hbm, grad_ref, fetch_sems.at[1]),
    ]
    for one in own_feed + fetches:
        one.start()
    here.call_all()

    @pl.loop(0, a_ref.shape[0] // block)
    def _(tile):
        some = pl.ds(pl.multiple_of(tile * block, block), block)
        attention_kernel(
            block,
            q_ref.at[some],
            k_ref,
            v_ref,
            open_ref.at[some],
            attended_ref.at[some],
            lse_ref.at[some],
            tile,
        )
        a_ref[some, :] = attended_ref[some, :].astype(BF16)

        @pl.when(tile == 0)
        def _():
            here.await_all()
            far.start()
            near.start()

    def between():
        far.finish()
        pl.loop(0, slots)(lambda slot: swap(slot, False).start())

    def filler(step):
        @pl.when(step == 2)
        def _():
            near.finish()
            for one in own_feed:
                one.wait()
            pl.loop(0, slots)(lambda slot: swap(slot, True).start())

    scatter_rows_of_products(
        here,
        [(False, a_ref, b_ref, middle_ref)],
        *scratch[:SCATTER_SCRATCH],
        between=between,
        filler=filler,
    )
    half = buf.shape[2]
    for part in range(2):

        @pl.loop(0, half // ROW_CHUNK)
        def _(i, part=part):
            into = pl.ds(pl.multiple_of(i * ROW_CHUNK, ROW_CHUNK), ROW_CHUNK)
            some = pl.ds(pl.multiple_of(part * half + i * ROW_CHUNK, ROW_CHUNK), ROW_CHUNK)
            middle = tokens_ref[some, :].astype(F32) + middle_ref[some, :]
            middle_ref[some, :] = middle
            buf[here.mine, part, into, :] = (middle * norm_factor(middle)).astype(BF16)

    def started():
        @pl.loop(0, slots)
        def _(slot):
            swap(slot, True).wait()
            swap(slot, False).wait()

        for one in fetches:
            one.wait()

    store = UnitStore(buf, normed_ref, store_sems)
    share = width // (2 * here.length)

    def outs(number, first):
        where = unit_rows(first, rows)
        some = pl.ds(pl.multiple_of(number * share, share), share)
        return [
            pltpu.make_async_copy(src, dst, out_sems.at[number, i])
            for i, (src, dst) in enumerate(
                [
                    (hidden_ref.at[where], hidden_out_ref.at[where]),
                    (back_ref.at[where], back_out_ref.at[where]),
                    (turned_ref.at[:, some], turned_out_ref.at[:, some]),
                ]
            )
        ]

    def compute(number, first):
        store.start(number, first)
        where = unit_rows(first, rows)
        normed = take_unit(buf, first)
        grad = grad_ref[where, :]

        @pl.loop(0, hidden // tile)
        def _(t):
            cols = pl.ds(pl.multiple_of(t * tile, tile), tile)
            later = pl.ds(pl.multiple_of(hidden + t * tile, tile), tile)
            gate = dot(normed, feed_ref[:, :, :, cols].reshape(width, tile))
            upward = dot(normed, feed_ref[:, :, :, later].reshape(width, tile))
            hidden_grad = dot_t(grad, down_ref[cols, :])
            sigmoid = jax.nn.sigmoid(gate)
            silu = gate * sigmoid
            hidden_ref[where, cols] = (silu * upward).astype(BF16)
            back_ref[where, cols] = (
                hidden_grad * upward * sigmoid * (1.0 + gate * (1.0 - sigmoid))
            ).astype(BF16)
            back_ref[where, later] = (hidden_grad * silu).astype(BF16)

        slabs = share // slab
        begin = number * slabs
        some = pl.ds(pl.multiple_of(number * share, share), share)
        weights = feed_ref[lax.div(begin, here.count), pl.ds(lax.rem(begin, here.count), slabs)]
        turned_ref[:, some] = weights.reshape(share, 2 * hidden).T
        for one in outs(number, first):
            one.start()

    gather_units(here, buf, send_sems, recv_sems, compute, started=started, level=True)

    @pl.loop(0, here.count // 2)
    def _(number):
        for one in outs(number, 0):
            one.wait()

    store.finish()


def feed_both_ways(
    queries, keys, values, opening, output, tokens, gate, up, grad_out, down, block, call_id
):
    seq = lax.axis_size("seq")
    rows, width = tokens.shape
    cols = queries.shape[1]
    hidden = down.shape[0]
    all_rows = seq * rows
    bf16 = lambda *shape: jax.ShapeDtypeStruct(shape, BF16)
    f32 = lambda *shape: jax.ShapeDtypeStruct(shape, F32)
    dma = pltpu.SemaphoreType.DMA
    return pl.pallas_call(
        functools.partial(feed_kernel, block),
        out_shape=[
            f32(all_rows, cols),
            f32(all_rows, cols // HEAD_DIM),
            bf16(all_rows, cols),
            f32(rows, width),
            bf16(all_rows, width),
            bf16(all_rows, hidden),
            bf16(all_rows, 2 * hidden),
            bf16(2 * hidden, width),
        ],
        in_specs=[VMEM] * 6 + [HBM] * 4,
        out_specs=[VMEM] * 4 + [HBM] * 4,
        scratch_shapes=scatter_scratch(seq, rows, width)
        + [
            pltpu.VMEM((2, seq, gate.shape[0], 2 * hidden), BF16),
            dma((2, 2, seq // 2)),
            dma((4,)),
            dma((2, seq // 2, 4)),
            dma((2, seq // 2, 4)),
        ]
        + gather_scratch(seq, rows // 2, width)
        + [
            dma((seq // 2, 2, 2)),
            pltpu.VMEM((all_rows, width), BF16),
            pltpu.VMEM((hidden, width), BF16),
            pltpu.VMEM((all_rows, hidden), BF16),
            pltpu.VMEM((all_rows, 2 * hidden), BF16),
            pltpu.VMEM((2 * hidden, width), BF16),
            dma((2,)),
            dma((seq // 2, 3)),
        ],
        compiler_params=params(call_id, 62),
        cost_estimate=cost(8 * all_rows * width * hidden, 8 * all_rows * width),
    )(queries, keys, values, opening, output, tokens, gate, up, grad_out, down)


def back_kernel(
    block,
    own_ref,
    weight_ref,
    low_ref,
    q_ref,
    k_ref,
    v_ref,
    att_ref,
    lse_ref,
    open_ref,
    cos_ref,
    sin_ref,
    heads_ref,
    hidden_hbm,
    out_grad_hbm,
    blocks_ref,
    normed_hbm,
    output_kept_ref,
    output_came_ref,
    down_kept_ref,
    down_came_ref,
    near_ref,
    far_ref,
    out_ref,
    qkv_ref,
    *scratch,
):
    here = Place()
    (
        buf,
        send_sems,
        recv_sems,
        part,
        hidden_ref,
        out_grad,
        grad_ref,
        output_away,
        down_away,
        dq_ref,
        dk_ref,
        dv_ref,
        share_out,
        share_in,
        back_ref,
        normed,
        kept,
        away,
        came,
        sums,
        near_sems,
        far_sems,
        local_sems,
        swap_sems,
        share_sems,
        fetch_sems,
        sum_sems,
        sum_near_sems,
        sum_far_sems,
    ) = scratch[SCATTER_SCRATCH:]
    rows, width = own_ref.shape
    cols = q_ref.shape[1]
    tile = 512
    units = 2 * here.length
    share = width // units

    hidden_copy = pltpu.make_async_copy(hidden_hbm, hidden_ref, local_sems.at[0])
    own_copy = pltpu.make_async_copy(
        blocks_ref.at[here.mine], near_ref.at[here.slot], local_sems.at[1]
    )
    near = block_spread(here, True, blocks_ref, near_ref, near_sems)
    far = block_spread(here, False, blocks_ref, far_ref, far_sems)
    swaps = [
        remote(src, dst, swap_sems.at[0, number], swap_sems.at[1, number], here.partner())
        for number, (src, dst) in enumerate(
            [(down_away, down_came_ref), (output_away, output_came_ref)]
        )
    ]

    def out_grad_copy(number):
        some = pl.ds(pl.multiple_of(number * share, share), share)
        slot = number % 2
        return pltpu.make_async_copy(
            out_grad_hbm.at[:, some], out_grad.at[slot], fetch_sems.at[0, slot]
        )

    hidden_copy.start()
    own_copy.start()
    out_grad_copy(jnp.int32(0)).start()
    here.call_all()
    put_own(here, own_ref, buf)
    part[...] = jnp.zeros_like(part)
    here.await_all()

    def split(values, kept_to, away_to, some):
        half = values.shape[0] // 2
        top, bottom = values[:half], values[half:]
        kept_to[:, some] = jnp.where(here.dp == 0, top, bottom)
        away_to[:, some] = jnp.where(here.dp == 0, bottom, top).astype(BF16)

    def compute(number, first):
        where = unit_rows(first, rows)
        unit = take_unit(buf, first)
        grad_ref[where, :] = dot_t(unit, weight_ref[...]).astype(BF16)
        attended = low_ref[where, :]
        for t in range(width // tile):
            some = slice(t * tile, (t + 1) * tile)
            part[:, some] += t_dot(attended, unit[:, some])
        pl.when(number == 0)(hidden_copy.wait)
        out_grad_copy(number).wait()
        pl.when(number + 1 < units)(lambda: out_grad_copy(number + 1).start())
        some = pl.ds(pl.multiple_of(number * share, share), share)
        split(t_dot(hidden_ref[...], out_grad[number % 2]), down_kept_ref, down_away, some)

    gather_units(here, buf, send_sems, recv_sems, compute, level=True)
    far.start()
    near.start()
    for t in range(width // tile):
        some = slice(t * tile, (t + 1) * tile)
        split(part[:, some], output_kept_ref, output_away, some)
    for one in swaps:
        one.start()

    tiles = q_ref.shape[0] // block
    scale = 1.0 / math.sqrt(HEAD_DIM)

    @pl.loop(0, tiles)
    def _(i):
        some = pl.ds(pl.multiple_of(i * block, block), block)
        attention_back_kernel(
            block,
            q_ref.at[some],
            k_ref,
            v_ref,
            grad_ref.at[some],
            att_ref.at[some],
            lse_ref.at[some],
            open_ref.at[some],
            dq_ref,
            dk_ref,
            dv_ref,
            i,
        )
        turned = rotated(dq_ref[...] * scale, cos_ref[some, :], -sin_ref[some, :])
        back_ref[some, :cols] = turned.astype(BF16)

    def share_copy(i):
        some = pl.ds(pl.multiple_of(i * block, block), block)
        return remote(
            share_out.at[some],
            share_in.at[some],
            share_sems.at[0, i],
            share_sems.at[1, i],
            here.sibling(),
        )

    @pl.loop(0, tiles)
    def _(i):
        some = pl.ds(pl.multiple_of(i * block, block), block)
        share_out[some, :] = jnp.where(here.core == 0, dv_ref[some, :], dk_ref[some, :]).astype(BF16)
        share_copy(i).start()

    @pl.loop(0, tiles)
    def _(i):
        some = pl.ds(pl.multiple_of(i * block, block), block)
        share_copy(i).wait()
        other = share_in[some, :].astype(F32)
        keys = rotated(dk_ref[some, :] + other, cos_ref[some, :], -sin_ref[some, :])
        back_ref[some, cols:] = jnp.where(here.core == 0, keys, dv_ref[some, :] + other).astype(BF16)

    swap = remote(away, came, sum_sems.at[0], sum_sems.at[1], here.partner())
    sum_near = block_spread(here, True, sums, qkv_ref.at[0], sum_near_sems)
    sum_far = block_spread(here, False, sums, qkv_ref.at[1], sum_far_sems)
    half = away.shape[0]
    chunk = normed.shape[2]
    chunks = half // chunk

    def normed_copy(number):
        dp = jnp.where(number < chunks, 1 - here.dp, here.dp)
        begin = dp * half + number % chunks * chunk
        slot = number % 2
        return pltpu.make_async_copy(
            normed_hbm.at[:, pl.ds(pl.multiple_of(begin, chunk), chunk)],
            normed.at[slot],
            fetch_sems.at[1, slot],
        )

    def heads_part(number):
        normed_copy(number).wait()
        pl.when(number + 1 < 2 * chunks)(lambda: normed_copy(number + 1).start())
        return t_dot(normed[number % 2], back_ref[...])

    normed_copy(jnp.int32(0)).start()

    def first(step):
        @pl.when(step == 2)
        def _():
            @pl.loop(0, chunks)
            def _(i):
                some = pl.ds(pl.multiple_of(i * chunk, chunk), chunk)
                away[some, :] = heads_part(i).astype(BF16)

            swap.start()

    def own_share():
        @pl.loop(0, chunks)
        def _(i):
            kept[pl.ds(pl.multiple_of(i * chunk, chunk), chunk), :] = heads_part(chunks + i)

    begin = 2
    each = 3

    def filler(step):
        @pl.when(step == begin)
        def _():
            swap.wait_recv()
            slab = sums.shape[1]

            @pl.loop(0, here.count)
            def _(i):
                some = pl.ds(pl.multiple_of(i * slab, slab), slab)
                sums[i] = (kept[some, :] + came[some, :].astype(F32)).astype(BF16)

            qkv_ref[0, here.slot] = sums[here.mine]

        @pl.when(step > begin)
        def _():
            @pl.loop(0, each)
            def _(i):
                number = (step - begin - 1) * each + i
                pl.when(number < sum_far.slots)(lambda: sum_far.start_one(number))

                @pl.when((number >= sum_far.slots) & (number < 2 * sum_far.slots - 1))
                def _():
                    sum_near.start_one(number - sum_far.slots + 1)

    scatter_rows_of_products(
        here,
        [(True, back_ref, heads_ref, out_ref)],
        *scratch[:SCATTER_SCRATCH],
        first=first,
        between=own_share,
        filler=filler,
    )
    swap.wait_send()
    for one in swaps:
        one.wait()
    near.finish()
    far.finish()
    own_copy.wait()
    sum_near.finish()
    sum_far.finish()


def attention_backwards(
    own,
    weight,
    attended,
    queries,
    keys,
    values,
    attended_sum,
    log_total,
    opening,
    cosine,
    sine,
    heads,
    hidden,
    grad_out,
    blocks,
    normed,
    block,
    call_id,
):
    seq = lax.axis_size("seq")
    rows, width = own.shape
    all_rows, cols = queries.shape
    slab = blocks.shape[1]
    half_hidden = hidden.shape[1] // 2
    chunk = width // 8
    bf16 = lambda *shape: jax.ShapeDtypeStruct(shape, BF16)
    f32 = lambda *shape: jax.ShapeDtypeStruct(shape, F32)
    dma = pltpu.SemaphoreType.DMA
    return pl.pallas_call(
        functools.partial(back_kernel, block),
        out_shape=[
            f32(cols // 2, width),
            bf16(cols // 2, width),
            f32(half_hidden, width),
            bf16(half_hidden, width),
            bf16(seq // 2, *blocks.shape[1:]),
            bf16(seq // 2, *blocks.shape[1:]),
            f32(rows, width),
            bf16(2, seq // 2, slab, 2 * cols),
        ],
        in_specs=[VMEM] * 12 + [HBM] * 4,
        out_specs=[VMEM, HBM, VMEM, HBM, HBM, HBM, VMEM, VMEM],
        scratch_shapes=scatter_scratch(seq, rows, width)
        + gather_scratch(seq, rows // 2, width)
        + [
            pltpu.VMEM((cols, width), F32),
            pltpu.VMEM(hidden.shape, BF16),
            pltpu.VMEM((2, all_rows, width // (seq // 2)), BF16),
            pltpu.VMEM((all_rows, cols), BF16),
            pltpu.VMEM((cols // 2, width), BF16),
            pltpu.VMEM((half_hidden, width), BF16),
            pltpu.VMEM((block, cols), F32),
            pltpu.VMEM((all_rows, cols), F32),
            pltpu.VMEM((all_rows, cols), F32),
            pltpu.VMEM((all_rows, cols), BF16),
            pltpu.VMEM((all_rows, cols), BF16),
            pltpu.VMEM((all_rows, 2 * cols), BF16),
            pltpu.VMEM((2, all_rows, chunk), BF16),
            pltpu.VMEM((width // 2, 2 * cols), F32),
            pltpu.VMEM((width // 2, 2 * cols), BF16),
            pltpu.VMEM((width // 2, 2 * cols), BF16),
            pltpu.VMEM((seq, slab, 2 * cols), BF16),
            dma((2, seq // 2)),
            dma((2, seq // 2)),
            dma((2,)),
            dma((2, 2)),
            dma((2, all_rows // block)),
            dma((2, 2)),
            dma((2,)),
            dma((2, seq // 2)),
            dma((2, seq // 2)),
        ],
        compiler_params=params(call_id, 62),
        cost_estimate=cost(12 * all_rows * width * cols, 12 * all_rows * width),
    )(
        own,
        weight,
        attended,
        queries,
        keys,
        values,
        attended_sum,
        log_total,
        opening,
        cosine,
        sine,
        heads,
        hidden,
        grad_out,
        blocks,
        normed,
    )


UNPACK_LINES = 4


def unpack_kernel(
    pair_ref,
    near_gate_ref,
    far_gate_ref,
    near_up_ref,
    far_up_ref,
    gate_ref,
    up_ref,
    qkv_ref,
    query_ref,
    key_ref,
    value_ref,
    gain_one_ref,
    gain_two_ref,
    tokens_ref,
    middle_ref,
    mixed_sum_ref,
    middle_grad_ref,
    upstream_ref,
    down_kept_ref,
    down_came_ref,
    output_kept_ref,
    output_came_ref,
    gate_out_ref,
    up_out_ref,
    query_out_ref,
    key_out_ref,
    value_out_ref,
    one_out_ref,
    two_out_ref,
    mixed_ref,
    token_grad_ref,
    down_out_ref,
    output_out_ref,
    total_two,
):
    pair = pair_ref[0]
    dp = lax.axis_size("dp")
    length = qkv_ref.shape[1] // 2
    slab = qkv_ref.shape[2]
    step = pl.program_id(0) * pl.num_programs(1) + pl.program_id(1)
    columns = near_gate_ref.shape[2]

    def along(grad, weight):
        return jnp.sum(grad * weight.astype(F32), axis=1, keepdims=True)

    @pl.when(step == 0)
    def _():
        total_two[...] = jnp.zeros_like(total_two)
        total = jnp.zeros((slab, 1), F32)
        gain = upright(gain_one_ref[...])

        def put(out_ref, weight_ref, begin, grad):
            cols = slice(begin, begin + grad.shape[1])
            out_ref[:, cols] = grad * gain
            return along(grad, weight_ref[:, cols])

        pairs = [{}, {}]
        for line in range(length):
            rows = []
            for number in range(4):
                slot = line * 2 + number % 2
                near, far = qkv_ref[0, slot].astype(F32), qkv_ref[1, slot].astype(F32)
                rows.append(jnp.where(number // 2 == pair, near, far))
            kv = [rows[core] + rows[core + 2] for core in range(2)]
            for half in range(dp):
                cols = slice(half * HEAD_DIM, (half + 1) * HEAD_DIM)
                for number in (0, 2):
                    two = jnp.concatenate([rows[number][:, cols], rows[number + 1][:, cols]], axis=1)
                    begin = (half * length * 4 + line * 4 + number) * HEAD_DIM
                    total = total + put(query_out_ref, query_ref, begin, two)
                for kind in range(2):
                    begin = (dp + half) * HEAD_DIM
                    pairs[kind][half, line] = kv[kind][:, begin : begin + HEAD_DIM]
        for kind, (out_ref, weight_ref) in enumerate(
            [(key_out_ref, key_ref), (value_out_ref, value_ref)]
        ):
            for half in range(dp):
                for line in range(0, length, 2):
                    two = [pairs[kind][half, line], pairs[kind][half, line + 1]]
                    begin = (half * length + line) * HEAD_DIM
                    total = total + put(
                        out_ref, weight_ref, begin, jnp.concatenate(two, axis=1)
                    )
        one_out_ref[...] = flat(total)

    mixed_ref[...] = middle_ref[...] + mixed_sum_ref[...]
    token_grad_ref[...] = middle_grad_ref[...] + norm_input_grad(
        tokens_ref[...].astype(F32), upstream_ref[...]
    )
    down_out_ref[...] = down_kept_ref[...] + down_came_ref[...].astype(F32)
    output_out_ref[...] = output_kept_ref[...] + output_came_ref[...].astype(F32)
    gain_two = upright(gain_two_ref[...])
    total = jnp.zeros((slab, 1), F32)
    for near_ref, far_ref, weight_ref, out_ref in (
        (near_gate_ref, far_gate_ref, gate_ref, gate_out_ref),
        (near_up_ref, far_up_ref, up_ref, up_out_ref),
    ):
        for number in range(2 * near_ref.shape[0]):
            slot = number // 4 * 2 + number % 2
            near, far = near_ref[slot].astype(F32), far_ref[slot].astype(F32)
            grad = jnp.where(number // 2 % 2 == pair, near, far)
            cols = slice(number * columns, (number + 1) * columns)
            total = total + along(grad, weight_ref[:, cols])
            out_ref[:, cols] = grad * gain_two
    total_two[...] += total

    @pl.when(step == pl.num_programs(0) * pl.num_programs(1) - 1)
    def _():
        two_out_ref[...] = flat(total_two[...])


def unpack(pair, near, far, gate, up, qkv, query, key, value, gain_one, gain_two, *rows):
    dp = lax.axis_size("dp")
    seq = lax.axis_size("seq")
    slab, ff = gate.shape
    length = seq // 4 // UNPACK_LINES
    columns = ff // (dp * seq)
    whole = lambda array: pl.BlockSpec(array.shape, lambda j, i: (0,) * array.ndim)
    block = lambda kind: pl.BlockSpec(
        (2 * UNPACK_LINES, slab, columns), lambda j, i: (i, 0, kind * dp + j)
    )
    tile = pl.BlockSpec((slab, 4 * UNPACK_LINES * columns), lambda j, i: (0, j * length + i))
    f32 = lambda array: jax.ShapeDtypeStruct(array.shape, F32)
    outs = [f32(gate), f32(up), f32(query), f32(key), f32(value), f32(gain_one), f32(gain_two)]
    sums = [f32(rows[0]), f32(rows[0]), f32(rows[5]), f32(rows[7])]
    steps = dp * length
    strip = lambda array: pl.BlockSpec(
        (array.shape[0] // steps, array.shape[1]), lambda j, i: (j * length + i, 0)
    )
    return pl.pallas_call(
        unpack_kernel,
        grid=(dp, length),
        in_specs=[pl.BlockSpec(memory_space=pltpu.SMEM)]
        + [block(0), block(0), block(1), block(1), tile, tile]
        + [whole(array) for array in (qkv, query, key, value, gain_one, gain_two)]
        + [strip(array) for array in rows],
        out_specs=[tile, tile]
        + [whole(array) for array in outs[2:]]
        + [strip(array) for array in sums],
        out_shape=outs + sums,
        scratch_shapes=[pltpu.VMEM((slab, 1), F32)],
        compiler_params=pltpu.CompilerParams(vmem_limit_bytes=60 << 20),
        cost_estimate=cost(slab * ff, 16 * slab * ff),
    )(
        pair,
        near,
        far,
        near,
        far,
        gate,
        up,
        qkv,
        query,
        key,
        value,
        gain_one,
        gain_two,
        *rows,
    )


def swap_dp(values):
    count = lax.axis_size("dp")
    return lax.ppermute(values, "dp", [(i, (i + 1) % count) for i in range(count)])


def gather_dp(values):
    return lax.all_gather(values, "dp", axis=0, tiled=True)


def sum_dp(partial):
    half = partial.shape[0] // 2
    mine = lax.axis_index("dp")
    away = lax.dynamic_slice_in_dim(partial, (1 - mine) * half, half, 0).astype(BF16)
    kept = lax.dynamic_slice_in_dim(partial, mine * half, half, 0)
    return kept + swap_dp(away).astype(F32)


def gather_rows(values):
    return lax.all_gather(values, "seq", axis=0, tiled=True)


def scatter_rows(partial):
    return lax.psum_scatter(partial.astype(BF16), "seq", scatter_dimension=0, tiled=True).astype(F32)


def exchange(blocks):
    return lax.all_to_all(blocks, "seq", split_axis=0, concat_axis=0, tiled=True)


def norm_factor(values):
    return lax.rsqrt(jnp.mean(values * values, axis=-1, keepdims=True) + EPS)


def norm_back(inputs, factor, gain_row, upstream):
    scaled_up = gain_row * upstream
    inner_mean = jnp.mean(scaled_up * inputs, axis=-1, keepdims=True)
    grad_in = factor * scaled_up - inputs * factor * factor * factor * inner_mean
    grad_gain = jnp.sum(upstream * inputs * factor, axis=0)
    return grad_in, grad_gain


def plain_shards(
    tokens,
    cotangent,
    doc_lengths,
    attn_gain,
    mlp_gain,
    query_weight,
    key_weight,
    value_weight,
    output_weight,
    gate_weight,
    up_weight,
    down_weight,
):
    dp = lax.axis_size("dp")
    seq = lax.axis_size("seq")
    mine = lax.axis_index("seq")
    tok_count, width = tokens.shape
    rows = tok_count * seq
    slab = query_weight.shape[0]
    share = HEAD_DIM // slab
    half_heads = HEADS // dp
    half_kv = KV_HEADS // dp
    hidden_dev = down_weight.shape[0]
    block = 512

    doc_ends = jnp.cumsum(doc_lengths[0])
    place = jnp.arange(rows, dtype=jnp.int32)
    passed = doc_ends[None, :] <= place[:, None]
    opening = jnp.max(jnp.where(passed, doc_ends[None, :], 0), axis=1)
    position = place - opening
    keeping = place < doc_ends[DOCS - 1]
    angles = position.astype(F32)[:, None] * rotary_table(HEAD_DIM)[None, :]
    cosine = jnp.cos(angles)
    sine = jnp.sin(angles)
    cos_heads = jnp.tile(cosine, (1, 2 * dp))
    sin_heads = jnp.tile(jnp.concatenate([-sine, sine], axis=1), (1, dp))
    own_keeping = lax.dynamic_slice_in_dim(keeping, mine * tok_count, tok_count, 0)

    def head_columns(weight, kept):
        split = weight.reshape(slab, dp, kept, HEAD_DIM)
        return jnp.repeat(split, seq // kept, axis=2)

    qkv_blocks = jnp.stack(
        [
            head_columns(query_weight, half_heads),
            head_columns(key_weight, half_kv),
            head_columns(value_weight, half_kv),
        ],
        axis=1,
    )
    qkv_blocks = jnp.transpose(qkv_blocks, (3, 0, 1, 2, 4)).reshape(seq * slab, 3 * dp * HEAD_DIM)
    qkv_weight = gather_dp(exchange(qkv_blocks))
    feed_blocks = jnp.stack(
        [w.reshape(slab, dp, seq, hidden_dev) for w in (gate_weight, up_weight)], axis=1
    )
    feed_blocks = jnp.transpose(feed_blocks, (3, 0, 1, 2, 4)).reshape(
        seq * slab, 2 * dp * hidden_dev
    )
    feed_weight = gather_dp(exchange(feed_blocks))
    down_own = gather_dp(down_weight)
    output_own = output_weight
    if share > 1:
        groups = [list(range(i, i + share)) for i in range(0, seq, share)]
        output_own = lax.all_gather(
            output_own, "seq", axis=0, tiled=True, axis_index_groups=groups
        )
    output_own = gather_dp(output_own)
    gains = lax.all_gather(
        jnp.stack([attn_gain, mlp_gain]), ("dp", "seq"), axis=1, tiled=True
    ).astype(F32)
    gain_one, gain_two = gains[0], gains[1]

    inputs_all = gather_rows(tokens).astype(F32)
    normed_one = (inputs_all * norm_factor(inputs_all) * gain_one).astype(BF16)
    qkv = dot(normed_one, qkv_weight)
    head_cols = dp * HEAD_DIM
    query_lin, key_lin = qkv[:, :head_cols], qkv[:, head_cols : 2 * head_cols]
    values = qkv[:, 2 * head_cols :].astype(BF16)
    scale = 1.0 / math.sqrt(HEAD_DIM)
    queries = (query_lin * cos_heads + swap_halves(query_lin) * sin_heads).astype(BF16) * BF16(scale)
    keys = (key_lin * cos_heads + swap_halves(key_lin) * sin_heads).astype(BF16)
    attended_sum, log_total = attention(queries, keys, values, opening[:, None], block)
    if share > 1:
        own_rows = ((place // tok_count) % share == mine % share)[:, None]
        attended_sum = jnp.where(own_rows, attended_sum, 0.0)
    attended = attended_sum.astype(BF16)
    inputs = tokens.astype(F32)
    middle = inputs + scatter_rows(dot(attended, output_own))

    factor_two = norm_factor(middle)
    normed_two = gather_rows((middle * factor_two * gain_two).astype(BF16))
    grad_own = jnp.where(own_keeping[:, None], cotangent, BF16(0))
    grad_out = gather_rows(grad_own)
    feed = dot(normed_two, feed_weight)
    feed_cols = dp * hidden_dev
    gate_lin, upward = feed[:, :feed_cols], feed[:, feed_cols:]
    sigmoid = jax.nn.sigmoid(gate_lin)
    hidden = (gate_lin * sigmoid * upward).astype(BF16)
    hidden_grad = dot_t(grad_out, down_own)
    gate_back = (hidden_grad * upward * sigmoid * (1.0 + gate_lin * (1.0 - sigmoid))).astype(BF16)
    up_back = (hidden_grad * gate_lin * sigmoid).astype(BF16)
    feed_back = jnp.concatenate([gate_back, up_back], axis=1)
    normed_two_grad = scatter_rows(dot_t(feed_back, feed_weight))
    mixed = middle + scatter_rows(dot(hidden, down_own))
    middle_in, gain_two_part = norm_back(middle, factor_two, gain_two, normed_two_grad)
    middle_grad = grad_own.astype(F32) + middle_in
    middle_back = gather_rows(middle_grad.astype(BF16))

    attended_grad = dot_t(middle_back, output_own).astype(BF16)
    if share > 1:
        attended_grad = jnp.where(own_rows, attended_grad, BF16(0))
    query_acc, key_acc, value_acc = attention_back(
        queries, keys, values, attended_grad, attended_sum, log_total, opening[:, None], block
    )
    query_acc = query_acc * scale
    query_back = query_acc * cos_heads - swap_halves(query_acc) * sin_heads
    key_back = key_acc * cos_heads - swap_halves(key_acc) * sin_heads
    qkv_back = jnp.concatenate([query_back, key_back, value_acc], axis=1).astype(BF16)
    normed_one_grad = scatter_rows(dot_t(qkv_back, qkv_weight))
    input_in, gain_one_part = norm_back(inputs, norm_factor(inputs), gain_one, normed_one_grad)
    token_grad = middle_grad + input_in

    feed_grad = exchange(sum_dp(t_dot(normed_two, feed_back)).astype(BF16)).astype(F32)
    feed_grad = feed_grad.reshape(seq, slab, 2, dp, hidden_dev)
    feed_grad = jnp.transpose(feed_grad, (2, 1, 3, 0, 4)).reshape(2, slab, dp * seq * hidden_dev)
    down_grad = sum_dp(t_dot(hidden, grad_out))
    output_part = t_dot(attended, middle_back)
    if share > 1:
        split = output_part.reshape(dp, share, slab, width)
        split = jnp.transpose(split, (1, 0, 2, 3)).reshape(share * dp * slab, width)
        output_part = lax.psum_scatter(
            split, "seq", scatter_dimension=0, tiled=True, axis_index_groups=groups
        )
    output_grad = sum_dp(output_part)
    qkv_grad = exchange(sum_dp(t_dot(normed_one, qkv_back)).astype(BF16)).astype(F32)
    qkv_grad = qkv_grad.reshape(seq, slab, 3, dp, HEAD_DIM)

    def own_columns(part, kept):
        summed = jnp.sum(part.reshape(kept, seq // kept, slab, dp, HEAD_DIM), axis=1)
        return jnp.transpose(summed, (1, 2, 0, 3)).reshape(slab, dp * kept * HEAD_DIM)

    query_grad = own_columns(qkv_grad[:, :, 0], half_heads)
    key_grad = own_columns(qkv_grad[:, :, 1], half_kv)
    value_grad = own_columns(qkv_grad[:, :, 2], half_kv)
    gain_parts = lax.psum(jnp.stack([gain_one_part, gain_two_part]), ("dp", "seq"))
    own = lax.axis_index("dp") * seq + mine
    gain_grads = lax.dynamic_slice_in_dim(gain_parts, own * slab, slab, 1)
    return (
        mixed,
        token_grad,
        gain_grads[0],
        gain_grads[1],
        query_grad,
        key_grad,
        value_grad,
        output_grad,
        feed_grad[0],
        feed_grad[1],
        down_grad,
    )


def frequencies():
    exponent = np.arange(0, HEAD_DIM, 2, dtype=np.float32) / np.float32(HEAD_DIM)
    inverse = np.power(np.float32(500000.0), -exponent)
    wavelength = np.float32(2.0 * math.pi) / inverse
    smooth = (np.float32(8192.0) / wavelength - np.float32(1.0)) / np.float32(3.0)
    blended = (np.float32(1.0) - smooth) * inverse / np.float32(32.0) + smooth * inverse
    scaled = np.where(
        wavelength < 2048.0,
        inverse,
        np.where(wavelength > 8192.0, inverse / np.float32(32.0), blended),
    )
    return np.tile(scaled.astype(np.float32), 4)


FREQUENCIES = frequencies()


def shards(
    tokens,
    cotangent,
    doc_lengths,
    attn_gain,
    mlp_gain,
    query_weight,
    key_weight,
    value_weight,
    output_weight,
    gate_weight,
    up_weight,
    down_weight,
):
    dp = lax.axis_size("dp")
    seq = lax.axis_size("seq")
    mine = lax.axis_index("seq")
    tok_count, width = tokens.shape
    slab = query_weight.shape[0]
    block = 512
    gain_one = attn_gain[None, :]
    gain_two = mlp_gain[None, :]

    (
        normed_one,
        grad_out,
        queries,
        keys,
        values,
        cosine,
        sine,
        opening,
        qkv_weight,
        gate_scaled,
        up_scaled,
        down_own,
        output_own,
    ) = gather_project(
        doc_lengths,
        tokens,
        cotangent,
        query_weight,
        key_weight,
        value_weight,
        gate_weight,
        up_weight,
        (gain_one, gain_two),
        jnp.asarray(FREQUENCIES)[None, :],
        down_weight,
        output_weight,
        0,
    )
    qkv_weight = qkv_weight.reshape(width, -1)
    down_own = down_own.reshape(-1, width)
    output_own = output_own.reshape(-1, width)
    attended_sum, log_total, attended, middle, normed_two, hidden, feed_back, feed_turned = (
        feed_both_ways(
            queries,
            keys,
            values,
            opening,
            output_own,
            tokens,
            gate_scaled,
            up_scaled,
            grad_out,
            down_own,
            block,
            1,
        )
    )

    middle_grad, middle_back, mixed_sum, feed_sums = product_scatter_both(
        feed_back, feed_turned, hidden, down_own, middle, grad_out, normed_two, 4
    )
    feed_sums = feed_sums.reshape(seq, slab, -1)
    (
        output_kept,
        output_came,
        down_kept,
        down_came,
        feed_grad_near,
        feed_grad_far,
        normed_one_grad,
        qkv_grads,
    ) = attention_backwards(
        middle_back,
        output_own,
        attended,
        queries,
        keys,
        values,
        attended_sum,
        log_total,
        opening,
        cosine,
        sine,
        qkv_weight,
        hidden,
        grad_out,
        feed_sums,
        normed_one,
        block,
        5,
    )

    pair = ((mine // 2) % 2).reshape(1)
    (
        gate_grad,
        up_grad,
        query_grad,
        key_grad,
        value_grad,
        attn_gain_grad,
        mlp_gain_grad,
        mixed,
        token_grad,
        down_grad,
        output_grad,
    ) = unpack(
        pair,
        feed_grad_near,
        feed_grad_far,
        gate_weight,
        up_weight,
        qkv_grads,
        query_weight,
        key_weight,
        value_weight,
        gain_one,
        gain_two,
        tokens,
        middle,
        mixed_sum,
        middle_grad,
        normed_one_grad,
        down_kept,
        down_came,
        output_kept,
        output_came,
    )
    return (
        mixed,
        token_grad,
        attn_gain_grad[0],
        mlp_gain_grad[0],
        query_grad,
        key_grad,
        value_grad,
        output_grad,
        gate_grad,
        up_grad,
        down_grad,
    )


def solution(mesh):
    both = P(("dp", "seq"), None)
    line = P(("dp", "seq"))
    dp, seq = mesh.shape["dp"], mesh.shape["seq"]

    def run(*args):
        tokens = args[0].shape[0]
        width = args[0].shape[1]
        suits = dp == 2 and seq % 4 == 0 and width == dp * seq * HEAD_DIM
        suits = suits and 2 * (tokens // dp) * width <= 16 << 20
        return jax.shard_map(
            shards if suits else plain_shards,
            mesh=mesh,
            in_specs=(both, both, P("dp", None), line, line) + (both,) * 7,
            out_specs=(both, both, line, line) + (both,) * 7,
            check_vma=False,
        )(*args)

    return run
```
